32 devices in a mesh: seq: 4 (over y, x), fsdp: 8 (over z, core).
Axes of the slice: x: 2, y: 2, z: 4, core: 2. Of those that a mesh axis runs over, the one named last changes fastest.
Arguments:
- tokens: bfloat16 [2, 4096, 2048], P(None, ('seq', 'fsdp')), may hold values from -6 to 6
- cotangent: bfloat16 [2, 4096, 2048], P(None, ('seq', 'fsdp')), may hold values from -6 to 6
- lengths: int32 [2, 4], replicated, may hold values from 1 to 2048, 4096 in all within a row
- gain_attn: bfloat16 [2048], P(('seq', 'fsdp')), may hold values from 0.5 to 1.5
- w_query: bfloat16 [2048, 2048], P(('seq', 'fsdp')), may hold values from -0.1875 to 0.1875
- w_key: bfloat16 [2048, 2048], P(('seq', 'fsdp')), may hold values from -0.1875 to 0.1875
- w_value: bfloat16 [2048, 2048], P(('seq', 'fsdp')), may hold values from -0.125 to 0.125
- w_out: bfloat16 [2048, 2048], P(('seq', 'fsdp')), may hold values from -0.75 to 0.75
- gain_mlp: bfloat16 [2048], P(('seq', 'fsdp')), may hold values from 0.5 to 1.5
- w_gate: bfloat16 [2048, 8192], P(('seq', 'fsdp')), may hold values from -0.125 to 0.125
- w_up: bfloat16 [2048, 8192], P(('seq', 'fsdp')), may hold values from -0.125 to 0.125
- w_down: bfloat16 [8192, 2048], P(('seq', 'fsdp')), may hold values from -0.125 to 0.125
Outputs:
- layer_out: bfloat16 [2, 4096, 2048], P(None, ('seq', 'fsdp'))
- input_grad: float32 [2, 4096, 2048], P(None, ('seq', 'fsdp'))
- gain_attn_grad: float32 [2048], P(('seq', 'fsdp'))
- w_query_grad: float32 [2048, 2048], P(('seq', 'fsdp'))
- w_key_grad: float32 [2048, 2048], P(('seq', 'fsdp'))
- w_value_grad: float32 [2048, 2048], P(('seq', 'fsdp'))
- w_out_grad: float32 [2048, 2048], P(('seq', 'fsdp'))
- gain_mlp_grad: float32 [2048], P(('seq', 'fsdp'))
- w_gate_grad: float32 [2048, 8192], P(('seq', 'fsdp'))
- w_up_grad: float32 [2048, 8192], P(('seq', 'fsdp'))
- w_down_grad: float32 [8192, 2048], P(('seq', 'fsdp'))
The draws below stay inside these ranges and needn't reach their ends.
Inputs may be any that keep to these rules, and one draw needn't show every extreme that they name: Row r lists in order the lengths of the 4 documents packed into sequence r, which is sequence r % 1 of micro-batch r; each row sums to 4096 and its longest document has exactly 2048 tokens.
All inputs are finite; a program needn't handle non-finite values.
Results may differ from the reference program's by a relative error of at most 0.02.
Values may be sent and summed in bfloat16 or wider, within the bound.
A program may use at most 256 MiB of HBM per device.

```python
import math
import jax
import jax.numpy as jnp
import numpy as np
from jax import lax

D = 2048
HEADS = 32
HEAD = 64
FF = 8192
MB = 2
WINDOW = 1024
DOCS = 4
MB_TOK = 4096
SEQ_LEN = 4096
SEQS = 2


def block_scale(stream_key, shape, pieces, smallest, largest):
    level = 1.0
    for position, shards_of in pieces:
        draws = jax.random.uniform(jax.random.fold_in(jax.random.fold_in(stream_key, 6), position), (shards_of,), jnp.float32, smallest / len(pieces), largest / len(pieces))
        level = level * jnp.repeat(jnp.exp(draws), shape[position] // shards_of).reshape((-1,) + (1,) * (len(shape) - 1 - position))
    return level


def length_profile(count, total, reach, skew):
    weights = [(1 << 20) // math.isqrt(standing ** skew) + 1 for standing in range(2, count + 1)]
    rest, counts = total - reach - (count - 1), [1] * (count - 1)
    while rest > 0:
        movable = [i for i in range(count - 1) if counts[i] < reach]
        mass, budget = sum([weights[i] for i in movable]), rest
        for i in movable:
            more = min(reach - counts[i], max(1, budget * weights[i] // mass), rest)
            counts[i] = counts[i] + more
            rest = rest - more
    return np.array([reach] + counts)


def ragged_sizes(rng, amount, total, most, lean):
    if amount == 2:
        one = jax.random.randint(rng, (), max(1, total - most), min(most, total - 1) + 1)
        return jnp.stack([one, total - one])
    sizes = jnp.asarray(length_profile(amount, total, most, lean), jnp.int32)
    twos = (amount - 1) // 2
    source_of, taker = sizes[1:1 + 2 * twos:2], sizes[2:2 + 2 * twos:2]
    margin = jnp.minimum(source_of - 1, most - taker)
    passed = jax.random.randint(jax.random.fold_in(rng, 1), (twos,), 0, 1 << 20) % (margin + 1)
    sizes = sizes.at[1:1 + 2 * twos:2].set(source_of - passed).at[2:2 + 2 * twos:2].set(taker + passed)
    return sizes[jax.random.permutation(jax.random.fold_in(rng, 2), amount)]


def bell_draw(own_key, dims, scale, most, shards=(), kind=jnp.bfloat16):
    array = jax.random.normal(own_key, dims, jnp.float32) * scale
    if len(shards) > 0:
        array = block_scale(own_key, dims, shards, -0.22, 0.18) * array
    return jnp.clip(array, min=-most, max=most).astype(kind)


def setup_inputs(seed: int = 0) -> dict:
    streams_of = jax.random.split(jax.random.key(seed), 13)
    tokens = bell_draw(streams_of[0], (MB, MB_TOK, D), 1.0, 6.0, ((1, 32),))
    cotangent = bell_draw(streams_of[1], (MB, MB_TOK, D), 1.0, 6.0, ((1, 32),))
    lengths = jax.vmap(lambda own: ragged_sizes(own, DOCS, SEQ_LEN, SEQ_LEN // 2, 2))(jax.random.split(streams_of[2], SEQS)).reshape((SEQS, DOCS)).astype(jnp.int32)
    gain_attn = jnp.clip(1.0 + 0.1 * jax.random.normal(streams_of[3], (D,), jnp.float32), 0.5, 1.5).astype(jnp.bfloat16)
    w_query = bell_draw(streams_of[4], (D, D), (D // 2) ** -0.5, 0.1875, ((0, 32),))
    w_key = bell_draw(streams_of[5], (D, D), (D // 2) ** -0.5, 0.1875, ((0, 32),))
    w_value = bell_draw(streams_of[6], (D, D), D ** -0.5, 0.125, ((0, 32),))
    w_out = bell_draw(streams_of[7], (D, D), (D // 32) ** -0.5, 0.75, ((0, 32),))
    gain_mlp = jnp.clip(1.0 + 0.1 * jax.random.normal(streams_of[8], (D,), jnp.float32), 0.5, 1.5).astype(jnp.bfloat16)
    w_gate = bell_draw(streams_of[9], (D, FF), D ** -0.5, 0.125, ((0, 32),))
    w_up = bell_draw(streams_of[10], (D, FF), D ** -0.5, 0.125, ((0, 32),))
    w_down = bell_draw(streams_of[11], (FF, D), (FF // 4) ** -0.5, 0.125, ((0, 32),))
    return dict(tokens=tokens, cotangent=cotangent, lengths=lengths, gain_attn=gain_attn, w_query=w_query, w_key=w_key, w_value=w_value, w_out=w_out, gain_mlp=gain_mlp, w_gate=w_gate, w_up=w_up, w_down=w_down)


EPS = 1e-05
HIGH = lax.Precision.HIGHEST

@jax.custom_vjp
def low(v):
    return lax.optimization_barrier(v.astype(jnp.bfloat16)).astype(jnp.float32)

@jax.custom_vjp
def low_back(v):
    return v

def low_keep(v):
    return (low(v), None)

def low_pass(kept, grad):
    return (grad,)

def back_keep(v):
    return (v, None)

def back_low(kept, grad):
    return (low(grad),)
low.defvjp(low_keep, low_pass)
low_back.defvjp(back_keep, back_low)

def doc_numbers(lengths, positions, batches, seq_len):
    table = lengths.reshape(batches, -1, lengths.shape[1])
    seq_count = table.shape[1]
    starts = jnp.cumsum(table, axis=2) - table
    valid = positions >= 0
    safe = jnp.maximum(positions, 0)
    which = safe // seq_len
    offset = safe % seq_len
    pick = which[:, None] == jnp.arange(seq_count, dtype=jnp.int32)[None, :]
    row_starts = lax.optimization_barrier(jnp.sum(jnp.where(pick[None, :, :, None], starts[:, None, :, :], 0), axis=2))
    count = lax.optimization_barrier(jnp.sum((row_starts[:, :, 1:] <= offset[None, :, None]).astype(jnp.int32), axis=2))
    batch_ids = jnp.arange(batches, dtype=jnp.int32)[:, None]
    number = (batch_ids * seq_count + which[None, :]) * lengths.shape[1] + count
    return jnp.where(valid[None, :], number, -1)

def matmul(left, right):
    return jnp.dot(left, right, precision=HIGH)

def normalize(values, gain):
    return values * lax.rsqrt(lax.optimization_barrier(jnp.mean(values * values, axis=-1, keepdims=True)) + EPS) * gain

def attend_block(start, query, key_pad, value_pad, doc_pad, docs):
    qblock = min(512, MB_TOK)
    query_block = lax.dynamic_slice_in_dim(query, start, qblock, 0)
    key_block = lax.dynamic_slice_in_dim(key_pad, start, qblock + WINDOW, 0)
    value_block = lax.dynamic_slice_in_dim(value_pad, start, qblock + WINDOW, 0)
    query_docs = lax.dynamic_slice_in_dim(docs, start, qblock, 0)
    key_docs = lax.dynamic_slice_in_dim(doc_pad, start, qblock + WINDOW, 0)
    query_pos = start + jnp.arange(qblock, dtype=jnp.int32)
    key_pos = start - WINDOW + jnp.arange(qblock + WINDOW, dtype=jnp.int32)
    gap = query_pos[:, None] - key_pos[None, :]
    visible = (query_docs[:, None] == key_docs[None, :]) & (gap >= 0) & (gap < WINDOW)
    q_three = query_block.reshape(qblock, HEADS, HEAD)
    k_three = key_block.reshape(qblock + WINDOW, HEADS, HEAD)
    v_three = value_block.reshape(qblock + WINDOW, HEADS, HEAD)
    scores = jnp.einsum('qhd,khd->hqk', q_three, k_three, precision=HIGH) * HEAD ** (-0.5)
    scores = low_back(scores)
    scores = jnp.where(visible[None], scores, -1e+30)
    top = lax.optimization_barrier(jnp.max(scores, axis=2, keepdims=True))
    expo = jnp.exp(scores - top)
    probs = expo / lax.optimization_barrier(jnp.sum(expo, axis=2, keepdims=True))
    mixed = jnp.einsum('hqk,khd->qhd', low(probs), v_three, precision=HIGH)
    return mixed.reshape(qblock, HEADS * HEAD)

def attend(query, key, value, docs):
    qblock = min(512, MB_TOK)
    blocks = MB_TOK // qblock
    padding = jnp.zeros((WINDOW, key.shape[1]), key.dtype)
    key_pad = jnp.concatenate([padding, key], axis=0)
    value_pad = jnp.concatenate([padding, value], axis=0)
    doc_pad = jnp.concatenate([jnp.full((WINDOW,), -1, docs.dtype), docs], axis=0)
    saved = jax.checkpoint(attend_block)
    starts = jnp.arange(blocks, dtype=jnp.int32) * qblock
    mixed = lax.map(lambda begin: saved(begin, query, key_pad, value_pad, doc_pad, docs), starts)
    return mixed.reshape(MB_TOK, HEADS * HEAD)

def layer(inputs, params, docs):
    gain_attn, w_query, w_key, w_value, w_out, gain_mlp, w_gate, w_up, w_down = params
    normed_a = low(normalize(inputs, gain_attn))
    query = low_back(low(matmul(normed_a, w_query)))
    key = low_back(low(matmul(normed_a, w_key)))
    value = low_back(low(matmul(normed_a, w_value)))
    mixed = attend(query, key, value, docs)
    attended = low_back(low(mixed))
    middle = inputs + low_back(matmul(attended, w_out))
    normed_b = low(normalize(middle, gain_mlp))
    gate = low_back(matmul(normed_b, w_gate))
    up = low_back(matmul(normed_b, w_up))
    hidden = low(gate * jax.nn.sigmoid(gate) * up)
    return middle + low_back(matmul(hidden, w_down))

def reference(tokens, cotangent, lengths, gain_attn, w_query, w_key, w_value, w_out, gain_mlp, w_gate, w_up, w_down):
    params = tuple((item.astype(jnp.float32) for item in (gain_attn, w_query, w_key, w_value, w_out, gain_mlp, w_gate, w_up, w_down)))
    docs = doc_numbers(lengths, jnp.arange(MB_TOK, dtype=jnp.int32), MB, SEQ_LEN)
    results = []
    input_grads = []
    totals = None
    for batch in range(MB):
        inputs = tokens[batch].astype(jnp.float32)
        batch_docs = docs[batch]
        result, pullback = jax.vjp(lambda values, *weights: layer(values, weights, batch_docs), inputs, *params)
        grads = pullback(cotangent[batch].astype(jnp.float32))
        results.append(result.astype(jnp.bfloat16))
        input_grads.append(grads[0])
        if totals is None:
            totals = list(grads[1:])
        else:
            totals = [left + right for left, right in zip(totals, grads[1:])]
    return (jnp.stack(results), jnp.stack(input_grads), totals[0], totals[1], totals[2], totals[3], totals[4], totals[5], totals[6], totals[7], totals[8])
```

```python
import functools

import jax
import jax.numpy as jnp
from jax import lax
from jax.experimental import pallas as pl
from jax.experimental.pallas import tpu as pltpu
from jax.sharding import PartitionSpec as P

HEAD = 64
FF = 8192
WINDOW = 1024
PAIR = 128
TILE = 512
LOW = -1e30
EPS = 1e-05
MESH = pl.DeviceIdType.MESH
MIB = 2**20


def to_half(values):
    return values.astype(jnp.bfloat16)


def normalize(values, gain):
    return values * lax.rsqrt(jnp.mean(values * values, axis=-1, keepdims=True) + EPS) * gain


def contract_rows(left, right):
    return lax.dot_general(
        left, right, (((0,), (0,)), ((), ())), preferred_element_type=jnp.float32
    )


def dot_nt(left, right):
    return lax.dot_general(
        left, right, (((1,), (1,)), ((), ())), preferred_element_type=jnp.float32
    )


def dot_nn(left, right):
    return jnp.dot(left, right, preferred_element_type=jnp.float32)


def gate_back(gate, up, d_hidden):
    sigma = jax.nn.sigmoid(gate)
    d_gate = d_hidden * up * sigma * (1.0 + gate * (1.0 - sigma))
    d_up = d_hidden * gate * sigma
    return (to_half(d_gate), to_half(d_up))


def head_lanes(values, half):
    lane = lax.broadcasted_iota(jnp.int32, values.shape, 1)
    return jnp.where((lane >= HEAD) == (half == 1), values, jnp.zeros_like(values))


def masked_scores(k_rows, q_head, low):
    keys, block = k_rows.shape[0], q_head.shape[0]
    scores = dot_nt(k_rows, q_head)
    at = lax.broadcasted_iota(jnp.int32, (keys, block), 0)
    query = lax.broadcasted_iota(jnp.int32, (keys, block), 1)
    seen = (at >= low) & (at <= query + WINDOW)
    return jnp.where(seen, scores, LOW)


def attend_kernel(block, q_ref, k_ref, v_ref, low_ref, out_ref, lse_ref, vt_ref):
    step = pl.program_id(1)
    span = q_ref.shape[2]

    @pl.when(step == 0)
    def _():
        vt_ref[...] = v_ref[0].T

    begin = pl.multiple_of(step * block, block)
    keys = pl.ds(begin, block + WINDOW)
    low = low_ref[0]
    for pair in range(span // PAIR):
        lanes = slice(pair * PAIR, (pair + 1) * PAIR)
        q_pair = q_ref[0, :, lanes] * jnp.asarray(HEAD**-0.5, jnp.bfloat16)
        k_rows = k_ref[0, keys, lanes]
        vt = vt_ref[lanes, keys]
        mixed = []
        for half in range(2):
            scores = masked_scores(k_rows, head_lanes(q_pair, half), low)
            top = jnp.max(scores, axis=0, keepdims=True)
            expo = jnp.exp(scores - top)
            total = jnp.sum(expo, axis=0, keepdims=True)
            mixed.append(dot_nn(vt, expo.astype(jnp.bfloat16)) / total)
            row = pair * 2 + half
            lse_ref[0, row : row + 1, :] = top + jnp.log(total)
        row = lax.broadcasted_iota(jnp.int32, mixed[0].shape, 0)
        out_ref[0, :, lanes] = jnp.where(row < HEAD, mixed[0], mixed[1]).T.astype(jnp.bfloat16)


def attend(query, kv_pad, low, block):
    batches, length, span = query.shape
    padded = kv_pad.shape[1]
    heads = span // HEAD
    return pl.pallas_call(
        functools.partial(attend_kernel, block),
        grid=(batches, length // block),
        in_specs=[
            pl.BlockSpec((1, block, span), lambda b, i: (b, i, 0)),
            pl.BlockSpec((1, padded, span), lambda b, i: (b, 0, 0)),
            pl.BlockSpec((1, padded, span), lambda b, i: (b, 0, 1)),
            pl.BlockSpec((1, 1, block), lambda b, i: (b, 0, i)),
        ],
        out_specs=[
            pl.BlockSpec((1, block, span), lambda b, i: (b, i, 0)),
            pl.BlockSpec((1, heads, block), lambda b, i: (b, 0, i)),
        ],
        out_shape=[
            jax.ShapeDtypeStruct((batches, length, span), jnp.bfloat16),
            jax.ShapeDtypeStruct((batches, heads, length), jnp.float32),
        ],
        scratch_shapes=[pltpu.VMEM((span, padded), jnp.bfloat16)],
        compiler_params=pltpu.CompilerParams(vmem_limit_bytes=48 * 2**20),
        name="attend",
    )(query, kv_pad, kv_pad, low)


def attend_back_kernel(
    block, q_ref, k_ref, v_ref, low_ref, lse_ref, d_ref, dq_ref, dk_ref, dv_ref, kt_ref
):
    step = pl.program_id(1)
    span = q_ref.shape[2]
    scale = jnp.asarray(HEAD**-0.5, jnp.bfloat16)

    @pl.when(step == 0)
    def _():
        kt_ref[...] = k_ref[0].T * scale
        dk_ref[...] = jnp.zeros_like(dk_ref)
        dv_ref[...] = jnp.zeros_like(dv_ref)

    begin = pl.multiple_of(step * block, block)
    keys = pl.ds(begin, block + WINDOW)
    low = low_ref[0]
    for pair in range(span // PAIR):
        lanes = slice(pair * PAIR, (pair + 1) * PAIR)
        q_pair = q_ref[0, :, lanes] * scale
        d_pair = d_ref[0, :, lanes]
        k_rows = k_ref[0, keys, lanes]
        v_rows = v_ref[0, keys, lanes]
        kt = kt_ref[lanes, keys]
        back = []
        for half in range(2):
            row = pair * 2 + half
            q_head = head_lanes(q_pair, half)
            d_head = head_lanes(d_pair, half)
            scores = masked_scores(k_rows, q_head, low)
            probs = jnp.exp(scores - lse_ref[0, row : row + 1, :])
            d_probs = dot_nt(v_rows, d_head)
            along = jnp.sum(probs * d_probs, axis=0, keepdims=True)
            d_scores = (probs * (d_probs - along)).astype(jnp.bfloat16)
            dv_ref[0, keys, lanes] += dot_nn(probs.astype(jnp.bfloat16), d_head)
            dk_ref[0, keys, lanes] += dot_nn(d_scores, q_head)
            back.append(dot_nn(kt, d_scores))
        at = lax.broadcasted_iota(jnp.int32, back[0].shape, 0)
        dq_ref[0, :, lanes] = jnp.where(at < HEAD, back[0], back[1]).T.astype(jnp.bfloat16)


def attend_back(query, kv_pad, low, lse, d_att, block):
    batches, length, span = query.shape
    padded = kv_pad.shape[1]
    heads = span // HEAD
    rows = pl.BlockSpec((1, block, span), lambda b, i: (b, i, 0))
    whole = pl.BlockSpec((1, padded, span), lambda b, i: (b, 0, 0))
    return pl.pallas_call(
        functools.partial(attend_back_kernel, block),
        grid=(batches, length // block),
        in_specs=[
            rows,
            whole,
            pl.BlockSpec((1, padded, span), lambda b, i: (b, 0, 1)),
            pl.BlockSpec((1, 1, block), lambda b, i: (b, 0, i)),
            pl.BlockSpec((1, heads, block), lambda b, i: (b, 0, i)),
            rows,
        ],
        out_specs=[rows, whole, whole],
        out_shape=[
            jax.ShapeDtypeStruct((batches, length, span), jnp.bfloat16),
            jax.ShapeDtypeStruct((batches, padded, span), jnp.float32),
            jax.ShapeDtypeStruct((batches, padded, span), jnp.float32),
        ],
        scratch_shapes=[pltpu.VMEM((span, padded), jnp.bfloat16)],
        compiler_params=pltpu.CompilerParams(vmem_limit_bytes=48 * 2**20),
        name="attend_back",
    )(query, kv_pad, kv_pad, low, lse, d_att)


def line_place():
    own = lax.axis_index("fsdp")
    chip = own // 2
    core = lax.rem(own, 2)
    return own, chip, core, own + 1 - 2 * core


def greet_line(chips, own, chip, other):
    barrier = pltpu.get_barrier_semaphore()
    has_left = chip > 0
    has_right = chip < chips - 1

    def greet(peer):
        pl.semaphore_signal(barrier, inc=1, device_id={"fsdp": peer}, device_id_type=MESH)

    greet(other)
    pl.when(has_left)(lambda: greet(own - 2))
    pl.when(has_right)(lambda: greet(own + 2))
    pl.semaphore_wait(barrier, 1 + has_left.astype(jnp.int32) + has_right.astype(jnp.int32))
    return has_left, has_right


def spread_line(chips, x_ref, buf, send_sem, recv_sem, use):
    own, chip, core, other = line_place()
    has_left, has_right = greet_line(chips, own, chip, other)

    def move(slot, way, peer):
        return pltpu.make_async_remote_copy(
            src_ref=buf.at[slot],
            dst_ref=buf.at[slot],
            send_sem=send_sem.at[way, slot],
            recv_sem=recv_sem.at[slot],
            device_id={"fsdp": peer},
            device_id_type=MESH,
        )

    buf[own] = x_ref[...]
    pl.when(has_right)(lambda: move(own, 1, own + 2).start())
    pl.when(has_left)(lambda: move(own, 0, own - 2).start())
    move(own, 2, other).start()

    @pl.loop(0, chips + 1)
    def _(far):
        @pl.when((far > 0) & (chip - far >= 0))
        def _():
            slot = (chip - far) * 2 + core
            move(slot, 1, own).wait_recv()
            pl.when(has_right)(lambda: move(slot, 1, own + 2).start())
            move(slot, 2, other).start()

        @pl.when((far > 0) & (chip + far < chips))
        def _():
            slot = (chip + far) * 2 + core
            move(slot, 0, own).wait_recv()
            pl.when(has_left)(lambda: move(slot, 0, own - 2).start())
            move(slot, 2, other).start()

        @pl.loop(0, 4)
        def _(turn):
            side = lax.rem(turn, 2)
            across = turn // 2
            away = far - across
            source = chip + away * (2 * side - 1)
            valid = (away >= 0) & (away < chips) & (source >= 0) & (source < chips)
            valid = valid & ((side == 0) | (away > 0))

            @pl.when(valid)
            def _():
                slot = source * 2 + core + across * (1 - 2 * core)
                pl.when(across == 1)(lambda: move(slot, 2, own).wait_recv())
                use(slot)

    @pl.loop(0, chips)
    def _(place):
        slot = place * 2 + core
        move(slot, 2, other).wait_send()
        pl.when(has_right & (place <= chip))(lambda: move(slot, 1, own + 2).wait_send())
        pl.when(has_left & (place >= chip))(lambda: move(slot, 0, own - 2).wait_send())


def reduce_line(chips, width, product, out_ref, acc, outs, ins, send_sem, recv_sem):
    own, chip, core, other = line_place()
    has_left, has_right = greet_line(chips, own, chip, other)
    cross_out, line_out = outs
    cross_in, line_in = ins
    tiles = width // TILE

    def cross(place):
        return pltpu.make_async_remote_copy(
            src_ref=cross_out.at[place],
            dst_ref=cross_in.at[place],
            send_sem=send_sem.at[0, place],
            recv_sem=recv_sem.at[0, place],
            device_id={"fsdp": other},
            device_id_type=MESH,
        )

    def along(place, landing, peer):
        return pltpu.make_async_remote_copy(
            src_ref=line_out.at[place],
            dst_ref=line_in.at[landing],
            send_sem=send_sem.at[1, place],
            recv_sem=recv_sem.at[1, landing],
            device_id={"fsdp": peer},
            device_id_type=MESH,
        )

    def columns(tile):
        return pl.ds(pl.multiple_of(tile * TILE, TILE), TILE)

    @pl.loop(0, 2 * chips - 1)
    def _(step):
        away = chips - 1 - step // 2
        side = lax.rem(step, 2)
        place = chip + away * (1 - 2 * side)

        @pl.when((place >= 0) & (place < chips))
        def _():
            @pl.loop(0, tiles)
            def _(tile):
                cross_out[place, :, columns(tile)] = to_half(product(place * 2 + 1 - core, tile))

            cross(place).start()

            @pl.loop(0, tiles)
            def _(tile):
                acc[:, columns(tile)] = product(place * 2 + core, tile)

            cross(place).wait_recv()

            @pl.when(away > 0)
            def _():
                rightward = side == 0
                upstream = (rightward & has_left) | (jnp.logical_not(rightward) & has_right)

                @pl.when(upstream)
                def _():
                    along(place, place, own).wait_recv()
                    line_out[place] = to_half(
                        acc[...]
                        + cross_in[place].astype(jnp.float32)
                        + line_in[place].astype(jnp.float32)
                    )

                @pl.when(jnp.logical_not(upstream))
                def _():
                    line_out[place] = to_half(acc[...] + cross_in[place].astype(jnp.float32))

                @pl.when(rightward)
                def _():
                    along(place, place, own + 2).start()

                @pl.when(jnp.logical_not(rightward))
                def _():
                    landing = jnp.where(away == 1, chips, place)
                    along(place, landing, own - 2).start()

            @pl.when(away == 0)
            def _():
                out_ref[...] = acc[...] + cross_in[place].astype(jnp.float32)

                @pl.when(has_left)
                def _():
                    along(place, place, own).wait_recv()
                    out_ref[...] += line_in[place].astype(jnp.float32)

                @pl.when(has_right)
                def _():
                    along(place, chips, own).wait_recv()
                    out_ref[...] += line_in[chips].astype(jnp.float32)

    @pl.loop(0, chips)
    def _(place):
        cross(place).wait_send()
        pl.when(place != chip)(lambda: along(place, place, own).wait_send())


def project_kernel(chips, batches, x_ref, w_ref, g_ref, q_ref, kv_ref, buf, send, recv, keep):
    piece = x_ref.shape[0] // batches
    span = q_ref.shape[2]

    def kept(slot, batch):
        return pltpu.make_async_copy(
            buf.at[slot, pl.ds(batch * piece, piece)],
            g_ref.at[batch, pl.ds(pl.multiple_of(slot * piece, piece), piece)],
            keep.at[slot, batch],
        )

    def use(slot):
        for batch in range(batches):
            kept(slot, batch).start()
        rows = pl.ds(pl.multiple_of(slot * piece, piece), piece)
        values = buf[slot]
        for part in range(3):
            got = to_half(dot_nn(values, w_ref[:, part * span : (part + 1) * span]))
            for batch in range(batches):
                own = got[batch * piece : (batch + 1) * piece]
                if part == 0:
                    q_ref[batch, rows, :] = own
                else:
                    kv_ref[batch, rows, (part - 1) * span : part * span] = own

    spread_line(chips, x_ref, buf, send, recv, use)

    @pl.loop(0, 2 * chips)
    def _(slot):
        for batch in range(batches):
            kept(slot, batch).wait()


def project_heads(chips, batches, x, w, collective):
    rows, width = x.shape
    slots = 2 * chips
    length = slots * rows // batches
    span = w.shape[1] // 3
    vmem = pl.BlockSpec(memory_space=pltpu.VMEM)
    return pl.pallas_call(
        functools.partial(project_kernel, chips, batches),
        out_shape=[
            jax.ShapeDtypeStruct((batches, length, width), jnp.bfloat16),
            jax.ShapeDtypeStruct((batches, length, span), jnp.bfloat16),
            jax.ShapeDtypeStruct((batches, length, 2 * span), jnp.bfloat16),
        ],
        in_specs=[vmem, vmem],
        out_specs=[pl.BlockSpec(memory_space=pl.ANY), vmem, vmem],
        scratch_shapes=[
            pltpu.VMEM((slots, rows, width), jnp.bfloat16),
            pltpu.SemaphoreType.DMA((3, slots)),
            pltpu.SemaphoreType.DMA((slots,)),
            pltpu.SemaphoreType.DMA((slots, batches)),
        ],
        compiler_params=pltpu.CompilerParams(
            collective_id=collective, has_side_effects=True, vmem_limit_bytes=56 * MIB
        ),
        cost_estimate=line_cost(slots, rows, width, w.shape[1]),
        name="project_heads",
    )(x, w)


def line_cost(slots, rows, width, depth):
    moved = slots * rows * width * 2
    return pl.CostEstimate(
        flops=2 * slots * rows * width * depth,
        bytes_accessed=24 * moved,
        transcendentals=0,
        remote_bytes_transferred=moved,
    )


def units_kernel(chips, x_ref, w_ref, g_ref, gate_ref, up_ref, hidden_ref, buf, send, recv, keep):
    rows = x_ref.shape[0]
    units = gate_ref.shape[1]

    def kept(slot):
        return pltpu.make_async_copy(buf.at[slot], g_ref.at[slot], keep.at[slot])

    def use(slot):
        kept(slot).start()
        place = pl.ds(pl.multiple_of(slot * rows, rows), rows)

        @pl.loop(0, units // TILE)
        def _(tile):
            first = pl.multiple_of(tile * TILE, TILE)
            columns = pl.ds(first, TILE)
            values = buf[slot]
            gate = dot_nn(values, w_ref[:, columns])
            up = dot_nn(values, w_ref[:, pl.ds(pl.multiple_of(units + first, TILE), TILE)])
            gate_ref[place, columns] = to_half(gate)
            up_ref[place, columns] = to_half(up)
            hidden_ref[place, columns] = to_half(gate * jax.nn.sigmoid(gate) * up)

    spread_line(chips, x_ref, buf, send, recv, use)

    @pl.loop(0, 2 * chips)
    def _(slot):
        kept(slot).wait()


def hidden_units(chips, x, w, collective):
    rows, width = x.shape
    slots = 2 * chips
    units = w.shape[1] // 2
    vmem = pl.BlockSpec(memory_space=pltpu.VMEM)
    part = jax.ShapeDtypeStruct((slots * rows, units), jnp.bfloat16)
    return pl.pallas_call(
        functools.partial(units_kernel, chips),
        out_shape=[jax.ShapeDtypeStruct((slots, rows, width), jnp.bfloat16), part, part, part],
        in_specs=[vmem, vmem],
        out_specs=[pl.BlockSpec(memory_space=pl.ANY), vmem, vmem, vmem],
        scratch_shapes=[
            pltpu.VMEM((slots, rows, width), jnp.bfloat16),
            pltpu.SemaphoreType.DMA((3, slots)),
            pltpu.SemaphoreType.DMA((slots,)),
            pltpu.SemaphoreType.DMA((slots,)),
        ],
        compiler_params=pltpu.CompilerParams(
            collective_id=collective, has_side_effects=True, vmem_limit_bytes=58 * MIB
        ),
        cost_estimate=line_cost(slots, rows, width, w.shape[1]),
        name="hidden_units",
    )(x, w)


def branch_back_kernel(chips, batches, x_ref, w_ref, g_ref, d_ref, buf, send, recv, keep):
    piece = x_ref.shape[0] // batches

    def kept(slot, batch):
        return pltpu.make_async_copy(
            buf.at[slot, pl.ds(batch * piece, piece)],
            g_ref.at[batch, pl.ds(pl.multiple_of(slot * piece, piece), piece)],
            keep.at[slot, batch],
        )

    def use(slot):
        for batch in range(batches):
            kept(slot, batch).start()
        rows = pl.ds(pl.multiple_of(slot * piece, piece), piece)
        got = to_half(dot_nt(buf[slot], w_ref[...]))
        for batch in range(batches):
            d_ref[batch, rows, :] = got[batch * piece : (batch + 1) * piece]

    spread_line(chips, x_ref, buf, send, recv, use)

    @pl.loop(0, 2 * chips)
    def _(slot):
        for batch in range(batches):
            kept(slot, batch).wait()


def branch_back(chips, batches, x, w, collective):
    rows, width = x.shape
    slots = 2 * chips
    length = slots * rows // batches
    span = w.shape[0]
    vmem = pl.BlockSpec(memory_space=pltpu.VMEM)
    return pl.pallas_call(
        functools.partial(branch_back_kernel, chips, batches),
        out_shape=[
            jax.ShapeDtypeStruct((batches, length, width), jnp.bfloat16),
            jax.ShapeDtypeStruct((batches, length, span), jnp.bfloat16),
        ],
        in_specs=[vmem, vmem],
        out_specs=[pl.BlockSpec(memory_space=pl.ANY), vmem],
        scratch_shapes=[
            pltpu.VMEM((slots, rows, width), jnp.bfloat16),
            pltpu.SemaphoreType.DMA((3, slots)),
            pltpu.SemaphoreType.DMA((slots,)),
            pltpu.SemaphoreType.DMA((slots, batches)),
        ],
        compiler_params=pltpu.CompilerParams(
            collective_id=collective, has_side_effects=True, vmem_limit_bytes=56 * MIB
        ),
        cost_estimate=line_cost(slots, rows, width, span),
        name="branch_back",
    )(x, w)


def sum_kernel(chips, across, a_ref, w_ref, out_ref, acc, *scratch):
    width = out_ref.shape[1]
    rows = out_ref.shape[0]
    outs, ins, send, recv = scratch[0:2], scratch[2:4], scratch[4], scratch[5]

    def product(slot, tile):
        if len(a_ref.shape) == 3:
            piece = rows // a_ref.shape[0]
            place = pl.ds(pl.multiple_of(slot * piece, piece), piece)
            left = jnp.concatenate([a_ref[batch, place, :] for batch in range(a_ref.shape[0])], axis=0)
        else:
            left = a_ref[pl.ds(pl.multiple_of(slot * rows, rows), rows), :]
        part = pl.ds(pl.multiple_of(tile * TILE, TILE), TILE)
        if across:
            return dot_nt(left, w_ref[part, :])
        return dot_nn(left, w_ref[:, part])

    reduce_line(chips, width, product, out_ref, acc, outs, ins, send, recv)


def sum_products(chips, a, w, across, name, collective):
    slots = 2 * chips
    width = w.shape[0] if across else w.shape[1]
    rows = (a.shape[0] * a.shape[1] if a.ndim == 3 else a.shape[0]) // slots
    vmem = pl.BlockSpec(memory_space=pltpu.VMEM)
    half = functools.partial(pltpu.VMEM, dtype=jnp.bfloat16)
    return pl.pallas_call(
        functools.partial(sum_kernel, chips, across),
        out_shape=jax.ShapeDtypeStruct((rows, width), jnp.float32),
        in_specs=[vmem, vmem],
        out_specs=vmem,
        scratch_shapes=[
            pltpu.VMEM((rows, width), jnp.float32),
            half((chips, rows, width)),
            half((chips, rows, width)),
            half((chips, rows, width)),
            half((chips + 1, rows, width)),
            pltpu.SemaphoreType.DMA((2, chips)),
            pltpu.SemaphoreType.DMA((2, chips + 1)),
        ],
        compiler_params=pltpu.CompilerParams(
            collective_id=collective, has_side_effects=True, vmem_limit_bytes=60 * MIB
        ),
        cost_estimate=line_cost(slots, rows, width, a.shape[-1]),
        name=name,
    )(a, w)


def swap_kernel(group, count, *refs):
    sources, targets = refs[:count], refs[count : 2 * count]
    send, recv, keep = refs[2 * count :]
    own = lax.axis_index("fsdp")
    barrier = pltpu.get_barrier_semaphore()

    @pl.loop(1, group)
    def _(ahead):
        peer = lax.rem(own + ahead, group)
        pl.semaphore_signal(barrier, inc=1, device_id={"fsdp": peer}, device_id_type=MESH)

    pl.semaphore_wait(barrier, group - 1)

    def move(item, peer, source):
        return pltpu.make_async_remote_copy(
            src_ref=sources[item].at[peer],
            dst_ref=targets[item].at[source],
            send_sem=send.at[item, peer],
            recv_sem=recv.at[item, source],
            device_id={"fsdp": peer},
            device_id_type=MESH,
        )

    for item in range(count):
        pltpu.make_async_copy(sources[item].at[own], targets[item].at[own], keep.at[item]).start()

        @pl.loop(1, group)
        def _(ahead, item=item):
            move(item, lax.rem(own + ahead, group), own).start()

    for item in range(count):
        pltpu.make_async_copy(sources[item].at[own], targets[item].at[own], keep.at[item]).wait()

        @pl.loop(1, group)
        def _(ahead, item=item):
            peer = lax.rem(own + ahead, group)
            move(item, peer, peer).wait_recv()
            move(item, peer, own).wait_send()


def swap_blocks(group, arrays, name, collective):
    count = len(arrays)
    anywhere = pl.BlockSpec(memory_space=pl.ANY)
    moved = sum(item.size * 2 for item in arrays)
    return pl.pallas_call(
        functools.partial(swap_kernel, group, count),
        out_shape=[jax.ShapeDtypeStruct(item.shape, item.dtype) for item in arrays],
        in_specs=[anywhere] * count,
        out_specs=[anywhere] * count,
        scratch_shapes=[
            pltpu.SemaphoreType.DMA((count, group)),
            pltpu.SemaphoreType.DMA((count, group)),
            pltpu.SemaphoreType.DMA((count,)),
        ],
        compiler_params=pltpu.CompilerParams(collective_id=collective, has_side_effects=True),
        cost_estimate=pl.CostEstimate(
            flops=0,
            bytes_accessed=40 * moved,
            transcendentals=0,
            remote_bytes_transferred=moved,
        ),
        name=name,
    )(*arrays)


def tiles_kernel(seqs, group, same, x_ref, out_ref, send, recv):
    devices = seqs * group
    own = lax.axis_index("seq") * group + lax.axis_index("fsdp")
    barrier = pltpu.get_barrier_semaphore()

    def place(peer):
        return {"seq": peer // group, "fsdp": lax.rem(peer, group)}

    @pl.loop(1, devices)
    def _(ahead):
        peer = lax.rem(own + ahead, devices)
        pl.semaphore_signal(barrier, inc=1, device_id=place(peer), device_id_type=MESH)

    pl.semaphore_wait(barrier, devices - 1)
    out_ref[own] = x_ref[0] if same else x_ref[own]

    def move(peer, source):
        return pltpu.make_async_remote_copy(
            src_ref=x_ref.at[0 if same else peer],
            dst_ref=out_ref.at[source],
            send_sem=send.at[peer],
            recv_sem=recv.at[source],
            device_id=place(peer),
            device_id_type=MESH,
        )

    @pl.loop(1, devices)
    def _(ahead):
        move(lax.rem(own + ahead, devices), own).start()

    @pl.loop(1, devices)
    def _(ahead):
        peer = lax.rem(own + ahead, devices)
        move(peer, peer).wait_recv()
        move(peer, own).wait_send()


def swap_tiles(seqs, group, x, same, name, collective):
    devices = seqs * group
    vmem = pl.BlockSpec(memory_space=pltpu.VMEM)
    return pl.pallas_call(
        functools.partial(tiles_kernel, seqs, group, same),
        out_shape=jax.ShapeDtypeStruct((devices, 8, 128), jnp.float32),
        in_specs=[vmem],
        out_specs=vmem,
        scratch_shapes=[
            pltpu.SemaphoreType.DMA((devices,)),
            pltpu.SemaphoreType.DMA((devices,)),
        ],
        compiler_params=pltpu.CompilerParams(collective_id=collective, has_side_effects=True),
        name=name,
    )(x)


def doc_starts(lengths, positions, batches, seq_len):
    table = lengths.reshape(batches, -1, lengths.shape[1])
    starts = jnp.cumsum(table, axis=2) - table
    per_batch = seq_len // table.shape[1]
    begins = (starts + (jnp.arange(table.shape[1], dtype=jnp.int32) * per_batch)[None, :, None]).reshape(
        batches, -1
    )
    before = begins[:, None, :] <= positions[None, :, None]
    return jnp.max(jnp.where(before, begins[:, None, :], 0), axis=2)


def body(
    tokens,
    cotangent,
    lengths,
    gain_attn,
    w_query,
    w_key,
    w_value,
    w_out,
    gain_mlp,
    w_gate,
    w_up,
    w_down,
):
    batches, piece, width = tokens.shape
    seqs = lax.axis_size("seq")
    group = lax.axis_size("fsdp")
    chips = group // 2
    devices = seqs * group
    seq_len = piece * devices
    rows = batches * piece
    share = w_query.shape[0]
    span = width // group
    length = group * piece
    group_rows = group * rows
    units = FF // group
    aligned = share == HEAD
    member = lax.axis_index("fsdp")

    def blocks(weight):
        part = weight.shape[1] // devices
        if part < HEAD:
            return weight.reshape(share, group, -1).transpose(1, 0, 2)
        return weight.reshape(share, seqs, group, part).transpose(2, 0, 1, 3).reshape(group, share, -1)

    def unblock(cols, total):
        part = total // devices
        if part < HEAD:
            return cols.transpose(1, 0, 2).reshape(share, total)
        return cols.reshape(group, share, seqs, part).transpose(1, 2, 0, 3).reshape(share, total)

    tile = jnp.zeros((1, 8, 128), jnp.float32)
    tile = tile.at[0, 0, :share].set(gain_attn.astype(jnp.float32))
    tile = tile.at[0, 0, 64 : 64 + share].set(gain_mlp.astype(jnp.float32))
    gains = swap_tiles(seqs, group, tile, True, "gains", 1)
    gain_one = gains[:, 0, :share].reshape(width)
    gain_two = gains[:, 0, 64 : 64 + share].reshape(width)

    inputs = tokens.astype(jnp.float32).reshape(rows, width)
    upstream = cotangent.astype(jnp.float32).reshape(rows, width)
    group_d = lax.all_gather(cotangent.reshape(rows, width), "fsdp", axis=0, tiled=True)
    wd_part = lax.all_gather(w_down, "seq", axis=0, tiled=True)
    if aligned:
        wo_part = lax.all_gather(w_out, "seq", axis=0, tiled=True)
    else:
        wo_all = lax.all_gather(w_out, ("seq", "fsdp"), axis=0, tiled=True)
        wo_part = lax.dynamic_slice_in_dim(wo_all, member * span, span, 0)

    attn_blocks = jnp.concatenate([blocks(w_query), blocks(w_key), blocks(w_value)], axis=2)
    unit_blocks = jnp.concatenate([blocks(w_gate), blocks(w_up)], axis=2)
    attn_own, unit_own = swap_blocks(group, [attn_blocks, unit_blocks], "weights", 2)
    w_heads = lax.all_gather(attn_own.reshape(group * share, -1), "seq", axis=0, tiled=True)
    w_units = lax.all_gather(unit_own.reshape(group * share, -1), "seq", axis=0, tiled=True)

    group_start = lax.axis_index("seq") * length
    positions = group_start + jnp.arange(length, dtype=jnp.int32)
    begins = doc_starts(lengths, positions, batches, seq_len)
    at = jnp.arange(length, dtype=jnp.int32)
    block = min(256, length)
    low = jnp.maximum(begins - group_start + WINDOW, at[None, :] + 1) - (at // block * block)[None, :]
    low = low[:, None, :]

    normed_a = to_half(normalize(inputs, gain_one))
    group_a, query, key_value = project_heads(chips, batches, normed_a, w_heads, 3)
    ahead = [(source, source + 1) for source in range(seqs - 1)]
    behind = [(source + 1, source) for source in range(seqs - 1)]
    tail = lax.ppermute(key_value[:, length - WINDOW :], "seq", ahead)
    kv_pad = jnp.concatenate([tail, key_value], axis=1)
    attended, lse = attend(query, kv_pad, low, block)
    branch = sum_products(chips, attended, wo_part, False, "branch", 4)
    middle = inputs + branch
    normed_b = to_half(normalize(middle, gain_two))
    group_b, gate, up, hidden = hidden_units(chips, normed_b, w_units, 5)
    d_hidden = dot_nt(group_d, wd_part)
    d_gate, d_up = gate_back(gate.astype(jnp.float32), up.astype(jnp.float32), d_hidden)
    d_units = jnp.concatenate([d_gate, d_up], axis=1)
    d_normed_b = sum_products(chips, d_units, w_units, True, "units_back", 6)
    mlp_out = lax.psum_scatter(
        to_half(dot_nn(hidden, wd_part)), "fsdp", scatter_dimension=0, tiled=True
    )
    outputs = middle + mlp_out.astype(jnp.float32)
    mlp_pull = jax.vjp(normalize, middle, gain_two)[1]
    d_middle_norm, gain_two_grad = mlp_pull(d_normed_b)
    d_middle = upstream + d_middle_norm
    d_branch = to_half(d_middle)

    def over_seq(values):
        return lax.psum_scatter(to_half(values), "seq", scatter_dimension=0, tiled=True)

    down_sum = over_seq(contract_rows(hidden, group_d))
    unit_sums = over_seq(contract_rows(group_b.reshape(group_rows, width), d_units))

    group_branch, d_attended = branch_back(chips, batches, d_branch, wo_part, 7)
    d_query, d_key_pad, d_value_pad = attend_back(query, kv_pad, low, lse, d_attended, block)
    back = lax.ppermute(
        to_half(jnp.concatenate([d_key_pad[:, :WINDOW], d_value_pad[:, :WINDOW]], axis=2)),
        "seq",
        behind,
    ).astype(jnp.float32)
    back = jnp.pad(back, ((0, 0), (length - WINDOW, 0), (0, 0)))
    d_heads = jnp.concatenate(
        [
            d_query,
            to_half(d_key_pad[:, WINDOW:] + back[:, :, :span]),
            to_half(d_value_pad[:, WINDOW:] + back[:, :, span:]),
        ],
        axis=2,
    )
    d_normed_a = sum_products(chips, d_heads, w_heads, True, "heads_back", 8)
    flat_a = group_a.reshape(group_rows, width)
    out_grad = contract_rows(
        attended.reshape(group_rows, span), group_branch.reshape(group_rows, width)
    )
    if aligned:
        out_sum = over_seq(out_grad)
    else:
        whole = lax.dynamic_update_slice_in_dim(
            jnp.zeros((width, width), jnp.bfloat16), to_half(out_grad), member * span, 0
        )
        out_sum = lax.psum_scatter(whole, ("seq", "fsdp"), scatter_dimension=0, tiled=True)
    head_sums = over_seq(contract_rows(flat_a, d_heads.reshape(group_rows, 3 * span)))
    head_cols, unit_cols = swap_blocks(
        group,
        [head_sums.reshape(group, share, -1), unit_sums.reshape(group, share, -1)],
        "weight_grads",
        9,
    )

    attn_pull = jax.vjp(normalize, inputs, gain_one)[1]
    d_input_norm, gain_one_grad = attn_pull(d_normed_a)
    input_grad = (d_middle + d_input_norm).reshape(batches, piece, width)
    layer_out = to_half(outputs).reshape(batches, piece, width)

    def lanes(values):
        return jnp.pad(values.reshape(devices, 1, share), ((0, 0), (0, 7), (0, 64 - share)))

    grad_tiles = jnp.concatenate([lanes(gain_one_grad), lanes(gain_two_grad)], axis=2)
    grad_sums = jnp.sum(swap_tiles(seqs, group, grad_tiles, False, "gain_grads", 10)[:, 0], axis=0)

    def whole_rows(cols, part, total):
        size = total // group
        return unblock(cols[:, :, part * size : (part + 1) * size], total).astype(jnp.float32)

    return (
        layer_out,
        input_grad,
        grad_sums[:share],
        whole_rows(head_cols, 0, width),
        whole_rows(head_cols, 1, width),
        whole_rows(head_cols, 2, width),
        out_sum.astype(jnp.float32),
        grad_sums[64 : 64 + share],
        whole_rows(unit_cols, 0, FF),
        whole_rows(unit_cols, 1, FF),
        down_sum.astype(jnp.float32),
    )


def solution(mesh):
    spread = ("seq", "fsdp")
    tokens, rows, gains = P(None, spread, None), P(spread, None), P(spread)
    in_specs = (tokens, tokens, P(), gains, rows, rows, rows, rows, gains, rows, rows, rows)
    out_specs = (tokens, tokens, gains, rows, rows, rows, rows, gains, rows, rows, rows)
    return jax.shard_map(body, mesh=mesh, in_specs=in_specs, out_specs=out_specs, check_vma=False)
```

```python
import functools

import jax
import jax.numpy as jnp
from jax import lax
from jax.experimental import pallas as pl
from jax.experimental.pallas import tpu as pltpu
from jax.sharding import PartitionSpec as P

HEAD = 64
FF = 8192
WINDOW = 1024
PAIR = 128
TILE = 512
LOW = -1e30
EPS = 1e-05
MESH = pl.DeviceIdType.MESH
MIB = 2**20


def to_half(values):
    return values.astype(jnp.bfloat16)


def normalize(values, gain):
    return values * lax.rsqrt(jnp.mean(values * values, axis=-1, keepdims=True) + EPS) * gain


def contract_rows(left, right):
    return lax.dot_general(
        left, right, (((0,), (0,)), ((), ())), preferred_element_type=jnp.float32
    )


def dot_nt(left, right):
    return lax.dot_general(
        left, right, (((1,), (1,)), ((), ())), preferred_element_type=jnp.float32
    )


def dot_nn(left, right):
    return jnp.dot(left, right, preferred_element_type=jnp.float32)


def gate_back(gate, up, d_hidden):
    sigma = jax.nn.sigmoid(gate)
    d_gate = d_hidden * up * sigma * (1.0 + gate * (1.0 - sigma))
    d_up = d_hidden * gate * sigma
    return (to_half(d_gate), to_half(d_up))


def head_lanes(values, half):
    lane = lax.broadcasted_iota(jnp.int32, values.shape, 1)
    return jnp.where((lane >= HEAD) == (half == 1), values, jnp.zeros_like(values))


def masked_scores(k_rows, q_head, low):
    keys, block = k_rows.shape[0], q_head.shape[0]
    scores = dot_nt(k_rows, q_head)
    at = lax.broadcasted_iota(jnp.int32, (keys, block), 0)
    query = lax.broadcasted_iota(jnp.int32, (keys, block), 1)
    seen = (at >= low) & (at <= query + WINDOW)
    return jnp.where(seen, scores, LOW)


class Line:
    def __init__(self, chips):
        self.chips = chips
        self.own = lax.axis_index("fsdp")
        self.chip = self.own // 2
        self.core = lax.rem(self.own, 2)
        self.other = self.own + 1 - 2 * self.core
        self.has_left = self.chip > 0
        self.has_right = self.chip < chips - 1

    def greet(self):
        signal_group(self.other)
        pl.when(self.has_left)(lambda: signal_group(self.own - 2))
        pl.when(self.has_right)(lambda: signal_group(self.own + 2))
        return 1 + self.has_left.astype(jnp.int32) + self.has_right.astype(jnp.int32)


def signal_group(peer):
    barrier = pltpu.get_barrier_semaphore()
    pl.semaphore_signal(barrier, inc=1, device_id={"fsdp": peer}, device_id_type=MESH)


def signal_seq(peer):
    barrier = pltpu.get_barrier_semaphore()
    pl.semaphore_signal(barrier, inc=1, device_id={"seq": peer}, device_id_type=MESH)


def greet_group(group):
    own = lax.axis_index("fsdp")
    pl.loop(1, group)(lambda ahead: signal_group(lax.rem(own + ahead, group)))
    return group - 1


def greet_seq(seqs):
    own = lax.axis_index("seq")
    pl.loop(1, seqs)(lambda ahead: signal_seq(lax.rem(own + ahead, seqs)))
    return seqs - 1


def meet(count):
    pl.semaphore_wait(pltpu.get_barrier_semaphore(), count)


def rows_at(index, size):
    return pl.ds(pl.multiple_of(index * size, size), size)


class Spread:
    def __init__(self, line, first, buf, send, recv):
        self.line, self.first, self.buf, self.send, self.recv = line, first, buf, send, recv

    def move(self, slot, way, peer, source=None):
        return pltpu.make_async_remote_copy(
            src_ref=self.buf.at[slot] if source is None else source,
            dst_ref=self.buf.at[slot],
            send_sem=self.send.at[way, slot],
            recv_sem=self.recv.at[slot],
            device_id={"fsdp": peer},
            device_id_type=MESH,
        )

    def begin(self):
        line = self.line
        pl.when(line.has_right)(lambda: self.move(line.own, 1, line.own + 2, self.first).start())
        pl.when(line.has_left)(lambda: self.move(line.own, 0, line.own - 2, self.first).start())
        self.move(line.own, 2, line.other, self.first).start()

    def relay(self, far):
        line = self.line

        @pl.when(line.chip - far >= 0)
        def _():
            slot = (line.chip - far) * 2 + line.core
            self.move(slot, 1, line.own).wait_recv()
            pl.when(line.has_right)(lambda: self.move(slot, 1, line.own + 2).start())
            self.move(slot, 2, line.other).start()

        @pl.when(line.chip + far < line.chips)
        def _():
            slot = (line.chip + far) * 2 + line.core
            self.move(slot, 0, line.own).wait_recv()
            pl.when(line.has_left)(lambda: self.move(slot, 0, line.own - 2).start())
            self.move(slot, 2, line.other).start()

    def each(self, far, use):
        line = self.line

        @pl.loop(0, 4)
        def _(turn):
            side = lax.rem(turn, 2)
            across = turn // 2
            away = far - across
            source = line.chip + away * (2 * side - 1)
            valid = (away >= 0) & (away < line.chips) & (source >= 0) & (source < line.chips)
            valid = valid & ((side == 0) | (away > 0))

            @pl.when(valid)
            def _():
                slot = source * 2 + line.core + across * (1 - 2 * line.core)
                pl.when(across == 1)(lambda: self.move(slot, 2, line.own).wait_recv())
                use(slot)

    def whole(self, use):
        @pl.loop(0, self.line.chips + 1)
        def _(far):
            pl.when(far > 0)(lambda: self.relay(far))
            self.each(far, use)

    def rest(self):
        pl.loop(0, self.line.chips)(
            lambda place: self.move(place * 2 + 1 - self.line.core, 2, self.line.own).wait_recv()
        )

    def sent(self):
        line = self.line

        @pl.loop(0, line.chips)
        def _(place):
            slot = place * 2 + line.core
            self.move(slot, 2, line.other).wait_send()
            pl.when(line.has_right & (place <= line.chip))(
                lambda: self.move(slot, 1, line.own + 2).wait_send()
            )
            pl.when(line.has_left & (place >= line.chip))(
                lambda: self.move(slot, 0, line.own - 2).wait_send()
            )


class Reduce:
    def __init__(self, line, product, out, acc, cross_out, line_out, cross_in, line_in, send, recv):
        self.line, self.product, self.out, self.acc = line, product, out, acc
        self.cross_out, self.line_out, self.cross_in, self.line_in = cross_out, line_out, cross_in, line_in
        self.send, self.recv = send, recv

    @staticmethod
    def scratch(chips, rows, width):
        part = pltpu.VMEM((chips, rows, width), jnp.bfloat16)
        return [
            pltpu.VMEM((rows, width), jnp.float32),
            part,
            part,
            part,
            pltpu.VMEM((chips + 1, rows, width), jnp.bfloat16),
            pltpu.SemaphoreType.DMA((2, chips)),
            pltpu.SemaphoreType.DMA((2, chips + 1)),
        ]

    def cross(self, place):
        return pltpu.make_async_remote_copy(
            src_ref=self.cross_out.at[place],
            dst_ref=self.cross_in.at[place],
            send_sem=self.send.at[0, place],
            recv_sem=self.recv.at[0, place],
            device_id={"fsdp": self.line.other},
            device_id_type=MESH,
        )

    def along(self, place, landing, peer):
        return pltpu.make_async_remote_copy(
            src_ref=self.line_out.at[place],
            dst_ref=self.line_in.at[landing],
            send_sem=self.send.at[1, place],
            recv_sem=self.recv.at[1, landing],
            device_id={"fsdp": peer},
            device_id_type=MESH,
        )

    def steps(self):
        return 2 * self.line.chips - 1

    def step(self, step):
        line, acc = self.line, self.acc
        tiles = acc.shape[1] // TILE
        away = line.chips - 1 - step // 2
        side = lax.rem(step, 2)
        place = line.chip + away * (1 - 2 * side)

        @pl.when((place >= 0) & (place < line.chips))
        def _():
            @pl.loop(0, tiles)
            def _(tile):
                got = self.product(place * 2 + 1 - line.core, tile)
                self.cross_out[place, :, rows_at(tile, TILE)] = to_half(got)

            self.cross(place).start()

            @pl.loop(0, tiles)
            def _(tile):
                acc[:, rows_at(tile, TILE)] = self.product(place * 2 + line.core, tile)

            self.cross(place).wait_recv()

            @pl.when(away > 0)
            def _():
                rightward = side == 0
                upstream = (rightward & line.has_left) | (jnp.logical_not(rightward) & line.has_right)

                @pl.when(upstream)
                def _():
                    self.along(place, place, line.own).wait_recv()
                    self.line_out[place] = to_half(
                        acc[...]
                        + self.cross_in[place].astype(jnp.float32)
                        + self.line_in[place].astype(jnp.float32)
                    )

                @pl.when(jnp.logical_not(upstream))
                def _():
                    self.line_out[place] = to_half(
                        acc[...] + self.cross_in[place].astype(jnp.float32)
                    )

                @pl.when(rightward)
                def _():
                    self.along(place, place, line.own + 2).start()

                @pl.when(jnp.logical_not(rightward))
                def _():
                    landing = jnp.where(away == 1, line.chips, place)
                    self.along(place, landing, line.own - 2).start()

            @pl.when(away == 0)
            def _():
                self.out[...] = acc[...] + self.cross_in[place].astype(jnp.float32)

                @pl.when(line.has_left)
                def _():
                    self.along(place, place, line.own).wait_recv()
                    self.out[...] += self.line_in[place].astype(jnp.float32)

                @pl.when(line.has_right)
                def _():
                    self.along(place, line.chips, line.own).wait_recv()
                    self.out[...] += self.line_in[line.chips].astype(jnp.float32)

    def sent(self):
        @pl.loop(0, self.line.chips)
        def _(place):
            self.cross(place).wait_send()
            pl.when(place != self.line.chip)(
                lambda: self.along(place, place, self.line.own).wait_send()
            )


class Swap:
    def __init__(self, group, source, target, send, recv, keep):
        self.group, self.source, self.target = group, source, target
        self.send, self.recv, self.keep = send, recv, keep
        self.own = lax.axis_index("fsdp")

    def move(self, peer, source):
        return pltpu.make_async_remote_copy(
            src_ref=self.source.at[peer],
            dst_ref=self.target.at[source],
            send_sem=self.send.at[peer],
            recv_sem=self.recv.at[source],
            device_id={"fsdp": peer},
            device_id_type=MESH,
        )

    def kept(self):
        return pltpu.make_async_copy(self.source.at[self.own], self.target.at[self.own], self.keep)

    def begin(self):
        self.kept().start()
        pl.loop(1, self.group)(
            lambda ahead: self.move(lax.rem(self.own + ahead, self.group), self.own).start()
        )

    def end(self):
        self.kept().wait()

        @pl.loop(1, self.group)
        def _(ahead):
            peer = lax.rem(self.own + ahead, self.group)
            self.move(peer, peer).wait_recv()
            self.move(peer, self.own).wait_send()


class Share:
    def __init__(self, seqs, source, target, send, recv, keep):
        self.seqs, self.source, self.target = seqs, source, target
        self.send, self.recv, self.keep = send, recv, keep
        self.own = lax.axis_index("seq")

    def move(self, peer, place):
        return pltpu.make_async_remote_copy(
            src_ref=self.source,
            dst_ref=self.target.at[place],
            send_sem=self.send.at[peer],
            recv_sem=self.recv.at[place],
            device_id={"seq": peer},
            device_id_type=MESH,
        )

    def kept(self):
        return pltpu.make_async_copy(self.source, self.target.at[self.own], self.keep)

    def begin(self):
        self.kept().start()
        pl.loop(1, self.seqs)(
            lambda ahead: self.move(lax.rem(self.own + ahead, self.seqs), self.own).start()
        )

    def end(self):
        self.kept().wait()

        @pl.loop(1, self.seqs)
        def _(ahead):
            peer = lax.rem(self.own + ahead, self.seqs)
            self.move(peer, peer).wait_recv()
            self.move(peer, self.own).wait_send()


VMEM_SPEC = pl.BlockSpec(memory_space=pltpu.VMEM)
ANY_SPEC = pl.BlockSpec(memory_space=pl.ANY)


def comm_params(collective, mib=58):
    return pltpu.CompilerParams(
        collective_id=collective, has_side_effects=True, vmem_limit_bytes=mib * MIB
    )


def cost(flops, local, remote):
    return pl.CostEstimate(
        flops=flops, bytes_accessed=local, transcendentals=0, remote_bytes_transferred=remote
    )


def sems(*shape):
    return pltpu.SemaphoreType.DMA(shape)


def start_kernel(
    seqs, chips, batches, tile_ref, x_ref, blocks_ref, g_ref, q_ref, kv_ref, gains_ref, w_out_ref,
    buf, normed, gain, gains, w, send, recv, keep, swap_send, share_send, w_recv,
    tile_send, tile_across, tile_recv, tile_back, w_keep, gain_keep,
):
    line = Line(chips)
    group = 2 * chips
    seq = lax.axis_index("seq")
    own = line.own
    share = blocks_ref.shape[1]
    piece = x_ref.shape[0] // batches
    span = q_ref.shape[2]
    width = x_ref.shape[1]
    per = 128 * seqs * group // width
    meet(greet_group(group) + greet_seq(seqs))

    def block_at(run, member):
        return w.at[rows_at(run * group + member, share)]

    def block_swap(peer, member):
        return pltpu.make_async_remote_copy(
            src_ref=blocks_ref.at[peer],
            dst_ref=block_at(seq, member),
            send_sem=swap_send.at[peer],
            recv_sem=w_recv.at[seq, member],
            device_id={"fsdp": peer},
            device_id_type=MESH,
        )

    def block_share(run, member, peer):
        return pltpu.make_async_remote_copy(
            src_ref=block_at(run, member),
            dst_ref=block_at(run, member),
            send_sem=share_send.at[peer, member],
            recv_sem=w_recv.at[run, member],
            device_id={"seq": peer},
            device_id_type=MESH,
        )

    def tile_to_seq(peer, place):
        return pltpu.make_async_remote_copy(
            src_ref=tile_ref.at[0],
            dst_ref=gains.at[own, place],
            send_sem=tile_send.at[peer],
            recv_sem=tile_recv.at[place],
            device_id={"seq": peer},
            device_id_type=MESH,
        )

    def tiles_to_group(peer, member):
        return pltpu.make_async_remote_copy(
            src_ref=gains.at[member],
            dst_ref=gains.at[member],
            send_sem=tile_across.at[peer],
            recv_sem=tile_back.at[member],
            device_id={"fsdp": peer},
            device_id_type=MESH,
        )

    def others(count, me, act):
        pl.loop(1, count)(lambda ahead: act(lax.rem(me + ahead, count)))

    others(seqs, seq, lambda peer: tile_to_seq(peer, seq).start())
    others(group, own, lambda peer: block_swap(peer, own).start())
    spread = Spread(line, x_ref, buf, send, recv)
    spread.begin()
    gains[own, seq] = tile_ref[0]
    w[rows_at(seq * group + own, share), :] = blocks_ref[own]
    others(seqs, seq, lambda peer: block_share(seq, own, peer).start())
    buf[own] = x_ref[...]
    others(seqs, seq, lambda peer: tile_to_seq(peer, peer).wait_recv())
    others(group, own, lambda peer: tiles_to_group(peer, own).start())

    def pass_block(member):
        block_swap(member, member).wait_recv()
        others(seqs, seq, lambda peer: block_share(seq, member, peer).start())

    others(group, own, pass_block)
    others(group, own, lambda peer: tiles_to_group(peer, peer).wait_recv())
    for column in range(width // 128):
        total = 0.0
        for place in range(column * per, (column + 1) * per):
            total = total + gains[place % group, place // group, 0:1, :]
        gain[0:1, column * 128 : (column + 1) * 128] = total

    def kept(slot, batch):
        return pltpu.make_async_copy(
            normed.at[slot, pl.ds(batch * piece, piece)],
            g_ref.at[batch, rows_at(slot, piece)],
            keep.at[slot, batch],
        )

    def use(slot):
        @pl.loop(0, x_ref.shape[0] // 16)
        def _(chunk):
            rows = rows_at(chunk, 16)
            values = buf[slot, rows, :].astype(jnp.float32)
            normed[slot, rows, :] = to_half(normalize(values, gain[0:1, :]))

        for batch in range(batches):
            kept(slot, batch).start()
        rows = rows_at(slot, piece)
        values = normed[slot]
        for part in range(3):
            got = to_half(dot_nn(values, w[:, part * span : (part + 1) * span]))
            for batch in range(batches):
                mine = got[batch * piece : (batch + 1) * piece]
                if part == 0:
                    q_ref[batch, rows, :] = mine
                else:
                    kv_ref[batch, rows, (part - 1) * span : part * span] = mine

    pl.loop(1, chips - 1)(spread.relay)

    def have_block(run, member):
        block_share(run, member, seq).wait_recv()

    others(seqs, seq, lambda run: pl.loop(0, group)(lambda member: have_block(run, member)))
    w_kept = pltpu.make_async_copy(w, w_out_ref, w_keep)
    w_kept.start()
    gains_kept = pltpu.make_async_copy(gains, gains_ref, gain_keep)
    gains_kept.start()

    pl.loop(0, chips - 1)(lambda far: spread.each(far, use))
    spread.relay(chips - 1)
    spread.each(chips - 1, use)
    spread.each(chips, use)
    spread.sent()
    others(seqs, seq, lambda peer: tile_to_seq(peer, seq).wait_send())
    others(group, own, lambda peer: block_swap(peer, own).wait_send())
    others(group, own, lambda peer: tiles_to_group(peer, own).wait_send())
    others(
        seqs,
        seq,
        lambda peer: pl.loop(0, group)(lambda member: block_share(seq, member, peer).wait_send()),
    )
    w_kept.wait()
    gains_kept.wait()

    @pl.loop(0, group)
    def _(slot):
        for batch in range(batches):
            kept(slot, batch).wait()


def start(seqs, chips, batches, tile, x, blocks, collective):
    rows, width = x.shape
    group = 2 * chips
    length = group * rows // batches
    share, cols = blocks.shape[1:]
    span = cols // 3
    half = jnp.bfloat16
    return pl.pallas_call(
        functools.partial(start_kernel, seqs, chips, batches),
        out_shape=[
            jax.ShapeDtypeStruct((batches, length, width), half),
            jax.ShapeDtypeStruct((batches, length, span), half),
            jax.ShapeDtypeStruct((batches, length, 2 * span), half),
            jax.ShapeDtypeStruct((group, seqs, 8, 128), jnp.float32),
            jax.ShapeDtypeStruct((width, cols), half),
        ],
        in_specs=[VMEM_SPEC] * 3,
        out_specs=[ANY_SPEC, VMEM_SPEC, VMEM_SPEC, ANY_SPEC, ANY_SPEC],
        scratch_shapes=[
            pltpu.VMEM((group, rows, width), half),
            pltpu.VMEM((group, rows, width), half),
            pltpu.VMEM((8, width), jnp.float32),
            pltpu.VMEM((group, seqs, 8, 128), jnp.float32),
            pltpu.VMEM((width, cols), half),
            sems(3, group),
            sems(group),
            sems(group, batches),
            sems(group),
            sems(seqs, group),
            sems(seqs, group),
            sems(seqs),
            sems(group),
            sems(seqs),
            sems(group),
            pltpu.SemaphoreType.DMA,
            pltpu.SemaphoreType.DMA,
        ],
        compiler_params=comm_params(collective),
        cost_estimate=cost(2 * group * rows * width * cols, 200 * MIB, group * rows * width * 2),
        name="start",
    )(tile, x, blocks)


def attend_kernel(
    seqs, group, block, q_ref, kv_ref, low_ref, units_ref, out_ref, lse_ref, pad_ref, own_units_ref,
    pad, vt, halo_send, halo_recv, pad_keep, swap_send, swap_recv, swap_keep,
):
    seq = lax.axis_index("seq")
    batches, length, span = q_ref.shape
    has_left, has_right = seq > 0, seq < seqs - 1
    pl.when(has_left)(lambda: signal_seq(seq - 1))
    pl.when(has_right)(lambda: signal_seq(seq + 1))
    meet(greet_group(group) + has_left.astype(jnp.int32) + has_right.astype(jnp.int32))

    def halo(batch, peer):
        return pltpu.make_async_remote_copy(
            src_ref=kv_ref.at[batch, pl.ds(length - WINDOW, WINDOW)],
            dst_ref=pad.at[batch, pl.ds(0, WINDOW)],
            send_sem=halo_send.at[batch],
            recv_sem=halo_recv.at[batch],
            device_id={"seq": peer},
            device_id_type=MESH,
        )

    for batch in range(batches):
        pl.when(has_right)(lambda batch=batch: halo(batch, seq + 1).start())
    swap = Swap(group, units_ref, own_units_ref, swap_send, swap_recv, swap_keep)
    swap.begin()
    pad[:, WINDOW:, :] = kv_ref[...]

    @pl.when(jnp.logical_not(has_left))
    def _():
        pad[:, :WINDOW, :] = jnp.zeros((batches, WINDOW, 2 * span), jnp.bfloat16)

    def kept(batch):
        return pltpu.make_async_copy(pad.at[batch], pad_ref.at[batch], pad_keep.at[batch])

    for batch in range(batches):
        pl.when(has_left)(lambda batch=batch: halo(batch, seq).wait_recv())
        kept(batch).start()
        vt[...] = pad[batch, :, span:].T

        @pl.loop(0, length // block)
        def _(step, batch=batch):
            begin = pl.multiple_of(step * block, block)
            keys = pl.ds(begin, block + WINDOW)
            rows = pl.ds(begin, block)
            low = low_ref[batch, :, rows]
            for pair in range(span // PAIR):
                lanes = slice(pair * PAIR, (pair + 1) * PAIR)
                q_pair = q_ref[batch, rows, lanes] * jnp.asarray(HEAD**-0.5, jnp.bfloat16)
                k_rows = pad[batch, keys, lanes]
                values = vt[lanes, keys]
                mixed = []
                for half in range(2):
                    scores = masked_scores(k_rows, head_lanes(q_pair, half), low)
                    top = jnp.max(scores, axis=0, keepdims=True)
                    expo = jnp.exp(scores - top)
                    total = jnp.sum(expo, axis=0, keepdims=True)
                    mixed.append(dot_nn(values, to_half(expo)) / total)
                    row = pair * 2 + half
                    lse_ref[batch, row : row + 1, rows] = top + jnp.log(total)
                lane = lax.broadcasted_iota(jnp.int32, mixed[0].shape, 0)
                out_ref[batch, rows, lanes] = to_half(jnp.where(lane < HEAD, mixed[0], mixed[1]).T)

    for batch in range(batches):
        kept(batch).wait()
        pl.when(has_right)(lambda batch=batch: halo(batch, seq + 1).wait_send())
    swap.end()


def attend(seqs, group, query, key_value, low, block, units, collective):
    batches, length, span = query.shape
    padded = length + WINDOW
    heads = span // HEAD
    half = jnp.bfloat16
    return pl.pallas_call(
        functools.partial(attend_kernel, seqs, group, block),
        in_specs=[VMEM_SPEC, VMEM_SPEC, VMEM_SPEC, ANY_SPEC],
        out_specs=[VMEM_SPEC, VMEM_SPEC, ANY_SPEC, ANY_SPEC],
        out_shape=[
            jax.ShapeDtypeStruct((batches, length, span), half),
            jax.ShapeDtypeStruct((batches, heads, length), jnp.float32),
            jax.ShapeDtypeStruct((batches, padded, 2 * span), half),
            jax.ShapeDtypeStruct(units.shape, half),
        ],
        scratch_shapes=[
            pltpu.VMEM((batches, padded, 2 * span), half),
            pltpu.VMEM((span, padded), half),
            sems(batches),
            sems(batches),
            sems(batches),
            sems(group),
            sems(group),
            pltpu.SemaphoreType.DMA,
        ],
        compiler_params=comm_params(collective),
        cost_estimate=cost(
            8 * batches * length * span * (WINDOW + block), 150 * MIB, units.size * 2
        ),
        name="attend",
    )(query, key_value, low, units)


def left_rows(a_ref, slot, rows):
    if len(a_ref.shape) == 2:
        return a_ref[rows_at(slot, rows), :]
    piece = rows // a_ref.shape[0]
    return jnp.concatenate(
        [a_ref[batch, rows_at(slot, piece), :] for batch in range(a_ref.shape[0])], axis=0
    )


def branch_kernel(
    seqs, chips, a_ref, w_ref, d_ref, units_ref, out_ref, gd_ref, w_units_ref,
    acc, cross_out, line_out, cross_in, line_in, sum_send, sum_recv,
    send, recv, d_keep, share_send, share_recv, share_keep,
):
    line = Line(chips)
    rows = out_ref.shape[0]

    def product(slot, tile):
        return dot_nn(left_rows(a_ref, slot, rows), w_ref[:, rows_at(tile, TILE)])

    meet(line.greet() + greet_seq(seqs))
    reduce = Reduce(
        line, product, out_ref, acc, cross_out, line_out, cross_in, line_in, sum_send, sum_recv
    )
    spread = Spread(line, d_ref, gd_ref, send, recv)
    units = Share(seqs, units_ref, w_units_ref, share_send, share_recv, share_keep)
    d_kept = pltpu.make_async_copy(d_ref, gd_ref.at[line.own], d_keep)
    units.begin()
    spread.begin()
    d_kept.start()

    @pl.loop(0, reduce.steps())
    def _(step):
        reduce.step(step)
        pl.when(lax.rem(step, 2) == 1)(lambda: spread.relay((step + 1) // 2))

    spread.rest()
    spread.sent()
    reduce.sent()
    d_kept.wait()
    units.end()


def branch_sum(seqs, chips, a, w, d_rows, units, collective):
    rows, width = d_rows.shape
    group = 2 * chips
    half = jnp.bfloat16
    return pl.pallas_call(
        functools.partial(branch_kernel, seqs, chips),
        out_shape=[
            jax.ShapeDtypeStruct((rows, width), jnp.float32),
            jax.ShapeDtypeStruct((group, rows, width), half),
            jax.ShapeDtypeStruct((seqs,) + units.shape, half),
        ],
        in_specs=[VMEM_SPEC, VMEM_SPEC, ANY_SPEC, ANY_SPEC],
        out_specs=[VMEM_SPEC, ANY_SPEC, ANY_SPEC],
        scratch_shapes=Reduce.scratch(chips, rows, width)
        + [sems(3, group), sems(group), pltpu.SemaphoreType.DMA]
        + [sems(seqs), sems(seqs), pltpu.SemaphoreType.DMA],
        compiler_params=comm_params(collective),
        cost_estimate=cost(
            2 * group * rows * width * w.shape[0], 250 * MIB, 3 * group * rows * width * 2
        ),
        name="branch_sum",
    )(a, w, d_rows, units)


def units_kernel(
    chips, x_ref, w_ref, wd_ref, gd_ref, g_ref, hidden_ref, d_ref, buf, d_buf, send, recv, keep, d_sem
):
    line = Line(chips)
    rows = x_ref.shape[0]
    units = hidden_ref.shape[1]
    part = min(units, 256)
    meet(line.greet())
    spread = Spread(line, x_ref, buf, send, recv)
    spread.begin()
    buf[line.own] = x_ref[...]

    def kept(slot):
        return pltpu.make_async_copy(buf.at[slot], g_ref.at[slot], keep.at[slot])

    def use(slot):
        kept(slot).start()
        fetch = pltpu.make_async_copy(gd_ref.at[slot], d_buf, d_sem)
        fetch.start()
        fetch.wait()
        place = rows_at(slot, rows)

        @pl.loop(0, units // part)
        def _(tile):
            here = rows_at(tile, part)
            there = rows_at(units // part + tile, part)
            values = buf[slot]
            gate = dot_nn(values, w_ref[:, here])
            up = dot_nn(values, w_ref[:, there])
            d_hidden = dot_nt(d_buf[...], wd_ref[here, :])
            sigma = jax.nn.sigmoid(gate)
            swish = gate * sigma
            hidden_ref[place, here] = to_half(swish * up)
            d_ref[place, here] = to_half(d_hidden * up * sigma * (1.0 + gate * (1.0 - sigma)))
            d_ref[place, there] = to_half(d_hidden * swish)

    spread.whole(use)
    spread.sent()
    pl.loop(0, 2 * chips)(lambda slot: kept(slot).wait())


def hidden_units(chips, x, w, wd, group_d, collective):
    rows, width = x.shape
    group = 2 * chips
    units = wd.shape[0]
    half = jnp.bfloat16
    return pl.pallas_call(
        functools.partial(units_kernel, chips),
        out_shape=[
            jax.ShapeDtypeStruct((group, rows, width), half),
            jax.ShapeDtypeStruct((group * rows, units), half),
            jax.ShapeDtypeStruct((group * rows, 2 * units), half),
        ],
        in_specs=[VMEM_SPEC, VMEM_SPEC, VMEM_SPEC, ANY_SPEC],
        out_specs=[ANY_SPEC, VMEM_SPEC, VMEM_SPEC],
        scratch_shapes=[
            pltpu.VMEM((group, rows, width), half),
            pltpu.VMEM((rows, width), half),
            sems(3, group),
            sems(group),
            sems(group),
            pltpu.SemaphoreType.DMA,
        ],
        compiler_params=comm_params(collective),
        cost_estimate=cost(
            6 * group * rows * width * units, 200 * MIB, group * rows * width * 2
        ),
        name="hidden_units",
    )(x, w, wd, group_d)


def branch_back_kernel(
    chips, batches, x_ref, w_ref, hidden_ref, wd_ref, g_ref, d_ref, out_ref,
    acc, cross_out, line_out, cross_in, line_in, sum_send, sum_recv, buf, send, recv, keep,
):
    line = Line(chips)
    rows = x_ref.shape[0]
    piece = rows // batches

    def product(slot, tile):
        return dot_nn(left_rows(hidden_ref, slot, rows), wd_ref[:, rows_at(tile, TILE)])

    meet(line.greet())
    spread = Spread(line, x_ref, buf, send, recv)
    reduce = Reduce(
        line, product, out_ref, acc, cross_out, line_out, cross_in, line_in, sum_send, sum_recv
    )
    spread.begin()
    buf[line.own] = x_ref[...]

    def kept(slot, batch):
        return pltpu.make_async_copy(
            buf.at[slot, pl.ds(batch * piece, piece)],
            g_ref.at[batch, rows_at(slot, piece)],
            keep.at[slot, batch],
        )

    def use(slot):
        for batch in range(batches):
            kept(slot, batch).start()
        got = to_half(dot_nt(buf[slot], w_ref[...]))
        for batch in range(batches):
            d_ref[batch, rows_at(slot, piece), :] = got[batch * piece : (batch + 1) * piece]

    @pl.loop(0, reduce.steps())
    def _(step):
        reduce.step(step)

        @pl.when(lax.rem(step, 2) == 1)
        def _():
            far = (step + 1) // 2
            spread.relay(far)
            spread.each(far - 1, use)

    spread.each(chips - 1, use)
    spread.each(chips, use)
    spread.sent()
    reduce.sent()

    @pl.loop(0, 2 * chips)
    def _(slot):
        for batch in range(batches):
            kept(slot, batch).wait()


def branch_back(chips, batches, x, w, hidden, wd, collective):
    rows, width = x.shape
    group = 2 * chips
    length = group * rows // batches
    span = w.shape[0]
    half = jnp.bfloat16
    return pl.pallas_call(
        functools.partial(branch_back_kernel, chips, batches),
        out_shape=[
            jax.ShapeDtypeStruct((batches, length, width), half),
            jax.ShapeDtypeStruct((batches, length, span), half),
            jax.ShapeDtypeStruct((rows, width), jnp.float32),
        ],
        in_specs=[VMEM_SPEC] * 4,
        out_specs=[ANY_SPEC, VMEM_SPEC, VMEM_SPEC],
        scratch_shapes=Reduce.scratch(chips, rows, width)
        + [
            pltpu.VMEM((group, rows, width), half),
            sems(3, group),
            sems(group),
            sems(group, batches),
        ],
        compiler_params=comm_params(collective, 62),
        cost_estimate=cost(
            2 * group * rows * width * (span + wd.shape[0]), 250 * MIB, 2 * group * rows * width * 2
        ),
        name="branch_back",
    )(x, w, hidden, wd)


def sum_kernel(chips, a_ref, w_ref, out_ref, *scratch):
    line = Line(chips)
    rows = out_ref.shape[0]

    def product(slot, tile):
        return dot_nt(left_rows(a_ref, slot, rows), w_ref[rows_at(tile, TILE), :])

    meet(line.greet())
    reduce = Reduce(line, product, out_ref, *scratch)
    pl.loop(0, reduce.steps())(reduce.step)
    reduce.sent()


def sum_products(chips, a, w, name, collective):
    group = 2 * chips
    width, depth = w.shape
    rows = a.size // depth // group
    return pl.pallas_call(
        functools.partial(sum_kernel, chips),
        out_shape=jax.ShapeDtypeStruct((rows, width), jnp.float32),
        in_specs=[VMEM_SPEC, VMEM_SPEC],
        out_specs=VMEM_SPEC,
        scratch_shapes=Reduce.scratch(chips, rows, width),
        compiler_params=comm_params(collective),
        cost_estimate=cost(2 * group * rows * width * depth, 200 * MIB, group * rows * width * 2),
        name=name,
    )(a, w)


def swap_kernel(group, count, *refs):
    sources, targets = refs[:count], refs[count : 2 * count]
    send, recv, keep = refs[2 * count :]
    meet(greet_group(group))
    swaps = [
        Swap(group, sources[item], targets[item], send.at[item], recv.at[item], keep.at[item])
        for item in range(count)
    ]
    for item in swaps:
        item.begin()
    for item in swaps:
        item.end()


def swap_blocks(group, arrays, name, collective):
    count = len(arrays)
    return pl.pallas_call(
        functools.partial(swap_kernel, group, count),
        out_shape=[jax.ShapeDtypeStruct(item.shape, item.dtype) for item in arrays],
        in_specs=[ANY_SPEC] * count,
        out_specs=[ANY_SPEC] * count,
        scratch_shapes=[sems(count, group), sems(count, group), sems(count)],
        compiler_params=comm_params(collective, 16),
        cost_estimate=cost(0, 150 * MIB, sum(item.size * 2 for item in arrays)),
        name=name,
    )(*arrays)


def tiles_kernel(seqs, group, x_ref, out_ref, send, recv):
    devices = seqs * group
    own = lax.axis_index("seq") * group + lax.axis_index("fsdp")
    barrier = pltpu.get_barrier_semaphore()

    def place(peer):
        return {"seq": peer // group, "fsdp": lax.rem(peer, group)}

    @pl.loop(1, devices)
    def _(ahead):
        peer = lax.rem(own + ahead, devices)
        pl.semaphore_signal(barrier, inc=1, device_id=place(peer), device_id_type=MESH)

    meet(devices - 1)
    out_ref[own] = x_ref[own]

    def move(peer, source):
        return pltpu.make_async_remote_copy(
            src_ref=x_ref.at[peer],
            dst_ref=out_ref.at[source],
            send_sem=send.at[peer],
            recv_sem=recv.at[source],
            device_id=place(peer),
            device_id_type=MESH,
        )

    pl.loop(1, devices)(lambda ahead: move(lax.rem(own + ahead, devices), own).start())

    @pl.loop(1, devices)
    def _(ahead):
        peer = lax.rem(own + ahead, devices)
        move(peer, peer).wait_recv()
        move(peer, own).wait_send()


def swap_tiles(seqs, group, x, name, collective):
    devices = seqs * group
    return pl.pallas_call(
        functools.partial(tiles_kernel, seqs, group),
        out_shape=jax.ShapeDtypeStruct((devices, 8, 128), jnp.float32),
        in_specs=[VMEM_SPEC],
        out_specs=VMEM_SPEC,
        scratch_shapes=[sems(devices), sems(devices)],
        compiler_params=comm_params(collective, 16),
        name=name,
    )(x)


def attend_back_kernel(
    block, q_ref, k_ref, v_ref, low_ref, lse_ref, d_ref, dq_ref, dk_ref, dv_ref, kt_ref
):
    step = pl.program_id(1)
    span = q_ref.shape[2]
    scale = jnp.asarray(HEAD**-0.5, jnp.bfloat16)

    @pl.when(step == 0)
    def _():
        kt_ref[...] = k_ref[0].T * scale
        dk_ref[...] = jnp.zeros_like(dk_ref)
        dv_ref[...] = jnp.zeros_like(dv_ref)

    begin = pl.multiple_of(step * block, block)
    keys = pl.ds(begin, block + WINDOW)
    low = low_ref[0]
    for pair in range(span // PAIR):
        lanes = slice(pair * PAIR, (pair + 1) * PAIR)
        q_pair = q_ref[0, :, lanes] * scale
        d_pair = d_ref[0, :, lanes]
        k_rows = k_ref[0, keys, lanes]
        v_rows = v_ref[0, keys, lanes]
        kt = kt_ref[lanes, keys]
        back = []
        for half in range(2):
            row = pair * 2 + half
            q_head = head_lanes(q_pair, half)
            d_head = head_lanes(d_pair, half)
            scores = masked_scores(k_rows, q_head, low)
            probs = jnp.exp(scores - lse_ref[0, row : row + 1, :])
            d_probs = dot_nt(v_rows, d_head)
            along = jnp.sum(probs * d_probs, axis=0, keepdims=True)
            d_scores = (probs * (d_probs - along)).astype(jnp.bfloat16)
            dv_ref[0, keys, lanes] += dot_nn(probs.astype(jnp.bfloat16), d_head)
            dk_ref[0, keys, lanes] += dot_nn(d_scores, q_head)
            back.append(dot_nn(kt, d_scores))
        at = lax.broadcasted_iota(jnp.int32, back[0].shape, 0)
        dq_ref[0, :, lanes] = jnp.where(at < HEAD, back[0], back[1]).T.astype(jnp.bfloat16)


def attend_back(query, kv_pad, low, lse, d_att, block):
    batches, length, span = query.shape
    padded = kv_pad.shape[1]
    heads = span // HEAD
    rows = pl.BlockSpec((1, block, span), lambda b, i: (b, i, 0))
    whole = pl.BlockSpec((1, padded, span), lambda b, i: (b, 0, 0))
    return pl.pallas_call(
        functools.partial(attend_back_kernel, block),
        grid=(batches, length // block),
        in_specs=[
            rows,
            whole,
            pl.BlockSpec((1, padded, span), lambda b, i: (b, 0, 1)),
            pl.BlockSpec((1, 1, block), lambda b, i: (b, 0, i)),
            pl.BlockSpec((1, heads, block), lambda b, i: (b, 0, i)),
            rows,
        ],
        out_specs=[rows, whole, whole],
        out_shape=[
            jax.ShapeDtypeStruct((batches, length, span), jnp.bfloat16),
            jax.ShapeDtypeStruct((batches, padded, span), jnp.float32),
            jax.ShapeDtypeStruct((batches, padded, span), jnp.float32),
        ],
        scratch_shapes=[pltpu.VMEM((span, padded), jnp.bfloat16)],
        compiler_params=pltpu.CompilerParams(vmem_limit_bytes=48 * 2**20),
        name="attend_back",
    )(query, kv_pad, kv_pad, low, lse, d_att)


def doc_starts(lengths, positions, batches, seq_len):
    table = lengths.reshape(batches, -1, lengths.shape[1])
    starts = jnp.cumsum(table, axis=2) - table
    per_batch = seq_len // table.shape[1]
    begins = (starts + (jnp.arange(table.shape[1], dtype=jnp.int32) * per_batch)[None, :, None]).reshape(
        batches, -1
    )
    before = begins[:, None, :] <= positions[None, :, None]
    return jnp.max(jnp.where(before, begins[:, None, :], 0), axis=2)


def body(
    tokens,
    cotangent,
    lengths,
    gain_attn,
    w_query,
    w_key,
    w_value,
    w_out,
    gain_mlp,
    w_gate,
    w_up,
    w_down,
):
    batches, piece, width = tokens.shape
    seqs = lax.axis_size("seq")
    group = lax.axis_size("fsdp")
    chips = group // 2
    devices = seqs * group
    seq_len = piece * devices
    rows = batches * piece
    share = w_query.shape[0]
    span = width // group
    length = group * piece
    group_rows = group * rows
    units = FF // group
    aligned = share == HEAD
    member = lax.axis_index("fsdp")

    def blocks(weight):
        part = weight.shape[1] // devices
        if part < HEAD:
            return weight.reshape(share, group, -1).transpose(1, 0, 2)
        return weight.reshape(share, seqs, group, part).transpose(2, 0, 1, 3).reshape(group, share, -1)

    def unblock(cols, total):
        part = total // devices
        if part < HEAD:
            return cols.transpose(1, 0, 2).reshape(share, total)
        return cols.reshape(group, share, seqs, part).transpose(1, 2, 0, 3).reshape(share, total)

    inputs = tokens.astype(jnp.float32).reshape(rows, width)
    upstream = cotangent.astype(jnp.float32).reshape(rows, width)
    wd_part = lax.all_gather(w_down, "seq", axis=0, tiled=True)
    if aligned:
        wo_part = lax.all_gather(w_out, "seq", axis=0, tiled=True)
    else:
        wo_all = lax.all_gather(w_out, ("seq", "fsdp"), axis=0, tiled=True)
        wo_part = lax.dynamic_slice_in_dim(wo_all, member * span, span, 0)

    attn_blocks = jnp.concatenate([blocks(w_query), blocks(w_key), blocks(w_value)], axis=2)
    unit_blocks = jnp.concatenate([blocks(w_gate), blocks(w_up)], axis=2)
    group_start = lax.axis_index("seq") * length
    positions = group_start + jnp.arange(length, dtype=jnp.int32)
    begins = doc_starts(lengths, positions, batches, seq_len)
    at = jnp.arange(length, dtype=jnp.int32)
    block = min(256, length)
    low = jnp.maximum(begins - group_start + WINDOW, at[None, :] + 1) - (at // block * block)[None, :]
    low = low[:, None, :]

    lane = jnp.arange(128, dtype=jnp.int32)
    device = lax.axis_index("seq") * group + member
    fold = 128 // share
    here = lane // share == lax.rem(device, fold)
    both = jnp.stack([gain_attn, gain_mlp]).astype(jnp.float32)
    tile = jnp.where(here[None], jnp.tile(both, (1, fold)), 0.0)
    tile = jnp.pad(tile, ((0, 6), (0, 0)))[None]
    group_a, query, key_value, gains, w_heads = start(
        seqs, chips, batches, tile, tokens.reshape(rows, width), attn_blocks, 1
    )
    gains = gains.transpose(1, 0, 2, 3).reshape(devices // fold, fold, 8, 128).sum(axis=1)
    gain_one = gains[:, 0].reshape(width)
    gain_two = gains[:, 1].reshape(width)
    attended, lse, kv_pad, unit_own = attend(
        seqs, group, query, key_value, low, block, unit_blocks, 2
    )
    branch, group_d, w_units = branch_sum(
        seqs, chips, attended, wo_part, cotangent.reshape(rows, width),
        unit_own.reshape(group * share, -1), 3,
    )
    w_units = w_units.reshape(width, -1)
    middle = inputs + branch
    normed_b = to_half(normalize(middle, gain_two))
    group_b, hidden, d_units = hidden_units(chips, normed_b, w_units, wd_part, group_d, 4)
    group_d = group_d.reshape(group_rows, width)
    d_normed_b = sum_products(chips, d_units, w_units, "units_back", 5)
    mlp_pull = jax.vjp(normalize, middle, gain_two)[1]
    d_middle_norm, gain_two_grad = mlp_pull(d_normed_b)
    d_middle = upstream + d_middle_norm
    d_branch = to_half(d_middle)

    def over_seq(values):
        return lax.psum_scatter(to_half(values), "seq", scatter_dimension=0, tiled=True)

    down_sum = over_seq(contract_rows(hidden, group_d))
    unit_sums = over_seq(contract_rows(group_b.reshape(group_rows, width), d_units))

    group_branch, d_attended, mlp_out = branch_back(
        chips, batches, d_branch, wo_part, hidden, wd_part, 6
    )
    outputs = middle + mlp_out
    d_query, d_key_pad, d_value_pad = attend_back(query, kv_pad, low, lse, d_attended, block)
    behind = [(source + 1, source) for source in range(seqs - 1)]
    back = lax.ppermute(
        to_half(jnp.concatenate([d_key_pad[:, :WINDOW], d_value_pad[:, :WINDOW]], axis=2)),
        "seq",
        behind,
    ).astype(jnp.float32)
    back = jnp.pad(back, ((0, 0), (length - WINDOW, 0), (0, 0)))
    d_heads = jnp.concatenate(
        [
            d_query,
            to_half(d_key_pad[:, WINDOW:] + back[:, :, :span]),
            to_half(d_value_pad[:, WINDOW:] + back[:, :, span:]),
        ],
        axis=2,
    )
    d_normed_a = sum_products(chips, d_heads, w_heads, "heads_back", 7)
    flat_a = group_a.reshape(group_rows, width)
    out_grad = contract_rows(
        attended.reshape(group_rows, span), group_branch.reshape(group_rows, width)
    )
    if aligned:
        out_sum = over_seq(out_grad)
    else:
        whole = lax.dynamic_update_slice_in_dim(
            jnp.zeros((width, width), jnp.bfloat16), to_half(out_grad), member * span, 0
        )
        out_sum = lax.psum_scatter(whole, ("seq", "fsdp"), scatter_dimension=0, tiled=True)
    head_sums = over_seq(contract_rows(flat_a, d_heads.reshape(group_rows, 3 * span)))
    head_cols, unit_cols = swap_blocks(
        group,
        [head_sums.reshape(group, share, -1), unit_sums.reshape(group, share, -1)],
        "weight_grads",
        8,
    )

    attn_pull = jax.vjp(normalize, inputs, gain_one)[1]
    d_input_norm, gain_one_grad = attn_pull(d_normed_a)
    input_grad = (d_middle + d_input_norm).reshape(batches, piece, width)
    layer_out = to_half(outputs).reshape(batches, piece, width)

    def lanes(values):
        return jnp.pad(values.reshape(devices, 1, share), ((0, 0), (0, 7), (0, 64 - share)))

    grad_tiles = jnp.concatenate([lanes(gain_one_grad), lanes(gain_two_grad)], axis=2)
    grad_sums = jnp.sum(swap_tiles(seqs, group, grad_tiles, "gain_grads", 9)[:, 0], axis=0)

    def whole_rows(cols, part, total):
        size = total // group
        return unblock(cols[:, :, part * size : (part + 1) * size], total).astype(jnp.float32)

    return (
        layer_out,
        input_grad,
        grad_sums[:share],
        whole_rows(head_cols, 0, width),
        whole_rows(head_cols, 1, width),
        whole_rows(head_cols, 2, width),
        out_sum.astype(jnp.float32),
        grad_sums[64 : 64 + share],
        whole_rows(unit_cols, 0, FF),
        whole_rows(unit_cols, 1, FF),
        down_sum.astype(jnp.float32),
    )


def solution(mesh):
    spread = ("seq", "fsdp")
    tokens, rows, gains = P(None, spread, None), P(spread, None), P(spread)
    in_specs = (tokens, tokens, P(), gains, rows, rows, rows, rows, gains, rows, rows, rows)
    out_specs = (tokens, tokens, gains, rows, rows, rows, rows, gains, rows, rows, rows)
    return jax.shard_map(body, mesh=mesh, in_specs=in_specs, out_specs=out_specs, check_vma=False)
```

```python
import functools

import jax
import jax.numpy as jnp
from jax import lax
from jax.experimental import pallas as pl
from jax.experimental.pallas import tpu as pltpu
from jax.sharding import PartitionSpec as P

HEAD = 64
FF = 8192
WINDOW = 1024
PAIR = 128
TILE = 512
LOW = -1e30
EPS = 1e-05
MESH = pl.DeviceIdType.MESH
MIB = 2**20


def to_half(values):
    return values.astype(jnp.bfloat16)


def normalize(values, gain):
    return values * lax.rsqrt(jnp.mean(values * values, axis=-1, keepdims=True) + EPS) * gain


def contract_rows(left, right):
    return lax.dot_general(
        left, right, (((0,), (0,)), ((), ())), preferred_element_type=jnp.float32
    )


def dot_nt(left, right):
    return lax.dot_general(
        left, right, (((1,), (1,)), ((), ())), preferred_element_type=jnp.float32
    )


def dot_nn(left, right):
    return jnp.dot(left, right, preferred_element_type=jnp.float32)


def head_lanes(values, half):
    lane = lax.broadcasted_iota(jnp.int32, values.shape, 1)
    return jnp.where((lane >= HEAD) == (half == 1), values, jnp.zeros_like(values))


def masked_scores(k_rows, q_head, low):
    keys, block = k_rows.shape[0], q_head.shape[0]
    scores = dot_nt(k_rows, q_head)
    at = lax.broadcasted_iota(jnp.int32, (keys, block), 0)
    query = lax.broadcasted_iota(jnp.int32, (keys, block), 1)
    seen = (at >= low) & (at <= query + WINDOW)
    return jnp.where(seen, scores, LOW)


class Line:
    def __init__(self, chips):
        self.chips = chips
        self.own = lax.axis_index("fsdp")
        self.chip = self.own // 2
        self.core = lax.rem(self.own, 2)
        self.other = self.own + 1 - 2 * self.core
        self.has_left = self.chip > 0
        self.has_right = self.chip < chips - 1

    def greet(self):
        signal_group(self.other)
        pl.when(self.has_left)(lambda: signal_group(self.own - 2))
        pl.when(self.has_right)(lambda: signal_group(self.own + 2))
        return 1 + self.has_left.astype(jnp.int32) + self.has_right.astype(jnp.int32)


def signal_group(peer):
    barrier = pltpu.get_barrier_semaphore()
    pl.semaphore_signal(barrier, inc=1, device_id={"fsdp": peer}, device_id_type=MESH)


def signal_seq(peer):
    barrier = pltpu.get_barrier_semaphore()
    pl.semaphore_signal(barrier, inc=1, device_id={"seq": peer}, device_id_type=MESH)


def greet_group(group):
    own = lax.axis_index("fsdp")
    pl.loop(1, group)(lambda ahead: signal_group(lax.rem(own + ahead, group)))
    return group - 1


def greet_seq(seqs):
    own = lax.axis_index("seq")
    pl.loop(1, seqs)(lambda ahead: signal_seq(lax.rem(own + ahead, seqs)))
    return seqs - 1


def meet(count):
    pl.semaphore_wait(pltpu.get_barrier_semaphore(), count)


def rows_at(index, size):
    return pl.ds(pl.multiple_of(index * size, size), size)


class Spread:
    def __init__(self, line, first, buf, send, recv):
        self.line, self.first, self.buf, self.send, self.recv = line, first, buf, send, recv

    def move(self, slot, way, peer, source=None):
        return pltpu.make_async_remote_copy(
            src_ref=self.buf.at[slot] if source is None else source,
            dst_ref=self.buf.at[slot],
            send_sem=self.send.at[way, slot],
            recv_sem=self.recv.at[slot],
            device_id={"fsdp": peer},
            device_id_type=MESH,
        )

    def begin(self):
        line = self.line
        pl.when(line.has_right)(lambda: self.move(line.own, 1, line.own + 2, self.first).start())
        pl.when(line.has_left)(lambda: self.move(line.own, 0, line.own - 2, self.first).start())
        self.move(line.own, 2, line.other, self.first).start()

    def relay(self, far):
        line = self.line

        @pl.when(line.chip - far >= 0)
        def _():
            slot = (line.chip - far) * 2 + line.core
            self.move(slot, 1, line.own).wait_recv()
            pl.when(line.has_right)(lambda: self.move(slot, 1, line.own + 2).start())
            self.move(slot, 2, line.other).start()

        @pl.when(line.chip + far < line.chips)
        def _():
            slot = (line.chip + far) * 2 + line.core
            self.move(slot, 0, line.own).wait_recv()
            pl.when(line.has_left)(lambda: self.move(slot, 0, line.own - 2).start())
            self.move(slot, 2, line.other).start()

    def each(self, far, use):
        line = self.line

        @pl.loop(0, 4)
        def _(turn):
            side = lax.rem(turn, 2)
            across = turn // 2
            away = far - across
            source = line.chip + away * (2 * side - 1)
            valid = (away >= 0) & (away < line.chips) & (source >= 0) & (source < line.chips)
            valid = valid & ((side == 0) | (away > 0))

            @pl.when(valid)
            def _():
                slot = source * 2 + line.core + across * (1 - 2 * line.core)
                pl.when(across == 1)(lambda: self.move(slot, 2, line.own).wait_recv())
                use(slot)

    def whole(self, use):
        @pl.loop(0, self.line.chips + 1)
        def _(far):
            pl.when(far > 0)(lambda: self.relay(far))
            self.each(far, use)

    def rest(self):
        pl.loop(0, self.line.chips)(
            lambda place: self.move(place * 2 + 1 - self.line.core, 2, self.line.own).wait_recv()
        )

    def sent(self):
        line = self.line

        @pl.loop(0, line.chips)
        def _(place):
            slot = place * 2 + line.core
            self.move(slot, 2, line.other).wait_send()
            pl.when(line.has_right & (place <= line.chip))(
                lambda: self.move(slot, 1, line.own + 2).wait_send()
            )
            pl.when(line.has_left & (place >= line.chip))(
                lambda: self.move(slot, 0, line.own - 2).wait_send()
            )


class Reduce:
    def __init__(self, line, product, out, acc, cross_out, line_out, cross_in, line_in, send, recv):
        self.line, self.product, self.out, self.acc = line, product, out, acc
        self.cross_out, self.line_out, self.cross_in, self.line_in = cross_out, line_out, cross_in, line_in
        self.send, self.recv = send, recv

    @staticmethod
    def scratch(chips, rows, width):
        part = pltpu.VMEM((chips, rows, width), jnp.bfloat16)
        return [
            pltpu.VMEM((rows, width), jnp.float32),
            pltpu.VMEM((rows, width), jnp.bfloat16),
            part,
            part,
            pltpu.VMEM((chips + 1, rows, width), jnp.bfloat16),
            pltpu.SemaphoreType.DMA((2, chips)),
            pltpu.SemaphoreType.DMA((2, chips + 1)),
        ]

    def cross(self, place):
        return pltpu.make_async_remote_copy(
            src_ref=self.cross_out,
            dst_ref=self.cross_in.at[place],
            send_sem=self.send.at[0, place],
            recv_sem=self.recv.at[0, place],
            device_id={"fsdp": self.line.other},
            device_id_type=MESH,
        )

    def along(self, place, landing, peer):
        return pltpu.make_async_remote_copy(
            src_ref=self.line_out.at[place],
            dst_ref=self.line_in.at[landing],
            send_sem=self.send.at[1, place],
            recv_sem=self.recv.at[1, landing],
            device_id={"fsdp": peer},
            device_id_type=MESH,
        )

    def steps(self):
        return 2 * self.line.chips - 1

    def step(self, step):
        line, acc = self.line, self.acc
        tiles = acc.shape[1] // TILE
        away = line.chips - 1 - step // 2
        side = lax.rem(step, 2)
        place = line.chip + away * (1 - 2 * side)

        @pl.when((place >= 0) & (place < line.chips))
        def _():
            @pl.loop(0, tiles)
            def _(tile):
                got = self.product(place * 2 + 1 - line.core, tile)
                self.cross_out[:, rows_at(tile, TILE)] = to_half(got)

            self.cross(place).start()

            @pl.loop(0, tiles)
            def _(tile):
                acc[:, rows_at(tile, TILE)] = self.product(place * 2 + line.core, tile)

            self.cross(place).wait()

            @pl.when(away > 0)
            def _():
                rightward = side == 0
                upstream = (rightward & line.has_left) | (jnp.logical_not(rightward) & line.has_right)

                @pl.when(upstream)
                def _():
                    self.along(place, place, line.own).wait_recv()
                    self.line_out[place] = to_half(
                        acc[...]
                        + self.cross_in[place].astype(jnp.float32)
                        + self.line_in[place].astype(jnp.float32)
                    )

                @pl.when(jnp.logical_not(upstream))
                def _():
                    self.line_out[place] = to_half(
                        acc[...] + self.cross_in[place].astype(jnp.float32)
                    )

                @pl.when(rightward)
                def _():
                    self.along(place, place, line.own + 2).start()

                @pl.when(jnp.logical_not(rightward))
                def _():
                    landing = jnp.where(away == 1, line.chips, place)
                    self.along(place, landing, line.own - 2).start()

            @pl.when(away == 0)
            def _():
                self.out[...] = acc[...] + self.cross_in[place].astype(jnp.float32)

                @pl.when(line.has_left)
                def _():
                    self.along(place, place, line.own).wait_recv()
                    self.out[...] += self.line_in[place].astype(jnp.float32)

                @pl.when(line.has_right)
                def _():
                    self.along(place, line.chips, line.own).wait_recv()
                    self.out[...] += self.line_in[line.chips].astype(jnp.float32)

    def sent(self):
        @pl.loop(0, self.line.chips)
        def _(place):
            pl.when(place != self.line.chip)(
                lambda: self.along(place, place, self.line.own).wait_send()
            )


class Swap:
    def __init__(self, group, source, target, send, recv, keep):
        self.group, self.source, self.target = group, source, target
        self.send, self.recv, self.keep = send, recv, keep
        self.own = lax.axis_index("fsdp")

    def move(self, peer, source):
        return pltpu.make_async_remote_copy(
            src_ref=self.source.at[peer],
            dst_ref=self.target.at[source],
            send_sem=self.send.at[peer],
            recv_sem=self.recv.at[source],
            device_id={"fsdp": peer},
            device_id_type=MESH,
        )

    def kept(self):
        return pltpu.make_async_copy(self.source.at[self.own], self.target.at[self.own], self.keep)

    def begin(self):
        self.kept().start()
        pl.loop(1, self.group)(
            lambda ahead: self.move(lax.rem(self.own + ahead, self.group), self.own).start()
        )

    def end(self):
        self.kept().wait()

        @pl.loop(1, self.group)
        def _(ahead):
            peer = lax.rem(self.own + ahead, self.group)
            self.move(peer, peer).wait_recv()
            self.move(peer, self.own).wait_send()


class Share:
    def __init__(self, seqs, source, target, send, recv, keep):
        self.seqs, self.source, self.target = seqs, source, target
        self.send, self.recv, self.keep = send, recv, keep
        self.own = lax.axis_index("seq")

    def move(self, peer, place):
        return pltpu.make_async_remote_copy(
            src_ref=self.source,
            dst_ref=self.target.at[place],
            send_sem=self.send.at[peer],
            recv_sem=self.recv.at[place],
            device_id={"seq": peer},
            device_id_type=MESH,
        )

    def kept(self):
        return pltpu.make_async_copy(self.source, self.target.at[self.own], self.keep)

    def begin(self):
        self.kept().start()
        pl.loop(1, self.seqs)(
            lambda ahead: self.move(lax.rem(self.own + ahead, self.seqs), self.own).start()
        )

    def end(self):
        self.kept().wait()

        @pl.loop(1, self.seqs)
        def _(ahead):
            peer = lax.rem(self.own + ahead, self.seqs)
            self.move(peer, peer).wait_recv()
            self.move(peer, self.own).wait_send()


VMEM_SPEC = pl.BlockSpec(memory_space=pltpu.VMEM)
ANY_SPEC = pl.BlockSpec(memory_space=pl.ANY)


def comm_params(collective, mib=58):
    return pltpu.CompilerParams(
        collective_id=collective, has_side_effects=True, vmem_limit_bytes=mib * MIB
    )


def cost(flops, local, remote):
    return pl.CostEstimate(
        flops=flops, bytes_accessed=local, transcendentals=0, remote_bytes_transferred=remote
    )


def sems(*shape):
    return pltpu.SemaphoreType.DMA(shape)


def left_rows(a_ref, slot, rows):
    if len(a_ref.shape) == 2:
        return a_ref[rows_at(slot, rows), :]
    piece = rows // a_ref.shape[0]
    return jnp.concatenate(
        [a_ref[batch, rows_at(slot, piece), :] for batch in range(a_ref.shape[0])], axis=0
    )


def norm_back(rows, v_ref, e_ref, gain_ref, gain_acc, put):
    gain_acc[...] = jnp.zeros_like(gain_acc)

    @pl.loop(0, rows // 16)
    def _(chunk):
        here = rows_at(chunk, 16)
        values = v_ref[here, :].astype(jnp.float32)
        error = e_ref[here, :]
        rate = lax.rsqrt(jnp.mean(values * values, axis=-1, keepdims=True) + EPS)
        unit = values * rate
        product = error * unit
        gain = gain_ref[0:1, :]
        mean = jnp.mean(product * gain, axis=-1, keepdims=True)
        gain_acc[...] += product[0:8] + product[8:16]
        put(here, rate * (gain * error - unit * mean))


def start_kernel(
    seqs, chips, batches, tile_ref, x_ref, blocks_ref, g_ref, q_ref, kv_ref, gains_ref, w_out_ref,
    buf, normed, gain, gains, w, send, recv, keep, swap_send, share_send, w_recv,
    tile_send, tile_across, tile_recv, tile_back, w_keep, gain_keep,
):
    line = Line(chips)
    group = 2 * chips
    seq = lax.axis_index("seq")
    own = line.own
    share = blocks_ref.shape[1]
    piece = x_ref.shape[0] // batches
    span = q_ref.shape[2]
    width = x_ref.shape[1]
    per = 128 * seqs * group // width
    meet(greet_group(group) + greet_seq(seqs))

    def block_at(run, member):
        return w.at[rows_at(run * group + member, share)]

    def block_swap(peer, member):
        return pltpu.make_async_remote_copy(
            src_ref=blocks_ref.at[peer],
            dst_ref=block_at(seq, member),
            send_sem=swap_send.at[peer],
            recv_sem=w_recv.at[seq, member],
            device_id={"fsdp": peer},
            device_id_type=MESH,
        )

    def block_share(run, member, peer):
        return pltpu.make_async_remote_copy(
            src_ref=block_at(run, member),
            dst_ref=block_at(run, member),
            send_sem=share_send.at[peer, member],
            recv_sem=w_recv.at[run, member],
            device_id={"seq": peer},
            device_id_type=MESH,
        )

    def tile_to_seq(peer, place):
        return pltpu.make_async_remote_copy(
            src_ref=tile_ref.at[0],
            dst_ref=gains.at[own, place],
            send_sem=tile_send.at[peer],
            recv_sem=tile_recv.at[place],
            device_id={"seq": peer},
            device_id_type=MESH,
        )

    def tiles_to_group(peer, member):
        return pltpu.make_async_remote_copy(
            src_ref=gains.at[member],
            dst_ref=gains.at[member],
            send_sem=tile_across.at[peer],
            recv_sem=tile_back.at[member],
            device_id={"fsdp": peer},
            device_id_type=MESH,
        )

    def others(count, me, act):
        pl.loop(1, count)(lambda ahead: act(lax.rem(me + ahead, count)))

    others(seqs, seq, lambda peer: tile_to_seq(peer, seq).start())
    others(group, own, lambda peer: block_swap(peer, own).start())
    spread = Spread(line, x_ref, buf, send, recv)
    spread.begin()
    gains[own, seq] = tile_ref[0]
    w[rows_at(seq * group + own, share), :] = blocks_ref[own]
    others(seqs, seq, lambda peer: block_share(seq, own, peer).start())
    buf[own] = x_ref[...]
    others(seqs, seq, lambda peer: tile_to_seq(peer, peer).wait_recv())
    others(group, own, lambda peer: tiles_to_group(peer, own).start())

    def pass_block(member):
        block_swap(member, member).wait_recv()
        others(seqs, seq, lambda peer: block_share(seq, member, peer).start())

    others(group, own, pass_block)
    others(group, own, lambda peer: tiles_to_group(peer, peer).wait_recv())
    for column in range(width // 128):
        total = 0.0
        for place in range(column * per, (column + 1) * per):
            total = total + gains[place % group, place // group, 0:1, :]
        gain[0:1, column * 128 : (column + 1) * 128] = total

    def kept(slot, batch):
        return pltpu.make_async_copy(
            normed.at[slot, pl.ds(batch * piece, piece)],
            g_ref.at[batch, rows_at(slot, piece)],
            keep.at[slot, batch],
        )

    def use(slot):
        @pl.loop(0, x_ref.shape[0] // 16)
        def _(chunk):
            rows = rows_at(chunk, 16)
            values = buf[slot, rows, :].astype(jnp.float32)
            normed[slot, rows, :] = to_half(normalize(values, gain[0:1, :]))

        for batch in range(batches):
            kept(slot, batch).start()
        rows = rows_at(slot, piece)
        values = normed[slot]
        for part in range(3):
            got = to_half(dot_nn(values, w[:, part * span : (part + 1) * span]))
            for batch in range(batches):
                mine = got[batch * piece : (batch + 1) * piece]
                if part == 0:
                    q_ref[batch, rows, :] = mine
                else:
                    kv_ref[batch, rows, (part - 1) * span : part * span] = mine

    pl.loop(1, chips - 1)(spread.relay)

    def have_block(run, member):
        block_share(run, member, seq).wait_recv()

    others(seqs, seq, lambda run: pl.loop(0, group)(lambda member: have_block(run, member)))
    w_kept = pltpu.make_async_copy(w, w_out_ref, w_keep)
    w_kept.start()
    gains_kept = pltpu.make_async_copy(gains, gains_ref, gain_keep)
    gains_kept.start()

    pl.loop(0, chips - 1)(lambda far: spread.each(far, use))
    spread.relay(chips - 1)
    spread.each(chips - 1, use)
    spread.each(chips, use)
    spread.sent()
    others(seqs, seq, lambda peer: tile_to_seq(peer, seq).wait_send())
    others(group, own, lambda peer: block_swap(peer, own).wait_send())
    others(group, own, lambda peer: tiles_to_group(peer, own).wait_send())
    others(
        seqs,
        seq,
        lambda peer: pl.loop(0, group)(lambda member: block_share(seq, member, peer).wait_send()),
    )
    w_kept.wait()
    gains_kept.wait()

    @pl.loop(0, group)
    def _(slot):
        for batch in range(batches):
            kept(slot, batch).wait()


def start(seqs, chips, batches, tile, x, blocks, collective):
    rows, width = x.shape
    group = 2 * chips
    length = group * rows // batches
    share, cols = blocks.shape[1:]
    span = cols // 3
    half = jnp.bfloat16
    return pl.pallas_call(
        functools.partial(start_kernel, seqs, chips, batches),
        out_shape=[
            jax.ShapeDtypeStruct((batches, length, width), half),
            jax.ShapeDtypeStruct((batches, length, span), half),
            jax.ShapeDtypeStruct((batches, length, 2 * span), half),
            jax.ShapeDtypeStruct((group, seqs, 8, 128), jnp.float32),
            jax.ShapeDtypeStruct((width, cols), half),
        ],
        in_specs=[VMEM_SPEC] * 3,
        out_specs=[ANY_SPEC, VMEM_SPEC, VMEM_SPEC, ANY_SPEC, ANY_SPEC],
        scratch_shapes=[
            pltpu.VMEM((group, rows, width), half),
            pltpu.VMEM((group, rows, width), half),
            pltpu.VMEM((8, width), jnp.float32),
            pltpu.VMEM((group, seqs, 8, 128), jnp.float32),
            pltpu.VMEM((width, cols), half),
            sems(3, group),
            sems(group),
            sems(group, batches),
            sems(group),
            sems(seqs, group),
            sems(seqs, group),
            sems(seqs),
            sems(group),
            sems(seqs),
            sems(group),
            pltpu.SemaphoreType.DMA,
            pltpu.SemaphoreType.DMA,
        ],
        compiler_params=comm_params(collective),
        cost_estimate=cost(2 * group * rows * width * cols, 200 * MIB, group * rows * width * 2),
        name="start",
    )(tile, x, blocks)


def attend_kernel(
    seqs, group, block, q_ref, kv_ref, low_ref, units_ref, out_ref, lse_ref, pad_ref, own_units_ref,
    pad, vt, halo_send, halo_recv, pad_keep, swap_send, swap_recv, swap_keep,
):
    seq = lax.axis_index("seq")
    batches, length, span = q_ref.shape
    has_left, has_right = seq > 0, seq < seqs - 1
    pl.when(has_left)(lambda: signal_seq(seq - 1))
    pl.when(has_right)(lambda: signal_seq(seq + 1))
    meet(greet_group(group) + has_left.astype(jnp.int32) + has_right.astype(jnp.int32))

    def halo(batch, peer):
        return pltpu.make_async_remote_copy(
            src_ref=kv_ref.at[batch, pl.ds(length - WINDOW, WINDOW)],
            dst_ref=pad.at[batch, pl.ds(0, WINDOW)],
            send_sem=halo_send.at[batch],
            recv_sem=halo_recv.at[batch],
            device_id={"seq": peer},
            device_id_type=MESH,
        )

    for batch in range(batches):
        pl.when(has_right)(lambda batch=batch: halo(batch, seq + 1).start())
    swap = Swap(group, units_ref, own_units_ref, swap_send, swap_recv, swap_keep)
    swap.begin()
    pad[:, WINDOW:, :] = kv_ref[...]

    @pl.when(jnp.logical_not(has_left))
    def _():
        pad[:, :WINDOW, :] = jnp.zeros((batches, WINDOW, 2 * span), jnp.bfloat16)

    def kept(batch):
        return pltpu.make_async_copy(pad.at[batch], pad_ref.at[batch], pad_keep.at[batch])

    for batch in range(batches):
        pl.when(has_left)(lambda batch=batch: halo(batch, seq).wait_recv())
        kept(batch).start()
        vt[...] = pad[batch, :, span:].T

        @pl.loop(0, length // block)
        def _(step, batch=batch):
            begin = pl.multiple_of(step * block, block)
            keys = pl.ds(begin, block + WINDOW)
            rows = pl.ds(begin, block)
            low = low_ref[batch, :, rows]
            for pair in range(span // PAIR):
                lanes = slice(pair * PAIR, (pair + 1) * PAIR)
                q_pair = q_ref[batch, rows, lanes] * jnp.asarray(HEAD**-0.5, jnp.bfloat16)
                k_rows = pad[batch, keys, lanes]
                values = vt[lanes, keys]
                mixed = []
                for half in range(2):
                    scores = masked_scores(k_rows, head_lanes(q_pair, half), low)
                    top = jnp.max(scores, axis=0, keepdims=True)
                    expo = jnp.exp(scores - top)
                    total = jnp.sum(expo, axis=0, keepdims=True)
                    mixed.append(dot_nn(values, to_half(expo)) / total)
                    row = pair * 2 + half
                    lse_ref[batch, row : row + 1, rows] = top + jnp.log(total)
                lane = lax.broadcasted_iota(jnp.int32, mixed[0].shape, 0)
                out_ref[batch, rows, lanes] = to_half(jnp.where(lane < HEAD, mixed[0], mixed[1]).T)

    for batch in range(batches):
        kept(batch).wait()
        pl.when(has_right)(lambda batch=batch: halo(batch, seq + 1).wait_send())
    swap.end()


def attend(seqs, group, query, key_value, low, block, units, collective):
    batches, length, span = query.shape
    padded = length + WINDOW
    heads = span // HEAD
    half = jnp.bfloat16
    return pl.pallas_call(
        functools.partial(attend_kernel, seqs, group, block),
        in_specs=[VMEM_SPEC, VMEM_SPEC, VMEM_SPEC, ANY_SPEC],
        out_specs=[VMEM_SPEC, VMEM_SPEC, ANY_SPEC, ANY_SPEC],
        out_shape=[
            jax.ShapeDtypeStruct((batches, length, span), half),
            jax.ShapeDtypeStruct((batches, heads, length), jnp.float32),
            jax.ShapeDtypeStruct((batches, padded, 2 * span), half),
            jax.ShapeDtypeStruct(units.shape, half),
        ],
        scratch_shapes=[
            pltpu.VMEM((batches, padded, 2 * span), half),
            pltpu.VMEM((span, padded), half),
            sems(batches),
            sems(batches),
            sems(batches),
            sems(group),
            sems(group),
            pltpu.SemaphoreType.DMA,
        ],
        compiler_params=comm_params(collective),
        cost_estimate=cost(
            8 * batches * length * span * (WINDOW + block), 150 * MIB, units.size * 2
        ),
        name="attend",
    )(query, key_value, low, units)


def branch_kernel(
    seqs, chips, a_ref, w_ref, d_ref, units_ref, out_ref, gd_ref, w_units_ref,
    acc, cross_out, line_out, cross_in, line_in, sum_send, sum_recv,
    send, recv, d_keep, share_send, share_recv, share_keep,
):
    line = Line(chips)
    rows = out_ref.shape[0]

    def product(slot, tile):
        return dot_nn(left_rows(a_ref, slot, rows), w_ref[:, rows_at(tile, TILE)])

    meet(line.greet() + greet_seq(seqs))
    reduce = Reduce(
        line, product, out_ref, acc, cross_out, line_out, cross_in, line_in, sum_send, sum_recv
    )
    spread = Spread(line, d_ref, gd_ref, send, recv)
    units = Share(seqs, units_ref, w_units_ref, share_send, share_recv, share_keep)
    d_kept = pltpu.make_async_copy(d_ref, gd_ref.at[line.own], d_keep)
    units.begin()
    spread.begin()
    d_kept.start()

    @pl.loop(0, reduce.steps())
    def _(step):
        reduce.step(step)
        pl.when(lax.rem(step, 2) == 1)(lambda: spread.relay((step + 1) // 2))

    spread.rest()
    spread.sent()
    reduce.sent()
    d_kept.wait()
    units.end()


def branch_sum(seqs, chips, a, w, d_rows, units, collective):
    rows, width = d_rows.shape
    group = 2 * chips
    half = jnp.bfloat16
    return pl.pallas_call(
        functools.partial(branch_kernel, seqs, chips),
        out_shape=[
            jax.ShapeDtypeStruct((rows, width), jnp.float32),
            jax.ShapeDtypeStruct((group, rows, width), half),
            jax.ShapeDtypeStruct((seqs,) + units.shape, half),
        ],
        in_specs=[VMEM_SPEC, VMEM_SPEC, ANY_SPEC, ANY_SPEC],
        out_specs=[VMEM_SPEC, ANY_SPEC, ANY_SPEC],
        scratch_shapes=Reduce.scratch(chips, rows, width)
        + [sems(3, group), sems(group), pltpu.SemaphoreType.DMA]
        + [sems(seqs), sems(seqs), pltpu.SemaphoreType.DMA],
        compiler_params=comm_params(collective),
        cost_estimate=cost(
            2 * group * rows * width * w.shape[0], 250 * MIB, 3 * group * rows * width * 2
        ),
        name="branch_sum",
    )(a, w, d_rows, units)


def units_kernel(
    chips, x_ref, w_hbm, wd_hbm, gd_ref, g_ref, hidden_hbm, d_hbm,
    buf, d_buf, w_ref, wd_ref, hidden_ref, d_ref, send, recv, keep, d_sem, load, store,
):
    line = Line(chips)
    rows = x_ref.shape[0]
    units = hidden_ref.shape[1]
    part = min(units, 256)
    loads = [
        pltpu.make_async_copy(w_hbm, w_ref, load.at[0]),
        pltpu.make_async_copy(wd_hbm, wd_ref, load.at[1]),
    ]
    for item in loads:
        item.start()
    meet(line.greet())
    spread = Spread(line, x_ref, buf, send, recv)
    spread.begin()
    buf[line.own] = x_ref[...]
    for item in loads:
        item.wait()

    def kept(slot):
        place = rows_at(slot, rows)
        return [
            pltpu.make_async_copy(buf.at[slot], g_ref.at[slot], keep.at[slot]),
            pltpu.make_async_copy(hidden_ref.at[place], hidden_hbm.at[place], store.at[0, slot]),
            pltpu.make_async_copy(d_ref.at[place], d_hbm.at[place], store.at[1, slot]),
        ]

    def use(slot):
        fetch = pltpu.make_async_copy(gd_ref.at[slot], d_buf, d_sem)
        fetch.start()
        place = rows_at(slot, rows)
        fetch.wait()

        @pl.loop(0, units // part)
        def _(tile):
            here = rows_at(tile, part)
            there = rows_at(units // part + tile, part)
            values = buf[slot]
            gate = dot_nn(values, w_ref[:, here])
            up = dot_nn(values, w_ref[:, there])
            d_hidden = dot_nt(d_buf[...], wd_ref[here, :])
            sigma = jax.nn.sigmoid(gate)
            swish = gate * sigma
            hidden_ref[place, here] = to_half(swish * up)
            d_ref[place, here] = to_half(d_hidden * up * sigma * (1.0 + gate * (1.0 - sigma)))
            d_ref[place, there] = to_half(d_hidden * swish)

        for item in kept(slot):
            item.start()

    spread.whole(use)
    spread.sent()

    @pl.loop(0, 2 * chips)
    def _(slot):
        for item in kept(slot):
            item.wait()


def hidden_units(chips, x, w, wd, group_d, collective):
    rows, width = x.shape
    group = 2 * chips
    units = wd.shape[0]
    half = jnp.bfloat16
    return pl.pallas_call(
        functools.partial(units_kernel, chips),
        out_shape=[
            jax.ShapeDtypeStruct((group, rows, width), half),
            jax.ShapeDtypeStruct((group * rows, units), half),
            jax.ShapeDtypeStruct((group * rows, 2 * units), half),
        ],
        in_specs=[VMEM_SPEC, ANY_SPEC, ANY_SPEC, ANY_SPEC],
        out_specs=[ANY_SPEC, ANY_SPEC, ANY_SPEC],
        scratch_shapes=[
            pltpu.VMEM((group, rows, width), half),
            pltpu.VMEM((rows, width), half),
            pltpu.VMEM(w.shape, half),
            pltpu.VMEM(wd.shape, half),
            pltpu.VMEM((group * rows, units), half),
            pltpu.VMEM((group * rows, 2 * units), half),
            sems(3, group),
            sems(group),
            sems(group),
            pltpu.SemaphoreType.DMA,
            sems(2),
            sems(2, group),
        ],
        compiler_params=comm_params(collective),
        cost_estimate=cost(
            6 * group * rows * width * units, 200 * MIB, group * rows * width * 2
        ),
        name="hidden_units",
    )(x, w, wd, group_d)


def units_back_kernel(
    chips, a_hbm, w_hbm, b_hbm, v_ref, cot_ref, gain_ref, dm_ref, db_ref, gain_grad_ref, grad_hbm,
    a_ref, w_ref, total, lefts, tiles, load, left_sem, tile_sem,
    acc, cross_out, line_out, cross_in, line_in, sum_send, sum_recv,
):
    line = Line(chips)
    rows, width = v_ref.shape
    group = 2 * chips
    part = lefts.shape[2]
    loads = [
        pltpu.make_async_copy(w_hbm, w_ref, load.at[0]),
        pltpu.make_async_copy(a_hbm, a_ref, load.at[1]),
    ]
    for item in loads:
        item.start()

    def left(tile):
        slot = lax.rem(tile, 2)
        return pltpu.make_async_copy(
            b_hbm.at[:, rows_at(tile, part)], lefts.at[slot], left_sem.at[slot]
        )

    def stored(tile):
        slot = lax.rem(tile, 2)
        return pltpu.make_async_copy(
            tiles.at[slot], grad_hbm.at[rows_at(tile, part)], tile_sem.at[slot]
        )

    def weight_grad(tile):
        left(tile).wait()
        pl.when(tile + 1 < width // part)(lambda: left(tile + 1).start())
        pl.when(tile >= 2)(lambda: stored(tile - 2).wait())
        slot = lax.rem(tile, 2)
        size = min(TILE, a_ref.shape[1])

        @pl.loop(0, a_ref.shape[1] // size)
        def _(column):
            here = rows_at(column, size)
            tiles[slot, :, here] = to_half(contract_rows(lefts[slot], a_ref[:, here]))

        stored(tile).start()

    def product(slot, tile):
        return dot_nt(left_rows(a_ref, slot, rows), w_ref[rows_at(tile, TILE), :])

    meet(line.greet())
    left(0).start()
    for item in loads:
        item.wait()
    reduce = Reduce(
        line, product, total, acc, cross_out, line_out, cross_in, line_in, sum_send, sum_recv
    )
    count = width // part
    per = -(-count // reduce.steps())

    @pl.loop(0, reduce.steps())
    def _(step):
        reduce.step(step)

        @pl.loop(0, per)
        def _(turn):
            tile = step * per + turn
            pl.when(tile < count)(lambda: weight_grad(tile))

    def put(here, d_values):
        d_middle = cot_ref[here, :].astype(jnp.float32) + d_values
        dm_ref[here, :] = d_middle
        db_ref[here, :] = to_half(d_middle)

    norm_back(rows, v_ref, total, gain_ref, gain_grad_ref, put)
    reduce.sent()
    stored(count - 2).wait()
    stored(count - 1).wait()


def units_back(chips, a, w, b, middle, cot, gain, collective):
    rows, width = middle.shape
    group = 2 * chips
    half = jnp.bfloat16
    part = 256 if a.shape[0] <= 2048 else 128
    return pl.pallas_call(
        functools.partial(units_back_kernel, chips),
        out_shape=[
            jax.ShapeDtypeStruct((rows, width), jnp.float32),
            jax.ShapeDtypeStruct((rows, width), half),
            jax.ShapeDtypeStruct((8, width), jnp.float32),
            jax.ShapeDtypeStruct((width, a.shape[1]), half),
        ],
        in_specs=[ANY_SPEC] * 3 + [VMEM_SPEC] * 3,
        out_specs=[VMEM_SPEC] * 3 + [ANY_SPEC],
        scratch_shapes=[
            pltpu.VMEM(a.shape, half),
            pltpu.VMEM(w.shape, half),
            pltpu.VMEM((rows, width), jnp.float32),
            pltpu.VMEM((2, a.shape[0], part), half),
            pltpu.VMEM((2, part, a.shape[1]), half),
            sems(2),
            sems(2),
            sems(2),
        ]
        + Reduce.scratch(chips, rows, width),
        compiler_params=comm_params(collective, 60),
        cost_estimate=cost(
            4 * group * rows * width * a.shape[1], 200 * MIB, group * rows * width * 2
        ),
        name="units_back",
    )(a, w, b.reshape(group * rows, width), middle, cot, gain)


def branch_back_kernel(
    chips, batches, x_ref, w_ref, att_ref, hidden_hbm, wd_hbm, gd_hbm,
    d_ref, out_ref, out_grad_ref, down_hbm,
    buf, hidden_ref, wd_ref, rights, tiles, grad_acc, send, recv, load, right_sem, tile_sem,
    acc, cross_out, line_out, cross_in, line_in, sum_send, sum_recv,
):
    line = Line(chips)
    rows = x_ref.shape[0]
    piece = rows // batches
    width = x_ref.shape[1]
    part = rights.shape[2]
    loads = [
        pltpu.make_async_copy(hidden_hbm, hidden_ref, load.at[0]),
        pltpu.make_async_copy(wd_hbm, wd_ref, load.at[1]),
    ]
    for item in loads:
        item.start()

    def product(slot, tile):
        return dot_nn(left_rows(hidden_ref, slot, rows), wd_ref[:, rows_at(tile, TILE)])

    def right(tile):
        slot = lax.rem(tile, 2)
        return pltpu.make_async_copy(
            gd_hbm.at[:, rows_at(tile, part)], rights.at[slot], right_sem.at[slot]
        )

    def stored(tile):
        slot = lax.rem(tile, 2)
        return pltpu.make_async_copy(
            tiles.at[slot], down_hbm.at[:, rows_at(tile, part)], tile_sem.at[slot]
        )

    def weight_grad(tile):
        right(tile).wait()
        pl.when(tile + 1 < width // part)(lambda: right(tile + 1).start())
        pl.when(tile >= 2)(lambda: stored(tile - 2).wait())
        slot = lax.rem(tile, 2)
        size = min(256, hidden_ref.shape[1])

        @pl.loop(0, hidden_ref.shape[1] // size)
        def _(row):
            here = rows_at(row, size)
            tiles[slot, here, :] = to_half(contract_rows(hidden_ref[:, here], rights[slot]))

        stored(tile).start()

    meet(line.greet())
    spread = Spread(line, x_ref, buf, send, recv)
    reduce = Reduce(
        line, product, out_ref, acc, cross_out, line_out, cross_in, line_in, sum_send, sum_recv
    )
    spread.begin()
    right(0).start()
    buf[line.own] = x_ref[...]
    grad_acc[...] = jnp.zeros_like(grad_acc)

    def use(slot):
        got = to_half(dot_nt(buf[slot], w_ref[...]))
        for batch in range(batches):
            d_ref[batch, rows_at(slot, piece), :] = got[batch * piece : (batch + 1) * piece]
        mixed = left_rows(att_ref, slot, rows)

        @pl.loop(0, width // TILE)
        def _(tile):
            here = rows_at(tile, TILE)
            grad_acc[:, here] += contract_rows(mixed, buf[slot, :, here])

    for item in loads:
        item.wait()
    count = width // part
    per = -(-count // reduce.steps())

    @pl.loop(0, reduce.steps())
    def _(step):
        reduce.step(step)

        @pl.when(lax.rem(step, 2) == 1)
        def _():
            far = (step + 1) // 2
            spread.relay(far)
            spread.each(far - 1, use)

        @pl.loop(0, per)
        def _(turn):
            tile = step * per + turn
            pl.when(tile < count)(lambda: weight_grad(tile))

    spread.each(chips - 1, use)
    spread.each(chips, use)
    out_grad_ref[...] = to_half(grad_acc[...])
    spread.sent()
    reduce.sent()
    stored(count - 2).wait()
    stored(count - 1).wait()


def branch_back(chips, batches, x, w, attended, hidden, wd, group_d, collective):
    rows, width = x.shape
    group = 2 * chips
    length = group * rows // batches
    span = w.shape[0]
    units = wd.shape[0]
    half = jnp.bfloat16
    part = 256 if group * rows <= 2048 else 128
    return pl.pallas_call(
        functools.partial(branch_back_kernel, chips, batches),
        out_shape=[
            jax.ShapeDtypeStruct((batches, length, span), half),
            jax.ShapeDtypeStruct((rows, width), jnp.float32),
            jax.ShapeDtypeStruct((span, width), half),
            jax.ShapeDtypeStruct((units, width), half),
        ],
        in_specs=[VMEM_SPEC] * 3 + [ANY_SPEC] * 3,
        out_specs=[VMEM_SPEC, VMEM_SPEC, VMEM_SPEC, ANY_SPEC],
        scratch_shapes=[
            pltpu.VMEM((group, rows, width), half),
            pltpu.VMEM(hidden.shape, half),
            pltpu.VMEM(wd.shape, half),
            pltpu.VMEM((2, group * rows, part), half),
            pltpu.VMEM((2, units, part), half),
            pltpu.VMEM((span, width), jnp.float32),
            sems(3, group),
            sems(group),
            sems(2),
            sems(2),
            sems(2),
        ]
        + Reduce.scratch(chips, rows, width),
        compiler_params=comm_params(collective, 62),
        cost_estimate=cost(
            2 * group * rows * width * (2 * span + 2 * units),
            250 * MIB,
            2 * group * rows * width * 2,
        ),
        name="branch_back",
    )(x, w, attended, hidden, wd, group_d.reshape(group * rows, width))


def attend_back_kernel(
    seqs, group, block, q_ref, pad_ref, low_ref, lse_ref, d_ref, sums_ref, heads_ref, cols_ref,
    dk, dv, kt, back_out, back_in, halo_send, halo_recv, swap_send, swap_recv, swap_keep,
):
    seq = lax.axis_index("seq")
    batches, length, span = q_ref.shape
    has_left, has_right = seq > 0, seq < seqs - 1
    pl.when(has_left)(lambda: signal_seq(seq - 1))
    pl.when(has_right)(lambda: signal_seq(seq + 1))
    meet(greet_group(group) + has_left.astype(jnp.int32) + has_right.astype(jnp.int32))
    swap = Swap(group, sums_ref, cols_ref, swap_send, swap_recv, swap_keep)
    swap.begin()
    steps = length // block
    scale = jnp.asarray(HEAD**-0.5, jnp.bfloat16)

    def halo(batch, step, peer):
        rows = rows_at(step, block)
        return pltpu.make_async_remote_copy(
            src_ref=back_out.at[batch, rows],
            dst_ref=back_in.at[batch, rows],
            send_sem=halo_send.at[batch, step],
            recv_sem=halo_recv.at[batch, step],
            device_id={"seq": peer},
            device_id_type=MESH,
        )

    dk[...] = jnp.zeros_like(dk)
    dv[...] = jnp.zeros_like(dv)
    for batch in range(batches):
        kt[...] = pad_ref[batch, :, :span].T * scale

        @pl.loop(0, steps)
        def _(step, batch=batch):
            begin = pl.multiple_of(step * block, block)
            keys = pl.ds(begin, block + WINDOW)
            rows = pl.ds(begin, block)
            low = low_ref[batch, :, rows]
            for pair in range(span // PAIR):
                lanes = slice(pair * PAIR, (pair + 1) * PAIR)
                q_pair = q_ref[batch, rows, lanes] * scale
                d_pair = d_ref[batch, rows, lanes]
                k_rows = pad_ref[batch, keys, lanes]
                v_rows = pad_ref[batch, keys, span + pair * PAIR : span + (pair + 1) * PAIR]
                k_cols = kt[lanes, keys]
                back = []
                for half in range(2):
                    row = pair * 2 + half
                    q_head = head_lanes(q_pair, half)
                    d_head = head_lanes(d_pair, half)
                    scores = masked_scores(k_rows, q_head, low)
                    probs = jnp.exp(scores - lse_ref[batch, row : row + 1, rows])
                    d_probs = dot_nt(v_rows, d_head)
                    along = jnp.sum(probs * d_probs, axis=0, keepdims=True)
                    d_scores = to_half(probs * (d_probs - along))
                    dv[batch, keys, lanes] += dot_nn(to_half(probs), d_head)
                    dk[batch, keys, lanes] += dot_nn(d_scores, q_head)
                    back.append(dot_nn(k_cols, d_scores))
                at = lax.broadcasted_iota(jnp.int32, back[0].shape, 0)
                heads_ref[batch, rows, lanes] = to_half(
                    jnp.where(at < HEAD, back[0], back[1]).T
                )

            @pl.when(has_left & (step < WINDOW // block))
            def _():
                back_out[batch, rows, :span] = to_half(dk[batch, rows, :])
                back_out[batch, rows, span:] = to_half(dv[batch, rows, :])
                halo(batch, step, seq - 1).start()

    first = length - WINDOW
    for batch in range(batches):
        if first:
            heads_ref[batch, :first, span : 2 * span] = to_half(dk[batch, WINDOW:length, :])
            heads_ref[batch, :first, 2 * span :] = to_half(dv[batch, WINDOW:length, :])

        @pl.loop(0, WINDOW // block)
        def _(step, batch=batch):
            inner = pl.ds(pl.multiple_of(step * block + length, block), block)
            rows = pl.ds(pl.multiple_of(step * block + first, block), block)

            @pl.when(has_right)
            def _():
                halo(batch, step, seq).wait_recv()
                got = back_in[batch, rows_at(step, block), :].astype(jnp.float32)
                heads_ref[batch, rows, span : 2 * span] = to_half(
                    dk[batch, inner, :] + got[:, :span]
                )
                heads_ref[batch, rows, 2 * span :] = to_half(dv[batch, inner, :] + got[:, span:])

            @pl.when(jnp.logical_not(has_right))
            def _():
                heads_ref[batch, rows, span : 2 * span] = to_half(dk[batch, inner, :])
                heads_ref[batch, rows, 2 * span :] = to_half(dv[batch, inner, :])

            pl.when(has_left)(lambda: halo(batch, step, seq).wait_send())

    swap.end()


def attend_back(seqs, group, query, kv_pad, low, lse, d_att, block, sums, collective):
    batches, length, span = query.shape
    padded = kv_pad.shape[1]
    half = jnp.bfloat16
    return pl.pallas_call(
        functools.partial(attend_back_kernel, seqs, group, block),
        in_specs=[VMEM_SPEC] * 5 + [ANY_SPEC],
        out_specs=[VMEM_SPEC, ANY_SPEC],
        out_shape=[
            jax.ShapeDtypeStruct((batches, length, 3 * span), half),
            jax.ShapeDtypeStruct(sums.shape, half),
        ],
        scratch_shapes=[
            pltpu.VMEM((batches, padded, span), jnp.float32),
            pltpu.VMEM((batches, padded, span), jnp.float32),
            pltpu.VMEM((span, padded), half),
            pltpu.VMEM((batches, WINDOW, 2 * span), half),
            pltpu.VMEM((batches, WINDOW, 2 * span), half),
            sems(batches, WINDOW // block),
            sems(batches, WINDOW // block),
            sems(group),
            sems(group),
            pltpu.SemaphoreType.DMA,
        ],
        compiler_params=comm_params(collective),
        cost_estimate=cost(
            20 * batches * length * span * (WINDOW + block), 180 * MIB, sums.size * 2
        ),
        name="attend_back",
    )(query, kv_pad, low, lse, d_att, sums)


def heads_back_kernel(
    seqs, chips, a_ref, w_ref, g_hbm, v_ref, dm_ref, gain_ref, mlp_gain_ref,
    grad_ref, cols_ref, tile_ref,
    total, gain_acc, lefts, parts, sums, cols, gain_out, gain_in, gain_sum, gain_back,
    left_sem, part_send, part_recv, cols_send, cols_recv, cols_keep,
    gain_send, gain_recv, back_send, back_recv,
    acc, cross_out, line_out, cross_in, line_in, sum_send, sum_recv,
):
    line = Line(chips)
    group = 2 * chips
    seq = lax.axis_index("seq")
    own = line.own
    rows, width = v_ref.shape
    batches = a_ref.shape[0]
    part = lefts.shape[3]
    run = width // seqs
    share = run // group
    depth = a_ref.shape[2]

    def left(tile):
        slot = lax.rem(tile, 2)
        return pltpu.make_async_copy(
            g_hbm.at[:, :, rows_at(tile, part)], lefts.at[slot], left_sem.at[slot]
        )

    def weight_grad(tile):
        left(tile).wait()
        pl.when(tile + 1 < width // part)(lambda: left(tile + 1).start())
        slot = lax.rem(tile, 2)
        got = contract_rows(lefts[slot, 0], a_ref[0])
        for batch in range(1, batches):
            got = got + contract_rows(lefts[slot, batch], a_ref[batch])
        parts[rows_at(tile, part), :] = to_half(got)

    def to_seq(peer, place):
        return pltpu.make_async_remote_copy(
            src_ref=parts.at[rows_at(peer, run)],
            dst_ref=sums.at[place],
            send_sem=part_send.at[peer],
            recv_sem=part_recv.at[place],
            device_id={"seq": peer},
            device_id_type=MESH,
        )

    def others(count, me, act):
        pl.loop(1, count)(lambda ahead: act(lax.rem(me + ahead, count)))

    def product(slot, tile):
        return dot_nt(left_rows(a_ref, slot, rows), w_ref[rows_at(tile, TILE), :])

    left(0).start()
    meet(greet_group(group) + greet_seq(seqs))
    reduce = Reduce(
        line, product, total, acc, cross_out, line_out, cross_in, line_in, sum_send, sum_recv
    )
    count = width // part
    per = -(-count // (2 * chips - 3))

    @pl.loop(0, 2 * chips - 3)
    def _(step):
        reduce.step(step)

        @pl.loop(0, per)
        def _(turn):
            tile = step * per + turn
            pl.when(tile < count)(lambda: weight_grad(tile))

    others(seqs, seq, lambda peer: to_seq(peer, seq).start())
    pl.loop(2 * chips - 3, 2 * chips - 1)(reduce.step)

    def put(here, d_values):
        grad_ref[here, :] = dm_ref[here, :] + d_values

    norm_back(rows, v_ref, total, gain_ref, gain_acc, put)
    fold = 128 // share
    near = group // fold
    attn_row = jnp.sum(gain_acc[...], axis=0, keepdims=True)
    mlp_row = jnp.sum(mlp_gain_ref[...], axis=0, keepdims=True)
    gain_out[...] = jnp.zeros_like(gain_out)
    for place in range(width // 128):
        lanes = slice(place * 128, (place + 1) * 128)
        gain_out[place % near, place // near, 0:1, :] = attn_row[:, lanes]
        gain_out[place % near, place // near, 1:2, :] = mlp_row[:, lanes]

    def gain_group(peer, member):
        return pltpu.make_async_remote_copy(
            src_ref=gain_out.at[peer // fold],
            dst_ref=gain_in.at[member],
            send_sem=gain_send.at[peer],
            recv_sem=gain_recv.at[member],
            device_id={"fsdp": peer},
            device_id_type=MESH,
        )

    def gain_seq(peer, place):
        return pltpu.make_async_remote_copy(
            src_ref=gain_sum.at[peer],
            dst_ref=gain_back.at[place],
            send_sem=back_send.at[peer],
            recv_sem=back_recv.at[place],
            device_id={"seq": peer},
            device_id_type=MESH,
        )

    def block_swap(peer, member):
        return pltpu.make_async_remote_copy(
            src_ref=parts.at[rows_at(seq * group + peer, share)],
            dst_ref=cols.at[member],
            send_sem=cols_send.at[peer],
            recv_sem=cols_recv.at[member],
            device_id={"fsdp": peer},
            device_id_type=MESH,
        )

    others(group, own, lambda peer: gain_group(peer, own).start())
    gain_in[own] = gain_out[own // fold]
    others(seqs, seq, lambda peer: to_seq(peer, peer).wait_recv())

    @pl.loop(0, run // 64)
    def _(chunk):
        here = rows_at(chunk, 64)
        there = pl.ds(pl.multiple_of(seq * run + chunk * 64, 64), 64)
        added = parts[there, :].astype(jnp.float32)
        for place in range(seqs):
            piece = sums[place, here, :].astype(jnp.float32)
            added = added + jnp.where(place == seq, 0.0, piece)
        parts[there, :] = to_half(added)

    others(group, own, lambda peer: block_swap(peer, own).start())
    cols[own] = parts[rows_at(seq * group + own, share), :]
    others(group, own, lambda peer: gain_group(peer, peer).wait_recv())
    gain_sum[...] = jnp.sum(gain_in[...], axis=0)
    others(seqs, seq, lambda peer: gain_seq(peer, seq).start())
    gain_back[seq] = gain_sum[seq]
    others(seqs, seq, lambda peer: gain_seq(peer, peer).wait_recv())
    tile_ref[...] = jnp.sum(gain_back[...], axis=0)
    others(group, own, lambda peer: block_swap(peer, peer).wait_recv())
    kept = pltpu.make_async_copy(cols, cols_ref, cols_keep)
    kept.start()
    reduce.sent()
    others(seqs, seq, lambda peer: to_seq(peer, seq).wait_send())
    others(group, own, lambda peer: gain_group(peer, own).wait_send())
    others(group, own, lambda peer: block_swap(peer, own).wait_send())
    others(seqs, seq, lambda peer: gain_seq(peer, seq).wait_send())
    kept.wait()


def heads_back(seqs, chips, a, w, group_a, x, d_middle, gain, mlp_gain, collective):
    rows, width = x.shape
    batches, length, depth = a.shape
    group = 2 * chips
    share = width // seqs // group
    near = group // (128 // share)
    half = jnp.bfloat16
    part = 256 if batches * length <= 2048 else 128
    return pl.pallas_call(
        functools.partial(heads_back_kernel, seqs, chips),
        out_shape=[
            jax.ShapeDtypeStruct((rows, width), jnp.float32),
            jax.ShapeDtypeStruct((group, share, depth), half),
            jax.ShapeDtypeStruct((8, 128), jnp.float32),
        ],
        in_specs=[VMEM_SPEC, VMEM_SPEC, ANY_SPEC] + [VMEM_SPEC] * 4,
        out_specs=[VMEM_SPEC, ANY_SPEC, VMEM_SPEC],
        scratch_shapes=[
            pltpu.VMEM((rows, width), jnp.float32),
            pltpu.VMEM((8, width), jnp.float32),
            pltpu.VMEM((2, batches, length, part), half),
            pltpu.VMEM((width, depth), half),
            pltpu.VMEM((seqs, width // seqs, depth), half),
            pltpu.VMEM((group, share, depth), half),
            pltpu.VMEM((near, seqs, 8, 128), jnp.float32),
            pltpu.VMEM((group, seqs, 8, 128), jnp.float32),
            pltpu.VMEM((seqs, 8, 128), jnp.float32),
            pltpu.VMEM((seqs, 8, 128), jnp.float32),
            sems(2),
            sems(seqs),
            sems(seqs),
            sems(group),
            sems(group),
            pltpu.SemaphoreType.DMA,
            sems(group),
            sems(group),
            sems(seqs),
            sems(seqs),
        ]
        + Reduce.scratch(chips, rows, width),
        compiler_params=comm_params(collective, 60),
        cost_estimate=cost(
            4 * group * rows * width * depth, 200 * MIB, 2 * group * rows * width * 2
        ),
        name="heads_back",
    )(a, w, group_a, x, d_middle, gain, mlp_gain)


def doc_starts(lengths, positions, batches, seq_len):
    table = lengths.reshape(batches, -1, lengths.shape[1])
    starts = jnp.cumsum(table, axis=2) - table
    per_batch = seq_len // table.shape[1]
    begins = (starts + (jnp.arange(table.shape[1], dtype=jnp.int32) * per_batch)[None, :, None]).reshape(
        batches, -1
    )
    before = begins[:, None, :] <= positions[None, :, None]
    return jnp.max(jnp.where(before, begins[:, None, :], 0), axis=2)


def body(
    tokens,
    cotangent,
    lengths,
    gain_attn,
    w_query,
    w_key,
    w_value,
    w_out,
    gain_mlp,
    w_gate,
    w_up,
    w_down,
):
    batches, piece, width = tokens.shape
    seqs = lax.axis_size("seq")
    group = lax.axis_size("fsdp")
    chips = group // 2
    devices = seqs * group
    seq_len = piece * devices
    rows = batches * piece
    share = w_query.shape[0]
    span = width // group
    length = group * piece
    aligned = share == HEAD
    member = lax.axis_index("fsdp")

    def blocks(weight):
        part = weight.shape[1] // devices
        if part < HEAD:
            return weight.reshape(share, group, -1).transpose(1, 0, 2)
        return weight.reshape(share, seqs, group, part).transpose(2, 0, 1, 3).reshape(group, share, -1)

    def unblock(cols, total):
        part = total // devices
        if part < HEAD:
            return cols.transpose(1, 0, 2).reshape(share, total)
        return cols.reshape(group, share, seqs, part).transpose(1, 2, 0, 3).reshape(share, total)

    inputs = tokens.astype(jnp.float32).reshape(rows, width)
    wd_part = lax.all_gather(w_down, "seq", axis=0, tiled=True)
    if aligned:
        wo_part = lax.all_gather(w_out, "seq", axis=0, tiled=True)
    else:
        wo_all = lax.all_gather(w_out, ("seq", "fsdp"), axis=0, tiled=True)
        wo_part = lax.dynamic_slice_in_dim(wo_all, member * span, span, 0)

    attn_blocks = jnp.concatenate([blocks(w_query), blocks(w_key), blocks(w_value)], axis=2)
    unit_blocks = jnp.concatenate([blocks(w_gate), blocks(w_up)], axis=2)
    group_start = lax.axis_index("seq") * length
    positions = group_start + jnp.arange(length, dtype=jnp.int32)
    begins = doc_starts(lengths, positions, batches, seq_len)
    at = jnp.arange(length, dtype=jnp.int32)
    block = min(256, length)
    low = jnp.maximum(begins - group_start + WINDOW, at[None, :] + 1) - (at // block * block)[None, :]
    low = low[:, None, :]

    lane = jnp.arange(128, dtype=jnp.int32)
    device = lax.axis_index("seq") * group + member
    fold = 128 // share
    here = lane // share == lax.rem(device, fold)
    both = jnp.stack([gain_attn, gain_mlp]).astype(jnp.float32)
    tile = jnp.where(here[None], jnp.tile(both, (1, fold)), 0.0)
    tile = jnp.pad(tile, ((0, 6), (0, 0)))[None]
    group_a, query, key_value, gains, w_heads = start(
        seqs, chips, batches, tile, tokens.reshape(rows, width), attn_blocks, 1
    )
    gains = gains.transpose(1, 0, 2, 3).reshape(devices // fold, fold, 8, 128).sum(axis=1)
    gain_one = gains[:, 0].reshape(width)
    gain_two = gains[:, 1].reshape(width)
    attended, lse, kv_pad, unit_own = attend(
        seqs, group, query, key_value, low, block, unit_blocks, 2
    )
    branch, group_d, w_units = branch_sum(
        seqs, chips, attended, wo_part, cotangent.reshape(rows, width),
        unit_own.reshape(group * share, -1), 3,
    )
    w_units = w_units.reshape(width, -1)
    middle = inputs + branch
    normed_b = to_half(normalize(middle, gain_two))
    group_b, hidden, d_units = hidden_units(chips, normed_b, w_units, wd_part, group_d, 4)
    d_middle, d_branch, mlp_gain_part, unit_part = units_back(
        chips, d_units, w_units, group_b, middle, cotangent.reshape(rows, width), gain_two[None], 5
    )

    def over_seq(values):
        return lax.psum_scatter(values, "seq", scatter_dimension=0, tiled=True)

    unit_sums = over_seq(unit_part).reshape(group, share, -1)
    d_attended, mlp_out, out_grad, down_grad = branch_back(
        chips, batches, d_branch, wo_part, attended, hidden, wd_part, group_d, 6
    )
    outputs = middle + mlp_out
    down_sum = over_seq(down_grad)
    d_heads, unit_cols = attend_back(
        seqs, group, query, kv_pad, low, lse, d_attended, block, unit_sums, 7
    )
    if aligned:
        out_sum = over_seq(out_grad)
    else:
        whole = lax.dynamic_update_slice_in_dim(
            jnp.zeros((width, width), jnp.bfloat16), out_grad, member * span, 0
        )
        out_sum = lax.psum_scatter(whole, ("seq", "fsdp"), scatter_dimension=0, tiled=True)
    input_grad, head_cols, gain_tile = heads_back(
        seqs, chips, d_heads, w_heads, group_a, tokens.reshape(rows, width), d_middle,
        gain_one[None], mlp_gain_part, 8,
    )
    input_grad = input_grad.reshape(batches, piece, width)
    layer_out = to_half(outputs).reshape(batches, piece, width)
    gain_grads = lax.dynamic_slice_in_dim(gain_tile[:2], lax.rem(device, fold) * share, share, 1)

    def whole_rows(cols, part, total):
        size = total // group
        return unblock(cols[:, :, part * size : (part + 1) * size], total).astype(jnp.float32)

    return (
        layer_out,
        input_grad,
        gain_grads[0],
        whole_rows(head_cols, 0, width),
        whole_rows(head_cols, 1, width),
        whole_rows(head_cols, 2, width),
        out_sum.astype(jnp.float32),
        gain_grads[1],
        whole_rows(unit_cols, 0, FF),
        whole_rows(unit_cols, 1, FF),
        down_sum.astype(jnp.float32),
    )


def solution(mesh):
    spread = ("seq", "fsdp")
    tokens, rows, gains = P(None, spread, None), P(spread, None), P(spread)
    in_specs = (tokens, tokens, P(), gains, rows, rows, rows, rows, gains, rows, rows, rows)
    out_specs = (tokens, tokens, gains, rows, rows, rows, rows, gains, rows, rows, rows)
    return jax.shard_map(body, mesh=mesh, in_specs=in_specs, out_specs=out_specs, check_vma=False)
```

```python
import functools

import jax
import jax.numpy as jnp
from jax import lax
from jax.experimental import pallas as pl
from jax.experimental.pallas import tpu as pltpu
from jax.sharding import PartitionSpec as P

HEAD = 64
FF = 8192
WINDOW = 1024
PAIR = 128
TILE = 512
LOW = -1e30
EPS = 1e-05
MESH = pl.DeviceIdType.MESH
MIB = 2**20


def to_half(values):
    return values.astype(jnp.bfloat16)


def normalize(values, gain):
    return values * lax.rsqrt(jnp.mean(values * values, axis=-1, keepdims=True) + EPS) * gain


def contract_rows(left, right):
    return lax.dot_general(
        left, right, (((0,), (0,)), ((), ())), preferred_element_type=jnp.float32
    )


def dot_nt(left, right):
    return lax.dot_general(
        left, right, (((1,), (1,)), ((), ())), preferred_element_type=jnp.float32
    )


def dot_nn(left, right):
    return jnp.dot(left, right, preferred_element_type=jnp.float32)


def head_lanes(values, half):
    lane = lax.broadcasted_iota(jnp.int32, values.shape, 1)
    return jnp.where((lane >= HEAD) == (half == 1), values, jnp.zeros_like(values))


def masked_scores(k_rows, q_head, low):
    keys, block = k_rows.shape[0], q_head.shape[0]
    scores = dot_nt(k_rows, q_head)
    at = lax.broadcasted_iota(jnp.int32, (keys, block), 0)
    query = lax.broadcasted_iota(jnp.int32, (keys, block), 1)
    seen = (at >= low) & (at <= query + WINDOW)
    return jnp.where(seen, scores, LOW)


class Line:
    def __init__(self, chips):
        self.chips = chips
        self.own = lax.axis_index("fsdp")
        self.chip = self.own // 2
        self.core = lax.rem(self.own, 2)
        self.other = self.own + 1 - 2 * self.core
        self.has_left = self.chip > 0
        self.has_right = self.chip < chips - 1

    def greet(self):
        signal_group(self.other)
        pl.when(self.has_left)(lambda: signal_group(self.own - 2))
        pl.when(self.has_right)(lambda: signal_group(self.own + 2))
        return 1 + self.has_left.astype(jnp.int32) + self.has_right.astype(jnp.int32)


def signal_group(peer):
    barrier = pltpu.get_barrier_semaphore()
    pl.semaphore_signal(barrier, inc=1, device_id={"fsdp": peer}, device_id_type=MESH)


def signal_seq(peer):
    barrier = pltpu.get_barrier_semaphore()
    pl.semaphore_signal(barrier, inc=1, device_id={"seq": peer}, device_id_type=MESH)


def greet_group(group):
    own = lax.axis_index("fsdp")
    pl.loop(1, group)(lambda ahead: signal_group(lax.rem(own + ahead, group)))
    return group - 1


def greet_seq(seqs):
    own = lax.axis_index("seq")
    pl.loop(1, seqs)(lambda ahead: signal_seq(lax.rem(own + ahead, seqs)))
    return seqs - 1


def meet(count):
    pl.semaphore_wait(pltpu.get_barrier_semaphore(), count)


def rows_at(index, size):
    return pl.ds(pl.multiple_of(index * size, size), size)


class Spread:
    def __init__(self, line, first, buf, send, recv):
        self.line, self.first, self.buf, self.send, self.recv = line, first, buf, send, recv

    def move(self, slot, way, peer, source=None):
        return pltpu.make_async_remote_copy(
            src_ref=self.buf.at[slot] if source is None else source,
            dst_ref=self.buf.at[slot],
            send_sem=self.send.at[way, slot],
            recv_sem=self.recv.at[slot],
            device_id={"fsdp": peer},
            device_id_type=MESH,
        )

    def begin(self):
        line = self.line
        pl.when(line.has_right)(lambda: self.move(line.own, 1, line.own + 2, self.first).start())
        pl.when(line.has_left)(lambda: self.move(line.own, 0, line.own - 2, self.first).start())
        self.move(line.own, 2, line.other, self.first).start()

    def relay(self, far):
        line = self.line

        @pl.when(line.chip - far >= 0)
        def _():
            slot = (line.chip - far) * 2 + line.core
            self.move(slot, 1, line.own).wait_recv()
            pl.when(line.has_right)(lambda: self.move(slot, 1, line.own + 2).start())
            self.move(slot, 2, line.other).start()

        @pl.when(line.chip + far < line.chips)
        def _():
            slot = (line.chip + far) * 2 + line.core
            self.move(slot, 0, line.own).wait_recv()
            pl.when(line.has_left)(lambda: self.move(slot, 0, line.own - 2).start())
            self.move(slot, 2, line.other).start()

    def each(self, far, use):
        line = self.line

        @pl.loop(0, 4)
        def _(turn):
            side = lax.rem(turn, 2)
            across = turn // 2
            away = far - across
            source = line.chip + away * (2 * side - 1)
            valid = (away >= 0) & (away < line.chips) & (source >= 0) & (source < line.chips)
            valid = valid & ((side == 0) | (away > 0))

            @pl.when(valid)
            def _():
                slot = source * 2 + line.core + across * (1 - 2 * line.core)
                pl.when(across == 1)(lambda: self.move(slot, 2, line.own).wait_recv())
                use(slot)

    def whole(self, use):
        @pl.loop(0, self.line.chips + 1)
        def _(far):
            pl.when(far > 0)(lambda: self.relay(far))
            self.each(far, use)

    def rest(self):
        pl.loop(0, self.line.chips)(
            lambda place: self.move(place * 2 + 1 - self.line.core, 2, self.line.own).wait_recv()
        )

    def sent(self):
        line = self.line

        @pl.loop(0, line.chips)
        def _(place):
            slot = place * 2 + line.core
            self.move(slot, 2, line.other).wait_send()
            pl.when(line.has_right & (place <= line.chip))(
                lambda: self.move(slot, 1, line.own + 2).wait_send()
            )
            pl.when(line.has_left & (place >= line.chip))(
                lambda: self.move(slot, 0, line.own - 2).wait_send()
            )


class Reduce:
    def __init__(self, line, product, out, acc, cross_out, line_out, cross_in, line_in, send, recv):
        self.line, self.product, self.out, self.acc = line, product, out, acc
        self.cross_out, self.line_out, self.cross_in, self.line_in = cross_out, line_out, cross_in, line_in
        self.send, self.recv = send, recv

    @staticmethod
    def scratch(chips, rows, width):
        part = pltpu.VMEM((chips, rows, width), jnp.bfloat16)
        return [
            pltpu.VMEM((rows, width), jnp.float32),
            pltpu.VMEM((rows, width), jnp.bfloat16),
            part,
            part,
            pltpu.VMEM((chips + 1, rows, width), jnp.bfloat16),
            pltpu.SemaphoreType.DMA((2, chips)),
            pltpu.SemaphoreType.DMA((2, chips + 1)),
        ]

    def cross(self, place):
        return pltpu.make_async_remote_copy(
            src_ref=self.cross_out,
            dst_ref=self.cross_in.at[place],
            send_sem=self.send.at[0, place],
            recv_sem=self.recv.at[0, place],
            device_id={"fsdp": self.line.other},
            device_id_type=MESH,
        )

    def along(self, place, landing, peer):
        return pltpu.make_async_remote_copy(
            src_ref=self.line_out.at[place],
            dst_ref=self.line_in.at[landing],
            send_sem=self.send.at[1, place],
            recv_sem=self.recv.at[1, landing],
            device_id={"fsdp": peer},
            device_id_type=MESH,
        )

    def steps(self):
        return 2 * self.line.chips - 1

    def step(self, step):
        line, acc = self.line, self.acc
        tiles = acc.shape[1] // TILE
        away = line.chips - 1 - step // 2
        side = lax.rem(step, 2)
        place = line.chip + away * (1 - 2 * side)

        @pl.when((place >= 0) & (place < line.chips))
        def _():
            @pl.loop(0, tiles)
            def _(tile):
                got = self.product(place * 2 + 1 - line.core, tile)
                self.cross_out[:, rows_at(tile, TILE)] = to_half(got)

            self.cross(place).start()

            @pl.loop(0, tiles)
            def _(tile):
                acc[:, rows_at(tile, TILE)] = self.product(place * 2 + line.core, tile)

            self.cross(place).wait()

            @pl.when(away > 0)
            def _():
                rightward = side == 0
                upstream = (rightward & line.has_left) | (jnp.logical_not(rightward) & line.has_right)

                @pl.when(upstream)
                def _():
                    self.along(place, place, line.own).wait_recv()
                    self.line_out[place] = to_half(
                        acc[...]
                        + self.cross_in[place].astype(jnp.float32)
                        + self.line_in[place].astype(jnp.float32)
                    )

                @pl.when(jnp.logical_not(upstream))
                def _():
                    self.line_out[place] = to_half(
                        acc[...] + self.cross_in[place].astype(jnp.float32)
                    )

                @pl.when(rightward)
                def _():
                    self.along(place, place, line.own + 2).start()

                @pl.when(jnp.logical_not(rightward))
                def _():
                    landing = jnp.where(away == 1, line.chips, place)
                    self.along(place, landing, line.own - 2).start()

            @pl.when(away == 0)
            def _():
                self.out[...] = acc[...] + self.cross_in[place].astype(jnp.float32)

                @pl.when(line.has_left)
                def _():
                    self.along(place, place, line.own).wait_recv()
                    self.out[...] += self.line_in[place].astype(jnp.float32)

                @pl.when(line.has_right)
                def _():
                    self.along(place, line.chips, line.own).wait_recv()
                    self.out[...] += self.line_in[line.chips].astype(jnp.float32)

    def sent(self):
        @pl.loop(0, self.line.chips)
        def _(place):
            pl.when(place != self.line.chip)(
                lambda: self.along(place, place, self.line.own).wait_send()
            )


class Swap:
    def __init__(self, group, source, target, send, recv, keep):
        self.group, self.source, self.target = group, source, target
        self.send, self.recv, self.keep = send, recv, keep
        self.own = lax.axis_index("fsdp")

    def move(self, peer, source):
        return pltpu.make_async_remote_copy(
            src_ref=self.source.at[peer],
            dst_ref=self.target.at[source],
            send_sem=self.send.at[peer],
            recv_sem=self.recv.at[source],
            device_id={"fsdp": peer},
            device_id_type=MESH,
        )

    def kept(self):
        return pltpu.make_async_copy(self.source.at[self.own], self.target.at[self.own], self.keep)

    def begin(self):
        self.kept().start()
        pl.loop(1, self.group)(
            lambda ahead: self.move(lax.rem(self.own + ahead, self.group), self.own).start()
        )

    def end(self):
        self.kept().wait()

        @pl.loop(1, self.group)
        def _(ahead):
            peer = lax.rem(self.own + ahead, self.group)
            self.move(peer, peer).wait_recv()
            self.move(peer, self.own).wait_send()


class Share:
    def __init__(self, seqs, source, target, send, recv, keep):
        self.seqs, self.source, self.target = seqs, source, target
        self.send, self.recv, self.keep = send, recv, keep
        self.own = lax.axis_index("seq")

    def move(self, peer, place):
        return pltpu.make_async_remote_copy(
            src_ref=self.source,
            dst_ref=self.target.at[place],
            send_sem=self.send.at[peer],
            recv_sem=self.recv.at[place],
            device_id={"seq": peer},
            device_id_type=MESH,
        )

    def kept(self):
        return pltpu.make_async_copy(self.source, self.target.at[self.own], self.keep)

    def begin(self):
        self.kept().start()
        pl.loop(1, self.seqs)(
            lambda ahead: self.move(lax.rem(self.own + ahead, self.seqs), self.own).start()
        )

    def end(self):
        self.kept().wait()

        @pl.loop(1, self.seqs)
        def _(ahead):
            peer = lax.rem(self.own + ahead, self.seqs)
            self.move(peer, peer).wait_recv()
            self.move(peer, self.own).wait_send()


class ToSeq:
    def __init__(self, seqs, source, target, send, recv):
        self.seqs, self.source, self.target, self.send, self.recv = seqs, source, target, send, recv
        self.own = lax.axis_index("seq")

    def move(self, peer, place):
        return pltpu.make_async_remote_copy(
            src_ref=self.source.at[rows_at(peer, self.target.shape[1])],
            dst_ref=self.target.at[place],
            send_sem=self.send.at[peer],
            recv_sem=self.recv.at[place],
            device_id={"seq": peer},
            device_id_type=MESH,
        )

    def begin(self):
        pl.loop(1, self.seqs)(
            lambda ahead: self.move(lax.rem(self.own + ahead, self.seqs), self.own).start()
        )

    def arrived(self):
        @pl.loop(1, self.seqs)
        def _(ahead):
            peer = lax.rem(self.own + ahead, self.seqs)
            self.move(peer, peer).wait_recv()

    def sent(self):
        @pl.loop(1, self.seqs)
        def _(ahead):
            peer = lax.rem(self.own + ahead, self.seqs)
            self.move(peer, self.own).wait_send()

    def end(self):
        self.arrived()
        self.sent()


VMEM_SPEC = pl.BlockSpec(memory_space=pltpu.VMEM)
ANY_SPEC = pl.BlockSpec(memory_space=pl.ANY)


def comm_params(collective, mib=58):
    return pltpu.CompilerParams(
        collective_id=collective, has_side_effects=True, vmem_limit_bytes=mib * MIB
    )


def cost(flops, local, remote):
    return pl.CostEstimate(
        flops=flops, bytes_accessed=local, transcendentals=0, remote_bytes_transferred=remote
    )


def sems(*shape):
    return pltpu.SemaphoreType.DMA(shape)


def left_rows(a_ref, slot, rows):
    if len(a_ref.shape) == 2:
        return a_ref[rows_at(slot, rows), :]
    piece = rows // a_ref.shape[0]
    return jnp.concatenate(
        [a_ref[batch, rows_at(slot, piece), :] for batch in range(a_ref.shape[0])], axis=0
    )


def norm_back(rows, v_ref, e_ref, gain_ref, gain_acc, put):
    gain_acc[...] = jnp.zeros_like(gain_acc)

    @pl.loop(0, rows // 16)
    def _(chunk):
        here = rows_at(chunk, 16)
        values = v_ref[here, :].astype(jnp.float32)
        error = e_ref[here, :]
        rate = lax.rsqrt(jnp.mean(values * values, axis=-1, keepdims=True) + EPS)
        unit = values * rate
        product = error * unit
        gain = gain_ref[0:1, :]
        mean = jnp.mean(product * gain, axis=-1, keepdims=True)
        gain_acc[...] += product[0:8] + product[8:16]
        put(here, rate * (gain * error - unit * mean))


def start_kernel(
    seqs, chips, batches, tile_ref, x_ref, blocks_ref, g_ref, q_ref, pad_ref, gains_ref, w_out_ref,
    buf, normed, kv_ref, zeros, halo_send, halo_recv, pad_keep, gain, gains, w, send, recv, keep, swap_send, share_send, w_recv,
    tile_send, tile_across, tile_recv, tile_back, w_keep, gain_keep,
):
    line = Line(chips)
    group = 2 * chips
    seq = lax.axis_index("seq")
    own = line.own
    share = blocks_ref.shape[1]
    piece = x_ref.shape[0] // batches
    span = q_ref.shape[2]
    width = x_ref.shape[1]
    per = 128 * seqs * group // width
    length = group * piece
    first = length - WINDOW
    has_left, has_right = seq > 0, seq < seqs - 1
    meet(greet_group(group) + greet_seq(seqs))

    def block_at(run, member):
        return w.at[rows_at(run * group + member, share)]

    def block_swap(peer, member):
        return pltpu.make_async_remote_copy(
            src_ref=blocks_ref.at[peer],
            dst_ref=block_at(seq, member),
            send_sem=swap_send.at[peer],
            recv_sem=w_recv.at[seq, member],
            device_id={"fsdp": peer},
            device_id_type=MESH,
        )

    def block_share(run, member, peer):
        return pltpu.make_async_remote_copy(
            src_ref=block_at(run, member),
            dst_ref=block_at(run, member),
            send_sem=share_send.at[peer, member],
            recv_sem=w_recv.at[run, member],
            device_id={"seq": peer},
            device_id_type=MESH,
        )

    def tile_to_seq(peer, place):
        return pltpu.make_async_remote_copy(
            src_ref=tile_ref.at[0],
            dst_ref=gains.at[own, place],
            send_sem=tile_send.at[peer],
            recv_sem=tile_recv.at[place],
            device_id={"seq": peer},
            device_id_type=MESH,
        )

    def tiles_to_group(peer, member):
        return pltpu.make_async_remote_copy(
            src_ref=gains.at[member],
            dst_ref=gains.at[member],
            send_sem=tile_across.at[peer],
            recv_sem=tile_back.at[member],
            device_id={"fsdp": peer},
            device_id_type=MESH,
        )

    def others(count, me, act):
        pl.loop(1, count)(lambda ahead: act(lax.rem(me + ahead, count)))

    others(seqs, seq, lambda peer: tile_to_seq(peer, seq).start())
    others(group, own, lambda peer: block_swap(peer, own).start())
    spread = Spread(line, x_ref, buf, send, recv)
    spread.begin()
    gains[own, seq] = tile_ref[0]
    w[rows_at(seq * group + own, share), :] = blocks_ref[own]
    others(seqs, seq, lambda peer: block_share(seq, own, peer).start())
    buf[own] = x_ref[...]
    others(seqs, seq, lambda peer: tile_to_seq(peer, peer).wait_recv())
    others(group, own, lambda peer: tiles_to_group(peer, own).start())

    def pass_block(member):
        block_swap(member, member).wait_recv()
        others(seqs, seq, lambda peer: block_share(seq, member, peer).start())

    others(group, own, pass_block)
    others(group, own, lambda peer: tiles_to_group(peer, peer).wait_recv())
    for column in range(width // 128):
        total = 0.0
        for place in range(column * per, (column + 1) * per):
            total = total + gains[place % group, place // group, 0:1, :]
        gain[0:1, column * 128 : (column + 1) * 128] = total

    def kept(slot, batch):
        return pltpu.make_async_copy(
            normed.at[slot, pl.ds(batch * piece, piece)],
            g_ref.at[batch, rows_at(slot, piece)],
            keep.at[slot, batch],
        )

    def own_rows(slot, batch):
        there = pl.ds(pl.multiple_of(slot * piece + WINDOW, piece), piece)
        return pltpu.make_async_copy(
            kv_ref.at[batch, rows_at(slot, piece)],
            pad_ref.at[batch, there],
            pad_keep.at[slot, batch],
        )

    def no_rows(place, batch):
        return pltpu.make_async_copy(
            zeros, pad_ref.at[batch, rows_at(place, piece)], halo_recv.at[place, batch]
        )

    def halo(slot, batch, peer):
        there = pl.ds(pl.multiple_of(slot * piece - first, piece), piece)
        return pltpu.make_async_remote_copy(
            src_ref=kv_ref.at[batch, rows_at(slot, piece)],
            dst_ref=pad_ref.at[batch, there],
            send_sem=halo_send.at[slot, batch],
            recv_sem=halo_recv.at[slot - first // piece, batch],
            device_id={"seq": peer},
            device_id_type=MESH,
        )

    @pl.when(jnp.logical_not(has_left))
    def _():
        zeros[...] = jnp.zeros_like(zeros)

        @pl.loop(0, WINDOW // piece)
        def _(place):
            for batch in range(batches):
                no_rows(place, batch).start()

    def use(slot):
        @pl.loop(0, x_ref.shape[0] // 16)
        def _(chunk):
            rows = rows_at(chunk, 16)
            values = buf[slot, rows, :].astype(jnp.float32)
            normed[slot, rows, :] = to_half(normalize(values, gain[0:1, :]))

        for batch in range(batches):
            kept(slot, batch).start()
        rows = rows_at(slot, piece)
        values = normed[slot]
        for part in range(3):
            got = to_half(dot_nn(values, w[:, part * span : (part + 1) * span]))
            for batch in range(batches):
                mine = got[batch * piece : (batch + 1) * piece]
                if part == 0:
                    q_ref[batch, rows, :] = mine
                else:
                    kv_ref[batch, rows, (part - 1) * span : part * span] = mine
        for batch in range(batches):
            own_rows(slot, batch).start()

        @pl.when(has_right & (slot * piece >= first))
        def _():
            for batch in range(batches):
                halo(slot, batch, seq + 1).start()

    pl.loop(1, chips - 1)(spread.relay)

    def have_block(run, member):
        block_share(run, member, seq).wait_recv()

    others(seqs, seq, lambda run: pl.loop(0, group)(lambda member: have_block(run, member)))
    w_kept = pltpu.make_async_copy(w, w_out_ref, w_keep)
    w_kept.start()
    gains_kept = pltpu.make_async_copy(gains, gains_ref, gain_keep)
    gains_kept.start()

    pl.loop(0, chips - 1)(lambda far: spread.each(far, use))
    spread.relay(chips - 1)
    spread.each(chips - 1, use)
    spread.each(chips, use)
    spread.sent()
    others(seqs, seq, lambda peer: tile_to_seq(peer, seq).wait_send())
    others(group, own, lambda peer: block_swap(peer, own).wait_send())
    others(group, own, lambda peer: tiles_to_group(peer, own).wait_send())
    others(
        seqs,
        seq,
        lambda peer: pl.loop(0, group)(lambda member: block_share(seq, member, peer).wait_send()),
    )
    w_kept.wait()
    gains_kept.wait()

    @pl.loop(0, group)
    def _(slot):
        for batch in range(batches):
            kept(slot, batch).wait()
            own_rows(slot, batch).wait()

    @pl.loop(0, WINDOW // piece)
    def _(place):
        slot = place + first // piece
        for batch in range(batches):
            pl.when(has_right)(lambda batch=batch: halo(slot, batch, seq).wait_send())
            pl.when(has_left)(lambda batch=batch: halo(slot, batch, seq).wait_recv())
            pl.when(jnp.logical_not(has_left))(lambda batch=batch: no_rows(place, batch).wait())


def start(seqs, chips, batches, tile, x, blocks, collective):
    rows, width = x.shape
    group = 2 * chips
    length = group * rows // batches
    share, cols = blocks.shape[1:]
    span = cols // 3
    half = jnp.bfloat16
    return pl.pallas_call(
        functools.partial(start_kernel, seqs, chips, batches),
        out_shape=[
            jax.ShapeDtypeStruct((batches, length, width), half),
            jax.ShapeDtypeStruct((batches, length, span), half),
            jax.ShapeDtypeStruct((batches, length + WINDOW, 2 * span), half),
            jax.ShapeDtypeStruct((group, seqs, 8, 128), jnp.float32),
            jax.ShapeDtypeStruct((width, cols), half),
        ],
        in_specs=[VMEM_SPEC] * 3,
        out_specs=[ANY_SPEC, VMEM_SPEC, ANY_SPEC, ANY_SPEC, ANY_SPEC],
        scratch_shapes=[
            pltpu.VMEM((group, rows, width), half),
            pltpu.VMEM((group, rows, width), half),
            pltpu.VMEM((batches, length, 2 * span), half),
            pltpu.VMEM((rows // batches, 2 * span), half),
            sems(group, batches),
            sems(WINDOW * group // length, batches),
            sems(group, batches),
            pltpu.VMEM((8, width), jnp.float32),
            pltpu.VMEM((group, seqs, 8, 128), jnp.float32),
            pltpu.VMEM((width, cols), half),
            sems(3, group),
            sems(group),
            sems(group, batches),
            sems(group),
            sems(seqs, group),
            sems(seqs, group),
            sems(seqs),
            sems(group),
            sems(seqs),
            sems(group),
            pltpu.SemaphoreType.DMA,
            pltpu.SemaphoreType.DMA,
        ],
        compiler_params=comm_params(collective),
        cost_estimate=cost(2 * group * rows * width * cols, 200 * MIB, group * rows * width * 2),
        name="start",
    )(tile, x, blocks)


def attend_kernel(
    group, block, q_ref, pad, low_ref, units_ref, out_ref, lse_ref, own_units_ref,
    vt, swap_send, swap_recv, swap_keep,
):
    batches, length, span = q_ref.shape
    meet(greet_group(group))
    swap = Swap(group, units_ref, own_units_ref, swap_send, swap_recv, swap_keep)
    swap.begin()
    for batch in range(batches):
        vt[...] = pad[batch, :, span:].T

        @pl.loop(0, length // block)
        def _(step, batch=batch):
            begin = pl.multiple_of(step * block, block)
            keys = pl.ds(begin, block + WINDOW)
            rows = pl.ds(begin, block)
            low = low_ref[batch, :, rows]
            for pair in range(span // PAIR):
                lanes = slice(pair * PAIR, (pair + 1) * PAIR)
                q_pair = q_ref[batch, rows, lanes] * jnp.asarray(HEAD**-0.5, jnp.bfloat16)
                k_rows = pad[batch, keys, lanes]
                values = vt[lanes, keys]
                mixed = []
                for half in range(2):
                    scores = masked_scores(k_rows, head_lanes(q_pair, half), low)
                    top = jnp.max(scores, axis=0, keepdims=True)
                    expo = jnp.exp(scores - top)
                    total = jnp.sum(expo, axis=0, keepdims=True)
                    mixed.append(dot_nn(values, to_half(expo)) / total)
                    row = pair * 2 + half
                    lse_ref[batch, row : row + 1, rows] = top + jnp.log(total)
                lane = lax.broadcasted_iota(jnp.int32, mixed[0].shape, 0)
                out_ref[batch, rows, lanes] = to_half(jnp.where(lane < HEAD, mixed[0], mixed[1]).T)

    swap.end()


def attend(group, query, kv_pad, low, block, units, collective):
    batches, length, span = query.shape
    padded = kv_pad.shape[1]
    heads = span // HEAD
    half = jnp.bfloat16
    return pl.pallas_call(
        functools.partial(attend_kernel, group, block),
        in_specs=[VMEM_SPEC, VMEM_SPEC, VMEM_SPEC, ANY_SPEC],
        out_specs=[VMEM_SPEC, VMEM_SPEC, ANY_SPEC],
        out_shape=[
            jax.ShapeDtypeStruct((batches, length, span), half),
            jax.ShapeDtypeStruct((batches, heads, length), jnp.float32),
            jax.ShapeDtypeStruct(units.shape, half),
        ],
        scratch_shapes=[
            pltpu.VMEM((span, padded), half),
            sems(group),
            sems(group),
            pltpu.SemaphoreType.DMA,
        ],
        compiler_params=comm_params(collective),
        cost_estimate=cost(
            8 * batches * length * span * (WINDOW + block), 150 * MIB, units.size * 2
        ),
        name="attend",
    )(query, kv_pad, low, units)


def branch_kernel(
    seqs, chips, a_ref, w_ref, d_ref, units_ref, out_ref, gd_ref, w_units_ref,
    acc, cross_out, line_out, cross_in, line_in, sum_send, sum_recv,
    send, recv, d_keep, share_send, share_recv, share_keep,
):
    line = Line(chips)
    rows = out_ref.shape[0]

    def product(slot, tile):
        return dot_nn(left_rows(a_ref, slot, rows), w_ref[:, rows_at(tile, TILE)])

    meet(line.greet() + greet_seq(seqs))
    reduce = Reduce(
        line, product, out_ref, acc, cross_out, line_out, cross_in, line_in, sum_send, sum_recv
    )
    spread = Spread(line, d_ref, gd_ref, send, recv)
    units = Share(seqs, units_ref, w_units_ref, share_send, share_recv, share_keep)
    d_kept = pltpu.make_async_copy(d_ref, gd_ref.at[line.own], d_keep)
    units.begin()
    spread.begin()
    d_kept.start()

    @pl.loop(0, reduce.steps())
    def _(step):
        reduce.step(step)
        pl.when(lax.rem(step, 2) == 1)(lambda: spread.relay((step + 1) // 2))

    spread.rest()
    spread.sent()
    reduce.sent()
    d_kept.wait()
    units.end()


def branch_sum(seqs, chips, a, w, d_rows, units, collective):
    rows, width = d_rows.shape
    group = 2 * chips
    half = jnp.bfloat16
    return pl.pallas_call(
        functools.partial(branch_kernel, seqs, chips),
        out_shape=[
            jax.ShapeDtypeStruct((rows, width), jnp.float32),
            jax.ShapeDtypeStruct((group, rows, width), half),
            jax.ShapeDtypeStruct((seqs,) + units.shape, half),
        ],
        in_specs=[VMEM_SPEC, VMEM_SPEC, ANY_SPEC, ANY_SPEC],
        out_specs=[VMEM_SPEC, ANY_SPEC, ANY_SPEC],
        scratch_shapes=Reduce.scratch(chips, rows, width)
        + [sems(3, group), sems(group), pltpu.SemaphoreType.DMA]
        + [sems(seqs), sems(seqs), pltpu.SemaphoreType.DMA],
        compiler_params=comm_params(collective),
        cost_estimate=cost(
            2 * group * rows * width * w.shape[0], 250 * MIB, 3 * group * rows * width * 2
        ),
        name="branch_sum",
    )(a, w, d_rows, units)


def units_kernel(
    chips, x_ref, w_hbm, wd_hbm, gd_ref, g_ref, hidden_hbm, d_hbm,
    buf, d_buf, w_ref, wd_ref, hidden_ref, d_ref, send, recv, keep, d_sem, load, store,
):
    line = Line(chips)
    rows = x_ref.shape[0]
    units = hidden_ref.shape[1]
    part = min(units, 256)
    loads = [
        pltpu.make_async_copy(w_hbm, w_ref, load.at[0]),
        pltpu.make_async_copy(wd_hbm, wd_ref, load.at[1]),
    ]
    for item in loads:
        item.start()
    meet(line.greet())
    spread = Spread(line, x_ref, buf, send, recv)
    spread.begin()
    buf[line.own] = x_ref[...]
    for item in loads:
        item.wait()

    def kept(slot):
        place = rows_at(slot, rows)
        return [
            pltpu.make_async_copy(buf.at[slot], g_ref.at[slot], keep.at[slot]),
            pltpu.make_async_copy(hidden_ref.at[place], hidden_hbm.at[place], store.at[0, slot]),
            pltpu.make_async_copy(d_ref.at[place], d_hbm.at[place], store.at[1, slot]),
        ]

    def use(slot):
        fetch = pltpu.make_async_copy(gd_ref.at[slot], d_buf, d_sem)
        fetch.start()
        place = rows_at(slot, rows)
        fetch.wait()

        @pl.loop(0, units // part)
        def _(tile):
            here = rows_at(tile, part)
            there = rows_at(units // part + tile, part)
            values = buf[slot]
            gate = dot_nn(values, w_ref[:, here])
            up = dot_nn(values, w_ref[:, there])
            d_hidden = dot_nt(d_buf[...], wd_ref[here, :])
            sigma = jax.nn.sigmoid(gate)
            swish = gate * sigma
            hidden_ref[place, here] = to_half(swish * up)
            d_ref[place, here] = to_half(d_hidden * up * sigma * (1.0 + gate * (1.0 - sigma)))
            d_ref[place, there] = to_half(d_hidden * swish)

        for item in kept(slot):
            item.start()

    spread.whole(use)
    spread.sent()

    @pl.loop(0, 2 * chips)
    def _(slot):
        for item in kept(slot):
            item.wait()


def hidden_units(chips, x, w, wd, group_d, collective):
    rows, width = x.shape
    group = 2 * chips
    units = wd.shape[0]
    half = jnp.bfloat16
    return pl.pallas_call(
        functools.partial(units_kernel, chips),
        out_shape=[
            jax.ShapeDtypeStruct((group, rows, width), half),
            jax.ShapeDtypeStruct((group * rows, units), half),
            jax.ShapeDtypeStruct((group * rows, 2 * units), half),
        ],
        in_specs=[VMEM_SPEC, ANY_SPEC, ANY_SPEC, ANY_SPEC],
        out_specs=[ANY_SPEC, ANY_SPEC, ANY_SPEC],
        scratch_shapes=[
            pltpu.VMEM((group, rows, width), half),
            pltpu.VMEM((rows, width), half),
            pltpu.VMEM(w.shape, half),
            pltpu.VMEM(wd.shape, half),
            pltpu.VMEM((group * rows, units), half),
            pltpu.VMEM((group * rows, 2 * units), half),
            sems(3, group),
            sems(group),
            sems(group),
            pltpu.SemaphoreType.DMA,
            sems(2),
            sems(2, group),
        ],
        compiler_params=comm_params(collective),
        cost_estimate=cost(
            6 * group * rows * width * units, 200 * MIB, group * rows * width * 2
        ),
        name="hidden_units",
    )(x, w, wd, group_d)


def units_back_kernel(
    chips, a_hbm, w_hbm, b_hbm, v_ref, cot_ref, gain_ref, dm_ref, db_ref, gain_grad_ref, grad_hbm,
    a_ref, w_ref, total, lefts, tiles, load, left_sem, tile_sem,
    acc, cross_out, line_out, cross_in, line_in, sum_send, sum_recv,
):
    line = Line(chips)
    rows, width = v_ref.shape
    group = 2 * chips
    part = lefts.shape[2]
    loads = [
        pltpu.make_async_copy(w_hbm, w_ref, load.at[0]),
        pltpu.make_async_copy(a_hbm, a_ref, load.at[1]),
    ]
    for item in loads:
        item.start()

    def left(tile):
        slot = lax.rem(tile, 2)
        return pltpu.make_async_copy(
            b_hbm.at[:, rows_at(tile, part)], lefts.at[slot], left_sem.at[slot]
        )

    def stored(tile):
        slot = lax.rem(tile, 2)
        return pltpu.make_async_copy(
            tiles.at[slot], grad_hbm.at[rows_at(tile, part)], tile_sem.at[slot]
        )

    def weight_grad(tile):
        left(tile).wait()
        pl.when(tile + 1 < width // part)(lambda: left(tile + 1).start())
        pl.when(tile >= 2)(lambda: stored(tile - 2).wait())
        slot = lax.rem(tile, 2)
        size = min(TILE, a_ref.shape[1])

        @pl.loop(0, a_ref.shape[1] // size)
        def _(column):
            here = rows_at(column, size)
            tiles[slot, :, here] = to_half(contract_rows(lefts[slot], a_ref[:, here]))

        stored(tile).start()

    def product(slot, tile):
        return dot_nt(left_rows(a_ref, slot, rows), w_ref[rows_at(tile, TILE), :])

    meet(line.greet())
    left(0).start()
    for item in loads:
        item.wait()
    reduce = Reduce(
        line, product, total, acc, cross_out, line_out, cross_in, line_in, sum_send, sum_recv
    )
    count = width // part
    per = -(-count // reduce.steps())

    @pl.loop(0, reduce.steps())
    def _(step):
        reduce.step(step)

        @pl.loop(0, per)
        def _(turn):
            tile = step * per + turn
            pl.when(tile < count)(lambda: weight_grad(tile))

    def put(here, d_values):
        d_middle = cot_ref[here, :].astype(jnp.float32) + d_values
        dm_ref[here, :] = d_middle
        db_ref[here, :] = to_half(d_middle)

    norm_back(rows, v_ref, total, gain_ref, gain_grad_ref, put)
    reduce.sent()
    stored(count - 2).wait()
    stored(count - 1).wait()


def units_back(chips, a, w, b, middle, cot, gain, collective):
    rows, width = middle.shape
    group = 2 * chips
    half = jnp.bfloat16
    part = 256 if a.shape[0] <= 2048 else 128
    return pl.pallas_call(
        functools.partial(units_back_kernel, chips),
        out_shape=[
            jax.ShapeDtypeStruct((rows, width), jnp.float32),
            jax.ShapeDtypeStruct((rows, width), half),
            jax.ShapeDtypeStruct((8, width), jnp.float32),
            jax.ShapeDtypeStruct((width, a.shape[1]), half),
        ],
        in_specs=[ANY_SPEC] * 3 + [VMEM_SPEC] * 3,
        out_specs=[VMEM_SPEC] * 3 + [ANY_SPEC],
        scratch_shapes=[
            pltpu.VMEM(a.shape, half),
            pltpu.VMEM(w.shape, half),
            pltpu.VMEM((rows, width), jnp.float32),
            pltpu.VMEM((2, a.shape[0], part), half),
            pltpu.VMEM((2, part, a.shape[1]), half),
            sems(2),
            sems(2),
            sems(2),
        ]
        + Reduce.scratch(chips, rows, width),
        compiler_params=comm_params(collective, 60),
        cost_estimate=cost(
            4 * group * rows * width * a.shape[1], 200 * MIB, group * rows * width * 2
        ),
        name="units_back",
    )(a, w, b.reshape(group * rows, width), middle, cot, gain)


def branch_back_kernel(
    seqs, chips, batches, x_ref, w_ref, att_ref, hidden_hbm, wd_hbm, gd_hbm, units_hbm,
    d_ref, out_ref, out_grad_ref, down_hbm, units_in,
    buf, hidden_ref, wd_ref, rights, tiles, grad_acc, send, recv, load, right_sem, tile_sem,
    part_send, part_recv, acc, cross_out, line_out, cross_in, line_in, sum_send, sum_recv,
):
    line = Line(chips)
    rows = x_ref.shape[0]
    piece = rows // batches
    width = x_ref.shape[1]
    part = rights.shape[2]
    loads = [
        pltpu.make_async_copy(hidden_hbm, hidden_ref, load.at[0]),
        pltpu.make_async_copy(wd_hbm, wd_ref, load.at[1]),
    ]
    for item in loads:
        item.start()

    def product(slot, tile):
        return dot_nn(left_rows(hidden_ref, slot, rows), wd_ref[:, rows_at(tile, TILE)])

    def right(tile):
        slot = lax.rem(tile, 2)
        return pltpu.make_async_copy(
            gd_hbm.at[:, rows_at(tile, part)], rights.at[slot], right_sem.at[slot]
        )

    def stored(tile):
        slot = lax.rem(tile, 2)
        return pltpu.make_async_copy(
            tiles.at[slot], down_hbm.at[:, rows_at(tile, part)], tile_sem.at[slot]
        )

    def weight_grad(tile):
        right(tile).wait()
        pl.when(tile + 1 < width // part)(lambda: right(tile + 1).start())
        pl.when(tile >= 2)(lambda: stored(tile - 2).wait())
        slot = lax.rem(tile, 2)
        size = min(256, hidden_ref.shape[1])

        @pl.loop(0, hidden_ref.shape[1] // size)
        def _(row):
            here = rows_at(row, size)
            tiles[slot, here, :] = to_half(contract_rows(hidden_ref[:, here], rights[slot]))

        stored(tile).start()

    meet(line.greet() + greet_seq(seqs))
    sums = ToSeq(seqs, units_hbm, units_in, part_send, part_recv)
    spread = Spread(line, x_ref, buf, send, recv)
    reduce = Reduce(
        line, product, out_ref, acc, cross_out, line_out, cross_in, line_in, sum_send, sum_recv
    )
    spread.begin()
    sums.begin()
    right(0).start()
    buf[line.own] = x_ref[...]
    grad_acc[...] = jnp.zeros_like(grad_acc)

    def use(slot):
        got = to_half(dot_nt(buf[slot], w_ref[...]))
        for batch in range(batches):
            d_ref[batch, rows_at(slot, piece), :] = got[batch * piece : (batch + 1) * piece]
        mixed = left_rows(att_ref, slot, rows)

        @pl.loop(0, width // TILE)
        def _(tile):
            here = rows_at(tile, TILE)
            grad_acc[:, here] += contract_rows(mixed, buf[slot, :, here])

    for item in loads:
        item.wait()
    count = width // part
    per = -(-count // reduce.steps())

    @pl.loop(0, reduce.steps())
    def _(step):
        reduce.step(step)

        @pl.when(lax.rem(step, 2) == 1)
        def _():
            far = (step + 1) // 2
            spread.relay(far)
            spread.each(far - 1, use)

        @pl.loop(0, per)
        def _(turn):
            tile = step * per + turn
            pl.when(tile < count)(lambda: weight_grad(tile))

    spread.each(chips - 1, use)
    spread.each(chips, use)
    out_grad_ref[...] = to_half(grad_acc[...])
    spread.sent()
    reduce.sent()
    sums.end()
    stored(count - 2).wait()
    stored(count - 1).wait()


def branch_back(seqs, chips, batches, x, w, attended, hidden, wd, group_d, unit_part, collective):
    rows, width = x.shape
    group = 2 * chips
    length = group * rows // batches
    span = w.shape[0]
    units = wd.shape[0]
    half = jnp.bfloat16
    part = 256 if group * rows <= 2048 else 128
    return pl.pallas_call(
        functools.partial(branch_back_kernel, seqs, chips, batches),
        out_shape=[
            jax.ShapeDtypeStruct((batches, length, span), half),
            jax.ShapeDtypeStruct((rows, width), jnp.float32),
            jax.ShapeDtypeStruct((span, width), half),
            jax.ShapeDtypeStruct((units, width), half),
            jax.ShapeDtypeStruct((seqs, width // seqs, unit_part.shape[1]), half),
        ],
        in_specs=[VMEM_SPEC] * 3 + [ANY_SPEC] * 4,
        out_specs=[VMEM_SPEC, VMEM_SPEC, VMEM_SPEC, ANY_SPEC, ANY_SPEC],
        scratch_shapes=[
            pltpu.VMEM((group, rows, width), half),
            pltpu.VMEM(hidden.shape, half),
            pltpu.VMEM(wd.shape, half),
            pltpu.VMEM((2, group * rows, part), half),
            pltpu.VMEM((2, units, part), half),
            pltpu.VMEM((span, width), jnp.float32),
            sems(3, group),
            sems(group),
            sems(2),
            sems(2),
            sems(2),
            sems(seqs),
            sems(seqs),
        ]
        + Reduce.scratch(chips, rows, width),
        compiler_params=comm_params(collective, 62),
        cost_estimate=cost(
            2 * group * rows * width * (2 * span + 2 * units),
            250 * MIB,
            2 * group * rows * width * 2,
        ),
        name="branch_back",
    )(x, w, attended, hidden, wd, group_d.reshape(group * rows, width), unit_part)


def attend_back_kernel(
    seqs, group, block, q_ref, pad_ref, low_ref, lse_ref, d_ref, part_hbm, in_hbm, heads_ref, cols_ref,
    dk, dv, kt, back_out, back_in, halo_send, halo_recv, swap_send, swap_recv, swap_keep,
    parts, sums_ref, load,
):
    seq = lax.axis_index("seq")
    batches, length, span = q_ref.shape
    has_left, has_right = seq > 0, seq < seqs - 1
    run = parts.shape[1]

    def loaded(place, own):
        source = part_hbm.at[rows_at(seq, run)] if own else in_hbm.at[place]
        return pltpu.make_async_copy(source, parts.at[place], load.at[place])

    for place in range(seqs):
        pl.when(place == seq)(lambda place=place: loaded(place, True).start())
        pl.when(place != seq)(lambda place=place: loaded(place, False).start())
    pl.when(has_left)(lambda: signal_seq(seq - 1))
    pl.when(has_right)(lambda: signal_seq(seq + 1))
    meet(greet_group(group) + has_left.astype(jnp.int32) + has_right.astype(jnp.int32))
    for place in range(seqs):
        loaded(place, False).wait()

    @pl.loop(0, group)
    def _(member):
        share = run // group

        @pl.loop(0, share // 16)
        def _(chunk):
            here = pl.ds(pl.multiple_of(member * share + chunk * 16, 16), 16)
            added = parts[0, here, :].astype(jnp.float32)
            for place in range(1, seqs):
                added = added + parts[place, here, :].astype(jnp.float32)
            sums_ref[member, rows_at(chunk, 16), :] = to_half(added)

    swap = Swap(group, sums_ref, cols_ref, swap_send, swap_recv, swap_keep)
    swap.begin()
    steps = length // block
    scale = jnp.asarray(HEAD**-0.5, jnp.bfloat16)

    def halo(batch, step, peer):
        rows = rows_at(step, block)
        return pltpu.make_async_remote_copy(
            src_ref=back_out.at[batch, rows],
            dst_ref=back_in.at[batch, rows],
            send_sem=halo_send.at[batch, step],
            recv_sem=halo_recv.at[batch, step],
            device_id={"seq": peer},
            device_id_type=MESH,
        )

    dk[...] = jnp.zeros_like(dk)
    dv[...] = jnp.zeros_like(dv)
    for batch in range(batches):
        kt[...] = pad_ref[batch, :, :span].T * scale

        @pl.loop(0, steps)
        def _(step, batch=batch):
            begin = pl.multiple_of(step * block, block)
            keys = pl.ds(begin, block + WINDOW)
            rows = pl.ds(begin, block)
            low = low_ref[batch, :, rows]
            for pair in range(span // PAIR):
                lanes = slice(pair * PAIR, (pair + 1) * PAIR)
                q_pair = q_ref[batch, rows, lanes] * scale
                d_pair = d_ref[batch, rows, lanes]
                k_rows = pad_ref[batch, keys, lanes]
                v_rows = pad_ref[batch, keys, span + pair * PAIR : span + (pair + 1) * PAIR]
                k_cols = kt[lanes, keys]
                back = []
                for half in range(2):
                    row = pair * 2 + half
                    q_head = head_lanes(q_pair, half)
                    d_head = head_lanes(d_pair, half)
                    scores = masked_scores(k_rows, q_head, low)
                    probs = jnp.exp(scores - lse_ref[batch, row : row + 1, rows])
                    d_probs = dot_nt(v_rows, d_head)
                    along = jnp.sum(probs * d_probs, axis=0, keepdims=True)
                    d_scores = to_half(probs * (d_probs - along))
                    dv[batch, keys, lanes] += dot_nn(to_half(probs), d_head)
                    dk[batch, keys, lanes] += dot_nn(d_scores, q_head)
                    back.append(dot_nn(k_cols, d_scores))
                at = lax.broadcasted_iota(jnp.int32, back[0].shape, 0)
                heads_ref[batch, rows, lanes] = to_half(
                    jnp.where(at < HEAD, back[0], back[1]).T
                )

            @pl.when(has_left & (step < WINDOW // block))
            def _():
                back_out[batch, rows, :span] = to_half(dk[batch, rows, :])
                back_out[batch, rows, span:] = to_half(dv[batch, rows, :])
                halo(batch, step, seq - 1).start()

    first = length - WINDOW
    for batch in range(batches):
        if first:
            heads_ref[batch, :first, span : 2 * span] = to_half(dk[batch, WINDOW:length, :])
            heads_ref[batch, :first, 2 * span :] = to_half(dv[batch, WINDOW:length, :])

        @pl.loop(0, WINDOW // block)
        def _(step, batch=batch):
            inner = pl.ds(pl.multiple_of(step * block + length, block), block)
            rows = pl.ds(pl.multiple_of(step * block + first, block), block)

            @pl.when(has_right)
            def _():
                halo(batch, step, seq).wait_recv()
                got = back_in[batch, rows_at(step, block), :].astype(jnp.float32)
                heads_ref[batch, rows, span : 2 * span] = to_half(
                    dk[batch, inner, :] + got[:, :span]
                )
                heads_ref[batch, rows, 2 * span :] = to_half(dv[batch, inner, :] + got[:, span:])

            @pl.when(jnp.logical_not(has_right))
            def _():
                heads_ref[batch, rows, span : 2 * span] = to_half(dk[batch, inner, :])
                heads_ref[batch, rows, 2 * span :] = to_half(dv[batch, inner, :])

            pl.when(has_left)(lambda: halo(batch, step, seq).wait_send())

    swap.end()


def attend_back(seqs, group, query, kv_pad, low, lse, d_att, block, part, parts_in, collective):
    batches, length, span = query.shape
    padded = kv_pad.shape[1]
    half = jnp.bfloat16
    share = part.shape[0] // seqs // group
    sums = (group, share, part.shape[1])
    return pl.pallas_call(
        functools.partial(attend_back_kernel, seqs, group, block),
        in_specs=[VMEM_SPEC] * 5 + [ANY_SPEC] * 2,
        out_specs=[VMEM_SPEC, ANY_SPEC],
        out_shape=[
            jax.ShapeDtypeStruct((batches, length, 3 * span), half),
            jax.ShapeDtypeStruct(sums, half),
        ],
        scratch_shapes=[
            pltpu.VMEM((batches, padded, span), jnp.float32),
            pltpu.VMEM((batches, padded, span), jnp.float32),
            pltpu.VMEM((span, padded), half),
            pltpu.VMEM((batches, WINDOW, 2 * span), half),
            pltpu.VMEM((batches, WINDOW, 2 * span), half),
            sems(batches, WINDOW // block),
            sems(batches, WINDOW // block),
            sems(group),
            sems(group),
            pltpu.SemaphoreType.DMA,
            pltpu.VMEM(parts_in.shape, half),
            pltpu.VMEM(sums, half),
            sems(seqs),
        ],
        compiler_params=comm_params(collective),
        cost_estimate=cost(
            20 * batches * length * span * (WINDOW + block), 180 * MIB, part.size // seqs * 2
        ),
        name="attend_back",
    )(query, kv_pad, low, lse, d_att, part, parts_in)


def heads_back_kernel(
    seqs, chips, a_ref, w_ref, g_hbm, v_ref, dm_ref, gain_ref, mlp_gain_ref, units_hbm,
    grad_ref, cols_ref, tile_ref, gate_ref, up_ref, units, unit_load, total, gain_acc, lefts, parts, sums, cols, gain_out, gain_in, gain_sum, gain_back,
    left_sem, part_send, part_recv, cols_send, cols_recv, cols_keep,
    gain_send, gain_recv, back_send, back_recv,
    acc, cross_out, line_out, cross_in, line_in, sum_send, sum_recv,
):
    line = Line(chips)
    group = 2 * chips
    seq = lax.axis_index("seq")
    own = line.own
    rows, width = v_ref.shape
    batches = a_ref.shape[0]
    part = lefts.shape[3]
    run = width // seqs
    share = run // group
    depth = a_ref.shape[2]

    def left(tile):
        slot = lax.rem(tile, 2)
        return pltpu.make_async_copy(
            g_hbm.at[:, :, rows_at(tile, part)], lefts.at[slot], left_sem.at[slot]
        )

    def weight_grad(tile):
        left(tile).wait()
        pl.when(tile + 1 < width // part)(lambda: left(tile + 1).start())
        slot = lax.rem(tile, 2)
        got = contract_rows(lefts[slot, 0], a_ref[0])
        for batch in range(1, batches):
            got = got + contract_rows(lefts[slot, batch], a_ref[batch])
        parts[rows_at(tile, part), :] = to_half(got)

    def to_seq(peer, place):
        return pltpu.make_async_remote_copy(
            src_ref=parts.at[rows_at(peer, run)],
            dst_ref=sums.at[place],
            send_sem=part_send.at[peer],
            recv_sem=part_recv.at[place],
            device_id={"seq": peer},
            device_id_type=MESH,
        )

    def others(count, me, act):
        pl.loop(1, count)(lambda ahead: act(lax.rem(me + ahead, count)))

    def product(slot, tile):
        return dot_nt(left_rows(a_ref, slot, rows), w_ref[rows_at(tile, TILE), :])

    units_in = pltpu.make_async_copy(units_hbm, units, unit_load)
    units_in.start()
    left(0).start()
    meet(greet_group(group) + greet_seq(seqs))
    reduce = Reduce(
        line, product, total, acc, cross_out, line_out, cross_in, line_in, sum_send, sum_recv
    )
    count = width // part
    per = -(-count // 2)

    @pl.loop(0, 2)
    def _(step):
        reduce.step(step)

        @pl.loop(0, per)
        def _(turn):
            tile = step * per + turn
            pl.when(tile < count)(lambda: weight_grad(tile))

    others(seqs, seq, lambda peer: to_seq(peer, seq).start())
    units_in.wait()
    block = units.shape[2] // 2 // seqs
    for member in range(group):
        for place in range(seqs):
            column = (place * group + member) * block
            for target, begin in ((gate_ref, 0), (up_ref, seqs * block)):
                here = slice(begin + place * block, begin + (place + 1) * block)
                target[:, column : column + block] = units[member, :, here].astype(jnp.float32)

    pl.loop(2, 2 * chips - 2)(reduce.step)

    def block_swap(peer, member):
        return pltpu.make_async_remote_copy(
            src_ref=parts.at[rows_at(seq * group + peer, share)],
            dst_ref=cols.at[member],
            send_sem=cols_send.at[peer],
            recv_sem=cols_recv.at[member],
            device_id={"fsdp": peer},
            device_id_type=MESH,
        )

    others(seqs, seq, lambda peer: to_seq(peer, peer).wait_recv())

    @pl.loop(0, run // 64)
    def _(chunk):
        here = rows_at(chunk, 64)
        there = pl.ds(pl.multiple_of(seq * run + chunk * 64, 64), 64)
        added = parts[there, :].astype(jnp.float32)
        for place in range(seqs):
            piece = sums[place, here, :].astype(jnp.float32)
            added = added + jnp.where(place == seq, 0.0, piece)
        parts[there, :] = to_half(added)

    others(group, own, lambda peer: block_swap(peer, own).start())
    cols[own] = parts[rows_at(seq * group + own, share), :]
    reduce.step(2 * chips - 2)

    def put(here, d_values):
        grad_ref[here, :] = dm_ref[here, :] + d_values

    norm_back(rows, v_ref, total, gain_ref, gain_acc, put)
    fold = 128 // share
    near = group // fold
    attn_row = jnp.sum(gain_acc[...], axis=0, keepdims=True)
    mlp_row = jnp.sum(mlp_gain_ref[...], axis=0, keepdims=True)
    gain_out[...] = jnp.zeros_like(gain_out)
    for place in range(width // 128):
        lanes = slice(place * 128, (place + 1) * 128)
        gain_out[place % near, place // near, 0:1, :] = attn_row[:, lanes]
        gain_out[place % near, place // near, 1:2, :] = mlp_row[:, lanes]

    def gain_group(peer, member):
        return pltpu.make_async_remote_copy(
            src_ref=gain_out.at[peer // fold],
            dst_ref=gain_in.at[member],
            send_sem=gain_send.at[peer],
            recv_sem=gain_recv.at[member],
            device_id={"fsdp": peer},
            device_id_type=MESH,
        )

    def gain_seq(peer, place):
        return pltpu.make_async_remote_copy(
            src_ref=gain_sum.at[peer],
            dst_ref=gain_back.at[place],
            send_sem=back_send.at[peer],
            recv_sem=back_recv.at[place],
            device_id={"seq": peer},
            device_id_type=MESH,
        )

    others(group, own, lambda peer: gain_group(peer, own).start())
    gain_in[own] = gain_out[own // fold]
    others(group, own, lambda peer: gain_group(peer, peer).wait_recv())
    gain_sum[...] = jnp.sum(gain_in[...], axis=0)
    others(seqs, seq, lambda peer: gain_seq(peer, seq).start())
    gain_back[seq] = gain_sum[seq]
    others(seqs, seq, lambda peer: gain_seq(peer, peer).wait_recv())
    tile_ref[...] = jnp.sum(gain_back[...], axis=0)
    others(group, own, lambda peer: block_swap(peer, peer).wait_recv())
    kept = pltpu.make_async_copy(cols, cols_ref, cols_keep)
    kept.start()
    reduce.sent()
    others(seqs, seq, lambda peer: to_seq(peer, seq).wait_send())
    others(group, own, lambda peer: gain_group(peer, own).wait_send())
    others(group, own, lambda peer: block_swap(peer, own).wait_send())
    others(seqs, seq, lambda peer: gain_seq(peer, seq).wait_send())
    kept.wait()


def heads_back(seqs, chips, a, w, group_a, x, d_middle, gain, mlp_gain, units, collective):
    rows, width = x.shape
    batches, length, depth = a.shape
    group = 2 * chips
    share = width // seqs // group
    near = group // (128 // share)
    half = jnp.bfloat16
    part = 256 if batches * length <= 2048 else 128
    return pl.pallas_call(
        functools.partial(heads_back_kernel, seqs, chips),
        out_shape=[
            jax.ShapeDtypeStruct((rows, width), jnp.float32),
            jax.ShapeDtypeStruct((group, share, depth), half),
            jax.ShapeDtypeStruct((8, 128), jnp.float32),
            jax.ShapeDtypeStruct((share, units.size // 2 // share), jnp.float32),
            jax.ShapeDtypeStruct((share, units.size // 2 // share), jnp.float32),
        ],
        in_specs=[VMEM_SPEC, VMEM_SPEC, ANY_SPEC] + [VMEM_SPEC] * 4 + [ANY_SPEC],
        out_specs=[VMEM_SPEC, ANY_SPEC, VMEM_SPEC, VMEM_SPEC, VMEM_SPEC],
        scratch_shapes=[
            pltpu.VMEM(units.shape, half),
            pltpu.SemaphoreType.DMA,
            pltpu.VMEM((rows, width), jnp.float32),
            pltpu.VMEM((8, width), jnp.float32),
            pltpu.VMEM((2, batches, length, part), half),
            pltpu.VMEM((width, depth), half),
            pltpu.VMEM((seqs, width // seqs, depth), half),
            pltpu.VMEM((group, share, depth), half),
            pltpu.VMEM((near, seqs, 8, 128), jnp.float32),
            pltpu.VMEM((group, seqs, 8, 128), jnp.float32),
            pltpu.VMEM((seqs, 8, 128), jnp.float32),
            pltpu.VMEM((seqs, 8, 128), jnp.float32),
            sems(2),
            sems(seqs),
            sems(seqs),
            sems(group),
            sems(group),
            pltpu.SemaphoreType.DMA,
            sems(group),
            sems(group),
            sems(seqs),
            sems(seqs),
        ]
        + Reduce.scratch(chips, rows, width),
        compiler_params=comm_params(collective, 60),
        cost_estimate=cost(
            4 * group * rows * width * depth, 200 * MIB, 2 * group * rows * width * 2
        ),
        name="heads_back",
    )(a, w, group_a, x, d_middle, gain, mlp_gain, units)


def doc_starts(lengths, positions, batches, seq_len):
    table = lengths.reshape(batches, -1, lengths.shape[1])
    starts = jnp.cumsum(table, axis=2) - table
    per_batch = seq_len // table.shape[1]
    begins = (starts + (jnp.arange(table.shape[1], dtype=jnp.int32) * per_batch)[None, :, None]).reshape(
        batches, -1
    )
    before = begins[:, None, :] <= positions[None, :, None]
    return jnp.max(jnp.where(before, begins[:, None, :], 0), axis=2)


def body(
    tokens,
    cotangent,
    lengths,
    gain_attn,
    w_query,
    w_key,
    w_value,
    w_out,
    gain_mlp,
    w_gate,
    w_up,
    w_down,
):
    batches, piece, width = tokens.shape
    seqs = lax.axis_size("seq")
    group = lax.axis_size("fsdp")
    chips = group // 2
    devices = seqs * group
    seq_len = piece * devices
    rows = batches * piece
    share = w_query.shape[0]
    span = width // group
    length = group * piece
    aligned = share == HEAD
    member = lax.axis_index("fsdp")

    def blocks(weight):
        part = weight.shape[1] // devices
        if part < HEAD:
            return weight.reshape(share, group, -1).transpose(1, 0, 2)
        return weight.reshape(share, seqs, group, part).transpose(2, 0, 1, 3).reshape(group, share, -1)

    def unblock(cols, total):
        part = total // devices
        if part < HEAD:
            return cols.transpose(1, 0, 2).reshape(share, total)
        return cols.reshape(group, share, seqs, part).transpose(1, 2, 0, 3).reshape(share, total)

    inputs = tokens.astype(jnp.float32).reshape(rows, width)
    wd_part = lax.all_gather(w_down, "seq", axis=0, tiled=True)
    if aligned:
        wo_part = lax.all_gather(w_out, "seq", axis=0, tiled=True)
    else:
        wo_all = lax.all_gather(w_out, ("seq", "fsdp"), axis=0, tiled=True)
        wo_part = lax.dynamic_slice_in_dim(wo_all, member * span, span, 0)

    attn_blocks = jnp.concatenate([blocks(w_query), blocks(w_key), blocks(w_value)], axis=2)
    unit_blocks = jnp.concatenate([blocks(w_gate), blocks(w_up)], axis=2)
    group_start = lax.axis_index("seq") * length
    positions = group_start + jnp.arange(length, dtype=jnp.int32)
    begins = doc_starts(lengths, positions, batches, seq_len)
    at = jnp.arange(length, dtype=jnp.int32)
    block = min(256, length)
    low = jnp.maximum(begins - group_start + WINDOW, at[None, :] + 1) - (at // block * block)[None, :]
    low = low[:, None, :]

    lane = jnp.arange(128, dtype=jnp.int32)
    device = lax.axis_index("seq") * group + member
    fold = 128 // share
    here = lane // share == lax.rem(device, fold)
    both = jnp.stack([gain_attn, gain_mlp]).astype(jnp.float32)
    tile = jnp.where(here[None], jnp.tile(both, (1, fold)), 0.0)
    tile = jnp.pad(tile, ((0, 6), (0, 0)))[None]
    group_a, query, kv_pad, gains, w_heads = start(
        seqs, chips, batches, tile, tokens.reshape(rows, width), attn_blocks, 1
    )
    gains = gains.transpose(1, 0, 2, 3).reshape(devices // fold, fold, 8, 128).sum(axis=1)
    gain_one = gains[:, 0].reshape(width)
    gain_two = gains[:, 1].reshape(width)
    attended, lse, unit_own = attend(group, query, kv_pad, low, block, unit_blocks, 2)
    branch, group_d, w_units = branch_sum(
        seqs, chips, attended, wo_part, cotangent.reshape(rows, width),
        unit_own.reshape(group * share, -1), 3,
    )
    w_units = w_units.reshape(width, -1)
    middle = inputs + branch
    normed_b = to_half(normalize(middle, gain_two))
    group_b, hidden, d_units = hidden_units(chips, normed_b, w_units, wd_part, group_d, 4)
    d_middle, d_branch, mlp_gain_part, unit_part = units_back(
        chips, d_units, w_units, group_b, middle, cotangent.reshape(rows, width), gain_two[None], 5
    )

    def over_seq(values):
        return lax.psum_scatter(values, "seq", scatter_dimension=0, tiled=True)

    d_attended, mlp_out, out_grad, down_grad, unit_in = branch_back(
        seqs, chips, batches, d_branch, wo_part, attended, hidden, wd_part, group_d, unit_part, 6
    )
    outputs = middle + mlp_out
    down_sum = over_seq(down_grad)
    d_heads, unit_cols = attend_back(
        seqs, group, query, kv_pad, low, lse, d_attended, block, unit_part, unit_in, 7
    )
    if aligned:
        out_sum = over_seq(out_grad)
    else:
        whole = lax.dynamic_update_slice_in_dim(
            jnp.zeros((width, width), jnp.bfloat16), out_grad, member * span, 0
        )
        out_sum = lax.psum_scatter(whole, ("seq", "fsdp"), scatter_dimension=0, tiled=True)
    input_grad, head_cols, gain_tile, w_gate_grad, w_up_grad = heads_back(
        seqs, chips, d_heads, w_heads, group_a, tokens.reshape(rows, width), d_middle,
        gain_one[None], mlp_gain_part, unit_cols, 8,
    )
    input_grad = input_grad.reshape(batches, piece, width)
    layer_out = to_half(outputs).reshape(batches, piece, width)
    gain_grads = lax.dynamic_slice_in_dim(gain_tile[:2], lax.rem(device, fold) * share, share, 1)

    def whole_rows(cols, part, total):
        size = total // group
        return unblock(cols[:, :, part * size : (part + 1) * size], total).astype(jnp.float32)

    return (
        layer_out,
        input_grad,
        gain_grads[0],
        whole_rows(head_cols, 0, width),
        whole_rows(head_cols, 1, width),
        whole_rows(head_cols, 2, width),
        out_sum.astype(jnp.float32),
        gain_grads[1],
        w_gate_grad,
        w_up_grad,
        down_sum.astype(jnp.float32),
    )


def solution(mesh):
    spread = ("seq", "fsdp")
    tokens, rows, gains = P(None, spread, None), P(spread, None), P(spread)
    in_specs = (tokens, tokens, P(), gains, rows, rows, rows, rows, gains, rows, rows, rows)
    out_specs = (tokens, tokens, gains, rows, rows, rows, rows, gains, rows, rows, rows)
    return jax.shard_map(body, mesh=mesh, in_specs=in_specs, out_specs=out_specs, check_vma=False)
```

```python
import functools

import jax
import jax.numpy as jnp
from jax import lax
from jax.experimental import pallas as pl
from jax.experimental.pallas import tpu as pltpu
from jax.sharding import PartitionSpec as P

HEAD = 64
FF = 8192
WINDOW = 1024
PAIR = 128
TILE = 512
LOW = -1e30
EPS = 1e-05
MESH = pl.DeviceIdType.MESH
MIB = 2**20


def to_half(values):
    return values.astype(jnp.bfloat16)


def normalize(values, gain):
    return values * lax.rsqrt(jnp.mean(values * values, axis=-1, keepdims=True) + EPS) * gain


def contract_rows(left, right):
    return lax.dot_general(
        left, right, (((0,), (0,)), ((), ())), preferred_element_type=jnp.float32
    )


def dot_nt(left, right):
    return lax.dot_general(
        left, right, (((1,), (1,)), ((), ())), preferred_element_type=jnp.float32
    )


def dot_nn(left, right):
    return jnp.dot(left, right, preferred_element_type=jnp.float32)


def head_lanes(values, half):
    lane = lax.broadcasted_iota(jnp.int32, values.shape, 1)
    return jnp.where((lane >= HEAD) == (half == 1), values, jnp.zeros_like(values))


def masked_scores(k_rows, q_head, low):
    keys, block = k_rows.shape[0], q_head.shape[0]
    scores = dot_nt(k_rows, q_head)
    at = lax.broadcasted_iota(jnp.int32, (keys, block), 0)
    query = lax.broadcasted_iota(jnp.int32, (keys, block), 1)
    seen = (at >= low) & (at <= query + WINDOW)
    return jnp.where(seen, scores, LOW)


class Line:
    def __init__(self, chips):
        self.chips = chips
        self.own = lax.axis_index("fsdp")
        self.chip = self.own // 2
        self.core = lax.rem(self.own, 2)
        self.other = self.own + 1 - 2 * self.core
        self.has_left = self.chip > 0
        self.has_right = self.chip < chips - 1

    def greet(self):
        signal_group(self.other)
        pl.when(self.has_left)(lambda: signal_group(self.own - 2))
        pl.when(self.has_right)(lambda: signal_group(self.own + 2))
        return 1 + self.has_left.astype(jnp.int32) + self.has_right.astype(jnp.int32)


def signal_group(peer):
    barrier = pltpu.get_barrier_semaphore()
    pl.semaphore_signal(barrier, inc=1, device_id={"fsdp": peer}, device_id_type=MESH)


def signal_seq(peer):
    barrier = pltpu.get_barrier_semaphore()
    pl.semaphore_signal(barrier, inc=1, device_id={"seq": peer}, device_id_type=MESH)


def greet_group(group):
    own = lax.axis_index("fsdp")
    pl.loop(1, group)(lambda ahead: signal_group(lax.rem(own + ahead, group)))
    return group - 1


def greet_seq(seqs):
    own = lax.axis_index("seq")
    pl.loop(1, seqs)(lambda ahead: signal_seq(lax.rem(own + ahead, seqs)))
    return seqs - 1


def meet(count):
    pl.semaphore_wait(pltpu.get_barrier_semaphore(), count)


def rows_at(index, size):
    return pl.ds(pl.multiple_of(index * size, size), size)


class Spread:
    def __init__(self, line, first, buf, send, recv):
        self.line, self.first, self.buf, self.send, self.recv = line, first, buf, send, recv

    def move(self, slot, way, peer, source=None):
        return pltpu.make_async_remote_copy(
            src_ref=self.buf.at[slot] if source is None else source,
            dst_ref=self.buf.at[slot],
            send_sem=self.send.at[way, slot],
            recv_sem=self.recv.at[slot],
            device_id={"fsdp": peer},
            device_id_type=MESH,
        )

    def begin(self):
        line = self.line
        pl.when(line.has_right)(lambda: self.move(line.own, 1, line.own + 2, self.first).start())
        pl.when(line.has_left)(lambda: self.move(line.own, 0, line.own - 2, self.first).start())
        self.move(line.own, 2, line.other, self.first).start()

    def relay(self, far):
        line = self.line

        @pl.when(line.chip - far >= 0)
        def _():
            slot = (line.chip - far) * 2 + line.core
            self.move(slot, 1, line.own).wait_recv()
            pl.when(line.has_right)(lambda: self.move(slot, 1, line.own + 2).start())
            self.move(slot, 2, line.other).start()

        @pl.when(line.chip + far < line.chips)
        def _():
            slot = (line.chip + far) * 2 + line.core
            self.move(slot, 0, line.own).wait_recv()
            pl.when(line.has_left)(lambda: self.move(slot, 0, line.own - 2).start())
            self.move(slot, 2, line.other).start()

    def each(self, far, use):
        line = self.line

        @pl.loop(0, 4)
        def _(turn):
            side = lax.rem(turn, 2)
            across = turn // 2
            away = far - across
            source = line.chip + away * (2 * side - 1)
            valid = (away >= 0) & (away < line.chips) & (source >= 0) & (source < line.chips)
            valid = valid & ((side == 0) | (away > 0))

            @pl.when(valid)
            def _():
                slot = source * 2 + line.core + across * (1 - 2 * line.core)
                pl.when(across == 1)(lambda: self.move(slot, 2, line.own).wait_recv())
                use(slot)

    def whole(self, use):
        @pl.loop(0, self.line.chips + 1)
        def _(far):
            pl.when(far > 0)(lambda: self.relay(far))
            self.each(far, use)

    def rest(self):
        pl.loop(0, self.line.chips)(
            lambda place: self.move(place * 2 + 1 - self.line.core, 2, self.line.own).wait_recv()
        )

    def sent(self):
        line = self.line

        @pl.loop(0, line.chips)
        def _(place):
            slot = place * 2 + line.core
            self.move(slot, 2, line.other).wait_send()
            pl.when(line.has_right & (place <= line.chip))(
                lambda: self.move(slot, 1, line.own + 2).wait_send()
            )
            pl.when(line.has_left & (place >= line.chip))(
                lambda: self.move(slot, 0, line.own - 2).wait_send()
            )


class Reduce:
    def __init__(self, line, product, out, acc, cross_out, line_out, cross_in, line_in, send, recv):
        self.line, self.product, self.out, self.acc = line, product, out, acc
        self.cross_out, self.line_out, self.cross_in, self.line_in = cross_out, line_out, cross_in, line_in
        self.send, self.recv = send, recv
        self.tiles = line_out.shape[2] // TILE

    @staticmethod
    def scratch(chips, rows, width):
        part = pltpu.VMEM((chips, rows, width), jnp.bfloat16)
        return [
            pltpu.VMEM((rows, TILE), jnp.float32),
            pltpu.VMEM((rows, width), jnp.bfloat16),
            part,
            part,
            pltpu.VMEM((chips + 1, rows, width), jnp.bfloat16),
            pltpu.SemaphoreType.DMA((2, chips, width // TILE)),
            pltpu.SemaphoreType.DMA((2, chips + 1, width // TILE)),
        ]

    def cross(self, place, tile):
        here = rows_at(tile, TILE)
        return pltpu.make_async_remote_copy(
            src_ref=self.cross_out.at[:, here],
            dst_ref=self.cross_in.at[place, :, here],
            send_sem=self.send.at[0, place, tile],
            recv_sem=self.recv.at[0, place, tile],
            device_id={"fsdp": self.line.other},
            device_id_type=MESH,
        )

    def along(self, place, landing, tile, peer):
        here = rows_at(tile, TILE)
        return pltpu.make_async_remote_copy(
            src_ref=self.line_out.at[place, :, here],
            dst_ref=self.line_in.at[landing, :, here],
            send_sem=self.send.at[1, place, tile],
            recv_sem=self.recv.at[1, landing, tile],
            device_id={"fsdp": peer},
            device_id_type=MESH,
        )

    def steps(self):
        return 2 * self.line.chips - 1

    def step(self, step):
        line, acc = self.line, self.acc
        away = line.chips - 1 - step // 2
        rightward = lax.rem(step, 2) == 0
        place = line.chip + jnp.where(rightward, away, -away)
        upstream = (rightward & line.has_left) | (jnp.logical_not(rightward) & line.has_right)

        @pl.when((place >= 0) & (place < line.chips))
        def _():
            @pl.loop(0, self.tiles)
            def _(tile):
                got = self.product(place * 2 + 1 - line.core, tile)
                self.cross_out[:, rows_at(tile, TILE)] = to_half(got)
                self.cross(place, tile).start()

            @pl.loop(0, self.tiles)
            def _(tile):
                here = rows_at(tile, TILE)
                acc[...] = self.product(place * 2 + line.core, tile)
                self.cross(place, tile).wait()
                acc[...] += self.cross_in[place, :, here].astype(jnp.float32)

                @pl.when(away > 0)
                def _():
                    @pl.when(upstream)
                    def _():
                        self.along(place, place, tile, line.own).wait_recv()
                        self.line_out[place, :, here] = to_half(
                            acc[...] + self.line_in[place, :, here].astype(jnp.float32)
                        )

                    @pl.when(jnp.logical_not(upstream))
                    def _():
                        self.line_out[place, :, here] = to_half(acc[...])

                    @pl.when(rightward)
                    def _():
                        self.along(place, place, tile, line.own + 2).start()

                    @pl.when(jnp.logical_not(rightward))
                    def _():
                        landing = jnp.where(away == 1, line.chips, place)
                        self.along(place, landing, tile, line.own - 2).start()

                @pl.when(away == 0)
                def _():
                    self.out[:, here] = acc[...]

                    @pl.when(line.has_left)
                    def _():
                        self.along(place, place, tile, line.own).wait_recv()
                        self.out[:, here] += self.line_in[place, :, here].astype(jnp.float32)

                    @pl.when(line.has_right)
                    def _():
                        self.along(place, line.chips, tile, line.own).wait_recv()
                        self.out[:, here] += self.line_in[line.chips, :, here].astype(jnp.float32)

    def sent(self):
        @pl.loop(0, self.line.chips)
        def _(place):
            @pl.when(place != self.line.chip)
            def _():
                pl.loop(0, self.tiles)(
                    lambda tile: self.along(place, place, tile, self.line.own).wait_send()
                )


class Swap:
    def __init__(self, group, source, target, send, recv, keep):
        self.group, self.source, self.target = group, source, target
        self.send, self.recv, self.keep = send, recv, keep
        self.own = lax.axis_index("fsdp")

    def move(self, peer, source):
        return pltpu.make_async_remote_copy(
            src_ref=self.source.at[peer],
            dst_ref=self.target.at[source],
            send_sem=self.send.at[peer],
            recv_sem=self.recv.at[source],
            device_id={"fsdp": peer},
            device_id_type=MESH,
        )

    def kept(self):
        return pltpu.make_async_copy(self.source.at[self.own], self.target.at[self.own], self.keep)

    def begin(self):
        self.kept().start()
        pl.loop(1, self.group)(
            lambda ahead: self.move(lax.rem(self.own + ahead, self.group), self.own).start()
        )

    def end(self):
        self.kept().wait()

        @pl.loop(1, self.group)
        def _(ahead):
            peer = lax.rem(self.own + ahead, self.group)
            self.move(peer, peer).wait_recv()
            self.move(peer, self.own).wait_send()


class Share:
    def __init__(self, seqs, source, target, send, recv, keep):
        self.seqs, self.source, self.target = seqs, source, target
        self.send, self.recv, self.keep = send, recv, keep
        self.own = lax.axis_index("seq")

    def move(self, peer, place):
        return pltpu.make_async_remote_copy(
            src_ref=self.source,
            dst_ref=self.target.at[place],
            send_sem=self.send.at[peer],
            recv_sem=self.recv.at[place],
            device_id={"seq": peer},
            device_id_type=MESH,
        )

    def kept(self):
        return pltpu.make_async_copy(self.source, self.target.at[self.own], self.keep)

    def begin(self):
        self.kept().start()
        pl.loop(1, self.seqs)(
            lambda ahead: self.move(lax.rem(self.own + ahead, self.seqs), self.own).start()
        )

    def end(self):
        self.kept().wait()

        @pl.loop(1, self.seqs)
        def _(ahead):
            peer = lax.rem(self.own + ahead, self.seqs)
            self.move(peer, peer).wait_recv()
            self.move(peer, self.own).wait_send()


class ToSeq:
    def __init__(self, seqs, source, target, send, recv):
        self.seqs, self.source, self.target, self.send, self.recv = seqs, source, target, send, recv
        self.own = lax.axis_index("seq")

    def move(self, peer, place):
        return pltpu.make_async_remote_copy(
            src_ref=self.source.at[rows_at(peer, self.target.shape[1])],
            dst_ref=self.target.at[place],
            send_sem=self.send.at[peer],
            recv_sem=self.recv.at[place],
            device_id={"seq": peer},
            device_id_type=MESH,
        )

    def begin(self):
        pl.loop(1, self.seqs)(
            lambda ahead: self.move(lax.rem(self.own + ahead, self.seqs), self.own).start()
        )

    def arrived(self):
        @pl.loop(1, self.seqs)
        def _(ahead):
            peer = lax.rem(self.own + ahead, self.seqs)
            self.move(peer, peer).wait_recv()

    def sent(self):
        @pl.loop(1, self.seqs)
        def _(ahead):
            peer = lax.rem(self.own + ahead, self.seqs)
            self.move(peer, self.own).wait_send()

    def end(self):
        self.arrived()
        self.sent()


VMEM_SPEC = pl.BlockSpec(memory_space=pltpu.VMEM)
ANY_SPEC = pl.BlockSpec(memory_space=pl.ANY)


def comm_params(collective, mib=58):
    return pltpu.CompilerParams(
        collective_id=collective, has_side_effects=True, vmem_limit_bytes=mib * MIB
    )


def cost(flops, local, remote):
    return pl.CostEstimate(
        flops=flops, bytes_accessed=local, transcendentals=0, remote_bytes_transferred=remote
    )


def sems(*shape):
    return pltpu.SemaphoreType.DMA(shape)


def left_rows(a_ref, slot, rows):
    if len(a_ref.shape) == 2:
        return a_ref[rows_at(slot, rows), :]
    piece = rows // a_ref.shape[0]
    return jnp.concatenate(
        [a_ref[batch, rows_at(slot, piece), :] for batch in range(a_ref.shape[0])], axis=0
    )


def norm_back(rows, v_ref, e_ref, gain_ref, gain_acc, put):
    gain_acc[...] = jnp.zeros_like(gain_acc)

    @pl.loop(0, rows // 32)
    def _(chunk):
        here = rows_at(chunk, 32)
        values = v_ref[here, :].astype(jnp.float32)
        error = e_ref[here, :]
        rate = lax.rsqrt(jnp.mean(values * values, axis=-1, keepdims=True) + EPS)
        unit = values * rate
        product = error * unit
        gain = gain_ref[0:1, :]
        mean = jnp.mean(product * gain, axis=-1, keepdims=True)
        gain_acc[...] += (product[0:8] + product[8:16]) + (product[16:24] + product[24:32])
        put(here, rate * (gain * error - unit * mean))


def add_from_seq(seqs, own_rows, got, here):
    seq = lax.axis_index("seq")
    added = own_rows.astype(jnp.float32)
    for place in range(seqs):
        piece = got[place, here, :].astype(jnp.float32)
        added = added + jnp.where(place == seq, 0.0, piece)
    return added


def column_parts(seqs, group, share, span):
    size = HEAD if share == HEAD else span
    parts = []
    for member in range(group):
        for run in range(span // size):
            home = (run * group + member) * size
            parts.append((member, run * size, home, size))
    return parts


def start_kernel(
    seqs, chips, batches, tile_ref, x_ref, wq_ref, wk_ref, wv_ref, g_ref, q_ref, kv_ref, gains_ref, w_out_ref,
    blocks_ref, buf, normed, gain, gains, w, send, recv, keep, swap_send, share_send, w_recv,
    tile_send, tile_across, tile_recv, tile_back, w_keep, gain_keep,
):
    line = Line(chips)
    group = 2 * chips
    seq = lax.axis_index("seq")
    own = line.own
    share = blocks_ref.shape[1]
    piece = x_ref.shape[0] // batches
    span = q_ref.shape[2]
    width = x_ref.shape[1]
    per = 128 * seqs * group // width
    for index, source in enumerate((wq_ref, wk_ref, wv_ref)):
        for member, first, home, size in column_parts(seqs, group, share, span):
            first = first + index * span
            blocks_ref[member, :, first : first + size] = source[:, home : home + size]
    meet(greet_group(group) + greet_seq(seqs))

    def block_at(run, member):
        return w.at[rows_at(run * group + member, share)]

    def block_swap(peer, member):
        return pltpu.make_async_remote_copy(
            src_ref=blocks_ref.at[peer],
            dst_ref=block_at(seq, member),
            send_sem=swap_send.at[peer],
            recv_sem=w_recv.at[seq, member],
            device_id={"fsdp": peer},
            device_id_type=MESH,
        )

    def block_share(run, member, peer):
        return pltpu.make_async_remote_copy(
            src_ref=block_at(run, member),
            dst_ref=block_at(run, member),
            send_sem=share_send.at[peer, member],
            recv_sem=w_recv.at[run, member],
            device_id={"seq": peer},
            device_id_type=MESH,
        )

    def tile_to_seq(peer, place):
        return pltpu.make_async_remote_copy(
            src_ref=tile_ref.at[0],
            dst_ref=gains.at[own, place],
            send_sem=tile_send.at[peer],
            recv_sem=tile_recv.at[place],
            device_id={"seq": peer},
            device_id_type=MESH,
        )

    def tiles_to_group(peer, member):
        return pltpu.make_async_remote_copy(
            src_ref=gains.at[member],
            dst_ref=gains.at[member],
            send_sem=tile_across.at[peer],
            recv_sem=tile_back.at[member],
            device_id={"fsdp": peer},
            device_id_type=MESH,
        )

    def others(count, me, act):
        pl.loop(1, count)(lambda ahead: act(lax.rem(me + ahead, count)))

    others(seqs, seq, lambda peer: tile_to_seq(peer, seq).start())
    others(group, own, lambda peer: block_swap(peer, own).start())
    spread = Spread(line, x_ref, buf, send, recv)
    spread.begin()
    gains[own, seq] = tile_ref[0]
    w[rows_at(seq * group + own, share), :] = blocks_ref[own]
    others(seqs, seq, lambda peer: block_share(seq, own, peer).start())
    buf[own] = x_ref[...]
    others(seqs, seq, lambda peer: tile_to_seq(peer, peer).wait_recv())
    others(group, own, lambda peer: tiles_to_group(peer, own).start())

    def pass_block(member):
        block_swap(member, member).wait_recv()
        others(seqs, seq, lambda peer: block_share(seq, member, peer).start())

    others(group, own, pass_block)
    others(group, own, lambda peer: tiles_to_group(peer, peer).wait_recv())
    for column in range(width // 128):
        total = 0.0
        for place in range(column * per, (column + 1) * per):
            total = total + gains[place % group, place // group, 0:1, :]
        gain[0:1, column * 128 : (column + 1) * 128] = total

    def kept(slot, batch):
        return pltpu.make_async_copy(
            normed.at[slot, pl.ds(batch * piece, piece)],
            g_ref.at[batch, rows_at(slot, piece)],
            keep.at[slot, batch],
        )

    def use(slot):
        @pl.loop(0, x_ref.shape[0] // 64)
        def _(chunk):
            rows = rows_at(chunk, 64)
            values = buf[slot, rows, :].astype(jnp.float32)
            normed[slot, rows, :] = to_half(normalize(values, gain[0:1, :]))

        for batch in range(batches):
            kept(slot, batch).start()
        rows = rows_at(slot, piece)
        got = to_half(dot_nn(normed[slot], w[...]))
        for batch in range(batches):
            mine = got[batch * piece : (batch + 1) * piece]
            q_ref[batch, rows, :] = mine[:, :span]
            kv_ref[batch, rows, :] = mine[:, span:]

    pl.loop(1, chips - 1)(spread.relay)

    def have_block(run, member):
        block_share(run, member, seq).wait_recv()

    others(seqs, seq, lambda run: pl.loop(0, group)(lambda member: have_block(run, member)))
    w_kept = pltpu.make_async_copy(w, w_out_ref, w_keep)
    w_kept.start()
    gains_kept = pltpu.make_async_copy(gains, gains_ref, gain_keep)
    gains_kept.start()

    pl.loop(0, chips - 1)(lambda far: spread.each(far, use))
    spread.relay(chips - 1)
    spread.each(chips - 1, use)
    spread.each(chips, use)
    spread.sent()
    others(seqs, seq, lambda peer: tile_to_seq(peer, seq).wait_send())
    others(group, own, lambda peer: block_swap(peer, own).wait_send())
    others(group, own, lambda peer: tiles_to_group(peer, own).wait_send())
    others(
        seqs,
        seq,
        lambda peer: pl.loop(0, group)(lambda member: block_share(seq, member, peer).wait_send()),
    )
    w_kept.wait()
    gains_kept.wait()

    @pl.loop(0, group)
    def _(slot):
        for batch in range(batches):
            kept(slot, batch).wait()


def start(seqs, chips, batches, tile, x, weights, collective):
    rows, width = x.shape
    group = 2 * chips
    length = group * rows // batches
    share = weights[0].shape[0]
    span = width // group
    cols = 3 * span
    half = jnp.bfloat16
    return pl.pallas_call(
        functools.partial(start_kernel, seqs, chips, batches),
        out_shape=[
            jax.ShapeDtypeStruct((batches, length, width), half),
            jax.ShapeDtypeStruct((batches, length, span), half),
            jax.ShapeDtypeStruct((batches, length, 2 * span), half),
            jax.ShapeDtypeStruct((group, seqs, 8, 128), jnp.float32),
            jax.ShapeDtypeStruct((width, cols), half),
        ],
        in_specs=[VMEM_SPEC] * 5,
        out_specs=[ANY_SPEC, VMEM_SPEC, VMEM_SPEC, ANY_SPEC, ANY_SPEC],
        scratch_shapes=[
            pltpu.VMEM((group, share, cols), half),
            pltpu.VMEM((group, rows, width), half),
            pltpu.VMEM((group, rows, width), half),
            pltpu.VMEM((8, width), jnp.float32),
            pltpu.VMEM((group, seqs, 8, 128), jnp.float32),
            pltpu.VMEM((width, cols), half),
            sems(3, group),
            sems(group),
            sems(group, batches),
            sems(group),
            sems(seqs, group),
            sems(seqs, group),
            sems(seqs),
            sems(group),
            sems(seqs),
            sems(group),
            pltpu.SemaphoreType.DMA,
            pltpu.SemaphoreType.DMA,
        ],
        compiler_params=comm_params(collective),
        cost_estimate=cost(2 * group * rows * width * cols, 200 * MIB, group * rows * width * 2),
        name="start",
    )(tile, x, *weights)


def attend_kernel(
    seqs, group, block, q_ref, kv_ref, low_ref, units_ref, out_ref, lse_ref, pad_ref, own_units_ref,
    pad, vt_ref, halo_send, halo_recv, pad_keep, swap_send, swap_recv, swap_keep,
):
    seq = lax.axis_index("seq")
    batches, length, span = q_ref.shape
    has_left, has_right = seq > 0, seq < seqs - 1
    pl.when(has_left)(lambda: signal_seq(seq - 1))
    pl.when(has_right)(lambda: signal_seq(seq + 1))
    meet(greet_group(group) + has_left.astype(jnp.int32) + has_right.astype(jnp.int32))

    steps, need = length // block, WINDOW // block

    def halo(batch, step, peer):
        return pltpu.make_async_remote_copy(
            src_ref=kv_ref.at[batch, rows_at(step + steps - need, block)],
            dst_ref=pad.at[batch, rows_at(step, block)],
            send_sem=halo_send.at[batch, step],
            recv_sem=halo_recv.at[batch, step],
            device_id={"seq": peer},
            device_id_type=MESH,
        )

    def send_halo(turn):
        batch, step = turn // need, need - 1 - lax.rem(turn, need)
        pl.when(has_right)(lambda: halo(batch, step, seq + 1).start())

    def halo_sent(turn):
        batch, step = turn // need, need - 1 - lax.rem(turn, need)
        pl.when(has_right)(lambda: halo(batch, step, seq + 1).wait_send())

    send_halo(0)
    send_halo(1)
    swap = Swap(group, units_ref, own_units_ref, swap_send, swap_recv, swap_keep)
    swap.begin()
    pad[:, WINDOW:, :] = kv_ref[...]

    @pl.when(jnp.logical_not(has_left))
    def _():
        pad[:, :WINDOW, :] = jnp.zeros((batches, WINDOW, 2 * span), jnp.bfloat16)

    def kept(batch):
        return pltpu.make_async_copy(pad.at[batch], pad_ref.at[batch], pad_keep.at[batch])

    vt = vt_ref
    for batch in range(batches):
        vt[:, WINDOW:] = pad[batch, WINDOW:, span:].T

        @pl.loop(0, steps)
        def _(turn, batch=batch):
            step = steps - 1 - turn

            @pl.when(step < need)
            def _():
                rows = rows_at(step, block)
                pl.when(has_left)(lambda: halo(batch, step, seq).wait_recv())
                vt[:, rows] = pad[batch, rows, span:].T
                place = batch * need + need - 1 - step
                halo_sent(place)
                pl.when(place + 2 < batches * need)(lambda: send_halo(place + 2))

            begin = pl.multiple_of(step * block, block)
            keys = pl.ds(begin, block + WINDOW)
            rows = pl.ds(begin, block)
            low = low_ref[batch, :, rows]
            for pair in range(span // PAIR):
                lanes = slice(pair * PAIR, (pair + 1) * PAIR)
                q_pair = q_ref[batch, rows, lanes] * jnp.asarray(HEAD**-0.5, jnp.bfloat16)
                k_rows = pad[batch, keys, lanes]
                values = vt[lanes, keys]
                mixed = []
                for half in range(2):
                    scores = masked_scores(k_rows, head_lanes(q_pair, half), low)
                    top = jnp.max(scores, axis=0, keepdims=True)
                    expo = jnp.exp(scores - top)
                    total = jnp.sum(expo, axis=0, keepdims=True)
                    mixed.append(dot_nn(values, to_half(expo)) / total)
                    row = pair * 2 + half
                    lse_ref[batch, row : row + 1, rows] = top + jnp.log(total)
                lane = lax.broadcasted_iota(jnp.int32, mixed[0].shape, 0)
                out_ref[batch, rows, lanes] = to_half(jnp.where(lane < HEAD, mixed[0], mixed[1]).T)

    for batch in range(batches):
        kept(batch).start()
    swap.end()
    for batch in range(batches):
        kept(batch).wait()


def attend(seqs, group, query, key_value, low, block, units, collective):
    batches, length, span = query.shape
    padded = length + WINDOW
    heads = span // HEAD
    half = jnp.bfloat16
    return pl.pallas_call(
        functools.partial(attend_kernel, seqs, group, block),
        in_specs=[VMEM_SPEC, VMEM_SPEC, VMEM_SPEC, ANY_SPEC],
        out_specs=[VMEM_SPEC, VMEM_SPEC, ANY_SPEC, ANY_SPEC],
        out_shape=[
            jax.ShapeDtypeStruct((batches, length, span), half),
            jax.ShapeDtypeStruct((batches, heads, length), jnp.float32),
            jax.ShapeDtypeStruct((batches, padded, 2 * span), half),
            jax.ShapeDtypeStruct(units.shape, half),
        ],
        scratch_shapes=[
            pltpu.VMEM((batches, padded, 2 * span), half),
            pltpu.VMEM((span, padded), half),
            sems(batches, WINDOW // block),
            sems(batches, WINDOW // block),
            sems(batches),
            sems(group),
            sems(group),
            pltpu.SemaphoreType.DMA,
        ],
        compiler_params=comm_params(collective),
        cost_estimate=cost(
            8 * batches * length * span * (WINDOW + block), 150 * MIB, units.size * 2
        ),
        name="attend",
    )(query, key_value, low, units)


def branch_kernel(
    seqs, chips, a_ref, w_ref, d_ref, units_ref, x_ref, gain_ref, middle_ref, normed_ref, gd_ref, w_units_ref,
    out_ref, acc, cross_out, line_out, cross_in, line_in, sum_send, sum_recv,
    send, recv, d_keep, share_send, share_recv, share_keep,
):
    line = Line(chips)
    rows = out_ref.shape[0]

    def product(slot, tile):
        return dot_nn(left_rows(a_ref, slot, rows), w_ref[:, rows_at(tile, TILE)])

    meet(line.greet() + greet_seq(seqs))
    reduce = Reduce(
        line, product, out_ref, acc, cross_out, line_out, cross_in, line_in, sum_send, sum_recv
    )
    spread = Spread(line, d_ref, gd_ref, send, recv)
    units = Share(seqs, units_ref, w_units_ref, share_send, share_recv, share_keep)
    d_kept = pltpu.make_async_copy(d_ref, gd_ref.at[line.own], d_keep)
    units.begin()
    spread.begin()
    d_kept.start()

    @pl.loop(0, reduce.steps())
    def _(step):
        reduce.step(step)
        pl.when(lax.rem(step, 2) == 1)(lambda: spread.relay((step + 1) // 2))

    @pl.loop(0, rows // 32)
    def _(chunk):
        here = rows_at(chunk, 32)
        middle = x_ref[here, :].astype(jnp.float32) + out_ref[here, :]
        middle_ref[here, :] = middle
        normed_ref[here, :] = to_half(normalize(middle, gain_ref[0:1, :]))

    spread.rest()
    spread.sent()
    reduce.sent()
    d_kept.wait()
    units.end()


def branch_sum(seqs, chips, a, w, d_rows, units, x, gain, collective):
    rows, width = d_rows.shape
    group = 2 * chips
    half = jnp.bfloat16
    return pl.pallas_call(
        functools.partial(branch_kernel, seqs, chips),
        out_shape=[
            jax.ShapeDtypeStruct((rows, width), jnp.float32),
            jax.ShapeDtypeStruct((rows, width), half),
            jax.ShapeDtypeStruct((group, rows, width), half),
            jax.ShapeDtypeStruct((seqs,) + units.shape, half),
        ],
        in_specs=[VMEM_SPEC, VMEM_SPEC, ANY_SPEC, ANY_SPEC, VMEM_SPEC, VMEM_SPEC],
        out_specs=[VMEM_SPEC, VMEM_SPEC, ANY_SPEC, ANY_SPEC],
        scratch_shapes=[pltpu.VMEM((rows, width), jnp.float32)]
        + Reduce.scratch(chips, rows, width)
        + [sems(3, group), sems(group), pltpu.SemaphoreType.DMA]
        + [sems(seqs), sems(seqs), pltpu.SemaphoreType.DMA],
        compiler_params=comm_params(collective),
        cost_estimate=cost(
            2 * group * rows * width * w.shape[0], 250 * MIB, 3 * group * rows * width * 2
        ),
        name="branch_sum",
    )(a, w, d_rows, units, x, gain)


def units_kernel(
    chips, x_ref, w_hbm, wd_hbm, gd_ref, g_ref, hidden_hbm, d_hbm, down_hbm,
    down, down_half, buf, d_buf, w_ref, wd_ref, hidden_ref, d_ref, send, recv, keep, d_sem, load, store, down_sem,
):
    line = Line(chips)
    rows = x_ref.shape[0]
    units = hidden_ref.shape[1]
    part = min(units, TILE)
    loads = [
        pltpu.make_async_copy(w_hbm, w_ref, load.at[0]),
        pltpu.make_async_copy(wd_hbm, wd_ref, load.at[1]),
    ]
    for item in loads:
        item.start()
    meet(line.greet())
    spread = Spread(line, x_ref, buf, send, recv)
    spread.begin()
    buf[line.own] = x_ref[...]
    down[...] = jnp.zeros_like(down)
    for item in loads:
        item.wait()

    def kept(slot):
        place = rows_at(slot, rows)
        return [
            pltpu.make_async_copy(buf.at[slot], g_ref.at[slot], keep.at[slot]),
            pltpu.make_async_copy(hidden_ref.at[place], hidden_hbm.at[place], store.at[0, slot]),
            pltpu.make_async_copy(d_ref.at[place], d_hbm.at[place], store.at[1, slot]),
        ]

    def use(slot):
        fetch = pltpu.make_async_copy(gd_ref.at[slot], d_buf, d_sem)
        fetch.start()
        place = rows_at(slot, rows)
        fetch.wait()

        @pl.loop(0, units // part)
        def _(tile):
            here = rows_at(tile, part)
            there = rows_at(units // part + tile, part)
            values = buf[slot]
            gate = dot_nn(values, w_ref[:, here])
            up = dot_nn(values, w_ref[:, there])
            d_hidden = dot_nt(d_buf[...], wd_ref[here, :])
            sigma = jax.nn.sigmoid(gate)
            swish = gate * sigma
            hidden_ref[place, here] = to_half(swish * up)
            d_ref[place, here] = to_half(d_hidden * up * sigma * (1.0 + gate * (1.0 - sigma)))
            d_ref[place, there] = to_half(d_hidden * swish)

            @pl.loop(0, x_ref.shape[1] // TILE)
            def _(column):
                cols = rows_at(column, TILE)
                down[here, cols] += contract_rows(hidden_ref[place, here], d_buf[:, cols])

        for item in kept(slot):
            item.start()

    spread.whole(use)

    @pl.loop(0, units // 64)
    def _(chunk):
        here = rows_at(chunk, 64)
        down_half[here, :] = to_half(down[here, :])

    down_kept = pltpu.make_async_copy(down_half, down_hbm, down_sem)
    down_kept.start()
    spread.sent()
    down_kept.wait()

    @pl.loop(0, 2 * chips)
    def _(slot):
        for item in kept(slot):
            item.wait()


def hidden_units(chips, x, w, wd, group_d, collective):
    rows, width = x.shape
    group = 2 * chips
    units = wd.shape[0]
    half = jnp.bfloat16
    return pl.pallas_call(
        functools.partial(units_kernel, chips),
        out_shape=[
            jax.ShapeDtypeStruct((group, rows, width), half),
            jax.ShapeDtypeStruct((group * rows, units), half),
            jax.ShapeDtypeStruct((group * rows, 2 * units), half),
            jax.ShapeDtypeStruct((units, width), half),
        ],
        in_specs=[VMEM_SPEC, ANY_SPEC, ANY_SPEC, ANY_SPEC],
        out_specs=[ANY_SPEC] * 4,
        scratch_shapes=[
            pltpu.VMEM((units, width), jnp.float32),
            pltpu.VMEM((units, width), half),
            pltpu.VMEM((group, rows, width), half),
            pltpu.VMEM((rows, width), half),
            pltpu.VMEM(w.shape, half),
            pltpu.VMEM(wd.shape, half),
            pltpu.VMEM((group * rows, units), half),
            pltpu.VMEM((group * rows, 2 * units), half),
            sems(3, group),
            sems(group),
            sems(group),
            pltpu.SemaphoreType.DMA,
            sems(2),
            sems(2, group),
            pltpu.SemaphoreType.DMA,
        ],
        compiler_params=comm_params(collective),
        cost_estimate=cost(
            6 * group * rows * width * units, 200 * MIB, group * rows * width * 2
        ),
        name="hidden_units",
    )(x, w, wd, group_d)


def units_back_kernel(
    seqs, chips, a_hbm, w_hbm, b_hbm, down_hbm, v_ref, cot_ref, gain_ref,
    dm_ref, db_ref, gain_grad_ref, grad_hbm, down_in,
    a_ref, w_ref, total, lefts, tiles, load, left_sem, tile_sem, down_send, down_recv,
    acc, cross_out, line_out, cross_in, line_in, sum_send, sum_recv,
):
    line = Line(chips)
    rows, width = v_ref.shape
    group = 2 * chips
    part = lefts.shape[2]
    loads = [
        pltpu.make_async_copy(w_hbm, w_ref, load.at[0]),
        pltpu.make_async_copy(a_hbm, a_ref, load.at[1]),
    ]
    for item in loads:
        item.start()

    def left(tile):
        slot = lax.rem(tile, 2)
        return pltpu.make_async_copy(
            b_hbm.at[:, rows_at(tile, part)], lefts.at[slot], left_sem.at[slot]
        )

    def stored(tile):
        slot = lax.rem(tile, 2)
        return pltpu.make_async_copy(
            tiles.at[slot], grad_hbm.at[rows_at(tile, part)], tile_sem.at[slot]
        )

    def weight_grad(tile):
        left(tile).wait()
        pl.when(tile + 1 < width // part)(lambda: left(tile + 1).start())
        pl.when(tile >= 2)(lambda: stored(tile - 2).wait())
        slot = lax.rem(tile, 2)
        size = min(TILE, a_ref.shape[1])

        @pl.loop(0, a_ref.shape[1] // size)
        def _(column):
            here = rows_at(column, size)
            tiles[slot, :, here] = to_half(contract_rows(lefts[slot], a_ref[:, here]))

        stored(tile).start()

    def product(slot, tile):
        return dot_nt(left_rows(a_ref, slot, rows), w_ref[rows_at(tile, TILE), :])

    meet(line.greet() + greet_seq(seqs))
    down = ToSeq(seqs, down_hbm, down_in, down_send, down_recv)
    down.begin()
    left(0).start()
    for item in loads:
        item.wait()
    reduce = Reduce(
        line, product, total, acc, cross_out, line_out, cross_in, line_in, sum_send, sum_recv
    )
    count = width // part
    per = -(-count // reduce.steps())

    @pl.loop(0, reduce.steps())
    def _(step):
        reduce.step(step)

        @pl.loop(0, per)
        def _(turn):
            tile = step * per + turn
            pl.when(tile < count)(lambda: weight_grad(tile))

    def put(here, d_values):
        d_middle = cot_ref[here, :].astype(jnp.float32) + d_values
        dm_ref[here, :] = d_middle
        db_ref[here, :] = to_half(d_middle)

    norm_back(rows, v_ref, total, gain_ref, gain_grad_ref, put)
    reduce.sent()
    down.end()
    stored(count - 2).wait()
    stored(count - 1).wait()


def units_back(seqs, chips, a, w, b, down, middle, cot, gain, collective):
    rows, width = middle.shape
    group = 2 * chips
    half = jnp.bfloat16
    part = 256 if a.shape[0] <= 2048 else 128
    return pl.pallas_call(
        functools.partial(units_back_kernel, seqs, chips),
        out_shape=[
            jax.ShapeDtypeStruct((rows, width), jnp.float32),
            jax.ShapeDtypeStruct((rows, width), half),
            jax.ShapeDtypeStruct((8, width), jnp.float32),
            jax.ShapeDtypeStruct((width, a.shape[1]), half),
            jax.ShapeDtypeStruct((seqs, down.shape[0] // seqs, width), half),
        ],
        in_specs=[ANY_SPEC] * 4 + [VMEM_SPEC] * 3,
        out_specs=[VMEM_SPEC] * 3 + [ANY_SPEC] * 2,
        scratch_shapes=[
            pltpu.VMEM(a.shape, half),
            pltpu.VMEM(w.shape, half),
            pltpu.VMEM((rows, width), jnp.float32),
            pltpu.VMEM((2, a.shape[0], part), half),
            pltpu.VMEM((2, part, a.shape[1]), half),
            sems(2),
            sems(2),
            sems(2),
            sems(seqs),
            sems(seqs),
        ]
        + Reduce.scratch(chips, rows, width),
        compiler_params=comm_params(collective, 60),
        cost_estimate=cost(
            4 * group * rows * width * a.shape[1], 200 * MIB, group * rows * width * 2
        ),
        name="units_back",
    )(a, w, b.reshape(group * rows, width), down, middle, cot, gain)


def branch_back_kernel(
    seqs, chips, batches, x_ref, w_ref, att_ref, middle_ref, hidden_hbm, wd_hbm, units_hbm,
    d_ref, layer_ref, out_grad_ref, units_in,
    out_ref, buf, hidden_ref, wd_ref, grad_acc, send, recv, load,
    part_send, part_recv, acc, cross_out, line_out, cross_in, line_in, sum_send, sum_recv,
):
    line = Line(chips)
    rows = x_ref.shape[0]
    piece = rows // batches
    width = x_ref.shape[1]
    loads = [
        pltpu.make_async_copy(hidden_hbm, hidden_ref, load.at[0]),
        pltpu.make_async_copy(wd_hbm, wd_ref, load.at[1]),
    ]
    for item in loads:
        item.start()

    def product(slot, tile):
        return dot_nn(left_rows(hidden_ref, slot, rows), wd_ref[:, rows_at(tile, TILE)])

    meet(line.greet() + greet_seq(seqs))
    sums = ToSeq(seqs, units_hbm, units_in, part_send, part_recv)
    spread = Spread(line, x_ref, buf, send, recv)
    reduce = Reduce(
        line, product, out_ref, acc, cross_out, line_out, cross_in, line_in, sum_send, sum_recv
    )
    spread.begin()
    sums.begin()
    buf[line.own] = x_ref[...]
    grad_acc[...] = jnp.zeros_like(grad_acc)

    def use(slot):
        got = to_half(dot_nt(buf[slot], w_ref[...]))
        for batch in range(batches):
            d_ref[batch, rows_at(slot, piece), :] = got[batch * piece : (batch + 1) * piece]
        mixed = left_rows(att_ref, slot, rows)

        @pl.loop(0, width // TILE)
        def _(tile):
            here = rows_at(tile, TILE)
            grad_acc[:, here] += contract_rows(mixed, buf[slot, :, here])

    for item in loads:
        item.wait()

    @pl.loop(0, reduce.steps())
    def _(step):
        reduce.step(step)

        @pl.when(lax.rem(step, 2) == 1)
        def _():
            far = (step + 1) // 2
            spread.relay(far)
            spread.each(far - 1, use)

    spread.each(chips - 1, use)
    spread.each(chips, use)

    @pl.loop(0, rows // 32)
    def _(chunk):
        here = rows_at(chunk, 32)
        layer_ref[here, :] = to_half(middle_ref[here, :] + out_ref[here, :])

    out_grad_ref[...] = to_half(grad_acc[...])
    spread.sent()
    reduce.sent()
    sums.end()


def branch_back(seqs, chips, batches, x, w, attended, middle, hidden, wd, unit_part, collective):
    rows, width = x.shape
    group = 2 * chips
    length = group * rows // batches
    span = w.shape[0]
    half = jnp.bfloat16
    return pl.pallas_call(
        functools.partial(branch_back_kernel, seqs, chips, batches),
        out_shape=[
            jax.ShapeDtypeStruct((batches, length, span), half),
            jax.ShapeDtypeStruct((rows, width), half),
            jax.ShapeDtypeStruct((span, width), half),
            jax.ShapeDtypeStruct((seqs, width // seqs, unit_part.shape[1]), half),
        ],
        in_specs=[VMEM_SPEC] * 4 + [ANY_SPEC] * 3,
        out_specs=[VMEM_SPEC, VMEM_SPEC, VMEM_SPEC, ANY_SPEC],
        scratch_shapes=[
            pltpu.VMEM((rows, width), jnp.float32),
            pltpu.VMEM((group, rows, width), half),
            pltpu.VMEM(hidden.shape, half),
            pltpu.VMEM(wd.shape, half),
            pltpu.VMEM((span, width), jnp.float32),
            sems(3, group),
            sems(group),
            sems(2),
            sems(seqs),
            sems(seqs),
        ]
        + Reduce.scratch(chips, rows, width),
        compiler_params=comm_params(collective, 62),
        cost_estimate=cost(
            2 * group * rows * width * (2 * span + wd.shape[0]),
            250 * MIB,
            2 * group * rows * width * 2,
        ),
        name="branch_back",
    )(x, w, attended, middle, hidden, wd, unit_part)


def attend_back_kernel(
    seqs, group, block, q_ref, pad_ref, low_ref, lse_ref, d_ref, part_hbm, in_hbm, heads_ref, cols_ref,
    dk, dv, kt, back_out, back_in, halo_send, halo_recv, swap_send, swap_recv, swap_keep,
    parts, sums_ref, load,
):
    seq = lax.axis_index("seq")
    batches, length, span = q_ref.shape
    has_left, has_right = seq > 0, seq < seqs - 1
    run = parts.shape[1]

    def loaded(place, own):
        source = part_hbm.at[rows_at(seq, run)] if own else in_hbm.at[place]
        return pltpu.make_async_copy(source, parts.at[place], load.at[place])

    for place in range(seqs):
        pl.when(place == seq)(lambda place=place: loaded(place, True).start())
        pl.when(place != seq)(lambda place=place: loaded(place, False).start())
    pl.when(has_left)(lambda: signal_seq(seq - 1))
    pl.when(has_right)(lambda: signal_seq(seq + 1))
    meet(greet_group(group) + has_left.astype(jnp.int32) + has_right.astype(jnp.int32))
    for place in range(seqs):
        loaded(place, False).wait()

    @pl.loop(0, group)
    def _(member):
        share = run // group

        @pl.loop(0, share // 16)
        def _(chunk):
            here = pl.ds(pl.multiple_of(member * share + chunk * 16, 16), 16)
            added = parts[0, here, :].astype(jnp.float32)
            for place in range(1, seqs):
                added = added + parts[place, here, :].astype(jnp.float32)
            sums_ref[member, rows_at(chunk, 16), :] = to_half(added)

    swap = Swap(group, sums_ref, cols_ref, swap_send, swap_recv, swap_keep)
    swap.begin()
    steps = length // block
    scale = jnp.asarray(HEAD**-0.5, jnp.bfloat16)

    def halo(batch, step, peer):
        rows = rows_at(step, block)
        return pltpu.make_async_remote_copy(
            src_ref=back_out.at[batch, rows],
            dst_ref=back_in.at[batch, rows],
            send_sem=halo_send.at[batch, step],
            recv_sem=halo_recv.at[batch, step],
            device_id={"seq": peer},
            device_id_type=MESH,
        )

    dk[...] = jnp.zeros_like(dk)
    dv[...] = jnp.zeros_like(dv)
    for batch in range(batches):
        kt[...] = pad_ref[batch, :, :span].T * scale

        @pl.loop(0, steps)
        def _(step, batch=batch):
            begin = pl.multiple_of(step * block, block)
            keys = pl.ds(begin, block + WINDOW)
            rows = pl.ds(begin, block)
            low = low_ref[batch, :, rows]
            for pair in range(span // PAIR):
                lanes = slice(pair * PAIR, (pair + 1) * PAIR)
                q_pair = q_ref[batch, rows, lanes] * scale
                d_pair = d_ref[batch, rows, lanes]
                k_rows = pad_ref[batch, keys, lanes]
                v_rows = pad_ref[batch, keys, span + pair * PAIR : span + (pair + 1) * PAIR]
                k_cols = kt[lanes, keys]
                back = []
                for half in range(2):
                    row = pair * 2 + half
                    q_head = head_lanes(q_pair, half)
                    d_head = head_lanes(d_pair, half)
                    scores = masked_scores(k_rows, q_head, low)
                    probs = jnp.exp(scores - lse_ref[batch, row : row + 1, rows])
                    d_probs = dot_nt(v_rows, d_head)
                    along = jnp.sum(probs * d_probs, axis=0, keepdims=True)
                    d_scores = to_half(probs * (d_probs - along))
                    dv[batch, keys, lanes] += dot_nn(to_half(probs), d_head)
                    dk[batch, keys, lanes] += dot_nn(d_scores, q_head)
                    back.append(dot_nn(k_cols, d_scores))
                at = lax.broadcasted_iota(jnp.int32, back[0].shape, 0)
                heads_ref[batch, rows, lanes] = to_half(
                    jnp.where(at < HEAD, back[0], back[1]).T
                )

            @pl.when(has_left & (step < WINDOW // block))
            def _():
                back_out[batch, rows, :span] = to_half(dk[batch, rows, :])
                back_out[batch, rows, span:] = to_half(dv[batch, rows, :])
                halo(batch, step, seq - 1).start()

    first = length - WINDOW
    for batch in range(batches):
        if first:
            heads_ref[batch, :first, span : 2 * span] = to_half(dk[batch, WINDOW:length, :])
            heads_ref[batch, :first, 2 * span :] = to_half(dv[batch, WINDOW:length, :])

        @pl.loop(0, WINDOW // block)
        def _(step, batch=batch):
            inner = pl.ds(pl.multiple_of(step * block + length, block), block)
            rows = pl.ds(pl.multiple_of(step * block + first, block), block)

            @pl.when(has_right)
            def _():
                halo(batch, step, seq).wait_recv()
                got = back_in[batch, rows_at(step, block), :].astype(jnp.float32)
                heads_ref[batch, rows, span : 2 * span] = to_half(
                    dk[batch, inner, :] + got[:, :span]
                )
                heads_ref[batch, rows, 2 * span :] = to_half(dv[batch, inner, :] + got[:, span:])

            @pl.when(jnp.logical_not(has_right))
            def _():
                heads_ref[batch, rows, span : 2 * span] = to_half(dk[batch, inner, :])
                heads_ref[batch, rows, 2 * span :] = to_half(dv[batch, inner, :])

            pl.when(has_left)(lambda: halo(batch, step, seq).wait_send())

    swap.end()


def attend_back(seqs, group, query, kv_pad, low, lse, d_att, block, part, parts_in, collective):
    batches, length, span = query.shape
    padded = kv_pad.shape[1]
    half = jnp.bfloat16
    share = part.shape[0] // seqs // group
    sums = (group, share, part.shape[1])
    return pl.pallas_call(
        functools.partial(attend_back_kernel, seqs, group, block),
        in_specs=[VMEM_SPEC] * 5 + [ANY_SPEC] * 2,
        out_specs=[VMEM_SPEC, ANY_SPEC],
        out_shape=[
            jax.ShapeDtypeStruct((batches, length, 3 * span), half),
            jax.ShapeDtypeStruct(sums, half),
        ],
        scratch_shapes=[
            pltpu.VMEM((batches, padded, span), jnp.float32),
            pltpu.VMEM((batches, padded, span), jnp.float32),
            pltpu.VMEM((span, padded), half),
            pltpu.VMEM((batches, WINDOW, 2 * span), half),
            pltpu.VMEM((batches, WINDOW, 2 * span), half),
            sems(batches, WINDOW // block),
            sems(batches, WINDOW // block),
            sems(group),
            sems(group),
            pltpu.SemaphoreType.DMA,
            pltpu.VMEM(parts_in.shape, half),
            pltpu.VMEM(sums, half),
            sems(seqs),
        ],
        compiler_params=comm_params(collective),
        cost_estimate=cost(
            20 * batches * length * span * (WINDOW + block), 180 * MIB, part.size // seqs * 2
        ),
        name="attend_back",
    )(query, kv_pad, low, lse, d_att, part, parts_in)


def heads_back_kernel(
    seqs, chips, a_ref, w_ref, g_hbm, v_ref, dm_ref, gain_ref, mlp_gain_ref, units_hbm, out_ref,
    grad_ref, q_ref, k_ref, v_out_ref, wo_ref, tile_ref, gate_ref, up_ref,
    units, unit_load, out_in, out_send, out_recv, total, gain_acc, lefts, parts, sums, cols, gain_out, gain_in, gain_sum, gain_back,
    left_sem, part_send, part_recv, cols_send, cols_recv,
    gain_send, gain_recv, back_send, back_recv,
    acc, cross_out, line_out, cross_in, line_in, sum_send, sum_recv,
):
    line = Line(chips)
    group = 2 * chips
    seq = lax.axis_index("seq")
    own = line.own
    rows, width = v_ref.shape
    batches = a_ref.shape[0]
    part = lefts.shape[3]
    run = width // seqs
    share = run // group
    depth = a_ref.shape[2]

    def left(tile):
        slot = lax.rem(tile, 2)
        return pltpu.make_async_copy(
            g_hbm.at[:, :, rows_at(tile, part)], lefts.at[slot], left_sem.at[slot]
        )

    def weight_grad(tile):
        left(tile).wait()
        pl.when(tile + 1 < width // part)(lambda: left(tile + 1).start())
        slot = lax.rem(tile, 2)
        got = contract_rows(lefts[slot, 0], a_ref[0])
        for batch in range(1, batches):
            got = got + contract_rows(lefts[slot, batch], a_ref[batch])
        parts[rows_at(tile, part), :] = to_half(got)

    def to_seq(peer, place):
        return pltpu.make_async_remote_copy(
            src_ref=parts.at[rows_at(peer, run)],
            dst_ref=sums.at[place],
            send_sem=part_send.at[peer],
            recv_sem=part_recv.at[place],
            device_id={"seq": peer},
            device_id_type=MESH,
        )

    def others(count, me, act):
        pl.loop(1, count)(lambda ahead: act(lax.rem(me + ahead, count)))

    def product(slot, tile):
        return dot_nt(left_rows(a_ref, slot, rows), w_ref[rows_at(tile, TILE), :])

    from_seq = ToSeq(seqs, out_ref, out_in, out_send, out_recv)
    units_in = pltpu.make_async_copy(units_hbm, units, unit_load)
    units_in.start()
    left(0).start()
    meet(greet_group(group) + greet_seq(seqs))
    reduce = Reduce(
        line, product, total, acc, cross_out, line_out, cross_in, line_in, sum_send, sum_recv
    )
    count = width // part
    per = -(-count // 2)

    @pl.loop(0, 2)
    def _(step):
        reduce.step(step)

        @pl.loop(0, per)
        def _(turn):
            tile = step * per + turn
            pl.when(tile < count)(lambda: weight_grad(tile))

    others(seqs, seq, lambda peer: to_seq(peer, seq).start())
    from_seq.begin()
    units_in.wait()
    block = units.shape[2] // 2 // seqs
    for member in range(group):
        for place in range(seqs):
            column = (place * group + member) * block
            for target, begin in ((gate_ref, 0), (up_ref, seqs * block)):
                here = slice(begin + place * block, begin + (place + 1) * block)
                target[:, column : column + block] = units[member, :, here]

    pl.loop(2, 2 * chips - 2)(reduce.step)

    def block_swap(peer, member):
        return pltpu.make_async_remote_copy(
            src_ref=parts.at[rows_at(seq * group + peer, share)],
            dst_ref=cols.at[member],
            send_sem=cols_send.at[peer],
            recv_sem=cols_recv.at[member],
            device_id={"fsdp": peer},
            device_id_type=MESH,
        )

    others(seqs, seq, lambda peer: to_seq(peer, peer).wait_recv())

    @pl.loop(0, run // 64)
    def _(chunk):
        here = rows_at(chunk, 64)
        there = pl.ds(pl.multiple_of(seq * run + chunk * 64, 64), 64)
        parts[there, :] = to_half(add_from_seq(seqs, parts[there, :], sums, here))

    others(group, own, lambda peer: block_swap(peer, own).start())
    cols[own] = parts[rows_at(seq * group + own, share), :]
    from_seq.arrived()
    size = out_in.shape[1]
    wo_ref[...] = add_from_seq(seqs, out_ref[rows_at(seq, size), :], out_in, slice(None))
    reduce.step(2 * chips - 2)

    def put(here, d_values):
        grad_ref[here, :] = dm_ref[here, :] + d_values

    norm_back(rows, v_ref, total, gain_ref, gain_acc, put)
    fold = 128 // share
    near = group // fold
    attn_row = jnp.sum(gain_acc[...], axis=0, keepdims=True)
    mlp_row = jnp.sum(mlp_gain_ref[...], axis=0, keepdims=True)
    gain_out[...] = jnp.zeros_like(gain_out)
    for place in range(width // 128):
        lanes = slice(place * 128, (place + 1) * 128)
        gain_out[place % near, place // near, 0:1, :] = attn_row[:, lanes]
        gain_out[place % near, place // near, 1:2, :] = mlp_row[:, lanes]

    def gain_group(peer, member):
        return pltpu.make_async_remote_copy(
            src_ref=gain_out.at[peer // fold],
            dst_ref=gain_in.at[member],
            send_sem=gain_send.at[peer],
            recv_sem=gain_recv.at[member],
            device_id={"fsdp": peer},
            device_id_type=MESH,
        )

    def gain_seq(peer, place):
        return pltpu.make_async_remote_copy(
            src_ref=gain_sum.at[peer],
            dst_ref=gain_back.at[place],
            send_sem=back_send.at[peer],
            recv_sem=back_recv.at[place],
            device_id={"seq": peer},
            device_id_type=MESH,
        )

    others(group, own, lambda peer: gain_group(peer, own).start())
    gain_in[own] = gain_out[own // fold]
    others(group, own, lambda peer: gain_group(peer, peer).wait_recv())
    gain_sum[...] = jnp.sum(gain_in[...], axis=0)
    others(seqs, seq, lambda peer: gain_seq(peer, seq).start())
    gain_back[seq] = gain_sum[seq]
    others(seqs, seq, lambda peer: gain_seq(peer, peer).wait_recv())
    tile_ref[...] = jnp.sum(gain_back[...], axis=0)
    others(group, own, lambda peer: block_swap(peer, peer).wait_recv())
    span = depth // 3
    for index, target in enumerate((q_ref, k_ref, v_out_ref)):
        for member, first, home, size in column_parts(seqs, group, share, span):
            first = first + index * span
            target[:, home : home + size] = cols[member, :, first : first + size]
    from_seq.sent()
    reduce.sent()
    others(seqs, seq, lambda peer: to_seq(peer, seq).wait_send())
    others(group, own, lambda peer: gain_group(peer, own).wait_send())
    others(group, own, lambda peer: block_swap(peer, own).wait_send())
    others(seqs, seq, lambda peer: gain_seq(peer, seq).wait_send())


def heads_back(seqs, chips, a, w, group_a, x, d_middle, gain, mlp_gain, units, out_part, collective):
    rows, width = x.shape
    batches, length, depth = a.shape
    group = 2 * chips
    share = width // seqs // group
    near = group // (128 // share)
    half = jnp.bfloat16
    part = 256 if batches * length <= 2048 else 128
    return pl.pallas_call(
        functools.partial(heads_back_kernel, seqs, chips),
        out_shape=[
            jax.ShapeDtypeStruct((rows, width), jnp.float32),
            jax.ShapeDtypeStruct((share, width), half),
            jax.ShapeDtypeStruct((share, width), half),
            jax.ShapeDtypeStruct((share, width), half),
            jax.ShapeDtypeStruct((out_part.shape[0] // seqs, width), jnp.float32),
            jax.ShapeDtypeStruct((8, 128), jnp.float32),
            jax.ShapeDtypeStruct((share, units.size // 2 // share), half),
            jax.ShapeDtypeStruct((share, units.size // 2 // share), half),
        ],
        in_specs=[VMEM_SPEC, VMEM_SPEC, ANY_SPEC] + [VMEM_SPEC] * 4 + [ANY_SPEC, VMEM_SPEC],
        out_specs=[VMEM_SPEC] * 8,
        scratch_shapes=[
            pltpu.VMEM(units.shape, half),
            pltpu.SemaphoreType.DMA,
            pltpu.VMEM((seqs, out_part.shape[0] // seqs, width), half),
            sems(seqs),
            sems(seqs),
            pltpu.VMEM((rows, width), jnp.float32),
            pltpu.VMEM((8, width), jnp.float32),
            pltpu.VMEM((2, batches, length, part), half),
            pltpu.VMEM((width, depth), half),
            pltpu.VMEM((seqs, width // seqs, depth), half),
            pltpu.VMEM((group, share, depth), half),
            pltpu.VMEM((near, seqs, 8, 128), jnp.float32),
            pltpu.VMEM((group, seqs, 8, 128), jnp.float32),
            pltpu.VMEM((seqs, 8, 128), jnp.float32),
            pltpu.VMEM((seqs, 8, 128), jnp.float32),
            sems(2),
            sems(seqs),
            sems(seqs),
            sems(group),
            sems(group),
            sems(group),
            sems(group),
            sems(seqs),
            sems(seqs),
        ]
        + Reduce.scratch(chips, rows, width),
        compiler_params=comm_params(collective, 60),
        cost_estimate=cost(
            4 * group * rows * width * depth, 200 * MIB, 2 * group * rows * width * 2
        ),
        name="heads_back",
    )(a, w, group_a, x, d_middle, gain, mlp_gain, units, out_part)


def doc_starts(lengths, positions, batches, seq_len):
    table = lengths.reshape(batches, -1, lengths.shape[1])
    starts = jnp.cumsum(table, axis=2) - table
    per_batch = seq_len // table.shape[1]
    begins = (starts + (jnp.arange(table.shape[1], dtype=jnp.int32) * per_batch)[None, :, None]).reshape(
        batches, -1
    )
    before = begins[:, None, :] <= positions[None, :, None]
    return jnp.max(jnp.where(before, begins[:, None, :], 0), axis=2)


def body(
    tokens,
    cotangent,
    lengths,
    gain_attn,
    w_query,
    w_key,
    w_value,
    w_out,
    gain_mlp,
    w_gate,
    w_up,
    w_down,
):
    batches, piece, width = tokens.shape
    seqs = lax.axis_size("seq")
    group = lax.axis_size("fsdp")
    chips = group // 2
    devices = seqs * group
    seq_len = piece * devices
    rows = batches * piece
    share = w_query.shape[0]
    span = width // group
    length = group * piece
    aligned = share == HEAD
    member = lax.axis_index("fsdp")

    def blocks(weight):
        part = weight.shape[1] // devices
        return weight.reshape(share, seqs, group, part).transpose(2, 0, 1, 3).reshape(group, share, -1)

    x_rows = tokens.reshape(rows, width)
    cot_rows = cotangent.reshape(rows, width)
    wd_part = lax.all_gather(w_down, "seq", axis=0, tiled=True)
    if aligned:
        wo_part = lax.all_gather(w_out, "seq", axis=0, tiled=True)
    else:
        wo_all = lax.all_gather(w_out, ("seq", "fsdp"), axis=0, tiled=True)
        wo_part = lax.dynamic_slice_in_dim(wo_all, member * span, span, 0)

    unit_blocks = jnp.concatenate([blocks(w_gate), blocks(w_up)], axis=2)
    lane = jnp.arange(128, dtype=jnp.int32)
    device = lax.axis_index("seq") * group + member
    fold = 128 // share
    here = lane // share == lax.rem(device, fold)
    both = jnp.stack([gain_attn, gain_mlp]).astype(jnp.float32)
    tile = jnp.where(here[None], jnp.tile(both, (1, fold)), 0.0)
    tile = jnp.pad(tile, ((0, 6), (0, 0)))[None]
    group_a, query, key_value, gains, w_heads = start(
        seqs, chips, batches, tile, x_rows, (w_query, w_key, w_value), 1
    )
    lengths, gains = lax.optimization_barrier((lengths, gains))
    group_start = lax.axis_index("seq") * length
    positions = group_start + jnp.arange(length, dtype=jnp.int32)
    begins = doc_starts(lengths, positions, batches, seq_len)
    at = jnp.arange(length, dtype=jnp.int32)
    block = min(256, length)
    low = jnp.maximum(begins - group_start + WINDOW, at[None, :] + 1) - (at // block * block)[None, :]
    low = low[:, None, :]

    gains = gains.transpose(1, 0, 2, 3).reshape(devices // fold, fold, 8, 128).sum(axis=1)
    gain_one = gains[:, 0].reshape(width)
    gain_two = gains[:, 1].reshape(width)
    attended, lse, kv_pad, unit_own = attend(
        seqs, group, query, key_value, low, block, unit_blocks, 2
    )
    middle, normed_b, group_d, w_units = branch_sum(
        seqs, chips, attended, wo_part, cot_rows, unit_own.reshape(group * share, -1),
        x_rows, gain_two[None], 3,
    )
    w_units = w_units.reshape(width, -1)
    group_b, hidden, d_units, down_part = hidden_units(
        chips, normed_b, w_units, wd_part, group_d, 4
    )
    d_middle, d_branch, mlp_gain_part, unit_part, down_in = units_back(
        seqs, chips, d_units, w_units, group_b, down_part, middle, cot_rows, gain_two[None], 5
    )
    d_attended, layer_out, out_part, unit_in = branch_back(
        seqs, chips, batches, d_branch, wo_part, attended, middle, hidden, wd_part, unit_part, 6
    )
    d_heads, unit_cols = attend_back(
        seqs, group, query, kv_pad, low, lse, d_attended, block, unit_part, unit_in, 7
    )
    if not aligned:
        whole = lax.dynamic_update_slice_in_dim(
            jnp.zeros((width, width), jnp.bfloat16), out_part, member * span, 0
        )
        out_part = lax.psum(whole, "fsdp").reshape(seqs, group, share, width)
        out_part = lax.dynamic_slice_in_dim(out_part, member, 1, 1).reshape(seqs * share, width)
    input_grad, wq_grad, wk_grad, wv_grad, wo_grad, gain_tile, gate_grad, up_grad = heads_back(
        seqs, chips, d_heads, w_heads, group_a, x_rows, d_middle, gain_one[None], mlp_gain_part,
        unit_cols, out_part, 8,
    )
    run = lax.axis_index("seq")
    down_own = lax.dynamic_slice_in_dim(down_part, run * w_down.shape[0], w_down.shape[0], 0)
    others = jnp.arange(seqs)[:, None, None] != run
    down_sum = jnp.sum(jnp.where(others, down_in.astype(jnp.float32), 0.0), axis=0)
    gain_grads = lax.dynamic_slice_in_dim(gain_tile[:2], lax.rem(device, fold) * share, share, 1)
    wide = jnp.float32
    return (
        layer_out.reshape(batches, piece, width),
        input_grad.reshape(batches, piece, width),
        gain_grads[0],
        wq_grad.astype(wide),
        wk_grad.astype(wide),
        wv_grad.astype(wide),
        wo_grad,
        gain_grads[1],
        gate_grad.astype(wide),
        up_grad.astype(wide),
        down_sum + down_own.astype(wide),
    )


def solution(mesh):
    spread = ("seq", "fsdp")
    tokens, rows, gains = P(None, spread, None), P(spread, None), P(spread)
    in_specs = (tokens, tokens, P(), gains, rows, rows, rows, rows, gains, rows, rows, rows)
    out_specs = (tokens, tokens, gains, rows, rows, rows, rows, gains, rows, rows, rows)
    return jax.shard_map(body, mesh=mesh, in_specs=in_specs, out_specs=out_specs, check_vma=False)
```

```python
import functools

import jax
import jax.numpy as jnp
from jax import lax
from jax.experimental import pallas as pl
from jax.experimental.pallas import tpu as pltpu
from jax.sharding import PartitionSpec as P

HEAD = 64
FF = 8192
WINDOW = 1024
PAIR = 128
TILE = 512
LOW = -1e30
EPS = 1e-05
MESH = pl.DeviceIdType.MESH
MIB = 2**20


def to_half(values):
    return values.astype(jnp.bfloat16)


def normalize(values, gain):
    return values * lax.rsqrt(jnp.mean(values * values, axis=-1, keepdims=True) + EPS) * gain


def contract_rows(left, right):
    return lax.dot_general(
        left, right, (((0,), (0,)), ((), ())), preferred_element_type=jnp.float32
    )


def dot_nt(left, right):
    return lax.dot_general(
        left, right, (((1,), (1,)), ((), ())), preferred_element_type=jnp.float32
    )


def dot_nn(left, right):
    return jnp.dot(left, right, preferred_element_type=jnp.float32)


def head_lanes(values, half):
    lane = lax.broadcasted_iota(jnp.int32, values.shape, 1)
    return jnp.where((lane >= HEAD) == (half == 1), values, jnp.zeros_like(values))


def masked_scores(k_rows, q_head, low):
    keys, block = k_rows.shape[0], q_head.shape[0]
    scores = dot_nt(k_rows, q_head)
    at = lax.broadcasted_iota(jnp.int32, (keys, block), 0)
    query = lax.broadcasted_iota(jnp.int32, (keys, block), 1)
    seen = (at >= low) & (at <= query + WINDOW)
    return jnp.where(seen, scores, LOW)


class Line:
    def __init__(self, chips):
        self.chips = chips
        self.own = lax.axis_index("fsdp")
        self.chip = self.own // 2
        self.core = lax.rem(self.own, 2)
        self.other = self.own + 1 - 2 * self.core
        self.has_left = self.chip > 0
        self.has_right = self.chip < chips - 1

    def greet(self):
        signal_group(self.other)
        pl.when(self.has_left)(lambda: signal_group(self.own - 2))
        pl.when(self.has_right)(lambda: signal_group(self.own + 2))
        return 1 + self.has_left.astype(jnp.int32) + self.has_right.astype(jnp.int32)


def signal_group(peer):
    barrier = pltpu.get_barrier_semaphore()
    pl.semaphore_signal(barrier, inc=1, device_id={"fsdp": peer}, device_id_type=MESH)


def signal_seq(peer):
    barrier = pltpu.get_barrier_semaphore()
    pl.semaphore_signal(barrier, inc=1, device_id={"seq": peer}, device_id_type=MESH)


def greet_group(group):
    own = lax.axis_index("fsdp")
    pl.loop(1, group)(lambda ahead: signal_group(lax.rem(own + ahead, group)))
    return group - 1


def greet_seq(seqs):
    own = lax.axis_index("seq")
    pl.loop(1, seqs)(lambda ahead: signal_seq(lax.rem(own + ahead, seqs)))
    return seqs - 1


def meet(count):
    pl.semaphore_wait(pltpu.get_barrier_semaphore(), count)


def rows_at(index, size):
    return pl.ds(pl.multiple_of(index * size, size), size)


class Spread:
    def __init__(self, line, first, buf, send, recv):
        self.line, self.first, self.buf, self.send, self.recv = line, first, buf, send, recv

    def move(self, slot, way, peer, source=None):
        return pltpu.make_async_remote_copy(
            src_ref=self.buf.at[slot] if source is None else source,
            dst_ref=self.buf.at[slot],
            send_sem=self.send.at[way, slot],
            recv_sem=self.recv.at[slot],
            device_id={"fsdp": peer},
            device_id_type=MESH,
        )

    def begin(self):
        line = self.line
        pl.when(line.has_right)(lambda: self.move(line.own, 1, line.own + 2, self.first).start())
        pl.when(line.has_left)(lambda: self.move(line.own, 0, line.own - 2, self.first).start())
        self.move(line.own, 2, line.other, self.first).start()

    def relay(self, far):
        line = self.line

        @pl.when(line.chip - far >= 0)
        def _():
            slot = (line.chip - far) * 2 + line.core
            self.move(slot, 1, line.own).wait_recv()
            pl.when(line.has_right)(lambda: self.move(slot, 1, line.own + 2).start())
            self.move(slot, 2, line.other).start()

        @pl.when(line.chip + far < line.chips)
        def _():
            slot = (line.chip + far) * 2 + line.core
            self.move(slot, 0, line.own).wait_recv()
            pl.when(line.has_left)(lambda: self.move(slot, 0, line.own - 2).start())
            self.move(slot, 2, line.other).start()

    def each(self, far, use):
        line = self.line

        @pl.loop(0, 4)
        def _(turn):
            side = lax.rem(turn, 2)
            across = turn // 2
            away = far - across
            source = line.chip + away * (2 * side - 1)
            valid = (away >= 0) & (away < line.chips) & (source >= 0) & (source < line.chips)
            valid = valid & ((side == 0) | (away > 0))

            @pl.when(valid)
            def _():
                slot = source * 2 + line.core + across * (1 - 2 * line.core)
                pl.when(across == 1)(lambda: self.move(slot, 2, line.own).wait_recv())
                use(slot)

    def whole(self, use):
        @pl.loop(0, self.line.chips + 1)
        def _(far):
            pl.when(far > 0)(lambda: self.relay(far))
            self.each(far, use)

    def rest(self):
        pl.loop(0, self.line.chips)(
            lambda place: self.move(place * 2 + 1 - self.line.core, 2, self.line.own).wait_recv()
        )

    def sent(self):
        line = self.line

        @pl.loop(0, line.chips)
        def _(place):
            slot = place * 2 + line.core
            self.move(slot, 2, line.other).wait_send()
            pl.when(line.has_right & (place <= line.chip))(
                lambda: self.move(slot, 1, line.own + 2).wait_send()
            )
            pl.when(line.has_left & (place >= line.chip))(
                lambda: self.move(slot, 0, line.own - 2).wait_send()
            )


class Reduce:
    def __init__(self, line, product, out, acc, cross_out, line_out, cross_in, line_in, send, recv):
        self.line, self.product, self.out, self.acc = line, product, out, acc
        self.cross_out, self.line_out, self.cross_in, self.line_in = cross_out, line_out, cross_in, line_in
        self.send, self.recv = send, recv
        self.tiles = line_out.shape[2] // TILE

    @staticmethod
    def scratch(chips, rows, width):
        part = pltpu.VMEM((chips, rows, width), jnp.bfloat16)
        return [
            pltpu.VMEM((rows, TILE), jnp.float32),
            pltpu.VMEM((rows, width), jnp.bfloat16),
            part,
            part,
            pltpu.VMEM((chips + 1, rows, width), jnp.bfloat16),
            pltpu.SemaphoreType.DMA((2, chips, width // TILE)),
            pltpu.SemaphoreType.DMA((2, chips + 1, width // TILE)),
        ]

    def cross(self, place, tile):
        here = rows_at(tile, TILE)
        return pltpu.make_async_remote_copy(
            src_ref=self.cross_out.at[:, here],
            dst_ref=self.cross_in.at[place, :, here],
            send_sem=self.send.at[0, place, tile],
            recv_sem=self.recv.at[0, place, tile],
            device_id={"fsdp": self.line.other},
            device_id_type=MESH,
        )

    def along(self, place, landing, tile, peer):
        here = rows_at(tile, TILE)
        return pltpu.make_async_remote_copy(
            src_ref=self.line_out.at[place, :, here],
            dst_ref=self.line_in.at[landing, :, here],
            send_sem=self.send.at[1, place, tile],
            recv_sem=self.recv.at[1, landing, tile],
            device_id={"fsdp": peer},
            device_id_type=MESH,
        )

    def steps(self):
        return 2 * self.line.chips - 1

    def step(self, step):
        line, acc = self.line, self.acc
        away = line.chips - 1 - step // 2
        rightward = lax.rem(step, 2) == 0
        place = line.chip + jnp.where(rightward, away, -away)
        upstream = (rightward & line.has_left) | (jnp.logical_not(rightward) & line.has_right)

        @pl.when((place >= 0) & (place < line.chips))
        def _():
            @pl.loop(0, self.tiles)
            def _(tile):
                got = self.product(place * 2 + 1 - line.core, tile)
                self.cross_out[:, rows_at(tile, TILE)] = to_half(got)
                self.cross(place, tile).start()

            @pl.loop(0, self.tiles)
            def _(tile):
                here = rows_at(tile, TILE)
                acc[...] = self.product(place * 2 + line.core, tile)
                self.cross(place, tile).wait()
                acc[...] += self.cross_in[place, :, here].astype(jnp.float32)

                @pl.when(away > 0)
                def _():
                    @pl.when(upstream)
                    def _():
                        self.along(place, place, tile, line.own).wait_recv()
                        self.line_out[place, :, here] = to_half(
                            acc[...] + self.line_in[place, :, here].astype(jnp.float32)
                        )

                    @pl.when(jnp.logical_not(upstream))
                    def _():
                        self.line_out[place, :, here] = to_half(acc[...])

                    @pl.when(rightward)
                    def _():
                        self.along(place, place, tile, line.own + 2).start()

                    @pl.when(jnp.logical_not(rightward))
                    def _():
                        landing = jnp.where(away == 1, line.chips, place)
                        self.along(place, landing, tile, line.own - 2).start()

                @pl.when(away == 0)
                def _():
                    self.out[:, here] = acc[...]

                    @pl.when(line.has_left)
                    def _():
                        self.along(place, place, tile, line.own).wait_recv()
                        self.out[:, here] += self.line_in[place, :, here].astype(jnp.float32)

                    @pl.when(line.has_right)
                    def _():
                        self.along(place, line.chips, tile, line.own).wait_recv()
                        self.out[:, here] += self.line_in[line.chips, :, here].astype(jnp.float32)

    def sent(self):
        @pl.loop(0, self.line.chips)
        def _(place):
            @pl.when(place != self.line.chip)
            def _():
                pl.loop(0, self.tiles)(
                    lambda tile: self.along(place, place, tile, self.line.own).wait_send()
                )


class Swap:
    def __init__(self, group, source, target, send, recv, keep):
        self.group, self.source, self.target = group, source, target
        self.send, self.recv, self.keep = send, recv, keep
        self.own = lax.axis_index("fsdp")

    def move(self, peer, source):
        return pltpu.make_async_remote_copy(
            src_ref=self.source.at[peer],
            dst_ref=self.target.at[source],
            send_sem=self.send.at[peer],
            recv_sem=self.recv.at[source],
            device_id={"fsdp": peer},
            device_id_type=MESH,
        )

    def kept(self):
        return pltpu.make_async_copy(self.source.at[self.own], self.target.at[self.own], self.keep)

    def begin(self):
        self.kept().start()
        pl.loop(1, self.group)(
            lambda ahead: self.move(lax.rem(self.own + ahead, self.group), self.own).start()
        )

    def end(self):
        self.kept().wait()

        @pl.loop(1, self.group)
        def _(ahead):
            peer = lax.rem(self.own + ahead, self.group)
            self.move(peer, peer).wait_recv()
            self.move(peer, self.own).wait_send()


class Share:
    def __init__(self, seqs, source, target, send, recv, keep):
        self.seqs, self.source, self.target = seqs, source, target
        self.send, self.recv, self.keep = send, recv, keep
        self.own = lax.axis_index("seq")

    def move(self, peer, place):
        return pltpu.make_async_remote_copy(
            src_ref=self.source,
            dst_ref=self.target.at[place],
            send_sem=self.send.at[peer],
            recv_sem=self.recv.at[place],
            device_id={"seq": peer},
            device_id_type=MESH,
        )

    def kept(self):
        return pltpu.make_async_copy(self.source, self.target.at[self.own], self.keep)

    def begin(self):
        self.kept().start()
        pl.loop(1, self.seqs)(
            lambda ahead: self.move(lax.rem(self.own + ahead, self.seqs), self.own).start()
        )

    def end(self):
        self.kept().wait()

        @pl.loop(1, self.seqs)
        def _(ahead):
            peer = lax.rem(self.own + ahead, self.seqs)
            self.move(peer, peer).wait_recv()
            self.move(peer, self.own).wait_send()


class ToSeq:
    def __init__(self, seqs, source, target, send, recv, first=0, count=None):
        self.seqs, self.source, self.target, self.send, self.recv = seqs, source, target, send, recv
        self.own = lax.axis_index("seq")
        self.first, self.count = first, target.shape[1] if count is None else count

    def move(self, peer, place):
        begin = pl.multiple_of(peer * self.target.shape[1] + self.first, 16)
        return pltpu.make_async_remote_copy(
            src_ref=self.source.at[pl.ds(begin, self.count)],
            dst_ref=self.target.at[place, pl.ds(self.first, self.count)],
            send_sem=self.send.at[peer],
            recv_sem=self.recv.at[place],
            device_id={"seq": peer},
            device_id_type=MESH,
        )

    def begin(self):
        pl.loop(1, self.seqs)(
            lambda ahead: self.move(lax.rem(self.own + ahead, self.seqs), self.own).start()
        )

    def arrived(self):
        @pl.loop(1, self.seqs)
        def _(ahead):
            peer = lax.rem(self.own + ahead, self.seqs)
            self.move(peer, peer).wait_recv()

    def sent(self):
        @pl.loop(1, self.seqs)
        def _(ahead):
            peer = lax.rem(self.own + ahead, self.seqs)
            self.move(peer, self.own).wait_send()

    def end(self):
        self.arrived()
        self.sent()


VMEM_SPEC = pl.BlockSpec(memory_space=pltpu.VMEM)
ANY_SPEC = pl.BlockSpec(memory_space=pl.ANY)


def comm_params(collective, mib=58):
    return pltpu.CompilerParams(
        collective_id=collective, has_side_effects=True, vmem_limit_bytes=mib * MIB
    )


def cost(flops, local, remote):
    return pl.CostEstimate(
        flops=flops, bytes_accessed=local, transcendentals=0, remote_bytes_transferred=remote
    )


def sems(*shape):
    return pltpu.SemaphoreType.DMA(shape)


def left_rows(a_ref, slot, rows):
    if len(a_ref.shape) == 2:
        return a_ref[rows_at(slot, rows), :]
    piece = rows // a_ref.shape[0]
    return jnp.concatenate(
        [a_ref[batch, rows_at(slot, piece), :] for batch in range(a_ref.shape[0])], axis=0
    )


def norm_back(rows, v_ref, e_ref, gain_ref, gain_acc, put):
    @pl.loop(0, rows // 32)
    def _(chunk):
        here = rows_at(chunk, 32)
        values = v_ref[here, :].astype(jnp.float32)
        error = e_ref[here, :]
        rate = lax.rsqrt(jnp.mean(values * values, axis=-1, keepdims=True) + EPS)
        unit = values * rate
        product = error * unit
        gain = gain_ref[0:1, :]
        mean = jnp.mean(product * gain, axis=-1, keepdims=True)
        gain_acc[...] += (product[0:8] + product[8:16]) + (product[16:24] + product[24:32])
        put(here, rate * (gain * error - unit * mean))


def add_from_seq(seqs, own_rows, got, here):
    seq = lax.axis_index("seq")
    added = own_rows.astype(jnp.float32)
    for place in range(seqs):
        piece = got[place, here, :].astype(jnp.float32)
        added = added + jnp.where(place == seq, 0.0, piece)
    return added


def column_parts(seqs, group, share, span):
    size = HEAD if share == HEAD else span
    parts = []
    for member in range(group):
        for run in range(span // size):
            home = (run * group + member) * size
            parts.append((member, run * size, home, size))
    return parts


def start_kernel(
    seqs, chips, batches, tile_ref, x_ref, wq_ref, wk_ref, wv_ref, g_ref, q_ref, kv_ref, gains_ref, w_out_ref,
    blocks_ref, buf, normed, gain, gains, w, send, recv, keep, swap_send, share_send, w_recv,
    tile_send, tile_across, tile_recv, tile_back, w_keep, gain_keep,
):
    line = Line(chips)
    group = 2 * chips
    seq = lax.axis_index("seq")
    own = line.own
    share = blocks_ref.shape[1]
    piece = x_ref.shape[0] // batches
    span = q_ref.shape[2]
    width = x_ref.shape[1]
    per = 128 * seqs * group // width
    for index, source in enumerate((wq_ref, wk_ref, wv_ref)):
        for member, first, home, size in column_parts(seqs, group, share, span):
            first = first + index * span
            blocks_ref[member, :, first : first + size] = source[:, home : home + size]
    meet(greet_group(group) + greet_seq(seqs))

    def block_at(run, member):
        return w.at[rows_at(run * group + member, share)]

    def block_swap(peer, member):
        return pltpu.make_async_remote_copy(
            src_ref=blocks_ref.at[peer],
            dst_ref=block_at(seq, member),
            send_sem=swap_send.at[peer],
            recv_sem=w_recv.at[seq, member],
            device_id={"fsdp": peer},
            device_id_type=MESH,
        )

    def block_share(run, member, peer):
        return pltpu.make_async_remote_copy(
            src_ref=block_at(run, member),
            dst_ref=block_at(run, member),
            send_sem=share_send.at[peer, member],
            recv_sem=w_recv.at[run, member],
            device_id={"seq": peer},
            device_id_type=MESH,
        )

    def tile_to_seq(peer, place):
        return pltpu.make_async_remote_copy(
            src_ref=tile_ref.at[0],
            dst_ref=gains.at[own, place],
            send_sem=tile_send.at[peer],
            recv_sem=tile_recv.at[place],
            device_id={"seq": peer},
            device_id_type=MESH,
        )

    def tiles_to_group(peer, member):
        return pltpu.make_async_remote_copy(
            src_ref=gains.at[member],
            dst_ref=gains.at[member],
            send_sem=tile_across.at[peer],
            recv_sem=tile_back.at[member],
            device_id={"fsdp": peer},
            device_id_type=MESH,
        )

    def others(count, me, act):
        pl.loop(1, count)(lambda ahead: act(lax.rem(me + ahead, count)))

    others(seqs, seq, lambda peer: tile_to_seq(peer, seq).start())
    others(group, own, lambda peer: block_swap(peer, own).start())
    spread = Spread(line, x_ref, buf, send, recv)
    spread.begin()
    gains[own, seq] = tile_ref[0]
    w[rows_at(seq * group + own, share), :] = blocks_ref[own]
    others(seqs, seq, lambda peer: block_share(seq, own, peer).start())
    buf[own] = x_ref[...]
    others(seqs, seq, lambda peer: tile_to_seq(peer, peer).wait_recv())
    others(group, own, lambda peer: tiles_to_group(peer, own).start())

    def pass_block(member):
        block_swap(member, member).wait_recv()
        others(seqs, seq, lambda peer: block_share(seq, member, peer).start())

    others(group, own, pass_block)
    others(group, own, lambda peer: tiles_to_group(peer, peer).wait_recv())
    for column in range(width // 128):
        total = 0.0
        for place in range(column * per, (column + 1) * per):
            total = total + gains[place % group, place // group, 0:1, :]
        gain[0:1, column * 128 : (column + 1) * 128] = total

    def kept(slot, batch):
        return pltpu.make_async_copy(
            normed.at[slot, pl.ds(batch * piece, piece)],
            g_ref.at[batch, rows_at(slot, piece)],
            keep.at[slot, batch],
        )

    def use(slot):
        @pl.loop(0, x_ref.shape[0] // 64)
        def _(chunk):
            rows = rows_at(chunk, 64)
            values = buf[slot, rows, :].astype(jnp.float32)
            normed[slot, rows, :] = to_half(normalize(values, gain[0:1, :]))

        for batch in range(batches):
            kept(slot, batch).start()
        rows = rows_at(slot, piece)
        got = to_half(dot_nn(normed[slot], w[...]))
        for batch in range(batches):
            mine = got[batch * piece : (batch + 1) * piece]
            q_ref[batch, rows, :] = mine[:, :span]
            kv_ref[batch, rows, :] = mine[:, span:]

    pl.loop(1, chips - 1)(spread.relay)

    def have_block(run, member):
        block_share(run, member, seq).wait_recv()

    others(seqs, seq, lambda run: pl.loop(0, group)(lambda member: have_block(run, member)))
    w_kept = pltpu.make_async_copy(w, w_out_ref, w_keep)
    w_kept.start()
    gains_kept = pltpu.make_async_copy(gains, gains_ref, gain_keep)
    gains_kept.start()

    pl.loop(0, chips - 1)(lambda far: spread.each(far, use))
    spread.relay(chips - 1)
    spread.each(chips - 1, use)
    spread.each(chips, use)
    spread.sent()
    others(seqs, seq, lambda peer: tile_to_seq(peer, seq).wait_send())
    others(group, own, lambda peer: block_swap(peer, own).wait_send())
    others(group, own, lambda peer: tiles_to_group(peer, own).wait_send())
    others(
        seqs,
        seq,
        lambda peer: pl.loop(0, group)(lambda member: block_share(seq, member, peer).wait_send()),
    )
    w_kept.wait()
    gains_kept.wait()

    @pl.loop(0, group)
    def _(slot):
        for batch in range(batches):
            kept(slot, batch).wait()


def start(seqs, chips, batches, tile, x, weights, collective):
    rows, width = x.shape
    group = 2 * chips
    length = group * rows // batches
    share = weights[0].shape[0]
    span = width // group
    cols = 3 * span
    half = jnp.bfloat16
    return pl.pallas_call(
        functools.partial(start_kernel, seqs, chips, batches),
        out_shape=[
            jax.ShapeDtypeStruct((batches, length, width), half),
            jax.ShapeDtypeStruct((batches, length, span), half),
            jax.ShapeDtypeStruct((batches, length, 2 * span), half),
            jax.ShapeDtypeStruct((group, seqs, 8, 128), jnp.float32),
            jax.ShapeDtypeStruct((width, cols), half),
        ],
        in_specs=[VMEM_SPEC] * 5,
        out_specs=[ANY_SPEC, VMEM_SPEC, VMEM_SPEC, ANY_SPEC, ANY_SPEC],
        scratch_shapes=[
            pltpu.VMEM((group, share, cols), half),
            pltpu.VMEM((group, rows, width), half),
            pltpu.VMEM((group, rows, width), half),
            pltpu.VMEM((8, width), jnp.float32),
            pltpu.VMEM((group, seqs, 8, 128), jnp.float32),
            pltpu.VMEM((width, cols), half),
            sems(3, group),
            sems(group),
            sems(group, batches),
            sems(group),
            sems(seqs, group),
            sems(seqs, group),
            sems(seqs),
            sems(group),
            sems(seqs),
            sems(group),
            pltpu.SemaphoreType.DMA,
            pltpu.SemaphoreType.DMA,
        ],
        compiler_params=comm_params(collective),
        cost_estimate=cost(2 * group * rows * width * cols, 200 * MIB, group * rows * width * 2),
        name="start",
    )(tile, x, *weights)


def attend_kernel(
    seqs, group, block, q_ref, kv_ref, low_ref, units_ref, out_ref, lse_ref, pad_ref, own_units_ref,
    pad, vt_ref, halo_send, halo_recv, pad_keep, swap_send, swap_recv, swap_keep,
):
    seq = lax.axis_index("seq")
    batches, length, span = q_ref.shape
    has_left, has_right = seq > 0, seq < seqs - 1
    pl.when(has_left)(lambda: signal_seq(seq - 1))
    pl.when(has_right)(lambda: signal_seq(seq + 1))
    meet(greet_group(group) + has_left.astype(jnp.int32) + has_right.astype(jnp.int32))

    steps, need = length // block, WINDOW // block

    def halo(batch, step, peer):
        return pltpu.make_async_remote_copy(
            src_ref=kv_ref.at[batch, rows_at(step + steps - need, block)],
            dst_ref=pad.at[batch, rows_at(step, block)],
            send_sem=halo_send.at[batch, step],
            recv_sem=halo_recv.at[batch, step],
            device_id={"seq": peer},
            device_id_type=MESH,
        )

    def send_halo(turn):
        batch, step = turn // need, need - 1 - lax.rem(turn, need)
        pl.when(has_right)(lambda: halo(batch, step, seq + 1).start())

    def halo_sent(turn):
        batch, step = turn // need, need - 1 - lax.rem(turn, need)
        pl.when(has_right)(lambda: halo(batch, step, seq + 1).wait_send())

    send_halo(0)
    send_halo(1)
    swap = Swap(group, units_ref, own_units_ref, swap_send, swap_recv, swap_keep)
    swap.begin()
    pad[:, WINDOW:, :] = kv_ref[...]

    @pl.when(jnp.logical_not(has_left))
    def _():
        pad[:, :WINDOW, :] = jnp.zeros((batches, WINDOW, 2 * span), jnp.bfloat16)

    def kept(batch):
        return pltpu.make_async_copy(pad.at[batch], pad_ref.at[batch], pad_keep.at[batch])

    vt = vt_ref
    for batch in range(batches):
        vt[:, WINDOW:] = pad[batch, WINDOW:, span:].T

        @pl.loop(0, steps)
        def _(turn, batch=batch):
            step = steps - 1 - turn

            @pl.when(step < need)
            def _():
                rows = rows_at(step, block)
                pl.when(has_left)(lambda: halo(batch, step, seq).wait_recv())
                vt[:, rows] = pad[batch, rows, span:].T
                place = batch * need + need - 1 - step
                halo_sent(place)
                pl.when(place + 2 < batches * need)(lambda: send_halo(place + 2))

            begin = pl.multiple_of(step * block, block)
            keys = pl.ds(begin, block + WINDOW)
            rows = pl.ds(begin, block)
            low = low_ref[batch, :, rows]
            for pair in range(span // PAIR):
                lanes = slice(pair * PAIR, (pair + 1) * PAIR)
                q_pair = q_ref[batch, rows, lanes] * jnp.asarray(HEAD**-0.5, jnp.bfloat16)
                k_rows = pad[batch, keys, lanes]
                values = vt[lanes, keys]
                mixed = []
                for half in range(2):
                    scores = masked_scores(k_rows, head_lanes(q_pair, half), low)
                    top = jnp.max(scores, axis=0, keepdims=True)
                    expo = jnp.exp(scores - top)
                    total = jnp.sum(expo, axis=0, keepdims=True)
                    mixed.append(dot_nn(values, to_half(expo)) / total)
                    row = pair * 2 + half
                    lse_ref[batch, row : row + 1, rows] = top + jnp.log(total)
                lane = lax.broadcasted_iota(jnp.int32, mixed[0].shape, 0)
                out_ref[batch, rows, lanes] = to_half(jnp.where(lane < HEAD, mixed[0], mixed[1]).T)

    for batch in range(batches):
        kept(batch).start()
    swap.end()
    for batch in range(batches):
        kept(batch).wait()


def attend(seqs, group, query, key_value, low, block, units, collective):
    batches, length, span = query.shape
    padded = length + WINDOW
    heads = span // HEAD
    half = jnp.bfloat16
    return pl.pallas_call(
        functools.partial(attend_kernel, seqs, group, block),
        in_specs=[VMEM_SPEC, VMEM_SPEC, VMEM_SPEC, ANY_SPEC],
        out_specs=[VMEM_SPEC, VMEM_SPEC, ANY_SPEC, ANY_SPEC],
        out_shape=[
            jax.ShapeDtypeStruct((batches, length, span), half),
            jax.ShapeDtypeStruct((batches, heads, length), jnp.float32),
            jax.ShapeDtypeStruct((batches, padded, 2 * span), half),
            jax.ShapeDtypeStruct(units.shape, half),
        ],
        scratch_shapes=[
            pltpu.VMEM((batches, padded, 2 * span), half),
            pltpu.VMEM((span, padded), half),
            sems(batches, WINDOW // block),
            sems(batches, WINDOW // block),
            sems(batches),
            sems(group),
            sems(group),
            pltpu.SemaphoreType.DMA,
        ],
        compiler_params=comm_params(collective),
        cost_estimate=cost(
            8 * batches * length * span * (WINDOW + block), 150 * MIB, units.size * 2
        ),
        name="attend",
    )(query, key_value, low, units)


def branch_kernel(
    seqs, chips, a_ref, w_ref, d_ref, units_ref, x_ref, gain_ref, middle_ref, normed_ref, gd_ref, w_units_ref,
    out_ref, acc, cross_out, line_out, cross_in, line_in, sum_send, sum_recv,
    send, recv, d_keep, share_send, share_recv, share_keep,
):
    line = Line(chips)
    rows = out_ref.shape[0]

    def product(slot, tile):
        return dot_nn(left_rows(a_ref, slot, rows), w_ref[:, rows_at(tile, TILE)])

    meet(line.greet() + greet_seq(seqs))
    reduce = Reduce(
        line, product, out_ref, acc, cross_out, line_out, cross_in, line_in, sum_send, sum_recv
    )
    spread = Spread(line, d_ref, gd_ref, send, recv)
    units = Share(seqs, units_ref, w_units_ref, share_send, share_recv, share_keep)
    d_kept = pltpu.make_async_copy(d_ref, gd_ref.at[line.own], d_keep)
    units.begin()
    spread.begin()
    d_kept.start()

    @pl.loop(0, reduce.steps())
    def _(step):
        reduce.step(step)
        pl.when(lax.rem(step, 2) == 1)(lambda: spread.relay((step + 1) // 2))

    @pl.loop(0, rows // 32)
    def _(chunk):
        here = rows_at(chunk, 32)
        middle = x_ref[here, :].astype(jnp.float32) + out_ref[here, :]
        middle_ref[here, :] = middle
        normed_ref[here, :] = to_half(normalize(middle, gain_ref[0:1, :]))

    spread.rest()
    spread.sent()
    reduce.sent()
    d_kept.wait()
    units.end()


def branch_sum(seqs, chips, a, w, d_rows, units, x, gain, collective):
    rows, width = d_rows.shape
    group = 2 * chips
    half = jnp.bfloat16
    return pl.pallas_call(
        functools.partial(branch_kernel, seqs, chips),
        out_shape=[
            jax.ShapeDtypeStruct((rows, width), jnp.float32),
            jax.ShapeDtypeStruct((rows, width), half),
            jax.ShapeDtypeStruct((group, rows, width), half),
            jax.ShapeDtypeStruct((seqs,) + units.shape, half),
        ],
        in_specs=[VMEM_SPEC, VMEM_SPEC, ANY_SPEC, ANY_SPEC, VMEM_SPEC, VMEM_SPEC],
        out_specs=[VMEM_SPEC, VMEM_SPEC, ANY_SPEC, ANY_SPEC],
        scratch_shapes=[pltpu.VMEM((rows, width), jnp.float32)]
        + Reduce.scratch(chips, rows, width)
        + [sems(3, group), sems(group), pltpu.SemaphoreType.DMA]
        + [sems(seqs), sems(seqs), pltpu.SemaphoreType.DMA],
        compiler_params=comm_params(collective),
        cost_estimate=cost(
            2 * group * rows * width * w.shape[0], 250 * MIB, 3 * group * rows * width * 2
        ),
        name="branch_sum",
    )(a, w, d_rows, units, x, gain)


class PairReduce:
    def __init__(self, line, product, out, acc, keep, cross_out, cross_in, line_out, line_in, send, recv):
        self.line, self.product, self.out, self.acc, self.keep = line, product, out, acc, keep
        self.cross_out, self.cross_in, self.line_out, self.line_in = cross_out, cross_in, line_out, line_in
        self.send, self.recv = send, recv
        self.tiles = keep.shape[1] // TILE

    @staticmethod
    def scratch(chips, piece, width):
        half = jnp.bfloat16
        return [
            pltpu.VMEM((piece, width), half),
            pltpu.VMEM((2, piece, width), half),
            pltpu.VMEM((2, piece, width), half),
            pltpu.VMEM((chips + 1, piece, width), half),
            pltpu.SemaphoreType.DMA((3, width // TILE)),
            pltpu.SemaphoreType.DMA((chips + 3, width // TILE)),
        ]

    def cross(self, parity, tile):
        here = rows_at(tile, TILE)
        return pltpu.make_async_remote_copy(
            src_ref=self.cross_out.at[:, here],
            dst_ref=self.cross_in.at[parity, :, here],
            send_sem=self.send.at[0, tile],
            recv_sem=self.recv.at[self.line.chips + 1 + parity, tile],
            device_id={"fsdp": self.line.other},
            device_id_type=MESH,
        )

    def along(self, parity, landing, tile, peer):
        here = rows_at(tile, TILE)
        return pltpu.make_async_remote_copy(
            src_ref=self.line_out.at[parity, :, here],
            dst_ref=self.line_in.at[landing, :, here],
            send_sem=self.send.at[1 + parity, tile],
            recv_sem=self.recv.at[landing, tile],
            device_id={"fsdp": peer},
            device_id_type=MESH,
        )

    def steps(self):
        return 2 * self.line.chips - 1

    def step(self, step):
        line, keep = self.line, self.keep
        piece = keep.shape[0]
        right_side = line.chips - 1 - line.chip
        away = line.chips - 1 - step // 2
        second = lax.rem(step, 2)
        rightward = (right_side >= line.chip) == (second == 0)
        place = line.chip + jnp.where(rightward, away, -away)
        longer = jnp.maximum(right_side, line.chip)
        shorter = jnp.minimum(right_side, line.chip)
        count = longer - away + jnp.maximum(shorter - away, 0) + second
        parity = lax.rem(count + 2 * line.chips, 2)
        upstream = (rightward & line.has_left) | (jnp.logical_not(rightward) & line.has_right)

        @pl.when((place >= 0) & (place < line.chips))
        def _():
            @pl.loop(0, self.tiles)
            def _(tile):
                here = rows_at(tile, TILE)
                self.acc[...] = self.product(place, tile)
                self.cross_out[:, here] = to_half(self.acc[rows_at(1 - line.core, piece), :])
                keep[:, here] = self.acc[rows_at(line.core, piece), :]
                self.cross(parity, tile).start()

            @pl.loop(0, self.tiles)
            def _(tile):
                here = rows_at(tile, TILE)
                self.cross(parity, tile).wait()
                keep[:, here] += self.cross_in[parity, :, here].astype(jnp.float32)

                @pl.when(away > 0)
                def _():
                    pl.when(count >= 2)(
                        lambda: self.along(parity, place, tile, line.own).wait_send()
                    )

                    @pl.when(upstream)
                    def _():
                        self.along(parity, place, tile, line.own).wait_recv()
                        self.line_out[parity, :, here] = to_half(
                            keep[:, here] + self.line_in[place, :, here].astype(jnp.float32)
                        )

                    @pl.when(jnp.logical_not(upstream))
                    def _():
                        self.line_out[parity, :, here] = to_half(keep[:, here])

                    @pl.when(rightward)
                    def _():
                        self.along(parity, place, tile, line.own + 2).start()

                    @pl.when(jnp.logical_not(rightward))
                    def _():
                        landing = jnp.where(away == 1, line.chips, place)
                        self.along(parity, landing, tile, line.own - 2).start()

                @pl.when(away == 0)
                def _():
                    self.out[:, here] = keep[:, here]

                    @pl.when(line.has_left)
                    def _():
                        self.along(parity, place, tile, line.own).wait_recv()
                        self.out[:, here] += self.line_in[place, :, here].astype(jnp.float32)

                    @pl.when(line.has_right)
                    def _():
                        self.along(parity, line.chips, tile, line.own).wait_recv()
                        self.out[:, here] += self.line_in[line.chips, :, here].astype(jnp.float32)

    def sent(self):
        for count in range(max(self.line.chips - 3, 0), self.line.chips - 1):
            pl.loop(0, self.tiles)(
                lambda tile, parity=count % 2: self.along(parity, 0, tile, self.line.own).wait_send()
            )


def feed_kernel(
    chips, batches, x_ref, w_hbm, wd_hbm, gd_hbm, v_ref, cot_ref, gain_ref,
    dm_ref, db_ref, gain_grad_ref, hidden_hbm, grad_hbm,
    buf, d_buf, h_buf, w_ref, wd_ref, d_ref, tiles, totals, acc, keep,
    load, d_sem, h_sem, tile_sem, send, recv, *sums,
):
    line = Line(chips)
    rows, width = x_ref.shape
    piece = rows // batches
    pair = 2 * piece
    units = wd_ref.shape[0]
    part = min(units, TILE)
    block = tiles.shape[1]
    loads = [
        pltpu.make_async_copy(w_hbm, w_ref, load.at[0]),
        pltpu.make_async_copy(wd_hbm, wd_ref, load.at[1]),
    ]
    for item in loads:
        item.start()
    meet(line.greet())
    spreads = [
        Spread(
            line,
            x_ref.at[pl.ds(batch * piece, piece)],
            buf.at[batch],
            send.at[batch],
            recv.at[batch],
        )
        for batch in range(batches)
    ]
    spreads[0].begin()
    for batch in range(batches):
        buf[batch, line.own] = x_ref[batch * piece : (batch + 1) * piece, :]

    def fetch(batch, place, side):
        return [
            pltpu.make_async_copy(
                gd_hbm.at[place * 2 + core, pl.ds(batch * piece, piece)],
                d_buf.at[side, pl.ds(core * piece, piece)],
                d_sem.at[side, core],
            )
            for core in range(2)
        ]

    def stored(batch, place):
        return [
            pltpu.make_async_copy(
                h_buf.at[pl.ds(core * piece, piece)],
                hidden_hbm.at[
                    pl.ds(pl.multiple_of((place * 2 + core) * rows + batch * piece, piece), piece)
                ],
                h_sem.at[core],
            )
            for core in range(2)
        ]

    def sides(far, act):
        @pl.loop(0, 2)
        def _(side):
            place = line.chip + far * (2 * side - 1)
            valid = (place >= 0) & (place < chips) & ((side == 0) | (far > 0))
            pl.when(valid)(lambda: act(place, side))

    def take(batch, far):
        def begin(place, side):
            for item in fetch(batch, place, side):
                item.start()

        sides(far, begin)
        pl.when(far > 0)(lambda: spreads[batch].relay(far))

    def compute(batch, far):
        def act(place, side):
            spreads[batch].move(place * 2 + 1 - line.core, 2, line.own).wait_recv()
            for item in fetch(batch, place, side):
                item.wait()

            def free():
                for item in stored(batch, place):
                    item.wait()

            if batch:
                free()
            else:
                pl.when((far > 0) | (side > 0))(free)
            there = rows_at(place, pair)

            @pl.loop(0, units // part)
            def _(tile):
                first = rows_at(tile, part)
                second = rows_at(units // part + tile, part)
                values = buf[batch, pl.ds(place * 2, 2), :, :].reshape(pair, width)
                gate = dot_nn(values, w_ref[:, first])
                up = dot_nn(values, w_ref[:, second])
                d_hidden = dot_nt(d_buf[side], wd_ref[first, :])
                sigma = jax.nn.sigmoid(gate)
                swish = gate * sigma
                h_buf[:, first] = to_half(swish * up)
                slope = sigma * (1.0 + gate * (1.0 - sigma))
                d_ref[batch, there, first] = to_half(d_hidden * up * slope)
                d_ref[batch, there, second] = to_half(d_hidden * swish)

            for item in stored(batch, place):
                item.start()

        sides(far, act)

    def product(batch):
        def get(place, tile):
            return dot_nt(d_ref[batch, rows_at(place, pair), :], w_ref[rows_at(tile, TILE), :])

        return get

    reduces = [
        PairReduce(line, product(batch), totals.at[batch], acc, keep, *sums[6 * batch : 6 * batch + 6])
        for batch in range(batches)
    ]

    def grad_stored(tile):
        slot = lax.rem(tile, 2)
        return pltpu.make_async_copy(
            tiles.at[slot], grad_hbm.at[rows_at(tile, block)], tile_sem.at[slot]
        )

    count = width // block

    def weight_grad(tile):
        pl.when(tile >= 2)(lambda: grad_stored(tile - 2).wait())
        slot = lax.rem(tile, 2)
        size = min(TILE, 2 * units)

        @pl.loop(0, 2 * units // size)
        def _(column):
            here = rows_at(column, size)
            got = 0.0
            for batch in range(batches):
                left = buf[batch, :, :, rows_at(tile, block)].reshape(2 * chips * piece, block)
                got = got + contract_rows(left, d_ref[batch, :, here])
            tiles[slot, :, here] = to_half(got)

        grad_stored(tile).start()

    def norm_batch(batch):
        own = pl.ds(batch * piece, piece)

        def put(here, d_values):
            there = pl.ds(pl.multiple_of(here.start + batch * piece, here.size), here.size)
            d_middle = cot_ref[there, :].astype(jnp.float32) + d_values
            dm_ref[there, :] = d_middle
            db_ref[there, :] = to_half(d_middle)

        norm_back(piece, v_ref.at[own], totals.at[batch], gain_ref, gain_grad_ref, put)

    gain_grad_ref[...] = jnp.zeros_like(gain_grad_ref)
    for item in loads:
        item.wait()
    last = 2 * chips - 2

    @pl.loop(0, chips)
    def _(far):
        take(0, far)
        pl.when(far == chips - 2)(spreads[1].begin)
        compute(0, far)

    @pl.loop(0, chips - 1)
    def _(far):
        take(1, far)
        reduces[0].step(2 * far)
        reduces[0].step(2 * far + 1)
        compute(1, far)

    take(1, chips - 1)
    compute(1, chips - 1)

    @pl.loop(0, 2)
    def _(step):
        reduces[1].step(step)
        weight_grad(step)

    reduces[0].step(last)
    norm_batch(0)

    @pl.loop(2, last)
    def _(step):
        reduces[1].step(step)
        pl.when(step < count)(lambda: weight_grad(step))

    @pl.loop(last, max(count, last))
    def _(tile):
        weight_grad(tile)

    reduces[1].step(last)
    norm_batch(1)
    for batch in range(batches):
        spreads[batch].sent()
        reduces[batch].sent()
    for item in stored(1, 0):
        item.wait()
    grad_stored(count - 2).wait()
    grad_stored(count - 1).wait()


def feed_forward(chips, batches, x, w, wd, group_d, middle, cot, gain, collective):
    rows, width = x.shape
    group = 2 * chips
    units = wd.shape[0]
    piece = rows // batches
    half = jnp.bfloat16
    return pl.pallas_call(
        functools.partial(feed_kernel, chips, batches),
        out_shape=[
            jax.ShapeDtypeStruct((rows, width), jnp.float32),
            jax.ShapeDtypeStruct((rows, width), half),
            jax.ShapeDtypeStruct((8, width), jnp.float32),
            jax.ShapeDtypeStruct((group * rows, units), half),
            jax.ShapeDtypeStruct((width, 2 * units), half),
        ],
        in_specs=[VMEM_SPEC] + [ANY_SPEC] * 3 + [VMEM_SPEC] * 3,
        out_specs=[VMEM_SPEC] * 3 + [ANY_SPEC] * 2,
        scratch_shapes=[
            pltpu.VMEM((batches, group, piece, width), half),
            pltpu.VMEM((2, 2 * piece, width), half),
            pltpu.VMEM((2 * piece, units), half),
            pltpu.VMEM(w.shape, half),
            pltpu.VMEM(wd.shape, half),
            pltpu.VMEM((batches, group * piece, 2 * units), half),
            pltpu.VMEM((2, 256, 2 * units), half),
            pltpu.VMEM((batches, piece, width), jnp.float32),
            pltpu.VMEM((2 * piece, TILE), jnp.float32),
            pltpu.VMEM((piece, width), jnp.float32),
            sems(2),
            sems(2, 2),
            sems(2),
            sems(2),
            sems(batches, 3, group),
            sems(batches, group),
        ]
        + PairReduce.scratch(chips, piece, width) * batches,
        compiler_params=comm_params(collective, 63),
        cost_estimate=cost(
            14 * group * rows * width * units, 400 * MIB, 2 * group * rows * width * 2
        ),
        name="feed_forward",
    )(x, w, wd, group_d, middle, cot, gain)


def branch_back_kernel(
    seqs, chips, batches, x_ref, w_ref, att_ref, middle_ref, hidden_hbm, wd_hbm, units_hbm, gd_hbm,
    d_ref, layer_ref, out_grad_ref, units_in, down_hbm,
    out_ref, buf, hidden_ref, wd_ref, grad_acc, rights, tiles, send, recv, load, right_sem, tile_sem,
    part_send, part_recv, acc, cross_out, line_out, cross_in, line_in, sum_send, sum_recv,
):
    line = Line(chips)
    rows = x_ref.shape[0]
    piece = rows // batches
    width = x_ref.shape[1]
    loads = [
        pltpu.make_async_copy(hidden_hbm, hidden_ref, load.at[0]),
        pltpu.make_async_copy(wd_hbm, wd_ref, load.at[1]),
    ]
    for item in loads:
        item.start()

    def product(slot, tile):
        return dot_nn(left_rows(hidden_ref, slot, rows), wd_ref[:, rows_at(tile, TILE)])

    part = rights.shape[2]
    count = width // part

    def right(tile):
        slot = lax.rem(tile, 2)
        return pltpu.make_async_copy(
            gd_hbm.at[:, rows_at(tile, part)], rights.at[slot], right_sem.at[slot]
        )

    def stored(tile):
        slot = lax.rem(tile, 2)
        return pltpu.make_async_copy(
            tiles.at[slot], down_hbm.at[:, rows_at(tile, part)], tile_sem.at[slot]
        )

    def weight_grad(tile):
        right(tile).wait()
        pl.when(tile + 1 < count)(lambda: right(tile + 1).start())
        pl.when(tile >= 2)(lambda: stored(tile - 2).wait())
        slot = lax.rem(tile, 2)
        size = min(TILE, hidden_ref.shape[1])

        @pl.loop(0, hidden_ref.shape[1] // size)
        def _(row):
            here = rows_at(row, size)
            tiles[slot, here, :] = to_half(contract_rows(hidden_ref[:, here], rights[slot]))

        stored(tile).start()

    right(0).start()
    meet(line.greet() + greet_seq(seqs))
    sums = ToSeq(seqs, units_hbm, units_in, part_send, part_recv)
    spread = Spread(line, x_ref, buf, send, recv)
    reduce = Reduce(
        line, product, out_ref, acc, cross_out, line_out, cross_in, line_in, sum_send, sum_recv
    )
    spread.begin()
    sums.begin()
    buf[line.own] = x_ref[...]
    grad_acc[...] = jnp.zeros_like(grad_acc)

    def use(slot):
        got = to_half(dot_nt(buf[slot], w_ref[...]))
        for batch in range(batches):
            d_ref[batch, rows_at(slot, piece), :] = got[batch * piece : (batch + 1) * piece]
        mixed = left_rows(att_ref, slot, rows)

        @pl.loop(0, width // TILE)
        def _(tile):
            here = rows_at(tile, TILE)
            grad_acc[:, here] += contract_rows(mixed, buf[slot, :, here])

    for item in loads:
        item.wait()

    per = -(-count // reduce.steps())

    @pl.loop(0, reduce.steps())
    def _(step):
        reduce.step(step)

        @pl.when(lax.rem(step, 2) == 1)
        def _():
            far = (step + 1) // 2
            spread.relay(far)
            spread.each(far - 1, use)

        @pl.loop(0, per)
        def _(turn):
            tile = step * per + turn
            pl.when(tile < count)(lambda: weight_grad(tile))

    spread.each(chips - 1, use)
    spread.each(chips, use)

    @pl.loop(0, rows // 32)
    def _(chunk):
        here = rows_at(chunk, 32)
        layer_ref[here, :] = to_half(middle_ref[here, :] + out_ref[here, :])

    out_grad_ref[...] = to_half(grad_acc[...])
    spread.sent()
    reduce.sent()
    sums.end()
    stored(count - 2).wait()
    stored(count - 1).wait()


def branch_back(seqs, chips, batches, x, w, attended, middle, hidden, wd, unit_part, group_d, collective):
    rows, width = x.shape
    group = 2 * chips
    length = group * rows // batches
    span = w.shape[0]
    half = jnp.bfloat16
    part = 256 if group * rows <= 2048 else 128
    return pl.pallas_call(
        functools.partial(branch_back_kernel, seqs, chips, batches),
        out_shape=[
            jax.ShapeDtypeStruct((batches, length, span), half),
            jax.ShapeDtypeStruct((rows, width), half),
            jax.ShapeDtypeStruct((span, width), half),
            jax.ShapeDtypeStruct((seqs, width // seqs, unit_part.shape[1]), half),
            jax.ShapeDtypeStruct((wd.shape[0], width), half),
        ],
        in_specs=[VMEM_SPEC] * 4 + [ANY_SPEC] * 4,
        out_specs=[VMEM_SPEC, VMEM_SPEC, VMEM_SPEC, ANY_SPEC, ANY_SPEC],
        scratch_shapes=[
            pltpu.VMEM((rows, width), jnp.float32),
            pltpu.VMEM((group, rows, width), half),
            pltpu.VMEM(hidden.shape, half),
            pltpu.VMEM(wd.shape, half),
            pltpu.VMEM((span, width), jnp.float32),
            pltpu.VMEM((2, group * rows, part), half),
            pltpu.VMEM((2, wd.shape[0], part), half),
            sems(3, group),
            sems(group),
            sems(2),
            sems(2),
            sems(2),
            sems(seqs),
            sems(seqs),
        ]
        + Reduce.scratch(chips, rows, width),
        compiler_params=comm_params(collective, 62),
        cost_estimate=cost(
            2 * group * rows * width * (2 * span + 2 * wd.shape[0]),
            250 * MIB,
            2 * group * rows * width * 2,
        ),
        name="branch_back",
    )(x, w, attended, middle, hidden, wd, unit_part, group_d.reshape(group * rows, width))


def attend_back_kernel(
    seqs, group, block, q_ref, pad_ref, low_ref, lse_ref, d_ref, part_hbm, in_hbm, heads_ref, cols_ref,
    dk, dv, kt, back_out, back_in, halo_send, halo_recv, swap_send, swap_recv, swap_keep,
    parts, sums_ref, load,
):
    seq = lax.axis_index("seq")
    batches, length, span = q_ref.shape
    has_left, has_right = seq > 0, seq < seqs - 1
    run = parts.shape[1]

    def loaded(place, own):
        source = part_hbm.at[rows_at(seq, run)] if own else in_hbm.at[place]
        return pltpu.make_async_copy(source, parts.at[place], load.at[place])

    for place in range(seqs):
        pl.when(place == seq)(lambda place=place: loaded(place, True).start())
        pl.when(place != seq)(lambda place=place: loaded(place, False).start())
    pl.when(has_left)(lambda: signal_seq(seq - 1))
    pl.when(has_right)(lambda: signal_seq(seq + 1))
    meet(greet_group(group) + has_left.astype(jnp.int32) + has_right.astype(jnp.int32))
    for place in range(seqs):
        loaded(place, False).wait()

    @pl.loop(0, group)
    def _(member):
        share = run // group

        @pl.loop(0, share // 16)
        def _(chunk):
            here = pl.ds(pl.multiple_of(member * share + chunk * 16, 16), 16)
            added = parts[0, here, :].astype(jnp.float32)
            for place in range(1, seqs):
                added = added + parts[place, here, :].astype(jnp.float32)
            sums_ref[member, rows_at(chunk, 16), :] = to_half(added)

    swap = Swap(group, sums_ref, cols_ref, swap_send, swap_recv, swap_keep)
    swap.begin()
    steps = length // block
    scale = jnp.asarray(HEAD**-0.5, jnp.bfloat16)

    def halo(batch, step, peer):
        rows = rows_at(step, block)
        return pltpu.make_async_remote_copy(
            src_ref=back_out.at[batch, rows],
            dst_ref=back_in.at[batch, rows],
            send_sem=halo_send.at[batch, step],
            recv_sem=halo_recv.at[batch, step],
            device_id={"seq": peer},
            device_id_type=MESH,
        )

    dk[...] = jnp.zeros_like(dk)
    dv[...] = jnp.zeros_like(dv)
    for batch in range(batches):
        kt[...] = pad_ref[batch, :, :span].T * scale

        @pl.loop(0, steps)
        def _(step, batch=batch):
            begin = pl.multiple_of(step * block, block)
            keys = pl.ds(begin, block + WINDOW)
            rows = pl.ds(begin, block)
            low = low_ref[batch, :, rows]
            for pair in range(span // PAIR):
                lanes = slice(pair * PAIR, (pair + 1) * PAIR)
                q_pair = q_ref[batch, rows, lanes] * scale
                d_pair = d_ref[batch, rows, lanes]
                k_rows = pad_ref[batch, keys, lanes]
                v_rows = pad_ref[batch, keys, span + pair * PAIR : span + (pair + 1) * PAIR]
                k_cols = kt[lanes, keys]
                back = []
                for half in range(2):
                    row = pair * 2 + half
                    q_head = head_lanes(q_pair, half)
                    d_head = head_lanes(d_pair, half)
                    scores = masked_scores(k_rows, q_head, low)
                    probs = jnp.exp(scores - lse_ref[batch, row : row + 1, rows])
                    d_probs = dot_nt(v_rows, d_head)
                    along = jnp.sum(probs * d_probs, axis=0, keepdims=True)
                    d_scores = to_half(probs * (d_probs - along))
                    dv[batch, keys, lanes] += dot_nn(to_half(probs), d_head)
                    dk[batch, keys, lanes] += dot_nn(d_scores, q_head)
                    back.append(dot_nn(k_cols, d_scores))
                at = lax.broadcasted_iota(jnp.int32, back[0].shape, 0)
                heads_ref[batch, rows, lanes] = to_half(
                    jnp.where(at < HEAD, back[0], back[1]).T
                )

            @pl.when(has_left & (step < WINDOW // block))
            def _():
                back_out[batch, rows, :span] = to_half(dk[batch, rows, :])
                back_out[batch, rows, span:] = to_half(dv[batch, rows, :])
                halo(batch, step, seq - 1).start()

    first = length - WINDOW
    for batch in range(batches):
        if first:
            heads_ref[batch, :first, span : 2 * span] = to_half(dk[batch, WINDOW:length, :])
            heads_ref[batch, :first, 2 * span :] = to_half(dv[batch, WINDOW:length, :])

        @pl.loop(0, WINDOW // block)
        def _(step, batch=batch):
            inner = pl.ds(pl.multiple_of(step * block + length, block), block)
            rows = pl.ds(pl.multiple_of(step * block + first, block), block)

            @pl.when(has_right)
            def _():
                halo(batch, step, seq).wait_recv()
                got = back_in[batch, rows_at(step, block), :].astype(jnp.float32)
                heads_ref[batch, rows, span : 2 * span] = to_half(
                    dk[batch, inner, :] + got[:, :span]
                )
                heads_ref[batch, rows, 2 * span :] = to_half(dv[batch, inner, :] + got[:, span:])

            @pl.when(jnp.logical_not(has_right))
            def _():
                heads_ref[batch, rows, span : 2 * span] = to_half(dk[batch, inner, :])
                heads_ref[batch, rows, 2 * span :] = to_half(dv[batch, inner, :])

            pl.when(has_left)(lambda: halo(batch, step, seq).wait_send())

    swap.end()


def attend_back(seqs, group, query, kv_pad, low, lse, d_att, block, part, parts_in, collective):
    batches, length, span = query.shape
    padded = kv_pad.shape[1]
    half = jnp.bfloat16
    share = part.shape[0] // seqs // group
    sums = (group, share, part.shape[1])
    return pl.pallas_call(
        functools.partial(attend_back_kernel, seqs, group, block),
        in_specs=[VMEM_SPEC] * 5 + [ANY_SPEC] * 2,
        out_specs=[VMEM_SPEC, ANY_SPEC],
        out_shape=[
            jax.ShapeDtypeStruct((batches, length, 3 * span), half),
            jax.ShapeDtypeStruct(sums, half),
        ],
        scratch_shapes=[
            pltpu.VMEM((batches, padded, span), jnp.float32),
            pltpu.VMEM((batches, padded, span), jnp.float32),
            pltpu.VMEM((span, padded), half),
            pltpu.VMEM((batches, WINDOW, 2 * span), half),
            pltpu.VMEM((batches, WINDOW, 2 * span), half),
            sems(batches, WINDOW // block),
            sems(batches, WINDOW // block),
            sems(group),
            sems(group),
            pltpu.SemaphoreType.DMA,
            pltpu.VMEM(parts_in.shape, half),
            pltpu.VMEM(sums, half),
            sems(seqs),
        ],
        compiler_params=comm_params(collective),
        cost_estimate=cost(
            20 * batches * length * span * (WINDOW + block), 180 * MIB, part.size // seqs * 2
        ),
        name="attend_back",
    )(query, kv_pad, low, lse, d_att, part, parts_in)


def heads_back_kernel(
    seqs, chips, a_ref, w_ref, g_hbm, v_ref, dm_ref, gain_ref, mlp_gain_ref, units_hbm, out_ref, down_hbm,
    grad_ref, q_ref, k_ref, v_out_ref, wo_ref, tile_ref, gate_ref, up_ref, down_in,
    down_send, down_recv,     units, unit_load, out_in, out_send, out_recv, total, gain_acc, lefts, parts, sums, cols, gain_out, gain_in, gain_sum, gain_back,
    left_sem, part_send, part_recv, cols_send, cols_recv,
    gain_send, gain_recv, back_send, back_recv,
    acc, cross_out, line_out, cross_in, line_in, sum_send, sum_recv,
):
    line = Line(chips)
    group = 2 * chips
    seq = lax.axis_index("seq")
    own = line.own
    rows, width = v_ref.shape
    batches = a_ref.shape[0]
    part = lefts.shape[3]
    run = width // seqs
    share = run // group
    depth = a_ref.shape[2]

    def left(tile):
        slot = lax.rem(tile, 2)
        return pltpu.make_async_copy(
            g_hbm.at[:, :, rows_at(tile, part)], lefts.at[slot], left_sem.at[slot]
        )

    def weight_grad(tile):
        left(tile).wait()
        pl.when(tile + 1 < width // part)(lambda: left(tile + 1).start())
        slot = lax.rem(tile, 2)
        got = contract_rows(lefts[slot, 0], a_ref[0])
        for batch in range(1, batches):
            got = got + contract_rows(lefts[slot, batch], a_ref[batch])
        parts[rows_at(tile, part), :] = to_half(got)

    def to_seq(peer, place):
        return pltpu.make_async_remote_copy(
            src_ref=parts.at[rows_at(peer, run)],
            dst_ref=sums.at[place],
            send_sem=part_send.at[peer],
            recv_sem=part_recv.at[place],
            device_id={"seq": peer},
            device_id_type=MESH,
        )

    def others(count, me, act):
        pl.loop(1, count)(lambda ahead: act(lax.rem(me + ahead, count)))

    def product(slot, tile):
        return dot_nt(left_rows(a_ref, slot, rows), w_ref[rows_at(tile, TILE), :])

    size = down_in.shape[1]
    cut = size // 16 * 3 // 8 * 16
    downs = [
        ToSeq(seqs, down_hbm, down_in, down_send.at[0], down_recv.at[0], 0, cut),
        ToSeq(seqs, down_hbm, down_in, down_send.at[1], down_recv.at[1], cut, size - cut),
    ]
    from_seq = ToSeq(seqs, out_ref, out_in, out_send, out_recv)
    units_in = pltpu.make_async_copy(units_hbm, units, unit_load)
    units_in.start()
    left(0).start()
    meet(greet_group(group) + greet_seq(seqs))
    downs[0].begin()
    reduce = Reduce(
        line, product, total, acc, cross_out, line_out, cross_in, line_in, sum_send, sum_recv
    )
    count = width // part
    per = -(-count // 2)

    @pl.loop(0, 2)
    def _(step):
        reduce.step(step)

        @pl.loop(0, per)
        def _(turn):
            tile = step * per + turn
            pl.when(tile < count)(lambda: weight_grad(tile))

    others(seqs, seq, lambda peer: to_seq(peer, seq).start())
    from_seq.begin()
    units_in.wait()
    block = units.shape[2] // 2 // seqs
    for member in range(group):
        for place in range(seqs):
            column = (place * group + member) * block
            for target, begin in ((gate_ref, 0), (up_ref, seqs * block)):
                here = slice(begin + place * block, begin + (place + 1) * block)
                target[:, column : column + block] = units[member, :, here]

    pl.loop(2, 2 * chips - 2)(reduce.step)

    def block_swap(peer, member):
        return pltpu.make_async_remote_copy(
            src_ref=parts.at[rows_at(seq * group + peer, share)],
            dst_ref=cols.at[member],
            send_sem=cols_send.at[peer],
            recv_sem=cols_recv.at[member],
            device_id={"fsdp": peer},
            device_id_type=MESH,
        )

    others(seqs, seq, lambda peer: to_seq(peer, peer).wait_recv())
    downs[1].begin()

    @pl.loop(0, run // 64)
    def _(chunk):
        here = rows_at(chunk, 64)
        there = pl.ds(pl.multiple_of(seq * run + chunk * 64, 64), 64)
        parts[there, :] = to_half(add_from_seq(seqs, parts[there, :], sums, here))

    others(group, own, lambda peer: block_swap(peer, own).start())
    cols[own] = parts[rows_at(seq * group + own, share), :]
    from_seq.arrived()
    size = out_in.shape[1]
    wo_ref[...] = add_from_seq(seqs, out_ref[rows_at(seq, size), :], out_in, slice(None))
    reduce.step(2 * chips - 2)

    def put(here, d_values):
        grad_ref[here, :] = dm_ref[here, :] + d_values

    gain_acc[...] = jnp.zeros_like(gain_acc)
    norm_back(rows, v_ref, total, gain_ref, gain_acc, put)
    fold = 128 // share
    near = group // fold
    attn_row = jnp.sum(gain_acc[...], axis=0, keepdims=True)
    mlp_row = jnp.sum(mlp_gain_ref[...], axis=0, keepdims=True)
    gain_out[...] = jnp.zeros_like(gain_out)
    for place in range(width // 128):
        lanes = slice(place * 128, (place + 1) * 128)
        gain_out[place % near, place // near, 0:1, :] = attn_row[:, lanes]
        gain_out[place % near, place // near, 1:2, :] = mlp_row[:, lanes]

    def gain_group(peer, member):
        return pltpu.make_async_remote_copy(
            src_ref=gain_out.at[peer // fold],
            dst_ref=gain_in.at[member],
            send_sem=gain_send.at[peer],
            recv_sem=gain_recv.at[member],
            device_id={"fsdp": peer},
            device_id_type=MESH,
        )

    def gain_seq(peer, place):
        return pltpu.make_async_remote_copy(
            src_ref=gain_sum.at[peer],
            dst_ref=gain_back.at[place],
            send_sem=back_send.at[peer],
            recv_sem=back_recv.at[place],
            device_id={"seq": peer},
            device_id_type=MESH,
        )

    others(group, own, lambda peer: gain_group(peer, own).start())
    gain_in[own] = gain_out[own // fold]
    others(group, own, lambda peer: gain_group(peer, peer).wait_recv())
    gain_sum[...] = jnp.sum(gain_in[...], axis=0)
    others(seqs, seq, lambda peer: gain_seq(peer, seq).start())
    gain_back[seq] = gain_sum[seq]
    others(seqs, seq, lambda peer: gain_seq(peer, peer).wait_recv())
    tile_ref[...] = jnp.sum(gain_back[...], axis=0)
    others(group, own, lambda peer: block_swap(peer, peer).wait_recv())
    span = depth // 3
    for index, target in enumerate((q_ref, k_ref, v_out_ref)):
        for member, first, home, size in column_parts(seqs, group, share, span):
            first = first + index * span
            target[:, home : home + size] = cols[member, :, first : first + size]
    from_seq.sent()
    for item in downs:
        item.end()
    reduce.sent()
    others(seqs, seq, lambda peer: to_seq(peer, seq).wait_send())
    others(group, own, lambda peer: gain_group(peer, own).wait_send())
    others(group, own, lambda peer: block_swap(peer, own).wait_send())
    others(seqs, seq, lambda peer: gain_seq(peer, seq).wait_send())


def heads_back(seqs, chips, a, w, group_a, x, d_middle, gain, mlp_gain, units, out_part, down, collective):
    rows, width = x.shape
    batches, length, depth = a.shape
    group = 2 * chips
    share = width // seqs // group
    near = group // (128 // share)
    half = jnp.bfloat16
    part = 256 if batches * length <= 2048 else 128
    return pl.pallas_call(
        functools.partial(heads_back_kernel, seqs, chips),
        out_shape=[
            jax.ShapeDtypeStruct((rows, width), jnp.float32),
            jax.ShapeDtypeStruct((share, width), half),
            jax.ShapeDtypeStruct((share, width), half),
            jax.ShapeDtypeStruct((share, width), half),
            jax.ShapeDtypeStruct((out_part.shape[0] // seqs, width), jnp.float32),
            jax.ShapeDtypeStruct((8, 128), jnp.float32),
            jax.ShapeDtypeStruct((share, units.size // 2 // share), half),
            jax.ShapeDtypeStruct((share, units.size // 2 // share), half),
            jax.ShapeDtypeStruct((seqs, down.shape[0] // seqs, width), half),
        ],
        in_specs=[VMEM_SPEC, VMEM_SPEC, ANY_SPEC] + [VMEM_SPEC] * 4 + [ANY_SPEC, VMEM_SPEC, ANY_SPEC],
        out_specs=[VMEM_SPEC] * 8 + [ANY_SPEC],
        scratch_shapes=[
            sems(2, seqs),
            sems(2, seqs),
            pltpu.VMEM(units.shape, half),
            pltpu.SemaphoreType.DMA,
            pltpu.VMEM((seqs, out_part.shape[0] // seqs, width), half),
            sems(seqs),
            sems(seqs),
            pltpu.VMEM((rows, width), jnp.float32),
            pltpu.VMEM((8, width), jnp.float32),
            pltpu.VMEM((2, batches, length, part), half),
            pltpu.VMEM((width, depth), half),
            pltpu.VMEM((seqs, width // seqs, depth), half),
            pltpu.VMEM((group, share, depth), half),
            pltpu.VMEM((near, seqs, 8, 128), jnp.float32),
            pltpu.VMEM((group, seqs, 8, 128), jnp.float32),
            pltpu.VMEM((seqs, 8, 128), jnp.float32),
            pltpu.VMEM((seqs, 8, 128), jnp.float32),
            sems(2),
            sems(seqs),
            sems(seqs),
            sems(group),
            sems(group),
            sems(group),
            sems(group),
            sems(seqs),
            sems(seqs),
        ]
        + Reduce.scratch(chips, rows, width),
        compiler_params=comm_params(collective, 60),
        cost_estimate=cost(
            4 * group * rows * width * depth, 200 * MIB, 2 * group * rows * width * 2
        ),
        name="heads_back",
    )(a, w, group_a, x, d_middle, gain, mlp_gain, units, out_part, down)


def doc_starts(lengths, positions, batches, seq_len):
    table = lengths.reshape(batches, -1, lengths.shape[1])
    starts = jnp.cumsum(table, axis=2) - table
    per_batch = seq_len // table.shape[1]
    begins = (starts + (jnp.arange(table.shape[1], dtype=jnp.int32) * per_batch)[None, :, None]).reshape(
        batches, -1
    )
    before = begins[:, None, :] <= positions[None, :, None]
    return jnp.max(jnp.where(before, begins[:, None, :], 0), axis=2)


def body(
    tokens,
    cotangent,
    lengths,
    gain_attn,
    w_query,
    w_key,
    w_value,
    w_out,
    gain_mlp,
    w_gate,
    w_up,
    w_down,
):
    batches, piece, width = tokens.shape
    seqs = lax.axis_size("seq")
    group = lax.axis_size("fsdp")
    chips = group // 2
    devices = seqs * group
    seq_len = piece * devices
    rows = batches * piece
    share = w_query.shape[0]
    span = width // group
    length = group * piece
    aligned = share == HEAD
    member = lax.axis_index("fsdp")

    def blocks(weight):
        part = weight.shape[1] // devices
        return weight.reshape(share, seqs, group, part).transpose(2, 0, 1, 3).reshape(group, share, -1)

    x_rows = tokens.reshape(rows, width)
    cot_rows = cotangent.reshape(rows, width)
    wd_part = lax.all_gather(w_down, "seq", axis=0, tiled=True)
    if aligned:
        wo_part = lax.all_gather(w_out, "seq", axis=0, tiled=True)
    else:
        wo_all = lax.all_gather(w_out, ("seq", "fsdp"), axis=0, tiled=True)
        wo_part = lax.dynamic_slice_in_dim(wo_all, member * span, span, 0)

    unit_blocks = jnp.concatenate([blocks(w_gate), blocks(w_up)], axis=2)
    lane = jnp.arange(128, dtype=jnp.int32)
    device = lax.axis_index("seq") * group + member
    fold = 128 // share
    here = lane // share == lax.rem(device, fold)
    both = jnp.stack([gain_attn, gain_mlp]).astype(jnp.float32)
    tile = jnp.where(here[None], jnp.tile(both, (1, fold)), 0.0)
    tile = jnp.pad(tile, ((0, 6), (0, 0)))[None]
    group_a, query, key_value, gains, w_heads = start(
        seqs, chips, batches, tile, x_rows, (w_query, w_key, w_value), 1
    )
    lengths, gains = lax.optimization_barrier((lengths, gains))
    group_start = lax.axis_index("seq") * length
    positions = group_start + jnp.arange(length, dtype=jnp.int32)
    begins = doc_starts(lengths, positions, batches, seq_len)
    at = jnp.arange(length, dtype=jnp.int32)
    block = min(256, length)
    low = jnp.maximum(begins - group_start + WINDOW, at[None, :] + 1) - (at // block * block)[None, :]
    low = low[:, None, :]

    gains = gains.transpose(1, 0, 2, 3).reshape(devices // fold, fold, 8, 128).sum(axis=1)
    gain_one = gains[:, 0].reshape(width)
    gain_two = gains[:, 1].reshape(width)
    attended, lse, kv_pad, unit_own = attend(
        seqs, group, query, key_value, low, block, unit_blocks, 2
    )
    middle, normed_b, group_d, w_units = branch_sum(
        seqs, chips, attended, wo_part, cot_rows, unit_own.reshape(group * share, -1),
        x_rows, gain_two[None], 3,
    )
    w_units = w_units.reshape(width, -1)
    d_middle, d_branch, mlp_gain_part, hidden, unit_part = feed_forward(
        chips, batches, normed_b, w_units, wd_part, group_d, middle, cot_rows, gain_two[None], 4
    )
    d_attended, layer_out, out_part, unit_in, down_part = branch_back(
        seqs, chips, batches, d_branch, wo_part, attended, middle, hidden, wd_part, unit_part,
        group_d, 5,
    )
    d_heads, unit_cols = attend_back(
        seqs, group, query, kv_pad, low, lse, d_attended, block, unit_part, unit_in, 6
    )
    if not aligned:
        whole = lax.dynamic_update_slice_in_dim(
            jnp.zeros((width, width), jnp.bfloat16), out_part, member * span, 0
        )
        out_part = lax.psum(whole, "fsdp").reshape(seqs, group, share, width)
        out_part = lax.dynamic_slice_in_dim(out_part, member, 1, 1).reshape(seqs * share, width)
    input_grad, wq_grad, wk_grad, wv_grad, wo_grad, gain_tile, gate_grad, up_grad, down_in = heads_back(
        seqs, chips, d_heads, w_heads, group_a, x_rows, d_middle, gain_one[None], mlp_gain_part,
        unit_cols, out_part, down_part, 7,
    )
    run = lax.axis_index("seq")
    down_own = lax.dynamic_slice_in_dim(down_part, run * w_down.shape[0], w_down.shape[0], 0)
    others = jnp.arange(seqs)[:, None, None] != run
    down_sum = jnp.sum(jnp.where(others, down_in.astype(jnp.float32), 0.0), axis=0)
    gain_grads = lax.dynamic_slice_in_dim(gain_tile[:2], lax.rem(device, fold) * share, share, 1)
    wide = jnp.float32
    return (
        layer_out.reshape(batches, piece, width),
        input_grad.reshape(batches, piece, width),
        gain_grads[0],
        wq_grad.astype(wide),
        wk_grad.astype(wide),
        wv_grad.astype(wide),
        wo_grad,
        gain_grads[1],
        gate_grad.astype(wide),
        up_grad.astype(wide),
        down_sum + down_own.astype(wide),
    )


def solution(mesh):
    spread = ("seq", "fsdp")
    tokens, rows, gains = P(None, spread, None), P(spread, None), P(spread)
    in_specs = (tokens, tokens, P(), gains, rows, rows, rows, rows, gains, rows, rows, rows)
    out_specs = (tokens, tokens, gains, rows, rows, rows, rows, gains, rows, rows, rows)
    return jax.shard_map(body, mesh=mesh, in_specs=in_specs, out_specs=out_specs, check_vma=False)
```

```python
import functools

import jax
import jax.numpy as jnp
from jax import lax
from jax.experimental import pallas as pl
from jax.experimental.pallas import tpu as pltpu
from jax.sharding import PartitionSpec as P

HEAD = 64
FF = 8192
WINDOW = 1024
PAIR = 128
TILE = 512
LOW = -1e30
EPS = 1e-05
MESH = pl.DeviceIdType.MESH
MIB = 2**20


def to_half(values):
    return values.astype(jnp.bfloat16)


def normalize(values, gain):
    return values * lax.rsqrt(jnp.mean(values * values, axis=-1, keepdims=True) + EPS) * gain


def contract_rows(left, right):
    return lax.dot_general(
        left, right, (((0,), (0,)), ((), ())), preferred_element_type=jnp.float32
    )


def dot_nt(left, right):
    return lax.dot_general(
        left, right, (((1,), (1,)), ((), ())), preferred_element_type=jnp.float32
    )


def dot_nn(left, right):
    return jnp.dot(left, right, preferred_element_type=jnp.float32)


def head_lanes(values, half):
    lane = lax.broadcasted_iota(jnp.int32, values.shape, 1)
    return jnp.where((lane >= HEAD) == (half == 1), values, jnp.zeros_like(values))


def masked_scores(k_rows, q_head, low):
    keys, block = k_rows.shape[0], q_head.shape[0]
    scores = dot_nt(k_rows, q_head)
    at = lax.broadcasted_iota(jnp.int32, (keys, block), 0)
    query = lax.broadcasted_iota(jnp.int32, (keys, block), 1)
    seen = (at >= low) & (at <= query + WINDOW)
    return jnp.where(seen, scores, LOW)


class Line:
    def __init__(self, chips):
        self.chips = chips
        self.own = lax.axis_index("fsdp")
        self.chip = self.own // 2
        self.core = lax.rem(self.own, 2)
        self.other = self.own + 1 - 2 * self.core
        self.has_left = self.chip > 0
        self.has_right = self.chip < chips - 1

    def greet(self):
        signal_group(self.other)
        pl.when(self.has_left)(lambda: signal_group(self.own - 2))
        pl.when(self.has_right)(lambda: signal_group(self.own + 2))
        return 1 + self.has_left.astype(jnp.int32) + self.has_right.astype(jnp.int32)


def signal_group(peer):
    barrier = pltpu.get_barrier_semaphore()
    pl.semaphore_signal(barrier, inc=1, device_id={"fsdp": peer}, device_id_type=MESH)


def signal_seq(peer):
    barrier = pltpu.get_barrier_semaphore()
    pl.semaphore_signal(barrier, inc=1, device_id={"seq": peer}, device_id_type=MESH)


def greet_group(group):
    own = lax.axis_index("fsdp")
    pl.loop(1, group)(lambda ahead: signal_group(lax.rem(own + ahead, group)))
    return group - 1


def greet_seq(seqs):
    own = lax.axis_index("seq")
    pl.loop(1, seqs)(lambda ahead: signal_seq(lax.rem(own + ahead, seqs)))
    return seqs - 1


def meet(count):
    pl.semaphore_wait(pltpu.get_barrier_semaphore(), count)


def rows_at(index, size):
    return pl.ds(pl.multiple_of(index * size, size), size)


class Spread:
    def __init__(self, line, first, buf, send, recv):
        self.line, self.first, self.buf, self.send, self.recv = line, first, buf, send, recv

    def move(self, slot, way, peer, source=None):
        return pltpu.make_async_remote_copy(
            src_ref=self.buf.at[slot] if source is None else source,
            dst_ref=self.buf.at[slot],
            send_sem=self.send.at[way, slot],
            recv_sem=self.recv.at[slot],
            device_id={"fsdp": peer},
            device_id_type=MESH,
        )

    def begin(self):
        line = self.line
        pl.when(line.has_right)(lambda: self.move(line.own, 1, line.own + 2, self.first).start())
        pl.when(line.has_left)(lambda: self.move(line.own, 0, line.own - 2, self.first).start())
        self.move(line.own, 2, line.other, self.first).start()

    def relay(self, far):
        line = self.line

        @pl.when(line.chip - far >= 0)
        def _():
            slot = (line.chip - far) * 2 + line.core
            self.move(slot, 1, line.own).wait_recv()
            pl.when(line.has_right)(lambda: self.move(slot, 1, line.own + 2).start())
            self.move(slot, 2, line.other).start()

        @pl.when(line.chip + far < line.chips)
        def _():
            slot = (line.chip + far) * 2 + line.core
            self.move(slot, 0, line.own).wait_recv()
            pl.when(line.has_left)(lambda: self.move(slot, 0, line.own - 2).start())
            self.move(slot, 2, line.other).start()

    def each(self, far, use):
        line = self.line

        @pl.loop(0, 4)
        def _(turn):
            side = lax.rem(turn, 2)
            across = turn // 2
            away = far - across
            source = line.chip + away * (2 * side - 1)
            valid = (away >= 0) & (away < line.chips) & (source >= 0) & (source < line.chips)
            valid = valid & ((side == 0) | (away > 0))

            @pl.when(valid)
            def _():
                slot = source * 2 + line.core + across * (1 - 2 * line.core)
                pl.when(across == 1)(lambda: self.move(slot, 2, line.own).wait_recv())
                use(slot)

    def whole(self, use):
        @pl.loop(0, self.line.chips + 1)
        def _(far):
            pl.when(far > 0)(lambda: self.relay(far))
            self.each(far, use)

    def rest(self):
        pl.loop(0, self.line.chips)(
            lambda place: self.move(place * 2 + 1 - self.line.core, 2, self.line.own).wait_recv()
        )

    def sent(self):
        line = self.line

        @pl.loop(0, line.chips)
        def _(place):
            slot = place * 2 + line.core
            self.move(slot, 2, line.other).wait_send()
            pl.when(line.has_right & (place <= line.chip))(
                lambda: self.move(slot, 1, line.own + 2).wait_send()
            )
            pl.when(line.has_left & (place >= line.chip))(
                lambda: self.move(slot, 0, line.own - 2).wait_send()
            )


class Reduce:
    def __init__(self, line, product, out, acc, cross_out, line_out, cross_in, line_in, send, recv):
        self.line, self.product, self.out, self.acc = line, product, out, acc
        self.cross_out, self.line_out, self.cross_in, self.line_in = cross_out, line_out, cross_in, line_in
        self.send, self.recv = send, recv
        self.tiles = line_out.shape[2] // TILE

    @staticmethod
    def scratch(chips, rows, width):
        part = pltpu.VMEM((chips, rows, width), jnp.bfloat16)
        return [
            pltpu.VMEM((rows, TILE), jnp.float32),
            pltpu.VMEM((rows, width), jnp.bfloat16),
            part,
            part,
            pltpu.VMEM((chips + 1, rows, width), jnp.bfloat16),
            pltpu.SemaphoreType.DMA((2, chips, width // TILE)),
            pltpu.SemaphoreType.DMA((2, chips + 1, width // TILE)),
        ]

    def cross(self, place, tile):
        here = rows_at(tile, TILE)
        return pltpu.make_async_remote_copy(
            src_ref=self.cross_out.at[:, here],
            dst_ref=self.cross_in.at[place, :, here],
            send_sem=self.send.at[0, place, tile],
            recv_sem=self.recv.at[0, place, tile],
            device_id={"fsdp": self.line.other},
            device_id_type=MESH,
        )

    def along(self, place, landing, tile, peer):
        here = rows_at(tile, TILE)
        return pltpu.make_async_remote_copy(
            src_ref=self.line_out.at[place, :, here],
            dst_ref=self.line_in.at[landing, :, here],
            send_sem=self.send.at[1, place, tile],
            recv_sem=self.recv.at[1, landing, tile],
            device_id={"fsdp": peer},
            device_id_type=MESH,
        )

    def steps(self):
        return 2 * self.line.chips - 1

    def step(self, step):
        line, acc = self.line, self.acc
        away = line.chips - 1 - step // 2
        rightward = lax.rem(step, 2) == 0
        place = line.chip + jnp.where(rightward, away, -away)
        upstream = (rightward & line.has_left) | (jnp.logical_not(rightward) & line.has_right)

        @pl.when((place >= 0) & (place < line.chips))
        def _():
            @pl.loop(0, self.tiles)
            def _(tile):
                got = self.product(place * 2 + 1 - line.core, tile)
                self.cross_out[:, rows_at(tile, TILE)] = to_half(got)
                self.cross(place, tile).start()

            @pl.loop(0, self.tiles)
            def _(tile):
                here = rows_at(tile, TILE)
                acc[...] = self.product(place * 2 + line.core, tile)
                self.cross(place, tile).wait()
                acc[...] += self.cross_in[place, :, here].astype(jnp.float32)

                @pl.when(away > 0)
                def _():
                    @pl.when(upstream)
                    def _():
                        self.along(place, place, tile, line.own).wait_recv()
                        self.line_out[place, :, here] = to_half(
                            acc[...] + self.line_in[place, :, here].astype(jnp.float32)
                        )

                    @pl.when(jnp.logical_not(upstream))
                    def _():
                        self.line_out[place, :, here] = to_half(acc[...])

                    @pl.when(rightward)
                    def _():
                        self.along(place, place, tile, line.own + 2).start()

                    @pl.when(jnp.logical_not(rightward))
                    def _():
                        landing = jnp.where(away == 1, line.chips, place)
                        self.along(place, landing, tile, line.own - 2).start()

                @pl.when(away == 0)
                def _():
                    self.out[:, here] = acc[...]

                    @pl.when(line.has_left)
                    def _():
                        self.along(place, place, tile, line.own).wait_recv()
                        self.out[:, here] += self.line_in[place, :, here].astype(jnp.float32)

                    @pl.when(line.has_right)
                    def _():
                        self.along(place, line.chips, tile, line.own).wait_recv()
                        self.out[:, here] += self.line_in[line.chips, :, here].astype(jnp.float32)

    def sent(self):
        @pl.loop(0, self.line.chips)
        def _(place):
            @pl.when(place != self.line.chip)
            def _():
                pl.loop(0, self.tiles)(
                    lambda tile: self.along(place, place, tile, self.line.own).wait_send()
                )


class Swap:
    def __init__(self, group, source, target, send, recv, keep):
        self.group, self.source, self.target = group, source, target
        self.send, self.recv, self.keep = send, recv, keep
        self.own = lax.axis_index("fsdp")

    def move(self, peer, source):
        return pltpu.make_async_remote_copy(
            src_ref=self.source.at[peer],
            dst_ref=self.target.at[source],
            send_sem=self.send.at[peer],
            recv_sem=self.recv.at[source],
            device_id={"fsdp": peer},
            device_id_type=MESH,
        )

    def kept(self):
        return pltpu.make_async_copy(self.source.at[self.own], self.target.at[self.own], self.keep)

    def begin(self):
        self.kept().start()
        pl.loop(1, self.group)(
            lambda ahead: self.move(lax.rem(self.own + ahead, self.group), self.own).start()
        )

    def end(self):
        self.kept().wait()

        @pl.loop(1, self.group)
        def _(ahead):
            peer = lax.rem(self.own + ahead, self.group)
            self.move(peer, peer).wait_recv()
            self.move(peer, self.own).wait_send()


class Share:
    def __init__(self, seqs, source, target, send, recv, keep):
        self.seqs, self.source, self.target = seqs, source, target
        self.send, self.recv, self.keep = send, recv, keep
        self.own = lax.axis_index("seq")

    def move(self, peer, place):
        return pltpu.make_async_remote_copy(
            src_ref=self.source,
            dst_ref=self.target.at[place],
            send_sem=self.send.at[peer],
            recv_sem=self.recv.at[place],
            device_id={"seq": peer},
            device_id_type=MESH,
        )

    def kept(self):
        return pltpu.make_async_copy(self.source, self.target.at[self.own], self.keep)

    def begin(self):
        self.kept().start()
        pl.loop(1, self.seqs)(
            lambda ahead: self.move(lax.rem(self.own + ahead, self.seqs), self.own).start()
        )

    def end(self):
        self.kept().wait()

        @pl.loop(1, self.seqs)
        def _(ahead):
            peer = lax.rem(self.own + ahead, self.seqs)
            self.move(peer, peer).wait_recv()
            self.move(peer, self.own).wait_send()


class ToSeq:
    def __init__(self, seqs, source, target, send, recv, first=0, count=None):
        self.seqs, self.source, self.target, self.send, self.recv = seqs, source, target, send, recv
        self.own = lax.axis_index("seq")
        self.first, self.count = first, target.shape[1] if count is None else count

    def move(self, peer, place):
        begin = pl.multiple_of(peer * self.target.shape[1] + self.first, 16)
        return pltpu.make_async_remote_copy(
            src_ref=self.source.at[pl.ds(begin, self.count)],
            dst_ref=self.target.at[place, pl.ds(self.first, self.count)],
            send_sem=self.send.at[peer],
            recv_sem=self.recv.at[place],
            device_id={"seq": peer},
            device_id_type=MESH,
        )

    def begin(self):
        pl.loop(1, self.seqs)(
            lambda ahead: self.move(lax.rem(self.own + ahead, self.seqs), self.own).start()
        )

    def arrived(self):
        @pl.loop(1, self.seqs)
        def _(ahead):
            peer = lax.rem(self.own + ahead, self.seqs)
            self.move(peer, peer).wait_recv()

    def sent(self):
        @pl.loop(1, self.seqs)
        def _(ahead):
            peer = lax.rem(self.own + ahead, self.seqs)
            self.move(peer, self.own).wait_send()

    def end(self):
        self.arrived()
        self.sent()


VMEM_SPEC = pl.BlockSpec(memory_space=pltpu.VMEM)
ANY_SPEC = pl.BlockSpec(memory_space=pl.ANY)


def comm_params(collective, mib=58):
    return pltpu.CompilerParams(
        collective_id=collective, has_side_effects=True, vmem_limit_bytes=mib * MIB
    )


def cost(flops, local, remote):
    return pl.CostEstimate(
        flops=flops, bytes_accessed=local, transcendentals=0, remote_bytes_transferred=remote
    )


def sems(*shape):
    return pltpu.SemaphoreType.DMA(shape)


def left_rows(a_ref, slot, rows):
    if len(a_ref.shape) == 2:
        return a_ref[rows_at(slot, rows), :]
    piece = rows // a_ref.shape[0]
    return jnp.concatenate(
        [a_ref[batch, rows_at(slot, piece), :] for batch in range(a_ref.shape[0])], axis=0
    )


def norm_back(rows, v_ref, e_ref, gain_ref, gain_acc, put):
    @pl.loop(0, rows // 32)
    def _(chunk):
        here = rows_at(chunk, 32)
        values = v_ref[here, :].astype(jnp.float32)
        error = e_ref[here, :]
        rate = lax.rsqrt(jnp.mean(values * values, axis=-1, keepdims=True) + EPS)
        unit = values * rate
        product = error * unit
        gain = gain_ref[0:1, :]
        mean = jnp.mean(product * gain, axis=-1, keepdims=True)
        gain_acc[...] += (product[0:8] + product[8:16]) + (product[16:24] + product[24:32])
        put(here, rate * (gain * error - unit * mean))


def add_from_seq(seqs, own_rows, got, here):
    seq = lax.axis_index("seq")
    added = own_rows.astype(jnp.float32)
    for place in range(seqs):
        piece = got[place, here, :].astype(jnp.float32)
        added = added + jnp.where(place == seq, 0.0, piece)
    return added


def column_parts(seqs, group, share, span):
    size = HEAD if share == HEAD else span
    parts = []
    for member in range(group):
        for run in range(span // size):
            home = (run * group + member) * size
            parts.append((member, run * size, home, size))
    return parts


def start_kernel(
    seqs, chips, batches, tile_ref, x_ref, wq_ref, wk_ref, wv_ref, g_ref, q_ref, kv_ref, gains_ref, w_out_ref,
    blocks_ref, buf, normed, gain, gains, w, send, recv, keep, swap_send, share_send, w_recv,
    tile_send, tile_across, tile_recv, tile_back, w_keep, gain_keep,
):
    line = Line(chips)
    group = 2 * chips
    seq = lax.axis_index("seq")
    own = line.own
    share = blocks_ref.shape[1]
    piece = x_ref.shape[0] // batches
    span = q_ref.shape[2]
    width = x_ref.shape[1]
    per = 128 * seqs * group // width
    for index, source in enumerate((wq_ref, wk_ref, wv_ref)):
        for member, first, home, size in column_parts(seqs, group, share, span):
            first = first + index * span
            blocks_ref[member, :, first : first + size] = source[:, home : home + size]
    meet(greet_group(group) + greet_seq(seqs))

    def block_at(run, member):
        return w.at[rows_at(run * group + member, share)]

    def block_swap(peer, member):
        return pltpu.make_async_remote_copy(
            src_ref=blocks_ref.at[peer],
            dst_ref=block_at(seq, member),
            send_sem=swap_send.at[peer],
            recv_sem=w_recv.at[seq, member],
            device_id={"fsdp": peer},
            device_id_type=MESH,
        )

    def block_share(run, member, peer):
        return pltpu.make_async_remote_copy(
            src_ref=block_at(run, member),
            dst_ref=block_at(run, member),
            send_sem=share_send.at[peer, member],
            recv_sem=w_recv.at[run, member],
            device_id={"seq": peer},
            device_id_type=MESH,
        )

    def tile_to_seq(peer, place):
        return pltpu.make_async_remote_copy(
            src_ref=tile_ref.at[0],
            dst_ref=gains.at[own, place],
            send_sem=tile_send.at[peer],
            recv_sem=tile_recv.at[place],
            device_id={"seq": peer},
            device_id_type=MESH,
        )

    def tiles_to_group(peer, member):
        return pltpu.make_async_remote_copy(
            src_ref=gains.at[member],
            dst_ref=gains.at[member],
            send_sem=tile_across.at[peer],
            recv_sem=tile_back.at[member],
            device_id={"fsdp": peer},
            device_id_type=MESH,
        )

    def others(count, me, act):
        pl.loop(1, count)(lambda ahead: act(lax.rem(me + ahead, count)))

    others(seqs, seq, lambda peer: tile_to_seq(peer, seq).start())
    others(group, own, lambda peer: block_swap(peer, own).start())
    spread = Spread(line, x_ref, buf, send, recv)
    spread.begin()
    gains[own, seq] = tile_ref[0]
    w[rows_at(seq * group + own, share), :] = blocks_ref[own]
    others(seqs, seq, lambda peer: block_share(seq, own, peer).start())
    buf[own] = x_ref[...]
    others(seqs, seq, lambda peer: tile_to_seq(peer, peer).wait_recv())
    others(group, own, lambda peer: tiles_to_group(peer, own).start())

    def pass_block(member):
        block_swap(member, member).wait_recv()
        others(seqs, seq, lambda peer: block_share(seq, member, peer).start())

    others(group, own, pass_block)
    others(group, own, lambda peer: tiles_to_group(peer, peer).wait_recv())
    for column in range(width // 128):
        total = 0.0
        for place in range(column * per, (column + 1) * per):
            total = total + gains[place % group, place // group, 0:1, :]
        gain[0:1, column * 128 : (column + 1) * 128] = total

    def kept(slot, batch):
        return pltpu.make_async_copy(
            normed.at[slot, pl.ds(batch * piece, piece)],
            g_ref.at[batch, rows_at(slot, piece)],
            keep.at[slot, batch],
        )

    def use(slot):
        @pl.loop(0, x_ref.shape[0] // 64)
        def _(chunk):
            rows = rows_at(chunk, 64)
            values = buf[slot, rows, :].astype(jnp.float32)
            normed[slot, rows, :] = to_half(normalize(values, gain[0:1, :]))

        for batch in range(batches):
            kept(slot, batch).start()
        rows = rows_at(slot, piece)
        got = to_half(dot_nn(normed[slot], w[...]))
        for batch in range(batches):
            mine = got[batch * piece : (batch + 1) * piece]
            q_ref[batch, rows, :] = mine[:, :span]
            kv_ref[batch, rows, :] = mine[:, span:]

    pl.loop(1, chips - 1)(spread.relay)

    def have_block(run, member):
        block_share(run, member, seq).wait_recv()

    others(seqs, seq, lambda run: pl.loop(0, group)(lambda member: have_block(run, member)))
    w_kept = pltpu.make_async_copy(w, w_out_ref, w_keep)
    w_kept.start()
    gains_kept = pltpu.make_async_copy(gains, gains_ref, gain_keep)
    gains_kept.start()

    pl.loop(0, chips - 1)(lambda far: spread.each(far, use))
    spread.relay(chips - 1)
    spread.each(chips - 1, use)
    spread.each(chips, use)
    spread.sent()
    others(seqs, seq, lambda peer: tile_to_seq(peer, seq).wait_send())
    others(group, own, lambda peer: block_swap(peer, own).wait_send())
    others(group, own, lambda peer: tiles_to_group(peer, own).wait_send())
    others(
        seqs,
        seq,
        lambda peer: pl.loop(0, group)(lambda member: block_share(seq, member, peer).wait_send()),
    )
    w_kept.wait()
    gains_kept.wait()

    @pl.loop(0, group)
    def _(slot):
        for batch in range(batches):
            kept(slot, batch).wait()


def start(seqs, chips, batches, tile, x, weights, collective):
    rows, width = x.shape
    group = 2 * chips
    length = group * rows // batches
    share = weights[0].shape[0]
    span = width // group
    cols = 3 * span
    half = jnp.bfloat16
    return pl.pallas_call(
        functools.partial(start_kernel, seqs, chips, batches),
        out_shape=[
            jax.ShapeDtypeStruct((batches, length, width), half),
            jax.ShapeDtypeStruct((batches, length, span), half),
            jax.ShapeDtypeStruct((batches, length, 2 * span), half),
            jax.ShapeDtypeStruct((group, seqs, 8, 128), jnp.float32),
            jax.ShapeDtypeStruct((width, cols), half),
        ],
        in_specs=[VMEM_SPEC] * 5,
        out_specs=[ANY_SPEC, VMEM_SPEC, VMEM_SPEC, ANY_SPEC, ANY_SPEC],
        scratch_shapes=[
            pltpu.VMEM((group, share, cols), half),
            pltpu.VMEM((group, rows, width), half),
            pltpu.VMEM((group, rows, width), half),
            pltpu.VMEM((8, width), jnp.float32),
            pltpu.VMEM((group, seqs, 8, 128), jnp.float32),
            pltpu.VMEM((width, cols), half),
            sems(3, group),
            sems(group),
            sems(group, batches),
            sems(group),
            sems(seqs, group),
            sems(seqs, group),
            sems(seqs),
            sems(group),
            sems(seqs),
            sems(group),
            pltpu.SemaphoreType.DMA,
            pltpu.SemaphoreType.DMA,
        ],
        compiler_params=comm_params(collective),
        cost_estimate=cost(2 * group * rows * width * cols, 200 * MIB, group * rows * width * 2),
        name="start",
    )(tile, x, *weights)


def attend_kernel(
    seqs, group, block, q_ref, kv_ref, low_ref, units_ref, out_ref, lse_ref, pad_ref, own_units_ref,
    pad, vt_ref, halo_send, halo_recv, pad_keep, swap_send, swap_recv, swap_keep,
):
    seq = lax.axis_index("seq")
    batches, length, span = q_ref.shape
    has_left, has_right = seq > 0, seq < seqs - 1
    pl.when(has_left)(lambda: signal_seq(seq - 1))
    pl.when(has_right)(lambda: signal_seq(seq + 1))
    meet(greet_group(group) + has_left.astype(jnp.int32) + has_right.astype(jnp.int32))

    steps, need = length // block, WINDOW // block

    def halo(batch, step, peer):
        return pltpu.make_async_remote_copy(
            src_ref=kv_ref.at[batch, rows_at(step + steps - need, block)],
            dst_ref=pad.at[batch, rows_at(step, block)],
            send_sem=halo_send.at[batch, step],
            recv_sem=halo_recv.at[batch, step],
            device_id={"seq": peer},
            device_id_type=MESH,
        )

    def send_halo(turn):
        batch, step = turn // need, need - 1 - lax.rem(turn, need)
        pl.when(has_right)(lambda: halo(batch, step, seq + 1).start())

    def halo_sent(turn):
        batch, step = turn // need, need - 1 - lax.rem(turn, need)
        pl.when(has_right)(lambda: halo(batch, step, seq + 1).wait_send())

    send_halo(0)
    send_halo(1)
    swap = Swap(group, units_ref, own_units_ref, swap_send, swap_recv, swap_keep)
    swap.begin()
    pad[:, WINDOW:, :] = kv_ref[...]

    @pl.when(jnp.logical_not(has_left))
    def _():
        pad[:, :WINDOW, :] = jnp.zeros((batches, WINDOW, 2 * span), jnp.bfloat16)

    def kept(batch):
        return pltpu.make_async_copy(pad.at[batch], pad_ref.at[batch], pad_keep.at[batch])

    vt = vt_ref
    for batch in range(batches):
        vt[:, WINDOW:] = pad[batch, WINDOW:, span:].T

        @pl.loop(0, steps)
        def _(turn, batch=batch):
            step = steps - 1 - turn

            @pl.when(step < need)
            def _():
                rows = rows_at(step, block)
                pl.when(has_left)(lambda: halo(batch, step, seq).wait_recv())
                vt[:, rows] = pad[batch, rows, span:].T
                place = batch * need + need - 1 - step
                halo_sent(place)
                pl.when(place + 2 < batches * need)(lambda: send_halo(place + 2))

            begin = pl.multiple_of(step * block, block)
            keys = pl.ds(begin, block + WINDOW)
            rows = pl.ds(begin, block)
            low = low_ref[batch, :, rows]
            for pair in range(span // PAIR):
                lanes = slice(pair * PAIR, (pair + 1) * PAIR)
                q_pair = q_ref[batch, rows, lanes] * jnp.asarray(HEAD**-0.5, jnp.bfloat16)
                k_rows = pad[batch, keys, lanes]
                values = vt[lanes, keys]
                mixed = []
                for half in range(2):
                    scores = masked_scores(k_rows, head_lanes(q_pair, half), low)
                    top = jnp.max(scores, axis=0, keepdims=True)
                    expo = jnp.exp(scores - top)
                    total = jnp.sum(expo, axis=0, keepdims=True)
                    mixed.append(dot_nn(values, to_half(expo)) / total)
                    row = pair * 2 + half
                    lse_ref[batch, row : row + 1, rows] = top + jnp.log(total)
                lane = lax.broadcasted_iota(jnp.int32, mixed[0].shape, 0)
                out_ref[batch, rows, lanes] = to_half(jnp.where(lane < HEAD, mixed[0], mixed[1]).T)

    for batch in range(batches):
        kept(batch).start()
    swap.end()
    for batch in range(batches):
        kept(batch).wait()


def attend(seqs, group, query, key_value, low, block, units, collective):
    batches, length, span = query.shape
    padded = length + WINDOW
    heads = span // HEAD
    half = jnp.bfloat16
    return pl.pallas_call(
        functools.partial(attend_kernel, seqs, group, block),
        in_specs=[VMEM_SPEC, VMEM_SPEC, VMEM_SPEC, ANY_SPEC],
        out_specs=[VMEM_SPEC, VMEM_SPEC, ANY_SPEC, ANY_SPEC],
        out_shape=[
            jax.ShapeDtypeStruct((batches, length, span), half),
            jax.ShapeDtypeStruct((batches, heads, length), jnp.float32),
            jax.ShapeDtypeStruct((batches, padded, 2 * span), half),
            jax.ShapeDtypeStruct(units.shape, half),
        ],
        scratch_shapes=[
            pltpu.VMEM((batches, padded, 2 * span), half),
            pltpu.VMEM((span, padded), half),
            sems(batches, WINDOW // block),
            sems(batches, WINDOW // block),
            sems(batches),
            sems(group),
            sems(group),
            pltpu.SemaphoreType.DMA,
        ],
        compiler_params=comm_params(collective),
        cost_estimate=cost(
            8 * batches * length * span * (WINDOW + block), 150 * MIB, units.size * 2
        ),
        name="attend",
    )(query, key_value, low, units)


def branch_kernel(
    seqs, chips, a_ref, w_ref, d_ref, units_ref, x_ref, gain_ref, middle_ref, normed_ref, gd_ref, w_units_ref,
    out_ref, acc, cross_out, line_out, cross_in, line_in, sum_send, sum_recv,
    send, recv, d_keep, share_send, share_recv, share_keep,
):
    line = Line(chips)
    rows = out_ref.shape[0]

    def product(slot, tile):
        return dot_nn(left_rows(a_ref, slot, rows), w_ref[:, rows_at(tile, TILE)])

    meet(line.greet() + greet_seq(seqs))
    reduce = Reduce(
        line, product, out_ref, acc, cross_out, line_out, cross_in, line_in, sum_send, sum_recv
    )
    spread = Spread(line, d_ref, gd_ref, send, recv)
    units = Share(seqs, units_ref, w_units_ref, share_send, share_recv, share_keep)
    d_kept = pltpu.make_async_copy(d_ref, gd_ref.at[line.own], d_keep)
    units.begin()
    spread.begin()
    d_kept.start()

    @pl.loop(0, reduce.steps())
    def _(step):
        reduce.step(step)
        pl.when(lax.rem(step, 2) == 1)(lambda: spread.relay((step + 1) // 2))

    @pl.loop(0, rows // 32)
    def _(chunk):
        here = rows_at(chunk, 32)
        middle = x_ref[here, :].astype(jnp.float32) + out_ref[here, :]
        middle_ref[here, :] = middle
        normed_ref[here, :] = to_half(normalize(middle, gain_ref[0:1, :]))

    spread.rest()
    spread.sent()
    reduce.sent()
    d_kept.wait()
    units.end()


def branch_sum(seqs, chips, a, w, d_rows, units, x, gain, collective):
    rows, width = d_rows.shape
    group = 2 * chips
    half = jnp.bfloat16
    return pl.pallas_call(
        functools.partial(branch_kernel, seqs, chips),
        out_shape=[
            jax.ShapeDtypeStruct((rows, width), jnp.float32),
            jax.ShapeDtypeStruct((rows, width), half),
            jax.ShapeDtypeStruct((group, rows, width), half),
            jax.ShapeDtypeStruct((seqs,) + units.shape, half),
        ],
        in_specs=[VMEM_SPEC, VMEM_SPEC, ANY_SPEC, ANY_SPEC, VMEM_SPEC, VMEM_SPEC],
        out_specs=[VMEM_SPEC, VMEM_SPEC, ANY_SPEC, ANY_SPEC],
        scratch_shapes=[pltpu.VMEM((rows, width), jnp.float32)]
        + Reduce.scratch(chips, rows, width)
        + [sems(3, group), sems(group), pltpu.SemaphoreType.DMA]
        + [sems(seqs), sems(seqs), pltpu.SemaphoreType.DMA],
        compiler_params=comm_params(collective),
        cost_estimate=cost(
            2 * group * rows * width * w.shape[0], 250 * MIB, 3 * group * rows * width * 2
        ),
        name="branch_sum",
    )(a, w, d_rows, units, x, gain)


class PairReduce:
    def __init__(self, line, product, out, acc, keep, cross_out, cross_in, line_out, line_in, send, recv):
        self.line, self.product, self.out, self.acc, self.keep = line, product, out, acc, keep
        self.cross_out, self.cross_in, self.line_out, self.line_in = cross_out, cross_in, line_out, line_in
        self.send, self.recv = send, recv
        self.tiles = keep.shape[1] // TILE

    @staticmethod
    def scratch(chips, piece, width):
        half = jnp.bfloat16
        return [
            pltpu.VMEM((piece, width), half),
            pltpu.VMEM((2, piece, width), half),
            pltpu.VMEM((2, piece, width), half),
            pltpu.VMEM((chips + 1, piece, width), half),
            pltpu.SemaphoreType.DMA((3, width // TILE)),
            pltpu.SemaphoreType.DMA((chips + 3, width // TILE)),
        ]

    def cross(self, parity, tile):
        here = rows_at(tile, TILE)
        return pltpu.make_async_remote_copy(
            src_ref=self.cross_out.at[:, here],
            dst_ref=self.cross_in.at[parity, :, here],
            send_sem=self.send.at[0, tile],
            recv_sem=self.recv.at[self.line.chips + 1 + parity, tile],
            device_id={"fsdp": self.line.other},
            device_id_type=MESH,
        )

    def along(self, parity, landing, tile, peer):
        here = rows_at(tile, TILE)
        return pltpu.make_async_remote_copy(
            src_ref=self.line_out.at[parity, :, here],
            dst_ref=self.line_in.at[landing, :, here],
            send_sem=self.send.at[1 + parity, tile],
            recv_sem=self.recv.at[landing, tile],
            device_id={"fsdp": peer},
            device_id_type=MESH,
        )

    def steps(self):
        return 2 * self.line.chips - 1

    def step(self, step):
        line, keep = self.line, self.keep
        piece = keep.shape[0]
        right_side = line.chips - 1 - line.chip
        away = line.chips - 1 - step // 2
        second = lax.rem(step, 2)
        rightward = (right_side >= line.chip) == (second == 0)
        place = line.chip + jnp.where(rightward, away, -away)
        longer = jnp.maximum(right_side, line.chip)
        shorter = jnp.minimum(right_side, line.chip)
        count = longer - away + jnp.maximum(shorter - away, 0) + second
        parity = lax.rem(count + 2 * line.chips, 2)
        upstream = (rightward & line.has_left) | (jnp.logical_not(rightward) & line.has_right)

        @pl.when((place >= 0) & (place < line.chips))
        def _():
            @pl.loop(0, self.tiles)
            def _(tile):
                here = rows_at(tile, TILE)
                self.acc[...] = self.product(place, tile)
                self.cross_out[:, here] = to_half(self.acc[rows_at(1 - line.core, piece), :])
                keep[:, here] = self.acc[rows_at(line.core, piece), :]
                self.cross(parity, tile).start()

            @pl.loop(0, self.tiles)
            def _(tile):
                here = rows_at(tile, TILE)
                self.cross(parity, tile).wait()
                keep[:, here] += self.cross_in[parity, :, here].astype(jnp.float32)

                @pl.when(away > 0)
                def _():
                    pl.when(count >= 2)(
                        lambda: self.along(parity, place, tile, line.own).wait_send()
                    )

                    @pl.when(upstream)
                    def _():
                        self.along(parity, place, tile, line.own).wait_recv()
                        self.line_out[parity, :, here] = to_half(
                            keep[:, here] + self.line_in[place, :, here].astype(jnp.float32)
                        )

                    @pl.when(jnp.logical_not(upstream))
                    def _():
                        self.line_out[parity, :, here] = to_half(keep[:, here])

                    @pl.when(rightward)
                    def _():
                        self.along(parity, place, tile, line.own + 2).start()

                    @pl.when(jnp.logical_not(rightward))
                    def _():
                        landing = jnp.where(away == 1, line.chips, place)
                        self.along(parity, landing, tile, line.own - 2).start()

                @pl.when(away == 0)
                def _():
                    self.out[:, here] = keep[:, here]

                    @pl.when(line.has_left)
                    def _():
                        self.along(parity, place, tile, line.own).wait_recv()
                        self.out[:, here] += self.line_in[place, :, here].astype(jnp.float32)

                    @pl.when(line.has_right)
                    def _():
                        self.along(parity, line.chips, tile, line.own).wait_recv()
                        self.out[:, here] += self.line_in[line.chips, :, here].astype(jnp.float32)

    def sent(self):
        for count in range(max(self.line.chips - 3, 0), self.line.chips - 1):
            pl.loop(0, self.tiles)(
                lambda tile, parity=count % 2: self.along(parity, 0, tile, self.line.own).wait_send()
            )


def feed_kernel(
    chips, batches, x_ref, w_hbm, wd_hbm, gd_hbm, v_ref, cot_ref, gain_ref,
    dm_ref, db_ref, gain_grad_ref, hidden_hbm, grad_hbm,
    buf, d_buf, h_buf, w_ref, wd_ref, d_ref, tiles, totals, acc, keep,
    load, d_sem, h_sem, tile_sem, send, recv, *sums,
):
    line = Line(chips)
    rows, width = x_ref.shape
    piece = rows // batches
    pair = 2 * piece
    units = wd_ref.shape[0]
    part = min(units, TILE)
    block = tiles.shape[1]
    loads = [
        pltpu.make_async_copy(w_hbm, w_ref, load.at[0]),
        pltpu.make_async_copy(wd_hbm, wd_ref, load.at[1]),
    ]
    for item in loads:
        item.start()
    meet(line.greet())
    spreads = [
        Spread(
            line,
            x_ref.at[pl.ds(batch * piece, piece)],
            buf.at[batch],
            send.at[batch],
            recv.at[batch],
        )
        for batch in range(batches)
    ]
    spreads[0].begin()
    for batch in range(batches):
        buf[batch, line.own] = x_ref[batch * piece : (batch + 1) * piece, :]

    def fetch(batch, place, side):
        return [
            pltpu.make_async_copy(
                gd_hbm.at[place * 2 + core, pl.ds(batch * piece, piece)],
                d_buf.at[side, pl.ds(core * piece, piece)],
                d_sem.at[side, core],
            )
            for core in range(2)
        ]

    def stored(batch, place):
        return [
            pltpu.make_async_copy(
                h_buf.at[pl.ds(core * piece, piece)],
                hidden_hbm.at[
                    pl.ds(pl.multiple_of((place * 2 + core) * rows + batch * piece, piece), piece)
                ],
                h_sem.at[core],
            )
            for core in range(2)
        ]

    def sides(far, act):
        @pl.loop(0, 2)
        def _(side):
            place = line.chip + far * (2 * side - 1)
            valid = (place >= 0) & (place < chips) & ((side == 0) | (far > 0))
            pl.when(valid)(lambda: act(place, side))

    def take(batch, far):
        def begin(place, side):
            for item in fetch(batch, place, side):
                item.start()

        sides(far, begin)
        pl.when(far > 0)(lambda: spreads[batch].relay(far))

    def compute(batch, far):
        def act(place, side):
            spreads[batch].move(place * 2 + 1 - line.core, 2, line.own).wait_recv()
            for item in fetch(batch, place, side):
                item.wait()

            def free():
                for item in stored(batch, place):
                    item.wait()

            if batch:
                free()
            else:
                pl.when((far > 0) | (side > 0))(free)
            there = rows_at(place, pair)

            @pl.loop(0, units // part)
            def _(tile):
                first = rows_at(tile, part)
                second = rows_at(units // part + tile, part)
                values = buf[batch, pl.ds(place * 2, 2), :, :].reshape(pair, width)
                gate = dot_nn(values, w_ref[:, first])
                up = dot_nn(values, w_ref[:, second])
                d_hidden = dot_nt(d_buf[side], wd_ref[first, :])
                sigma = jax.nn.sigmoid(gate)
                swish = gate * sigma
                h_buf[:, first] = to_half(swish * up)
                slope = sigma * (1.0 + gate * (1.0 - sigma))
                d_ref[batch, there, first] = to_half(d_hidden * up * slope)
                d_ref[batch, there, second] = to_half(d_hidden * swish)

            for item in stored(batch, place):
                item.start()

        sides(far, act)

    def product(batch):
        def get(place, tile):
            return dot_nt(d_ref[batch, rows_at(place, pair), :], w_ref[rows_at(tile, TILE), :])

        return get

    reduces = [
        PairReduce(line, product(batch), totals.at[batch], acc, keep, *sums[6 * batch : 6 * batch + 6])
        for batch in range(batches)
    ]

    def grad_stored(tile):
        slot = lax.rem(tile, 2)
        return pltpu.make_async_copy(
            tiles.at[slot], grad_hbm.at[rows_at(tile, block)], tile_sem.at[slot]
        )

    count = width // block

    def weight_grad(tile):
        pl.when(tile >= 2)(lambda: grad_stored(tile - 2).wait())
        slot = lax.rem(tile, 2)
        size = min(TILE, 2 * units)

        @pl.loop(0, 2 * units // size)
        def _(column):
            here = rows_at(column, size)
            got = 0.0
            for batch in range(batches):
                left = buf[batch, :, :, rows_at(tile, block)].reshape(2 * chips * piece, block)
                got = got + contract_rows(left, d_ref[batch, :, here])
            tiles[slot, :, here] = to_half(got)

        grad_stored(tile).start()

    def norm_batch(batch):
        own = pl.ds(batch * piece, piece)

        def put(here, d_values):
            there = pl.ds(pl.multiple_of(here.start + batch * piece, here.size), here.size)
            d_middle = cot_ref[there, :].astype(jnp.float32) + d_values
            dm_ref[there, :] = d_middle
            db_ref[there, :] = to_half(d_middle)

        norm_back(piece, v_ref.at[own], totals.at[batch], gain_ref, gain_grad_ref, put)

    gain_grad_ref[...] = jnp.zeros_like(gain_grad_ref)
    for item in loads:
        item.wait()
    last = 2 * chips - 2

    @pl.loop(0, chips)
    def _(far):
        take(0, far)
        pl.when(far == chips - 2)(spreads[1].begin)
        compute(0, far)

    @pl.loop(0, chips - 1)
    def _(far):
        take(1, far)
        reduces[0].step(2 * far)
        reduces[0].step(2 * far + 1)
        compute(1, far)

    take(1, chips - 1)
    compute(1, chips - 1)

    @pl.loop(0, 2)
    def _(step):
        reduces[1].step(step)
        weight_grad(step)

    reduces[0].step(last)
    norm_batch(0)

    @pl.loop(2, last)
    def _(step):
        reduces[1].step(step)
        pl.when(step < count)(lambda: weight_grad(step))

    @pl.loop(last, max(count, last))
    def _(tile):
        weight_grad(tile)

    reduces[1].step(last)
    norm_batch(1)
    for batch in range(batches):
        spreads[batch].sent()
        reduces[batch].sent()
    for item in stored(1, 0):
        item.wait()
    grad_stored(count - 2).wait()
    grad_stored(count - 1).wait()


def feed_forward(chips, batches, x, w, wd, group_d, middle, cot, gain, collective):
    rows, width = x.shape
    group = 2 * chips
    units = wd.shape[0]
    piece = rows // batches
    half = jnp.bfloat16
    return pl.pallas_call(
        functools.partial(feed_kernel, chips, batches),
        out_shape=[
            jax.ShapeDtypeStruct((rows, width), jnp.float32),
            jax.ShapeDtypeStruct((rows, width), half),
            jax.ShapeDtypeStruct((8, width), jnp.float32),
            jax.ShapeDtypeStruct((group * rows, units), half),
            jax.ShapeDtypeStruct((width, 2 * units), half),
        ],
        in_specs=[VMEM_SPEC] + [ANY_SPEC] * 3 + [VMEM_SPEC] * 3,
        out_specs=[VMEM_SPEC] * 3 + [ANY_SPEC] * 2,
        scratch_shapes=[
            pltpu.VMEM((batches, group, piece, width), half),
            pltpu.VMEM((2, 2 * piece, width), half),
            pltpu.VMEM((2 * piece, units), half),
            pltpu.VMEM(w.shape, half),
            pltpu.VMEM(wd.shape, half),
            pltpu.VMEM((batches, group * piece, 2 * units), half),
            pltpu.VMEM((2, 256, 2 * units), half),
            pltpu.VMEM((batches, piece, width), jnp.float32),
            pltpu.VMEM((2 * piece, TILE), jnp.float32),
            pltpu.VMEM((piece, width), jnp.float32),
            sems(2),
            sems(2, 2),
            sems(2),
            sems(2),
            sems(batches, 3, group),
            sems(batches, group),
        ]
        + PairReduce.scratch(chips, piece, width) * batches,
        compiler_params=comm_params(collective, 63),
        cost_estimate=cost(
            14 * group * rows * width * units, 400 * MIB, 2 * group * rows * width * 2
        ),
        name="feed_forward",
    )(x, w, wd, group_d, middle, cot, gain)


def branch_back_kernel(
    seqs, chips, batches, x_ref, w_ref, att_ref, middle_ref, hidden_hbm, wd_hbm, units_hbm, gd_hbm,
    d_ref, layer_ref, out_grad_ref, units_in, down_hbm,
    out_ref, buf, hidden_ref, wd_ref, grad_acc, rights, tiles, send, recv, load, right_sem, tile_sem,
    part_send, part_recv, acc, cross_out, line_out, cross_in, line_in, sum_send, sum_recv,
):
    line = Line(chips)
    rows = x_ref.shape[0]
    piece = rows // batches
    width = x_ref.shape[1]
    loads = [
        pltpu.make_async_copy(hidden_hbm, hidden_ref, load.at[0]),
        pltpu.make_async_copy(wd_hbm, wd_ref, load.at[1]),
    ]
    for item in loads:
        item.start()

    def product(slot, tile):
        return dot_nn(left_rows(hidden_ref, slot, rows), wd_ref[:, rows_at(tile, TILE)])

    part = rights.shape[2]
    count = width // part

    def right(tile):
        slot = lax.rem(tile, 2)
        return pltpu.make_async_copy(
            gd_hbm.at[:, rows_at(tile, part)], rights.at[slot], right_sem.at[slot]
        )

    def stored(tile):
        slot = lax.rem(tile, 2)
        return pltpu.make_async_copy(
            tiles.at[slot], down_hbm.at[:, rows_at(tile, part)], tile_sem.at[slot]
        )

    def weight_grad(tile):
        right(tile).wait()
        pl.when(tile + 1 < count)(lambda: right(tile + 1).start())
        pl.when(tile >= 2)(lambda: stored(tile - 2).wait())
        slot = lax.rem(tile, 2)
        size = min(TILE, hidden_ref.shape[1])

        @pl.loop(0, hidden_ref.shape[1] // size)
        def _(row):
            here = rows_at(row, size)
            tiles[slot, here, :] = to_half(contract_rows(hidden_ref[:, here], rights[slot]))

        stored(tile).start()

    right(0).start()
    meet(line.greet() + greet_seq(seqs))
    sums = ToSeq(seqs, units_hbm, units_in, part_send, part_recv)
    spread = Spread(line, x_ref, buf, send, recv)
    reduce = Reduce(
        line, product, out_ref, acc, cross_out, line_out, cross_in, line_in, sum_send, sum_recv
    )
    spread.begin()
    sums.begin()
    buf[line.own] = x_ref[...]
    grad_acc[...] = jnp.zeros_like(grad_acc)

    def use(slot):
        got = to_half(dot_nt(buf[slot], w_ref[...]))
        for batch in range(batches):
            d_ref[batch, rows_at(slot, piece), :] = got[batch * piece : (batch + 1) * piece]
        mixed = left_rows(att_ref, slot, rows)

        @pl.loop(0, width // TILE)
        def _(tile):
            here = rows_at(tile, TILE)
            grad_acc[:, here] += contract_rows(mixed, buf[slot, :, here])

    for item in loads:
        item.wait()

    per = -(-count // reduce.steps())

    @pl.loop(0, reduce.steps())
    def _(step):
        reduce.step(step)

        @pl.when(lax.rem(step, 2) == 1)
        def _():
            far = (step + 1) // 2
            spread.relay(far)
            spread.each(far - 1, use)

        @pl.loop(0, per)
        def _(turn):
            tile = step * per + turn
            pl.when(tile < count)(lambda: weight_grad(tile))

    spread.each(chips - 1, use)
    spread.each(chips, use)

    @pl.loop(0, rows // 32)
    def _(chunk):
        here = rows_at(chunk, 32)
        layer_ref[here, :] = to_half(middle_ref[here, :] + out_ref[here, :])

    out_grad_ref[...] = to_half(grad_acc[...])
    spread.sent()
    reduce.sent()
    sums.end()
    stored(count - 2).wait()
    stored(count - 1).wait()


def branch_back(seqs, chips, batches, x, w, attended, middle, hidden, wd, unit_part, group_d, collective):
    rows, width = x.shape
    group = 2 * chips
    length = group * rows // batches
    span = w.shape[0]
    half = jnp.bfloat16
    part = 256 if group * rows <= 2048 else 128
    return pl.pallas_call(
        functools.partial(branch_back_kernel, seqs, chips, batches),
        out_shape=[
            jax.ShapeDtypeStruct((batches, length, span), half),
            jax.ShapeDtypeStruct((rows, width), half),
            jax.ShapeDtypeStruct((span, width), half),
            jax.ShapeDtypeStruct((seqs, width // seqs, unit_part.shape[1]), half),
            jax.ShapeDtypeStruct((wd.shape[0], width), half),
        ],
        in_specs=[VMEM_SPEC] * 4 + [ANY_SPEC] * 4,
        out_specs=[VMEM_SPEC, VMEM_SPEC, VMEM_SPEC, ANY_SPEC, ANY_SPEC],
        scratch_shapes=[
            pltpu.VMEM((rows, width), jnp.float32),
            pltpu.VMEM((group, rows, width), half),
            pltpu.VMEM(hidden.shape, half),
            pltpu.VMEM(wd.shape, half),
            pltpu.VMEM((span, width), jnp.float32),
            pltpu.VMEM((2, group * rows, part), half),
            pltpu.VMEM((2, wd.shape[0], part), half),
            sems(3, group),
            sems(group),
            sems(2),
            sems(2),
            sems(2),
            sems(seqs),
            sems(seqs),
        ]
        + Reduce.scratch(chips, rows, width),
        compiler_params=comm_params(collective, 62),
        cost_estimate=cost(
            2 * group * rows * width * (2 * span + 2 * wd.shape[0]),
            250 * MIB,
            2 * group * rows * width * 2,
        ),
        name="branch_back",
    )(x, w, attended, middle, hidden, wd, unit_part, group_d.reshape(group * rows, width))


def attention_back_kernel(
    seqs, chips, block, q_ref, pad_ref, low_ref, lse_ref, d_ref, part_hbm, in_hbm,
    w_ref, g_hbm, v_ref, dm_hbm, gain_ref, mlp_gain_ref, out_ref, down_hbm,
    grad_ref, wq_ref, wk_ref, wv_ref, wo_ref, tile_ref, gate_ref, up_ref, down_in,
    dk, dv, kt, heads, back_out, back_in, unit_parts, unit_sums, units, lefts, parts, sums, cols, out_in,
    totals, gain_acc, gain_out, gain_in, gain_sum, gain_back, acc, keep,
    halo_send, halo_recv, unit_load, unit_send, unit_recv, unit_keep, dm_load, left_sem,
    part_send, part_recv, cols_send, cols_recv, out_send, out_recv, down_send, down_recv,
    gain_send, gain_recv, back_send, back_recv, *line_sums,
):
    line = Line(chips)
    group = 2 * chips
    seq = lax.axis_index("seq")
    own = line.own
    batches, length, span = q_ref.shape
    rows, width = v_ref.shape
    piece = rows // batches
    pair_rows = 2 * piece
    depth = 3 * span
    run = width // seqs
    share = run // group
    part = lefts.shape[3]
    steps, need = length // block, WINDOW // block
    first = length - WINDOW
    has_left, has_right = seq > 0, seq < seqs - 1
    scale = jnp.asarray(HEAD**-0.5, jnp.bfloat16)

    def others(count, me, act):
        pl.loop(1, count)(lambda ahead: act(lax.rem(me + ahead, count)))

    def unit_loaded(turn, place, mine):
        member = lax.rem(own + turn, group)
        slot = lax.rem(turn, 2)
        if mine:
            source = part_hbm.at[rows_at(seq * group + member, share)]
        else:
            source = in_hbm.at[place, rows_at(member, share)]
        return pltpu.make_async_copy(source, unit_parts.at[slot, place], unit_load.at[slot, place])

    def load_units(turn):
        for place in range(seqs):
            pl.when(place == seq)(lambda place=place: unit_loaded(turn, place, True).start())
            pl.when(place != seq)(lambda place=place: unit_loaded(turn, place, False).start())

    load_units(1)
    dm_loaded = pltpu.make_async_copy(dm_hbm, grad_ref, dm_load)
    dm_loaded.start()
    meet(greet_group(group) + greet_seq(seqs))
    size = down_in.shape[1]
    cut = size // 16 * 3 // 8 * 16
    downs = [
        ToSeq(seqs, down_hbm, down_in, down_send.at[0], down_recv.at[0], 0, cut),
        ToSeq(seqs, down_hbm, down_in, down_send.at[1], down_recv.at[1], cut, size - cut),
    ]
    downs[0].begin()
    swap = Swap(group, unit_sums, units, unit_send, unit_recv, unit_keep)

    @pl.loop(1, group + 1)
    def _(turn):
        member = lax.rem(own + turn, group)
        slot = lax.rem(turn, 2)
        pl.when(turn < group)(lambda: load_units(turn + 1))
        for place in range(seqs):
            unit_loaded(turn, place, False).wait()

        @pl.loop(0, share // 16)
        def _(chunk):
            here = rows_at(chunk, 16)
            added = unit_parts[slot, 0, here, :].astype(jnp.float32)
            for place in range(1, seqs):
                added = added + unit_parts[slot, place, here, :].astype(jnp.float32)
            unit_sums[member, here, :] = to_half(added)

        pl.when(turn < group)(lambda: swap.move(member, own).start())
        pl.when(turn == group)(lambda: swap.kept().start())

    def halo(batch, step, peer):
        here = rows_at(step, block)
        return pltpu.make_async_remote_copy(
            src_ref=back_out.at[batch, here],
            dst_ref=back_in.at[batch, here],
            send_sem=halo_send.at[batch, step],
            recv_sem=halo_recv.at[batch, step],
            device_id={"seq": peer},
            device_id_type=MESH,
        )

    def attend_block(batch, step):
        begin = pl.multiple_of(step * block, block)
        keys = pl.ds(begin, block + WINDOW)
        rows = pl.ds(begin, block)
        low = low_ref[batch, :, rows]
        for pair in range(span // PAIR):
            lanes = slice(pair * PAIR, (pair + 1) * PAIR)
            q_pair = q_ref[batch, rows, lanes] * scale
            d_pair = d_ref[batch, rows, lanes]
            k_rows = pad_ref[batch, keys, lanes]
            v_rows = pad_ref[batch, keys, span + pair * PAIR : span + (pair + 1) * PAIR]
            k_cols = kt[lanes, keys]
            back = []
            for half in range(2):
                row = pair * 2 + half
                q_head = head_lanes(q_pair, half)
                d_head = head_lanes(d_pair, half)
                scores = masked_scores(k_rows, q_head, low)
                probs = jnp.exp(scores - lse_ref[batch, row : row + 1, rows])
                d_probs = dot_nt(v_rows, d_head)
                along = jnp.sum(probs * d_probs, axis=0, keepdims=True)
                d_scores = to_half(probs * (d_probs - along))
                dv[keys, lanes] += dot_nn(to_half(probs), d_head)
                dk[keys, lanes] += dot_nn(d_scores, q_head)
                back.append(dot_nn(k_cols, d_scores))
            at = lax.broadcasted_iota(jnp.int32, back[0].shape, 0)
            heads[batch, rows, lanes] = to_half(
                jnp.where(at < HEAD, back[0], back[1]).T
            )


        @pl.when(has_left & (step < need))
        def _():
            back_out[batch, rows, :span] = to_half(dk[rows, :])
            back_out[batch, rows, span:] = to_half(dv[rows, :])
            halo(batch, step, seq - 1).start()

        @pl.when(step == steps - 1)
        def _():
            heads[batch, :, span : 2 * span] = to_half(dk[WINDOW:, :])
            heads[batch, :, 2 * span :] = to_half(dv[WINDOW:, :])

    def add_halo(batch):
        @pl.when(has_right)
        def _():
            @pl.loop(0, need)
            def _(step):
                there = pl.ds(pl.multiple_of(step * block + first, block), block)
                halo(batch, step, seq).wait_recv()
                got = back_in[batch, rows_at(step, block), :].astype(jnp.float32)
                mine = heads[batch, there, span:].astype(jnp.float32)
                heads[batch, there, span:] = to_half(mine + got)

    def product(batch):
        def get(place, tile):
            return dot_nt(heads[batch, rows_at(place, pair_rows), :], w_ref[rows_at(tile, TILE), :])

        return get

    reduces = [
        PairReduce(
            line, product(batch), totals.at[batch], acc, keep, *line_sums[6 * batch : 6 * batch + 6]
        )
        for batch in range(batches)
    ]
    last = 2 * chips - 2

    @pl.loop(0, 2 * steps)
    def _(turn):
        batch, step = turn // steps, lax.rem(turn, steps)

        @pl.when(step == 0)
        def _():
            kt[...] = pad_ref[batch, :, :span].T * scale
            dk[...] = jnp.zeros_like(dk)
            dv[...] = jnp.zeros_like(dv)

        attend_block(batch, step)
        after = turn - steps - 1
        pl.when(after == 0)(lambda: add_halo(0))

        @pl.when((after >= 0) & (2 * after < last))
        def _():
            reduces[0].step(2 * after)
            reduces[0].step(2 * after + 1)

    for after in range(steps - 1, chips - 1):
        reduces[0].step(2 * after)
        reduces[0].step(2 * after + 1)

    def left(tile):
        slot = lax.rem(tile, 2)
        return pltpu.make_async_copy(
            g_hbm.at[:, :, rows_at(tile, part)], lefts.at[slot], left_sem.at[slot]
        )

    def to_seq(peer, place):
        return pltpu.make_async_remote_copy(
            src_ref=parts.at[rows_at(peer, run)],
            dst_ref=sums.at[place],
            send_sem=part_send.at[peer],
            recv_sem=part_recv.at[place],
            device_id={"seq": peer},
            device_id_type=MESH,
        )

    left(0).start()
    add_halo(1)

    @pl.loop(0, width // part)
    def _(tile):
        left(tile).wait()
        pl.when(tile + 1 < width // part)(lambda: left(tile + 1).start())
        slot = lax.rem(tile, 2)
        got = contract_rows(lefts[slot, 0], heads[0])
        for batch in range(1, batches):
            got = got + contract_rows(lefts[slot, batch], heads[batch])
        parts[rows_at(tile, part), :] = to_half(got)

    others(seqs, seq, lambda peer: to_seq(peer, seq).start())
    from_seq = ToSeq(seqs, out_ref, out_in, out_send, out_recv)
    from_seq.begin()
    gain_acc[...] = jnp.zeros_like(gain_acc)
    dm_loaded.wait()

    def norm_batch(batch):
        mine = pl.ds(batch * piece, piece)

        def put(here, d_values):
            there = pl.ds(pl.multiple_of(here.start + batch * piece, here.size), here.size)
            grad_ref[there, :] += d_values

        norm_back(piece, v_ref.at[mine], totals.at[batch], gain_ref, gain_acc, put)

    pl.loop(0, 2)(reduces[1].step)
    reduces[0].step(last)
    norm_batch(0)
    pl.loop(2, last)(reduces[1].step)
    swap.end()
    cell = units.shape[2] // 2 // seqs
    for member in range(group):
        for place in range(seqs):
            column = (place * group + member) * cell
            for target, begin in ((gate_ref, 0), (up_ref, seqs * cell)):
                here = slice(begin + place * cell, begin + (place + 1) * cell)
                target[:, column : column + cell] = units[member, :, here]

    def block_swap(peer, member):
        return pltpu.make_async_remote_copy(
            src_ref=parts.at[rows_at(seq * group + peer, share)],
            dst_ref=cols.at[member],
            send_sem=cols_send.at[peer],
            recv_sem=cols_recv.at[member],
            device_id={"fsdp": peer},
            device_id_type=MESH,
        )

    others(seqs, seq, lambda peer: to_seq(peer, peer).wait_recv())
    downs[1].begin()

    @pl.loop(0, run // 64)
    def _(chunk):
        here = rows_at(chunk, 64)
        there = pl.ds(pl.multiple_of(seq * run + chunk * 64, 64), 64)
        parts[there, :] = to_half(add_from_seq(seqs, parts[there, :], sums, here))

    others(group, own, lambda peer: block_swap(peer, own).start())
    cols[own] = parts[rows_at(seq * group + own, share), :]
    from_seq.arrived()
    out_rows = out_in.shape[1]
    wo_ref[...] = add_from_seq(seqs, out_ref[rows_at(seq, out_rows), :], out_in, slice(None))
    reduces[1].step(last)
    norm_batch(1)
    fold = 128 // share
    near = group // fold
    attn_row = jnp.sum(gain_acc[...], axis=0, keepdims=True)
    mlp_row = jnp.sum(mlp_gain_ref[...], axis=0, keepdims=True)
    gain_out[...] = jnp.zeros_like(gain_out)
    for place in range(width // 128):
        lanes = slice(place * 128, (place + 1) * 128)
        gain_out[place % near, place // near, 0:1, :] = attn_row[:, lanes]
        gain_out[place % near, place // near, 1:2, :] = mlp_row[:, lanes]

    def gain_group(peer, member):
        return pltpu.make_async_remote_copy(
            src_ref=gain_out.at[peer // fold],
            dst_ref=gain_in.at[member],
            send_sem=gain_send.at[peer],
            recv_sem=gain_recv.at[member],
            device_id={"fsdp": peer},
            device_id_type=MESH,
        )

    def gain_seq(peer, place):
        return pltpu.make_async_remote_copy(
            src_ref=gain_sum.at[peer],
            dst_ref=gain_back.at[place],
            send_sem=back_send.at[peer],
            recv_sem=back_recv.at[place],
            device_id={"seq": peer},
            device_id_type=MESH,
        )

    others(group, own, lambda peer: gain_group(peer, own).start())
    gain_in[own] = gain_out[own // fold]
    others(group, own, lambda peer: gain_group(peer, peer).wait_recv())
    gain_sum[...] = jnp.sum(gain_in[...], axis=0)
    others(seqs, seq, lambda peer: gain_seq(peer, seq).start())
    gain_back[seq] = gain_sum[seq]
    others(seqs, seq, lambda peer: gain_seq(peer, peer).wait_recv())
    tile_ref[...] = jnp.sum(gain_back[...], axis=0)
    others(group, own, lambda peer: block_swap(peer, peer).wait_recv())
    for index, target in enumerate((wq_ref, wk_ref, wv_ref)):
        for member, first, home, size in column_parts(seqs, group, share, span):
            first = first + index * span
            target[:, home : home + size] = cols[member, :, first : first + size]
    from_seq.sent()
    for item in downs:
        item.end()
    for batch in range(batches):
        reduces[batch].sent()

        @pl.when(has_left)
        def _(batch=batch):
            pl.loop(0, need)(lambda step: halo(batch, step, seq).wait_send())

    others(seqs, seq, lambda peer: to_seq(peer, seq).wait_send())
    others(group, own, lambda peer: gain_group(peer, own).wait_send())
    others(group, own, lambda peer: block_swap(peer, own).wait_send())
    others(seqs, seq, lambda peer: gain_seq(peer, seq).wait_send())


def attention_back(
    seqs, chips, block, query, kv_pad, low, lse, d_att, part_own, parts_in, w, group_a, x, d_middle,
    gain, mlp_gain, out_part, down, collective,
):
    batches, length, span = query.shape
    padded = kv_pad.shape[1]
    rows, width = x.shape
    piece = rows // batches
    group = 2 * chips
    depth = w.shape[1]
    run = width // seqs
    share = run // group
    near = group // (128 // share)
    cells = part_own.shape[1]
    out_rows = out_part.shape[0] // seqs
    half, wide = jnp.bfloat16, jnp.float32
    part = 256 if batches * length <= 2048 else 128
    return pl.pallas_call(
        functools.partial(attention_back_kernel, seqs, chips, block),
        out_shape=[
            jax.ShapeDtypeStruct((rows, width), wide),
            jax.ShapeDtypeStruct((share, width), half),
            jax.ShapeDtypeStruct((share, width), half),
            jax.ShapeDtypeStruct((share, width), half),
            jax.ShapeDtypeStruct((out_rows, width), wide),
            jax.ShapeDtypeStruct((8, 128), wide),
            jax.ShapeDtypeStruct((share, cells // 2 * group), half),
            jax.ShapeDtypeStruct((share, cells // 2 * group), half),
            jax.ShapeDtypeStruct((seqs, down.shape[0] // seqs, width), half),
        ],
        in_specs=[VMEM_SPEC] * 5
        + [ANY_SPEC] * 2
        + [VMEM_SPEC, ANY_SPEC, VMEM_SPEC, ANY_SPEC]
        + [VMEM_SPEC] * 3
        + [ANY_SPEC],
        out_specs=[VMEM_SPEC] * 8 + [ANY_SPEC],
        scratch_shapes=[
            pltpu.VMEM((padded, span), wide),
            pltpu.VMEM((padded, span), wide),
            pltpu.VMEM((span, padded), half),
            pltpu.VMEM((batches, length, depth), half),
            pltpu.VMEM((batches, WINDOW, 2 * span), half),
            pltpu.VMEM((batches, WINDOW, 2 * span), half),
            pltpu.VMEM((2, seqs, share, cells), half),
            pltpu.VMEM((group, share, cells), half),
            pltpu.VMEM((group, share, cells), half),
            pltpu.VMEM((2, batches, length, part), half),
            pltpu.VMEM((width, depth), half),
            pltpu.VMEM((seqs, run, depth), half),
            pltpu.VMEM((group, share, depth), half),
            pltpu.VMEM((seqs, out_rows, width), half),
            pltpu.VMEM((batches, piece, width), wide),
            pltpu.VMEM((8, width), wide),
            pltpu.VMEM((near, seqs, 8, 128), wide),
            pltpu.VMEM((group, seqs, 8, 128), wide),
            pltpu.VMEM((seqs, 8, 128), wide),
            pltpu.VMEM((seqs, 8, 128), wide),
            pltpu.VMEM((2 * piece, TILE), wide),
            pltpu.VMEM((piece, width), wide),
            sems(batches, WINDOW // block),
            sems(batches, WINDOW // block),
            sems(2, seqs),
            sems(group),
            sems(group),
            pltpu.SemaphoreType.DMA,
            pltpu.SemaphoreType.DMA,
            sems(2),
            sems(seqs),
            sems(seqs),
            sems(group),
            sems(group),
            sems(seqs),
            sems(seqs),
            sems(2, seqs),
            sems(2, seqs),
            sems(group),
            sems(group),
            sems(seqs),
            sems(seqs),
        ]
        + PairReduce.scratch(chips, piece, width) * batches,
        compiler_params=comm_params(collective, 63),
        cost_estimate=cost(
            20 * batches * length * span * (WINDOW + block) + 4 * group * rows * width * depth,
            400 * MIB,
            3 * group * rows * width * 2,
        ),
        name="attention_back",
    )(
        query, kv_pad, low, lse, d_att, part_own, parts_in, w, group_a, x, d_middle, gain, mlp_gain,
        out_part, down,
    )


def doc_starts(lengths, positions, batches, seq_len):
    table = lengths.reshape(batches, -1, lengths.shape[1])
    starts = jnp.cumsum(table, axis=2) - table
    per_batch = seq_len // table.shape[1]
    begins = (starts + (jnp.arange(table.shape[1], dtype=jnp.int32) * per_batch)[None, :, None]).reshape(
        batches, -1
    )
    before = begins[:, None, :] <= positions[None, :, None]
    return jnp.max(jnp.where(before, begins[:, None, :], 0), axis=2)


def body(
    tokens,
    cotangent,
    lengths,
    gain_attn,
    w_query,
    w_key,
    w_value,
    w_out,
    gain_mlp,
    w_gate,
    w_up,
    w_down,
):
    batches, piece, width = tokens.shape
    seqs = lax.axis_size("seq")
    group = lax.axis_size("fsdp")
    chips = group // 2
    devices = seqs * group
    seq_len = piece * devices
    rows = batches * piece
    share = w_query.shape[0]
    span = width // group
    length = group * piece
    aligned = share == HEAD
    member = lax.axis_index("fsdp")

    def blocks(weight):
        part = weight.shape[1] // devices
        return weight.reshape(share, seqs, group, part).transpose(2, 0, 1, 3).reshape(group, share, -1)

    x_rows = tokens.reshape(rows, width)
    cot_rows = cotangent.reshape(rows, width)
    wd_part = lax.all_gather(w_down, "seq", axis=0, tiled=True)
    if aligned:
        wo_part = lax.all_gather(w_out, "seq", axis=0, tiled=True)
    else:
        wo_all = lax.all_gather(w_out, ("seq", "fsdp"), axis=0, tiled=True)
        wo_part = lax.dynamic_slice_in_dim(wo_all, member * span, span, 0)

    unit_blocks = jnp.concatenate([blocks(w_gate), blocks(w_up)], axis=2)
    lane = jnp.arange(128, dtype=jnp.int32)
    device = lax.axis_index("seq") * group + member
    fold = 128 // share
    here = lane // share == lax.rem(device, fold)
    both = jnp.stack([gain_attn, gain_mlp]).astype(jnp.float32)
    tile = jnp.where(here[None], jnp.tile(both, (1, fold)), 0.0)
    tile = jnp.pad(tile, ((0, 6), (0, 0)))[None]
    group_a, query, key_value, gains, w_heads = start(
        seqs, chips, batches, tile, x_rows, (w_query, w_key, w_value), 1
    )
    lengths, gains = lax.optimization_barrier((lengths, gains))
    group_start = lax.axis_index("seq") * length
    positions = group_start + jnp.arange(length, dtype=jnp.int32)
    begins = doc_starts(lengths, positions, batches, seq_len)
    at = jnp.arange(length, dtype=jnp.int32)
    block = min(256, length)
    low = jnp.maximum(begins - group_start + WINDOW, at[None, :] + 1) - (at // block * block)[None, :]
    low = low[:, None, :]

    gains = gains.transpose(1, 0, 2, 3).reshape(devices // fold, fold, 8, 128).sum(axis=1)
    gain_one = gains[:, 0].reshape(width)
    gain_two = gains[:, 1].reshape(width)
    attended, lse, kv_pad, unit_own = attend(
        seqs, group, query, key_value, low, block, unit_blocks, 2
    )
    middle, normed_b, group_d, w_units = branch_sum(
        seqs, chips, attended, wo_part, cot_rows, unit_own.reshape(group * share, -1),
        x_rows, gain_two[None], 3,
    )
    w_units = w_units.reshape(width, -1)
    d_middle, d_branch, mlp_gain_part, hidden, unit_part = feed_forward(
        chips, batches, normed_b, w_units, wd_part, group_d, middle, cot_rows, gain_two[None], 4
    )
    d_attended, layer_out, out_part, unit_in, down_part = branch_back(
        seqs, chips, batches, d_branch, wo_part, attended, middle, hidden, wd_part, unit_part,
        group_d, 5,
    )
    if not aligned:
        whole = lax.dynamic_update_slice_in_dim(
            jnp.zeros((width, width), jnp.bfloat16), out_part, member * span, 0
        )
        out_part = lax.psum(whole, "fsdp").reshape(seqs, group, share, width)
        out_part = lax.dynamic_slice_in_dim(out_part, member, 1, 1).reshape(seqs * share, width)
    input_grad, wq_grad, wk_grad, wv_grad, wo_grad, gain_tile, gate_grad, up_grad, down_in = (
        attention_back(
            seqs, chips, block, query, kv_pad, low, lse, d_attended, unit_part, unit_in, w_heads,
            group_a, x_rows, d_middle, gain_one[None], mlp_gain_part, out_part, down_part, 6,
        )
    )
    run = lax.axis_index("seq")
    down_own = lax.dynamic_slice_in_dim(down_part, run * w_down.shape[0], w_down.shape[0], 0)
    others = jnp.arange(seqs)[:, None, None] != run
    down_sum = jnp.sum(jnp.where(others, down_in.astype(jnp.float32), 0.0), axis=0)
    gain_grads = lax.dynamic_slice_in_dim(gain_tile[:2], lax.rem(device, fold) * share, share, 1)
    wide = jnp.float32
    return (
        layer_out.reshape(batches, piece, width),
        input_grad.reshape(batches, piece, width),
        gain_grads[0],
        wq_grad.astype(wide),
        wk_grad.astype(wide),
        wv_grad.astype(wide),
        wo_grad,
        gain_grads[1],
        gate_grad.astype(wide),
        up_grad.astype(wide),
        down_sum + down_own.astype(wide),
    )


def solution(mesh):
    spread = ("seq", "fsdp")
    tokens, rows, gains = P(None, spread, None), P(spread, None), P(spread)
    in_specs = (tokens, tokens, P(), gains, rows, rows, rows, rows, gains, rows, rows, rows)
    out_specs = (tokens, tokens, gains, rows, rows, rows, rows, gains, rows, rows, rows)
    return jax.shard_map(body, mesh=mesh, in_specs=in_specs, out_specs=out_specs, check_vma=False)
```

```python
import functools

import jax
import jax.numpy as jnp
from jax import lax
from jax.experimental import pallas as pl
from jax.experimental.pallas import tpu as pltpu
from jax.sharding import PartitionSpec as P

HEAD = 64
FF = 8192
WINDOW = 1024
PAIR = 128
TILE = 512
PARTS = 4
LOW = -1e30
EPS = 1e-05
MESH = pl.DeviceIdType.MESH
MIB = 2**20


def to_half(values):
    return values.astype(jnp.bfloat16)


def normalize(values, gain):
    return values * lax.rsqrt(jnp.mean(values * values, axis=-1, keepdims=True) + EPS) * gain


def contract_rows(left, right):
    return lax.dot_general(
        left, right, (((0,), (0,)), ((), ())), preferred_element_type=jnp.float32
    )


def dot_nt(left, right):
    return lax.dot_general(
        left, right, (((1,), (1,)), ((), ())), preferred_element_type=jnp.float32
    )


def dot_nn(left, right):
    return jnp.dot(left, right, preferred_element_type=jnp.float32)


def head_lanes(values, half):
    lane = lax.broadcasted_iota(jnp.int32, values.shape, 1)
    return jnp.where((lane >= HEAD) == (half == 1), values, jnp.zeros_like(values))


def masked_scores(k_rows, q_head, low):
    keys, block = k_rows.shape[0], q_head.shape[0]
    scores = dot_nt(k_rows, q_head)
    at = lax.broadcasted_iota(jnp.int32, (keys, block), 0)
    query = lax.broadcasted_iota(jnp.int32, (keys, block), 1)
    seen = (at >= low) & (at <= query + WINDOW)
    return jnp.where(seen, scores, LOW)


class Line:
    def __init__(self, chips):
        self.chips = chips
        self.own = lax.axis_index("fsdp")
        self.chip = self.own // 2
        self.core = lax.rem(self.own, 2)
        self.other = self.own + 1 - 2 * self.core
        self.has_left = self.chip > 0
        self.has_right = self.chip < chips - 1

    def greet(self):
        signal_group(self.other)
        pl.when(self.has_left)(lambda: signal_group(self.own - 2))
        pl.when(self.has_right)(lambda: signal_group(self.own + 2))
        return 1 + self.has_left.astype(jnp.int32) + self.has_right.astype(jnp.int32)


def signal_group(peer):
    barrier = pltpu.get_barrier_semaphore()
    pl.semaphore_signal(barrier, inc=1, device_id={"fsdp": peer}, device_id_type=MESH)


def signal_seq(peer):
    barrier = pltpu.get_barrier_semaphore()
    pl.semaphore_signal(barrier, inc=1, device_id={"seq": peer}, device_id_type=MESH)


def greet_group(group):
    own = lax.axis_index("fsdp")
    pl.loop(1, group)(lambda ahead: signal_group(lax.rem(own + ahead, group)))
    return group - 1


def greet_seq(seqs):
    own = lax.axis_index("seq")
    pl.loop(1, seqs)(lambda ahead: signal_seq(lax.rem(own + ahead, seqs)))
    return seqs - 1


def meet(count):
    pl.semaphore_wait(pltpu.get_barrier_semaphore(), count)


def rows_at(index, size):
    return pl.ds(pl.multiple_of(index * size, size), size)


class Spread:
    def __init__(self, line, first, buf, send, recv):
        self.line, self.first, self.buf, self.send, self.recv = line, first, buf, send, recv
        self.parts = recv.shape[1]
        self.size = first.shape[0] // self.parts

    def move(self, slot, part, way, peer, source=None):
        here = rows_at(part, self.size)
        return pltpu.make_async_remote_copy(
            src_ref=self.buf.at[slot, here] if source is None else source.at[here],
            dst_ref=self.buf.at[slot, here],
            send_sem=self.send.at[way, slot, part],
            recv_sem=self.recv.at[slot, part],
            device_id={"fsdp": peer},
            device_id_type=MESH,
        )

    def begin(self):
        line = self.line

        @pl.loop(0, self.parts)
        def _(part):
            pl.when(line.has_right)(
                lambda: self.move(line.own, part, 1, line.own + 2, self.first).start()
            )
            pl.when(line.has_left)(
                lambda: self.move(line.own, part, 0, line.own - 2, self.first).start()
            )
            self.move(line.own, part, 2, line.other, self.first).start()

    def relay_part(self, far, part):
        line = self.line

        @pl.when(line.chip - far >= 0)
        def _():
            slot = (line.chip - far) * 2 + line.core
            self.move(slot, part, 1, line.own).wait_recv()
            pl.when(line.has_right)(lambda: self.move(slot, part, 1, line.own + 2).start())
            self.move(slot, part, 2, line.other).start()

        @pl.when(line.chip + far < line.chips)
        def _():
            slot = (line.chip + far) * 2 + line.core
            self.move(slot, part, 0, line.own).wait_recv()
            pl.when(line.has_left)(lambda: self.move(slot, part, 0, line.own - 2).start())
            self.move(slot, part, 2, line.other).start()

    def relay(self, far):
        pl.loop(0, self.parts)(lambda part: self.relay_part(far, part))

    def across(self, slot):
        pl.loop(0, self.parts)(lambda part: self.move(slot, part, 2, self.line.own).wait_recv())

    def each(self, far, use):
        line = self.line

        @pl.loop(0, 4)
        def _(turn):
            side = lax.rem(turn, 2)
            over = turn // 2
            away = far - over
            source = line.chip + away * (2 * side - 1)
            valid = (away >= 0) & (away < line.chips) & (source >= 0) & (source < line.chips)
            valid = valid & ((side == 0) | (away > 0))

            @pl.when(valid)
            def _():
                slot = source * 2 + line.core + over * (1 - 2 * line.core)
                pl.when(over == 1)(lambda: self.across(slot))
                use(slot)

    def rest(self):
        pl.loop(0, self.line.chips)(lambda place: self.across(place * 2 + 1 - self.line.core))

    def sent(self):
        line = self.line

        @pl.loop(0, line.chips)
        def _(place):
            slot = place * 2 + line.core

            @pl.loop(0, self.parts)
            def _(part):
                self.move(slot, part, 2, line.other).wait_send()
                pl.when(line.has_right & (place <= line.chip))(
                    lambda: self.move(slot, part, 1, line.own + 2).wait_send()
                )
                pl.when(line.has_left & (place >= line.chip))(
                    lambda: self.move(slot, part, 0, line.own - 2).wait_send()
                )


class Reduce:
    def __init__(self, line, product, out, acc, cross_out, line_out, cross_in, line_in, send, recv):
        self.line, self.product, self.out, self.acc = line, product, out, acc
        self.cross_out, self.line_out, self.cross_in, self.line_in = cross_out, line_out, cross_in, line_in
        self.send, self.recv = send, recv
        self.tiles = line_out.shape[2] // TILE

    @staticmethod
    def scratch(chips, rows, width):
        part = pltpu.VMEM((chips, rows, width), jnp.bfloat16)
        return [
            pltpu.VMEM((rows, TILE), jnp.float32),
            pltpu.VMEM((2, rows, width), jnp.bfloat16),
            part,
            part,
            pltpu.VMEM((chips + 1, rows, width), jnp.bfloat16),
            pltpu.SemaphoreType.DMA((2, chips, width // TILE)),
            pltpu.SemaphoreType.DMA((2, chips + 1, width // TILE)),
        ]

    def cross(self, side, place, tile):
        here = rows_at(tile, TILE)
        return pltpu.make_async_remote_copy(
            src_ref=self.cross_out.at[side, :, here],
            dst_ref=self.cross_in.at[place, :, here],
            send_sem=self.send.at[0, place, tile],
            recv_sem=self.recv.at[0, place, tile],
            device_id={"fsdp": self.line.other},
            device_id_type=MESH,
        )

    def along(self, place, landing, tile, peer):
        here = rows_at(tile, TILE)
        return pltpu.make_async_remote_copy(
            src_ref=self.line_out.at[place, :, here],
            dst_ref=self.line_in.at[landing, :, here],
            send_sem=self.send.at[1, place, tile],
            recv_sem=self.recv.at[1, landing, tile],
            device_id={"fsdp": peer},
            device_id_type=MESH,
        )

    def where(self, away, side):
        line = self.line
        rightward = (line.chips - 1 - line.chip >= line.chip) == (side == 0)
        place = line.chip + jnp.where(rightward, away, -away)
        valid = (place >= 0) & (place < line.chips) & ((away > 0) | (side == 0))
        return valid, place, rightward

    def level(self, away, also):
        @pl.loop(0, 2)
        def _(side):
            valid, place, _ = self.where(away, side)

            @pl.when(valid)
            def _():
                @pl.loop(0, self.tiles)
                def _(tile):
                    got = self.product(place * 2 + 1 - self.line.core, tile)
                    self.cross_out[side, :, rows_at(tile, TILE)] = to_half(got)
                    self.cross(side, place, tile).start()

        @pl.loop(0, self.tiles)
        def _(tile):
            @pl.loop(0, 2)
            def _(side):
                valid, place, rightward = self.where(away, side)
                pl.when(valid)(lambda: self.close(away, side, place, rightward, tile))

            also(tile)

    def close(self, away, side, place, rightward, tile):
        line, acc = self.line, self.acc
        here = rows_at(tile, TILE)
        upstream = (rightward & line.has_left) | (jnp.logical_not(rightward) & line.has_right)
        acc[...] = self.product(place * 2 + line.core, tile)
        self.cross(side, place, tile).wait()
        acc[...] += self.cross_in[place, :, here].astype(jnp.float32)

        @pl.when(away > 0)
        def _():
            @pl.when(upstream)
            def _():
                self.along(place, place, tile, line.own).wait_recv()
                self.line_out[place, :, here] = to_half(
                    acc[...] + self.line_in[place, :, here].astype(jnp.float32)
                )

            @pl.when(jnp.logical_not(upstream))
            def _():
                self.line_out[place, :, here] = to_half(acc[...])

            @pl.when(rightward)
            def _():
                self.along(place, place, tile, line.own + 2).start()

            @pl.when(jnp.logical_not(rightward))
            def _():
                landing = jnp.where(away == 1, line.chips, place)
                self.along(place, landing, tile, line.own - 2).start()

        @pl.when(away == 0)
        def _():
            self.out[:, here] = acc[...]

            @pl.when(line.has_left)
            def _():
                self.along(place, place, tile, line.own).wait_recv()
                self.out[:, here] += self.line_in[place, :, here].astype(jnp.float32)

            @pl.when(line.has_right)
            def _():
                self.along(place, line.chips, tile, line.own).wait_recv()
                self.out[:, here] += self.line_in[line.chips, :, here].astype(jnp.float32)

    def sent(self):
        @pl.loop(0, self.line.chips)
        def _(place):
            @pl.when(place != self.line.chip)
            def _():
                pl.loop(0, self.tiles)(
                    lambda tile: self.along(place, place, tile, self.line.own).wait_send()
                )


class Swap:
    def __init__(self, group, source, target, send, recv, keep):
        self.group, self.source, self.target = group, source, target
        self.send, self.recv, self.keep = send, recv, keep
        self.own = lax.axis_index("fsdp")

    def move(self, peer, source):
        return pltpu.make_async_remote_copy(
            src_ref=self.source.at[peer],
            dst_ref=self.target.at[source],
            send_sem=self.send.at[peer],
            recv_sem=self.recv.at[source],
            device_id={"fsdp": peer},
            device_id_type=MESH,
        )

    def kept(self):
        return pltpu.make_async_copy(self.source.at[self.own], self.target.at[self.own], self.keep)

    def begin(self):
        self.kept().start()
        pl.loop(1, self.group)(
            lambda ahead: self.move(lax.rem(self.own + ahead, self.group), self.own).start()
        )

    def end(self):
        self.kept().wait()

        @pl.loop(1, self.group)
        def _(ahead):
            peer = lax.rem(self.own + ahead, self.group)
            self.move(peer, peer).wait_recv()
            self.move(peer, self.own).wait_send()


class Share:
    def __init__(self, seqs, source, target, send, recv, keep):
        self.seqs, self.source, self.target = seqs, source, target
        self.send, self.recv, self.keep = send, recv, keep
        self.own = lax.axis_index("seq")
        self.half = source.shape[0] // 2

    def move(self, peer, place):
        return pltpu.make_async_remote_copy(
            src_ref=self.source,
            dst_ref=self.target.at[place],
            send_sem=self.send.at[peer, 0],
            recv_sem=self.recv.at[place, 0],
            device_id={"seq": peer},
            device_id_type=MESH,
        )

    def relay(self, peer, place, part):
        here = pl.ds(part * self.half, self.half)
        return pltpu.make_async_remote_copy(
            src_ref=self.target.at[place, here],
            dst_ref=self.target.at[place, here],
            send_sem=self.send.at[peer, 1],
            recv_sem=self.recv.at[place, part],
            device_id={"seq": peer},
            device_id_type=MESH,
        )

    def near(self):
        one = self.own + 1 - 2 * lax.rem(self.own, 2)
        two = lax.rem(self.own + 2, 4)
        return one, two, lax.rem(one + 2, 4)

    def kept(self):
        return pltpu.make_async_copy(self.source, self.target.at[self.own], self.keep)

    def begin(self):
        self.kept().start()
        if self.seqs == 4:
            one, two, _ = self.near()
            self.move(one, self.own).start()
            self.move(two, self.own).start()
        else:
            pl.loop(1, self.seqs)(
                lambda ahead: self.move(lax.rem(self.own + ahead, self.seqs), self.own).start()
            )

    def pass_on(self):
        if self.seqs == 4:
            one, two, _ = self.near()
            self.move(one, one).wait_recv()
            self.relay(two, one, 0).start()
            self.move(two, two).wait_recv()
            self.relay(one, two, 1).start()

    def end(self):
        self.kept().wait()
        if self.seqs == 4:
            one, two, far = self.near()
            self.relay(two, far, 0).wait_recv()
            self.relay(one, far, 1).wait_recv()
            self.move(one, self.own).wait_send()
            self.move(two, self.own).wait_send()
            self.relay(two, one, 0).wait_send()
            self.relay(one, two, 1).wait_send()
        else:

            @pl.loop(1, self.seqs)
            def _(ahead):
                peer = lax.rem(self.own + ahead, self.seqs)
                self.move(peer, peer).wait_recv()
                self.move(peer, self.own).wait_send()


class ToSeq:
    def __init__(self, seqs, source, target, send, recv, first=0):
        self.seqs, self.source, self.target, self.send, self.recv = seqs, source, target, send, recv
        self.own = lax.axis_index("seq")
        self.first = first

    def move(self, peer, place):
        run = self.source.shape[0] // self.seqs
        begin = pl.multiple_of(peer * run + self.first, 16)
        return pltpu.make_async_remote_copy(
            src_ref=self.source.at[pl.ds(begin, self.target.shape[1])],
            dst_ref=self.target.at[place],
            send_sem=self.send.at[peer],
            recv_sem=self.recv.at[place],
            device_id={"seq": peer},
            device_id_type=MESH,
        )

    def begin(self):
        pl.loop(1, self.seqs)(
            lambda ahead: self.move(lax.rem(self.own + ahead, self.seqs), self.own).start()
        )

    def arrived(self):
        @pl.loop(1, self.seqs)
        def _(ahead):
            peer = lax.rem(self.own + ahead, self.seqs)
            self.move(peer, peer).wait_recv()

    def sent(self):
        @pl.loop(1, self.seqs)
        def _(ahead):
            peer = lax.rem(self.own + ahead, self.seqs)
            self.move(peer, self.own).wait_send()

    def end(self):
        self.arrived()
        self.sent()


VMEM_SPEC = pl.BlockSpec(memory_space=pltpu.VMEM)
ANY_SPEC = pl.BlockSpec(memory_space=pl.ANY)


def comm_params(collective, mib=58):
    return pltpu.CompilerParams(
        collective_id=collective, has_side_effects=True, vmem_limit_bytes=mib * MIB
    )


def cost(flops, local, remote):
    return pl.CostEstimate(
        flops=flops, bytes_accessed=local, transcendentals=0, remote_bytes_transferred=remote
    )


def sems(*shape):
    return pltpu.SemaphoreType.DMA(shape)


def left_rows(a_ref, slot, rows):
    if len(a_ref.shape) == 2:
        return a_ref[rows_at(slot, rows), :]
    piece = rows // a_ref.shape[0]
    return jnp.concatenate(
        [a_ref[batch, rows_at(slot, piece), :] for batch in range(a_ref.shape[0])], axis=0
    )


def norm_back(rows, v_ref, e_ref, gain_ref, gain_acc, put):
    @pl.loop(0, rows // 32)
    def _(chunk):
        here = rows_at(chunk, 32)
        values = v_ref[here, :].astype(jnp.float32)
        error = e_ref[here, :]
        rate = lax.rsqrt(jnp.mean(values * values, axis=-1, keepdims=True) + EPS)
        unit = values * rate
        product = error * unit
        gain = gain_ref[0:1, :]
        mean = jnp.mean(product * gain, axis=-1, keepdims=True)
        gain_acc[...] += (product[0:8] + product[8:16]) + (product[16:24] + product[24:32])
        put(here, rate * (gain * error - unit * mean))


def add_from_seq(seqs, own_rows, got, here):
    seq = lax.axis_index("seq")
    added = own_rows.astype(jnp.float32)
    for place in range(seqs):
        piece = got[place, here, :].astype(jnp.float32)
        added = added + jnp.where(place == seq, 0.0, piece)
    return added


def column_parts(seqs, group, share, span):
    size = HEAD if share == HEAD else span
    parts = []
    for member in range(group):
        for run in range(span // size):
            home = (run * group + member) * size
            parts.append((member, run * size, home, size))
    return parts


def start_kernel(
    seqs, chips, batches, tile_ref, x_ref, wq_ref, wk_ref, wv_ref, gate_hbm, up_hbm,
    g_ref, q_ref, kv_ref, gains_ref, w_out_ref, units_ref,
    gate, up, units, unit_sem,
    blocks_ref, buf, normed, gain, gains, w, send, recv, keep, swap_send, share_send, w_recv,
    tile_send, tile_across, tile_recv, tile_back, w_keep, gain_keep,
):
    line = Line(chips)
    group = 2 * chips
    seq = lax.axis_index("seq")
    own = line.own
    share = blocks_ref.shape[1]
    piece = x_ref.shape[0] // batches
    span = q_ref.shape[2]
    width = x_ref.shape[1]
    per = 128 * seqs * group // width
    unit_loads = [
        pltpu.make_async_copy(gate_hbm, gate, unit_sem.at[0]),
        pltpu.make_async_copy(up_hbm, up, unit_sem.at[1]),
    ]
    for item in unit_loads:
        item.start()
    for index, source in enumerate((wq_ref, wk_ref, wv_ref)):
        for member, first, home, size in column_parts(seqs, group, share, span):
            first = first + index * span
            blocks_ref[member, :, first : first + size] = source[:, home : home + size]
    meet(greet_group(group) + greet_seq(seqs))

    def block_at(run, member):
        return w.at[rows_at(run * group + member, share)]

    def block_swap(peer, member):
        return pltpu.make_async_remote_copy(
            src_ref=blocks_ref.at[peer],
            dst_ref=block_at(seq, member),
            send_sem=swap_send.at[peer],
            recv_sem=w_recv.at[seq, member],
            device_id={"fsdp": peer},
            device_id_type=MESH,
        )

    def block_share(run, member, peer):
        return pltpu.make_async_remote_copy(
            src_ref=block_at(run, member),
            dst_ref=block_at(run, member),
            send_sem=share_send.at[peer, member],
            recv_sem=w_recv.at[run, member],
            device_id={"seq": peer},
            device_id_type=MESH,
        )

    def tile_to_seq(peer, place):
        return pltpu.make_async_remote_copy(
            src_ref=tile_ref.at[0],
            dst_ref=gains.at[own, place],
            send_sem=tile_send.at[peer],
            recv_sem=tile_recv.at[place],
            device_id={"seq": peer},
            device_id_type=MESH,
        )

    def tiles_to_group(peer, member):
        return pltpu.make_async_remote_copy(
            src_ref=gains.at[member],
            dst_ref=gains.at[member],
            send_sem=tile_across.at[peer],
            recv_sem=tile_back.at[member],
            device_id={"fsdp": peer},
            device_id_type=MESH,
        )

    def others(count, me, act):
        pl.loop(1, count)(lambda ahead: act(lax.rem(me + ahead, count)))

    others(seqs, seq, lambda peer: tile_to_seq(peer, seq).start())
    others(group, own, lambda peer: block_swap(peer, own).start())
    spread = Spread(line, x_ref, buf, send, recv)
    spread.begin()
    gains[own, seq] = tile_ref[0]
    w[rows_at(seq * group + own, share), :] = blocks_ref[own]
    others(seqs, seq, lambda peer: block_share(seq, own, peer).start())
    buf[own] = x_ref[...]
    others(seqs, seq, lambda peer: tile_to_seq(peer, peer).wait_recv())
    others(group, own, lambda peer: tiles_to_group(peer, own).start())
    for item in unit_loads:
        item.wait()
    cell = units.shape[2] // 2 // seqs
    for member in range(group):
        for run in range(seqs):
            home = (run * group + member) * cell
            for index, source in enumerate((gate, up)):
                first = (index * seqs + run) * cell
                units[member, :, first : first + cell] = source[:, home : home + cell]
    units_kept = pltpu.make_async_copy(units, units_ref, unit_sem.at[2])
    units_kept.start()

    def pass_block(member):
        block_swap(member, member).wait_recv()
        others(seqs, seq, lambda peer: block_share(seq, member, peer).start())

    others(group, own, pass_block)
    others(group, own, lambda peer: tiles_to_group(peer, peer).wait_recv())
    for column in range(width // 128):
        total = 0.0
        for place in range(column * per, (column + 1) * per):
            total = total + gains[place % group, place // group, 0:1, :]
        gain[0:1, column * 128 : (column + 1) * 128] = total

    def kept(slot, batch):
        return pltpu.make_async_copy(
            normed.at[slot, pl.ds(batch * piece, piece)],
            g_ref.at[batch, rows_at(slot, piece)],
            keep.at[slot, batch],
        )

    def use(slot):
        @pl.loop(0, x_ref.shape[0] // 64)
        def _(chunk):
            rows = rows_at(chunk, 64)
            values = buf[slot, rows, :].astype(jnp.float32)
            normed[slot, rows, :] = to_half(normalize(values, gain[0:1, :]))

        for batch in range(batches):
            kept(slot, batch).start()
        rows = rows_at(slot, piece)
        got = to_half(dot_nn(normed[slot], w[...]))
        for batch in range(batches):
            mine = got[batch * piece : (batch + 1) * piece]
            q_ref[batch, rows, :] = mine[:, :span]
            kv_ref[batch, rows, :] = mine[:, span:]

    pl.loop(1, chips - 1)(spread.relay)

    def have_block(run, member):
        block_share(run, member, seq).wait_recv()

    others(seqs, seq, lambda run: pl.loop(0, group)(lambda member: have_block(run, member)))
    w_kept = pltpu.make_async_copy(w, w_out_ref, w_keep)
    w_kept.start()
    gains_kept = pltpu.make_async_copy(gains, gains_ref, gain_keep)
    gains_kept.start()

    pl.loop(0, chips - 1)(lambda far: spread.each(far, use))
    spread.relay(chips - 1)
    spread.each(chips - 1, use)
    spread.each(chips, use)
    spread.sent()
    others(seqs, seq, lambda peer: tile_to_seq(peer, seq).wait_send())
    others(group, own, lambda peer: block_swap(peer, own).wait_send())
    others(group, own, lambda peer: tiles_to_group(peer, own).wait_send())
    others(
        seqs,
        seq,
        lambda peer: pl.loop(0, group)(lambda member: block_share(seq, member, peer).wait_send()),
    )
    w_kept.wait()
    gains_kept.wait()
    units_kept.wait()

    @pl.loop(0, group)
    def _(slot):
        for batch in range(batches):
            kept(slot, batch).wait()


def start(seqs, chips, batches, tile, x, weights, unit_weights, collective):
    rows, width = x.shape
    group = 2 * chips
    length = group * rows // batches
    share = weights[0].shape[0]
    span = width // group
    cols = 3 * span
    wide = unit_weights[0].shape[1]
    half = jnp.bfloat16
    return pl.pallas_call(
        functools.partial(start_kernel, seqs, chips, batches),
        out_shape=[
            jax.ShapeDtypeStruct((batches, length, width), half),
            jax.ShapeDtypeStruct((batches, length, span), half),
            jax.ShapeDtypeStruct((batches, length, 2 * span), half),
            jax.ShapeDtypeStruct((group, seqs, 8, 128), jnp.float32),
            jax.ShapeDtypeStruct((width, cols), half),
            jax.ShapeDtypeStruct((group, share, 2 * wide // group), half),
        ],
        in_specs=[VMEM_SPEC] * 5 + [ANY_SPEC] * 2,
        out_specs=[ANY_SPEC, VMEM_SPEC, VMEM_SPEC, ANY_SPEC, ANY_SPEC, ANY_SPEC],
        scratch_shapes=[
            pltpu.VMEM((share, wide), half),
            pltpu.VMEM((share, wide), half),
            pltpu.VMEM((group, share, 2 * wide // group), half),
            sems(3),
            pltpu.VMEM((group, share, cols), half),
            pltpu.VMEM((group, rows, width), half),
            pltpu.VMEM((group, rows, width), half),
            pltpu.VMEM((8, width), jnp.float32),
            pltpu.VMEM((group, seqs, 8, 128), jnp.float32),
            pltpu.VMEM((width, cols), half),
            sems(3, group, PARTS),
            sems(group, PARTS),
            sems(group, batches),
            sems(group),
            sems(seqs, group),
            sems(seqs, group),
            sems(seqs),
            sems(group),
            sems(seqs),
            sems(group),
            pltpu.SemaphoreType.DMA,
            pltpu.SemaphoreType.DMA,
        ],
        compiler_params=comm_params(collective),
        cost_estimate=cost(2 * group * rows * width * cols, 200 * MIB, group * rows * width * 2),
        name="start",
    )(tile, x, *weights, *unit_weights)


def attend_kernel(
    seqs, group, block, q_ref, kv_ref, low_ref, units_ref, out_ref, lse_ref, pad_ref, own_units_ref,
    pad, vt_ref, halo_send, halo_recv, pad_keep, swap_send, swap_recv, swap_keep,
):
    seq = lax.axis_index("seq")
    batches, length, span = q_ref.shape
    has_left, has_right = seq > 0, seq < seqs - 1
    pl.when(has_left)(lambda: signal_seq(seq - 1))
    pl.when(has_right)(lambda: signal_seq(seq + 1))
    meet(greet_group(group) + has_left.astype(jnp.int32) + has_right.astype(jnp.int32))

    steps, need = length // block, WINDOW // block

    def halo(batch, step, peer):
        return pltpu.make_async_remote_copy(
            src_ref=kv_ref.at[batch, rows_at(step + steps - need, block)],
            dst_ref=pad.at[batch, rows_at(step, block)],
            send_sem=halo_send.at[batch, step],
            recv_sem=halo_recv.at[batch, step],
            device_id={"seq": peer},
            device_id_type=MESH,
        )

    def send_halo(turn):
        batch, step = turn // need, need - 1 - lax.rem(turn, need)
        pl.when(has_right)(lambda: halo(batch, step, seq + 1).start())

    def halo_sent(turn):
        batch, step = turn // need, need - 1 - lax.rem(turn, need)
        pl.when(has_right)(lambda: halo(batch, step, seq + 1).wait_send())

    send_halo(0)
    send_halo(1)
    swap = Swap(group, units_ref, own_units_ref, swap_send, swap_recv, swap_keep)
    swap.begin()
    pad[:, WINDOW:, :] = kv_ref[...]

    @pl.when(jnp.logical_not(has_left))
    def _():
        pad[:, :WINDOW, :] = jnp.zeros((batches, WINDOW, 2 * span), jnp.bfloat16)

    def kept(batch):
        return pltpu.make_async_copy(pad.at[batch], pad_ref.at[batch], pad_keep.at[batch])

    vt = vt_ref
    for batch in range(batches):
        vt[:, WINDOW:] = pad[batch, WINDOW:, span:].T

        @pl.loop(0, steps)
        def _(turn, batch=batch):
            step = steps - 1 - turn

            @pl.when(step < need)
            def _():
                rows = rows_at(step, block)
                pl.when(has_left)(lambda: halo(batch, step, seq).wait_recv())
                vt[:, rows] = pad[batch, rows, span:].T
                place = batch * need + need - 1 - step
                halo_sent(place)
                pl.when(place + 2 < batches * need)(lambda: send_halo(place + 2))

            begin = pl.multiple_of(step * block, block)
            keys = pl.ds(begin, block + WINDOW)
            rows = pl.ds(begin, block)
            low = low_ref[batch, :, rows]
            for pair in range(span // PAIR):
                lanes = slice(pair * PAIR, (pair + 1) * PAIR)
                q_pair = q_ref[batch, rows, lanes] * jnp.asarray(HEAD**-0.5, jnp.bfloat16)
                k_rows = pad[batch, keys, lanes]
                values = vt[lanes, keys]
                mixed = []
                for half in range(2):
                    scores = masked_scores(k_rows, head_lanes(q_pair, half), low)
                    top = jnp.max(scores, axis=0, keepdims=True)
                    expo = jnp.exp(scores - top)
                    total = jnp.sum(expo, axis=0, keepdims=True)
                    mixed.append(dot_nn(values, to_half(expo)) / total)
                    row = pair * 2 + half
                    lse_ref[batch, row : row + 1, rows] = top + jnp.log(total)
                lane = lax.broadcasted_iota(jnp.int32, mixed[0].shape, 0)
                out_ref[batch, rows, lanes] = to_half(jnp.where(lane < HEAD, mixed[0], mixed[1]).T)

    for batch in range(batches):
        kept(batch).start()
    swap.end()
    for batch in range(batches):
        kept(batch).wait()


def attend(seqs, group, query, key_value, low, block, units, collective):
    batches, length, span = query.shape
    padded = length + WINDOW
    heads = span // HEAD
    half = jnp.bfloat16
    return pl.pallas_call(
        functools.partial(attend_kernel, seqs, group, block),
        in_specs=[VMEM_SPEC, VMEM_SPEC, VMEM_SPEC, ANY_SPEC],
        out_specs=[VMEM_SPEC, VMEM_SPEC, ANY_SPEC, ANY_SPEC],
        out_shape=[
            jax.ShapeDtypeStruct((batches, length, span), half),
            jax.ShapeDtypeStruct((batches, heads, length), jnp.float32),
            jax.ShapeDtypeStruct((batches, padded, 2 * span), half),
            jax.ShapeDtypeStruct(units.shape, half),
        ],
        scratch_shapes=[
            pltpu.VMEM((batches, padded, 2 * span), half),
            pltpu.VMEM((span, padded), half),
            sems(batches, WINDOW // block),
            sems(batches, WINDOW // block),
            sems(batches),
            sems(group),
            sems(group),
            pltpu.SemaphoreType.DMA,
        ],
        compiler_params=comm_params(collective),
        cost_estimate=cost(
            8 * batches * length * span * (WINDOW + block), 150 * MIB, units.size * 2
        ),
        name="attend",
    )(query, key_value, low, units)


def branch_kernel(
    seqs, chips, a_ref, w_ref, d_ref, units_ref, x_ref, gain_ref, middle_ref, normed_ref, gd_ref, w_units_ref,
    out_ref, acc, cross_out, line_out, cross_in, line_in, sum_send, sum_recv,
    send, recv, d_keep, share_send, share_recv, share_keep,
):
    line = Line(chips)
    rows = out_ref.shape[0]

    def product(slot, tile):
        return dot_nn(left_rows(a_ref, slot, rows), w_ref[:, rows_at(tile, TILE)])

    meet(line.greet() + greet_seq(seqs))
    reduce = Reduce(
        line, product, out_ref, acc, cross_out, line_out, cross_in, line_in, sum_send, sum_recv
    )
    spread = Spread(line, d_ref, gd_ref, send, recv)
    units = Share(seqs, units_ref, w_units_ref, share_send, share_recv, share_keep)
    d_kept = pltpu.make_async_copy(d_ref, gd_ref.at[line.own], d_keep)
    units.begin()
    spread.begin()
    d_kept.start()

    @pl.loop(0, chips)
    def _(step):
        def also(tile):
            pl.when(step < chips - 1)(lambda: spread.relay_part(step + 1, tile))

        reduce.level(chips - 1 - step, also)
        pl.when(step == chips - 2)(units.pass_on)

    @pl.loop(0, rows // 32)
    def _(chunk):
        here = rows_at(chunk, 32)
        middle = x_ref[here, :].astype(jnp.float32) + out_ref[here, :]
        middle_ref[here, :] = middle
        normed_ref[here, :] = to_half(normalize(middle, gain_ref[0:1, :]))

    spread.rest()
    spread.sent()
    reduce.sent()
    d_kept.wait()
    units.end()


def branch_sum(seqs, chips, a, w, d_rows, units, x, gain, collective):
    rows, width = d_rows.shape
    group = 2 * chips
    half = jnp.bfloat16
    return pl.pallas_call(
        functools.partial(branch_kernel, seqs, chips),
        out_shape=[
            jax.ShapeDtypeStruct((rows, width), jnp.float32),
            jax.ShapeDtypeStruct((rows, width), half),
            jax.ShapeDtypeStruct((group, rows, width), half),
            jax.ShapeDtypeStruct((seqs,) + units.shape, half),
        ],
        in_specs=[VMEM_SPEC, VMEM_SPEC, ANY_SPEC, ANY_SPEC, VMEM_SPEC, VMEM_SPEC],
        out_specs=[VMEM_SPEC, VMEM_SPEC, ANY_SPEC, ANY_SPEC],
        scratch_shapes=[pltpu.VMEM((rows, width), jnp.float32)]
        + Reduce.scratch(chips, rows, width)
        + [sems(3, group, PARTS), sems(group, PARTS), pltpu.SemaphoreType.DMA]
        + [sems(seqs, 2), sems(seqs, 2), pltpu.SemaphoreType.DMA],
        compiler_params=comm_params(collective),
        cost_estimate=cost(
            2 * group * rows * width * w.shape[0], 250 * MIB, 3 * group * rows * width * 2
        ),
        name="branch_sum",
    )(a, w, d_rows, units, x, gain)


class PairReduce:
    def __init__(self, line, product, out, acc, keep, cross_out, cross_in, line_out, line_in, send, recv):
        self.line, self.product, self.out, self.acc, self.keep = line, product, out, acc, keep
        self.cross_out, self.cross_in, self.line_out, self.line_in = cross_out, cross_in, line_out, line_in
        self.send, self.recv = send, recv
        self.tiles = keep.shape[1] // TILE

    @staticmethod
    def scratch(chips, piece, width):
        half = jnp.bfloat16
        return [
            pltpu.VMEM((piece, width), half),
            pltpu.VMEM((2, piece, width), half),
            pltpu.VMEM((2, piece, width), half),
            pltpu.VMEM((chips + 1, piece, width), half),
            pltpu.SemaphoreType.DMA((3, width // TILE)),
            pltpu.SemaphoreType.DMA((chips + 3, width // TILE)),
        ]

    def cross(self, parity, tile):
        here = rows_at(tile, TILE)
        return pltpu.make_async_remote_copy(
            src_ref=self.cross_out.at[:, here],
            dst_ref=self.cross_in.at[parity, :, here],
            send_sem=self.send.at[0, tile],
            recv_sem=self.recv.at[self.line.chips + 1 + parity, tile],
            device_id={"fsdp": self.line.other},
            device_id_type=MESH,
        )

    def along(self, parity, landing, tile, peer):
        here = rows_at(tile, TILE)
        return pltpu.make_async_remote_copy(
            src_ref=self.line_out.at[parity, :, here],
            dst_ref=self.line_in.at[landing, :, here],
            send_sem=self.send.at[1 + parity, tile],
            recv_sem=self.recv.at[landing, tile],
            device_id={"fsdp": peer},
            device_id_type=MESH,
        )

    def steps(self):
        return 2 * self.line.chips - 1

    def step(self, step):
        line, keep = self.line, self.keep
        piece = keep.shape[0]
        right_side = line.chips - 1 - line.chip
        away = line.chips - 1 - step // 2
        second = lax.rem(step, 2)
        rightward = (right_side >= line.chip) == (second == 0)
        place = line.chip + jnp.where(rightward, away, -away)
        longer = jnp.maximum(right_side, line.chip)
        shorter = jnp.minimum(right_side, line.chip)
        count = longer - away + jnp.maximum(shorter - away, 0) + second
        parity = lax.rem(count + 2 * line.chips, 2)
        upstream = (rightward & line.has_left) | (jnp.logical_not(rightward) & line.has_right)

        @pl.when((place >= 0) & (place < line.chips))
        def _():
            @pl.loop(0, self.tiles)
            def _(tile):
                here = rows_at(tile, TILE)
                self.acc[...] = self.product(place, tile)
                self.cross_out[:, here] = to_half(self.acc[rows_at(1 - line.core, piece), :])
                keep[:, here] = self.acc[rows_at(line.core, piece), :]
                self.cross(parity, tile).start()

            @pl.loop(0, self.tiles)
            def _(tile):
                here = rows_at(tile, TILE)
                self.cross(parity, tile).wait()
                keep[:, here] += self.cross_in[parity, :, here].astype(jnp.float32)

                @pl.when(away > 0)
                def _():
                    pl.when(count >= 2)(
                        lambda: self.along(parity, place, tile, line.own).wait_send()
                    )

                    @pl.when(upstream)
                    def _():
                        self.along(parity, place, tile, line.own).wait_recv()
                        self.line_out[parity, :, here] = to_half(
                            keep[:, here] + self.line_in[place, :, here].astype(jnp.float32)
                        )

                    @pl.when(jnp.logical_not(upstream))
                    def _():
                        self.line_out[parity, :, here] = to_half(keep[:, here])

                    @pl.when(rightward)
                    def _():
                        self.along(parity, place, tile, line.own + 2).start()

                    @pl.when(jnp.logical_not(rightward))
                    def _():
                        landing = jnp.where(away == 1, line.chips, place)
                        self.along(parity, landing, tile, line.own - 2).start()

                @pl.when(away == 0)
                def _():
                    self.out[:, here] = keep[:, here]

                    @pl.when(line.has_left)
                    def _():
                        self.along(parity, place, tile, line.own).wait_recv()
                        self.out[:, here] += self.line_in[place, :, here].astype(jnp.float32)

                    @pl.when(line.has_right)
                    def _():
                        self.along(parity, line.chips, tile, line.own).wait_recv()
                        self.out[:, here] += self.line_in[line.chips, :, here].astype(jnp.float32)

    def sent(self):
        for count in range(max(self.line.chips - 3, 0), self.line.chips - 1):
            pl.loop(0, self.tiles)(
                lambda tile, parity=count % 2: self.along(parity, 0, tile, self.line.own).wait_send()
            )


def feed_kernel(
    seqs, chips, batches, x_ref, w_hbm, wd_hbm, gd_hbm, v_ref, cot_ref, gain_ref,
    dm_ref, db_ref, gain_grad_ref, hidden_hbm, grad_hbm, grad_in,
    buf, d_buf, h_buf, w_ref, wd_ref, d_ref, tiles, totals, acc, keep,
    load, d_sem, h_sem, tile_sem, send, recv, part_send, part_recv, *sums,
):
    line = Line(chips)
    rows, width = x_ref.shape
    piece = rows // batches
    pair = 2 * piece
    units = wd_ref.shape[0]
    part = min(units, TILE)
    block = tiles.shape[1]
    loads = [
        pltpu.make_async_copy(w_hbm, w_ref, load.at[0]),
        pltpu.make_async_copy(wd_hbm, wd_ref, load.at[1]),
    ]
    for item in loads:
        item.start()
    meet(line.greet() + greet_seq(seqs))
    spreads = [
        Spread(
            line,
            x_ref.at[pl.ds(batch * piece, piece)],
            buf.at[batch],
            send.at[batch],
            recv.at[batch],
        )
        for batch in range(batches)
    ]
    spreads[0].begin()
    for batch in range(batches):
        buf[batch, line.own] = x_ref[batch * piece : (batch + 1) * piece, :]

    def fetch(batch, place, side):
        return [
            pltpu.make_async_copy(
                gd_hbm.at[place * 2 + core, pl.ds(batch * piece, piece)],
                d_buf.at[side, pl.ds(core * piece, piece)],
                d_sem.at[side, core],
            )
            for core in range(2)
        ]

    def stored(batch, place):
        return [
            pltpu.make_async_copy(
                h_buf.at[pl.ds(core * piece, piece)],
                hidden_hbm.at[
                    pl.ds(pl.multiple_of((place * 2 + core) * rows + batch * piece, piece), piece)
                ],
                h_sem.at[core],
            )
            for core in range(2)
        ]

    def sides(far, act):
        @pl.loop(0, 2)
        def _(side):
            place = line.chip + far * (2 * side - 1)
            valid = (place >= 0) & (place < chips) & ((side == 0) | (far > 0))
            pl.when(valid)(lambda: act(place, side))

    def take(batch, far):
        def begin(place, side):
            for item in fetch(batch, place, side):
                item.start()

        sides(far, begin)
        pl.when(far > 0)(lambda: spreads[batch].relay(far))

    def compute(batch, far):
        def act(place, side):
            spreads[batch].across(place * 2 + 1 - line.core)
            for item in fetch(batch, place, side):
                item.wait()

            def free():
                for item in stored(batch, place):
                    item.wait()

            if batch:
                free()
            else:
                pl.when((far > 0) | (side > 0))(free)
            there = rows_at(place, pair)

            @pl.loop(0, units // part)
            def _(tile):
                first = rows_at(tile, part)
                second = rows_at(units // part + tile, part)
                values = buf[batch, pl.ds(place * 2, 2), :, :].reshape(pair, width)
                gate = dot_nn(values, w_ref[:, first])
                up = dot_nn(values, w_ref[:, second])
                d_hidden = dot_nt(d_buf[side], wd_ref[first, :])
                sigma = jax.nn.sigmoid(gate)
                swish = gate * sigma
                h_buf[:, first] = to_half(swish * up)
                slope = sigma * (1.0 + gate * (1.0 - sigma))
                d_ref[batch, there, first] = to_half(d_hidden * up * slope)
                d_ref[batch, there, second] = to_half(d_hidden * swish)

            for item in stored(batch, place):
                item.start()

        sides(far, act)

    def product(batch):
        def get(place, tile):
            return dot_nt(d_ref[batch, rows_at(place, pair), :], w_ref[rows_at(tile, TILE), :])

        return get

    reduces = [
        PairReduce(line, product(batch), totals.at[batch], acc, keep, *sums[6 * batch : 6 * batch + 6])
        for batch in range(batches)
    ]

    count = width // block
    seq = lax.axis_index("seq")

    def tile_at(turn):
        early = turn < seqs - 1
        late = turn - (seqs - 1)
        dest = lax.rem(seq + jnp.where(early, turn + 1, late), seqs)
        return dest, dest * 2 + jnp.where(early | (late == 0), 0, 1)

    def grad_stored(turn):
        slot = lax.rem(turn, 2)
        return pltpu.make_async_copy(
            tiles.at[slot], grad_hbm.at[rows_at(tile_at(turn)[1], block)], tile_sem.at[slot]
        )

    parts = ToSeq(seqs, grad_hbm, grad_in, part_send, part_recv)

    def leave(turn):
        grad_stored(turn).wait()
        pl.when(turn < seqs - 1)(lambda: parts.move(tile_at(turn)[0], seq).start())

    def weight_grad(turn):
        slot = lax.rem(turn, 2)
        size = min(TILE, 2 * units)
        tile = tile_at(turn)[1]

        @pl.loop(0, 2 * units // size)
        def _(column):
            here = rows_at(column, size)
            got = 0.0
            for batch in range(batches):
                left = buf[batch, :, :, rows_at(tile, block)].reshape(2 * chips * piece, block)
                got = got + contract_rows(left, d_ref[batch, :, here])
            tiles[slot, :, here] = to_half(got)

        pl.when(turn > 0)(lambda: leave(turn - 1))
        grad_stored(turn).start()

    def norm_batch(batch):
        own = pl.ds(batch * piece, piece)

        def put(here, d_values):
            there = pl.ds(pl.multiple_of(here.start + batch * piece, here.size), here.size)
            d_middle = cot_ref[there, :].astype(jnp.float32) + d_values
            dm_ref[there, :] = d_middle
            db_ref[there, :] = to_half(d_middle)

        norm_back(piece, v_ref.at[own], totals.at[batch], gain_ref, gain_grad_ref, put)

    gain_grad_ref[...] = jnp.zeros_like(gain_grad_ref)
    for item in loads:
        item.wait()
    last = 2 * chips - 2

    @pl.loop(0, chips)
    def _(far):
        take(0, far)
        pl.when(far == chips - 2)(spreads[1].begin)
        compute(0, far)

    @pl.loop(0, chips - 1)
    def _(far):
        take(1, far)
        reduces[0].step(2 * far)
        reduces[0].step(2 * far + 1)
        compute(1, far)

    take(1, chips - 1)
    compute(1, chips - 1)

    @pl.loop(0, 2)
    def _(step):
        reduces[1].step(step)
        weight_grad(step)

    reduces[0].step(last)
    norm_batch(0)

    @pl.loop(2, last)
    def _(step):
        reduces[1].step(step)
        pl.when(step < count)(lambda: weight_grad(step))

    @pl.loop(last, max(count, last))
    def _(tile):
        weight_grad(tile)

    reduces[1].step(last)
    norm_batch(1)
    for batch in range(batches):
        spreads[batch].sent()
        reduces[batch].sent()
    for item in stored(1, 0):
        item.wait()
    leave(count - 1)
    parts.end()


def feed_forward(seqs, chips, batches, x, w, wd, group_d, middle, cot, gain, collective):
    rows, width = x.shape
    group = 2 * chips
    units = wd.shape[0]
    piece = rows // batches
    block = width // seqs // 2
    half = jnp.bfloat16
    return pl.pallas_call(
        functools.partial(feed_kernel, seqs, chips, batches),
        out_shape=[
            jax.ShapeDtypeStruct((rows, width), jnp.float32),
            jax.ShapeDtypeStruct((rows, width), half),
            jax.ShapeDtypeStruct((8, width), jnp.float32),
            jax.ShapeDtypeStruct((group * rows, units), half),
            jax.ShapeDtypeStruct((width, 2 * units), half),
            jax.ShapeDtypeStruct((seqs, block, 2 * units), half),
        ],
        in_specs=[VMEM_SPEC] + [ANY_SPEC] * 3 + [VMEM_SPEC] * 3,
        out_specs=[VMEM_SPEC] * 3 + [ANY_SPEC] * 3,
        scratch_shapes=[
            pltpu.VMEM((batches, group, piece, width), half),
            pltpu.VMEM((2, 2 * piece, width), half),
            pltpu.VMEM((2 * piece, units), half),
            pltpu.VMEM(w.shape, half),
            pltpu.VMEM(wd.shape, half),
            pltpu.VMEM((batches, group * piece, 2 * units), half),
            pltpu.VMEM((2, block, 2 * units), half),
            pltpu.VMEM((batches, piece, width), jnp.float32),
            pltpu.VMEM((2 * piece, TILE), jnp.float32),
            pltpu.VMEM((piece, width), jnp.float32),
            sems(2),
            sems(2, 2),
            sems(2),
            sems(2),
            sems(batches, 3, group, PARTS // 2),
            sems(batches, group, PARTS // 2),
            sems(seqs),
            sems(seqs),
        ]
        + PairReduce.scratch(chips, piece, width) * batches,
        compiler_params=comm_params(collective, 63),
        cost_estimate=cost(
            14 * group * rows * width * units, 400 * MIB, 2 * group * rows * width * 2
        ),
        name="feed_forward",
    )(x, w, wd, group_d, middle, cot, gain)


def branch_back_kernel(
    seqs, chips, batches, x_ref, w_ref, att_ref, middle_ref, hidden_hbm, wd_hbm, units_hbm, gd_hbm,
    d_ref, layer_ref, out_grad_ref, units_in, down_hbm, down_in,
    out_ref, buf, hidden_ref, wd_ref, grad_acc, rights, tiles, send, recv, load, right_sem, tile_sem,
    part_send, part_recv, down_send, down_recv, down_keep, acc, cross_out, line_out, cross_in, line_in, sum_send, sum_recv,
):
    line = Line(chips)
    rows = x_ref.shape[0]
    piece = rows // batches
    width = x_ref.shape[1]
    loads = [
        pltpu.make_async_copy(hidden_hbm, hidden_ref, load.at[0]),
        pltpu.make_async_copy(wd_hbm, wd_ref, load.at[1]),
    ]
    for item in loads:
        item.start()

    def product(slot, tile):
        return dot_nn(left_rows(hidden_ref, slot, rows), wd_ref[:, rows_at(tile, TILE)])

    part = rights.shape[2]
    count = width // part

    def right(tile):
        slot = lax.rem(tile, 2)
        return pltpu.make_async_copy(
            gd_hbm.at[:, rows_at(tile, part)], rights.at[slot], right_sem.at[slot]
        )

    def stored(tile):
        slot = lax.rem(tile, 2)
        return pltpu.make_async_copy(
            tiles.at[slot], down_hbm.at[:, rows_at(tile, part)], tile_sem.at[slot]
        )

    def weight_grad(tile):
        right(tile).wait()
        pl.when(tile + 1 < count)(lambda: right(tile + 1).start())
        pl.when(tile >= 2)(lambda: stored(tile - 2).wait())
        slot = lax.rem(tile, 2)
        size = min(TILE, hidden_ref.shape[1])

        @pl.loop(0, hidden_ref.shape[1] // size)
        def _(row):
            here = rows_at(row, size)
            tiles[slot, here, :] = to_half(contract_rows(hidden_ref[:, here], rights[slot]))

        stored(tile).start()

    right(0).start()
    meet(line.greet() + greet_seq(seqs))
    sums = ToSeq(seqs, units_hbm, units_in, part_send, part_recv, units_in.shape[1])
    down = ToSeq(seqs, down_hbm, down_in, down_send, down_recv)
    down_rows = down_in.shape[1]
    down_kept = pltpu.make_async_copy(
        down_hbm.at[rows_at(down.own, down_rows)], down_in.at[down.own], down_keep
    )
    spread = Spread(line, x_ref, buf, send, recv)
    reduce = Reduce(
        line, product, out_ref, acc, cross_out, line_out, cross_in, line_in, sum_send, sum_recv
    )
    spread.begin()
    sums.begin()
    buf[line.own] = x_ref[...]
    grad_acc[...] = jnp.zeros_like(grad_acc)

    def use(slot):
        got = to_half(dot_nt(buf[slot], w_ref[...]))
        for batch in range(batches):
            d_ref[batch, rows_at(slot, piece), :] = got[batch * piece : (batch + 1) * piece]
        mixed = left_rows(att_ref, slot, rows)

        @pl.loop(0, width // TILE)
        def _(tile):
            here = rows_at(tile, TILE)
            grad_acc[:, here] += contract_rows(mixed, buf[slot, :, here])

    for item in loads:
        item.wait()

    per = -(-count // 2)

    @pl.loop(0, chips)
    def _(step):
        def also(tile):
            pl.when(step < chips - 1)(lambda: spread.relay_part(step + 1, tile))

        reduce.level(chips - 1 - step, also)
        spread.each(step, use)

        @pl.when(step < 2)
        def _():
            @pl.loop(0, per)
            def _(turn):
                tile = step * per + turn
                pl.when(tile < count)(lambda: weight_grad(tile))

        @pl.when(step == 1)
        def _():
            stored(count - 2).wait()
            stored(count - 1).wait()
            down.begin()
            down_kept.start()

    spread.each(chips, use)

    @pl.loop(0, rows // 32)
    def _(chunk):
        here = rows_at(chunk, 32)
        layer_ref[here, :] = to_half(middle_ref[here, :] + out_ref[here, :])

    out_grad_ref[...] = to_half(grad_acc[...])
    spread.sent()
    reduce.sent()
    sums.end()
    down.end()
    down_kept.wait()


def branch_back(seqs, chips, batches, x, w, attended, middle, hidden, wd, unit_part, group_d, collective):
    rows, width = x.shape
    group = 2 * chips
    length = group * rows // batches
    span = w.shape[0]
    half = jnp.bfloat16
    part = 256 if group * rows <= 2048 else 128
    return pl.pallas_call(
        functools.partial(branch_back_kernel, seqs, chips, batches),
        out_shape=[
            jax.ShapeDtypeStruct((batches, length, span), half),
            jax.ShapeDtypeStruct((rows, width), half),
            jax.ShapeDtypeStruct((span, width), half),
            jax.ShapeDtypeStruct((seqs, width // seqs // 2, unit_part.shape[1]), half),
            jax.ShapeDtypeStruct((wd.shape[0], width), half),
            jax.ShapeDtypeStruct((seqs, wd.shape[0] // seqs, width), half),
        ],
        in_specs=[VMEM_SPEC] * 4 + [ANY_SPEC] * 4,
        out_specs=[VMEM_SPEC, VMEM_SPEC, VMEM_SPEC, ANY_SPEC, ANY_SPEC, ANY_SPEC],
        scratch_shapes=[
            pltpu.VMEM((rows, width), jnp.float32),
            pltpu.VMEM((group, rows, width), half),
            pltpu.VMEM(hidden.shape, half),
            pltpu.VMEM(wd.shape, half),
            pltpu.VMEM((span, width), jnp.float32),
            pltpu.VMEM((2, group * rows, part), half),
            pltpu.VMEM((2, wd.shape[0], part), half),
            sems(3, group, PARTS),
            sems(group, PARTS),
            sems(2),
            sems(2),
            sems(2),
            sems(seqs),
            sems(seqs),
            sems(seqs),
            sems(seqs),
            pltpu.SemaphoreType.DMA,
        ]
        + Reduce.scratch(chips, rows, width),
        compiler_params=comm_params(collective, 62),
        cost_estimate=cost(
            2 * group * rows * width * (2 * span + 2 * wd.shape[0]),
            250 * MIB,
            2 * group * rows * width * 2,
        ),
        name="branch_back",
    )(x, w, attended, middle, hidden, wd, unit_part, group_d.reshape(group * rows, width))


def attention_back_kernel(
    seqs, chips, block, q_ref, pad_ref, low_ref, lse_ref, d_ref, part_hbm, in_one, in_two,
    w_ref, g_hbm, v_ref, dm_hbm, gain_ref, mlp_gain_ref, out_ref,
    grad_ref, wq_ref, wk_ref, wv_ref, wo_ref, tile_ref, gate_ref, up_ref,
    dk, dv, kt, heads, back_out, back_in, unit_parts, unit_sums, units, lefts, parts, sums, cols, out_in,
    totals, gain_acc, gain_out, gain_in, gain_sum, gain_back, acc, keep,
    halo_send, halo_recv, unit_load, unit_send, unit_recv, unit_keep, dm_load, left_sem,
    part_send, part_recv, cols_send, cols_recv, out_send, out_recv,
    gain_send, gain_recv, back_send, back_recv, *line_sums,
):
    line = Line(chips)
    group = 2 * chips
    seq = lax.axis_index("seq")
    own = line.own
    batches, length, span = q_ref.shape
    rows, width = v_ref.shape
    piece = rows // batches
    pair_rows = 2 * piece
    depth = 3 * span
    run = width // seqs
    share = run // group
    part = lefts.shape[3]
    steps, need = length // block, WINDOW // block
    first = length - WINDOW
    has_left, has_right = seq > 0, seq < seqs - 1
    scale = jnp.asarray(HEAD**-0.5, jnp.bfloat16)

    def others(count, me, act):
        pl.loop(1, count)(lambda ahead: act(lax.rem(me + ahead, count)))

    def unit_loaded(turn, place, source):
        slot = lax.rem(turn, 2)
        return pltpu.make_async_copy(source, unit_parts.at[slot, place], unit_load.at[slot, place])

    def load_units(turn):
        member = lax.rem(own + turn, group)
        mine = part_hbm.at[rows_at(seq * group + member, share)]
        for place in range(seqs):

            def fetch(source, place=place):
                unit_loaded(turn, place, source).start()

            pl.when(place == seq)(lambda: fetch(mine))

            @pl.when((place != seq) & (member < chips))
            def _(place=place):
                fetch(in_one.at[place, rows_at(member, share)])

            @pl.when((place != seq) & (member >= chips))
            def _(place=place):
                fetch(in_two.at[place, rows_at(member - chips, share)])

    load_units(1)
    dm_loaded = pltpu.make_async_copy(dm_hbm, grad_ref, dm_load)
    dm_loaded.start()
    meet(greet_group(group) + greet_seq(seqs))
    swap = Swap(group, unit_sums, units, unit_send, unit_recv, unit_keep)

    @pl.loop(1, group + 1)
    def _(turn):
        member = lax.rem(own + turn, group)
        slot = lax.rem(turn, 2)
        pl.when(turn < group)(lambda: load_units(turn + 1))
        for place in range(seqs):
            unit_loaded(turn, place, part_hbm.at[rows_at(0, share)]).wait()

        @pl.loop(0, share // 16)
        def _(chunk):
            here = rows_at(chunk, 16)
            added = unit_parts[slot, 0, here, :].astype(jnp.float32)
            for place in range(1, seqs):
                added = added + unit_parts[slot, place, here, :].astype(jnp.float32)
            unit_sums[member, here, :] = to_half(added)

        pl.when(turn < group)(lambda: swap.move(member, own).start())
        pl.when(turn == group)(lambda: swap.kept().start())

    def halo(batch, step, peer):
        here = rows_at(step, block)
        return pltpu.make_async_remote_copy(
            src_ref=back_out.at[batch, here],
            dst_ref=back_in.at[batch, here],
            send_sem=halo_send.at[batch, step],
            recv_sem=halo_recv.at[batch, step],
            device_id={"seq": peer},
            device_id_type=MESH,
        )

    def attend_block(batch, step):
        begin = pl.multiple_of(step * block, block)
        keys = pl.ds(begin, block + WINDOW)
        rows = pl.ds(begin, block)
        low = low_ref[batch, :, rows]
        for pair in range(span // PAIR):
            lanes = slice(pair * PAIR, (pair + 1) * PAIR)
            q_pair = q_ref[batch, rows, lanes] * scale
            d_pair = d_ref[batch, rows, lanes]
            k_rows = pad_ref[batch, keys, lanes]
            v_rows = pad_ref[batch, keys, span + pair * PAIR : span + (pair + 1) * PAIR]
            k_cols = kt[lanes, keys]
            back = []
            for half in range(2):
                row = pair * 2 + half
                q_head = head_lanes(q_pair, half)
                d_head = head_lanes(d_pair, half)
                scores = masked_scores(k_rows, q_head, low)
                probs = jnp.exp(scores - lse_ref[batch, row : row + 1, rows])
                d_probs = dot_nt(v_rows, d_head)
                along = jnp.sum(probs * d_probs, axis=0, keepdims=True)
                d_scores = to_half(probs * (d_probs - along))
                dv[keys, lanes] += dot_nn(to_half(probs), d_head)
                dk[keys, lanes] += dot_nn(d_scores, q_head)
                back.append(dot_nn(k_cols, d_scores))
            at = lax.broadcasted_iota(jnp.int32, back[0].shape, 0)
            heads[batch, rows, lanes] = to_half(
                jnp.where(at < HEAD, back[0], back[1]).T
            )


        @pl.when(has_left & (step < need))
        def _():
            back_out[batch, rows, :span] = to_half(dk[rows, :])
            back_out[batch, rows, span:] = to_half(dv[rows, :])
            halo(batch, step, seq - 1).start()

        @pl.when(step == steps - 1)
        def _():
            heads[batch, :, span : 2 * span] = to_half(dk[WINDOW:, :])
            heads[batch, :, 2 * span :] = to_half(dv[WINDOW:, :])

    def add_halo(batch):
        @pl.when(has_right)
        def _():
            @pl.loop(0, need)
            def _(step):
                there = pl.ds(pl.multiple_of(step * block + first, block), block)
                halo(batch, step, seq).wait_recv()
                got = back_in[batch, rows_at(step, block), :].astype(jnp.float32)
                mine = heads[batch, there, span:].astype(jnp.float32)
                heads[batch, there, span:] = to_half(mine + got)

    def product(batch):
        def get(place, tile):
            return dot_nt(heads[batch, rows_at(place, pair_rows), :], w_ref[rows_at(tile, TILE), :])

        return get

    reduces = [
        PairReduce(
            line, product(batch), totals.at[batch], acc, keep, *line_sums[6 * batch : 6 * batch + 6]
        )
        for batch in range(batches)
    ]
    last = 2 * chips - 2

    @pl.loop(0, 2 * steps)
    def _(turn):
        batch, step = turn // steps, lax.rem(turn, steps)

        @pl.when(step == 0)
        def _():
            kt[...] = pad_ref[batch, :, :span].T * scale
            dk[...] = jnp.zeros_like(dk)
            dv[...] = jnp.zeros_like(dv)

        attend_block(batch, step)
        after = turn - steps - 1
        pl.when(after == 0)(lambda: add_halo(0))

        @pl.when((after >= 0) & (2 * after < last))
        def _():
            reduces[0].step(2 * after)
            reduces[0].step(2 * after + 1)

    for after in range(steps - 1, chips - 1):
        reduces[0].step(2 * after)
        reduces[0].step(2 * after + 1)

    def left(tile):
        slot = lax.rem(tile, 2)
        return pltpu.make_async_copy(
            g_hbm.at[:, :, rows_at(tile, part)], lefts.at[slot], left_sem.at[slot]
        )

    def to_seq(peer, place):
        return pltpu.make_async_remote_copy(
            src_ref=parts.at[rows_at(peer, run)],
            dst_ref=sums.at[place],
            send_sem=part_send.at[peer],
            recv_sem=part_recv.at[place],
            device_id={"seq": peer},
            device_id_type=MESH,
        )

    left(0).start()
    add_halo(1)

    @pl.loop(0, width // part)
    def _(tile):
        left(tile).wait()
        pl.when(tile + 1 < width // part)(lambda: left(tile + 1).start())
        slot = lax.rem(tile, 2)
        got = contract_rows(lefts[slot, 0], heads[0])
        for batch in range(1, batches):
            got = got + contract_rows(lefts[slot, batch], heads[batch])
        parts[rows_at(tile, part), :] = to_half(got)

    others(seqs, seq, lambda peer: to_seq(peer, seq).start())
    from_seq = ToSeq(seqs, out_ref, out_in, out_send, out_recv)
    from_seq.begin()
    gain_acc[...] = jnp.zeros_like(gain_acc)
    dm_loaded.wait()

    def norm_batch(batch):
        mine = pl.ds(batch * piece, piece)

        def put(here, d_values):
            there = pl.ds(pl.multiple_of(here.start + batch * piece, here.size), here.size)
            grad_ref[there, :] += d_values

        norm_back(piece, v_ref.at[mine], totals.at[batch], gain_ref, gain_acc, put)

    pl.loop(0, 2)(reduces[1].step)
    reduces[0].step(last)
    norm_batch(0)
    pl.loop(2, last)(reduces[1].step)
    swap.end()
    cell = units.shape[2] // 2 // seqs
    for member in range(group):
        for place in range(seqs):
            column = (place * group + member) * cell
            for target, begin in ((gate_ref, 0), (up_ref, seqs * cell)):
                here = slice(begin + place * cell, begin + (place + 1) * cell)
                target[:, column : column + cell] = units[member, :, here]

    def block_swap(peer, member):
        return pltpu.make_async_remote_copy(
            src_ref=parts.at[rows_at(seq * group + peer, share)],
            dst_ref=cols.at[member],
            send_sem=cols_send.at[peer],
            recv_sem=cols_recv.at[member],
            device_id={"fsdp": peer},
            device_id_type=MESH,
        )

    others(seqs, seq, lambda peer: to_seq(peer, peer).wait_recv())

    @pl.loop(0, run // 64)
    def _(chunk):
        here = rows_at(chunk, 64)
        there = pl.ds(pl.multiple_of(seq * run + chunk * 64, 64), 64)
        parts[there, :] = to_half(add_from_seq(seqs, parts[there, :], sums, here))

    others(group, own, lambda peer: block_swap(peer, own).start())
    cols[own] = parts[rows_at(seq * group + own, share), :]
    from_seq.arrived()
    out_rows = out_in.shape[1]
    wo_ref[...] = add_from_seq(seqs, out_ref[rows_at(seq, out_rows), :], out_in, slice(None))
    reduces[1].step(last)
    norm_batch(1)
    fold = 128 // share
    near = group // fold
    attn_row = jnp.sum(gain_acc[...], axis=0, keepdims=True)
    mlp_row = jnp.sum(mlp_gain_ref[...], axis=0, keepdims=True)
    gain_out[...] = jnp.zeros_like(gain_out)
    for place in range(width // 128):
        lanes = slice(place * 128, (place + 1) * 128)
        gain_out[place % near, place // near, 0:1, :] = attn_row[:, lanes]
        gain_out[place % near, place // near, 1:2, :] = mlp_row[:, lanes]

    def gain_group(peer, member):
        return pltpu.make_async_remote_copy(
            src_ref=gain_out.at[peer // fold],
            dst_ref=gain_in.at[member],
            send_sem=gain_send.at[peer],
            recv_sem=gain_recv.at[member],
            device_id={"fsdp": peer},
            device_id_type=MESH,
        )

    def gain_seq(peer, place):
        return pltpu.make_async_remote_copy(
            src_ref=gain_sum.at[peer],
            dst_ref=gain_back.at[place],
            send_sem=back_send.at[peer],
            recv_sem=back_recv.at[place],
            device_id={"seq": peer},
            device_id_type=MESH,
        )

    others(group, own, lambda peer: gain_group(peer, own).start())
    gain_in[own] = gain_out[own // fold]
    others(group, own, lambda peer: gain_group(peer, peer).wait_recv())
    gain_sum[...] = jnp.sum(gain_in[...], axis=0)
    others(seqs, seq, lambda peer: gain_seq(peer, seq).start())
    gain_back[seq] = gain_sum[seq]
    others(seqs, seq, lambda peer: gain_seq(peer, peer).wait_recv())
    tile_ref[...] = jnp.sum(gain_back[...], axis=0)
    others(group, own, lambda peer: block_swap(peer, peer).wait_recv())
    for index, target in enumerate((wq_ref, wk_ref, wv_ref)):
        for member, first, home, size in column_parts(seqs, group, share, span):
            first = first + index * span
            target[:, home : home + size] = cols[member, :, first : first + size]
    from_seq.sent()
    for batch in range(batches):
        reduces[batch].sent()

        @pl.when(has_left)
        def _(batch=batch):
            pl.loop(0, need)(lambda step: halo(batch, step, seq).wait_send())

    others(seqs, seq, lambda peer: to_seq(peer, seq).wait_send())
    others(group, own, lambda peer: gain_group(peer, own).wait_send())
    others(group, own, lambda peer: block_swap(peer, own).wait_send())
    others(seqs, seq, lambda peer: gain_seq(peer, seq).wait_send())


def attention_back(
    seqs, chips, block, query, kv_pad, low, lse, d_att, part_own, parts_one, parts_two, w, group_a, x,
    d_middle, gain, mlp_gain, out_part, collective,
):
    batches, length, span = query.shape
    padded = kv_pad.shape[1]
    rows, width = x.shape
    piece = rows // batches
    group = 2 * chips
    depth = w.shape[1]
    run = width // seqs
    share = run // group
    near = group // (128 // share)
    cells = part_own.shape[1]
    out_rows = out_part.shape[0] // seqs
    half, wide = jnp.bfloat16, jnp.float32
    part = 256 if batches * length <= 2048 else 128
    return pl.pallas_call(
        functools.partial(attention_back_kernel, seqs, chips, block),
        out_shape=[
            jax.ShapeDtypeStruct((rows, width), wide),
            jax.ShapeDtypeStruct((share, width), half),
            jax.ShapeDtypeStruct((share, width), half),
            jax.ShapeDtypeStruct((share, width), half),
            jax.ShapeDtypeStruct((out_rows, width), wide),
            jax.ShapeDtypeStruct((8, 128), wide),
            jax.ShapeDtypeStruct((share, cells // 2 * group), half),
            jax.ShapeDtypeStruct((share, cells // 2 * group), half),
        ],
        in_specs=[VMEM_SPEC] * 5
        + [ANY_SPEC] * 3
        + [VMEM_SPEC, ANY_SPEC, VMEM_SPEC, ANY_SPEC]
        + [VMEM_SPEC] * 3,
        out_specs=[VMEM_SPEC] * 8,
        scratch_shapes=[
            pltpu.VMEM((padded, span), wide),
            pltpu.VMEM((padded, span), wide),
            pltpu.VMEM((span, padded), half),
            pltpu.VMEM((batches, length, depth), half),
            pltpu.VMEM((batches, WINDOW, 2 * span), half),
            pltpu.VMEM((batches, WINDOW, 2 * span), half),
            pltpu.VMEM((2, seqs, share, cells), half),
            pltpu.VMEM((group, share, cells), half),
            pltpu.VMEM((group, share, cells), half),
            pltpu.VMEM((2, batches, length, part), half),
            pltpu.VMEM((width, depth), half),
            pltpu.VMEM((seqs, run, depth), half),
            pltpu.VMEM((group, share, depth), half),
            pltpu.VMEM((seqs, out_rows, width), half),
            pltpu.VMEM((batches, piece, width), wide),
            pltpu.VMEM((8, width), wide),
            pltpu.VMEM((near, seqs, 8, 128), wide),
            pltpu.VMEM((group, seqs, 8, 128), wide),
            pltpu.VMEM((seqs, 8, 128), wide),
            pltpu.VMEM((seqs, 8, 128), wide),
            pltpu.VMEM((2 * piece, TILE), wide),
            pltpu.VMEM((piece, width), wide),
            sems(batches, WINDOW // block),
            sems(batches, WINDOW // block),
            sems(2, seqs),
            sems(group),
            sems(group),
            pltpu.SemaphoreType.DMA,
            pltpu.SemaphoreType.DMA,
            sems(2),
            sems(seqs),
            sems(seqs),
            sems(group),
            sems(group),
            sems(seqs),
            sems(seqs),
            sems(group),
            sems(group),
            sems(seqs),
            sems(seqs),
        ]
        + PairReduce.scratch(chips, piece, width) * batches,
        compiler_params=comm_params(collective, 63),
        cost_estimate=cost(
            20 * batches * length * span * (WINDOW + block) + 4 * group * rows * width * depth,
            400 * MIB,
            3 * group * rows * width * 2,
        ),
        name="attention_back",
    )(
        query, kv_pad, low, lse, d_att, part_own, parts_one, parts_two, w, group_a, x, d_middle,
        gain, mlp_gain, out_part,
    )


def doc_starts(lengths, positions, batches, seq_len):
    table = lengths.reshape(batches, -1, lengths.shape[1])
    starts = jnp.cumsum(table, axis=2) - table
    per_batch = seq_len // table.shape[1]
    begins = (starts + (jnp.arange(table.shape[1], dtype=jnp.int32) * per_batch)[None, :, None]).reshape(
        batches, -1
    )
    before = begins[:, None, :] <= positions[None, :, None]
    return jnp.max(jnp.where(before, begins[:, None, :], 0), axis=2)


def body(
    tokens,
    cotangent,
    lengths,
    gain_attn,
    w_query,
    w_key,
    w_value,
    w_out,
    gain_mlp,
    w_gate,
    w_up,
    w_down,
):
    batches, piece, width = tokens.shape
    seqs = lax.axis_size("seq")
    group = lax.axis_size("fsdp")
    chips = group // 2
    devices = seqs * group
    seq_len = piece * devices
    rows = batches * piece
    share = w_query.shape[0]
    span = width // group
    length = group * piece
    aligned = share == HEAD
    member = lax.axis_index("fsdp")

    x_rows = tokens.reshape(rows, width)
    cot_rows = cotangent.reshape(rows, width)
    wd_part = lax.all_gather(w_down, "seq", axis=0, tiled=True)
    if aligned:
        wo_part = lax.all_gather(w_out, "seq", axis=0, tiled=True)
    else:
        wo_all = lax.all_gather(w_out, ("seq", "fsdp"), axis=0, tiled=True)
        wo_part = lax.dynamic_slice_in_dim(wo_all, member * span, span, 0)

    lane = jnp.arange(128, dtype=jnp.int32)
    device = lax.axis_index("seq") * group + member
    fold = 128 // share
    here = lane // share == lax.rem(device, fold)
    both = jnp.stack([gain_attn, gain_mlp]).astype(jnp.float32)
    tile = jnp.where(here[None], jnp.tile(both, (1, fold)), 0.0)
    tile = jnp.pad(tile, ((0, 6), (0, 0)))[None]
    group_a, query, key_value, gains, w_heads, unit_blocks = start(
        seqs, chips, batches, tile, x_rows, (w_query, w_key, w_value), (w_gate, w_up), 1
    )
    lengths, gains = lax.optimization_barrier((lengths, gains))
    group_start = lax.axis_index("seq") * length
    positions = group_start + jnp.arange(length, dtype=jnp.int32)
    begins = doc_starts(lengths, positions, batches, seq_len)
    at = jnp.arange(length, dtype=jnp.int32)
    block = min(256, length)
    low = jnp.maximum(begins - group_start + WINDOW, at[None, :] + 1) - (at // block * block)[None, :]
    low = low[:, None, :]

    gains = gains.transpose(1, 0, 2, 3).reshape(devices // fold, fold, 8, 128).sum(axis=1)
    gain_one = gains[:, 0].reshape(width)
    gain_two = gains[:, 1].reshape(width)
    attended, lse, kv_pad, unit_own = attend(
        seqs, group, query, key_value, low, block, unit_blocks, 2
    )
    middle, normed_b, group_d, w_units = branch_sum(
        seqs, chips, attended, wo_part, cot_rows, unit_own.reshape(group * share, -1),
        x_rows, gain_two[None], 3,
    )
    w_units = w_units.reshape(width, -1)
    d_middle, d_branch, mlp_gain_part, hidden, unit_part, unit_one = feed_forward(
        seqs, chips, batches, normed_b, w_units, wd_part, group_d, middle, cot_rows,
        gain_two[None], 4,
    )
    d_attended, layer_out, out_part, unit_two, _, down_in = branch_back(
        seqs, chips, batches, d_branch, wo_part, attended, middle, hidden, wd_part, unit_part,
        group_d, 5,
    )
    if not aligned:
        whole = lax.dynamic_update_slice_in_dim(
            jnp.zeros((width, width), jnp.bfloat16), out_part, member * span, 0
        )
        out_part = lax.psum(whole, "fsdp").reshape(seqs, group, share, width)
        out_part = lax.dynamic_slice_in_dim(out_part, member, 1, 1).reshape(seqs * share, width)
    input_grad, wq_grad, wk_grad, wv_grad, wo_grad, gain_tile, gate_grad, up_grad = attention_back(
        seqs, chips, block, query, kv_pad, low, lse, d_attended, unit_part, unit_one, unit_two,
        w_heads, group_a, x_rows, d_middle, gain_one[None], mlp_gain_part, out_part, 6,
    )
    down_grad = jnp.sum(down_in.astype(jnp.float32), axis=0)
    gain_grads = lax.dynamic_slice_in_dim(gain_tile[:2], lax.rem(device, fold) * share, share, 1)
    wide = jnp.float32
    return (
        layer_out.reshape(batches, piece, width),
        input_grad.reshape(batches, piece, width),
        gain_grads[0],
        wq_grad.astype(wide),
        wk_grad.astype(wide),
        wv_grad.astype(wide),
        wo_grad,
        gain_grads[1],
        gate_grad.astype(wide),
        up_grad.astype(wide),
        down_grad,
    )


def solution(mesh):
    spread = ("seq", "fsdp")
    tokens, rows, gains = P(None, spread, None), P(spread, None), P(spread)
    in_specs = (tokens, tokens, P(), gains, rows, rows, rows, rows, gains, rows, rows, rows)
    out_specs = (tokens, tokens, gains, rows, rows, rows, rows, gains, rows, rows, rows)
    return jax.shard_map(body, mesh=mesh, in_specs=in_specs, out_specs=out_specs, check_vma=False)
```

```python
import functools

import jax
import jax.numpy as jnp
from jax import lax
from jax.experimental import pallas as pl
from jax.experimental.pallas import tpu as pltpu
from jax.sharding import PartitionSpec as P

HEAD = 64
FF = 8192
WINDOW = 1024
PAIR = 128
TILE = 512
PARTS = 4
LOW = -1e30
EPS = 1e-05
MESH = pl.DeviceIdType.MESH
MIB = 2**20


def to_half(values):
    return values.astype(jnp.bfloat16)


def normalize(values, gain):
    return values * lax.rsqrt(jnp.mean(values * values, axis=-1, keepdims=True) + EPS) * gain


def contract_rows(left, right):
    return lax.dot_general(
        left, right, (((0,), (0,)), ((), ())), preferred_element_type=jnp.float32
    )


def dot_nt(left, right):
    return lax.dot_general(
        left, right, (((1,), (1,)), ((), ())), preferred_element_type=jnp.float32
    )


def dot_nn(left, right):
    return jnp.dot(left, right, preferred_element_type=jnp.float32)


def head_lanes(values, half):
    lane = lax.broadcasted_iota(jnp.int32, values.shape, 1)
    return jnp.where((lane >= HEAD) == (half == 1), values, jnp.zeros_like(values))


def masked_scores(k_rows, q_head, low):
    keys, block = k_rows.shape[0], q_head.shape[0]
    scores = dot_nt(k_rows, q_head)
    at = lax.broadcasted_iota(jnp.int32, (keys, block), 0)
    query = lax.broadcasted_iota(jnp.int32, (keys, block), 1)
    seen = (at >= low) & (at <= query + WINDOW)
    return jnp.where(seen, scores, LOW)


class Line:
    def __init__(self, chips):
        self.chips = chips
        self.own = lax.axis_index("fsdp")
        self.chip = self.own // 2
        self.core = lax.rem(self.own, 2)
        self.other = self.own + 1 - 2 * self.core
        self.has_left = self.chip > 0
        self.has_right = self.chip < chips - 1

    def greet(self):
        signal_group(self.other)
        pl.when(self.has_left)(lambda: signal_group(self.own - 2))
        pl.when(self.has_right)(lambda: signal_group(self.own + 2))
        return 1 + self.has_left.astype(jnp.int32) + self.has_right.astype(jnp.int32)


def signal_group(peer):
    barrier = pltpu.get_barrier_semaphore()
    pl.semaphore_signal(barrier, inc=1, device_id={"fsdp": peer}, device_id_type=MESH)


def signal_seq(peer):
    barrier = pltpu.get_barrier_semaphore()
    pl.semaphore_signal(barrier, inc=1, device_id={"seq": peer}, device_id_type=MESH)


def greet_group(group):
    own = lax.axis_index("fsdp")
    pl.loop(1, group)(lambda ahead: signal_group(lax.rem(own + ahead, group)))
    return group - 1


def greet_seq(seqs):
    own = lax.axis_index("seq")
    pl.loop(1, seqs)(lambda ahead: signal_seq(lax.rem(own + ahead, seqs)))
    return seqs - 1


def meet(count):
    pl.semaphore_wait(pltpu.get_barrier_semaphore(), count)


def rows_at(index, size):
    return pl.ds(pl.multiple_of(index * size, size), size)


class Spread:
    def __init__(self, line, first, buf, send, recv):
        self.line, self.first, self.buf, self.send, self.recv = line, first, buf, send, recv
        self.parts = recv.shape[1]
        self.size = first.shape[0] // self.parts

    def move(self, slot, part, way, peer, source=None):
        here = rows_at(part, self.size)
        return pltpu.make_async_remote_copy(
            src_ref=self.buf.at[slot, here] if source is None else source.at[here],
            dst_ref=self.buf.at[slot, here],
            send_sem=self.send.at[way, slot, part],
            recv_sem=self.recv.at[slot, part],
            device_id={"fsdp": peer},
            device_id_type=MESH,
        )

    def begin(self):
        line = self.line

        @pl.loop(0, self.parts)
        def _(part):
            pl.when(line.has_right)(
                lambda: self.move(line.own, part, 1, line.own + 2, self.first).start()
            )
            pl.when(line.has_left)(
                lambda: self.move(line.own, part, 0, line.own - 2, self.first).start()
            )
            self.move(line.own, part, 2, line.other, self.first).start()

    def relay_part(self, far, part):
        line = self.line

        @pl.when(line.chip - far >= 0)
        def _():
            slot = (line.chip - far) * 2 + line.core
            self.move(slot, part, 1, line.own).wait_recv()
            pl.when(line.has_right)(lambda: self.move(slot, part, 1, line.own + 2).start())
            self.move(slot, part, 2, line.other).start()

        @pl.when(line.chip + far < line.chips)
        def _():
            slot = (line.chip + far) * 2 + line.core
            self.move(slot, part, 0, line.own).wait_recv()
            pl.when(line.has_left)(lambda: self.move(slot, part, 0, line.own - 2).start())
            self.move(slot, part, 2, line.other).start()

    def relay(self, far):
        pl.loop(0, self.parts)(lambda part: self.relay_part(far, part))

    def across(self, slot):
        pl.loop(0, self.parts)(lambda part: self.move(slot, part, 2, self.line.own).wait_recv())

    def each(self, far, use):
        line = self.line

        @pl.loop(0, 4)
        def _(turn):
            side = lax.rem(turn, 2)
            over = turn // 2
            away = far - over
            source = line.chip + away * (2 * side - 1)
            valid = (away >= 0) & (away < line.chips) & (source >= 0) & (source < line.chips)
            valid = valid & ((side == 0) | (away > 0))

            @pl.when(valid)
            def _():
                slot = source * 2 + line.core + over * (1 - 2 * line.core)
                pl.when(over == 1)(lambda: self.across(slot))
                use(slot)

    def rest(self):
        pl.loop(0, self.line.chips)(lambda place: self.across(place * 2 + 1 - self.line.core))

    def sent(self):
        line = self.line

        @pl.loop(0, line.chips)
        def _(place):
            slot = place * 2 + line.core

            @pl.loop(0, self.parts)
            def _(part):
                self.move(slot, part, 2, line.other).wait_send()
                pl.when(line.has_right & (place <= line.chip))(
                    lambda: self.move(slot, part, 1, line.own + 2).wait_send()
                )
                pl.when(line.has_left & (place >= line.chip))(
                    lambda: self.move(slot, part, 0, line.own - 2).wait_send()
                )


class Reduce:
    def __init__(self, line, product, out, acc, cross_out, line_out, cross_in, line_in, send, recv):
        self.line, self.product, self.out, self.acc = line, product, out, acc
        self.cross_out, self.line_out, self.cross_in, self.line_in = cross_out, line_out, cross_in, line_in
        self.send, self.recv = send, recv
        self.tiles = line_out.shape[2] // TILE

    @staticmethod
    def scratch(chips, rows, width):
        part = pltpu.VMEM((chips, rows, width), jnp.bfloat16)
        return [
            pltpu.VMEM((rows, TILE), jnp.float32),
            pltpu.VMEM((2, rows, width), jnp.bfloat16),
            part,
            part,
            pltpu.VMEM((chips + 1, rows, width), jnp.bfloat16),
            pltpu.SemaphoreType.DMA((2, chips, width // TILE)),
            pltpu.SemaphoreType.DMA((2, chips + 1, width // TILE)),
        ]

    def cross(self, side, place, tile):
        here = rows_at(tile, TILE)
        return pltpu.make_async_remote_copy(
            src_ref=self.cross_out.at[side, :, here],
            dst_ref=self.cross_in.at[place, :, here],
            send_sem=self.send.at[0, place, tile],
            recv_sem=self.recv.at[0, place, tile],
            device_id={"fsdp": self.line.other},
            device_id_type=MESH,
        )

    def along(self, place, landing, tile, peer):
        here = rows_at(tile, TILE)
        return pltpu.make_async_remote_copy(
            src_ref=self.line_out.at[place, :, here],
            dst_ref=self.line_in.at[landing, :, here],
            send_sem=self.send.at[1, place, tile],
            recv_sem=self.recv.at[1, landing, tile],
            device_id={"fsdp": peer},
            device_id_type=MESH,
        )

    def where(self, away, side):
        line = self.line
        rightward = (line.chips - 1 - line.chip >= line.chip) == (side == 0)
        place = line.chip + jnp.where(rightward, away, -away)
        valid = (place >= 0) & (place < line.chips) & ((away > 0) | (side == 0))
        return valid, place, rightward

    def level(self, away, also):
        @pl.loop(0, 2)
        def _(side):
            valid, place, _ = self.where(away, side)

            @pl.when(valid)
            def _():
                @pl.loop(0, self.tiles)
                def _(tile):
                    got = self.product(place * 2 + 1 - self.line.core, tile)
                    self.cross_out[side, :, rows_at(tile, TILE)] = to_half(got)
                    self.cross(side, place, tile).start()

        @pl.loop(0, self.tiles)
        def _(tile):
            @pl.loop(0, 2)
            def _(side):
                valid, place, rightward = self.where(away, side)
                pl.when(valid)(lambda: self.close(away, side, place, rightward, tile))

            also(tile)

    def close(self, away, side, place, rightward, tile):
        line, acc = self.line, self.acc
        here = rows_at(tile, TILE)
        upstream = (rightward & line.has_left) | (jnp.logical_not(rightward) & line.has_right)
        acc[...] = self.product(place * 2 + line.core, tile)
        self.cross(side, place, tile).wait()
        acc[...] += self.cross_in[place, :, here].astype(jnp.float32)

        @pl.when(away > 0)
        def _():
            @pl.when(upstream)
            def _():
                self.along(place, place, tile, line.own).wait_recv()
                self.line_out[place, :, here] = to_half(
                    acc[...] + self.line_in[place, :, here].astype(jnp.float32)
                )

            @pl.when(jnp.logical_not(upstream))
            def _():
                self.line_out[place, :, here] = to_half(acc[...])

            @pl.when(rightward)
            def _():
                self.along(place, place, tile, line.own + 2).start()

            @pl.when(jnp.logical_not(rightward))
            def _():
                landing = jnp.where(away == 1, line.chips, place)
                self.along(place, landing, tile, line.own - 2).start()

        @pl.when(away == 0)
        def _():
            self.out[:, here] = acc[...]

            @pl.when(line.has_left)
            def _():
                self.along(place, place, tile, line.own).wait_recv()
                self.out[:, here] += self.line_in[place, :, here].astype(jnp.float32)

            @pl.when(line.has_right)
            def _():
                self.along(place, line.chips, tile, line.own).wait_recv()
                self.out[:, here] += self.line_in[line.chips, :, here].astype(jnp.float32)

    def sent(self):
        @pl.loop(0, self.line.chips)
        def _(place):
            @pl.when(place != self.line.chip)
            def _():
                pl.loop(0, self.tiles)(
                    lambda tile: self.along(place, place, tile, self.line.own).wait_send()
                )


class Swap:
    def __init__(self, group, source, target, send, recv, keep):
        self.group, self.source, self.target = group, source, target
        self.send, self.recv, self.keep = send, recv, keep
        self.own = lax.axis_index("fsdp")

    def move(self, peer, source):
        return pltpu.make_async_remote_copy(
            src_ref=self.source.at[peer],
            dst_ref=self.target.at[source],
            send_sem=self.send.at[peer],
            recv_sem=self.recv.at[source],
            device_id={"fsdp": peer},
            device_id_type=MESH,
        )

    def kept(self):
        return pltpu.make_async_copy(self.source.at[self.own], self.target.at[self.own], self.keep)

    def begin(self):
        self.kept().start()
        pl.loop(1, self.group)(
            lambda ahead: self.move(lax.rem(self.own + ahead, self.group), self.own).start()
        )

    def end(self):
        self.kept().wait()

        @pl.loop(1, self.group)
        def _(ahead):
            peer = lax.rem(self.own + ahead, self.group)
            self.move(peer, peer).wait_recv()
            self.move(peer, self.own).wait_send()


class Share:
    def __init__(self, seqs, source, target, send, recv, keep):
        self.seqs, self.source, self.target = seqs, source, target
        self.send, self.recv, self.keep = send, recv, keep
        self.own = lax.axis_index("seq")
        self.half = source.shape[0] // 2

    def move(self, peer, place):
        return pltpu.make_async_remote_copy(
            src_ref=self.source,
            dst_ref=self.target.at[place],
            send_sem=self.send.at[peer, 0],
            recv_sem=self.recv.at[place, 0],
            device_id={"seq": peer},
            device_id_type=MESH,
        )

    def relay(self, peer, place, part):
        here = pl.ds(part * self.half, self.half)
        return pltpu.make_async_remote_copy(
            src_ref=self.target.at[place, here],
            dst_ref=self.target.at[place, here],
            send_sem=self.send.at[peer, 1],
            recv_sem=self.recv.at[place, part],
            device_id={"seq": peer},
            device_id_type=MESH,
        )

    def near(self):
        one = self.own + 1 - 2 * lax.rem(self.own, 2)
        two = lax.rem(self.own + 2, 4)
        return one, two, lax.rem(one + 2, 4)

    def kept(self):
        return pltpu.make_async_copy(self.source, self.target.at[self.own], self.keep)

    def begin(self):
        self.kept().start()
        if self.seqs == 4:
            one, two, _ = self.near()
            self.move(one, self.own).start()
            self.move(two, self.own).start()
        else:
            pl.loop(1, self.seqs)(
                lambda ahead: self.move(lax.rem(self.own + ahead, self.seqs), self.own).start()
            )

    def pass_on(self):
        if self.seqs == 4:
            one, two, _ = self.near()
            self.move(one, one).wait_recv()
            self.relay(two, one, 0).start()
            self.move(two, two).wait_recv()
            self.relay(one, two, 1).start()

    def end(self):
        self.kept().wait()
        if self.seqs == 4:
            one, two, far = self.near()
            self.relay(two, far, 0).wait_recv()
            self.relay(one, far, 1).wait_recv()
            self.move(one, self.own).wait_send()
            self.move(two, self.own).wait_send()
            self.relay(two, one, 0).wait_send()
            self.relay(one, two, 1).wait_send()
        else:

            @pl.loop(1, self.seqs)
            def _(ahead):
                peer = lax.rem(self.own + ahead, self.seqs)
                self.move(peer, peer).wait_recv()
                self.move(peer, self.own).wait_send()


class ToSeq:
    def __init__(self, seqs, source, target, send, recv, first=0):
        self.seqs, self.source, self.target, self.send, self.recv = seqs, source, target, send, recv
        self.own = lax.axis_index("seq")
        self.first = first

    def move(self, peer, place):
        run = self.source.shape[0] // self.seqs
        begin = pl.multiple_of(peer * run + self.first, 16)
        return pltpu.make_async_remote_copy(
            src_ref=self.source.at[pl.ds(begin, self.target.shape[1])],
            dst_ref=self.target.at[place],
            send_sem=self.send.at[peer],
            recv_sem=self.recv.at[place],
            device_id={"seq": peer},
            device_id_type=MESH,
        )

    def begin(self):
        pl.loop(1, self.seqs)(
            lambda ahead: self.move(lax.rem(self.own + ahead, self.seqs), self.own).start()
        )

    def arrived(self):
        @pl.loop(1, self.seqs)
        def _(ahead):
            peer = lax.rem(self.own + ahead, self.seqs)
            self.move(peer, peer).wait_recv()

    def sent(self):
        @pl.loop(1, self.seqs)
        def _(ahead):
            peer = lax.rem(self.own + ahead, self.seqs)
            self.move(peer, self.own).wait_send()

    def end(self):
        self.arrived()
        self.sent()


VMEM_SPEC = pl.BlockSpec(memory_space=pltpu.VMEM)
ANY_SPEC = pl.BlockSpec(memory_space=pl.ANY)


def comm_params(collective, mib=58):
    return pltpu.CompilerParams(
        collective_id=collective, has_side_effects=True, vmem_limit_bytes=mib * MIB
    )


def cost(flops, local, remote):
    return pl.CostEstimate(
        flops=flops, bytes_accessed=local, transcendentals=0, remote_bytes_transferred=remote
    )


def sems(*shape):
    return pltpu.SemaphoreType.DMA(shape)


def left_rows(a_ref, slot, rows):
    if len(a_ref.shape) == 2:
        return a_ref[rows_at(slot, rows), :]
    piece = rows // a_ref.shape[0]
    return jnp.concatenate(
        [a_ref[batch, rows_at(slot, piece), :] for batch in range(a_ref.shape[0])], axis=0
    )


def norm_back(rows, v_ref, e_ref, gain_ref, gain_acc, put):
    @pl.loop(0, rows // 32)
    def _(chunk):
        here = rows_at(chunk, 32)
        values = v_ref[here, :].astype(jnp.float32)
        error = e_ref[here, :]
        rate = lax.rsqrt(jnp.mean(values * values, axis=-1, keepdims=True) + EPS)
        unit = values * rate
        product = error * unit
        gain = gain_ref[0:1, :]
        mean = jnp.mean(product * gain, axis=-1, keepdims=True)
        gain_acc[...] += (product[0:8] + product[8:16]) + (product[16:24] + product[24:32])
        put(here, rate * (gain * error - unit * mean))


def add_from_seq(seqs, own_rows, got, here):
    seq = lax.axis_index("seq")
    added = own_rows.astype(jnp.float32)
    for place in range(seqs):
        piece = got[place, here, :].astype(jnp.float32)
        added = added + jnp.where(place == seq, 0.0, piece)
    return added


def column_parts(seqs, group, share, span):
    size = HEAD if share == HEAD else span
    parts = []
    for member in range(group):
        for run in range(span // size):
            home = (run * group + member) * size
            parts.append((member, run * size, home, size))
    return parts


def start_kernel(
    seqs, chips, batches, tile_ref, x_ref, wq_ref, wk_ref, wv_ref, gate_hbm, up_hbm,
    g_ref, q_ref, kv_ref, gains_ref, w_out_ref, units_ref,
    gate, up, units, unit_sem,
    blocks_ref, buf, normed, gain, gains, w, send, recv, keep, swap_send, share_send, w_recv,
    tile_send, tile_across, tile_recv, tile_back, w_keep, gain_keep,
):
    line = Line(chips)
    group = 2 * chips
    seq = lax.axis_index("seq")
    own = line.own
    share = blocks_ref.shape[1]
    piece = x_ref.shape[0] // batches
    span = q_ref.shape[2]
    width = x_ref.shape[1]
    per = 128 * seqs * group // width
    unit_loads = [
        pltpu.make_async_copy(gate_hbm, gate, unit_sem.at[0]),
        pltpu.make_async_copy(up_hbm, up, unit_sem.at[1]),
    ]
    for item in unit_loads:
        item.start()
    for index, source in enumerate((wq_ref, wk_ref, wv_ref)):
        for member, first, home, size in column_parts(seqs, group, share, span):
            first = first + index * span
            blocks_ref[member, :, first : first + size] = source[:, home : home + size]
    meet(greet_group(group) + greet_seq(seqs))

    def block_at(run, member):
        return w.at[rows_at(run * group + member, share)]

    def block_swap(peer, member):
        return pltpu.make_async_remote_copy(
            src_ref=blocks_ref.at[peer],
            dst_ref=block_at(seq, member),
            send_sem=swap_send.at[peer],
            recv_sem=w_recv.at[seq, member],
            device_id={"fsdp": peer},
            device_id_type=MESH,
        )

    def block_share(run, member, peer):
        return pltpu.make_async_remote_copy(
            src_ref=block_at(run, member),
            dst_ref=block_at(run, member),
            send_sem=share_send.at[peer, member],
            recv_sem=w_recv.at[run, member],
            device_id={"seq": peer},
            device_id_type=MESH,
        )

    def tile_to_seq(peer, place):
        return pltpu.make_async_remote_copy(
            src_ref=tile_ref.at[0],
            dst_ref=gains.at[own, place],
            send_sem=tile_send.at[peer],
            recv_sem=tile_recv.at[place],
            device_id={"seq": peer},
            device_id_type=MESH,
        )

    def tiles_to_group(peer, member):
        return pltpu.make_async_remote_copy(
            src_ref=gains.at[member],
            dst_ref=gains.at[member],
            send_sem=tile_across.at[peer],
            recv_sem=tile_back.at[member],
            device_id={"fsdp": peer},
            device_id_type=MESH,
        )

    def others(count, me, act):
        pl.loop(1, count)(lambda ahead: act(lax.rem(me + ahead, count)))

    others(seqs, seq, lambda peer: tile_to_seq(peer, seq).start())
    others(group, own, lambda peer: block_swap(peer, own).start())
    spread = Spread(line, x_ref, buf, send, recv)
    spread.begin()
    gains[own, seq] = tile_ref[0]
    w[rows_at(seq * group + own, share), :] = blocks_ref[own]
    others(seqs, seq, lambda peer: block_share(seq, own, peer).start())
    buf[own] = x_ref[...]
    others(seqs, seq, lambda peer: tile_to_seq(peer, peer).wait_recv())
    others(group, own, lambda peer: tiles_to_group(peer, own).start())
    for item in unit_loads:
        item.wait()
    cell = units.shape[2] // 2 // seqs
    for member in range(group):
        for run in range(seqs):
            home = (run * group + member) * cell
            for index, source in enumerate((gate, up)):
                first = (index * seqs + run) * cell
                units[member, :, first : first + cell] = source[:, home : home + cell]
    units_kept = pltpu.make_async_copy(units, units_ref, unit_sem.at[2])
    units_kept.start()

    def pass_block(member):
        block_swap(member, member).wait_recv()
        others(seqs, seq, lambda peer: block_share(seq, member, peer).start())

    others(group, own, pass_block)
    others(group, own, lambda peer: tiles_to_group(peer, peer).wait_recv())
    for column in range(width // 128):
        total = 0.0
        for place in range(column * per, (column + 1) * per):
            total = total + gains[place % group, place // group, 0:1, :]
        gain[0:1, column * 128 : (column + 1) * 128] = total

    def kept(slot, batch):
        return pltpu.make_async_copy(
            normed.at[slot, pl.ds(batch * piece, piece)],
            g_ref.at[batch, rows_at(slot, piece)],
            keep.at[slot, batch],
        )

    def use(slot):
        @pl.loop(0, x_ref.shape[0] // 64)
        def _(chunk):
            rows = rows_at(chunk, 64)
            values = buf[slot, rows, :].astype(jnp.float32)
            normed[slot, rows, :] = to_half(normalize(values, gain[0:1, :]))

        for batch in range(batches):
            kept(slot, batch).start()
        rows = rows_at(slot, piece)
        got = to_half(dot_nn(normed[slot], w[...]))
        for batch in range(batches):
            mine = got[batch * piece : (batch + 1) * piece]
            q_ref[batch, rows, :] = mine[:, :span]
            kv_ref[batch, rows, :] = mine[:, span:]

    pl.loop(1, chips - 1)(spread.relay)

    def have_block(run, member):
        block_share(run, member, seq).wait_recv()

    others(seqs, seq, lambda run: pl.loop(0, group)(lambda member: have_block(run, member)))
    w_kept = pltpu.make_async_copy(w, w_out_ref, w_keep)
    w_kept.start()
    gains_kept = pltpu.make_async_copy(gains, gains_ref, gain_keep)
    gains_kept.start()

    pl.loop(0, chips - 1)(lambda far: spread.each(far, use))
    spread.relay(chips - 1)
    spread.each(chips - 1, use)
    spread.each(chips, use)
    spread.sent()
    others(seqs, seq, lambda peer: tile_to_seq(peer, seq).wait_send())
    others(group, own, lambda peer: block_swap(peer, own).wait_send())
    others(group, own, lambda peer: tiles_to_group(peer, own).wait_send())
    others(
        seqs,
        seq,
        lambda peer: pl.loop(0, group)(lambda member: block_share(seq, member, peer).wait_send()),
    )
    w_kept.wait()
    gains_kept.wait()
    units_kept.wait()

    @pl.loop(0, group)
    def _(slot):
        for batch in range(batches):
            kept(slot, batch).wait()


def start(seqs, chips, batches, tile, x, weights, unit_weights, collective):
    rows, width = x.shape
    group = 2 * chips
    length = group * rows // batches
    share = weights[0].shape[0]
    span = width // group
    cols = 3 * span
    wide = unit_weights[0].shape[1]
    half = jnp.bfloat16
    return pl.pallas_call(
        functools.partial(start_kernel, seqs, chips, batches),
        out_shape=[
            jax.ShapeDtypeStruct((batches, length, width), half),
            jax.ShapeDtypeStruct((batches, length, span), half),
            jax.ShapeDtypeStruct((batches, length, 2 * span), half),
            jax.ShapeDtypeStruct((group, seqs, 8, 128), jnp.float32),
            jax.ShapeDtypeStruct((width, cols), half),
            jax.ShapeDtypeStruct((group, share, 2 * wide // group), half),
        ],
        in_specs=[VMEM_SPEC] * 5 + [ANY_SPEC] * 2,
        out_specs=[ANY_SPEC, VMEM_SPEC, VMEM_SPEC, ANY_SPEC, ANY_SPEC, ANY_SPEC],
        scratch_shapes=[
            pltpu.VMEM((share, wide), half),
            pltpu.VMEM((share, wide), half),
            pltpu.VMEM((group, share, 2 * wide // group), half),
            sems(3),
            pltpu.VMEM((group, share, cols), half),
            pltpu.VMEM((group, rows, width), half),
            pltpu.VMEM((group, rows, width), half),
            pltpu.VMEM((8, width), jnp.float32),
            pltpu.VMEM((group, seqs, 8, 128), jnp.float32),
            pltpu.VMEM((width, cols), half),
            sems(3, group, PARTS),
            sems(group, PARTS),
            sems(group, batches),
            sems(group),
            sems(seqs, group),
            sems(seqs, group),
            sems(seqs),
            sems(group),
            sems(seqs),
            sems(group),
            pltpu.SemaphoreType.DMA,
            pltpu.SemaphoreType.DMA,
        ],
        compiler_params=comm_params(collective),
        cost_estimate=cost(2 * group * rows * width * cols, 200 * MIB, group * rows * width * 2),
        name="start",
    )(tile, x, *weights, *unit_weights)


def attend_kernel(
    seqs, group, block, q_ref, kv_ref, low_ref, units_ref, out_ref, lse_ref, pad_ref, own_units_ref,
    pad, vt_ref, halo_send, halo_recv, pad_keep, swap_send, swap_recv, swap_keep,
):
    seq = lax.axis_index("seq")
    batches, length, span = q_ref.shape
    has_left, has_right = seq > 0, seq < seqs - 1
    pl.when(has_left)(lambda: signal_seq(seq - 1))
    pl.when(has_right)(lambda: signal_seq(seq + 1))
    meet(greet_group(group) + has_left.astype(jnp.int32) + has_right.astype(jnp.int32))

    steps, need = length // block, WINDOW // block

    def halo(batch, step, peer):
        return pltpu.make_async_remote_copy(
            src_ref=kv_ref.at[batch, rows_at(step + steps - need, block)],
            dst_ref=pad.at[batch, rows_at(step, block)],
            send_sem=halo_send.at[batch, step],
            recv_sem=halo_recv.at[batch, step],
            device_id={"seq": peer},
            device_id_type=MESH,
        )

    def send_halo(turn):
        batch, step = turn // need, need - 1 - lax.rem(turn, need)
        pl.when(has_right)(lambda: halo(batch, step, seq + 1).start())

    def halo_sent(turn):
        batch, step = turn // need, need - 1 - lax.rem(turn, need)
        pl.when(has_right)(lambda: halo(batch, step, seq + 1).wait_send())

    send_halo(0)
    send_halo(1)
    swap = Swap(group, units_ref, own_units_ref, swap_send, swap_recv, swap_keep)
    swap.begin()
    pad[:, WINDOW:, :] = kv_ref[...]

    @pl.when(jnp.logical_not(has_left))
    def _():
        pad[:, :WINDOW, :] = jnp.zeros((batches, WINDOW, 2 * span), jnp.bfloat16)

    def kept(batch):
        return pltpu.make_async_copy(pad.at[batch], pad_ref.at[batch], pad_keep.at[batch])

    vt = vt_ref
    for batch in range(batches):
        vt[:, WINDOW:] = pad[batch, WINDOW:, span:].T

        @pl.loop(0, steps)
        def _(turn, batch=batch):
            step = steps - 1 - turn

            @pl.when(step < need)
            def _():
                rows = rows_at(step, block)
                pl.when(has_left)(lambda: halo(batch, step, seq).wait_recv())
                vt[:, rows] = pad[batch, rows, span:].T
                place = batch * need + need - 1 - step
                halo_sent(place)
                pl.when(place + 2 < batches * need)(lambda: send_halo(place + 2))

            begin = pl.multiple_of(step * block, block)
            keys = pl.ds(begin, block + WINDOW)
            rows = pl.ds(begin, block)
            low = low_ref[batch, :, rows]
            for pair in range(span // PAIR):
                lanes = slice(pair * PAIR, (pair + 1) * PAIR)
                q_pair = q_ref[batch, rows, lanes] * jnp.asarray(HEAD**-0.5, jnp.bfloat16)
                k_rows = pad[batch, keys, lanes]
                values = vt[lanes, keys]
                mixed = []
                for half in range(2):
                    scores = masked_scores(k_rows, head_lanes(q_pair, half), low)
                    top = jnp.max(scores, axis=0, keepdims=True)
                    expo = jnp.exp(scores - top)
                    total = jnp.sum(expo, axis=0, keepdims=True)
                    mixed.append(dot_nn(values, to_half(expo)) / total)
                    row = pair * 2 + half
                    lse_ref[batch, row : row + 1, rows] = top + jnp.log(total)
                lane = lax.broadcasted_iota(jnp.int32, mixed[0].shape, 0)
                out_ref[batch, rows, lanes] = to_half(jnp.where(lane < HEAD, mixed[0], mixed[1]).T)

    for batch in range(batches):
        kept(batch).start()
    swap.end()
    for batch in range(batches):
        kept(batch).wait()


def attend(seqs, group, query, key_value, low, block, units, collective):
    batches, length, span = query.shape
    padded = length + WINDOW
    heads = span // HEAD
    half = jnp.bfloat16
    return pl.pallas_call(
        functools.partial(attend_kernel, seqs, group, block),
        in_specs=[VMEM_SPEC, VMEM_SPEC, VMEM_SPEC, ANY_SPEC],
        out_specs=[VMEM_SPEC, VMEM_SPEC, ANY_SPEC, ANY_SPEC],
        out_shape=[
            jax.ShapeDtypeStruct((batches, length, span), half),
            jax.ShapeDtypeStruct((batches, heads, length), jnp.float32),
            jax.ShapeDtypeStruct((batches, padded, 2 * span), half),
            jax.ShapeDtypeStruct(units.shape, half),
        ],
        scratch_shapes=[
            pltpu.VMEM((batches, padded, 2 * span), half),
            pltpu.VMEM((span, padded), half),
            sems(batches, WINDOW // block),
            sems(batches, WINDOW // block),
            sems(batches),
            sems(group),
            sems(group),
            pltpu.SemaphoreType.DMA,
        ],
        compiler_params=comm_params(collective),
        cost_estimate=cost(
            8 * batches * length * span * (WINDOW + block), 150 * MIB, units.size * 2
        ),
        name="attend",
    )(query, key_value, low, units)


def branch_kernel(
    seqs, chips, a_ref, w_ref, d_ref, units_ref, x_ref, gain_ref, middle_ref, normed_ref, gd_ref, w_units_ref,
    out_ref, acc, cross_out, line_out, cross_in, line_in, sum_send, sum_recv,
    send, recv, d_keep, share_send, share_recv, share_keep,
):
    line = Line(chips)
    rows = out_ref.shape[0]

    def product(slot, tile):
        return dot_nn(left_rows(a_ref, slot, rows), w_ref[:, rows_at(tile, TILE)])

    meet(line.greet() + greet_seq(seqs))
    reduce = Reduce(
        line, product, out_ref, acc, cross_out, line_out, cross_in, line_in, sum_send, sum_recv
    )
    spread = Spread(line, d_ref, gd_ref, send, recv)
    units = Share(seqs, units_ref, w_units_ref, share_send, share_recv, share_keep)
    d_kept = pltpu.make_async_copy(d_ref, gd_ref.at[line.own], d_keep)
    units.begin()
    spread.begin()
    d_kept.start()

    @pl.loop(0, chips)
    def _(step):
        def also(tile):
            pl.when(step < chips - 1)(lambda: spread.relay_part(step + 1, tile))

        reduce.level(chips - 1 - step, also)
        pl.when(step == chips - 2)(units.pass_on)

    @pl.loop(0, rows // 32)
    def _(chunk):
        here = rows_at(chunk, 32)
        middle = x_ref[here, :].astype(jnp.float32) + out_ref[here, :]
        middle_ref[here, :] = middle
        normed_ref[here, :] = to_half(normalize(middle, gain_ref[0:1, :]))

    spread.rest()
    spread.sent()
    reduce.sent()
    d_kept.wait()
    units.end()


def branch_sum(seqs, chips, a, w, d_rows, units, x, gain, collective):
    rows, width = d_rows.shape
    group = 2 * chips
    half = jnp.bfloat16
    return pl.pallas_call(
        functools.partial(branch_kernel, seqs, chips),
        out_shape=[
            jax.ShapeDtypeStruct((rows, width), jnp.float32),
            jax.ShapeDtypeStruct((rows, width), half),
            jax.ShapeDtypeStruct((group, rows, width), half),
            jax.ShapeDtypeStruct((seqs,) + units.shape, half),
        ],
        in_specs=[VMEM_SPEC, VMEM_SPEC, ANY_SPEC, ANY_SPEC, VMEM_SPEC, VMEM_SPEC],
        out_specs=[VMEM_SPEC, VMEM_SPEC, ANY_SPEC, ANY_SPEC],
        scratch_shapes=[pltpu.VMEM((rows, width), jnp.float32)]
        + Reduce.scratch(chips, rows, width)
        + [sems(3, group, PARTS), sems(group, PARTS), pltpu.SemaphoreType.DMA]
        + [sems(seqs, 2), sems(seqs, 2), pltpu.SemaphoreType.DMA],
        compiler_params=comm_params(collective),
        cost_estimate=cost(
            2 * group * rows * width * w.shape[0], 250 * MIB, 3 * group * rows * width * 2
        ),
        name="branch_sum",
    )(a, w, d_rows, units, x, gain)


class PairReduce:
    def __init__(self, line, product, out, acc, keep, cross_out, cross_in, line_out, line_in, send, recv):
        self.line, self.product, self.out, self.acc, self.keep = line, product, out, acc, keep
        self.cross_out, self.cross_in, self.line_out, self.line_in = cross_out, cross_in, line_out, line_in
        self.send, self.recv = send, recv
        self.tiles = keep.shape[1] // TILE

    @staticmethod
    def scratch(chips, piece, width):
        half = jnp.bfloat16
        return [
            pltpu.VMEM((piece, width), half),
            pltpu.VMEM((2, piece, width), half),
            pltpu.VMEM((2, piece, width), half),
            pltpu.VMEM((chips + 1, piece, width), half),
            pltpu.SemaphoreType.DMA((3, width // TILE)),
            pltpu.SemaphoreType.DMA((chips + 3, width // TILE)),
        ]

    def cross(self, parity, tile):
        here = rows_at(tile, TILE)
        return pltpu.make_async_remote_copy(
            src_ref=self.cross_out.at[:, here],
            dst_ref=self.cross_in.at[parity, :, here],
            send_sem=self.send.at[0, tile],
            recv_sem=self.recv.at[self.line.chips + 1 + parity, tile],
            device_id={"fsdp": self.line.other},
            device_id_type=MESH,
        )

    def along(self, parity, landing, tile, peer):
        here = rows_at(tile, TILE)
        return pltpu.make_async_remote_copy(
            src_ref=self.line_out.at[parity, :, here],
            dst_ref=self.line_in.at[landing, :, here],
            send_sem=self.send.at[1 + parity, tile],
            recv_sem=self.recv.at[landing, tile],
            device_id={"fsdp": peer},
            device_id_type=MESH,
        )

    def steps(self):
        return 2 * self.line.chips - 1

    def step(self, step):
        line, keep = self.line, self.keep
        piece = keep.shape[0]
        right_side = line.chips - 1 - line.chip
        away = line.chips - 1 - step // 2
        second = lax.rem(step, 2)
        rightward = (right_side >= line.chip) == (second == 0)
        place = line.chip + jnp.where(rightward, away, -away)
        longer = jnp.maximum(right_side, line.chip)
        shorter = jnp.minimum(right_side, line.chip)
        count = longer - away + jnp.maximum(shorter - away, 0) + second
        parity = lax.rem(count + 2 * line.chips, 2)
        upstream = (rightward & line.has_left) | (jnp.logical_not(rightward) & line.has_right)

        @pl.when((place >= 0) & (place < line.chips))
        def _():
            wide = self.acc.shape[1]

            @pl.loop(0, keep.shape[1] // wide)
            def _(tile):
                here = rows_at(tile, wide)
                self.acc[...] = self.product(place, here)
                self.cross_out[:, here] = to_half(self.acc[rows_at(1 - line.core, piece), :])
                keep[:, here] = self.acc[rows_at(line.core, piece), :]
                for piece_of in range(wide // TILE):
                    self.cross(parity, tile * (wide // TILE) + piece_of).start()

            @pl.loop(0, self.tiles)
            def _(tile):
                here = rows_at(tile, TILE)
                self.cross(parity, tile).wait()
                keep[:, here] += self.cross_in[parity, :, here].astype(jnp.float32)

                @pl.when(away > 0)
                def _():
                    pl.when(count >= 2)(
                        lambda: self.along(parity, place, tile, line.own).wait_send()
                    )

                    @pl.when(upstream)
                    def _():
                        self.along(parity, place, tile, line.own).wait_recv()
                        self.line_out[parity, :, here] = to_half(
                            keep[:, here] + self.line_in[place, :, here].astype(jnp.float32)
                        )

                    @pl.when(jnp.logical_not(upstream))
                    def _():
                        self.line_out[parity, :, here] = to_half(keep[:, here])

                    @pl.when(rightward)
                    def _():
                        self.along(parity, place, tile, line.own + 2).start()

                    @pl.when(jnp.logical_not(rightward))
                    def _():
                        landing = jnp.where(away == 1, line.chips, place)
                        self.along(parity, landing, tile, line.own - 2).start()

                @pl.when(away == 0)
                def _():
                    self.out[:, here] = keep[:, here]

                    @pl.when(line.has_left)
                    def _():
                        self.along(parity, place, tile, line.own).wait_recv()
                        self.out[:, here] += self.line_in[place, :, here].astype(jnp.float32)

                    @pl.when(line.has_right)
                    def _():
                        self.along(parity, line.chips, tile, line.own).wait_recv()
                        self.out[:, here] += self.line_in[line.chips, :, here].astype(jnp.float32)

    def sent(self):
        for count in range(max(self.line.chips - 3, 0), self.line.chips - 1):
            pl.loop(0, self.tiles)(
                lambda tile, parity=count % 2: self.along(parity, 0, tile, self.line.own).wait_send()
            )


def feed_kernel(
    seqs, chips, batches, x_ref, w_hbm, wd_hbm, gd_hbm, v_ref, cot_ref, gain_ref,
    dm_ref, db_ref, gain_grad_ref, hidden_hbm, grad_hbm, grad_in, branch_hbm,
    buf, d_buf, h_buf, w_ref, wd_ref, d_ref, tiles, totals, acc, keep,
    load, d_sem, h_sem, tile_sem, send, recv, part_send, part_recv,
    branch_send, branch_recv, branch_keep, *sums,
):
    line = Line(chips)
    rows, width = x_ref.shape
    piece = rows // batches
    pair = 2 * piece
    units = wd_ref.shape[0]
    part = min(units, 2 * TILE)
    block = tiles.shape[1]
    loads = [
        pltpu.make_async_copy(w_hbm, w_ref, load.at[0]),
        pltpu.make_async_copy(wd_hbm, wd_ref, load.at[1]),
    ]
    for item in loads:
        item.start()
    meet(line.greet() + greet_seq(seqs))
    spreads = [
        Spread(
            line,
            x_ref.at[pl.ds(batch * piece, piece)],
            buf.at[batch],
            send.at[batch],
            recv.at[batch],
        )
        for batch in range(batches)
    ]
    spreads[0].begin()
    for batch in range(batches):
        buf[batch, line.own] = x_ref[batch * piece : (batch + 1) * piece, :]

    def fetch(batch, place, side):
        return [
            pltpu.make_async_copy(
                gd_hbm.at[place * 2 + core, pl.ds(batch * piece, piece)],
                d_buf.at[side, pl.ds(core * piece, piece)],
                d_sem.at[side, core],
            )
            for core in range(2)
        ]

    def stored(batch, place):
        return [
            pltpu.make_async_copy(
                h_buf.at[pl.ds(core * piece, piece)],
                hidden_hbm.at[
                    pl.ds(pl.multiple_of((place * 2 + core) * rows + batch * piece, piece), piece)
                ],
                h_sem.at[core],
            )
            for core in range(2)
        ]

    def sides(far, act):
        @pl.loop(0, 2)
        def _(side):
            place = line.chip + far * (2 * side - 1)
            valid = (place >= 0) & (place < chips) & ((side == 0) | (far > 0))
            pl.when(valid)(lambda: act(place, side))

    def take(batch, far):
        def begin(place, side):
            for item in fetch(batch, place, side):
                item.start()

        sides(far, begin)
        pl.when(far > 0)(lambda: spreads[batch].relay(far))

    def compute(batch, far):
        def act(place, side):
            spreads[batch].across(place * 2 + 1 - line.core)
            for item in fetch(batch, place, side):
                item.wait()

            def free():
                for item in stored(batch, place):
                    item.wait()

            if batch:
                free()
            else:
                pl.when((far > 0) | (side > 0))(free)
            there = rows_at(place, pair)

            @pl.loop(0, units // part)
            def _(tile):
                first = rows_at(tile, part)
                second = rows_at(units // part + tile, part)
                values = buf[batch, pl.ds(place * 2, 2), :, :].reshape(pair, width)
                gate = dot_nn(values, w_ref[:, first])
                up = dot_nn(values, w_ref[:, second])
                d_hidden = dot_nt(d_buf[side], wd_ref[first, :])
                sigma = jax.nn.sigmoid(gate)
                swish = gate * sigma
                h_buf[:, first] = to_half(swish * up)
                slope = sigma * (1.0 + gate * (1.0 - sigma))
                d_ref[batch, there, first] = to_half(d_hidden * up * slope)
                d_ref[batch, there, second] = to_half(d_hidden * swish)

            for item in stored(batch, place):
                item.start()

        sides(far, act)

    def product(batch):
        def get(place, here):
            return dot_nt(d_ref[batch, rows_at(place, pair), :], w_ref[here, :])

        return get

    reduces = [
        PairReduce(line, product(batch), totals.at[batch], acc, keep, *sums[6 * batch : 6 * batch + 6])
        for batch in range(batches)
    ]

    count = width // block
    seq = lax.axis_index("seq")

    def tile_at(turn):
        early = turn < seqs - 1
        late = turn - (seqs - 1)
        dest = lax.rem(seq + jnp.where(early, turn + 1, late), seqs)
        return dest, dest * 2 + jnp.where(early | (late == 0), 0, 1)

    def grad_stored(turn):
        slot = lax.rem(turn, 2)
        return pltpu.make_async_copy(
            tiles.at[slot], grad_hbm.at[rows_at(tile_at(turn)[1], block)], tile_sem.at[slot]
        )

    parts = ToSeq(seqs, grad_hbm, grad_in, part_send, part_recv)

    def leave(turn):
        grad_stored(turn).wait()
        pl.when(turn < seqs - 1)(lambda: parts.move(tile_at(turn)[0], seq).start())

    def weight_grad(turn):
        slot = lax.rem(turn, 2)
        size = min(4 * TILE, 2 * units)
        tile = tile_at(turn)[1]

        @pl.loop(0, 2 * units // size)
        def _(column):
            here = rows_at(column, size)
            got = 0.0
            for batch in range(batches):
                left = buf[batch, :, :, rows_at(tile, block)].reshape(2 * chips * piece, block)
                got = got + contract_rows(left, d_ref[batch, :, here])
            tiles[slot, :, here] = to_half(got)

        pl.when(turn > 0)(lambda: leave(turn - 1))
        grad_stored(turn).start()

    def norm_batch(batch):
        own = pl.ds(batch * piece, piece)

        def put(here, d_values):
            there = pl.ds(pl.multiple_of(here.start + batch * piece, here.size), here.size)
            d_middle = cot_ref[there, :].astype(jnp.float32) + d_values
            dm_ref[there, :] = d_middle
            db_ref[there, :] = to_half(d_middle)

        norm_back(piece, v_ref.at[own], totals.at[batch], gain_ref, gain_grad_ref, put)

    gain_grad_ref[...] = jnp.zeros_like(gain_grad_ref)
    for item in loads:
        item.wait()
    last = 2 * chips - 2

    @pl.loop(0, chips)
    def _(far):
        take(0, far)
        pl.when(far == chips - 2)(spreads[1].begin)
        compute(0, far)

    @pl.loop(0, chips - 1)
    def _(far):
        take(1, far)
        reduces[0].step(2 * far)
        reduces[0].step(2 * far + 1)
        compute(1, far)

    take(1, chips - 1)
    compute(1, chips - 1)

    @pl.loop(0, 2)
    def _(step):
        reduces[1].step(step)
        weight_grad(step)

    reduces[0].step(last)
    norm_batch(0)
    first = db_ref.at[pl.ds(0, piece)]
    branch = Spread(line, first, branch_hbm, branch_send, branch_recv)
    branch_kept = pltpu.make_async_copy(first, branch_hbm.at[line.own], branch_keep)
    branch.begin()
    branch_kept.start()

    @pl.loop(2, last)
    def _(step):
        reduces[1].step(step)
        pl.when(step < count)(lambda: weight_grad(step))
        pl.when(lax.rem(step, 2) == 1)(lambda: branch.relay((step - 1) // 2))

    @pl.loop(last, max(count, last))
    def _(tile):
        weight_grad(tile)

    branch.relay(chips - 1)
    reduces[1].step(last)
    norm_batch(1)
    for batch in range(batches):
        spreads[batch].sent()
        reduces[batch].sent()
    for item in stored(1, 0):
        item.wait()
    leave(count - 1)
    parts.end()
    branch.rest()
    branch.sent()
    branch_kept.wait()


def feed_forward(seqs, chips, batches, x, w, wd, group_d, middle, cot, gain, collective):
    rows, width = x.shape
    group = 2 * chips
    units = wd.shape[0]
    piece = rows // batches
    block = width // seqs // 2
    half = jnp.bfloat16
    return pl.pallas_call(
        functools.partial(feed_kernel, seqs, chips, batches),
        out_shape=[
            jax.ShapeDtypeStruct((rows, width), jnp.float32),
            jax.ShapeDtypeStruct((rows, width), half),
            jax.ShapeDtypeStruct((8, width), jnp.float32),
            jax.ShapeDtypeStruct((group * rows, units), half),
            jax.ShapeDtypeStruct((width, 2 * units), half),
            jax.ShapeDtypeStruct((seqs, block, 2 * units), half),
            jax.ShapeDtypeStruct((group, piece, width), half),
        ],
        in_specs=[VMEM_SPEC] + [ANY_SPEC] * 3 + [VMEM_SPEC] * 3,
        out_specs=[VMEM_SPEC] * 3 + [ANY_SPEC] * 4,
        scratch_shapes=[
            pltpu.VMEM((batches, group, piece, width), half),
            pltpu.VMEM((2, 2 * piece, width), half),
            pltpu.VMEM((2 * piece, units), half),
            pltpu.VMEM(w.shape, half),
            pltpu.VMEM(wd.shape, half),
            pltpu.VMEM((batches, group * piece, 2 * units), half),
            pltpu.VMEM((2, block, 2 * units), half),
            pltpu.VMEM((batches, piece, width), jnp.float32),
            pltpu.VMEM((2 * piece, 2 * TILE), jnp.float32),
            pltpu.VMEM((piece, width), jnp.float32),
            sems(2),
            sems(2, 2),
            sems(2),
            sems(2),
            sems(batches, 3, group, PARTS // 2),
            sems(batches, group, PARTS // 2),
            sems(seqs),
            sems(seqs),
            sems(3, group, PARTS // 2),
            sems(group, PARTS // 2),
            pltpu.SemaphoreType.DMA,
        ]
        + PairReduce.scratch(chips, piece, width) * batches,
        compiler_params=comm_params(collective, 63),
        cost_estimate=cost(
            14 * group * rows * width * units, 400 * MIB, 2 * group * rows * width * 2
        ),
        name="feed_forward",
    )(x, w, wd, group_d, middle, cot, gain)


def branch_back_kernel(
    seqs, chips, batches, x_ref, b_hbm, w_ref, att_ref, middle_ref, hidden_hbm, wd_hbm, units_hbm, gd_hbm,
    d_ref, layer_ref, out_grad_ref, units_in, down_hbm, down_in,
    out_ref, early, buf, hidden_ref, wd_ref, grad_acc, rights, tiles, send, recv, load, right_sem, tile_sem,
    part_send, part_recv, down_send, down_recv, down_keep, acc, cross_out, line_out, cross_in, line_in, sum_send, sum_recv,
):
    line = Line(chips)
    rows = x_ref.shape[0]
    piece = rows // batches
    width = x_ref.shape[1]
    loads = [
        pltpu.make_async_copy(hidden_hbm, hidden_ref, load.at[0]),
        pltpu.make_async_copy(wd_hbm, wd_ref, load.at[1]),
        pltpu.make_async_copy(b_hbm, early, load.at[2]),
    ]
    for item in loads:
        item.start()

    def product(slot, tile):
        return dot_nn(left_rows(hidden_ref, slot, rows), wd_ref[:, rows_at(tile, TILE)])

    part = rights.shape[2]
    count = width // part

    def right(tile):
        slot = lax.rem(tile, 2)
        return pltpu.make_async_copy(
            gd_hbm.at[:, rows_at(tile, part)], rights.at[slot], right_sem.at[slot]
        )

    def stored(tile):
        slot = lax.rem(tile, 2)
        return pltpu.make_async_copy(
            tiles.at[slot], down_hbm.at[:, rows_at(tile, part)], tile_sem.at[slot]
        )

    def weight_grad(tile):
        right(tile).wait()
        pl.when(tile + 1 < count)(lambda: right(tile + 1).start())
        pl.when(tile >= 2)(lambda: stored(tile - 2).wait())
        slot = lax.rem(tile, 2)
        size = min(TILE, hidden_ref.shape[1])

        @pl.loop(0, hidden_ref.shape[1] // size)
        def _(row):
            here = rows_at(row, size)
            tiles[slot, here, :] = to_half(contract_rows(hidden_ref[:, here], rights[slot]))

        stored(tile).start()

    right(0).start()
    meet(line.greet() + greet_seq(seqs))
    sums = ToSeq(seqs, units_hbm, units_in, part_send, part_recv, units_in.shape[1])
    down = ToSeq(seqs, down_hbm, down_in, down_send, down_recv)
    down_rows = down_in.shape[1]
    down_kept = pltpu.make_async_copy(
        down_hbm.at[rows_at(down.own, down_rows)], down_in.at[down.own], down_keep
    )
    late = x_ref.at[pl.ds(piece, piece)]
    spread = Spread(line, late, buf, send, recv)
    reduce = Reduce(
        line, product, out_ref, acc, cross_out, line_out, cross_in, line_in, sum_send, sum_recv
    )
    spread.begin()
    sums.begin()
    buf[line.own] = late[...]
    grad_acc[...] = jnp.zeros_like(grad_acc)

    def use(slot):
        both = jnp.concatenate([early[slot], buf[slot]], axis=0)
        got = to_half(dot_nt(both, w_ref[...]))
        for batch in range(batches):
            d_ref[batch, rows_at(slot, piece), :] = got[batch * piece : (batch + 1) * piece]
        mixed = left_rows(att_ref, slot, rows)

        @pl.loop(0, width // TILE)
        def _(tile):
            here = rows_at(tile, TILE)
            right = jnp.concatenate([early[slot, :, here], buf[slot, :, here]], axis=0)
            grad_acc[:, here] += contract_rows(mixed, right)

    for item in loads:
        item.wait()

    reduce.level(chips - 1, lambda tile: None)
    pl.loop(0, count)(weight_grad)
    stored(count - 2).wait()
    stored(count - 1).wait()
    down.begin()
    down_kept.start()
    spread.relay(1)
    spread.each(0, use)

    @pl.loop(1, chips)
    def _(step):
        def also(tile):
            pl.when((step < chips - 1) & (tile < spread.parts))(
                lambda: spread.relay_part(step + 1, tile)
            )

        reduce.level(chips - 1 - step, also)
        spread.each(step, use)

    spread.each(chips, use)

    @pl.loop(0, rows // 32)
    def _(chunk):
        here = rows_at(chunk, 32)
        layer_ref[here, :] = to_half(middle_ref[here, :] + out_ref[here, :])

    out_grad_ref[...] = to_half(grad_acc[...])
    spread.sent()
    reduce.sent()
    sums.end()
    down.end()
    down_kept.wait()


def branch_back(seqs, chips, batches, x, early, w, attended, middle, hidden, wd, unit_part, group_d, collective):
    rows, width = x.shape
    group = 2 * chips
    length = group * rows // batches
    span = w.shape[0]
    half = jnp.bfloat16
    part = 256 if group * rows <= 2048 else 128
    return pl.pallas_call(
        functools.partial(branch_back_kernel, seqs, chips, batches),
        out_shape=[
            jax.ShapeDtypeStruct((batches, length, span), half),
            jax.ShapeDtypeStruct((rows, width), half),
            jax.ShapeDtypeStruct((span, width), half),
            jax.ShapeDtypeStruct((seqs, width // seqs // 2, unit_part.shape[1]), half),
            jax.ShapeDtypeStruct((wd.shape[0], width), half),
            jax.ShapeDtypeStruct((seqs, wd.shape[0] // seqs, width), half),
        ],
        in_specs=[VMEM_SPEC, ANY_SPEC] + [VMEM_SPEC] * 3 + [ANY_SPEC] * 4,
        out_specs=[VMEM_SPEC, VMEM_SPEC, VMEM_SPEC, ANY_SPEC, ANY_SPEC, ANY_SPEC],
        scratch_shapes=[
            pltpu.VMEM((rows, width), jnp.float32),
            pltpu.VMEM((group, rows // batches, width), half),
            pltpu.VMEM((group, rows // batches, width), half),
            pltpu.VMEM(hidden.shape, half),
            pltpu.VMEM(wd.shape, half),
            pltpu.VMEM((span, width), jnp.float32),
            pltpu.VMEM((2, group * rows, part), half),
            pltpu.VMEM((2, wd.shape[0], part), half),
            sems(3, group, PARTS // 2),
            sems(group, PARTS // 2),
            sems(3),
            sems(2),
            sems(2),
            sems(seqs),
            sems(seqs),
            sems(seqs),
            sems(seqs),
            pltpu.SemaphoreType.DMA,
        ]
        + Reduce.scratch(chips, rows, width),
        compiler_params=comm_params(collective, 62),
        cost_estimate=cost(
            2 * group * rows * width * (2 * span + 2 * wd.shape[0]),
            250 * MIB,
            2 * group * rows * width * 2,
        ),
        name="branch_back",
    )(x, early, w, attended, middle, hidden, wd, unit_part, group_d.reshape(group * rows, width))


def attention_back_kernel(
    seqs, chips, block, q_ref, pad_ref, low_ref, lse_ref, d_ref, part_hbm, in_one, in_two,
    w_ref, g_hbm, v_ref, dm_hbm, gain_ref, mlp_gain_ref, out_ref,
    grad_ref, wq_ref, wk_ref, wv_ref, wo_ref, tile_ref, gate_ref, up_ref,
    dk, dv, kt, heads, back_out, back_in, unit_parts, unit_sums, units, lefts, parts, sums, cols, out_in,
    totals, gain_acc, gain_out, gain_in, gain_sum, gain_back, acc, keep,
    halo_send, halo_recv, unit_load, unit_send, unit_recv, unit_keep, dm_load, left_sem,
    part_send, part_recv, cols_send, cols_recv, out_send, out_recv,
    gain_send, gain_recv, back_send, back_recv, *line_sums,
):
    line = Line(chips)
    group = 2 * chips
    seq = lax.axis_index("seq")
    own = line.own
    batches, length, span = q_ref.shape
    rows, width = v_ref.shape
    piece = rows // batches
    pair_rows = 2 * piece
    depth = 3 * span
    run = width // seqs
    share = run // group
    part = lefts.shape[3]
    steps, need = length // block, WINDOW // block
    first = length - WINDOW
    has_left, has_right = seq > 0, seq < seqs - 1
    scale = jnp.asarray(HEAD**-0.5, jnp.bfloat16)

    def others(count, me, act):
        pl.loop(1, count)(lambda ahead: act(lax.rem(me + ahead, count)))

    def unit_loaded(turn, place, source):
        slot = lax.rem(turn, 2)
        return pltpu.make_async_copy(source, unit_parts.at[slot, place], unit_load.at[slot, place])

    def load_units(turn):
        member = lax.rem(own + turn, group)
        mine = part_hbm.at[rows_at(seq * group + member, share)]
        for place in range(seqs):

            def fetch(source, place=place):
                unit_loaded(turn, place, source).start()

            pl.when(place == seq)(lambda: fetch(mine))

            @pl.when((place != seq) & (member < chips))
            def _(place=place):
                fetch(in_one.at[place, rows_at(member, share)])

            @pl.when((place != seq) & (member >= chips))
            def _(place=place):
                fetch(in_two.at[place, rows_at(member - chips, share)])

    load_units(1)
    dm_loaded = pltpu.make_async_copy(dm_hbm, grad_ref, dm_load)
    dm_loaded.start()
    meet(greet_group(group) + greet_seq(seqs))
    swap = Swap(group, unit_sums, units, unit_send, unit_recv, unit_keep)

    @pl.loop(1, group + 1)
    def _(turn):
        member = lax.rem(own + turn, group)
        slot = lax.rem(turn, 2)
        pl.when(turn < group)(lambda: load_units(turn + 1))
        for place in range(seqs):
            unit_loaded(turn, place, part_hbm.at[rows_at(0, share)]).wait()

        @pl.loop(0, share // 16)
        def _(chunk):
            here = rows_at(chunk, 16)
            added = unit_parts[slot, 0, here, :].astype(jnp.float32)
            for place in range(1, seqs):
                added = added + unit_parts[slot, place, here, :].astype(jnp.float32)
            unit_sums[member, here, :] = to_half(added)

        pl.when(turn < group)(lambda: swap.move(member, own).start())
        pl.when(turn == group)(lambda: swap.kept().start())

    def halo(batch, step, peer):
        here = rows_at(step, block)
        return pltpu.make_async_remote_copy(
            src_ref=back_out.at[batch, here],
            dst_ref=back_in.at[batch, here],
            send_sem=halo_send.at[batch, step],
            recv_sem=halo_recv.at[batch, step],
            device_id={"seq": peer},
            device_id_type=MESH,
        )

    def attend_block(batch, step):
        begin = pl.multiple_of(step * block, block)
        keys = pl.ds(begin, block + WINDOW)
        rows = pl.ds(begin, block)
        low = low_ref[batch, :, rows]
        for pair in range(span // PAIR):
            lanes = slice(pair * PAIR, (pair + 1) * PAIR)
            q_pair = q_ref[batch, rows, lanes] * scale
            d_pair = d_ref[batch, rows, lanes]
            k_rows = pad_ref[batch, keys, lanes]
            v_rows = pad_ref[batch, keys, span + pair * PAIR : span + (pair + 1) * PAIR]
            k_cols = kt[lanes, keys]
            back = []
            for half in range(2):
                row = pair * 2 + half
                q_head = head_lanes(q_pair, half)
                d_head = head_lanes(d_pair, half)
                scores = masked_scores(k_rows, q_head, low)
                probs = jnp.exp(scores - lse_ref[batch, row : row + 1, rows])
                d_probs = dot_nt(v_rows, d_head)
                along = jnp.sum(probs * d_probs, axis=0, keepdims=True)
                d_scores = to_half(probs * (d_probs - along))
                dv[keys, lanes] += dot_nn(to_half(probs), d_head)
                dk[keys, lanes] += dot_nn(d_scores, q_head)
                back.append(dot_nn(k_cols, d_scores))
            at = lax.broadcasted_iota(jnp.int32, back[0].shape, 0)
            heads[batch, rows, lanes] = to_half(
                jnp.where(at < HEAD, back[0], back[1]).T
            )


        @pl.when(has_left & (step < need))
        def _():
            back_out[batch, rows, :span] = to_half(dk[rows, :])
            back_out[batch, rows, span:] = to_half(dv[rows, :])
            halo(batch, step, seq - 1).start()

        @pl.when(step == steps - 1)
        def _():
            heads[batch, :, span : 2 * span] = to_half(dk[WINDOW:, :])
            heads[batch, :, 2 * span :] = to_half(dv[WINDOW:, :])

    def add_halo(batch):
        @pl.when(has_right)
        def _():
            @pl.loop(0, need)
            def _(step):
                there = pl.ds(pl.multiple_of(step * block + first, block), block)
                halo(batch, step, seq).wait_recv()
                got = back_in[batch, rows_at(step, block), :].astype(jnp.float32)
                mine = heads[batch, there, span:].astype(jnp.float32)
                heads[batch, there, span:] = to_half(mine + got)

    def product(batch):
        def get(place, here):
            return dot_nt(heads[batch, rows_at(place, pair_rows), :], w_ref[here, :])

        return get

    reduces = [
        PairReduce(
            line, product(batch), totals.at[batch], acc, keep, *line_sums[6 * batch : 6 * batch + 6]
        )
        for batch in range(batches)
    ]
    last = 2 * chips - 2

    @pl.loop(0, 2 * steps)
    def _(turn):
        batch, step = turn // steps, lax.rem(turn, steps)

        @pl.when(step == 0)
        def _():
            kt[...] = pad_ref[batch, :, :span].T * scale
            dk[...] = jnp.zeros_like(dk)
            dv[...] = jnp.zeros_like(dv)

        attend_block(batch, step)
        after = turn - steps - 1
        pl.when(after == 0)(lambda: add_halo(0))

        @pl.when((after >= 0) & (2 * after < last))
        def _():
            reduces[0].step(2 * after)
            reduces[0].step(2 * after + 1)

    for after in range(steps - 1, chips - 1):
        reduces[0].step(2 * after)
        reduces[0].step(2 * after + 1)

    def left(tile):
        slot = lax.rem(tile, 2)
        return pltpu.make_async_copy(
            g_hbm.at[:, :, rows_at(tile, part)], lefts.at[slot], left_sem.at[slot]
        )

    def to_seq(peer, place):
        return pltpu.make_async_remote_copy(
            src_ref=parts.at[rows_at(peer, run)],
            dst_ref=sums.at[place],
            send_sem=part_send.at[peer],
            recv_sem=part_recv.at[place],
            device_id={"seq": peer},
            device_id_type=MESH,
        )

    left(0).start()
    add_halo(1)

    @pl.loop(0, width // part)
    def _(tile):
        left(tile).wait()
        pl.when(tile + 1 < width // part)(lambda: left(tile + 1).start())
        slot = lax.rem(tile, 2)
        got = contract_rows(lefts[slot, 0], heads[0])
        for batch in range(1, batches):
            got = got + contract_rows(lefts[slot, batch], heads[batch])
        parts[rows_at(tile, part), :] = to_half(got)

    others(seqs, seq, lambda peer: to_seq(peer, seq).start())
    from_seq = ToSeq(seqs, out_ref, out_in, out_send, out_recv)
    from_seq.begin()
    gain_acc[...] = jnp.zeros_like(gain_acc)
    dm_loaded.wait()

    def norm_batch(batch):
        mine = pl.ds(batch * piece, piece)

        def put(here, d_values):
            there = pl.ds(pl.multiple_of(here.start + batch * piece, here.size), here.size)
            grad_ref[there, :] += d_values

        norm_back(piece, v_ref.at[mine], totals.at[batch], gain_ref, gain_acc, put)

    pl.loop(0, 2)(reduces[1].step)
    reduces[0].step(last)
    norm_batch(0)
    pl.loop(2, last)(reduces[1].step)
    swap.end()
    cell = units.shape[2] // 2 // seqs
    for member in range(group):
        for place in range(seqs):
            column = (place * group + member) * cell
            for target, begin in ((gate_ref, 0), (up_ref, seqs * cell)):
                here = slice(begin + place * cell, begin + (place + 1) * cell)
                target[:, column : column + cell] = units[member, :, here]

    def block_swap(peer, member):
        return pltpu.make_async_remote_copy(
            src_ref=parts.at[rows_at(seq * group + peer, share)],
            dst_ref=cols.at[member],
            send_sem=cols_send.at[peer],
            recv_sem=cols_recv.at[member],
            device_id={"fsdp": peer},
            device_id_type=MESH,
        )

    others(seqs, seq, lambda peer: to_seq(peer, peer).wait_recv())

    @pl.loop(0, run // 64)
    def _(chunk):
        here = rows_at(chunk, 64)
        there = pl.ds(pl.multiple_of(seq * run + chunk * 64, 64), 64)
        parts[there, :] = to_half(add_from_seq(seqs, parts[there, :], sums, here))

    others(group, own, lambda peer: block_swap(peer, own).start())
    cols[own] = parts[rows_at(seq * group + own, share), :]
    from_seq.arrived()
    out_rows = out_in.shape[1]
    wo_ref[...] = add_from_seq(seqs, out_ref[rows_at(seq, out_rows), :], out_in, slice(None))
    reduces[1].step(last)
    norm_batch(1)
    fold = 128 // share
    near = group // fold
    attn_row = jnp.sum(gain_acc[...], axis=0, keepdims=True)
    mlp_row = jnp.sum(mlp_gain_ref[...], axis=0, keepdims=True)
    gain_out[...] = jnp.zeros_like(gain_out)
    for place in range(width // 128):
        lanes = slice(place * 128, (place + 1) * 128)
        gain_out[place % near, place // near, 0:1, :] = attn_row[:, lanes]
        gain_out[place % near, place // near, 1:2, :] = mlp_row[:, lanes]

    def gain_group(peer, member):
        return pltpu.make_async_remote_copy(
            src_ref=gain_out.at[peer // fold],
            dst_ref=gain_in.at[member],
            send_sem=gain_send.at[peer],
            recv_sem=gain_recv.at[member],
            device_id={"fsdp": peer},
            device_id_type=MESH,
        )

    def gain_seq(peer, place):
        return pltpu.make_async_remote_copy(
            src_ref=gain_sum.at[peer],
            dst_ref=gain_back.at[place],
            send_sem=back_send.at[peer],
            recv_sem=back_recv.at[place],
            device_id={"seq": peer},
            device_id_type=MESH,
        )

    others(group, own, lambda peer: gain_group(peer, own).start())
    gain_in[own] = gain_out[own // fold]
    others(group, own, lambda peer: gain_group(peer, peer).wait_recv())
    gain_sum[...] = jnp.sum(gain_in[...], axis=0)
    others(seqs, seq, lambda peer: gain_seq(peer, seq).start())
    gain_back[seq] = gain_sum[seq]
    others(seqs, seq, lambda peer: gain_seq(peer, peer).wait_recv())
    tile_ref[...] = jnp.sum(gain_back[...], axis=0)
    others(group, own, lambda peer: block_swap(peer, peer).wait_recv())
    for index, target in enumerate((wq_ref, wk_ref, wv_ref)):
        for member, first, home, size in column_parts(seqs, group, share, span):
            first = first + index * span
            target[:, home : home + size] = cols[member, :, first : first + size]
    from_seq.sent()
    for batch in range(batches):
        reduces[batch].sent()

        @pl.when(has_left)
        def _(batch=batch):
            pl.loop(0, need)(lambda step: halo(batch, step, seq).wait_send())

    others(seqs, seq, lambda peer: to_seq(peer, seq).wait_send())
    others(group, own, lambda peer: gain_group(peer, own).wait_send())
    others(group, own, lambda peer: block_swap(peer, own).wait_send())
    others(seqs, seq, lambda peer: gain_seq(peer, seq).wait_send())


def attention_back(
    seqs, chips, block, query, kv_pad, low, lse, d_att, part_own, parts_one, parts_two, w, group_a, x,
    d_middle, gain, mlp_gain, out_part, collective,
):
    batches, length, span = query.shape
    padded = kv_pad.shape[1]
    rows, width = x.shape
    piece = rows // batches
    group = 2 * chips
    depth = w.shape[1]
    run = width // seqs
    share = run // group
    near = group // (128 // share)
    cells = part_own.shape[1]
    out_rows = out_part.shape[0] // seqs
    half, wide = jnp.bfloat16, jnp.float32
    part = 256 if batches * length <= 2048 else 128
    return pl.pallas_call(
        functools.partial(attention_back_kernel, seqs, chips, block),
        out_shape=[
            jax.ShapeDtypeStruct((rows, width), wide),
            jax.ShapeDtypeStruct((share, width), half),
            jax.ShapeDtypeStruct((share, width), half),
            jax.ShapeDtypeStruct((share, width), half),
            jax.ShapeDtypeStruct((out_rows, width), wide),
            jax.ShapeDtypeStruct((8, 128), wide),
            jax.ShapeDtypeStruct((share, cells // 2 * group), half),
            jax.ShapeDtypeStruct((share, cells // 2 * group), half),
        ],
        in_specs=[VMEM_SPEC] * 5
        + [ANY_SPEC] * 3
        + [VMEM_SPEC, ANY_SPEC, VMEM_SPEC, ANY_SPEC]
        + [VMEM_SPEC] * 3,
        out_specs=[VMEM_SPEC] * 8,
        scratch_shapes=[
            pltpu.VMEM((padded, span), wide),
            pltpu.VMEM((padded, span), wide),
            pltpu.VMEM((span, padded), half),
            pltpu.VMEM((batches, length, depth), half),
            pltpu.VMEM((batches, WINDOW, 2 * span), half),
            pltpu.VMEM((batches, WINDOW, 2 * span), half),
            pltpu.VMEM((2, seqs, share, cells), half),
            pltpu.VMEM((group, share, cells), half),
            pltpu.VMEM((group, share, cells), half),
            pltpu.VMEM((2, batches, length, part), half),
            pltpu.VMEM((width, depth), half),
            pltpu.VMEM((seqs, run, depth), half),
            pltpu.VMEM((group, share, depth), half),
            pltpu.VMEM((seqs, out_rows, width), half),
            pltpu.VMEM((batches, piece, width), wide),
            pltpu.VMEM((8, width), wide),
            pltpu.VMEM((near, seqs, 8, 128), wide),
            pltpu.VMEM((group, seqs, 8, 128), wide),
            pltpu.VMEM((seqs, 8, 128), wide),
            pltpu.VMEM((seqs, 8, 128), wide),
            pltpu.VMEM((2 * piece, TILE), wide),
            pltpu.VMEM((piece, width), wide),
            sems(batches, WINDOW // block),
            sems(batches, WINDOW // block),
            sems(2, seqs),
            sems(group),
            sems(group),
            pltpu.SemaphoreType.DMA,
            pltpu.SemaphoreType.DMA,
            sems(2),
            sems(seqs),
            sems(seqs),
            sems(group),
            sems(group),
            sems(seqs),
            sems(seqs),
            sems(group),
            sems(group),
            sems(seqs),
            sems(seqs),
        ]
        + PairReduce.scratch(chips, piece, width) * batches,
        compiler_params=comm_params(collective, 63),
        cost_estimate=cost(
            20 * batches * length * span * (WINDOW + block) + 4 * group * rows * width * depth,
            400 * MIB,
            3 * group * rows * width * 2,
        ),
        name="attention_back",
    )(
        query, kv_pad, low, lse, d_att, part_own, parts_one, parts_two, w, group_a, x, d_middle,
        gain, mlp_gain, out_part,
    )


def finish_kernel(*refs):
    half = len(refs) // 2
    for source, target in zip(refs[:half], refs[half:]):
        if len(source.shape) == len(target.shape):
            target[...] = source[...].astype(target.dtype)
        else:
            target[...] = jnp.sum(source[...].astype(jnp.float32), axis=0)


def finish(steps, arrays, kinds):
    in_specs, out_specs, out_shape = [], [], []
    for item, kind in zip(arrays, kinds):
        rows, width = item.shape[-2:]
        block = (rows // steps, width)
        out_specs.append(pl.BlockSpec(block, lambda i: (i, 0)))
        out_shape.append(jax.ShapeDtypeStruct((rows, width), kind))
        if item.ndim == 3:
            in_specs.append(pl.BlockSpec((item.shape[0],) + block, lambda i: (0, i, 0)))
        else:
            in_specs.append(out_specs[-1])
    return pl.pallas_call(
        finish_kernel,
        grid=(steps,),
        in_specs=in_specs,
        out_specs=out_specs,
        out_shape=out_shape,
        compiler_params=pltpu.CompilerParams(vmem_limit_bytes=48 * MIB),
        name="finish",
    )(*arrays)


def doc_starts(lengths, positions, batches, seq_len):
    table = lengths.reshape(batches, -1, lengths.shape[1])
    starts = jnp.cumsum(table, axis=2) - table
    per_batch = seq_len // table.shape[1]
    begins = (starts + (jnp.arange(table.shape[1], dtype=jnp.int32) * per_batch)[None, :, None]).reshape(
        batches, -1
    )
    before = begins[:, None, :] <= positions[None, :, None]
    return jnp.max(jnp.where(before, begins[:, None, :], 0), axis=2)


def body(
    tokens,
    cotangent,
    lengths,
    gain_attn,
    w_query,
    w_key,
    w_value,
    w_out,
    gain_mlp,
    w_gate,
    w_up,
    w_down,
):
    batches, piece, width = tokens.shape
    seqs = lax.axis_size("seq")
    group = lax.axis_size("fsdp")
    chips = group // 2
    devices = seqs * group
    seq_len = piece * devices
    rows = batches * piece
    share = w_query.shape[0]
    span = width // group
    length = group * piece
    aligned = share == HEAD
    member = lax.axis_index("fsdp")

    x_rows = tokens.reshape(rows, width)
    cot_rows = cotangent.reshape(rows, width)
    wd_part = lax.all_gather(w_down, "seq", axis=0, tiled=True)
    if aligned:
        wo_part = lax.all_gather(w_out, "seq", axis=0, tiled=True)
    else:
        wo_all = lax.all_gather(w_out, ("seq", "fsdp"), axis=0, tiled=True)
        wo_part = lax.dynamic_slice_in_dim(wo_all, member * span, span, 0)

    lane = jnp.arange(128, dtype=jnp.int32)
    device = lax.axis_index("seq") * group + member
    fold = 128 // share
    here = lane // share == lax.rem(device, fold)
    both = jnp.stack([gain_attn, gain_mlp]).astype(jnp.float32)
    tile = jnp.where(here[None], jnp.tile(both, (1, fold)), 0.0)
    tile = jnp.pad(tile, ((0, 6), (0, 0)))[None]
    group_a, query, key_value, gains, w_heads, unit_blocks = start(
        seqs, chips, batches, tile, x_rows, (w_query, w_key, w_value), (w_gate, w_up), 1
    )
    lengths, gains = lax.optimization_barrier((lengths, gains))
    group_start = lax.axis_index("seq") * length
    positions = group_start + jnp.arange(length, dtype=jnp.int32)
    begins = doc_starts(lengths, positions, batches, seq_len)
    at = jnp.arange(length, dtype=jnp.int32)
    block = min(256, length)
    low = jnp.maximum(begins - group_start + WINDOW, at[None, :] + 1) - (at // block * block)[None, :]
    low = low[:, None, :]

    gains = gains.transpose(1, 0, 2, 3).reshape(devices // fold, fold, 8, 128).sum(axis=1)
    gain_one = gains[:, 0].reshape(width)
    gain_two = gains[:, 1].reshape(width)
    attended, lse, kv_pad, unit_own = attend(
        seqs, group, query, key_value, low, block, unit_blocks, 2
    )
    middle, normed_b, group_d, w_units = branch_sum(
        seqs, chips, attended, wo_part, cot_rows, unit_own.reshape(group * share, -1),
        x_rows, gain_two[None], 3,
    )
    w_units = w_units.reshape(width, -1)
    d_middle, d_branch, mlp_gain_part, hidden, unit_part, unit_one, early = feed_forward(
        seqs, chips, batches, normed_b, w_units, wd_part, group_d, middle, cot_rows,
        gain_two[None], 4,
    )
    d_attended, layer_out, out_part, unit_two, _, down_in = branch_back(
        seqs, chips, batches, d_branch, early, wo_part, attended, middle, hidden, wd_part, unit_part,
        group_d, 5,
    )
    if not aligned:
        whole = lax.dynamic_update_slice_in_dim(
            jnp.zeros((width, width), jnp.bfloat16), out_part, member * span, 0
        )
        out_part = lax.psum(whole, "fsdp").reshape(seqs, group, share, width)
        out_part = lax.dynamic_slice_in_dim(out_part, member, 1, 1).reshape(seqs * share, width)
    input_grad, wq_grad, wk_grad, wv_grad, wo_grad, gain_tile, gate_grad, up_grad = attention_back(
        seqs, chips, block, query, kv_pad, low, lse, d_attended, unit_part, unit_one, unit_two,
        w_heads, group_a, x_rows, d_middle, gain_one[None], mlp_gain_part, out_part, 6,
    )
    gain_grads = lax.dynamic_slice_in_dim(gain_tile[:2], lax.rem(device, fold) * share, share, 1)
    wide = jnp.float32
    (layer_out, input_grad, wq_grad, wk_grad, wv_grad, wo_grad, gate_grad, up_grad, down_grad) = finish(
        share // 16,
        [layer_out, input_grad, wq_grad, wk_grad, wv_grad, wo_grad, gate_grad, up_grad, down_in],
        [jnp.bfloat16] + [wide] * 8,
    )
    return (
        layer_out.reshape(batches, piece, width),
        input_grad.reshape(batches, piece, width),
        gain_grads[0],
        wq_grad,
        wk_grad,
        wv_grad,
        wo_grad,
        gain_grads[1],
        gate_grad,
        up_grad,
        down_grad,
    )


def solution(mesh):
    spread = ("seq", "fsdp")
    tokens, rows, gains = P(None, spread, None), P(spread, None), P(spread)
    in_specs = (tokens, tokens, P(), gains, rows, rows, rows, rows, gains, rows, rows, rows)
    out_specs = (tokens, tokens, gains, rows, rows, rows, rows, gains, rows, rows, rows)
    return jax.shard_map(body, mesh=mesh, in_specs=in_specs, out_specs=out_specs, check_vma=False)
```

```python
import functools

import jax
import jax.numpy as jnp
from jax import lax
from jax.experimental import pallas as pl
from jax.experimental.pallas import tpu as pltpu
from jax.sharding import PartitionSpec as P

HEAD = 64
FF = 8192
WINDOW = 1024
PAIR = 128
TILE = 512
PARTS = 4
LOW = -1e30
EPS = 1e-05
MESH = pl.DeviceIdType.MESH
MIB = 2**20


def to_half(values):
    return values.astype(jnp.bfloat16)


def normalize(values, gain):
    return values * lax.rsqrt(jnp.mean(values * values, axis=-1, keepdims=True) + EPS) * gain


def contract_rows(left, right):
    return lax.dot_general(
        left, right, (((0,), (0,)), ((), ())), preferred_element_type=jnp.float32
    )


def dot_nt(left, right):
    return lax.dot_general(
        left, right, (((1,), (1,)), ((), ())), preferred_element_type=jnp.float32
    )


def dot_nn(left, right):
    return jnp.dot(left, right, preferred_element_type=jnp.float32)


def head_lanes(values, half):
    lane = lax.broadcasted_iota(jnp.int32, values.shape, 1)
    return jnp.where((lane >= HEAD) == (half == 1), values, jnp.zeros_like(values))


def masked_scores(k_rows, q_head, low):
    keys, block = k_rows.shape[0], q_head.shape[0]
    scores = dot_nt(k_rows, q_head)
    at = lax.broadcasted_iota(jnp.int32, (keys, block), 0)
    query = lax.broadcasted_iota(jnp.int32, (keys, block), 1)
    seen = (at >= low) & (at <= query + WINDOW)
    return jnp.where(seen, scores, LOW)


class Line:
    def __init__(self, chips):
        self.chips = chips
        self.own = lax.axis_index("fsdp")
        self.chip = self.own // 2
        self.core = lax.rem(self.own, 2)
        self.other = self.own + 1 - 2 * self.core
        self.has_left = self.chip > 0
        self.has_right = self.chip < chips - 1

    def greet(self):
        signal_group(self.other)
        pl.when(self.has_left)(lambda: signal_group(self.own - 2))
        pl.when(self.has_right)(lambda: signal_group(self.own + 2))
        return 1 + self.has_left.astype(jnp.int32) + self.has_right.astype(jnp.int32)


def signal_group(peer):
    barrier = pltpu.get_barrier_semaphore()
    pl.semaphore_signal(barrier, inc=1, device_id={"fsdp": peer}, device_id_type=MESH)


def signal_seq(peer):
    barrier = pltpu.get_barrier_semaphore()
    pl.semaphore_signal(barrier, inc=1, device_id={"seq": peer}, device_id_type=MESH)


def greet_group(group):
    own = lax.axis_index("fsdp")
    pl.loop(1, group)(lambda ahead: signal_group(lax.rem(own + ahead, group)))
    return group - 1


def greet_seq(seqs):
    own = lax.axis_index("seq")
    pl.loop(1, seqs)(lambda ahead: signal_seq(lax.rem(own + ahead, seqs)))
    return seqs - 1


def meet(count):
    pl.semaphore_wait(pltpu.get_barrier_semaphore(), count)


def rows_at(index, size):
    return pl.ds(pl.multiple_of(index * size, size), size)


class Spread:
    def __init__(self, line, first, buf, send, recv):
        self.line, self.first, self.buf, self.send, self.recv = line, first, buf, send, recv
        self.parts = recv.shape[1]
        self.size = first.shape[0] // self.parts

    def move(self, slot, part, way, peer, source=None):
        here = rows_at(part, self.size)
        return pltpu.make_async_remote_copy(
            src_ref=self.buf.at[slot, here] if source is None else source.at[here],
            dst_ref=self.buf.at[slot, here],
            send_sem=self.send.at[way, slot, part],
            recv_sem=self.recv.at[slot, part],
            device_id={"fsdp": peer},
            device_id_type=MESH,
        )

    def begin(self):
        line = self.line

        @pl.loop(0, self.parts)
        def _(part):
            pl.when(line.has_right)(
                lambda: self.move(line.own, part, 1, line.own + 2, self.first).start()
            )
            pl.when(line.has_left)(
                lambda: self.move(line.own, part, 0, line.own - 2, self.first).start()
            )
            self.move(line.own, part, 2, line.other, self.first).start()

    def relay_part(self, far, part):
        line = self.line

        @pl.when(line.chip - far >= 0)
        def _():
            slot = (line.chip - far) * 2 + line.core
            self.move(slot, part, 1, line.own).wait_recv()
            pl.when(line.has_right)(lambda: self.move(slot, part, 1, line.own + 2).start())
            self.move(slot, part, 2, line.other).start()

        @pl.when(line.chip + far < line.chips)
        def _():
            slot = (line.chip + far) * 2 + line.core
            self.move(slot, part, 0, line.own).wait_recv()
            pl.when(line.has_left)(lambda: self.move(slot, part, 0, line.own - 2).start())
            self.move(slot, part, 2, line.other).start()

    def relay(self, far):
        pl.loop(0, self.parts)(lambda part: self.relay_part(far, part))

    def across(self, slot):
        pl.loop(0, self.parts)(lambda part: self.move(slot, part, 2, self.line.own).wait_recv())

    def each(self, far, use):
        line = self.line

        @pl.loop(0, 4)
        def _(turn):
            side = lax.rem(turn, 2)
            over = turn // 2
            away = far - over
            source = line.chip + away * (2 * side - 1)
            valid = (away >= 0) & (away < line.chips) & (source >= 0) & (source < line.chips)
            valid = valid & ((side == 0) | (away > 0))

            @pl.when(valid)
            def _():
                slot = source * 2 + line.core + over * (1 - 2 * line.core)
                pl.when(over == 1)(lambda: self.across(slot))
                use(slot)

    def rest(self):
        pl.loop(0, self.line.chips)(lambda place: self.across(place * 2 + 1 - self.line.core))

    def sent(self):
        line = self.line

        @pl.loop(0, line.chips)
        def _(place):
            slot = place * 2 + line.core

            @pl.loop(0, self.parts)
            def _(part):
                self.move(slot, part, 2, line.other).wait_send()
                pl.when(line.has_right & (place <= line.chip))(
                    lambda: self.move(slot, part, 1, line.own + 2).wait_send()
                )
                pl.when(line.has_left & (place >= line.chip))(
                    lambda: self.move(slot, part, 0, line.own - 2).wait_send()
                )


class Reduce:
    def __init__(self, line, product, out, acc, cross_out, line_out, cross_in, line_in, send, recv):
        self.line, self.product, self.out, self.acc = line, product, out, acc
        self.cross_out, self.line_out, self.cross_in, self.line_in = cross_out, line_out, cross_in, line_in
        self.send, self.recv = send, recv
        self.tiles = line_out.shape[2] // TILE

    @staticmethod
    def scratch(chips, rows, width):
        part = pltpu.VMEM((chips, rows, width), jnp.bfloat16)
        return [
            pltpu.VMEM((rows, TILE), jnp.float32),
            pltpu.VMEM((2, rows, width), jnp.bfloat16),
            part,
            part,
            pltpu.VMEM((chips + 1, rows, width), jnp.bfloat16),
            pltpu.SemaphoreType.DMA((2, chips, width // TILE)),
            pltpu.SemaphoreType.DMA((2, chips + 1, width // TILE)),
        ]

    def cross(self, side, place, tile):
        here = rows_at(tile, TILE)
        return pltpu.make_async_remote_copy(
            src_ref=self.cross_out.at[side, :, here],
            dst_ref=self.cross_in.at[place, :, here],
            send_sem=self.send.at[0, place, tile],
            recv_sem=self.recv.at[0, place, tile],
            device_id={"fsdp": self.line.other},
            device_id_type=MESH,
        )

    def along(self, place, landing, tile, peer):
        here = rows_at(tile, TILE)
        return pltpu.make_async_remote_copy(
            src_ref=self.line_out.at[place, :, here],
            dst_ref=self.line_in.at[landing, :, here],
            send_sem=self.send.at[1, place, tile],
            recv_sem=self.recv.at[1, landing, tile],
            device_id={"fsdp": peer},
            device_id_type=MESH,
        )

    def where(self, away, side):
        line = self.line
        rightward = (line.chips - 1 - line.chip >= line.chip) == (side == 0)
        place = line.chip + jnp.where(rightward, away, -away)
        valid = (place >= 0) & (place < line.chips) & ((away > 0) | (side == 0))
        return valid, place, rightward

    def level(self, away, also):
        @pl.loop(0, 2)
        def _(side):
            valid, place, _ = self.where(away, side)

            @pl.when(valid)
            def _():
                @pl.loop(0, self.tiles)
                def _(tile):
                    got = self.product(place * 2 + 1 - self.line.core, tile)
                    self.cross_out[side, :, rows_at(tile, TILE)] = to_half(got)
                    self.cross(side, place, tile).start()

        @pl.loop(0, self.tiles)
        def _(tile):
            @pl.loop(0, 2)
            def _(side):
                valid, place, rightward = self.where(away, side)
                pl.when(valid)(lambda: self.close(away, side, place, rightward, tile))

            also(tile)

    def close(self, away, side, place, rightward, tile):
        line, acc = self.line, self.acc
        here = rows_at(tile, TILE)
        upstream = (rightward & line.has_left) | (jnp.logical_not(rightward) & line.has_right)
        acc[...] = self.product(place * 2 + line.core, tile)
        self.cross(side, place, tile).wait()
        acc[...] += self.cross_in[place, :, here].astype(jnp.float32)

        @pl.when(away > 0)
        def _():
            @pl.when(upstream)
            def _():
                self.along(place, place, tile, line.own).wait_recv()
                self.line_out[place, :, here] = to_half(
                    acc[...] + self.line_in[place, :, here].astype(jnp.float32)
                )

            @pl.when(jnp.logical_not(upstream))
            def _():
                self.line_out[place, :, here] = to_half(acc[...])

            @pl.when(rightward)
            def _():
                self.along(place, place, tile, line.own + 2).start()

            @pl.when(jnp.logical_not(rightward))
            def _():
                landing = jnp.where(away == 1, line.chips, place)
                self.along(place, landing, tile, line.own - 2).start()

        @pl.when(away == 0)
        def _():
            self.out[:, here] = acc[...]

            @pl.when(line.has_left)
            def _():
                self.along(place, place, tile, line.own).wait_recv()
                self.out[:, here] += self.line_in[place, :, here].astype(jnp.float32)

            @pl.when(line.has_right)
            def _():
                self.along(place, line.chips, tile, line.own).wait_recv()
                self.out[:, here] += self.line_in[line.chips, :, here].astype(jnp.float32)

    def sent(self):
        @pl.loop(0, self.line.chips)
        def _(place):
            @pl.when(place != self.line.chip)
            def _():
                pl.loop(0, self.tiles)(
                    lambda tile: self.along(place, place, tile, self.line.own).wait_send()
                )


class Swap:
    def __init__(self, group, source, target, send, recv, keep):
        self.group, self.source, self.target = group, source, target
        self.send, self.recv, self.keep = send, recv, keep
        self.own = lax.axis_index("fsdp")

    def move(self, peer, source):
        return pltpu.make_async_remote_copy(
            src_ref=self.source.at[peer],
            dst_ref=self.target.at[source],
            send_sem=self.send.at[peer],
            recv_sem=self.recv.at[source],
            device_id={"fsdp": peer},
            device_id_type=MESH,
        )

    def kept(self):
        return pltpu.make_async_copy(self.source.at[self.own], self.target.at[self.own], self.keep)

    def begin(self):
        self.kept().start()
        pl.loop(1, self.group)(
            lambda ahead: self.move(lax.rem(self.own + ahead, self.group), self.own).start()
        )

    def end(self):
        self.kept().wait()

        @pl.loop(1, self.group)
        def _(ahead):
            peer = lax.rem(self.own + ahead, self.group)
            self.move(peer, peer).wait_recv()
            self.move(peer, self.own).wait_send()


class Share:
    def __init__(self, seqs, source, target, send, recv, keep):
        self.seqs, self.source, self.target = seqs, source, target
        self.send, self.recv, self.keep = send, recv, keep
        self.own = lax.axis_index("seq")
        self.half = source.shape[0] // 2

    def move(self, peer, place):
        return pltpu.make_async_remote_copy(
            src_ref=self.source,
            dst_ref=self.target.at[place],
            send_sem=self.send.at[peer, 0],
            recv_sem=self.recv.at[place, 0],
            device_id={"seq": peer},
            device_id_type=MESH,
        )

    def relay(self, peer, place, part):
        here = pl.ds(part * self.half, self.half)
        return pltpu.make_async_remote_copy(
            src_ref=self.target.at[place, here],
            dst_ref=self.target.at[place, here],
            send_sem=self.send.at[peer, 1],
            recv_sem=self.recv.at[place, part],
            device_id={"seq": peer},
            device_id_type=MESH,
        )

    def near(self):
        one = self.own + 1 - 2 * lax.rem(self.own, 2)
        two = lax.rem(self.own + 2, 4)
        return one, two, lax.rem(one + 2, 4)

    def kept(self):
        return pltpu.make_async_copy(self.source, self.target.at[self.own], self.keep)

    def begin(self):
        self.kept().start()
        if self.seqs == 4:
            one, two, _ = self.near()
            self.move(one, self.own).start()
            self.move(two, self.own).start()
        else:
            pl.loop(1, self.seqs)(
                lambda ahead: self.move(lax.rem(self.own + ahead, self.seqs), self.own).start()
            )

    def pass_on(self):
        if self.seqs == 4:
            one, two, _ = self.near()
            self.move(one, one).wait_recv()
            self.relay(two, one, 0).start()
            self.move(two, two).wait_recv()
            self.relay(one, two, 1).start()

    def end(self):
        self.kept().wait()
        if self.seqs == 4:
            one, two, far = self.near()
            self.relay(two, far, 0).wait_recv()
            self.relay(one, far, 1).wait_recv()
            self.move(one, self.own).wait_send()
            self.move(two, self.own).wait_send()
            self.relay(two, one, 0).wait_send()
            self.relay(one, two, 1).wait_send()
        else:

            @pl.loop(1, self.seqs)
            def _(ahead):
                peer = lax.rem(self.own + ahead, self.seqs)
                self.move(peer, peer).wait_recv()
                self.move(peer, self.own).wait_send()


def seq_peers(seqs):
    own = lax.axis_index("seq")
    if seqs == 4:
        one = own + 1 - 2 * lax.rem(own, 2)
        return [one, lax.rem(own + 2, 4)], [lax.rem(one + 2, 4)]
    ahead = [lax.rem(own + step, seqs) for step in range(1, seqs)]
    return ahead[:1], ahead[1:]


def near_count(seqs):
    return 2 if seqs == 4 else 1


class ToPeers:
    def __init__(self, seqs, peers, source, target, send, recv, first=0):
        self.peers, self.source, self.target, self.send, self.recv = peers, source, target, send, recv
        self.run, self.first = source.shape[0] // seqs, first

    def move(self, index):
        begin = pl.multiple_of(self.peers[index] * self.run + self.first, 16)
        return pltpu.make_async_remote_copy(
            src_ref=self.source.at[pl.ds(begin, self.target.shape[1])],
            dst_ref=self.target.at[index],
            send_sem=self.send.at[index],
            recv_sem=self.recv.at[index],
            device_id={"seq": self.peers[index]},
            device_id_type=MESH,
        )

    def begin(self):
        for index in range(len(self.peers)):
            self.move(index).start()

    def arrived(self):
        for index in range(len(self.peers)):
            self.move(index).wait_recv()

    def sent(self):
        for index in range(len(self.peers)):
            self.move(index).wait_send()

    def end(self):
        self.arrived()
        self.sent()


VMEM_SPEC = pl.BlockSpec(memory_space=pltpu.VMEM)
ANY_SPEC = pl.BlockSpec(memory_space=pl.ANY)


def comm_params(collective, mib=58):
    return pltpu.CompilerParams(
        collective_id=collective, has_side_effects=True, vmem_limit_bytes=mib * MIB
    )


def cost(flops, local, remote):
    return pl.CostEstimate(
        flops=flops, bytes_accessed=local, transcendentals=0, remote_bytes_transferred=remote
    )


def sems(*shape):
    return pltpu.SemaphoreType.DMA(shape)


def left_rows(a_ref, slot, rows):
    if len(a_ref.shape) == 2:
        return a_ref[rows_at(slot, rows), :]
    piece = rows // a_ref.shape[0]
    return jnp.concatenate(
        [a_ref[batch, rows_at(slot, piece), :] for batch in range(a_ref.shape[0])], axis=0
    )


def norm_back(rows, v_ref, e_ref, gain_ref, gain_acc, put):
    @pl.loop(0, rows // 32)
    def _(chunk):
        here = rows_at(chunk, 32)
        values = v_ref[here, :].astype(jnp.float32)
        error = e_ref[here, :]
        rate = lax.rsqrt(jnp.mean(values * values, axis=-1, keepdims=True) + EPS)
        unit = values * rate
        product = error * unit
        gain = gain_ref[0:1, :]
        mean = jnp.mean(product * gain, axis=-1, keepdims=True)
        gain_acc[...] += (product[0:8] + product[8:16]) + (product[16:24] + product[24:32])
        put(here, rate * (gain * error - unit * mean))


def add_from_seq(own_rows, got, here):
    added = own_rows.astype(jnp.float32)
    for index in range(got.shape[0]):
        added = added + got[index, here, :].astype(jnp.float32)
    return added


def column_parts(seqs, group, share, span):
    size = HEAD if share == HEAD else span
    parts = []
    for member in range(group):
        for run in range(span // size):
            home = (run * group + member) * size
            parts.append((member, run * size, home, size))
    return parts


def start_kernel(
    seqs, chips, batches, tile_ref, x_ref, wq_ref, wk_ref, wv_ref, gate_hbm, up_hbm,
    g_ref, q_ref, kv_ref, gains_ref, w_out_ref, units_ref,
    gate, up, units, unit_sem,
    blocks_ref, buf, normed, gain, gains, w, send, recv, keep, swap_send, share_send, w_recv,
    tile_send, tile_across, tile_recv, tile_back, w_keep, gain_keep,
):
    line = Line(chips)
    group = 2 * chips
    seq = lax.axis_index("seq")
    own = line.own
    share = blocks_ref.shape[1]
    piece = x_ref.shape[0] // batches
    span = q_ref.shape[2]
    width = x_ref.shape[1]
    per = 128 * seqs * group // width
    unit_loads = [
        pltpu.make_async_copy(gate_hbm, gate, unit_sem.at[0]),
        pltpu.make_async_copy(up_hbm, up, unit_sem.at[1]),
    ]
    for item in unit_loads:
        item.start()
    for index, source in enumerate((wq_ref, wk_ref, wv_ref)):
        for member, first, home, size in column_parts(seqs, group, share, span):
            first = first + index * span
            blocks_ref[member, :, first : first + size] = source[:, home : home + size]
    meet(greet_group(group) + greet_seq(seqs))

    def block_at(run, member):
        return w.at[rows_at(run * group + member, share)]

    def block_swap(peer, member):
        return pltpu.make_async_remote_copy(
            src_ref=blocks_ref.at[peer],
            dst_ref=block_at(seq, member),
            send_sem=swap_send.at[peer],
            recv_sem=w_recv.at[seq, member],
            device_id={"fsdp": peer},
            device_id_type=MESH,
        )

    def block_share(run, member, peer):
        return pltpu.make_async_remote_copy(
            src_ref=block_at(run, member),
            dst_ref=block_at(run, member),
            send_sem=share_send.at[peer, member],
            recv_sem=w_recv.at[run, member],
            device_id={"seq": peer},
            device_id_type=MESH,
        )

    def tile_to_seq(peer, place):
        return pltpu.make_async_remote_copy(
            src_ref=tile_ref.at[0],
            dst_ref=gains.at[own, place],
            send_sem=tile_send.at[peer],
            recv_sem=tile_recv.at[place],
            device_id={"seq": peer},
            device_id_type=MESH,
        )

    def tiles_to_group(peer, member):
        return pltpu.make_async_remote_copy(
            src_ref=gains.at[member],
            dst_ref=gains.at[member],
            send_sem=tile_across.at[peer],
            recv_sem=tile_back.at[member],
            device_id={"fsdp": peer},
            device_id_type=MESH,
        )

    def others(count, me, act):
        pl.loop(1, count)(lambda ahead: act(lax.rem(me + ahead, count)))

    others(seqs, seq, lambda peer: tile_to_seq(peer, seq).start())
    others(group, own, lambda peer: block_swap(peer, own).start())
    spread = Spread(line, x_ref, buf, send, recv)
    spread.begin()
    gains[own, seq] = tile_ref[0]
    w[rows_at(seq * group + own, share), :] = blocks_ref[own]
    others(seqs, seq, lambda peer: block_share(seq, own, peer).start())
    buf[own] = x_ref[...]
    others(seqs, seq, lambda peer: tile_to_seq(peer, peer).wait_recv())
    others(group, own, lambda peer: tiles_to_group(peer, own).start())
    for item in unit_loads:
        item.wait()
    cell = units.shape[2] // 2 // seqs
    for member in range(group):
        for run in range(seqs):
            home = (run * group + member) * cell
            for index, source in enumerate((gate, up)):
                first = (index * seqs + run) * cell
                units[member, :, first : first + cell] = source[:, home : home + cell]
    units_kept = pltpu.make_async_copy(units, units_ref, unit_sem.at[2])
    units_kept.start()

    def pass_block(member):
        block_swap(member, member).wait_recv()
        others(seqs, seq, lambda peer: block_share(seq, member, peer).start())

    others(group, own, pass_block)
    others(group, own, lambda peer: tiles_to_group(peer, peer).wait_recv())
    for column in range(width // 128):
        total = 0.0
        for place in range(column * per, (column + 1) * per):
            total = total + gains[place % group, place // group, 0:1, :]
        gain[0:1, column * 128 : (column + 1) * 128] = total

    def kept(slot, batch):
        return pltpu.make_async_copy(
            normed.at[slot, pl.ds(batch * piece, piece)],
            g_ref.at[batch, rows_at(slot, piece)],
            keep.at[slot, batch],
        )

    def use(slot):
        @pl.loop(0, x_ref.shape[0] // 64)
        def _(chunk):
            rows = rows_at(chunk, 64)
            values = buf[slot, rows, :].astype(jnp.float32)
            normed[slot, rows, :] = to_half(normalize(values, gain[0:1, :]))

        for batch in range(batches):
            kept(slot, batch).start()
        rows = rows_at(slot, piece)
        got = to_half(dot_nn(normed[slot], w[...]))
        for batch in range(batches):
            mine = got[batch * piece : (batch + 1) * piece]
            q_ref[batch, rows, :] = mine[:, :span]
            kv_ref[batch, rows, :] = mine[:, span:]

    pl.loop(1, chips - 1)(spread.relay)

    def have_block(run, member):
        block_share(run, member, seq).wait_recv()

    others(seqs, seq, lambda run: pl.loop(0, group)(lambda member: have_block(run, member)))
    w_kept = pltpu.make_async_copy(w, w_out_ref, w_keep)
    w_kept.start()
    gains_kept = pltpu.make_async_copy(gains, gains_ref, gain_keep)
    gains_kept.start()

    pl.loop(0, chips - 1)(lambda far: spread.each(far, use))
    spread.relay(chips - 1)
    spread.each(chips - 1, use)
    spread.each(chips, use)
    spread.sent()
    others(seqs, seq, lambda peer: tile_to_seq(peer, seq).wait_send())
    others(group, own, lambda peer: block_swap(peer, own).wait_send())
    others(group, own, lambda peer: tiles_to_group(peer, own).wait_send())
    others(
        seqs,
        seq,
        lambda peer: pl.loop(0, group)(lambda member: block_share(seq, member, peer).wait_send()),
    )
    w_kept.wait()
    gains_kept.wait()
    units_kept.wait()

    @pl.loop(0, group)
    def _(slot):
        for batch in range(batches):
            kept(slot, batch).wait()


def start(seqs, chips, batches, tile, x, weights, unit_weights, collective):
    rows, width = x.shape
    group = 2 * chips
    length = group * rows // batches
    share = weights[0].shape[0]
    span = width // group
    cols = 3 * span
    wide = unit_weights[0].shape[1]
    half = jnp.bfloat16
    return pl.pallas_call(
        functools.partial(start_kernel, seqs, chips, batches),
        out_shape=[
            jax.ShapeDtypeStruct((batches, length, width), half),
            jax.ShapeDtypeStruct((batches, length, span), half),
            jax.ShapeDtypeStruct((batches, length, 2 * span), half),
            jax.ShapeDtypeStruct((group, seqs, 8, 128), jnp.float32),
            jax.ShapeDtypeStruct((width, cols), half),
            jax.ShapeDtypeStruct((group, share, 2 * wide // group), half),
        ],
        in_specs=[VMEM_SPEC] * 5 + [ANY_SPEC] * 2,
        out_specs=[ANY_SPEC, VMEM_SPEC, VMEM_SPEC, ANY_SPEC, ANY_SPEC, ANY_SPEC],
        scratch_shapes=[
            pltpu.VMEM((share, wide), half),
            pltpu.VMEM((share, wide), half),
            pltpu.VMEM((group, share, 2 * wide // group), half),
            sems(3),
            pltpu.VMEM((group, share, cols), half),
            pltpu.VMEM((group, rows, width), half),
            pltpu.VMEM((group, rows, width), half),
            pltpu.VMEM((8, width), jnp.float32),
            pltpu.VMEM((group, seqs, 8, 128), jnp.float32),
            pltpu.VMEM((width, cols), half),
            sems(3, group, PARTS),
            sems(group, PARTS),
            sems(group, batches),
            sems(group),
            sems(seqs, group),
            sems(seqs, group),
            sems(seqs),
            sems(group),
            sems(seqs),
            sems(group),
            pltpu.SemaphoreType.DMA,
            pltpu.SemaphoreType.DMA,
        ],
        compiler_params=comm_params(collective),
        cost_estimate=cost(2 * group * rows * width * cols, 200 * MIB, group * rows * width * 2),
        name="start",
    )(tile, x, *weights, *unit_weights)


def attend_kernel(
    seqs, group, block, q_ref, kv_ref, low_ref, units_ref, out_ref, lse_ref, pad_ref, own_units_ref,
    pad, vt_ref, halo_send, halo_recv, pad_keep, swap_send, swap_recv, swap_keep,
):
    seq = lax.axis_index("seq")
    batches, length, span = q_ref.shape
    has_left, has_right = seq > 0, seq < seqs - 1
    pl.when(has_left)(lambda: signal_seq(seq - 1))
    pl.when(has_right)(lambda: signal_seq(seq + 1))
    meet(greet_group(group) + has_left.astype(jnp.int32) + has_right.astype(jnp.int32))

    steps, need = length // block, WINDOW // block

    def halo(batch, step, peer):
        return pltpu.make_async_remote_copy(
            src_ref=kv_ref.at[batch, rows_at(step + steps - need, block)],
            dst_ref=pad.at[batch, rows_at(step, block)],
            send_sem=halo_send.at[batch, step],
            recv_sem=halo_recv.at[batch, step],
            device_id={"seq": peer},
            device_id_type=MESH,
        )

    def send_halo(turn):
        batch, step = turn // need, need - 1 - lax.rem(turn, need)
        pl.when(has_right)(lambda: halo(batch, step, seq + 1).start())

    def halo_sent(turn):
        batch, step = turn // need, need - 1 - lax.rem(turn, need)
        pl.when(has_right)(lambda: halo(batch, step, seq + 1).wait_send())

    send_halo(0)
    send_halo(1)
    swap = Swap(group, units_ref, own_units_ref, swap_send, swap_recv, swap_keep)
    swap.begin()
    pad[:, WINDOW:, :] = kv_ref[...]

    @pl.when(jnp.logical_not(has_left))
    def _():
        pad[:, :WINDOW, :] = jnp.zeros((batches, WINDOW, 2 * span), jnp.bfloat16)

    def kept(batch):
        return pltpu.make_async_copy(pad.at[batch], pad_ref.at[batch], pad_keep.at[batch])

    vt = vt_ref
    for batch in range(batches):
        vt[:, WINDOW:] = pad[batch, WINDOW:, span:].T

        @pl.loop(0, steps)
        def _(turn, batch=batch):
            step = steps - 1 - turn

            @pl.when(step < need)
            def _():
                rows = rows_at(step, block)
                pl.when(has_left)(lambda: halo(batch, step, seq).wait_recv())
                vt[:, rows] = pad[batch, rows, span:].T
                place = batch * need + need - 1 - step
                halo_sent(place)
                pl.when(place + 2 < batches * need)(lambda: send_halo(place + 2))

            begin = pl.multiple_of(step * block, block)
            keys = pl.ds(begin, block + WINDOW)
            rows = pl.ds(begin, block)
            low = low_ref[batch, :, rows]
            for pair in range(span // PAIR):
                lanes = slice(pair * PAIR, (pair + 1) * PAIR)
                q_pair = q_ref[batch, rows, lanes] * jnp.asarray(HEAD**-0.5, jnp.bfloat16)
                k_rows = pad[batch, keys, lanes]
                values = vt[lanes, keys]
                mixed = []
                for half in range(2):
                    scores = masked_scores(k_rows, head_lanes(q_pair, half), low)
                    top = jnp.max(scores, axis=0, keepdims=True)
                    expo = jnp.exp(scores - top)
                    total = jnp.sum(expo, axis=0, keepdims=True)
                    mixed.append(dot_nn(values, to_half(expo)) / total)
                    row = pair * 2 + half
                    lse_ref[batch, row : row + 1, rows] = top + jnp.log(total)
                lane = lax.broadcasted_iota(jnp.int32, mixed[0].shape, 0)
                out_ref[batch, rows, lanes] = to_half(jnp.where(lane < HEAD, mixed[0], mixed[1]).T)

    for batch in range(batches):
        kept(batch).start()
    swap.end()
    for batch in range(batches):
        kept(batch).wait()


def attend(seqs, group, query, key_value, low, block, units, collective):
    batches, length, span = query.shape
    padded = length + WINDOW
    heads = span // HEAD
    half = jnp.bfloat16
    return pl.pallas_call(
        functools.partial(attend_kernel, seqs, group, block),
        in_specs=[VMEM_SPEC, VMEM_SPEC, VMEM_SPEC, ANY_SPEC],
        out_specs=[VMEM_SPEC, VMEM_SPEC, ANY_SPEC, ANY_SPEC],
        out_shape=[
            jax.ShapeDtypeStruct((batches, length, span), half),
            jax.ShapeDtypeStruct((batches, heads, length), jnp.float32),
            jax.ShapeDtypeStruct((batches, padded, 2 * span), half),
            jax.ShapeDtypeStruct(units.shape, half),
        ],
        scratch_shapes=[
            pltpu.VMEM((batches, padded, 2 * span), half),
            pltpu.VMEM((span, padded), half),
            sems(batches, WINDOW // block),
            sems(batches, WINDOW // block),
            sems(batches),
            sems(group),
            sems(group),
            pltpu.SemaphoreType.DMA,
        ],
        compiler_params=comm_params(collective),
        cost_estimate=cost(
            8 * batches * length * span * (WINDOW + block), 150 * MIB, units.size * 2
        ),
        name="attend",
    )(query, key_value, low, units)


def branch_kernel(
    seqs, chips, a_ref, w_ref, d_ref, units_ref, x_ref, gain_ref, middle_ref, normed_ref, gd_ref, w_units_ref,
    out_ref, acc, cross_out, line_out, cross_in, line_in, sum_send, sum_recv,
    send, recv, d_keep, share_send, share_recv, share_keep,
):
    line = Line(chips)
    rows = out_ref.shape[0]

    def product(slot, tile):
        return dot_nn(left_rows(a_ref, slot, rows), w_ref[:, rows_at(tile, TILE)])

    meet(line.greet() + greet_seq(seqs))
    reduce = Reduce(
        line, product, out_ref, acc, cross_out, line_out, cross_in, line_in, sum_send, sum_recv
    )
    spread = Spread(line, d_ref, gd_ref, send, recv)
    units = Share(seqs, units_ref, w_units_ref, share_send, share_recv, share_keep)
    d_kept = pltpu.make_async_copy(d_ref, gd_ref.at[line.own], d_keep)
    units.begin()
    spread.begin()
    d_kept.start()

    @pl.loop(0, chips)
    def _(step):
        def also(tile):
            pl.when(step < chips - 1)(lambda: spread.relay_part(step + 1, tile))

        reduce.level(chips - 1 - step, also)
        pl.when(step == chips - 2)(units.pass_on)

    @pl.loop(0, rows // 32)
    def _(chunk):
        here = rows_at(chunk, 32)
        middle = x_ref[here, :].astype(jnp.float32) + out_ref[here, :]
        middle_ref[here, :] = middle
        normed_ref[here, :] = to_half(normalize(middle, gain_ref[0:1, :]))

    spread.rest()
    spread.sent()
    reduce.sent()
    d_kept.wait()
    units.end()


def branch_sum(seqs, chips, a, w, d_rows, units, x, gain, collective):
    rows, width = d_rows.shape
    group = 2 * chips
    half = jnp.bfloat16
    return pl.pallas_call(
        functools.partial(branch_kernel, seqs, chips),
        out_shape=[
            jax.ShapeDtypeStruct((rows, width), jnp.float32),
            jax.ShapeDtypeStruct((rows, width), half),
            jax.ShapeDtypeStruct((group, rows, width), half),
            jax.ShapeDtypeStruct((seqs,) + units.shape, half),
        ],
        in_specs=[VMEM_SPEC, VMEM_SPEC, ANY_SPEC, ANY_SPEC, VMEM_SPEC, VMEM_SPEC],
        out_specs=[VMEM_SPEC, VMEM_SPEC, ANY_SPEC, ANY_SPEC],
        scratch_shapes=[pltpu.VMEM((rows, width), jnp.float32)]
        + Reduce.scratch(chips, rows, width)
        + [sems(3, group, PARTS), sems(group, PARTS), pltpu.SemaphoreType.DMA]
        + [sems(seqs, 2), sems(seqs, 2), pltpu.SemaphoreType.DMA],
        compiler_params=comm_params(collective),
        cost_estimate=cost(
            2 * group * rows * width * w.shape[0], 250 * MIB, 3 * group * rows * width * 2
        ),
        name="branch_sum",
    )(a, w, d_rows, units, x, gain)


class PairReduce:
    def __init__(self, line, product, out, acc, keep, cross_out, cross_in, line_out, line_in, send, recv):
        self.line, self.product, self.out, self.acc, self.keep = line, product, out, acc, keep
        self.cross_out, self.cross_in, self.line_out, self.line_in = cross_out, cross_in, line_out, line_in
        self.send, self.recv = send, recv
        self.tiles = keep.shape[1] // TILE

    @staticmethod
    def scratch(chips, piece, width):
        half = jnp.bfloat16
        return [
            pltpu.VMEM((piece, width), half),
            pltpu.VMEM((2, piece, width), half),
            pltpu.VMEM((2, piece, width), half),
            pltpu.VMEM((chips + 1, piece, width), half),
            pltpu.SemaphoreType.DMA((3, width // TILE)),
            pltpu.SemaphoreType.DMA((chips + 3, width // TILE)),
        ]

    def cross(self, parity, tile):
        here = rows_at(tile, TILE)
        return pltpu.make_async_remote_copy(
            src_ref=self.cross_out.at[:, here],
            dst_ref=self.cross_in.at[parity, :, here],
            send_sem=self.send.at[0, tile],
            recv_sem=self.recv.at[self.line.chips + 1 + parity, tile],
            device_id={"fsdp": self.line.other},
            device_id_type=MESH,
        )

    def along(self, parity, landing, tile, peer):
        here = rows_at(tile, TILE)
        return pltpu.make_async_remote_copy(
            src_ref=self.line_out.at[parity, :, here],
            dst_ref=self.line_in.at[landing, :, here],
            send_sem=self.send.at[1 + parity, tile],
            recv_sem=self.recv.at[landing, tile],
            device_id={"fsdp": peer},
            device_id_type=MESH,
        )

    def steps(self):
        return 2 * self.line.chips - 1

    def step(self, step):
        line, keep = self.line, self.keep
        piece = keep.shape[0]
        right_side = line.chips - 1 - line.chip
        away = line.chips - 1 - step // 2
        second = lax.rem(step, 2)
        rightward = (right_side >= line.chip) == (second == 0)
        place = line.chip + jnp.where(rightward, away, -away)
        longer = jnp.maximum(right_side, line.chip)
        shorter = jnp.minimum(right_side, line.chip)
        count = longer - away + jnp.maximum(shorter - away, 0) + second
        parity = lax.rem(count + 2 * line.chips, 2)
        upstream = (rightward & line.has_left) | (jnp.logical_not(rightward) & line.has_right)

        @pl.when((place >= 0) & (place < line.chips))
        def _():
            wide = self.acc.shape[1]

            @pl.loop(0, keep.shape[1] // wide)
            def _(tile):
                here = rows_at(tile, wide)
                self.acc[...] = self.product(place, here)
                self.cross_out[:, here] = to_half(self.acc[rows_at(1 - line.core, piece), :])
                keep[:, here] = self.acc[rows_at(line.core, piece), :]
                for piece_of in range(wide // TILE):
                    self.cross(parity, tile * (wide // TILE) + piece_of).start()

            @pl.loop(0, self.tiles)
            def _(tile):
                here = rows_at(tile, TILE)
                self.cross(parity, tile).wait()
                keep[:, here] += self.cross_in[parity, :, here].astype(jnp.float32)

                @pl.when(away > 0)
                def _():
                    pl.when(count >= 2)(
                        lambda: self.along(parity, place, tile, line.own).wait_send()
                    )

                    @pl.when(upstream)
                    def _():
                        self.along(parity, place, tile, line.own).wait_recv()
                        self.line_out[parity, :, here] = to_half(
                            keep[:, here] + self.line_in[place, :, here].astype(jnp.float32)
                        )

                    @pl.when(jnp.logical_not(upstream))
                    def _():
                        self.line_out[parity, :, here] = to_half(keep[:, here])

                    @pl.when(rightward)
                    def _():
                        self.along(parity, place, tile, line.own + 2).start()

                    @pl.when(jnp.logical_not(rightward))
                    def _():
                        landing = jnp.where(away == 1, line.chips, place)
                        self.along(parity, landing, tile, line.own - 2).start()

                @pl.when(away == 0)
                def _():
                    self.out[:, here] = keep[:, here]

                    @pl.when(line.has_left)
                    def _():
                        self.along(parity, place, tile, line.own).wait_recv()
                        self.out[:, here] += self.line_in[place, :, here].astype(jnp.float32)

                    @pl.when(line.has_right)
                    def _():
                        self.along(parity, line.chips, tile, line.own).wait_recv()
                        self.out[:, here] += self.line_in[line.chips, :, here].astype(jnp.float32)

    def sent(self):
        for count in range(max(self.line.chips - 3, 0), self.line.chips - 1):
            pl.loop(0, self.tiles)(
                lambda tile, parity=count % 2: self.along(parity, 0, tile, self.line.own).wait_send()
            )


def feed_kernel(
    seqs, chips, batches, x_ref, w_hbm, wd_hbm, gd_hbm, v_ref, cot_ref, gain_ref,
    dm_ref, db_ref, gain_grad_ref, hidden_hbm, grad_hbm, grad_in,
    buf, d_buf, h_buf, w_ref, wd_ref, d_ref, tiles, totals, acc, keep,
    load, d_sem, h_sem, tile_sem, send, recv, part_send, part_recv, *sums,
):
    line = Line(chips)
    rows, width = x_ref.shape
    piece = rows // batches
    pair = 2 * piece
    units = wd_ref.shape[0]
    part = min(units, 2 * TILE)
    block = tiles.shape[1]
    loads = [
        pltpu.make_async_copy(w_hbm, w_ref, load.at[0]),
        pltpu.make_async_copy(wd_hbm, wd_ref, load.at[1]),
    ]
    for item in loads:
        item.start()
    meet(line.greet() + greet_seq(seqs))
    spreads = [
        Spread(
            line,
            x_ref.at[pl.ds(batch * piece, piece)],
            buf.at[batch],
            send.at[batch],
            recv.at[batch],
        )
        for batch in range(batches)
    ]
    spreads[0].begin()
    for batch in range(batches):
        buf[batch, line.own] = x_ref[batch * piece : (batch + 1) * piece, :]

    def fetch(batch, place, side):
        return [
            pltpu.make_async_copy(
                gd_hbm.at[place * 2 + core, pl.ds(batch * piece, piece)],
                d_buf.at[side, pl.ds(core * piece, piece)],
                d_sem.at[side, core],
            )
            for core in range(2)
        ]

    def stored(batch, place):
        return [
            pltpu.make_async_copy(
                h_buf.at[pl.ds(core * piece, piece)],
                hidden_hbm.at[
                    pl.ds(pl.multiple_of((place * 2 + core) * rows + batch * piece, piece), piece)
                ],
                h_sem.at[core],
            )
            for core in range(2)
        ]

    def sides(far, act):
        @pl.loop(0, 2)
        def _(side):
            place = line.chip + far * (2 * side - 1)
            valid = (place >= 0) & (place < chips) & ((side == 0) | (far > 0))
            pl.when(valid)(lambda: act(place, side))

    def take(batch, far):
        def begin(place, side):
            for item in fetch(batch, place, side):
                item.start()

        sides(far, begin)
        pl.when(far > 0)(lambda: spreads[batch].relay(far))

    def compute(batch, far):
        def act(place, side):
            spreads[batch].across(place * 2 + 1 - line.core)
            for item in fetch(batch, place, side):
                item.wait()

            def free():
                for item in stored(batch, place):
                    item.wait()

            if batch:
                free()
            else:
                pl.when((far > 0) | (side > 0))(free)
            there = rows_at(place, pair)

            @pl.loop(0, units // part)
            def _(tile):
                first = rows_at(tile, part)
                second = rows_at(units // part + tile, part)
                values = buf[batch, pl.ds(place * 2, 2), :, :].reshape(pair, width)
                gate = dot_nn(values, w_ref[:, first])
                up = dot_nn(values, w_ref[:, second])
                d_hidden = dot_nt(d_buf[side], wd_ref[first, :])
                sigma = jax.nn.sigmoid(gate)
                swish = gate * sigma
                h_buf[:, first] = to_half(swish * up)
                slope = sigma * (1.0 + gate * (1.0 - sigma))
                d_ref[batch, there, first] = to_half(d_hidden * up * slope)
                d_ref[batch, there, second] = to_half(d_hidden * swish)

            for item in stored(batch, place):
                item.start()

        sides(far, act)

    def product(batch):
        def get(place, here):
            return dot_nt(d_ref[batch, rows_at(place, pair), :], w_ref[here, :])

        return get

    reduces = [
        PairReduce(line, product(batch), totals.at[batch], acc, keep, *sums[6 * batch : 6 * batch + 6])
        for batch in range(batches)
    ]

    count = width // block
    seq = lax.axis_index("seq")

    near, far_off = seq_peers(seqs)
    soon = len(near)
    order = [peer * 2 for peer in near] + [peer * 2 for peer in far_off] + [seq * 2]
    order = order + [peer * 2 + 1 for peer in near] + [peer * 2 + 1 for peer in far_off] + [seq * 2 + 1]

    def tile_at(turn):
        tile = order[-1]
        for index in range(len(order) - 1):
            tile = jnp.where(turn == index, order[index], tile)
        return tile

    def grad_stored(turn):
        slot = lax.rem(turn, 2)
        return pltpu.make_async_copy(
            tiles.at[slot], grad_hbm.at[rows_at(tile_at(turn), block)], tile_sem.at[slot]
        )

    parts = ToPeers(seqs, near, grad_hbm, grad_in, part_send, part_recv)

    def leave(turn):
        grad_stored(turn).wait()
        for index in range(soon):
            pl.when(turn == index)(lambda index=index: parts.move(index).start())

    def weight_grad(turn):
        slot = lax.rem(turn, 2)
        size = min(4 * TILE, 2 * units)
        tile = tile_at(turn)

        @pl.loop(0, 2 * units // size)
        def _(column):
            here = rows_at(column, size)
            got = 0.0
            for batch in range(batches):
                left = buf[batch, :, :, rows_at(tile, block)].reshape(2 * chips * piece, block)
                got = got + contract_rows(left, d_ref[batch, :, here])
            tiles[slot, :, here] = to_half(got)

        pl.when(turn > 0)(lambda: leave(turn - 1))
        grad_stored(turn).start()

    def norm_batch(batch):
        own = pl.ds(batch * piece, piece)

        def put(here, d_values):
            there = pl.ds(pl.multiple_of(here.start + batch * piece, here.size), here.size)
            d_middle = cot_ref[there, :].astype(jnp.float32) + d_values
            dm_ref[there, :] = d_middle
            db_ref[there, :] = to_half(d_middle)

        norm_back(piece, v_ref.at[own], totals.at[batch], gain_ref, gain_grad_ref, put)

    gain_grad_ref[...] = jnp.zeros_like(gain_grad_ref)
    for item in loads:
        item.wait()
    last = 2 * chips - 2

    @pl.loop(0, chips)
    def _(far):
        take(0, far)
        pl.when(far == chips - 2)(spreads[1].begin)
        compute(0, far)

    @pl.loop(0, chips - 1)
    def _(far):
        take(1, far)
        reduces[0].step(2 * far)
        reduces[0].step(2 * far + 1)
        compute(1, far)

    take(1, chips - 1)
    compute(1, chips - 1)

    @pl.loop(0, 2)
    def _(step):
        reduces[1].step(step)
        weight_grad(step)

    reduces[0].step(last)
    norm_batch(0)

    @pl.loop(2, last)
    def _(step):
        reduces[1].step(step)
        pl.when(step < count)(lambda: weight_grad(step))

    @pl.loop(last, max(count, last))
    def _(tile):
        weight_grad(tile)

    reduces[1].step(last)
    norm_batch(1)
    for batch in range(batches):
        spreads[batch].sent()
        reduces[batch].sent()
    for item in stored(1, 0):
        item.wait()
    leave(count - 1)
    parts.end()


def feed_forward(seqs, chips, batches, x, w, wd, group_d, middle, cot, gain, collective):
    rows, width = x.shape
    group = 2 * chips
    units = wd.shape[0]
    piece = rows // batches
    block = width // seqs // 2
    half = jnp.bfloat16
    return pl.pallas_call(
        functools.partial(feed_kernel, seqs, chips, batches),
        out_shape=[
            jax.ShapeDtypeStruct((rows, width), jnp.float32),
            jax.ShapeDtypeStruct((rows, width), half),
            jax.ShapeDtypeStruct((8, width), jnp.float32),
            jax.ShapeDtypeStruct((group * rows, units), half),
            jax.ShapeDtypeStruct((width, 2 * units), half),
            jax.ShapeDtypeStruct((near_count(seqs), block, 2 * units), half),
        ],
        in_specs=[VMEM_SPEC] + [ANY_SPEC] * 3 + [VMEM_SPEC] * 3,
        out_specs=[VMEM_SPEC] * 3 + [ANY_SPEC] * 3,
        scratch_shapes=[
            pltpu.VMEM((batches, group, piece, width), half),
            pltpu.VMEM((2, 2 * piece, width), half),
            pltpu.VMEM((2 * piece, units), half),
            pltpu.VMEM(w.shape, half),
            pltpu.VMEM(wd.shape, half),
            pltpu.VMEM((batches, group * piece, 2 * units), half),
            pltpu.VMEM((2, block, 2 * units), half),
            pltpu.VMEM((batches, piece, width), jnp.float32),
            pltpu.VMEM((2 * piece, 2 * TILE), jnp.float32),
            pltpu.VMEM((piece, width), jnp.float32),
            sems(2),
            sems(2, 2),
            sems(2),
            sems(2),
            sems(batches, 3, group, PARTS // 2),
            sems(batches, group, PARTS // 2),
            sems(seqs),
            sems(seqs),
        ]
        + PairReduce.scratch(chips, piece, width) * batches,
        compiler_params=comm_params(collective, 63),
        cost_estimate=cost(
            14 * group * rows * width * units, 400 * MIB, 2 * group * rows * width * 2
        ),
        name="feed_forward",
    )(x, w, wd, group_d, middle, cot, gain)


def branch_back_kernel(
    seqs, chips, batches, x_ref, w_ref, att_ref, middle_ref, hidden_hbm, wd_hbm, units_hbm, gd_hbm,
    d_ref, layer_ref, out_grad_ref, half_in, whole_in, down_hbm, down_in,
    out_ref, buf, hidden_ref, wd_ref, grad_acc, rights, tiles, send, recv, load, right_sem, tile_sem,
    part_send, part_recv, down_send, down_recv, down_keep, acc, cross_out, line_out, cross_in, line_in, sum_send, sum_recv,
):
    line = Line(chips)
    rows = x_ref.shape[0]
    piece = rows // batches
    width = x_ref.shape[1]
    loads = [
        pltpu.make_async_copy(hidden_hbm, hidden_ref, load.at[0]),
        pltpu.make_async_copy(wd_hbm, wd_ref, load.at[1]),
    ]
    for item in loads:
        item.start()

    def product(slot, tile):
        return dot_nn(left_rows(hidden_ref, slot, rows), wd_ref[:, rows_at(tile, TILE)])

    part = rights.shape[2]
    count = width // part

    def right(tile):
        slot = lax.rem(tile, 2)
        return pltpu.make_async_copy(
            gd_hbm.at[:, rows_at(tile, part)], rights.at[slot], right_sem.at[slot]
        )

    def stored(tile):
        slot = lax.rem(tile, 2)
        return pltpu.make_async_copy(
            tiles.at[slot], down_hbm.at[:, rows_at(tile, part)], tile_sem.at[slot]
        )

    def weight_grad(tile):
        right(tile).wait()
        pl.when(tile + 1 < count)(lambda: right(tile + 1).start())
        pl.when(tile >= 2)(lambda: stored(tile - 2).wait())
        slot = lax.rem(tile, 2)
        size = min(TILE, hidden_ref.shape[1])

        @pl.loop(0, hidden_ref.shape[1] // size)
        def _(row):
            here = rows_at(row, size)
            tiles[slot, here, :] = to_half(contract_rows(hidden_ref[:, here], rights[slot]))

        stored(tile).start()

    right(0).start()
    meet(line.greet() + greet_seq(seqs))
    near, far_off = seq_peers(seqs)
    soon = len(near)
    halves = ToPeers(
        seqs, near, units_hbm, half_in, part_send.at[0], part_recv.at[0], half_in.shape[1]
    )
    wholes = ToPeers(seqs, far_off, units_hbm, whole_in, part_send.at[1], part_recv.at[1])
    down = ToPeers(
        seqs, near, down_hbm, down_in.at[pl.ds(0, soon)], down_send, down_recv
    )
    down_kept = pltpu.make_async_copy(
        down_hbm.at[rows_at(lax.axis_index("seq"), down_in.shape[1])], down_in.at[soon], down_keep
    )
    spread = Spread(line, x_ref, buf, send, recv)
    reduce = Reduce(
        line, product, out_ref, acc, cross_out, line_out, cross_in, line_in, sum_send, sum_recv
    )
    spread.begin()
    halves.begin()
    wholes.begin()
    buf[line.own] = x_ref[...]
    grad_acc[...] = jnp.zeros_like(grad_acc)

    def use(slot):
        got = to_half(dot_nt(buf[slot], w_ref[...]))
        for batch in range(batches):
            d_ref[batch, rows_at(slot, piece), :] = got[batch * piece : (batch + 1) * piece]
        mixed = left_rows(att_ref, slot, rows)

        @pl.loop(0, width // TILE)
        def _(tile):
            here = rows_at(tile, TILE)
            grad_acc[:, here] += contract_rows(mixed, buf[slot, :, here])

    for item in loads:
        item.wait()

    reduce.level(chips - 1, lambda tile: None)
    pl.loop(0, count)(weight_grad)
    stored(count - 2).wait()
    stored(count - 1).wait()
    down.begin()
    down_kept.start()
    spread.relay(1)
    spread.each(0, use)

    @pl.loop(1, chips)
    def _(step):
        def also(tile):
            pl.when(step < chips - 1)(lambda: spread.relay_part(step + 1, tile))

        reduce.level(chips - 1 - step, also)
        spread.each(step, use)

    spread.each(chips, use)

    @pl.loop(0, rows // 32)
    def _(chunk):
        here = rows_at(chunk, 32)
        layer_ref[here, :] = to_half(middle_ref[here, :] + out_ref[here, :])

    out_grad_ref[...] = to_half(grad_acc[...])
    spread.sent()
    reduce.sent()
    halves.end()
    wholes.end()
    down.end()
    down_kept.wait()


def branch_back(seqs, chips, batches, x, w, attended, middle, hidden, wd, unit_part, group_d, collective):
    rows, width = x.shape
    group = 2 * chips
    length = group * rows // batches
    span = w.shape[0]
    half = jnp.bfloat16
    part = 256 if group * rows <= 2048 else 128
    near, run = near_count(seqs), width // seqs
    return pl.pallas_call(
        functools.partial(branch_back_kernel, seqs, chips, batches),
        out_shape=[
            jax.ShapeDtypeStruct((batches, length, span), half),
            jax.ShapeDtypeStruct((rows, width), half),
            jax.ShapeDtypeStruct((span, width), half),
            jax.ShapeDtypeStruct((near, run // 2, unit_part.shape[1]), half),
            jax.ShapeDtypeStruct((seqs - 1 - near, run, unit_part.shape[1]), half),
            jax.ShapeDtypeStruct((wd.shape[0], width), half),
            jax.ShapeDtypeStruct((near + 1, wd.shape[0] // seqs, width), half),
        ],
        in_specs=[VMEM_SPEC] * 4 + [ANY_SPEC] * 4,
        out_specs=[VMEM_SPEC, VMEM_SPEC, VMEM_SPEC, ANY_SPEC, ANY_SPEC, ANY_SPEC, ANY_SPEC],
        scratch_shapes=[
            pltpu.VMEM((rows, width), jnp.float32),
            pltpu.VMEM((group, rows, width), half),
            pltpu.VMEM(hidden.shape, half),
            pltpu.VMEM(wd.shape, half),
            pltpu.VMEM((span, width), jnp.float32),
            pltpu.VMEM((2, group * rows, part), half),
            pltpu.VMEM((2, wd.shape[0], part), half),
            sems(3, group, PARTS),
            sems(group, PARTS),
            sems(2),
            sems(2),
            sems(2),
            sems(2, seqs),
            sems(2, seqs),
            sems(seqs),
            sems(seqs),
            pltpu.SemaphoreType.DMA,
        ]
        + Reduce.scratch(chips, rows, width),
        compiler_params=comm_params(collective, 62),
        cost_estimate=cost(
            2 * group * rows * width * (2 * span + 2 * wd.shape[0]),
            250 * MIB,
            2 * group * rows * width * 2,
        ),
        name="branch_back",
    )(x, w, attended, middle, hidden, wd, unit_part, group_d.reshape(group * rows, width))


def attention_back_kernel(
    seqs, chips, block, q_ref, pad_ref, low_ref, lse_ref, d_ref, part_hbm, in_one, in_two, in_far,
    w_ref, g_hbm, v_ref, dm_hbm, gain_ref, mlp_gain_ref, out_ref, down_hbm,
    grad_hbm, wq_ref, wk_ref, wv_ref, wo_hbm, tile_ref, gate_hbm, up_hbm, down_in,
    grad_ref, wo_ref, gate_ref, up_ref, result_sem, down_send, down_recv,
    dk, dv, kt, heads, back_out, back_in, unit_parts, unit_sums, units, lefts, parts, sums, cols, out_in,
    totals, gain_acc, gain_out, gain_in, gain_sum, gain_back, acc, keep,
    halo_send, halo_recv, unit_load, unit_send, unit_recv, unit_keep, dm_load, left_sem,
    part_send, part_recv, cols_send, cols_recv, out_send, out_recv,
    gain_send, gain_recv, back_send, back_recv, *line_sums,
):
    line = Line(chips)
    group = 2 * chips
    seq = lax.axis_index("seq")
    own = line.own
    batches, length, span = q_ref.shape
    rows, width = v_ref.shape
    piece = rows // batches
    pair_rows = 2 * piece
    depth = 3 * span
    run = width // seqs
    share = run // group
    part = lefts.shape[3]
    steps, need = length // block, WINDOW // block
    first = length - WINDOW
    has_left, has_right = seq > 0, seq < seqs - 1
    scale = jnp.asarray(HEAD**-0.5, jnp.bfloat16)

    def others(count, me, act):
        pl.loop(1, count)(lambda ahead: act(lax.rem(me + ahead, count)))

    def unit_loaded(turn, place, source):
        slot = lax.rem(turn, 2)
        return pltpu.make_async_copy(source, unit_parts.at[slot, place], unit_load.at[slot, place])

    def load_units(turn):
        member = lax.rem(own + turn, group)
        unit_loaded(turn, 0, part_hbm.at[rows_at(seq * group + member, share)]).start()
        soon = in_one.shape[0]
        for index in range(seqs - 1):

            def fetch(source, index=index):
                unit_loaded(turn, index + 1, source).start()

            if index < soon:

                @pl.when(member < chips)
                def _(index=index, fetch=fetch):
                    fetch(in_one.at[index, rows_at(member, share)])

                @pl.when(member >= chips)
                def _(index=index, fetch=fetch):
                    fetch(in_two.at[index, rows_at(member - chips, share)])

            else:
                fetch(in_far.at[index - soon, rows_at(member, share)])

    load_units(1)
    dm_loaded = pltpu.make_async_copy(dm_hbm, grad_ref, dm_load)
    dm_loaded.start()
    meet(greet_group(group) + greet_seq(seqs))
    near, far_off = seq_peers(seqs)
    down = ToPeers(seqs, far_off, down_hbm, down_in, down_send, down_recv)
    down.begin()
    swap = Swap(group, unit_sums, units, unit_send, unit_recv, unit_keep)

    @pl.loop(1, group + 1)
    def _(turn):
        member = lax.rem(own + turn, group)
        slot = lax.rem(turn, 2)
        pl.when(turn < group)(lambda: load_units(turn + 1))
        for place in range(seqs):
            unit_loaded(turn, place, part_hbm.at[rows_at(0, share)]).wait()

        @pl.loop(0, share // 16)
        def _(chunk):
            here = rows_at(chunk, 16)
            added = unit_parts[slot, 0, here, :].astype(jnp.float32)
            for place in range(1, seqs):
                added = added + unit_parts[slot, place, here, :].astype(jnp.float32)
            unit_sums[member, here, :] = to_half(added)

        pl.when(turn < group)(lambda: swap.move(member, own).start())
        pl.when(turn == group)(lambda: swap.kept().start())

    def halo(batch, step, peer):
        here = rows_at(step, block)
        return pltpu.make_async_remote_copy(
            src_ref=back_out.at[batch, here],
            dst_ref=back_in.at[batch, here],
            send_sem=halo_send.at[batch, step],
            recv_sem=halo_recv.at[batch, step],
            device_id={"seq": peer},
            device_id_type=MESH,
        )

    def attend_block(batch, step):
        begin = pl.multiple_of(step * block, block)
        keys = pl.ds(begin, block + WINDOW)
        rows = pl.ds(begin, block)
        low = low_ref[batch, :, rows]
        for pair in range(span // PAIR):
            lanes = slice(pair * PAIR, (pair + 1) * PAIR)
            q_pair = q_ref[batch, rows, lanes] * scale
            d_pair = d_ref[batch, rows, lanes]
            k_rows = pad_ref[batch, keys, lanes]
            v_rows = pad_ref[batch, keys, span + pair * PAIR : span + (pair + 1) * PAIR]
            k_cols = kt[lanes, keys]
            back = []
            for half in range(2):
                row = pair * 2 + half
                q_head = head_lanes(q_pair, half)
                d_head = head_lanes(d_pair, half)
                scores = masked_scores(k_rows, q_head, low)
                probs = jnp.exp(scores - lse_ref[batch, row : row + 1, rows])
                d_probs = dot_nt(v_rows, d_head)
                along = jnp.sum(probs * d_probs, axis=0, keepdims=True)
                d_scores = to_half(probs * (d_probs - along))
                dv[keys, lanes] += dot_nn(to_half(probs), d_head)
                dk[keys, lanes] += dot_nn(d_scores, q_head)
                back.append(dot_nn(k_cols, d_scores))
            at = lax.broadcasted_iota(jnp.int32, back[0].shape, 0)
            heads[batch, rows, lanes] = to_half(
                jnp.where(at < HEAD, back[0], back[1]).T
            )


        @pl.when(has_left & (step < need))
        def _():
            back_out[batch, rows, :span] = to_half(dk[rows, :])
            back_out[batch, rows, span:] = to_half(dv[rows, :])
            halo(batch, step, seq - 1).start()

        @pl.when(step == steps - 1)
        def _():
            heads[batch, :, span : 2 * span] = to_half(dk[WINDOW:, :])
            heads[batch, :, 2 * span :] = to_half(dv[WINDOW:, :])

    def add_halo(batch):
        @pl.when(has_right)
        def _():
            @pl.loop(0, need)
            def _(step):
                there = pl.ds(pl.multiple_of(step * block + first, block), block)
                halo(batch, step, seq).wait_recv()
                got = back_in[batch, rows_at(step, block), :].astype(jnp.float32)
                mine = heads[batch, there, span:].astype(jnp.float32)
                heads[batch, there, span:] = to_half(mine + got)

    def product(batch):
        def get(place, here):
            return dot_nt(heads[batch, rows_at(place, pair_rows), :], w_ref[here, :])

        return get

    reduces = [
        PairReduce(
            line, product(batch), totals.at[batch], acc, keep, *line_sums[6 * batch : 6 * batch + 6]
        )
        for batch in range(batches)
    ]
    last = 2 * chips - 2

    @pl.loop(0, 2 * steps)
    def _(turn):
        batch, step = turn // steps, lax.rem(turn, steps)

        @pl.when(step == 0)
        def _():
            kt[...] = pad_ref[batch, :, :span].T * scale
            dk[...] = jnp.zeros_like(dk)
            dv[...] = jnp.zeros_like(dv)

        attend_block(batch, step)
        after = turn - steps - 1
        pl.when(after == 0)(lambda: add_halo(0))

        @pl.when((after >= 0) & (2 * after < last))
        def _():
            reduces[0].step(2 * after)
            reduces[0].step(2 * after + 1)

    for after in range(steps - 1, chips - 1):
        reduces[0].step(2 * after)
        reduces[0].step(2 * after + 1)

    def left(tile):
        slot = lax.rem(tile, 2)
        return pltpu.make_async_copy(
            g_hbm.at[:, :, rows_at(tile, part)], lefts.at[slot], left_sem.at[slot]
        )

    heads_near = ToPeers(seqs, near + far_off, parts, sums, part_send, part_recv)
    left(0).start()
    add_halo(1)

    @pl.loop(0, width // part)
    def _(tile):
        left(tile).wait()
        pl.when(tile + 1 < width // part)(lambda: left(tile + 1).start())
        slot = lax.rem(tile, 2)
        got = contract_rows(lefts[slot, 0], heads[0])
        for batch in range(1, batches):
            got = got + contract_rows(lefts[slot, batch], heads[batch])
        parts[rows_at(tile, part), :] = to_half(got)

    heads_near.begin()
    from_seq = ToPeers(seqs, near + far_off, out_ref, out_in, out_send, out_recv)
    from_seq.begin()
    gain_acc[...] = jnp.zeros_like(gain_acc)
    dm_loaded.wait()

    def norm_batch(batch):
        mine = pl.ds(batch * piece, piece)

        def put(here, d_values):
            there = pl.ds(pl.multiple_of(here.start + batch * piece, here.size), here.size)
            grad_ref[there, :] += d_values

        norm_back(piece, v_ref.at[mine], totals.at[batch], gain_ref, gain_acc, put)

    pl.loop(0, 2)(reduces[1].step)
    reduces[0].step(last)
    norm_batch(0)
    pl.loop(2, last)(reduces[1].step)
    swap.end()
    cell = units.shape[2] // 2 // seqs
    for member in range(group):
        for place in range(seqs):
            column = (place * group + member) * cell
            for target, begin in ((gate_ref, 0), (up_ref, seqs * cell)):
                here = slice(begin + place * cell, begin + (place + 1) * cell)
                target[:, column : column + cell] = units[member, :, here]

    results = [
        pltpu.make_async_copy(source, target, result_sem.at[index])
        for index, (source, target) in enumerate(
            ((gate_ref, gate_hbm), (up_ref, up_hbm), (wo_ref, wo_hbm), (grad_ref, grad_hbm))
        )
    ]
    results[0].start()
    results[1].start()

    def block_swap(peer, member):
        return pltpu.make_async_remote_copy(
            src_ref=parts.at[rows_at(seq * group + peer, share)],
            dst_ref=cols.at[member],
            send_sem=cols_send.at[peer],
            recv_sem=cols_recv.at[member],
            device_id={"fsdp": peer},
            device_id_type=MESH,
        )

    heads_near.arrived()

    @pl.loop(0, run // 64)
    def _(chunk):
        here = rows_at(chunk, 64)
        there = pl.ds(pl.multiple_of(seq * run + chunk * 64, 64), 64)
        parts[there, :] = to_half(add_from_seq(parts[there, :], sums, here))

    others(group, own, lambda peer: block_swap(peer, own).start())
    cols[own] = parts[rows_at(seq * group + own, share), :]
    from_seq.arrived()
    out_rows = out_in.shape[1]
    wo_ref[...] = add_from_seq(out_ref[rows_at(seq, out_rows), :], out_in, slice(None))
    results[2].start()
    reduces[1].step(last)
    norm_batch(1)
    results[3].start()
    fold = 128 // share
    near = group // fold
    attn_row = jnp.sum(gain_acc[...], axis=0, keepdims=True)
    mlp_row = jnp.sum(mlp_gain_ref[...], axis=0, keepdims=True)
    gain_out[...] = jnp.zeros_like(gain_out)
    for place in range(width // 128):
        lanes = slice(place * 128, (place + 1) * 128)
        gain_out[place % near, place // near, 0:1, :] = attn_row[:, lanes]
        gain_out[place % near, place // near, 1:2, :] = mlp_row[:, lanes]

    def gain_group(peer, member):
        return pltpu.make_async_remote_copy(
            src_ref=gain_out.at[peer // fold],
            dst_ref=gain_in.at[member],
            send_sem=gain_send.at[peer],
            recv_sem=gain_recv.at[member],
            device_id={"fsdp": peer},
            device_id_type=MESH,
        )

    def gain_seq(peer, place):
        return pltpu.make_async_remote_copy(
            src_ref=gain_sum.at[peer],
            dst_ref=gain_back.at[place],
            send_sem=back_send.at[peer],
            recv_sem=back_recv.at[place],
            device_id={"seq": peer},
            device_id_type=MESH,
        )

    others(group, own, lambda peer: gain_group(peer, own).start())
    gain_in[own] = gain_out[own // fold]
    others(group, own, lambda peer: gain_group(peer, peer).wait_recv())
    gain_sum[...] = jnp.sum(gain_in[...], axis=0)
    others(seqs, seq, lambda peer: gain_seq(peer, seq).start())
    gain_back[seq] = gain_sum[seq]
    others(seqs, seq, lambda peer: gain_seq(peer, peer).wait_recv())
    tile_ref[...] = jnp.sum(gain_back[...], axis=0)
    others(group, own, lambda peer: block_swap(peer, peer).wait_recv())
    for index, target in enumerate((wq_ref, wk_ref, wv_ref)):
        for member, first, home, size in column_parts(seqs, group, share, span):
            first = first + index * span
            target[:, home : home + size] = cols[member, :, first : first + size]
    from_seq.sent()
    for item in results:
        item.wait()
    for batch in range(batches):
        reduces[batch].sent()

        @pl.when(has_left)
        def _(batch=batch):
            pl.loop(0, need)(lambda step: halo(batch, step, seq).wait_send())

    heads_near.sent()
    down.end()
    others(group, own, lambda peer: gain_group(peer, own).wait_send())
    others(group, own, lambda peer: block_swap(peer, own).wait_send())
    others(seqs, seq, lambda peer: gain_seq(peer, seq).wait_send())


def attention_back(
    seqs, chips, block, query, kv_pad, low, lse, d_att, part_own, parts_one, parts_two, parts_far, w, group_a,
    x, d_middle, gain, mlp_gain, out_part, down, collective,
):
    batches, length, span = query.shape
    padded = kv_pad.shape[1]
    rows, width = x.shape
    piece = rows // batches
    group = 2 * chips
    depth = w.shape[1]
    run = width // seqs
    share = run // group
    near = group // (128 // share)
    cells = part_own.shape[1]
    out_rows = out_part.shape[0] // seqs
    half, wide = jnp.bfloat16, jnp.float32
    part = 256 if batches * length <= 2048 else 128
    return pl.pallas_call(
        functools.partial(attention_back_kernel, seqs, chips, block),
        out_shape=[
            jax.ShapeDtypeStruct((rows, width), wide),
            jax.ShapeDtypeStruct((share, width), half),
            jax.ShapeDtypeStruct((share, width), half),
            jax.ShapeDtypeStruct((share, width), half),
            jax.ShapeDtypeStruct((out_rows, width), wide),
            jax.ShapeDtypeStruct((8, 128), wide),
            jax.ShapeDtypeStruct((share, cells // 2 * group), half),
            jax.ShapeDtypeStruct((share, cells // 2 * group), half),
            jax.ShapeDtypeStruct((seqs - 1 - near_count(seqs), down.shape[0] // seqs, width), half),
        ],
        in_specs=[VMEM_SPEC] * 5
        + [ANY_SPEC] * 4
        + [VMEM_SPEC, ANY_SPEC, VMEM_SPEC, ANY_SPEC]
        + [VMEM_SPEC] * 3
        + [ANY_SPEC],
        out_specs=[ANY_SPEC, VMEM_SPEC, VMEM_SPEC, VMEM_SPEC, ANY_SPEC, VMEM_SPEC]
        + [ANY_SPEC] * 3,
        scratch_shapes=[
            pltpu.VMEM((rows, width), wide),
            pltpu.VMEM((out_rows, width), wide),
            pltpu.VMEM((share, cells // 2 * group), half),
            pltpu.VMEM((share, cells // 2 * group), half),
            sems(4),
            sems(seqs),
            sems(seqs),
            pltpu.VMEM((padded, span), wide),
            pltpu.VMEM((padded, span), wide),
            pltpu.VMEM((span, padded), half),
            pltpu.VMEM((batches, length, depth), half),
            pltpu.VMEM((batches, WINDOW, 2 * span), half),
            pltpu.VMEM((batches, WINDOW, 2 * span), half),
            pltpu.VMEM((2, seqs, share, cells), half),
            pltpu.VMEM((group, share, cells), half),
            pltpu.VMEM((group, share, cells), half),
            pltpu.VMEM((2, batches, length, part), half),
            pltpu.VMEM((width, depth), half),
            pltpu.VMEM((seqs - 1, run, depth), half),
            pltpu.VMEM((group, share, depth), half),
            pltpu.VMEM((seqs - 1, out_rows, width), half),
            pltpu.VMEM((batches, piece, width), wide),
            pltpu.VMEM((8, width), wide),
            pltpu.VMEM((near, seqs, 8, 128), wide),
            pltpu.VMEM((group, seqs, 8, 128), wide),
            pltpu.VMEM((seqs, 8, 128), wide),
            pltpu.VMEM((seqs, 8, 128), wide),
            pltpu.VMEM((2 * piece, TILE), wide),
            pltpu.VMEM((piece, width), wide),
            sems(batches, WINDOW // block),
            sems(batches, WINDOW // block),
            sems(2, seqs),
            sems(group),
            sems(group),
            pltpu.SemaphoreType.DMA,
            pltpu.SemaphoreType.DMA,
            sems(2),
            sems(seqs),
            sems(seqs),
            sems(group),
            sems(group),
            sems(seqs),
            sems(seqs),
            sems(group),
            sems(group),
            sems(seqs),
            sems(seqs),
        ]
        + PairReduce.scratch(chips, piece, width) * batches,
        compiler_params=comm_params(collective, 63),
        cost_estimate=cost(
            20 * batches * length * span * (WINDOW + block) + 4 * group * rows * width * depth,
            400 * MIB,
            3 * group * rows * width * 2,
        ),
        name="attention_back",
    )(
        query, kv_pad, low, lse, d_att, part_own, parts_one, parts_two, parts_far, w, group_a, x,
        d_middle, gain, mlp_gain, out_part, down,
    )


def finish_kernel(count, *refs):
    sources, targets = refs[:-count], refs[-count:]
    for source, target in zip(sources, targets[:-1]):
        target[...] = source[...].astype(target.dtype)
    added = 0.0
    for source in sources[count - 1 :]:
        added = added + jnp.sum(source[...].astype(jnp.float32), axis=0)
    targets[-1][...] = added


def finish(steps, arrays, parts, kinds):
    in_specs, out_specs, out_shape = [], [], []
    for item, kind in zip(arrays + parts[:1], kinds):
        rows, width = item.shape[-2:]
        block = (rows // steps, width)
        out_specs.append(pl.BlockSpec(block, lambda i: (i, 0)))
        out_shape.append(jax.ShapeDtypeStruct((rows, width), kind))
        if item.ndim == 2:
            in_specs.append(out_specs[-1])
    for item in parts:
        in_specs.append(pl.BlockSpec((item.shape[0],) + block, lambda i: (0, i, 0)))
    return pl.pallas_call(
        functools.partial(finish_kernel, len(kinds)),
        grid=(steps,),
        in_specs=in_specs,
        out_specs=out_specs,
        out_shape=out_shape,
        compiler_params=pltpu.CompilerParams(vmem_limit_bytes=48 * MIB),
        name="finish",
    )(*arrays, *parts)


def doc_starts(lengths, positions, batches, seq_len):
    table = lengths.reshape(batches, -1, lengths.shape[1])
    starts = jnp.cumsum(table, axis=2) - table
    per_batch = seq_len // table.shape[1]
    begins = (starts + (jnp.arange(table.shape[1], dtype=jnp.int32) * per_batch)[None, :, None]).reshape(
        batches, -1
    )
    before = begins[:, None, :] <= positions[None, :, None]
    return jnp.max(jnp.where(before, begins[:, None, :], 0), axis=2)


def body(
    tokens,
    cotangent,
    lengths,
    gain_attn,
    w_query,
    w_key,
    w_value,
    w_out,
    gain_mlp,
    w_gate,
    w_up,
    w_down,
):
    batches, piece, width = tokens.shape
    seqs = lax.axis_size("seq")
    group = lax.axis_size("fsdp")
    chips = group // 2
    devices = seqs * group
    seq_len = piece * devices
    rows = batches * piece
    share = w_query.shape[0]
    span = width // group
    length = group * piece
    aligned = share == HEAD
    member = lax.axis_index("fsdp")

    x_rows = tokens.reshape(rows, width)
    cot_rows = cotangent.reshape(rows, width)
    wd_part = lax.all_gather(w_down, "seq", axis=0, tiled=True)
    if aligned:
        wo_part = lax.all_gather(w_out, "seq", axis=0, tiled=True)
    else:
        wo_all = lax.all_gather(w_out, ("seq", "fsdp"), axis=0, tiled=True)
        wo_part = lax.dynamic_slice_in_dim(wo_all, member * span, span, 0)

    lane = jnp.arange(128, dtype=jnp.int32)
    device = lax.axis_index("seq") * group + member
    fold = 128 // share
    here = lane // share == lax.rem(device, fold)
    both = jnp.stack([gain_attn, gain_mlp]).astype(jnp.float32)
    tile = jnp.where(here[None], jnp.tile(both, (1, fold)), 0.0)
    tile = jnp.pad(tile, ((0, 6), (0, 0)))[None]
    group_a, query, key_value, gains, w_heads, unit_blocks = start(
        seqs, chips, batches, tile, x_rows, (w_query, w_key, w_value), (w_gate, w_up), 1
    )
    lengths, gains = lax.optimization_barrier((lengths, gains))
    group_start = lax.axis_index("seq") * length
    positions = group_start + jnp.arange(length, dtype=jnp.int32)
    begins = doc_starts(lengths, positions, batches, seq_len)
    at = jnp.arange(length, dtype=jnp.int32)
    block = min(256, length)
    low = jnp.maximum(begins - group_start + WINDOW, at[None, :] + 1) - (at // block * block)[None, :]
    low = low[:, None, :]

    gains = gains.transpose(1, 0, 2, 3).reshape(devices // fold, fold, 8, 128).sum(axis=1)
    gain_one = gains[:, 0].reshape(width)
    gain_two = gains[:, 1].reshape(width)
    attended, lse, kv_pad, unit_own = attend(
        seqs, group, query, key_value, low, block, unit_blocks, 2
    )
    middle, normed_b, group_d, w_units = branch_sum(
        seqs, chips, attended, wo_part, cot_rows, unit_own.reshape(group * share, -1),
        x_rows, gain_two[None], 3,
    )
    w_units = w_units.reshape(width, -1)
    d_middle, d_branch, mlp_gain_part, hidden, unit_part, unit_one = feed_forward(
        seqs, chips, batches, normed_b, w_units, wd_part, group_d, middle, cot_rows,
        gain_two[None], 4,
    )
    d_attended, layer_out, out_part, unit_two, unit_far, down_part, down_near = branch_back(
        seqs, chips, batches, d_branch, wo_part, attended, middle, hidden, wd_part, unit_part,
        group_d, 5,
    )
    if not aligned:
        whole = lax.dynamic_update_slice_in_dim(
            jnp.zeros((width, width), jnp.bfloat16), out_part, member * span, 0
        )
        out_part = lax.psum(whole, "fsdp").reshape(seqs, group, share, width)
        out_part = lax.dynamic_slice_in_dim(out_part, member, 1, 1).reshape(seqs * share, width)
    (
        input_grad, wq_grad, wk_grad, wv_grad, wo_grad, gain_tile, gate_grad, up_grad, down_far,
    ) = attention_back(
        seqs, chips, block, query, kv_pad, low, lse, d_attended, unit_part, unit_one, unit_two,
        unit_far, w_heads, group_a, x_rows, d_middle, gain_one[None], mlp_gain_part, out_part,
        down_part, 6,
    )
    gain_grads = lax.dynamic_slice_in_dim(gain_tile[:2], lax.rem(device, fold) * share, share, 1)
    wide = jnp.float32
    (layer_out, input_grad, wq_grad, wk_grad, wv_grad, wo_grad, gate_grad, up_grad, down_grad) = finish(
        share // 16,
        [layer_out, input_grad, wq_grad, wk_grad, wv_grad, wo_grad, gate_grad, up_grad],
        [down_near, down_far],
        [jnp.bfloat16] + [wide] * 8,
    )
    return (
        layer_out.reshape(batches, piece, width),
        input_grad.reshape(batches, piece, width),
        gain_grads[0],
        wq_grad,
        wk_grad,
        wv_grad,
        wo_grad,
        gain_grads[1],
        gate_grad,
        up_grad,
        down_grad,
    )


def solution(mesh):
    spread = ("seq", "fsdp")
    tokens, rows, gains = P(None, spread, None), P(spread, None), P(spread)
    in_specs = (tokens, tokens, P(), gains, rows, rows, rows, rows, gains, rows, rows, rows)
    out_specs = (tokens, tokens, gains, rows, rows, rows, rows, gains, rows, rows, rows)
    return jax.shard_map(body, mesh=mesh, in_specs=in_specs, out_specs=out_specs, check_vma=False)
```

```python
import functools

import jax
import jax.numpy as jnp
from jax import lax
from jax.experimental import pallas as pl
from jax.experimental.pallas import tpu as pltpu
from jax.sharding import PartitionSpec as P

HEAD = 64
FF = 8192
WINDOW = 1024
PAIR = 128
TILE = 512
PARTS = 4
LOW = -1e30
EPS = 1e-05
MESH = pl.DeviceIdType.MESH
MIB = 2**20


def to_half(values):
    return values.astype(jnp.bfloat16)


def normalize(values, gain):
    return values * lax.rsqrt(jnp.mean(values * values, axis=-1, keepdims=True) + EPS) * gain


def contract_rows(left, right):
    return lax.dot_general(
        left, right, (((0,), (0,)), ((), ())), preferred_element_type=jnp.float32
    )


def dot_nt(left, right):
    return lax.dot_general(
        left, right, (((1,), (1,)), ((), ())), preferred_element_type=jnp.float32
    )


def dot_nn(left, right):
    return jnp.dot(left, right, preferred_element_type=jnp.float32)


def head_lanes(values, half):
    lane = lax.broadcasted_iota(jnp.int32, values.shape, 1)
    return jnp.where((lane >= HEAD) == (half == 1), values, jnp.zeros_like(values))


def masked_scores(k_rows, q_head, low):
    keys, block = k_rows.shape[0], q_head.shape[0]
    scores = dot_nt(k_rows, q_head)
    at = lax.broadcasted_iota(jnp.int32, (keys, block), 0)
    query = lax.broadcasted_iota(jnp.int32, (keys, block), 1)
    seen = (at >= low) & (at <= query + WINDOW)
    return jnp.where(seen, scores, LOW)


class Line:
    def __init__(self, chips):
        self.chips = chips
        self.own = lax.axis_index("fsdp")
        self.chip = self.own // 2
        self.core = lax.rem(self.own, 2)
        self.other = self.own + 1 - 2 * self.core
        self.has_left = self.chip > 0
        self.has_right = self.chip < chips - 1

    def greet(self):
        signal_group(self.other)
        pl.when(self.has_left)(lambda: signal_group(self.own - 2))
        pl.when(self.has_right)(lambda: signal_group(self.own + 2))
        return 1 + self.has_left.astype(jnp.int32) + self.has_right.astype(jnp.int32)


def signal_group(peer):
    barrier = pltpu.get_barrier_semaphore()
    pl.semaphore_signal(barrier, inc=1, device_id={"fsdp": peer}, device_id_type=MESH)


def signal_seq(peer):
    barrier = pltpu.get_barrier_semaphore()
    pl.semaphore_signal(barrier, inc=1, device_id={"seq": peer}, device_id_type=MESH)


def greet_group(group):
    own = lax.axis_index("fsdp")
    pl.loop(1, group)(lambda ahead: signal_group(lax.rem(own + ahead, group)))
    return group - 1


def greet_seq(seqs):
    own = lax.axis_index("seq")
    pl.loop(1, seqs)(lambda ahead: signal_seq(lax.rem(own + ahead, seqs)))
    return seqs - 1


def meet(count):
    pl.semaphore_wait(pltpu.get_barrier_semaphore(), count)


def rows_at(index, size):
    return pl.ds(pl.multiple_of(index * size, size), size)


class Spread:
    def __init__(self, line, first, buf, send, recv):
        self.line, self.first, self.buf, self.send, self.recv = line, first, buf, send, recv
        self.parts = recv.shape[1]
        self.size = first.shape[0] // self.parts

    def move(self, slot, part, way, peer, source=None):
        here = rows_at(part, self.size)
        return pltpu.make_async_remote_copy(
            src_ref=self.buf.at[slot, here] if source is None else source.at[here],
            dst_ref=self.buf.at[slot, here],
            send_sem=self.send.at[way, slot, part],
            recv_sem=self.recv.at[slot, part],
            device_id={"fsdp": peer},
            device_id_type=MESH,
        )

    def begin(self):
        line = self.line

        @pl.loop(0, self.parts)
        def _(part):
            pl.when(line.has_right)(
                lambda: self.move(line.own, part, 1, line.own + 2, self.first).start()
            )
            pl.when(line.has_left)(
                lambda: self.move(line.own, part, 0, line.own - 2, self.first).start()
            )
            self.move(line.own, part, 2, line.other, self.first).start()

    def relay_part(self, far, part):
        line = self.line

        @pl.when(line.chip - far >= 0)
        def _():
            slot = (line.chip - far) * 2 + line.core
            self.move(slot, part, 1, line.own).wait_recv()
            pl.when(line.has_right)(lambda: self.move(slot, part, 1, line.own + 2).start())
            self.move(slot, part, 2, line.other).start()

        @pl.when(line.chip + far < line.chips)
        def _():
            slot = (line.chip + far) * 2 + line.core
            self.move(slot, part, 0, line.own).wait_recv()
            pl.when(line.has_left)(lambda: self.move(slot, part, 0, line.own - 2).start())
            self.move(slot, part, 2, line.other).start()

    def relay(self, far):
        pl.loop(0, self.parts)(lambda part: self.relay_part(far, part))

    def across(self, slot):
        pl.loop(0, self.parts)(lambda part: self.move(slot, part, 2, self.line.own).wait_recv())

    def each(self, far, use):
        line = self.line

        @pl.loop(0, 4)
        def _(turn):
            side = lax.rem(turn, 2)
            over = turn // 2
            away = far - over
            source = line.chip + away * (2 * side - 1)
            valid = (away >= 0) & (away < line.chips) & (source >= 0) & (source < line.chips)
            valid = valid & ((side == 0) | (away > 0))

            @pl.when(valid)
            def _():
                slot = source * 2 + line.core + over * (1 - 2 * line.core)
                pl.when(over == 1)(lambda: self.across(slot))
                use(slot)

    def rest(self):
        pl.loop(0, self.line.chips)(lambda place: self.across(place * 2 + 1 - self.line.core))

    def sent(self):
        line = self.line

        @pl.loop(0, line.chips)
        def _(place):
            slot = place * 2 + line.core

            @pl.loop(0, self.parts)
            def _(part):
                self.move(slot, part, 2, line.other).wait_send()
                pl.when(line.has_right & (place <= line.chip))(
                    lambda: self.move(slot, part, 1, line.own + 2).wait_send()
                )
                pl.when(line.has_left & (place >= line.chip))(
                    lambda: self.move(slot, part, 0, line.own - 2).wait_send()
                )


class Reduce:
    def __init__(self, line, product, out, acc, cross_out, line_out, cross_in, line_in, send, recv):
        self.line, self.product, self.out, self.acc = line, product, out, acc
        self.cross_out, self.line_out, self.cross_in, self.line_in = cross_out, line_out, cross_in, line_in
        self.send, self.recv = send, recv
        self.tiles = line_out.shape[2] // TILE

    @staticmethod
    def scratch(chips, rows, width):
        part = pltpu.VMEM((chips, rows, width), jnp.bfloat16)
        return [
            pltpu.VMEM((rows, TILE), jnp.float32),
            pltpu.VMEM((2, rows, width), jnp.bfloat16),
            part,
            part,
            pltpu.VMEM((chips + 1, rows, width), jnp.bfloat16),
            pltpu.SemaphoreType.DMA((2, chips, width // TILE)),
            pltpu.SemaphoreType.DMA((2, chips + 1, width // TILE)),
        ]

    def cross(self, side, place, tile):
        here = rows_at(tile, TILE)
        return pltpu.make_async_remote_copy(
            src_ref=self.cross_out.at[side, :, here],
            dst_ref=self.cross_in.at[place, :, here],
            send_sem=self.send.at[0, place, tile],
            recv_sem=self.recv.at[0, place, tile],
            device_id={"fsdp": self.line.other},
            device_id_type=MESH,
        )

    def along(self, place, landing, tile, peer):
        here = rows_at(tile, TILE)
        return pltpu.make_async_remote_copy(
            src_ref=self.line_out.at[place, :, here],
            dst_ref=self.line_in.at[landing, :, here],
            send_sem=self.send.at[1, place, tile],
            recv_sem=self.recv.at[1, landing, tile],
            device_id={"fsdp": peer},
            device_id_type=MESH,
        )

    def where(self, away, side):
        line = self.line
        rightward = (line.chips - 1 - line.chip >= line.chip) == (side == 0)
        place = line.chip + jnp.where(rightward, away, -away)
        valid = (place >= 0) & (place < line.chips) & ((away > 0) | (side == 0))
        return valid, place, rightward

    def level(self, away, also):
        @pl.loop(0, 2)
        def _(side):
            valid, place, _ = self.where(away, side)

            @pl.when(valid)
            def _():
                @pl.loop(0, self.tiles)
                def _(tile):
                    got = self.product(place * 2 + 1 - self.line.core, tile)
                    self.cross_out[side, :, rows_at(tile, TILE)] = to_half(got)
                    self.cross(side, place, tile).start()

        @pl.loop(0, self.tiles)
        def _(tile):
            @pl.loop(0, 2)
            def _(side):
                valid, place, rightward = self.where(away, side)
                pl.when(valid)(lambda: self.close(away, side, place, rightward, tile))

            also(tile)

    def close(self, away, side, place, rightward, tile):
        line, acc = self.line, self.acc
        here = rows_at(tile, TILE)
        upstream = (rightward & line.has_left) | (jnp.logical_not(rightward) & line.has_right)
        acc[...] = self.product(place * 2 + line.core, tile)
        self.cross(side, place, tile).wait()
        acc[...] += self.cross_in[place, :, here].astype(jnp.float32)

        @pl.when(away > 0)
        def _():
            @pl.when(upstream)
            def _():
                self.along(place, place, tile, line.own).wait_recv()
                self.line_out[place, :, here] = to_half(
                    acc[...] + self.line_in[place, :, here].astype(jnp.float32)
                )

            @pl.when(jnp.logical_not(upstream))
            def _():
                self.line_out[place, :, here] = to_half(acc[...])

            @pl.when(rightward)
            def _():
                self.along(place, place, tile, line.own + 2).start()

            @pl.when(jnp.logical_not(rightward))
            def _():
                landing = jnp.where(away == 1, line.chips, place)
                self.along(place, landing, tile, line.own - 2).start()

        @pl.when(away == 0)
        def _():
            self.out[:, here] = acc[...]

            @pl.when(line.has_left)
            def _():
                self.along(place, place, tile, line.own).wait_recv()
                self.out[:, here] += self.line_in[place, :, here].astype(jnp.float32)

            @pl.when(line.has_right)
            def _():
                self.along(place, line.chips, tile, line.own).wait_recv()
                self.out[:, here] += self.line_in[line.chips, :, here].astype(jnp.float32)

    def sent(self):
        @pl.loop(0, self.line.chips)
        def _(place):
            @pl.when(place != self.line.chip)
            def _():
                pl.loop(0, self.tiles)(
                    lambda tile: self.along(place, place, tile, self.line.own).wait_send()
                )


class Swap:
    def __init__(self, group, source, target, send, recv, keep):
        self.group, self.source, self.target = group, source, target
        self.send, self.recv, self.keep = send, recv, keep
        self.own = lax.axis_index("fsdp")

    def move(self, peer, source):
        return pltpu.make_async_remote_copy(
            src_ref=self.source.at[peer],
            dst_ref=self.target.at[source],
            send_sem=self.send.at[peer],
            recv_sem=self.recv.at[source],
            device_id={"fsdp": peer},
            device_id_type=MESH,
        )

    def kept(self):
        return pltpu.make_async_copy(self.source.at[self.own], self.target.at[self.own], self.keep)

    def begin(self):
        self.kept().start()
        pl.loop(1, self.group)(
            lambda ahead: self.move(lax.rem(self.own + ahead, self.group), self.own).start()
        )

    def end(self):
        self.kept().wait()

        @pl.loop(1, self.group)
        def _(ahead):
            peer = lax.rem(self.own + ahead, self.group)
            self.move(peer, peer).wait_recv()
            self.move(peer, self.own).wait_send()


class Share:
    def __init__(self, seqs, source, target, send, recv, keep):
        self.seqs, self.source, self.target = seqs, source, target
        self.send, self.recv, self.keep = send, recv, keep
        self.own = lax.axis_index("seq")
        self.half = source.shape[0] // 2

    def move(self, peer, place):
        return pltpu.make_async_remote_copy(
            src_ref=self.source,
            dst_ref=self.target.at[place],
            send_sem=self.send.at[peer, 0],
            recv_sem=self.recv.at[place, 0],
            device_id={"seq": peer},
            device_id_type=MESH,
        )

    def relay(self, peer, place, part):
        here = pl.ds(part * self.half, self.half)
        return pltpu.make_async_remote_copy(
            src_ref=self.target.at[place, here],
            dst_ref=self.target.at[place, here],
            send_sem=self.send.at[peer, 1],
            recv_sem=self.recv.at[place, part],
            device_id={"seq": peer},
            device_id_type=MESH,
        )

    def near(self):
        one = self.own + 1 - 2 * lax.rem(self.own, 2)
        two = lax.rem(self.own + 2, 4)
        return one, two, lax.rem(one + 2, 4)

    def kept(self):
        return pltpu.make_async_copy(self.source, self.target.at[self.own], self.keep)

    def begin(self):
        self.kept().start()
        if self.seqs == 4:
            one, two, _ = self.near()
            self.move(one, self.own).start()
            self.move(two, self.own).start()
        else:
            pl.loop(1, self.seqs)(
                lambda ahead: self.move(lax.rem(self.own + ahead, self.seqs), self.own).start()
            )

    def pass_on(self):
        if self.seqs == 4:
            one, two, _ = self.near()
            self.move(one, one).wait_recv()
            self.relay(two, one, 0).start()
            self.move(two, two).wait_recv()
            self.relay(one, two, 1).start()

    def end(self):
        self.kept().wait()
        if self.seqs == 4:
            one, two, far = self.near()
            self.relay(two, far, 0).wait_recv()
            self.relay(one, far, 1).wait_recv()
            self.move(one, self.own).wait_send()
            self.move(two, self.own).wait_send()
            self.relay(two, one, 0).wait_send()
            self.relay(one, two, 1).wait_send()
        else:

            @pl.loop(1, self.seqs)
            def _(ahead):
                peer = lax.rem(self.own + ahead, self.seqs)
                self.move(peer, peer).wait_recv()
                self.move(peer, self.own).wait_send()


def seq_peers(seqs):
    own = lax.axis_index("seq")
    if seqs == 4:
        one = own + 1 - 2 * lax.rem(own, 2)
        return [one, lax.rem(own + 2, 4)], [lax.rem(one + 2, 4)]
    ahead = [lax.rem(own + step, seqs) for step in range(1, seqs)]
    return ahead[:1], ahead[1:]


def near_count(seqs):
    return 2 if seqs == 4 else 1


class ToPeers:
    def __init__(self, seqs, peers, source, target, send, recv, first=0):
        self.peers, self.source, self.target, self.send, self.recv = peers, source, target, send, recv
        self.run, self.first = source.shape[0] // seqs, first

    def move(self, index):
        begin = pl.multiple_of(self.peers[index] * self.run + self.first, 16)
        return pltpu.make_async_remote_copy(
            src_ref=self.source.at[pl.ds(begin, self.target.shape[1])],
            dst_ref=self.target.at[index],
            send_sem=self.send.at[index],
            recv_sem=self.recv.at[index],
            device_id={"seq": self.peers[index]},
            device_id_type=MESH,
        )

    def begin(self):
        for index in range(len(self.peers)):
            self.move(index).start()

    def arrived(self):
        for index in range(len(self.peers)):
            self.move(index).wait_recv()

    def sent(self):
        for index in range(len(self.peers)):
            self.move(index).wait_send()

    def end(self):
        self.arrived()
        self.sent()


VMEM_SPEC = pl.BlockSpec(memory_space=pltpu.VMEM)
ANY_SPEC = pl.BlockSpec(memory_space=pl.ANY)


def comm_params(collective, mib=58):
    return pltpu.CompilerParams(
        collective_id=collective, has_side_effects=True, vmem_limit_bytes=mib * MIB
    )


def cost(flops, local, remote):
    return pl.CostEstimate(
        flops=flops, bytes_accessed=local, transcendentals=0, remote_bytes_transferred=remote
    )


def sems(*shape):
    return pltpu.SemaphoreType.DMA(shape)


def left_rows(a_ref, slot, rows):
    if len(a_ref.shape) == 2:
        return a_ref[rows_at(slot, rows), :]
    piece = rows // a_ref.shape[0]
    return jnp.concatenate(
        [a_ref[batch, rows_at(slot, piece), :] for batch in range(a_ref.shape[0])], axis=0
    )


def norm_back(rows, v_ref, e_ref, gain_ref, gain_acc, put):
    @pl.loop(0, rows // 32)
    def _(chunk):
        here = rows_at(chunk, 32)
        values = v_ref[here, :].astype(jnp.float32)
        error = e_ref[here, :]
        rate = lax.rsqrt(jnp.mean(values * values, axis=-1, keepdims=True) + EPS)
        unit = values * rate
        product = error * unit
        gain = gain_ref[0:1, :]
        mean = jnp.mean(product * gain, axis=-1, keepdims=True)
        gain_acc[...] += (product[0:8] + product[8:16]) + (product[16:24] + product[24:32])
        put(here, rate * (gain * error - unit * mean))


def add_from_seq(own_rows, got, here):
    added = own_rows.astype(jnp.float32)
    for index in range(got.shape[0]):
        added = added + got[index, here, :].astype(jnp.float32)
    return added


def column_parts(seqs, group, share, span):
    size = HEAD if share == HEAD else span
    parts = []
    for member in range(group):
        for run in range(span // size):
            home = (run * group + member) * size
            parts.append((member, run * size, home, size))
    return parts


def start_kernel(
    seqs, chips, batches, block, tile_ref, x_ref, wq_ref, wk_ref, wv_ref, gate_hbm, up_hbm, low_ref,
    g_ref, q_ref, out_ref, lse_ref, pad_ref, gains_ref, w_out_ref, own_units_ref,
    gate, up, units, blocks_ref, buf, normed, pad, vt, gain, gains, w,
    unit_sem, send, recv, keep, swap_send, share_send, w_recv,
    tile_send, tile_across, tile_recv, tile_back, w_keep, gain_keep,
    halo_send, halo_recv, pad_keep, unit_send, unit_recv, unit_keep,
):
    line = Line(chips)
    group = 2 * chips
    seq = lax.axis_index("seq")
    own = line.own
    share = blocks_ref.shape[1]
    rows, width = x_ref.shape
    piece = rows // batches
    length, span = q_ref.shape[1:]
    per = 128 * seqs * group // width
    steps, need = length // block, WINDOW // block
    has_left, has_right = seq > 0, seq < seqs - 1
    unit_loads = [
        pltpu.make_async_copy(gate_hbm, gate, unit_sem.at[0]),
        pltpu.make_async_copy(up_hbm, up, unit_sem.at[1]),
    ]
    for item in unit_loads:
        item.start()
    for index, source in enumerate((wq_ref, wk_ref, wv_ref)):
        for member, first, home, size in column_parts(seqs, group, share, span):
            first = first + index * span
            blocks_ref[member, :, first : first + size] = source[:, home : home + size]
    meet(greet_group(group) + greet_seq(seqs))

    def block_at(run, member):
        return w.at[rows_at(run * group + member, share)]

    def block_swap(peer, member):
        return pltpu.make_async_remote_copy(
            src_ref=blocks_ref.at[peer],
            dst_ref=block_at(seq, member),
            send_sem=swap_send.at[peer],
            recv_sem=w_recv.at[seq, member],
            device_id={"fsdp": peer},
            device_id_type=MESH,
        )

    def block_share(run, member, peer):
        return pltpu.make_async_remote_copy(
            src_ref=block_at(run, member),
            dst_ref=block_at(run, member),
            send_sem=share_send.at[peer, member],
            recv_sem=w_recv.at[run, member],
            device_id={"seq": peer},
            device_id_type=MESH,
        )

    def tile_to_seq(peer, place):
        return pltpu.make_async_remote_copy(
            src_ref=tile_ref.at[0],
            dst_ref=gains.at[own, place],
            send_sem=tile_send.at[peer],
            recv_sem=tile_recv.at[place],
            device_id={"seq": peer},
            device_id_type=MESH,
        )

    def tiles_to_group(peer, member):
        return pltpu.make_async_remote_copy(
            src_ref=gains.at[member],
            dst_ref=gains.at[member],
            send_sem=tile_across.at[peer],
            recv_sem=tile_back.at[member],
            device_id={"fsdp": peer},
            device_id_type=MESH,
        )

    def others(count, me, act):
        pl.loop(1, count)(lambda ahead: act(lax.rem(me + ahead, count)))

    others(seqs, seq, lambda peer: tile_to_seq(peer, seq).start())
    others(group, own, lambda peer: block_swap(peer, own).start())
    spreads = [
        Spread(line, x_ref.at[pl.ds(batch * piece, piece)], buf.at[batch], send.at[batch], recv.at[batch])
        for batch in range(batches)
    ]
    spreads[0].begin()
    gains[own, seq] = tile_ref[0]
    w[rows_at(seq * group + own, share), :] = blocks_ref[own]
    others(seqs, seq, lambda peer: block_share(seq, own, peer).start())
    for batch in range(batches):
        buf[batch, own] = x_ref[batch * piece : (batch + 1) * piece, :]
    others(seqs, seq, lambda peer: tile_to_seq(peer, peer).wait_recv())
    others(group, own, lambda peer: tiles_to_group(peer, own).start())
    for item in unit_loads:
        item.wait()
    cell = units.shape[2] // 2 // seqs
    for member in range(group):
        for run in range(seqs):
            home = (run * group + member) * cell
            for index, source in enumerate((gate, up)):
                first = (index * seqs + run) * cell
                units[member, :, first : first + cell] = source[:, home : home + cell]
    unit_swap = Swap(group, units, own_units_ref, unit_send, unit_recv, unit_keep)

    @pl.when(jnp.logical_not(has_left))
    def _():
        pad[:, :WINDOW, :] = jnp.zeros((batches, WINDOW, 2 * span), jnp.bfloat16)

    def pass_block(member):
        block_swap(member, member).wait_recv()
        others(seqs, seq, lambda peer: block_share(seq, member, peer).start())

    others(group, own, pass_block)
    others(group, own, lambda peer: tiles_to_group(peer, peer).wait_recv())
    for column in range(width // 128):
        total = 0.0
        for place in range(column * per, (column + 1) * per):
            total = total + gains[place % group, place // group, 0:1, :]
        gain[0:1, column * 128 : (column + 1) * 128] = total

    def sides(far, act):
        @pl.loop(0, 2)
        def _(side):
            place = line.chip + far * (2 * side - 1)
            valid = (place >= 0) & (place < chips) & ((side == 0) | (far > 0))
            pl.when(valid)(lambda: act(place))

    def kept(batch, place):
        here = rows_at(place, block)
        return pltpu.make_async_copy(
            normed.at[batch, here], g_ref.at[batch, here], keep.at[batch, place]
        )

    def norm_pair(batch, place):
        spreads[batch].across(place * 2 + 1 - line.core)

        @pl.loop(0, 2)
        def _(member):
            @pl.loop(0, piece // 64)
            def _(chunk):
                values = buf[batch, place * 2 + member, rows_at(chunk, 64), :].astype(jnp.float32)
                there = pl.multiple_of(place * block + member * piece + chunk * 64, 64)
                normed[batch, pl.ds(there, 64), :] = to_half(normalize(values, gain[0:1, :]))

        kept(batch, place).start()

    def halo(batch, step, peer):
        there = pl.multiple_of(WINDOW + (step + steps - need) * block, block)
        return pltpu.make_async_remote_copy(
            src_ref=pad.at[batch, pl.ds(there, block)],
            dst_ref=pad.at[batch, rows_at(step, block)],
            send_sem=halo_send.at[batch, step],
            recv_sem=halo_recv.at[batch, step],
            device_id={"seq": peer},
            device_id_type=MESH,
        )

    def project(batch, place):
        here = rows_at(place, block)
        got = to_half(dot_nn(normed[batch, here, :], w[...]))
        q_ref[batch, here, :] = got[:, :span]
        pad[batch, pl.ds(pl.multiple_of(WINDOW + place * block, block), block), :] = got[:, span:]

        @pl.when(has_right & (place >= steps - need))
        def _():
            halo(batch, place - (steps - need), seq + 1).start()

    @pl.loop(0, chips)
    def _(far):
        pl.when(far > 0)(lambda: spreads[0].relay(far))
        pl.when(far == chips - 2)(spreads[1].begin)
        sides(far, lambda place: norm_pair(0, place))

    spreads[1].relay(1)

    def have_block(run, member):
        block_share(run, member, seq).wait_recv()

    others(seqs, seq, lambda run: pl.loop(0, group)(lambda member: have_block(run, member)))
    w_kept = pltpu.make_async_copy(w, w_out_ref, w_keep)
    w_kept.start()
    gains_kept = pltpu.make_async_copy(gains, gains_ref, gain_keep)
    gains_kept.start()
    pl.loop(0, steps)(lambda place: project(0, place))

    @pl.loop(2, chips)
    def _(far):
        spreads[1].relay(far)

    unit_swap.begin()

    @pl.loop(0, chips)
    def _(far):
        sides(far, lambda place: norm_pair(1, place))
        sides(far, lambda place: project(1, place))

    def pad_kept(batch):
        return pltpu.make_async_copy(pad.at[batch], pad_ref.at[batch], pad_keep.at[batch])

    for batch in range(batches):
        vt[:, WINDOW:] = pad[batch, WINDOW:, span:].T

        @pl.loop(0, steps)
        def _(turn, batch=batch):
            step = steps - 1 - turn

            @pl.when(step < need)
            def _():
                arrived = rows_at(step, block)
                pl.when(has_left)(lambda: halo(batch, step, seq).wait_recv())
                vt[:, arrived] = pad[batch, arrived, span:].T

            begin = pl.multiple_of(step * block, block)
            keys = pl.ds(begin, block + WINDOW)
            rows = pl.ds(begin, block)
            low = low_ref[batch, :, rows]
            for pair in range(span // PAIR):
                lanes = slice(pair * PAIR, (pair + 1) * PAIR)
                q_pair = q_ref[batch, rows, lanes] * jnp.asarray(HEAD**-0.5, jnp.bfloat16)
                k_rows = pad[batch, keys, lanes]
                values = vt[lanes, keys]
                mixed = []
                for half in range(2):
                    scores = masked_scores(k_rows, head_lanes(q_pair, half), low)
                    top = jnp.max(scores, axis=0, keepdims=True)
                    expo = jnp.exp(scores - top)
                    total = jnp.sum(expo, axis=0, keepdims=True)
                    mixed.append(dot_nn(values, to_half(expo)) / total)
                    row = pair * 2 + half
                    lse_ref[batch, row : row + 1, rows] = top + jnp.log(total)
                lane = lax.broadcasted_iota(jnp.int32, mixed[0].shape, 0)
                out_ref[batch, rows, lanes] = to_half(jnp.where(lane < HEAD, mixed[0], mixed[1]).T)

        pad_kept(batch).start()

    for batch in range(batches):
        spreads[batch].sent()
    others(seqs, seq, lambda peer: tile_to_seq(peer, seq).wait_send())
    others(group, own, lambda peer: block_swap(peer, own).wait_send())
    others(group, own, lambda peer: tiles_to_group(peer, own).wait_send())
    others(
        seqs,
        seq,
        lambda peer: pl.loop(0, group)(lambda member: block_share(seq, member, peer).wait_send()),
    )

    @pl.loop(0, need)
    def _(step):
        for batch in range(batches):
            pl.when(has_right)(lambda batch=batch: halo(batch, step, seq).wait_send())

    w_kept.wait()
    gains_kept.wait()
    unit_swap.end()
    for batch in range(batches):
        pad_kept(batch).wait()

        @pl.loop(0, steps)
        def _(place, batch=batch):
            kept(batch, place).wait()


def start(seqs, chips, batches, block, tile, x, weights, unit_weights, low, collective):
    rows, width = x.shape
    group = 2 * chips
    length = group * rows // batches
    share = weights[0].shape[0]
    span = width // group
    cols = 3 * span
    wide = unit_weights[0].shape[1]
    cells = 2 * wide // group
    piece = rows // batches
    padded = length + WINDOW
    half = jnp.bfloat16
    need = WINDOW // block
    return pl.pallas_call(
        functools.partial(start_kernel, seqs, chips, batches, block),
        out_shape=[
            jax.ShapeDtypeStruct((batches, length, width), half),
            jax.ShapeDtypeStruct((batches, length, span), half),
            jax.ShapeDtypeStruct((batches, length, span), half),
            jax.ShapeDtypeStruct((batches, span // HEAD, length), jnp.float32),
            jax.ShapeDtypeStruct((batches, padded, 2 * span), half),
            jax.ShapeDtypeStruct((group, seqs, 8, 128), jnp.float32),
            jax.ShapeDtypeStruct((width, cols), half),
            jax.ShapeDtypeStruct((group, share, cells), half),
        ],
        in_specs=[VMEM_SPEC] * 5 + [ANY_SPEC] * 2 + [VMEM_SPEC],
        out_specs=[ANY_SPEC] + [VMEM_SPEC] * 3 + [ANY_SPEC] * 4,
        scratch_shapes=[
            pltpu.VMEM((share, wide), half),
            pltpu.VMEM((share, wide), half),
            pltpu.VMEM((group, share, cells), half),
            pltpu.VMEM((group, share, cols), half),
            pltpu.VMEM((batches, group, piece, width), half),
            pltpu.VMEM((batches, length, width), half),
            pltpu.VMEM((batches, padded, 2 * span), half),
            pltpu.VMEM((span, padded), half),
            pltpu.VMEM((8, width), jnp.float32),
            pltpu.VMEM((group, seqs, 8, 128), jnp.float32),
            pltpu.VMEM((width, cols), half),
            sems(2),
            sems(batches, 3, group, PARTS // 2),
            sems(batches, group, PARTS // 2),
            sems(batches, chips),
            sems(group),
            sems(seqs, group),
            sems(seqs, group),
            sems(seqs),
            sems(group),
            sems(seqs),
            sems(group),
            pltpu.SemaphoreType.DMA,
            pltpu.SemaphoreType.DMA,
            sems(batches, need),
            sems(batches, need),
            sems(batches),
            sems(group),
            sems(group),
            pltpu.SemaphoreType.DMA,
        ],
        compiler_params=comm_params(collective, 62),
        cost_estimate=cost(
            2 * group * rows * width * cols + 8 * batches * length * span * (WINDOW + block),
            300 * MIB,
            2 * group * rows * width * 2,
        ),
        name="start",
    )(tile, x, *weights, *unit_weights, low)


def branch_kernel(
    seqs, chips, a_ref, w_ref, d_ref, units_ref, x_ref, gain_ref, middle_ref, normed_ref, gd_ref, w_units_ref,
    out_ref, acc, cross_out, line_out, cross_in, line_in, sum_send, sum_recv,
    send, recv, d_keep, share_send, share_recv, share_keep,
):
    line = Line(chips)
    rows = out_ref.shape[0]

    def product(slot, tile):
        return dot_nn(left_rows(a_ref, slot, rows), w_ref[:, rows_at(tile, TILE)])

    meet(line.greet() + greet_seq(seqs))
    reduce = Reduce(
        line, product, out_ref, acc, cross_out, line_out, cross_in, line_in, sum_send, sum_recv
    )
    spread = Spread(line, d_ref, gd_ref, send, recv)
    units = Share(seqs, units_ref, w_units_ref, share_send, share_recv, share_keep)
    d_kept = pltpu.make_async_copy(d_ref, gd_ref.at[line.own], d_keep)
    units.begin()
    spread.begin()
    d_kept.start()

    @pl.loop(0, chips)
    def _(step):
        def also(tile):
            pl.when(step < chips - 1)(lambda: spread.relay_part(step + 1, tile))

        reduce.level(chips - 1 - step, also)
        pl.when(step == chips - 2)(units.pass_on)

    @pl.loop(0, rows // 32)
    def _(chunk):
        here = rows_at(chunk, 32)
        middle = x_ref[here, :].astype(jnp.float32) + out_ref[here, :]
        middle_ref[here, :] = middle
        normed_ref[here, :] = to_half(normalize(middle, gain_ref[0:1, :]))

    spread.rest()
    spread.sent()
    reduce.sent()
    d_kept.wait()
    units.end()


def branch_sum(seqs, chips, a, w, d_rows, units, x, gain, collective):
    rows, width = d_rows.shape
    group = 2 * chips
    half = jnp.bfloat16
    return pl.pallas_call(
        functools.partial(branch_kernel, seqs, chips),
        out_shape=[
            jax.ShapeDtypeStruct((rows, width), jnp.float32),
            jax.ShapeDtypeStruct((rows, width), half),
            jax.ShapeDtypeStruct((group, rows, width), half),
            jax.ShapeDtypeStruct((seqs,) + units.shape, half),
        ],
        in_specs=[VMEM_SPEC, VMEM_SPEC, ANY_SPEC, ANY_SPEC, VMEM_SPEC, VMEM_SPEC],
        out_specs=[VMEM_SPEC, VMEM_SPEC, ANY_SPEC, ANY_SPEC],
        scratch_shapes=[pltpu.VMEM((rows, width), jnp.float32)]
        + Reduce.scratch(chips, rows, width)
        + [sems(3, group, PARTS), sems(group, PARTS), pltpu.SemaphoreType.DMA]
        + [sems(seqs, 2), sems(seqs, 2), pltpu.SemaphoreType.DMA],
        compiler_params=comm_params(collective),
        cost_estimate=cost(
            2 * group * rows * width * w.shape[0], 250 * MIB, 3 * group * rows * width * 2
        ),
        name="branch_sum",
    )(a, w, d_rows, units, x, gain)


class PairReduce:
    def __init__(self, line, product, out, acc, keep, cross_out, cross_in, line_out, line_in, send, recv):
        self.line, self.product, self.out, self.acc, self.keep = line, product, out, acc, keep
        self.cross_out, self.cross_in, self.line_out, self.line_in = cross_out, cross_in, line_out, line_in
        self.send, self.recv = send, recv
        self.tiles = keep.shape[1] // TILE

    @staticmethod
    def scratch(chips, piece, width):
        half = jnp.bfloat16
        return [
            pltpu.VMEM((piece, width), half),
            pltpu.VMEM((2, piece, width), half),
            pltpu.VMEM((2, piece, width), half),
            pltpu.VMEM((chips + 1, piece, width), half),
            pltpu.SemaphoreType.DMA((3, width // TILE)),
            pltpu.SemaphoreType.DMA((chips + 3, width // TILE)),
        ]

    def cross(self, parity, tile):
        here = rows_at(tile, TILE)
        return pltpu.make_async_remote_copy(
            src_ref=self.cross_out.at[:, here],
            dst_ref=self.cross_in.at[parity, :, here],
            send_sem=self.send.at[0, tile],
            recv_sem=self.recv.at[self.line.chips + 1 + parity, tile],
            device_id={"fsdp": self.line.other},
            device_id_type=MESH,
        )

    def along(self, parity, landing, tile, peer):
        here = rows_at(tile, TILE)
        return pltpu.make_async_remote_copy(
            src_ref=self.line_out.at[parity, :, here],
            dst_ref=self.line_in.at[landing, :, here],
            send_sem=self.send.at[1 + parity, tile],
            recv_sem=self.recv.at[landing, tile],
            device_id={"fsdp": peer},
            device_id_type=MESH,
        )

    def steps(self):
        return 2 * self.line.chips - 1

    def step(self, step):
        line, keep = self.line, self.keep
        piece = keep.shape[0]
        right_side = line.chips - 1 - line.chip
        away = line.chips - 1 - step // 2
        second = lax.rem(step, 2)
        rightward = (right_side >= line.chip) == (second == 0)
        place = line.chip + jnp.where(rightward, away, -away)
        longer = jnp.maximum(right_side, line.chip)
        shorter = jnp.minimum(right_side, line.chip)
        count = longer - away + jnp.maximum(shorter - away, 0) + second
        parity = lax.rem(count + 2 * line.chips, 2)
        upstream = (rightward & line.has_left) | (jnp.logical_not(rightward) & line.has_right)

        @pl.when((place >= 0) & (place < line.chips))
        def _():
            wide = self.acc.shape[1]

            @pl.loop(0, keep.shape[1] // wide)
            def _(tile):
                here = rows_at(tile, wide)
                self.acc[...] = self.product(place, here)
                self.cross_out[:, here] = to_half(self.acc[rows_at(1 - line.core, piece), :])
                keep[:, here] = self.acc[rows_at(line.core, piece), :]
                for piece_of in range(wide // TILE):
                    self.cross(parity, tile * (wide // TILE) + piece_of).start()

            @pl.loop(0, self.tiles)
            def _(tile):
                here = rows_at(tile, TILE)
                self.cross(parity, tile).wait()
                keep[:, here] += self.cross_in[parity, :, here].astype(jnp.float32)

                @pl.when(away > 0)
                def _():
                    pl.when(count >= 2)(
                        lambda: self.along(parity, place, tile, line.own).wait_send()
                    )

                    @pl.when(upstream)
                    def _():
                        self.along(parity, place, tile, line.own).wait_recv()
                        self.line_out[parity, :, here] = to_half(
                            keep[:, here] + self.line_in[place, :, here].astype(jnp.float32)
                        )

                    @pl.when(jnp.logical_not(upstream))
                    def _():
                        self.line_out[parity, :, here] = to_half(keep[:, here])

                    @pl.when(rightward)
                    def _():
                        self.along(parity, place, tile, line.own + 2).start()

                    @pl.when(jnp.logical_not(rightward))
                    def _():
                        landing = jnp.where(away == 1, line.chips, place)
                        self.along(parity, landing, tile, line.own - 2).start()

                @pl.when(away == 0)
                def _():
                    self.out[:, here] = keep[:, here]

                    @pl.when(line.has_left)
                    def _():
                        self.along(parity, place, tile, line.own).wait_recv()
                        self.out[:, here] += self.line_in[place, :, here].astype(jnp.float32)

                    @pl.when(line.has_right)
                    def _():
                        self.along(parity, line.chips, tile, line.own).wait_recv()
                        self.out[:, here] += self.line_in[line.chips, :, here].astype(jnp.float32)

    def sent(self):
        for count in range(max(self.line.chips - 3, 0), self.line.chips - 1):
            pl.loop(0, self.tiles)(
                lambda tile, parity=count % 2: self.along(parity, 0, tile, self.line.own).wait_send()
            )


def feed_kernel(
    seqs, chips, batches, x_ref, w_hbm, wd_hbm, gd_hbm, v_ref, cot_ref, gain_ref,
    dm_ref, db_ref, gain_grad_ref, hidden_hbm, grad_hbm, grad_in,
    buf, d_buf, h_buf, w_ref, wd_ref, d_ref, tiles, totals, acc, keep,
    load, d_sem, h_sem, tile_sem, send, recv, part_send, part_recv, *sums,
):
    line = Line(chips)
    rows, width = x_ref.shape
    piece = rows // batches
    pair = 2 * piece
    units = wd_ref.shape[0]
    part = min(units, 2 * TILE)
    block = tiles.shape[1]
    loads = [
        pltpu.make_async_copy(w_hbm, w_ref, load.at[0]),
        pltpu.make_async_copy(wd_hbm, wd_ref, load.at[1]),
    ]
    for item in loads:
        item.start()
    meet(line.greet() + greet_seq(seqs))
    spreads = [
        Spread(
            line,
            x_ref.at[pl.ds(batch * piece, piece)],
            buf.at[batch],
            send.at[batch],
            recv.at[batch],
        )
        for batch in range(batches)
    ]
    spreads[0].begin()
    for batch in range(batches):
        buf[batch, line.own] = x_ref[batch * piece : (batch + 1) * piece, :]

    def fetch(batch, place, side):
        return [
            pltpu.make_async_copy(
                gd_hbm.at[place * 2 + core, pl.ds(batch * piece, piece)],
                d_buf.at[side, pl.ds(core * piece, piece)],
                d_sem.at[side, core],
            )
            for core in range(2)
        ]

    def stored(batch, place):
        return [
            pltpu.make_async_copy(
                h_buf.at[pl.ds(core * piece, piece)],
                hidden_hbm.at[
                    pl.ds(pl.multiple_of((place * 2 + core) * rows + batch * piece, piece), piece)
                ],
                h_sem.at[core],
            )
            for core in range(2)
        ]

    def sides(far, act):
        @pl.loop(0, 2)
        def _(side):
            place = line.chip + far * (2 * side - 1)
            valid = (place >= 0) & (place < chips) & ((side == 0) | (far > 0))
            pl.when(valid)(lambda: act(place, side))

    def take(batch, far):
        def begin(place, side):
            for item in fetch(batch, place, side):
                item.start()

        sides(far, begin)
        pl.when(far > 0)(lambda: spreads[batch].relay(far))

    def compute(batch, far):
        def act(place, side):
            spreads[batch].across(place * 2 + 1 - line.core)
            for item in fetch(batch, place, side):
                item.wait()

            def free():
                for item in stored(batch, place):
                    item.wait()

            if batch:
                free()
            else:
                pl.when((far > 0) | (side > 0))(free)
            there = rows_at(place, pair)

            @pl.loop(0, units // part)
            def _(tile):
                first = rows_at(tile, part)
                second = rows_at(units // part + tile, part)
                values = buf[batch, pl.ds(place * 2, 2), :, :].reshape(pair, width)
                gate = dot_nn(values, w_ref[:, first])
                up = dot_nn(values, w_ref[:, second])
                d_hidden = dot_nt(d_buf[side], wd_ref[first, :])
                sigma = jax.nn.sigmoid(gate)
                swish = gate * sigma
                h_buf[:, first] = to_half(swish * up)
                slope = sigma * (1.0 + gate * (1.0 - sigma))
                d_ref[batch, there, first] = to_half(d_hidden * up * slope)
                d_ref[batch, there, second] = to_half(d_hidden * swish)

            for item in stored(batch, place):
                item.start()

        sides(far, act)

    def product(batch):
        def get(place, here):
            return dot_nt(d_ref[batch, rows_at(place, pair), :], w_ref[here, :])

        return get

    reduces = [
        PairReduce(line, product(batch), totals.at[batch], acc, keep, *sums[6 * batch : 6 * batch + 6])
        for batch in range(batches)
    ]

    count = width // block
    seq = lax.axis_index("seq")

    near, far_off = seq_peers(seqs)
    soon = len(near)
    order = [peer * 2 for peer in near] + [peer * 2 for peer in far_off] + [seq * 2]
    order = order + [peer * 2 + 1 for peer in near] + [peer * 2 + 1 for peer in far_off] + [seq * 2 + 1]

    def tile_at(turn):
        tile = order[-1]
        for index in range(len(order) - 1):
            tile = jnp.where(turn == index, order[index], tile)
        return tile

    def grad_stored(turn):
        slot = lax.rem(turn, 2)
        return pltpu.make_async_copy(
            tiles.at[slot], grad_hbm.at[rows_at(tile_at(turn), block)], tile_sem.at[slot]
        )

    parts = ToPeers(seqs, near, grad_hbm, grad_in, part_send, part_recv)

    def leave(turn):
        grad_stored(turn).wait()
        for index in range(soon):
            pl.when(turn == index)(lambda index=index: parts.move(index).start())

    def weight_grad(turn):
        slot = lax.rem(turn, 2)
        size = min(4 * TILE, 2 * units)
        tile = tile_at(turn)

        @pl.loop(0, 2 * units // size)
        def _(column):
            here = rows_at(column, size)
            got = 0.0
            for batch in range(batches):
                left = buf[batch, :, :, rows_at(tile, block)].reshape(2 * chips * piece, block)
                got = got + contract_rows(left, d_ref[batch, :, here])
            tiles[slot, :, here] = to_half(got)

        pl.when(turn > 0)(lambda: leave(turn - 1))
        grad_stored(turn).start()

    def norm_batch(batch):
        own = pl.ds(batch * piece, piece)

        def put(here, d_values):
            there = pl.ds(pl.multiple_of(here.start + batch * piece, here.size), here.size)
            d_middle = cot_ref[there, :].astype(jnp.float32) + d_values
            dm_ref[there, :] = d_middle
            db_ref[there, :] = to_half(d_middle)

        norm_back(piece, v_ref.at[own], totals.at[batch], gain_ref, gain_grad_ref, put)

    gain_grad_ref[...] = jnp.zeros_like(gain_grad_ref)
    for item in loads:
        item.wait()
    last = 2 * chips - 2

    @pl.loop(0, chips)
    def _(far):
        take(0, far)
        pl.when(far == chips - 2)(spreads[1].begin)
        compute(0, far)

    @pl.loop(0, chips - 1)
    def _(far):
        take(1, far)
        reduces[0].step(2 * far)
        reduces[0].step(2 * far + 1)
        compute(1, far)

    take(1, chips - 1)
    compute(1, chips - 1)

    @pl.loop(0, 2)
    def _(step):
        reduces[1].step(step)
        weight_grad(step)

    reduces[0].step(last)
    norm_batch(0)

    @pl.loop(2, last)
    def _(step):
        reduces[1].step(step)
        pl.when(step < count)(lambda: weight_grad(step))

    @pl.loop(last, max(count, last))
    def _(tile):
        weight_grad(tile)

    reduces[1].step(last)
    norm_batch(1)
    for batch in range(batches):
        spreads[batch].sent()
        reduces[batch].sent()
    for item in stored(1, 0):
        item.wait()
    leave(count - 1)
    parts.end()


def feed_forward(seqs, chips, batches, x, w, wd, group_d, middle, cot, gain, collective):
    rows, width = x.shape
    group = 2 * chips
    units = wd.shape[0]
    piece = rows // batches
    block = width // seqs // 2
    half = jnp.bfloat16
    return pl.pallas_call(
        functools.partial(feed_kernel, seqs, chips, batches),
        out_shape=[
            jax.ShapeDtypeStruct((rows, width), jnp.float32),
            jax.ShapeDtypeStruct((rows, width), half),
            jax.ShapeDtypeStruct((8, width), jnp.float32),
            jax.ShapeDtypeStruct((group * rows, units), half),
            jax.ShapeDtypeStruct((width, 2 * units), half),
            jax.ShapeDtypeStruct((near_count(seqs), block, 2 * units), half),
        ],
        in_specs=[VMEM_SPEC] + [ANY_SPEC] * 3 + [VMEM_SPEC] * 3,
        out_specs=[VMEM_SPEC] * 3 + [ANY_SPEC] * 3,
        scratch_shapes=[
            pltpu.VMEM((batches, group, piece, width), half),
            pltpu.VMEM((2, 2 * piece, width), half),
            pltpu.VMEM((2 * piece, units), half),
            pltpu.VMEM(w.shape, half),
            pltpu.VMEM(wd.shape, half),
            pltpu.VMEM((batches, group * piece, 2 * units), half),
            pltpu.VMEM((2, block, 2 * units), half),
            pltpu.VMEM((batches, piece, width), jnp.float32),
            pltpu.VMEM((2 * piece, 2 * TILE), jnp.float32),
            pltpu.VMEM((piece, width), jnp.float32),
            sems(2),
            sems(2, 2),
            sems(2),
            sems(2),
            sems(batches, 3, group, PARTS // 2),
            sems(batches, group, PARTS // 2),
            sems(seqs),
            sems(seqs),
        ]
        + PairReduce.scratch(chips, piece, width) * batches,
        compiler_params=comm_params(collective, 63),
        cost_estimate=cost(
            14 * group * rows * width * units, 400 * MIB, 2 * group * rows * width * 2
        ),
        name="feed_forward",
    )(x, w, wd, group_d, middle, cot, gain)


def branch_back_kernel(
    seqs, chips, batches, x_ref, w_ref, att_ref, middle_ref, hidden_hbm, wd_hbm, units_hbm, gd_hbm,
    d_ref, layer_ref, out_grad_ref, half_in, whole_in, down_hbm, down_in,
    out_ref, buf, hidden_ref, wd_ref, grad_acc, rights, tiles, send, recv, load, right_sem, tile_sem,
    part_send, part_recv, down_send, down_recv, down_keep, acc, cross_out, line_out, cross_in, line_in, sum_send, sum_recv,
):
    line = Line(chips)
    rows = x_ref.shape[0]
    piece = rows // batches
    width = x_ref.shape[1]
    loads = [
        pltpu.make_async_copy(hidden_hbm, hidden_ref, load.at[0]),
        pltpu.make_async_copy(wd_hbm, wd_ref, load.at[1]),
    ]
    for item in loads:
        item.start()

    def product(slot, tile):
        return dot_nn(left_rows(hidden_ref, slot, rows), wd_ref[:, rows_at(tile, TILE)])

    part = rights.shape[2]
    count = width // part

    def right(tile):
        slot = lax.rem(tile, 2)
        return pltpu.make_async_copy(
            gd_hbm.at[:, rows_at(tile, part)], rights.at[slot], right_sem.at[slot]
        )

    def stored(tile):
        slot = lax.rem(tile, 2)
        return pltpu.make_async_copy(
            tiles.at[slot], down_hbm.at[:, rows_at(tile, part)], tile_sem.at[slot]
        )

    def weight_grad(tile):
        right(tile).wait()
        pl.when(tile + 1 < count)(lambda: right(tile + 1).start())
        pl.when(tile >= 2)(lambda: stored(tile - 2).wait())
        slot = lax.rem(tile, 2)
        size = min(TILE, hidden_ref.shape[1])

        @pl.loop(0, hidden_ref.shape[1] // size)
        def _(row):
            here = rows_at(row, size)
            tiles[slot, here, :] = to_half(contract_rows(hidden_ref[:, here], rights[slot]))

        stored(tile).start()

    right(0).start()
    meet(line.greet() + greet_seq(seqs))
    near, far_off = seq_peers(seqs)
    soon = len(near)
    halves = ToPeers(
        seqs, near, units_hbm, half_in, part_send.at[0], part_recv.at[0], half_in.shape[1]
    )
    wholes = ToPeers(seqs, far_off, units_hbm, whole_in, part_send.at[1], part_recv.at[1])
    down = ToPeers(
        seqs, near, down_hbm, down_in.at[pl.ds(0, soon)], down_send, down_recv
    )
    down_kept = pltpu.make_async_copy(
        down_hbm.at[rows_at(lax.axis_index("seq"), down_in.shape[1])], down_in.at[soon], down_keep
    )
    spread = Spread(line, x_ref, buf, send, recv)
    reduce = Reduce(
        line, product, out_ref, acc, cross_out, line_out, cross_in, line_in, sum_send, sum_recv
    )
    spread.begin()
    halves.begin()
    wholes.begin()
    buf[line.own] = x_ref[...]
    grad_acc[...] = jnp.zeros_like(grad_acc)

    def use(slot):
        got = to_half(dot_nt(buf[slot], w_ref[...]))
        for batch in range(batches):
            d_ref[batch, rows_at(slot, piece), :] = got[batch * piece : (batch + 1) * piece]
        mixed = left_rows(att_ref, slot, rows)

        @pl.loop(0, width // TILE)
        def _(tile):
            here = rows_at(tile, TILE)
            grad_acc[:, here] += contract_rows(mixed, buf[slot, :, here])

    for item in loads:
        item.wait()

    reduce.level(chips - 1, lambda tile: None)
    pl.loop(0, count)(weight_grad)
    stored(count - 2).wait()
    stored(count - 1).wait()
    down.begin()
    down_kept.start()
    spread.relay(1)
    spread.each(0, use)

    @pl.loop(1, chips)
    def _(step):
        def also(tile):
            pl.when(step < chips - 1)(lambda: spread.relay_part(step + 1, tile))

        reduce.level(chips - 1 - step, also)
        spread.each(step, use)

    spread.each(chips, use)

    @pl.loop(0, rows // 32)
    def _(chunk):
        here = rows_at(chunk, 32)
        layer_ref[here, :] = to_half(middle_ref[here, :] + out_ref[here, :])

    out_grad_ref[...] = to_half(grad_acc[...])
    spread.sent()
    reduce.sent()
    halves.end()
    wholes.end()
    down.end()
    down_kept.wait()


def branch_back(seqs, chips, batches, x, w, attended, middle, hidden, wd, unit_part, group_d, collective):
    rows, width = x.shape
    group = 2 * chips
    length = group * rows // batches
    span = w.shape[0]
    half = jnp.bfloat16
    part = 256 if group * rows <= 2048 else 128
    near, run = near_count(seqs), width // seqs
    return pl.pallas_call(
        functools.partial(branch_back_kernel, seqs, chips, batches),
        out_shape=[
            jax.ShapeDtypeStruct((batches, length, span), half),
            jax.ShapeDtypeStruct((rows, width), half),
            jax.ShapeDtypeStruct((span, width), half),
            jax.ShapeDtypeStruct((near, run // 2, unit_part.shape[1]), half),
            jax.ShapeDtypeStruct((seqs - 1 - near, run, unit_part.shape[1]), half),
            jax.ShapeDtypeStruct((wd.shape[0], width), half),
            jax.ShapeDtypeStruct((near + 1, wd.shape[0] // seqs, width), half),
        ],
        in_specs=[VMEM_SPEC] * 4 + [ANY_SPEC] * 4,
        out_specs=[VMEM_SPEC, VMEM_SPEC, VMEM_SPEC, ANY_SPEC, ANY_SPEC, ANY_SPEC, ANY_SPEC],
        scratch_shapes=[
            pltpu.VMEM((rows, width), jnp.float32),
            pltpu.VMEM((group, rows, width), half),
            pltpu.VMEM(hidden.shape, half),
            pltpu.VMEM(wd.shape, half),
            pltpu.VMEM((span, width), jnp.float32),
            pltpu.VMEM((2, group * rows, part), half),
            pltpu.VMEM((2, wd.shape[0], part), half),
            sems(3, group, PARTS),
            sems(group, PARTS),
            sems(2),
            sems(2),
            sems(2),
            sems(2, seqs),
            sems(2, seqs),
            sems(seqs),
            sems(seqs),
            pltpu.SemaphoreType.DMA,
        ]
        + Reduce.scratch(chips, rows, width),
        compiler_params=comm_params(collective, 62),
        cost_estimate=cost(
            2 * group * rows * width * (2 * span + 2 * wd.shape[0]),
            250 * MIB,
            2 * group * rows * width * 2,
        ),
        name="branch_back",
    )(x, w, attended, middle, hidden, wd, unit_part, group_d.reshape(group * rows, width))


def attention_back_kernel(
    seqs, chips, block, q_ref, pad_ref, low_ref, lse_ref, d_ref, part_hbm, in_one, in_two, in_far,
    w_ref, g_hbm, v_ref, dm_hbm, gain_ref, mlp_gain_ref, out_ref, down_hbm,
    grad_hbm, wq_ref, wk_ref, wv_ref, wo_hbm, tile_ref, gate_hbm, up_hbm, down_in,
    grad_ref, wo_ref, gate_ref, up_ref, result_sem, down_send, down_recv,
    dk, dv, kt, heads, back_out, back_in, unit_parts, unit_sums, units, lefts, parts, sums, cols, out_in,
    totals, gain_acc, gain_out, gain_in, gain_sum, gain_back, acc, keep,
    halo_send, halo_recv, unit_load, unit_send, unit_recv, unit_keep, dm_load, left_sem,
    part_send, part_recv, cols_send, cols_recv, out_send, out_recv,
    gain_send, gain_recv, back_send, back_recv, *line_sums,
):
    line = Line(chips)
    group = 2 * chips
    seq = lax.axis_index("seq")
    own = line.own
    batches, length, span = q_ref.shape
    rows, width = v_ref.shape
    piece = rows // batches
    pair_rows = 2 * piece
    depth = 3 * span
    run = width // seqs
    share = run // group
    part = lefts.shape[3]
    steps, need = length // block, WINDOW // block
    first = length - WINDOW
    has_left, has_right = seq > 0, seq < seqs - 1
    scale = jnp.asarray(HEAD**-0.5, jnp.bfloat16)

    def others(count, me, act):
        pl.loop(1, count)(lambda ahead: act(lax.rem(me + ahead, count)))

    def unit_loaded(turn, place, source):
        slot = lax.rem(turn, 2)
        return pltpu.make_async_copy(source, unit_parts.at[slot, place], unit_load.at[slot, place])

    def load_units(turn):
        member = lax.rem(own + turn, group)
        unit_loaded(turn, 0, part_hbm.at[rows_at(seq * group + member, share)]).start()
        soon = in_one.shape[0]
        for index in range(seqs - 1):

            def fetch(source, index=index):
                unit_loaded(turn, index + 1, source).start()

            if index < soon:

                @pl.when(member < chips)
                def _(index=index, fetch=fetch):
                    fetch(in_one.at[index, rows_at(member, share)])

                @pl.when(member >= chips)
                def _(index=index, fetch=fetch):
                    fetch(in_two.at[index, rows_at(member - chips, share)])

            else:
                fetch(in_far.at[index - soon, rows_at(member, share)])

    load_units(1)
    dm_loaded = pltpu.make_async_copy(dm_hbm, grad_ref, dm_load)
    dm_loaded.start()
    meet(greet_group(group) + greet_seq(seqs))
    near, far_off = seq_peers(seqs)
    down = ToPeers(seqs, far_off, down_hbm, down_in, down_send, down_recv)
    swap = Swap(group, unit_sums, units, unit_send, unit_recv, unit_keep)

    @pl.loop(1, group + 1)
    def _(turn):
        member = lax.rem(own + turn, group)
        slot = lax.rem(turn, 2)
        pl.when(turn < group)(lambda: load_units(turn + 1))
        for place in range(seqs):
            unit_loaded(turn, place, part_hbm.at[rows_at(0, share)]).wait()

        @pl.loop(0, share // 16)
        def _(chunk):
            here = rows_at(chunk, 16)
            added = unit_parts[slot, 0, here, :].astype(jnp.float32)
            for place in range(1, seqs):
                added = added + unit_parts[slot, place, here, :].astype(jnp.float32)
            unit_sums[member, here, :] = to_half(added)

        pl.when(turn < group)(lambda: swap.move(member, own).start())
        pl.when(turn == group)(lambda: swap.kept().start())

    def halo(batch, step, peer):
        here = rows_at(step, block)
        return pltpu.make_async_remote_copy(
            src_ref=back_out.at[batch, here],
            dst_ref=back_in.at[batch, here],
            send_sem=halo_send.at[batch, step],
            recv_sem=halo_recv.at[batch, step],
            device_id={"seq": peer},
            device_id_type=MESH,
        )

    def attend_block(batch, step):
        begin = pl.multiple_of(step * block, block)
        keys = pl.ds(begin, block + WINDOW)
        rows = pl.ds(begin, block)
        low = low_ref[batch, :, rows]
        for pair in range(span // PAIR):
            lanes = slice(pair * PAIR, (pair + 1) * PAIR)
            q_pair = q_ref[batch, rows, lanes] * scale
            d_pair = d_ref[batch, rows, lanes]
            k_rows = pad_ref[batch, keys, lanes]
            v_rows = pad_ref[batch, keys, span + pair * PAIR : span + (pair + 1) * PAIR]
            k_cols = kt[lanes, keys]
            back = []
            for half in range(2):
                row = pair * 2 + half
                q_head = head_lanes(q_pair, half)
                d_head = head_lanes(d_pair, half)
                scores = masked_scores(k_rows, q_head, low)
                probs = jnp.exp(scores - lse_ref[batch, row : row + 1, rows])
                d_probs = dot_nt(v_rows, d_head)
                along = jnp.sum(probs * d_probs, axis=0, keepdims=True)
                d_scores = to_half(probs * (d_probs - along))
                dv[keys, lanes] += dot_nn(to_half(probs), d_head)
                dk[keys, lanes] += dot_nn(d_scores, q_head)
                back.append(dot_nn(k_cols, d_scores))
            at = lax.broadcasted_iota(jnp.int32, back[0].shape, 0)
            heads[batch, rows, lanes] = to_half(
                jnp.where(at < HEAD, back[0], back[1]).T
            )


        @pl.when(has_left & (step < need))
        def _():
            back_out[batch, rows, :span] = to_half(dk[rows, :])
            back_out[batch, rows, span:] = to_half(dv[rows, :])
            halo(batch, step, seq - 1).start()

        @pl.when(step == steps - 1)
        def _():
            heads[batch, :, span : 2 * span] = to_half(dk[WINDOW:, :])
            heads[batch, :, 2 * span :] = to_half(dv[WINDOW:, :])

    def add_halo(batch):
        @pl.when(has_right)
        def _():
            @pl.loop(0, need)
            def _(step):
                there = pl.ds(pl.multiple_of(step * block + first, block), block)
                halo(batch, step, seq).wait_recv()
                got = back_in[batch, rows_at(step, block), :].astype(jnp.float32)
                mine = heads[batch, there, span:].astype(jnp.float32)
                heads[batch, there, span:] = to_half(mine + got)

    def product(batch):
        def get(place, here):
            return dot_nt(heads[batch, rows_at(place, pair_rows), :], w_ref[here, :])

        return get

    reduces = [
        PairReduce(
            line, product(batch), totals.at[batch], acc, keep, *line_sums[6 * batch : 6 * batch + 6]
        )
        for batch in range(batches)
    ]
    last = 2 * chips - 2

    @pl.loop(0, 2 * steps)
    def _(turn):
        batch, step = turn // steps, lax.rem(turn, steps)

        @pl.when(step == 0)
        def _():
            kt[...] = pad_ref[batch, :, :span].T * scale
            dk[...] = jnp.zeros_like(dk)
            dv[...] = jnp.zeros_like(dv)

        attend_block(batch, step)
        after = turn - steps - 1
        pl.when(after == 0)(lambda: add_halo(0))

        @pl.when((after >= 0) & (2 * after < last))
        def _():
            reduces[0].step(2 * after)
            reduces[0].step(2 * after + 1)

    for after in range(steps - 1, chips - 1):
        reduces[0].step(2 * after)
        reduces[0].step(2 * after + 1)

    def left(tile):
        slot = lax.rem(tile, 2)
        return pltpu.make_async_copy(
            g_hbm.at[:, :, rows_at(tile, part)], lefts.at[slot], left_sem.at[slot]
        )

    heads_near = ToPeers(seqs, near + far_off, parts, sums, part_send, part_recv)
    left(0).start()
    add_halo(1)

    @pl.loop(0, width // part)
    def _(tile):
        left(tile).wait()
        pl.when(tile + 1 < width // part)(lambda: left(tile + 1).start())
        slot = lax.rem(tile, 2)
        got = contract_rows(lefts[slot, 0], heads[0])
        for batch in range(1, batches):
            got = got + contract_rows(lefts[slot, batch], heads[batch])
        parts[rows_at(tile, part), :] = to_half(got)

    heads_near.begin()
    from_seq = ToPeers(seqs, near + far_off, out_ref, out_in, out_send, out_recv)
    from_seq.begin()
    gain_acc[...] = jnp.zeros_like(gain_acc)
    dm_loaded.wait()

    def norm_batch(batch):
        mine = pl.ds(batch * piece, piece)

        def put(here, d_values):
            there = pl.ds(pl.multiple_of(here.start + batch * piece, here.size), here.size)
            grad_ref[there, :] += d_values

        norm_back(piece, v_ref.at[mine], totals.at[batch], gain_ref, gain_acc, put)

    pl.loop(0, 2)(reduces[1].step)
    reduces[0].step(last)
    norm_batch(0)
    pl.loop(2, last)(reduces[1].step)
    swap.end()
    cell = units.shape[2] // 2 // seqs
    for member in range(group):
        for place in range(seqs):
            column = (place * group + member) * cell
            for target, begin in ((gate_ref, 0), (up_ref, seqs * cell)):
                here = slice(begin + place * cell, begin + (place + 1) * cell)
                target[:, column : column + cell] = units[member, :, here]

    results = [
        pltpu.make_async_copy(source, target, result_sem.at[index])
        for index, (source, target) in enumerate(
            ((gate_ref, gate_hbm), (up_ref, up_hbm), (wo_ref, wo_hbm), (grad_ref, grad_hbm))
        )
    ]
    results[0].start()
    results[1].start()

    def block_swap(peer, member):
        return pltpu.make_async_remote_copy(
            src_ref=parts.at[rows_at(seq * group + peer, share)],
            dst_ref=cols.at[member],
            send_sem=cols_send.at[peer],
            recv_sem=cols_recv.at[member],
            device_id={"fsdp": peer},
            device_id_type=MESH,
        )

    heads_near.arrived()
    down.begin()

    @pl.loop(0, run // 64)
    def _(chunk):
        here = rows_at(chunk, 64)
        there = pl.ds(pl.multiple_of(seq * run + chunk * 64, 64), 64)
        parts[there, :] = to_half(add_from_seq(parts[there, :], sums, here))

    others(group, own, lambda peer: block_swap(peer, own).start())
    cols[own] = parts[rows_at(seq * group + own, share), :]
    from_seq.arrived()
    out_rows = out_in.shape[1]
    wo_ref[...] = add_from_seq(out_ref[rows_at(seq, out_rows), :], out_in, slice(None))
    results[2].start()
    reduces[1].step(last)
    norm_batch(1)
    results[3].start()
    fold = 128 // share
    near = group // fold
    attn_row = jnp.sum(gain_acc[...], axis=0, keepdims=True)
    mlp_row = jnp.sum(mlp_gain_ref[...], axis=0, keepdims=True)
    gain_out[...] = jnp.zeros_like(gain_out)
    for place in range(width // 128):
        lanes = slice(place * 128, (place + 1) * 128)
        gain_out[place % near, place // near, 0:1, :] = attn_row[:, lanes]
        gain_out[place % near, place // near, 1:2, :] = mlp_row[:, lanes]

    def gain_group(peer, member):
        return pltpu.make_async_remote_copy(
            src_ref=gain_out.at[peer // fold],
            dst_ref=gain_in.at[member],
            send_sem=gain_send.at[peer],
            recv_sem=gain_recv.at[member],
            device_id={"fsdp": peer},
            device_id_type=MESH,
        )

    def gain_seq(peer, place):
        return pltpu.make_async_remote_copy(
            src_ref=gain_sum.at[peer],
            dst_ref=gain_back.at[place],
            send_sem=back_send.at[peer],
            recv_sem=back_recv.at[place],
            device_id={"seq": peer},
            device_id_type=MESH,
        )

    others(group, own, lambda peer: gain_group(peer, own).start())
    gain_in[own] = gain_out[own // fold]
    others(group, own, lambda peer: gain_group(peer, peer).wait_recv())
    gain_sum[...] = jnp.sum(gain_in[...], axis=0)
    others(seqs, seq, lambda peer: gain_seq(peer, seq).start())
    gain_back[seq] = gain_sum[seq]
    others(seqs, seq, lambda peer: gain_seq(peer, peer).wait_recv())
    tile_ref[...] = jnp.sum(gain_back[...], axis=0)
    others(group, own, lambda peer: block_swap(peer, peer).wait_recv())
    for index, target in enumerate((wq_ref, wk_ref, wv_ref)):
        for member, first, home, size in column_parts(seqs, group, share, span):
            first = first + index * span
            target[:, home : home + size] = cols[member, :, first : first + size]
    from_seq.sent()
    for item in results:
        item.wait()
    for batch in range(batches):
        reduces[batch].sent()

        @pl.when(has_left)
        def _(batch=batch):
            pl.loop(0, need)(lambda step: halo(batch, step, seq).wait_send())

    heads_near.sent()
    down.end()
    others(group, own, lambda peer: gain_group(peer, own).wait_send())
    others(group, own, lambda peer: block_swap(peer, own).wait_send())
    others(seqs, seq, lambda peer: gain_seq(peer, seq).wait_send())


def attention_back(
    seqs, chips, block, query, kv_pad, low, lse, d_att, part_own, parts_one, parts_two, parts_far, w, group_a,
    x, d_middle, gain, mlp_gain, out_part, down, collective,
):
    batches, length, span = query.shape
    padded = kv_pad.shape[1]
    rows, width = x.shape
    piece = rows // batches
    group = 2 * chips
    depth = w.shape[1]
    run = width // seqs
    share = run // group
    near = group // (128 // share)
    cells = part_own.shape[1]
    out_rows = out_part.shape[0] // seqs
    half, wide = jnp.bfloat16, jnp.float32
    part = 256 if batches * length <= 2048 else 128
    return pl.pallas_call(
        functools.partial(attention_back_kernel, seqs, chips, block),
        out_shape=[
            jax.ShapeDtypeStruct((rows, width), wide),
            jax.ShapeDtypeStruct((share, width), half),
            jax.ShapeDtypeStruct((share, width), half),
            jax.ShapeDtypeStruct((share, width), half),
            jax.ShapeDtypeStruct((out_rows, width), wide),
            jax.ShapeDtypeStruct((8, 128), wide),
            jax.ShapeDtypeStruct((share, cells // 2 * group), half),
            jax.ShapeDtypeStruct((share, cells // 2 * group), half),
            jax.ShapeDtypeStruct((seqs - 1 - near_count(seqs), down.shape[0] // seqs, width), half),
        ],
        in_specs=[VMEM_SPEC] * 5
        + [ANY_SPEC] * 4
        + [VMEM_SPEC, ANY_SPEC, VMEM_SPEC, ANY_SPEC]
        + [VMEM_SPEC] * 3
        + [ANY_SPEC],
        out_specs=[ANY_SPEC, VMEM_SPEC, VMEM_SPEC, VMEM_SPEC, ANY_SPEC, VMEM_SPEC]
        + [ANY_SPEC] * 3,
        scratch_shapes=[
            pltpu.VMEM((rows, width), wide),
            pltpu.VMEM((out_rows, width), wide),
            pltpu.VMEM((share, cells // 2 * group), half),
            pltpu.VMEM((share, cells // 2 * group), half),
            sems(4),
            sems(seqs),
            sems(seqs),
            pltpu.VMEM((padded, span), wide),
            pltpu.VMEM((padded, span), wide),
            pltpu.VMEM((span, padded), half),
            pltpu.VMEM((batches, length, depth), half),
            pltpu.VMEM((batches, WINDOW, 2 * span), half),
            pltpu.VMEM((batches, WINDOW, 2 * span), half),
            pltpu.VMEM((2, seqs, share, cells), half),
            pltpu.VMEM((group, share, cells), half),
            pltpu.VMEM((group, share, cells), half),
            pltpu.VMEM((2, batches, length, part), half),
            pltpu.VMEM((width, depth), half),
            pltpu.VMEM((seqs - 1, run, depth), half),
            pltpu.VMEM((group, share, depth), half),
            pltpu.VMEM((seqs - 1, out_rows, width), half),
            pltpu.VMEM((batches, piece, width), wide),
            pltpu.VMEM((8, width), wide),
            pltpu.VMEM((near, seqs, 8, 128), wide),
            pltpu.VMEM((group, seqs, 8, 128), wide),
            pltpu.VMEM((seqs, 8, 128), wide),
            pltpu.VMEM((seqs, 8, 128), wide),
            pltpu.VMEM((2 * piece, TILE), wide),
            pltpu.VMEM((piece, width), wide),
            sems(batches, WINDOW // block),
            sems(batches, WINDOW // block),
            sems(2, seqs),
            sems(group),
            sems(group),
            pltpu.SemaphoreType.DMA,
            pltpu.SemaphoreType.DMA,
            sems(2),
            sems(seqs),
            sems(seqs),
            sems(group),
            sems(group),
            sems(seqs),
            sems(seqs),
            sems(group),
            sems(group),
            sems(seqs),
            sems(seqs),
        ]
        + PairReduce.scratch(chips, piece, width) * batches,
        compiler_params=comm_params(collective, 63),
        cost_estimate=cost(
            20 * batches * length * span * (WINDOW + block) + 4 * group * rows * width * depth,
            400 * MIB,
            3 * group * rows * width * 2,
        ),
        name="attention_back",
    )(
        query, kv_pad, low, lse, d_att, part_own, parts_one, parts_two, parts_far, w, group_a, x,
        d_middle, gain, mlp_gain, out_part, down,
    )


def finish_kernel(count, *refs):
    sources, targets = refs[:-count], refs[-count:]
    for source, target in zip(sources, targets[:-1]):
        target[...] = source[...].astype(target.dtype)
    added = 0.0
    for source in sources[count - 1 :]:
        added = added + jnp.sum(source[...].astype(jnp.float32), axis=0)
    targets[-1][...] = added


def finish(steps, arrays, parts, kinds):
    in_specs, out_specs, out_shape = [], [], []
    for item, kind in zip(arrays + parts[:1], kinds):
        rows, width = item.shape[-2:]
        block = (rows // steps, width)
        out_specs.append(pl.BlockSpec(block, lambda i: (i, 0)))
        out_shape.append(jax.ShapeDtypeStruct((rows, width), kind))
        if item.ndim == 2:
            in_specs.append(out_specs[-1])
    for item in parts:
        in_specs.append(pl.BlockSpec((item.shape[0],) + block, lambda i: (0, i, 0)))
    return pl.pallas_call(
        functools.partial(finish_kernel, len(kinds)),
        grid=(steps,),
        in_specs=in_specs,
        out_specs=out_specs,
        out_shape=out_shape,
        compiler_params=pltpu.CompilerParams(vmem_limit_bytes=63 * MIB),
        name="finish",
    )(*arrays, *parts)


def doc_starts(lengths, positions, batches, seq_len):
    table = lengths.reshape(batches, -1, lengths.shape[1])
    starts = jnp.cumsum(table, axis=2) - table
    per_batch = seq_len // table.shape[1]
    begins = (starts + (jnp.arange(table.shape[1], dtype=jnp.int32) * per_batch)[None, :, None]).reshape(
        batches, -1
    )
    before = begins[:, None, :] <= positions[None, :, None]
    return jnp.max(jnp.where(before, begins[:, None, :], 0), axis=2)


def body(
    tokens,
    cotangent,
    lengths,
    gain_attn,
    w_query,
    w_key,
    w_value,
    w_out,
    gain_mlp,
    w_gate,
    w_up,
    w_down,
):
    batches, piece, width = tokens.shape
    seqs = lax.axis_size("seq")
    group = lax.axis_size("fsdp")
    chips = group // 2
    devices = seqs * group
    seq_len = piece * devices
    rows = batches * piece
    share = w_query.shape[0]
    span = width // group
    length = group * piece
    aligned = share == HEAD
    member = lax.axis_index("fsdp")

    x_rows = tokens.reshape(rows, width)
    cot_rows = cotangent.reshape(rows, width)
    wd_part = lax.all_gather(w_down, "seq", axis=0, tiled=True)
    if aligned:
        wo_part = lax.all_gather(w_out, "seq", axis=0, tiled=True)
    else:
        wo_all = lax.all_gather(w_out, ("seq", "fsdp"), axis=0, tiled=True)
        wo_part = lax.dynamic_slice_in_dim(wo_all, member * span, span, 0)

    lane = jnp.arange(128, dtype=jnp.int32)
    device = lax.axis_index("seq") * group + member
    fold = 128 // share
    here = lane // share == lax.rem(device, fold)
    both = jnp.stack([gain_attn, gain_mlp]).astype(jnp.float32)
    tile = jnp.where(here[None], jnp.tile(both, (1, fold)), 0.0)
    tile = jnp.pad(tile, ((0, 6), (0, 0)))[None]
    group_start = lax.axis_index("seq") * length
    positions = group_start + jnp.arange(length, dtype=jnp.int32)
    begins = doc_starts(lengths, positions, batches, seq_len)
    at = jnp.arange(length, dtype=jnp.int32)
    block = min(256, length)
    low = jnp.maximum(begins - group_start + WINDOW, at[None, :] + 1) - (at // block * block)[None, :]
    low = low[:, None, :]
    group_a, query, attended, lse, kv_pad, gains, w_heads, unit_own = start(
        seqs, chips, batches, block, tile, x_rows, (w_query, w_key, w_value), (w_gate, w_up), low, 1
    )
    gains = gains.transpose(1, 0, 2, 3).reshape(devices // fold, fold, 8, 128).sum(axis=1)
    gain_one = gains[:, 0].reshape(width)
    gain_two = gains[:, 1].reshape(width)
    middle, normed_b, group_d, w_units = branch_sum(
        seqs, chips, attended, wo_part, cot_rows, unit_own.reshape(group * share, -1),
        x_rows, gain_two[None], 3,
    )
    w_units = w_units.reshape(width, -1)
    d_middle, d_branch, mlp_gain_part, hidden, unit_part, unit_one = feed_forward(
        seqs, chips, batches, normed_b, w_units, wd_part, group_d, middle, cot_rows,
        gain_two[None], 4,
    )
    d_attended, layer_out, out_part, unit_two, unit_far, down_part, down_near = branch_back(
        seqs, chips, batches, d_branch, wo_part, attended, middle, hidden, wd_part, unit_part,
        group_d, 5,
    )
    if not aligned:
        whole = lax.dynamic_update_slice_in_dim(
            jnp.zeros((width, width), jnp.bfloat16), out_part, member * span, 0
        )
        out_part = lax.psum(whole, "fsdp").reshape(seqs, group, share, width)
        out_part = lax.dynamic_slice_in_dim(out_part, member, 1, 1).reshape(seqs * share, width)
    (
        input_grad, wq_grad, wk_grad, wv_grad, wo_grad, gain_tile, gate_grad, up_grad, down_far,
    ) = attention_back(
        seqs, chips, block, query, kv_pad, low, lse, d_attended, unit_part, unit_one, unit_two,
        unit_far, w_heads, group_a, x_rows, d_middle, gain_one[None], mlp_gain_part, out_part,
        down_part, 6,
    )
    gain_grads = lax.dynamic_slice_in_dim(gain_tile[:2], lax.rem(device, fold) * share, share, 1)
    wide = jnp.float32
    (layer_out, input_grad, wq_grad, wk_grad, wv_grad, wo_grad, gate_grad, up_grad, down_grad) = finish(
        share // 16,
        [layer_out, input_grad, wq_grad, wk_grad, wv_grad, wo_grad, gate_grad, up_grad],
        [down_near, down_far],
        [jnp.bfloat16] + [wide] * 8,
    )
    return (
        layer_out.reshape(batches, piece, width),
        input_grad.reshape(batches, piece, width),
        gain_grads[0],
        wq_grad,
        wk_grad,
        wv_grad,
        wo_grad,
        gain_grads[1],
        gate_grad,
        up_grad,
        down_grad,
    )


def solution(mesh):
    spread = ("seq", "fsdp")
    tokens, rows, gains = P(None, spread, None), P(spread, None), P(spread)
    in_specs = (tokens, tokens, P(), gains, rows, rows, rows, rows, gains, rows, rows, rows)
    out_specs = (tokens, tokens, gains, rows, rows, rows, rows, gains, rows, rows, rows)
    return jax.shard_map(body, mesh=mesh, in_specs=in_specs, out_specs=out_specs, check_vma=False)
```

```python
import functools

import jax
import jax.numpy as jnp
from jax import lax
from jax.experimental import pallas as pl
from jax.experimental.pallas import tpu as pltpu
from jax.sharding import PartitionSpec as P

HEAD = 64
FF = 8192
WINDOW = 1024
PAIR = 128
TILE = 512
PARTS = 4
LOW = -1e30
EPS = 1e-05
MESH = pl.DeviceIdType.MESH
MIB = 2**20


def to_half(values):
    return values.astype(jnp.bfloat16)


def normalize(values, gain):
    return values * lax.rsqrt(jnp.mean(values * values, axis=-1, keepdims=True) + EPS) * gain


def contract_rows(left, right):
    return lax.dot_general(
        left, right, (((0,), (0,)), ((), ())), preferred_element_type=jnp.float32
    )


def dot_nt(left, right):
    return lax.dot_general(
        left, right, (((1,), (1,)), ((), ())), preferred_element_type=jnp.float32
    )


def dot_nn(left, right):
    return jnp.dot(left, right, preferred_element_type=jnp.float32)


def head_lanes(values, half):
    lane = lax.broadcasted_iota(jnp.int32, values.shape, 1)
    return jnp.where((lane >= HEAD) == (half == 1), values, jnp.zeros_like(values))


def masked_scores(k_rows, q_head, low):
    keys, block = k_rows.shape[0], q_head.shape[0]
    scores = dot_nt(k_rows, q_head)
    at = lax.broadcasted_iota(jnp.int32, (keys, block), 0)
    query = lax.broadcasted_iota(jnp.int32, (keys, block), 1)
    seen = (at >= low) & (at <= query + WINDOW)
    return jnp.where(seen, scores, LOW)


class Line:
    def __init__(self, chips):
        self.chips = chips
        self.own = lax.axis_index("fsdp")
        self.chip = self.own // 2
        self.core = lax.rem(self.own, 2)
        self.other = self.own + 1 - 2 * self.core
        self.has_left = self.chip > 0
        self.has_right = self.chip < chips - 1

    def greet(self):
        signal_group(self.other)
        pl.when(self.has_left)(lambda: signal_group(self.own - 2))
        pl.when(self.has_right)(lambda: signal_group(self.own + 2))
        return 1 + self.has_left.astype(jnp.int32) + self.has_right.astype(jnp.int32)


def signal_group(peer):
    barrier = pltpu.get_barrier_semaphore()
    pl.semaphore_signal(barrier, inc=1, device_id={"fsdp": peer}, device_id_type=MESH)


def signal_seq(peer):
    barrier = pltpu.get_barrier_semaphore()
    pl.semaphore_signal(barrier, inc=1, device_id={"seq": peer}, device_id_type=MESH)


def greet_group(group):
    own = lax.axis_index("fsdp")
    pl.loop(1, group)(lambda ahead: signal_group(lax.rem(own + ahead, group)))
    return group - 1


def greet_seq(seqs):
    own = lax.axis_index("seq")
    pl.loop(1, seqs)(lambda ahead: signal_seq(lax.rem(own + ahead, seqs)))
    return seqs - 1


def meet(count):
    pl.semaphore_wait(pltpu.get_barrier_semaphore(), count)


def rows_at(index, size):
    return pl.ds(pl.multiple_of(index * size, size), size)


class Spread:
    def __init__(self, line, first, buf, send, recv):
        self.line, self.first, self.buf, self.send, self.recv = line, first, buf, send, recv
        self.parts = recv.shape[1]
        self.size = first.shape[0] // self.parts

    def move(self, slot, part, way, peer, source=None):
        here = rows_at(part, self.size)
        return pltpu.make_async_remote_copy(
            src_ref=self.buf.at[slot, here] if source is None else source.at[here],
            dst_ref=self.buf.at[slot, here],
            send_sem=self.send.at[way, slot, part],
            recv_sem=self.recv.at[slot, part],
            device_id={"fsdp": peer},
            device_id_type=MESH,
        )

    def begin(self):
        line = self.line

        @pl.loop(0, self.parts)
        def _(part):
            pl.when(line.has_right)(
                lambda: self.move(line.own, part, 1, line.own + 2, self.first).start()
            )
            pl.when(line.has_left)(
                lambda: self.move(line.own, part, 0, line.own - 2, self.first).start()
            )
            self.move(line.own, part, 2, line.other, self.first).start()

    def relay_part(self, far, part):
        line = self.line

        @pl.when(line.chip - far >= 0)
        def _():
            slot = (line.chip - far) * 2 + line.core
            self.move(slot, part, 1, line.own).wait_recv()
            pl.when(line.has_right)(lambda: self.move(slot, part, 1, line.own + 2).start())
            self.move(slot, part, 2, line.other).start()

        @pl.when(line.chip + far < line.chips)
        def _():
            slot = (line.chip + far) * 2 + line.core
            self.move(slot, part, 0, line.own).wait_recv()
            pl.when(line.has_left)(lambda: self.move(slot, part, 0, line.own - 2).start())
            self.move(slot, part, 2, line.other).start()

    def relay(self, far):
        pl.loop(0, self.parts)(lambda part: self.relay_part(far, part))

    def across(self, slot):
        pl.loop(0, self.parts)(lambda part: self.move(slot, part, 2, self.line.own).wait_recv())

    def each(self, far, use):
        line = self.line

        @pl.loop(0, 4)
        def _(turn):
            side = lax.rem(turn, 2)
            over = turn // 2
            away = far - over
            source = line.chip + away * (2 * side - 1)
            valid = (away >= 0) & (away < line.chips) & (source >= 0) & (source < line.chips)
            valid = valid & ((side == 0) | (away > 0))

            @pl.when(valid)
            def _():
                slot = source * 2 + line.core + over * (1 - 2 * line.core)
                pl.when(over == 1)(lambda: self.across(slot))
                use(slot)

    def rest(self):
        pl.loop(0, self.line.chips)(lambda place: self.across(place * 2 + 1 - self.line.core))

    def sent(self):
        line = self.line

        @pl.loop(0, line.chips)
        def _(place):
            slot = place * 2 + line.core

            @pl.loop(0, self.parts)
            def _(part):
                self.move(slot, part, 2, line.other).wait_send()
                pl.when(line.has_right & (place <= line.chip))(
                    lambda: self.move(slot, part, 1, line.own + 2).wait_send()
                )
                pl.when(line.has_left & (place >= line.chip))(
                    lambda: self.move(slot, part, 0, line.own - 2).wait_send()
                )


class Reduce:
    def __init__(self, line, product, out, acc, cross_out, line_out, cross_in, line_in, send, recv):
        self.line, self.product, self.out, self.acc = line, product, out, acc
        self.cross_out, self.line_out, self.cross_in, self.line_in = cross_out, line_out, cross_in, line_in
        self.send, self.recv = send, recv
        self.tiles = line_out.shape[2] // TILE

    @staticmethod
    def scratch(chips, rows, width):
        part = pltpu.VMEM((chips, rows, width), jnp.bfloat16)
        return [
            pltpu.VMEM((rows, TILE), jnp.float32),
            pltpu.VMEM((2, rows, width), jnp.bfloat16),
            part,
            part,
            pltpu.VMEM((chips + 1, rows, width), jnp.bfloat16),
            pltpu.SemaphoreType.DMA((2, chips, width // TILE)),
            pltpu.SemaphoreType.DMA((2, chips + 1, width // TILE)),
        ]

    def cross(self, side, place, tile):
        here = rows_at(tile, TILE)
        return pltpu.make_async_remote_copy(
            src_ref=self.cross_out.at[side, :, here],
            dst_ref=self.cross_in.at[place, :, here],
            send_sem=self.send.at[0, place, tile],
            recv_sem=self.recv.at[0, place, tile],
            device_id={"fsdp": self.line.other},
            device_id_type=MESH,
        )

    def along(self, place, landing, tile, peer):
        here = rows_at(tile, TILE)
        return pltpu.make_async_remote_copy(
            src_ref=self.line_out.at[place, :, here],
            dst_ref=self.line_in.at[landing, :, here],
            send_sem=self.send.at[1, place, tile],
            recv_sem=self.recv.at[1, landing, tile],
            device_id={"fsdp": peer},
            device_id_type=MESH,
        )

    def where(self, away, side):
        line = self.line
        rightward = (line.chips - 1 - line.chip >= line.chip) == (side == 0)
        place = line.chip + jnp.where(rightward, away, -away)
        valid = (place >= 0) & (place < line.chips) & ((away > 0) | (side == 0))
        return valid, place, rightward

    def level(self, away, also):
        @pl.loop(0, 2)
        def _(side):
            valid, place, _ = self.where(away, side)

            @pl.when(valid)
            def _():
                @pl.loop(0, self.tiles)
                def _(tile):
                    got = self.product(place * 2 + 1 - self.line.core, tile)
                    self.cross_out[side, :, rows_at(tile, TILE)] = to_half(got)
                    self.cross(side, place, tile).start()

        @pl.loop(0, self.tiles)
        def _(tile):
            @pl.loop(0, 2)
            def _(side):
                valid, place, rightward = self.where(away, side)
                pl.when(valid)(lambda: self.close(away, side, place, rightward, tile))

            also(tile)

    def close(self, away, side, place, rightward, tile):
        line, acc = self.line, self.acc
        here = rows_at(tile, TILE)
        upstream = (rightward & line.has_left) | (jnp.logical_not(rightward) & line.has_right)
        acc[...] = self.product(place * 2 + line.core, tile)
        self.cross(side, place, tile).wait()
        acc[...] += self.cross_in[place, :, here].astype(jnp.float32)

        @pl.when(away > 0)
        def _():
            @pl.when(upstream)
            def _():
                self.along(place, place, tile, line.own).wait_recv()
                self.line_out[place, :, here] = to_half(
                    acc[...] + self.line_in[place, :, here].astype(jnp.float32)
                )

            @pl.when(jnp.logical_not(upstream))
            def _():
                self.line_out[place, :, here] = to_half(acc[...])

            @pl.when(rightward)
            def _():
                self.along(place, place, tile, line.own + 2).start()

            @pl.when(jnp.logical_not(rightward))
            def _():
                landing = jnp.where(away == 1, line.chips, place)
                self.along(place, landing, tile, line.own - 2).start()

        @pl.when(away == 0)
        def _():
            self.out[:, here] = acc[...]

            @pl.when(line.has_left)
            def _():
                self.along(place, place, tile, line.own).wait_recv()
                self.out[:, here] += self.line_in[place, :, here].astype(jnp.float32)

            @pl.when(line.has_right)
            def _():
                self.along(place, line.chips, tile, line.own).wait_recv()
                self.out[:, here] += self.line_in[line.chips, :, here].astype(jnp.float32)

    def sent(self):
        @pl.loop(0, self.line.chips)
        def _(place):
            @pl.when(place != self.line.chip)
            def _():
                pl.loop(0, self.tiles)(
                    lambda tile: self.along(place, place, tile, self.line.own).wait_send()
                )


class Swap:
    def __init__(self, group, source, target, send, recv, keep):
        self.group, self.source, self.target = group, source, target
        self.send, self.recv, self.keep = send, recv, keep
        self.own = lax.axis_index("fsdp")

    def move(self, peer, source):
        return pltpu.make_async_remote_copy(
            src_ref=self.source.at[peer],
            dst_ref=self.target.at[source],
            send_sem=self.send.at[peer],
            recv_sem=self.recv.at[source],
            device_id={"fsdp": peer},
            device_id_type=MESH,
        )

    def kept(self):
        return pltpu.make_async_copy(self.source.at[self.own], self.target.at[self.own], self.keep)

    def begin(self):
        self.kept().start()
        pl.loop(1, self.group)(
            lambda ahead: self.move(lax.rem(self.own + ahead, self.group), self.own).start()
        )

    def end(self):
        self.kept().wait()

        @pl.loop(1, self.group)
        def _(ahead):
            peer = lax.rem(self.own + ahead, self.group)
            self.move(peer, peer).wait_recv()
            self.move(peer, self.own).wait_send()


class Share:
    def __init__(self, seqs, source, target, send, recv, keep):
        self.seqs, self.source, self.target = seqs, source, target
        self.send, self.recv, self.keep = send, recv, keep
        self.own = lax.axis_index("seq")
        self.half = source.shape[0] // 2

    def move(self, peer, place):
        return pltpu.make_async_remote_copy(
            src_ref=self.source,
            dst_ref=self.target.at[place],
            send_sem=self.send.at[peer, 0],
            recv_sem=self.recv.at[place, 0],
            device_id={"seq": peer},
            device_id_type=MESH,
        )

    def relay(self, peer, place, part):
        here = pl.ds(part * self.half, self.half)
        return pltpu.make_async_remote_copy(
            src_ref=self.target.at[place, here],
            dst_ref=self.target.at[place, here],
            send_sem=self.send.at[peer, 1],
            recv_sem=self.recv.at[place, part],
            device_id={"seq": peer},
            device_id_type=MESH,
        )

    def near(self):
        one = self.own + 1 - 2 * lax.rem(self.own, 2)
        two = lax.rem(self.own + 2, 4)
        return one, two, lax.rem(one + 2, 4)

    def kept(self):
        return pltpu.make_async_copy(self.source, self.target.at[self.own], self.keep)

    def begin(self):
        self.kept().start()
        if self.seqs == 4:
            one, two, _ = self.near()
            self.move(one, self.own).start()
            self.move(two, self.own).start()
        else:
            pl.loop(1, self.seqs)(
                lambda ahead: self.move(lax.rem(self.own + ahead, self.seqs), self.own).start()
            )

    def pass_on(self):
        if self.seqs == 4:
            one, two, _ = self.near()
            self.move(one, one).wait_recv()
            self.relay(two, one, 0).start()
            self.move(two, two).wait_recv()
            self.relay(one, two, 1).start()

    def end(self):
        self.kept().wait()
        if self.seqs == 4:
            one, two, far = self.near()
            self.relay(two, far, 0).wait_recv()
            self.relay(one, far, 1).wait_recv()
            self.move(one, self.own).wait_send()
            self.move(two, self.own).wait_send()
            self.relay(two, one, 0).wait_send()
            self.relay(one, two, 1).wait_send()
        else:

            @pl.loop(1, self.seqs)
            def _(ahead):
                peer = lax.rem(self.own + ahead, self.seqs)
                self.move(peer, peer).wait_recv()
                self.move(peer, self.own).wait_send()


def seq_peers(seqs):
    own = lax.axis_index("seq")
    if seqs == 4:
        one = own + 1 - 2 * lax.rem(own, 2)
        return [one, lax.rem(own + 2, 4)], [lax.rem(one + 2, 4)]
    ahead = [lax.rem(own + step, seqs) for step in range(1, seqs)]
    return ahead[:1], ahead[1:]


def near_count(seqs):
    return 2 if seqs == 4 else 1


class ToPeers:
    def __init__(self, seqs, peers, source, target, send, recv, first=0):
        self.peers, self.source, self.target, self.send, self.recv = peers, source, target, send, recv
        self.run, self.first = source.shape[0] // seqs, first

    def move(self, index):
        begin = pl.multiple_of(self.peers[index] * self.run + self.first, 16)
        return pltpu.make_async_remote_copy(
            src_ref=self.source.at[pl.ds(begin, self.target.shape[1])],
            dst_ref=self.target.at[index],
            send_sem=self.send.at[index],
            recv_sem=self.recv.at[index],
            device_id={"seq": self.peers[index]},
            device_id_type=MESH,
        )

    def begin(self):
        for index in range(len(self.peers)):
            self.move(index).start()

    def arrived(self):
        for index in range(len(self.peers)):
            self.move(index).wait_recv()

    def sent(self):
        for index in range(len(self.peers)):
            self.move(index).wait_send()

    def end(self):
        self.arrived()
        self.sent()


def load_halves(halves, target, load):
    copies = []
    rows = halves[0].shape[1]
    for index, half in enumerate(halves):
        for place in range(half.shape[0]):
            there = pl.ds((2 * place + index) * rows, rows)
            copies.append(pltpu.make_async_copy(half.at[place], target.at[there], load.at[index, place]))
    return copies


VMEM_SPEC = pl.BlockSpec(memory_space=pltpu.VMEM)
ANY_SPEC = pl.BlockSpec(memory_space=pl.ANY)


def comm_params(collective, mib=58):
    return pltpu.CompilerParams(
        collective_id=collective, has_side_effects=True, vmem_limit_bytes=mib * MIB
    )


def cost(flops, local, remote):
    return pl.CostEstimate(
        flops=flops, bytes_accessed=local, transcendentals=0, remote_bytes_transferred=remote
    )


def sems(*shape):
    return pltpu.SemaphoreType.DMA(shape)


def left_rows(a_ref, slot, rows):
    if len(a_ref.shape) == 2:
        return a_ref[rows_at(slot, rows), :]
    piece = rows // a_ref.shape[0]
    return jnp.concatenate(
        [a_ref[batch, rows_at(slot, piece), :] for batch in range(a_ref.shape[0])], axis=0
    )


def norm_back(rows, v_ref, e_ref, gain_ref, gain_acc, put):
    @pl.loop(0, rows // 32)
    def _(chunk):
        here = rows_at(chunk, 32)
        values = v_ref[here, :].astype(jnp.float32)
        error = e_ref[here, :]
        rate = lax.rsqrt(jnp.mean(values * values, axis=-1, keepdims=True) + EPS)
        unit = values * rate
        product = error * unit
        gain = gain_ref[0:1, :]
        mean = jnp.mean(product * gain, axis=-1, keepdims=True)
        gain_acc[...] += (product[0:8] + product[8:16]) + (product[16:24] + product[24:32])
        put(here, rate * (gain * error - unit * mean))


def add_from_seq(own_rows, got, here):
    added = own_rows.astype(jnp.float32)
    for index in range(got.shape[0]):
        added = added + got[index, here, :].astype(jnp.float32)
    return added


def column_parts(seqs, group, share, span):
    size = HEAD if share == HEAD else span
    parts = []
    for member in range(group):
        for run in range(span // size):
            home = (run * group + member) * size
            parts.append((member, run * size, home, size))
    return parts


def start_kernel(
    seqs, chips, batches, block, tile_ref, x_ref, wq_ref, wk_ref, wv_ref, gate_hbm, up_hbm, down_hbm, low_ref,
    g_ref, q_ref, out_ref, lse_ref, pad_ref, gains_ref, w_out_ref, own_units_ref, wd_ref,
    gate, up, units, blocks_ref, buf, normed, pad, vt, gain, gains, w,
    unit_sem, send, recv, keep, swap_send, share_send, w_recv,
    tile_send, tile_across, tile_recv, tile_back, w_keep, gain_keep,
    halo_send, halo_recv, pad_keep, unit_send, unit_recv, unit_keep,
    down_send, down_recv, down_keep,
):
    line = Line(chips)
    group = 2 * chips
    seq = lax.axis_index("seq")
    own = line.own
    share = blocks_ref.shape[1]
    rows, width = x_ref.shape
    piece = rows // batches
    length, span = q_ref.shape[1:]
    per = 128 * seqs * group // width
    steps, need = length // block, WINDOW // block
    has_left, has_right = seq > 0, seq < seqs - 1
    unit_loads = [
        pltpu.make_async_copy(gate_hbm, gate, unit_sem.at[0]),
        pltpu.make_async_copy(up_hbm, up, unit_sem.at[1]),
    ]
    for item in unit_loads:
        item.start()
    for index, source in enumerate((wq_ref, wk_ref, wv_ref)):
        for member, first, home, size in column_parts(seqs, group, share, span):
            first = first + index * span
            blocks_ref[member, :, first : first + size] = source[:, home : home + size]
    meet(greet_group(group) + greet_seq(seqs))

    def block_at(run, member):
        return w.at[rows_at(run * group + member, share)]

    def block_swap(peer, member):
        return pltpu.make_async_remote_copy(
            src_ref=blocks_ref.at[peer],
            dst_ref=block_at(seq, member),
            send_sem=swap_send.at[peer],
            recv_sem=w_recv.at[seq, member],
            device_id={"fsdp": peer},
            device_id_type=MESH,
        )

    def block_share(run, member, peer):
        return pltpu.make_async_remote_copy(
            src_ref=block_at(run, member),
            dst_ref=block_at(run, member),
            send_sem=share_send.at[peer, member],
            recv_sem=w_recv.at[run, member],
            device_id={"seq": peer},
            device_id_type=MESH,
        )

    def tile_to_seq(peer, place):
        return pltpu.make_async_remote_copy(
            src_ref=tile_ref.at[0],
            dst_ref=gains.at[own, place],
            send_sem=tile_send.at[peer],
            recv_sem=tile_recv.at[place],
            device_id={"seq": peer},
            device_id_type=MESH,
        )

    def tiles_to_group(peer, member):
        return pltpu.make_async_remote_copy(
            src_ref=gains.at[member],
            dst_ref=gains.at[member],
            send_sem=tile_across.at[peer],
            recv_sem=tile_back.at[member],
            device_id={"fsdp": peer},
            device_id_type=MESH,
        )

    def others(count, me, act):
        pl.loop(1, count)(lambda ahead: act(lax.rem(me + ahead, count)))

    others(seqs, seq, lambda peer: tile_to_seq(peer, seq).start())
    down = Share(
        seqs, down_hbm.at[pl.ds(0, wd_ref.shape[1])], wd_ref, down_send, down_recv, down_keep
    )
    down.begin()
    others(group, own, lambda peer: block_swap(peer, own).start())
    spreads = [
        Spread(line, x_ref.at[pl.ds(batch * piece, piece)], buf.at[batch], send.at[batch], recv.at[batch])
        for batch in range(batches)
    ]
    spreads[0].begin()
    gains[own, seq] = tile_ref[0]
    w[rows_at(seq * group + own, share), :] = blocks_ref[own]
    others(seqs, seq, lambda peer: block_share(seq, own, peer).start())
    for batch in range(batches):
        buf[batch, own] = x_ref[batch * piece : (batch + 1) * piece, :]
    others(seqs, seq, lambda peer: tile_to_seq(peer, peer).wait_recv())
    others(group, own, lambda peer: tiles_to_group(peer, own).start())
    for item in unit_loads:
        item.wait()
    cell = units.shape[2] // 2 // seqs
    for member in range(group):
        for run in range(seqs):
            home = (run * group + member) * cell
            for index, source in enumerate((gate, up)):
                first = (index * seqs + run) * cell
                units[member, :, first : first + cell] = source[:, home : home + cell]
    unit_swap = Swap(group, units, own_units_ref, unit_send, unit_recv, unit_keep)

    @pl.when(jnp.logical_not(has_left))
    def _():
        pad[:, :WINDOW, :] = jnp.zeros((batches, WINDOW, 2 * span), jnp.bfloat16)

    def pass_block(member):
        block_swap(member, member).wait_recv()
        others(seqs, seq, lambda peer: block_share(seq, member, peer).start())

    others(group, own, pass_block)
    down.pass_on()
    others(group, own, lambda peer: tiles_to_group(peer, peer).wait_recv())
    for column in range(width // 128):
        total = 0.0
        for place in range(column * per, (column + 1) * per):
            total = total + gains[place % group, place // group, 0:1, :]
        gain[0:1, column * 128 : (column + 1) * 128] = total

    def sides(far, act):
        @pl.loop(0, 2)
        def _(side):
            place = line.chip + far * (2 * side - 1)
            valid = (place >= 0) & (place < chips) & ((side == 0) | (far > 0))
            pl.when(valid)(lambda: act(place))

    def kept(batch, place):
        here = rows_at(place, block)
        return pltpu.make_async_copy(
            normed.at[batch, here], g_ref.at[batch, here], keep.at[batch, place]
        )

    def norm_pair(batch, place):
        spreads[batch].across(place * 2 + 1 - line.core)

        @pl.loop(0, 2)
        def _(member):
            @pl.loop(0, piece // 64)
            def _(chunk):
                values = buf[batch, place * 2 + member, rows_at(chunk, 64), :].astype(jnp.float32)
                there = pl.multiple_of(place * block + member * piece + chunk * 64, 64)
                normed[batch, pl.ds(there, 64), :] = to_half(normalize(values, gain[0:1, :]))

        kept(batch, place).start()

    def halo(batch, step, peer):
        there = pl.multiple_of(WINDOW + (step + steps - need) * block, block)
        return pltpu.make_async_remote_copy(
            src_ref=pad.at[batch, pl.ds(there, block)],
            dst_ref=pad.at[batch, rows_at(step, block)],
            send_sem=halo_send.at[batch, step],
            recv_sem=halo_recv.at[batch, step],
            device_id={"seq": peer},
            device_id_type=MESH,
        )

    def project(batch, place):
        here = rows_at(place, block)
        got = to_half(dot_nn(normed[batch, here, :], w[...]))
        q_ref[batch, here, :] = got[:, :span]
        pad[batch, pl.ds(pl.multiple_of(WINDOW + place * block, block), block), :] = got[:, span:]

        @pl.when(has_right & (place >= steps - need))
        def _():
            halo(batch, place - (steps - need), seq + 1).start()

    @pl.loop(0, chips)
    def _(far):
        pl.when(far > 0)(lambda: spreads[0].relay(far))
        pl.when(far == chips - 2)(spreads[1].begin)
        sides(far, lambda place: norm_pair(0, place))

    spreads[1].relay(1)

    def have_block(run, member):
        block_share(run, member, seq).wait_recv()

    others(seqs, seq, lambda run: pl.loop(0, group)(lambda member: have_block(run, member)))
    w_kept = pltpu.make_async_copy(w, w_out_ref, w_keep)
    w_kept.start()
    gains_kept = pltpu.make_async_copy(gains, gains_ref, gain_keep)
    gains_kept.start()
    pl.loop(0, steps)(lambda place: project(0, place))

    @pl.loop(2, chips)
    def _(far):
        spreads[1].relay(far)

    unit_swap.begin()

    @pl.loop(0, chips)
    def _(far):
        sides(far, lambda place: norm_pair(1, place))
        sides(far, lambda place: project(1, place))

    def pad_kept(batch):
        return pltpu.make_async_copy(pad.at[batch], pad_ref.at[batch], pad_keep.at[batch])

    for batch in range(batches):
        vt[:, WINDOW:] = pad[batch, WINDOW:, span:].T

        @pl.loop(0, steps)
        def _(turn, batch=batch):
            step = steps - 1 - turn

            @pl.when(step < need)
            def _():
                arrived = rows_at(step, block)
                pl.when(has_left)(lambda: halo(batch, step, seq).wait_recv())
                vt[:, arrived] = pad[batch, arrived, span:].T

            begin = pl.multiple_of(step * block, block)
            keys = pl.ds(begin, block + WINDOW)
            rows = pl.ds(begin, block)
            low = low_ref[batch, :, rows]
            for pair in range(span // PAIR):
                lanes = slice(pair * PAIR, (pair + 1) * PAIR)
                q_pair = q_ref[batch, rows, lanes] * jnp.asarray(HEAD**-0.5, jnp.bfloat16)
                k_rows = pad[batch, keys, lanes]
                values = vt[lanes, keys]
                mixed = []
                for half in range(2):
                    scores = masked_scores(k_rows, head_lanes(q_pair, half), low)
                    top = jnp.max(scores, axis=0, keepdims=True)
                    expo = jnp.exp(scores - top)
                    total = jnp.sum(expo, axis=0, keepdims=True)
                    mixed.append(dot_nn(values, to_half(expo)) / total)
                    row = pair * 2 + half
                    lse_ref[batch, row : row + 1, rows] = top + jnp.log(total)
                lane = lax.broadcasted_iota(jnp.int32, mixed[0].shape, 0)
                out_ref[batch, rows, lanes] = to_half(jnp.where(lane < HEAD, mixed[0], mixed[1]).T)

        pad_kept(batch).start()

    for batch in range(batches):
        spreads[batch].sent()
    others(seqs, seq, lambda peer: tile_to_seq(peer, seq).wait_send())
    others(group, own, lambda peer: block_swap(peer, own).wait_send())
    others(group, own, lambda peer: tiles_to_group(peer, own).wait_send())
    others(
        seqs,
        seq,
        lambda peer: pl.loop(0, group)(lambda member: block_share(seq, member, peer).wait_send()),
    )

    @pl.loop(0, need)
    def _(step):
        for batch in range(batches):
            pl.when(has_right)(lambda batch=batch: halo(batch, step, seq).wait_send())

    w_kept.wait()
    gains_kept.wait()
    unit_swap.end()
    down.end()
    for batch in range(batches):
        pad_kept(batch).wait()

        @pl.loop(0, steps)
        def _(place, batch=batch):
            kept(batch, place).wait()


def start(seqs, chips, batches, block, tile, x, weights, unit_weights, down, low, collective):
    rows, width = x.shape
    group = 2 * chips
    length = group * rows // batches
    share = weights[0].shape[0]
    span = width // group
    cols = 3 * span
    wide = unit_weights[0].shape[1]
    cells = 2 * wide // group
    piece = rows // batches
    padded = length + WINDOW
    half = jnp.bfloat16
    need = WINDOW // block
    return pl.pallas_call(
        functools.partial(start_kernel, seqs, chips, batches, block),
        out_shape=[
            jax.ShapeDtypeStruct((batches, length, width), half),
            jax.ShapeDtypeStruct((batches, length, span), half),
            jax.ShapeDtypeStruct((batches, length, span), half),
            jax.ShapeDtypeStruct((batches, span // HEAD, length), jnp.float32),
            jax.ShapeDtypeStruct((batches, padded, 2 * span), half),
            jax.ShapeDtypeStruct((group, seqs, 8, 128), jnp.float32),
            jax.ShapeDtypeStruct((width, cols), half),
            jax.ShapeDtypeStruct((group, share, cells), half),
            jax.ShapeDtypeStruct((seqs, down.shape[0] // 2, width), half),
        ],
        in_specs=[VMEM_SPEC] * 5 + [ANY_SPEC] * 3 + [VMEM_SPEC],
        out_specs=[ANY_SPEC] + [VMEM_SPEC] * 3 + [ANY_SPEC] * 5,
        scratch_shapes=[
            pltpu.VMEM((share, wide), half),
            pltpu.VMEM((share, wide), half),
            pltpu.VMEM((group, share, cells), half),
            pltpu.VMEM((group, share, cols), half),
            pltpu.VMEM((batches, group, piece, width), half),
            pltpu.VMEM((batches, length, width), half),
            pltpu.VMEM((batches, padded, 2 * span), half),
            pltpu.VMEM((span, padded), half),
            pltpu.VMEM((8, width), jnp.float32),
            pltpu.VMEM((group, seqs, 8, 128), jnp.float32),
            pltpu.VMEM((width, cols), half),
            sems(2),
            sems(batches, 3, group, PARTS // 2),
            sems(batches, group, PARTS // 2),
            sems(batches, chips),
            sems(group),
            sems(seqs, group),
            sems(seqs, group),
            sems(seqs),
            sems(group),
            sems(seqs),
            sems(group),
            pltpu.SemaphoreType.DMA,
            pltpu.SemaphoreType.DMA,
            sems(batches, need),
            sems(batches, need),
            sems(batches),
            sems(group),
            sems(group),
            pltpu.SemaphoreType.DMA,
            sems(seqs, 2),
            sems(seqs, 2),
            pltpu.SemaphoreType.DMA,
        ],
        compiler_params=comm_params(collective, 62),
        cost_estimate=cost(
            2 * group * rows * width * cols + 8 * batches * length * span * (WINDOW + block),
            300 * MIB,
            2 * group * rows * width * 2,
        ),
        name="start",
    )(tile, x, *weights, *unit_weights, down, low)


def branch_kernel(
    seqs, chips, a_ref, w_ref, d_ref, units_ref, down_hbm, x_ref, gain_ref,
    middle_ref, normed_ref, gd_ref, w_units_ref, wd_ref,
    out_ref, acc, cross_out, line_out, cross_in, line_in, sum_send, sum_recv,
    send, recv, d_keep, share_send, share_recv, share_keep,
    down_send, down_recv, down_keep,
):
    line = Line(chips)
    rows = out_ref.shape[0]

    def product(slot, tile):
        return dot_nn(left_rows(a_ref, slot, rows), w_ref[:, rows_at(tile, TILE)])

    meet(line.greet() + greet_seq(seqs))
    reduce = Reduce(
        line, product, out_ref, acc, cross_out, line_out, cross_in, line_in, sum_send, sum_recv
    )
    spread = Spread(line, d_ref, gd_ref, send, recv)
    units = Share(seqs, units_ref, w_units_ref, share_send, share_recv, share_keep)
    d_kept = pltpu.make_async_copy(d_ref, gd_ref.at[line.own], d_keep)
    half = wd_ref.shape[1]
    down = Share(seqs, down_hbm.at[pl.ds(half, half)], wd_ref, down_send, down_recv, down_keep)
    units.begin()
    down.begin()
    spread.begin()
    d_kept.start()

    @pl.loop(0, chips)
    def _(step):
        def also(tile):
            pl.when(step < chips - 1)(lambda: spread.relay_part(step + 1, tile))

        reduce.level(chips - 1 - step, also)

        @pl.when(step == chips - 2)
        def _():
            units.pass_on()
            down.pass_on()

    @pl.loop(0, rows // 32)
    def _(chunk):
        here = rows_at(chunk, 32)
        middle = x_ref[here, :].astype(jnp.float32) + out_ref[here, :]
        middle_ref[here, :] = middle
        normed_ref[here, :] = to_half(normalize(middle, gain_ref[0:1, :]))

    spread.rest()
    spread.sent()
    reduce.sent()
    d_kept.wait()
    units.end()
    down.end()


def branch_sum(seqs, chips, a, w, d_rows, units, down, x, gain, collective):
    rows, width = d_rows.shape
    group = 2 * chips
    half = jnp.bfloat16
    return pl.pallas_call(
        functools.partial(branch_kernel, seqs, chips),
        out_shape=[
            jax.ShapeDtypeStruct((rows, width), jnp.float32),
            jax.ShapeDtypeStruct((rows, width), half),
            jax.ShapeDtypeStruct((group, rows, width), half),
            jax.ShapeDtypeStruct((seqs,) + units.shape, half),
            jax.ShapeDtypeStruct((seqs, down.shape[0] // 2, width), half),
        ],
        in_specs=[VMEM_SPEC, VMEM_SPEC] + [ANY_SPEC] * 3 + [VMEM_SPEC, VMEM_SPEC],
        out_specs=[VMEM_SPEC, VMEM_SPEC] + [ANY_SPEC] * 3,
        scratch_shapes=[pltpu.VMEM((rows, width), jnp.float32)]
        + Reduce.scratch(chips, rows, width)
        + [sems(3, group, PARTS), sems(group, PARTS), pltpu.SemaphoreType.DMA]
        + [sems(seqs, 2), sems(seqs, 2), pltpu.SemaphoreType.DMA] * 2,
        compiler_params=comm_params(collective),
        cost_estimate=cost(
            2 * group * rows * width * w.shape[0], 250 * MIB, 3 * group * rows * width * 2
        ),
        name="branch_sum",
    )(a, w, d_rows, units, down, x, gain)


class PairReduce:
    def __init__(self, line, product, out, acc, keep, cross_out, cross_in, line_out, line_in, send, recv):
        self.line, self.product, self.out, self.acc, self.keep = line, product, out, acc, keep
        self.cross_out, self.cross_in, self.line_out, self.line_in = cross_out, cross_in, line_out, line_in
        self.send, self.recv = send, recv
        self.tiles = keep.shape[1] // TILE

    @staticmethod
    def scratch(chips, piece, width):
        half = jnp.bfloat16
        return [
            pltpu.VMEM((piece, width), half),
            pltpu.VMEM((2, piece, width), half),
            pltpu.VMEM((2, piece, width), half),
            pltpu.VMEM((chips + 1, piece, width), half),
            pltpu.SemaphoreType.DMA((3, width // TILE)),
            pltpu.SemaphoreType.DMA((chips + 3, width // TILE)),
        ]

    def cross(self, parity, tile):
        here = rows_at(tile, TILE)
        return pltpu.make_async_remote_copy(
            src_ref=self.cross_out.at[:, here],
            dst_ref=self.cross_in.at[parity, :, here],
            send_sem=self.send.at[0, tile],
            recv_sem=self.recv.at[self.line.chips + 1 + parity, tile],
            device_id={"fsdp": self.line.other},
            device_id_type=MESH,
        )

    def along(self, parity, landing, tile, peer):
        here = rows_at(tile, TILE)
        return pltpu.make_async_remote_copy(
            src_ref=self.line_out.at[parity, :, here],
            dst_ref=self.line_in.at[landing, :, here],
            send_sem=self.send.at[1 + parity, tile],
            recv_sem=self.recv.at[landing, tile],
            device_id={"fsdp": peer},
            device_id_type=MESH,
        )

    def steps(self):
        return 2 * self.line.chips - 1

    def step(self, step):
        line, keep = self.line, self.keep
        piece = keep.shape[0]
        right_side = line.chips - 1 - line.chip
        away = line.chips - 1 - step // 2
        second = lax.rem(step, 2)
        rightward = (right_side >= line.chip) == (second == 0)
        place = line.chip + jnp.where(rightward, away, -away)
        longer = jnp.maximum(right_side, line.chip)
        shorter = jnp.minimum(right_side, line.chip)
        count = longer - away + jnp.maximum(shorter - away, 0) + second
        parity = lax.rem(count + 2 * line.chips, 2)
        upstream = (rightward & line.has_left) | (jnp.logical_not(rightward) & line.has_right)

        @pl.when((place >= 0) & (place < line.chips))
        def _():
            wide = self.acc.shape[1]

            @pl.loop(0, keep.shape[1] // wide)
            def _(tile):
                here = rows_at(tile, wide)
                self.acc[...] = self.product(place, here)
                self.cross_out[:, here] = to_half(self.acc[rows_at(1 - line.core, piece), :])
                keep[:, here] = self.acc[rows_at(line.core, piece), :]
                for piece_of in range(wide // TILE):
                    self.cross(parity, tile * (wide // TILE) + piece_of).start()

            @pl.loop(0, self.tiles)
            def _(tile):
                here = rows_at(tile, TILE)
                self.cross(parity, tile).wait()
                keep[:, here] += self.cross_in[parity, :, here].astype(jnp.float32)

                @pl.when(away > 0)
                def _():
                    pl.when(count >= 2)(
                        lambda: self.along(parity, place, tile, line.own).wait_send()
                    )

                    @pl.when(upstream)
                    def _():
                        self.along(parity, place, tile, line.own).wait_recv()
                        self.line_out[parity, :, here] = to_half(
                            keep[:, here] + self.line_in[place, :, here].astype(jnp.float32)
                        )

                    @pl.when(jnp.logical_not(upstream))
                    def _():
                        self.line_out[parity, :, here] = to_half(keep[:, here])

                    @pl.when(rightward)
                    def _():
                        self.along(parity, place, tile, line.own + 2).start()

                    @pl.when(jnp.logical_not(rightward))
                    def _():
                        landing = jnp.where(away == 1, line.chips, place)
                        self.along(parity, landing, tile, line.own - 2).start()

                @pl.when(away == 0)
                def _():
                    self.out[:, here] = keep[:, here]

                    @pl.when(line.has_left)
                    def _():
                        self.along(parity, place, tile, line.own).wait_recv()
                        self.out[:, here] += self.line_in[place, :, here].astype(jnp.float32)

                    @pl.when(line.has_right)
                    def _():
                        self.along(parity, line.chips, tile, line.own).wait_recv()
                        self.out[:, here] += self.line_in[line.chips, :, here].astype(jnp.float32)

    def sent(self):
        for count in range(max(self.line.chips - 3, 0), self.line.chips - 1):
            pl.loop(0, self.tiles)(
                lambda tile, parity=count % 2: self.along(parity, 0, tile, self.line.own).wait_send()
            )


def feed_kernel(
    seqs, chips, batches, x_ref, w_hbm, wd_one, wd_two, gd_hbm, v_ref, cot_ref, gain_ref,
    dm_ref, db_ref, gain_grad_ref, hidden_hbm, grad_hbm, grad_in,
    buf, d_buf, h_buf, w_ref, wd_ref, d_ref, tiles, totals, acc, keep,
    load, d_sem, h_sem, tile_sem, send, recv, part_send, part_recv, wd_load, *sums,
):
    line = Line(chips)
    rows, width = x_ref.shape
    piece = rows // batches
    pair = 2 * piece
    units = wd_ref.shape[0]
    part = min(units, 2 * TILE)
    block = tiles.shape[1]
    loads = [
        pltpu.make_async_copy(w_hbm, w_ref, load.at[0]),
    ] + load_halves([wd_one, wd_two], wd_ref, wd_load)
    for item in loads:
        item.start()
    meet(line.greet() + greet_seq(seqs))
    spreads = [
        Spread(
            line,
            x_ref.at[pl.ds(batch * piece, piece)],
            buf.at[batch],
            send.at[batch],
            recv.at[batch],
        )
        for batch in range(batches)
    ]
    spreads[0].begin()
    for batch in range(batches):
        buf[batch, line.own] = x_ref[batch * piece : (batch + 1) * piece, :]

    def fetch(batch, place, side):
        return [
            pltpu.make_async_copy(
                gd_hbm.at[place * 2 + core, pl.ds(batch * piece, piece)],
                d_buf.at[side, pl.ds(core * piece, piece)],
                d_sem.at[side, core],
            )
            for core in range(2)
        ]

    def stored(batch, place):
        return [
            pltpu.make_async_copy(
                h_buf.at[pl.ds(core * piece, piece)],
                hidden_hbm.at[
                    pl.ds(pl.multiple_of((place * 2 + core) * rows + batch * piece, piece), piece)
                ],
                h_sem.at[core],
            )
            for core in range(2)
        ]

    def sides(far, act):
        @pl.loop(0, 2)
        def _(side):
            place = line.chip + far * (2 * side - 1)
            valid = (place >= 0) & (place < chips) & ((side == 0) | (far > 0))
            pl.when(valid)(lambda: act(place, side))

    def take(batch, far):
        def begin(place, side):
            for item in fetch(batch, place, side):
                item.start()

        sides(far, begin)
        pl.when(far > 0)(lambda: spreads[batch].relay(far))

    def compute(batch, far):
        def act(place, side):
            spreads[batch].across(place * 2 + 1 - line.core)
            for item in fetch(batch, place, side):
                item.wait()

            def free():
                for item in stored(batch, place):
                    item.wait()

            if batch:
                free()
            else:
                pl.when((far > 0) | (side > 0))(free)
            there = rows_at(place, pair)

            @pl.loop(0, units // part)
            def _(tile):
                first = rows_at(tile, part)
                second = rows_at(units // part + tile, part)
                values = buf[batch, pl.ds(place * 2, 2), :, :].reshape(pair, width)
                gate = dot_nn(values, w_ref[:, first])
                up = dot_nn(values, w_ref[:, second])
                d_hidden = dot_nt(d_buf[side], wd_ref[first, :])
                sigma = jax.nn.sigmoid(gate)
                swish = gate * sigma
                h_buf[:, first] = to_half(swish * up)
                slope = sigma * (1.0 + gate * (1.0 - sigma))
                d_ref[batch, there, first] = to_half(d_hidden * up * slope)
                d_ref[batch, there, second] = to_half(d_hidden * swish)

            for item in stored(batch, place):
                item.start()

        sides(far, act)

    def product(batch):
        def get(place, here):
            return dot_nt(d_ref[batch, rows_at(place, pair), :], w_ref[here, :])

        return get

    reduces = [
        PairReduce(line, product(batch), totals.at[batch], acc, keep, *sums[6 * batch : 6 * batch + 6])
        for batch in range(batches)
    ]

    count = width // block
    seq = lax.axis_index("seq")

    near, far_off = seq_peers(seqs)
    soon = seqs - 1
    order = [peer * 2 for peer in near] + [peer * 2 for peer in far_off] + [seq * 2]
    order = order + [peer * 2 + 1 for peer in near] + [peer * 2 + 1 for peer in far_off] + [seq * 2 + 1]

    def tile_at(turn):
        tile = order[-1]
        for index in range(len(order) - 1):
            tile = jnp.where(turn == index, order[index], tile)
        return tile

    def grad_stored(turn):
        slot = lax.rem(turn, 2)
        return pltpu.make_async_copy(
            tiles.at[slot], grad_hbm.at[rows_at(tile_at(turn), block)], tile_sem.at[slot]
        )

    parts = ToPeers(seqs, near + far_off, grad_hbm, grad_in, part_send, part_recv)

    def leave(turn):
        grad_stored(turn).wait()
        for index in range(soon):
            pl.when(turn == index)(lambda index=index: parts.move(index).start())

    def weight_grad(turn):
        slot = lax.rem(turn, 2)
        size = min(4 * TILE, 2 * units)
        tile = tile_at(turn)

        @pl.loop(0, 2 * units // size)
        def _(column):
            here = rows_at(column, size)
            got = 0.0
            for batch in range(batches):
                left = buf[batch, :, :, rows_at(tile, block)].reshape(2 * chips * piece, block)
                got = got + contract_rows(left, d_ref[batch, :, here])
            tiles[slot, :, here] = to_half(got)

        pl.when(turn > 0)(lambda: leave(turn - 1))
        grad_stored(turn).start()

    def norm_batch(batch):
        own = pl.ds(batch * piece, piece)

        def put(here, d_values):
            there = pl.ds(pl.multiple_of(here.start + batch * piece, here.size), here.size)
            d_middle = cot_ref[there, :].astype(jnp.float32) + d_values
            dm_ref[there, :] = d_middle
            db_ref[there, :] = to_half(d_middle)

        norm_back(piece, v_ref.at[own], totals.at[batch], gain_ref, gain_grad_ref, put)

    gain_grad_ref[...] = jnp.zeros_like(gain_grad_ref)
    for item in loads:
        item.wait()
    last = 2 * chips - 2

    @pl.loop(0, chips)
    def _(far):
        take(0, far)
        pl.when(far == chips - 2)(spreads[1].begin)
        compute(0, far)

    @pl.loop(0, chips - 1)
    def _(far):
        take(1, far)
        reduces[0].step(2 * far)
        reduces[0].step(2 * far + 1)
        compute(1, far)

    take(1, chips - 1)
    compute(1, chips - 1)

    @pl.loop(0, 2)
    def _(step):
        reduces[1].step(step)
        weight_grad(step)

    reduces[0].step(last)
    norm_batch(0)

    @pl.loop(2, last)
    def _(step):
        reduces[1].step(step)
        pl.when(step < count)(lambda: weight_grad(step))

    @pl.loop(last, max(count, last))
    def _(tile):
        weight_grad(tile)

    reduces[1].step(last)
    norm_batch(1)
    for batch in range(batches):
        spreads[batch].sent()
        reduces[batch].sent()
    for item in stored(1, 0):
        item.wait()
    leave(count - 1)
    parts.end()


def feed_forward(seqs, chips, batches, x, w, wd_halves, group_d, middle, cot, gain, collective):
    rows, width = x.shape
    group = 2 * chips
    units = w.shape[1] // 2
    piece = rows // batches
    block = width // seqs // 2
    half = jnp.bfloat16
    return pl.pallas_call(
        functools.partial(feed_kernel, seqs, chips, batches),
        out_shape=[
            jax.ShapeDtypeStruct((rows, width), jnp.float32),
            jax.ShapeDtypeStruct((rows, width), half),
            jax.ShapeDtypeStruct((8, width), jnp.float32),
            jax.ShapeDtypeStruct((group * rows, units), half),
            jax.ShapeDtypeStruct((width, 2 * units), half),
            jax.ShapeDtypeStruct((seqs - 1, block, 2 * units), half),
        ],
        in_specs=[VMEM_SPEC] + [ANY_SPEC] * 4 + [VMEM_SPEC] * 3,
        out_specs=[VMEM_SPEC] * 3 + [ANY_SPEC] * 3,
        scratch_shapes=[
            pltpu.VMEM((batches, group, piece, width), half),
            pltpu.VMEM((2, 2 * piece, width), half),
            pltpu.VMEM((2 * piece, units), half),
            pltpu.VMEM(w.shape, half),
            pltpu.VMEM((units, width), half),
            pltpu.VMEM((batches, group * piece, 2 * units), half),
            pltpu.VMEM((2, block, 2 * units), half),
            pltpu.VMEM((batches, piece, width), jnp.float32),
            pltpu.VMEM((2 * piece, 2 * TILE), jnp.float32),
            pltpu.VMEM((piece, width), jnp.float32),
            sems(2),
            sems(2, 2),
            sems(2),
            sems(2),
            sems(batches, 3, group, PARTS // 2),
            sems(batches, group, PARTS // 2),
            sems(seqs),
            sems(seqs),
            sems(2, seqs),
        ]
        + PairReduce.scratch(chips, piece, width) * batches,
        compiler_params=comm_params(collective, 63),
        cost_estimate=cost(
            14 * group * rows * width * units, 400 * MIB, 2 * group * rows * width * 2
        ),
        name="feed_forward",
    )(x, w, *wd_halves, group_d, middle, cot, gain)


def branch_back_kernel(
    seqs, chips, batches, x_ref, w_ref, att_ref, middle_ref, hidden_hbm, wd_one, wd_two, units_hbm, gd_hbm,
    d_ref, layer_ref, out_grad_ref, half_in, down_hbm, down_in,
    out_ref, buf, hidden_ref, wd_ref, grad_acc, rights, tiles, send, recv, load, right_sem, tile_sem,
    part_send, part_recv, wd_load, down_send, down_recv, down_keep, acc, cross_out, line_out, cross_in, line_in, sum_send, sum_recv,
):
    line = Line(chips)
    rows = x_ref.shape[0]
    piece = rows // batches
    width = x_ref.shape[1]
    loads = [
        pltpu.make_async_copy(hidden_hbm, hidden_ref, load.at[0]),
    ] + load_halves([wd_one, wd_two], wd_ref, wd_load)
    for item in loads:
        item.start()

    def product(slot, tile):
        return dot_nn(left_rows(hidden_ref, slot, rows), wd_ref[:, rows_at(tile, TILE)])

    part = rights.shape[2]
    count = width // part

    def right(tile):
        slot = lax.rem(tile, 2)
        return pltpu.make_async_copy(
            gd_hbm.at[:, rows_at(tile, part)], rights.at[slot], right_sem.at[slot]
        )

    def stored(tile):
        slot = lax.rem(tile, 2)
        return pltpu.make_async_copy(
            tiles.at[slot], down_hbm.at[:, rows_at(tile, part)], tile_sem.at[slot]
        )

    def weight_grad(tile):
        right(tile).wait()
        pl.when(tile + 1 < count)(lambda: right(tile + 1).start())
        pl.when(tile >= 2)(lambda: stored(tile - 2).wait())
        slot = lax.rem(tile, 2)
        size = min(TILE, hidden_ref.shape[1])

        @pl.loop(0, hidden_ref.shape[1] // size)
        def _(row):
            here = rows_at(row, size)
            tiles[slot, here, :] = to_half(contract_rows(hidden_ref[:, here], rights[slot]))

        stored(tile).start()

    right(0).start()
    meet(line.greet() + greet_seq(seqs))
    near, far_off = seq_peers(seqs)
    peers = near + far_off
    halves = ToPeers(seqs, peers, units_hbm, half_in, part_send, part_recv, half_in.shape[1])
    down = ToPeers(seqs, peers, down_hbm, down_in.at[pl.ds(0, seqs - 1)], down_send, down_recv)
    down_kept = pltpu.make_async_copy(
        down_hbm.at[rows_at(lax.axis_index("seq"), down_in.shape[1])],
        down_in.at[seqs - 1],
        down_keep,
    )
    spread = Spread(line, x_ref, buf, send, recv)
    reduce = Reduce(
        line, product, out_ref, acc, cross_out, line_out, cross_in, line_in, sum_send, sum_recv
    )
    spread.begin()
    halves.begin()
    buf[line.own] = x_ref[...]
    grad_acc[...] = jnp.zeros_like(grad_acc)

    def use(slot):
        got = to_half(dot_nt(buf[slot], w_ref[...]))
        for batch in range(batches):
            d_ref[batch, rows_at(slot, piece), :] = got[batch * piece : (batch + 1) * piece]
        mixed = left_rows(att_ref, slot, rows)

        @pl.loop(0, width // TILE)
        def _(tile):
            here = rows_at(tile, TILE)
            grad_acc[:, here] += contract_rows(mixed, buf[slot, :, here])

    for item in loads:
        item.wait()

    reduce.level(chips - 1, lambda tile: None)
    pl.loop(0, count)(weight_grad)
    stored(count - 2).wait()
    stored(count - 1).wait()
    down.begin()
    down_kept.start()
    spread.relay(1)
    spread.each(0, use)

    @pl.loop(1, chips)
    def _(step):
        def also(tile):
            pl.when(step < chips - 1)(lambda: spread.relay_part(step + 1, tile))

        reduce.level(chips - 1 - step, also)
        spread.each(step, use)

    spread.each(chips, use)

    @pl.loop(0, rows // 32)
    def _(chunk):
        here = rows_at(chunk, 32)
        layer_ref[here, :] = to_half(middle_ref[here, :] + out_ref[here, :])

    out_grad_ref[...] = to_half(grad_acc[...])
    spread.sent()
    reduce.sent()
    halves.end()
    down.end()
    down_kept.wait()


def branch_back(seqs, chips, batches, x, w, attended, middle, hidden, wd_halves, unit_part, group_d, collective):
    rows, width = x.shape
    group = 2 * chips
    length = group * rows // batches
    span = w.shape[0]
    half = jnp.bfloat16
    part = 256 if group * rows <= 2048 else 128
    run = width // seqs
    units = hidden.shape[1]
    return pl.pallas_call(
        functools.partial(branch_back_kernel, seqs, chips, batches),
        out_shape=[
            jax.ShapeDtypeStruct((batches, length, span), half),
            jax.ShapeDtypeStruct((rows, width), half),
            jax.ShapeDtypeStruct((span, width), half),
            jax.ShapeDtypeStruct((seqs - 1, run // 2, unit_part.shape[1]), half),
            jax.ShapeDtypeStruct((units, width), half),
            jax.ShapeDtypeStruct((seqs, units // seqs, width), half),
        ],
        in_specs=[VMEM_SPEC] * 4 + [ANY_SPEC] * 5,
        out_specs=[VMEM_SPEC] * 3 + [ANY_SPEC] * 3,
        scratch_shapes=[
            pltpu.VMEM((rows, width), jnp.float32),
            pltpu.VMEM((group, rows, width), half),
            pltpu.VMEM(hidden.shape, half),
            pltpu.VMEM((units, width), half),
            pltpu.VMEM((span, width), jnp.float32),
            pltpu.VMEM((2, group * rows, part), half),
            pltpu.VMEM((2, units, part), half),
            sems(3, group, PARTS),
            sems(group, PARTS),
            sems(2),
            sems(2),
            sems(2),
            sems(seqs),
            sems(seqs),
            sems(2, seqs),
            sems(seqs),
            sems(seqs),
            pltpu.SemaphoreType.DMA,
        ]
        + Reduce.scratch(chips, rows, width),
        compiler_params=comm_params(collective, 62),
        cost_estimate=cost(
            2 * group * rows * width * (2 * span + 2 * units),
            250 * MIB,
            2 * group * rows * width * 2,
        ),
        name="branch_back",
    )(x, w, attended, middle, hidden, *wd_halves, unit_part, group_d.reshape(group * rows, width))


def attention_back_kernel(
    seqs, chips, block, q_ref, pad_ref, low_ref, lse_ref, d_ref, part_hbm, in_one, in_two,
    w_ref, g_hbm, v_ref, dm_hbm, gain_ref, mlp_gain_ref, out_ref,
    grad_hbm, wq_ref, wk_ref, wv_ref, wo_hbm, tile_ref, gate_hbm, up_hbm,
    grad_ref, wo_ref, gate_ref, up_ref, result_sem,
    dk, dv, kt, heads, back_out, back_in, unit_parts, unit_sums, units, lefts, parts, sums, cols, out_in,
    totals, gain_acc, gain_out, gain_in, gain_sum, gain_back, acc, keep,
    halo_send, halo_recv, unit_load, unit_send, unit_recv, unit_keep, dm_load, left_sem,
    part_send, part_recv, cols_send, cols_recv, out_send, out_recv,
    gain_send, gain_recv, back_send, back_recv, *line_sums,
):
    line = Line(chips)
    group = 2 * chips
    seq = lax.axis_index("seq")
    own = line.own
    batches, length, span = q_ref.shape
    rows, width = v_ref.shape
    piece = rows // batches
    pair_rows = 2 * piece
    depth = 3 * span
    run = width // seqs
    share = run // group
    part = lefts.shape[3]
    steps, need = length // block, WINDOW // block
    first = length - WINDOW
    has_left, has_right = seq > 0, seq < seqs - 1
    scale = jnp.asarray(HEAD**-0.5, jnp.bfloat16)

    def others(count, me, act):
        pl.loop(1, count)(lambda ahead: act(lax.rem(me + ahead, count)))

    def unit_loaded(turn, place, source):
        slot = lax.rem(turn, 2)
        return pltpu.make_async_copy(source, unit_parts.at[slot, place], unit_load.at[slot, place])

    def load_units(turn):
        member = lax.rem(own + turn, group)
        unit_loaded(turn, 0, part_hbm.at[rows_at(seq * group + member, share)]).start()
        for index in range(seqs - 1):

            @pl.when(member < chips)
            def _(index=index):
                unit_loaded(turn, index + 1, in_one.at[index, rows_at(member, share)]).start()

            @pl.when(member >= chips)
            def _(index=index):
                unit_loaded(turn, index + 1, in_two.at[index, rows_at(member - chips, share)]).start()

    load_units(1)
    dm_loaded = pltpu.make_async_copy(dm_hbm, grad_ref, dm_load)
    dm_loaded.start()
    meet(greet_group(group) + greet_seq(seqs))
    near, far_off = seq_peers(seqs)
    swap = Swap(group, unit_sums, units, unit_send, unit_recv, unit_keep)

    @pl.loop(1, group + 1)
    def _(turn):
        member = lax.rem(own + turn, group)
        slot = lax.rem(turn, 2)
        pl.when(turn < group)(lambda: load_units(turn + 1))
        for place in range(seqs):
            unit_loaded(turn, place, part_hbm.at[rows_at(0, share)]).wait()

        @pl.loop(0, share // 16)
        def _(chunk):
            here = rows_at(chunk, 16)
            added = unit_parts[slot, 0, here, :].astype(jnp.float32)
            for place in range(1, seqs):
                added = added + unit_parts[slot, place, here, :].astype(jnp.float32)
            unit_sums[member, here, :] = to_half(added)

        pl.when(turn < group)(lambda: swap.move(member, own).start())
        pl.when(turn == group)(lambda: swap.kept().start())

    def halo(batch, step, peer):
        here = rows_at(step, block)
        return pltpu.make_async_remote_copy(
            src_ref=back_out.at[batch, here],
            dst_ref=back_in.at[batch, here],
            send_sem=halo_send.at[batch, step],
            recv_sem=halo_recv.at[batch, step],
            device_id={"seq": peer},
            device_id_type=MESH,
        )

    def attend_block(batch, step):
        begin = pl.multiple_of(step * block, block)
        keys = pl.ds(begin, block + WINDOW)
        rows = pl.ds(begin, block)
        low = low_ref[batch, :, rows]
        for pair in range(span // PAIR):
            lanes = slice(pair * PAIR, (pair + 1) * PAIR)
            q_pair = q_ref[batch, rows, lanes] * scale
            d_pair = d_ref[batch, rows, lanes]
            k_rows = pad_ref[batch, keys, lanes]
            v_rows = pad_ref[batch, keys, span + pair * PAIR : span + (pair + 1) * PAIR]
            k_cols = kt[lanes, keys]
            back = []
            for half in range(2):
                row = pair * 2 + half
                q_head = head_lanes(q_pair, half)
                d_head = head_lanes(d_pair, half)
                scores = masked_scores(k_rows, q_head, low)
                probs = jnp.exp(scores - lse_ref[batch, row : row + 1, rows])
                d_probs = dot_nt(v_rows, d_head)
                along = jnp.sum(probs * d_probs, axis=0, keepdims=True)
                d_scores = to_half(probs * (d_probs - along))
                dv[keys, lanes] += dot_nn(to_half(probs), d_head)
                dk[keys, lanes] += dot_nn(d_scores, q_head)
                back.append(dot_nn(k_cols, d_scores))
            at = lax.broadcasted_iota(jnp.int32, back[0].shape, 0)
            heads[batch, rows, lanes] = to_half(
                jnp.where(at < HEAD, back[0], back[1]).T
            )


        @pl.when(has_left & (step < need))
        def _():
            back_out[batch, rows, :span] = to_half(dk[rows, :])
            back_out[batch, rows, span:] = to_half(dv[rows, :])
            halo(batch, step, seq - 1).start()

        @pl.when(step == steps - 1)
        def _():
            heads[batch, :, span : 2 * span] = to_half(dk[WINDOW:, :])
            heads[batch, :, 2 * span :] = to_half(dv[WINDOW:, :])

    def add_halo(batch):
        @pl.when(has_right)
        def _():
            @pl.loop(0, need)
            def _(step):
                there = pl.ds(pl.multiple_of(step * block + first, block), block)
                halo(batch, step, seq).wait_recv()
                got = back_in[batch, rows_at(step, block), :].astype(jnp.float32)
                mine = heads[batch, there, span:].astype(jnp.float32)
                heads[batch, there, span:] = to_half(mine + got)

    def product(batch):
        def get(place, here):
            return dot_nt(heads[batch, rows_at(place, pair_rows), :], w_ref[here, :])

        return get

    reduces = [
        PairReduce(
            line, product(batch), totals.at[batch], acc, keep, *line_sums[6 * batch : 6 * batch + 6]
        )
        for batch in range(batches)
    ]
    last = 2 * chips - 2

    @pl.loop(0, 2 * steps)
    def _(turn):
        batch, step = turn // steps, lax.rem(turn, steps)

        @pl.when(step == 0)
        def _():
            kt[...] = pad_ref[batch, :, :span].T * scale
            dk[...] = jnp.zeros_like(dk)
            dv[...] = jnp.zeros_like(dv)

        attend_block(batch, step)
        after = turn - steps - 1
        pl.when(after == 0)(lambda: add_halo(0))

        @pl.when((after >= 0) & (2 * after < last))
        def _():
            reduces[0].step(2 * after)
            reduces[0].step(2 * after + 1)

    for after in range(steps - 1, chips - 1):
        reduces[0].step(2 * after)
        reduces[0].step(2 * after + 1)

    def left(tile):
        slot = lax.rem(tile, 2)
        return pltpu.make_async_copy(
            g_hbm.at[:, :, rows_at(tile, part)], lefts.at[slot], left_sem.at[slot]
        )

    heads_near = ToPeers(seqs, near + far_off, parts, sums, part_send, part_recv)
    left(0).start()
    add_halo(1)

    @pl.loop(0, width // part)
    def _(tile):
        left(tile).wait()
        pl.when(tile + 1 < width // part)(lambda: left(tile + 1).start())
        slot = lax.rem(tile, 2)
        got = contract_rows(lefts[slot, 0], heads[0])
        for batch in range(1, batches):
            got = got + contract_rows(lefts[slot, batch], heads[batch])
        parts[rows_at(tile, part), :] = to_half(got)

    heads_near.begin()
    from_seq = ToPeers(seqs, near + far_off, out_ref, out_in, out_send, out_recv)
    from_seq.begin()
    gain_acc[...] = jnp.zeros_like(gain_acc)
    dm_loaded.wait()

    def norm_batch(batch):
        mine = pl.ds(batch * piece, piece)

        def put(here, d_values):
            there = pl.ds(pl.multiple_of(here.start + batch * piece, here.size), here.size)
            grad_ref[there, :] += d_values

        norm_back(piece, v_ref.at[mine], totals.at[batch], gain_ref, gain_acc, put)

    pl.loop(0, 2)(reduces[1].step)
    reduces[0].step(last)
    norm_batch(0)
    pl.loop(2, last)(reduces[1].step)
    swap.end()
    cell = units.shape[2] // 2 // seqs
    for member in range(group):
        for place in range(seqs):
            column = (place * group + member) * cell
            for target, begin in ((gate_ref, 0), (up_ref, seqs * cell)):
                here = slice(begin + place * cell, begin + (place + 1) * cell)
                target[:, column : column + cell] = units[member, :, here]

    results = [
        pltpu.make_async_copy(source, target, result_sem.at[index])
        for index, (source, target) in enumerate(
            ((gate_ref, gate_hbm), (up_ref, up_hbm), (wo_ref, wo_hbm), (grad_ref, grad_hbm))
        )
    ]
    results[0].start()
    results[1].start()

    def block_swap(peer, member):
        return pltpu.make_async_remote_copy(
            src_ref=parts.at[rows_at(seq * group + peer, share)],
            dst_ref=cols.at[member],
            send_sem=cols_send.at[peer],
            recv_sem=cols_recv.at[member],
            device_id={"fsdp": peer},
            device_id_type=MESH,
        )

    heads_near.arrived()

    @pl.loop(0, run // 64)
    def _(chunk):
        here = rows_at(chunk, 64)
        there = pl.ds(pl.multiple_of(seq * run + chunk * 64, 64), 64)
        parts[there, :] = to_half(add_from_seq(parts[there, :], sums, here))

    others(group, own, lambda peer: block_swap(peer, own).start())
    cols[own] = parts[rows_at(seq * group + own, share), :]
    from_seq.arrived()
    out_rows = out_in.shape[1]
    wo_ref[...] = add_from_seq(out_ref[rows_at(seq, out_rows), :], out_in, slice(None))
    results[2].start()
    reduces[1].step(last)
    norm_batch(1)
    results[3].start()
    fold = 128 // share
    near = group // fold
    attn_row = jnp.sum(gain_acc[...], axis=0, keepdims=True)
    mlp_row = jnp.sum(mlp_gain_ref[...], axis=0, keepdims=True)
    gain_out[...] = jnp.zeros_like(gain_out)
    for place in range(width // 128):
        lanes = slice(place * 128, (place + 1) * 128)
        gain_out[place % near, place // near, 0:1, :] = attn_row[:, lanes]
        gain_out[place % near, place // near, 1:2, :] = mlp_row[:, lanes]

    def gain_group(peer, member):
        return pltpu.make_async_remote_copy(
            src_ref=gain_out.at[peer // fold],
            dst_ref=gain_in.at[member],
            send_sem=gain_send.at[peer],
            recv_sem=gain_recv.at[member],
            device_id={"fsdp": peer},
            device_id_type=MESH,
        )

    def gain_seq(peer, place):
        return pltpu.make_async_remote_copy(
            src_ref=gain_sum.at[peer],
            dst_ref=gain_back.at[place],
            send_sem=back_send.at[peer],
            recv_sem=back_recv.at[place],
            device_id={"seq": peer},
            device_id_type=MESH,
        )

    others(group, own, lambda peer: gain_group(peer, own).start())
    gain_in[own] = gain_out[own // fold]
    others(group, own, lambda peer: gain_group(peer, peer).wait_recv())
    gain_sum[...] = jnp.sum(gain_in[...], axis=0)
    others(seqs, seq, lambda peer: gain_seq(peer, seq).start())
    gain_back[seq] = gain_sum[seq]
    others(seqs, seq, lambda peer: gain_seq(peer, peer).wait_recv())
    tile_ref[...] = jnp.sum(gain_back[...], axis=0)
    others(group, own, lambda peer: block_swap(peer, peer).wait_recv())
    for index, target in enumerate((wq_ref, wk_ref, wv_ref)):
        for member, first, home, size in column_parts(seqs, group, share, span):
            first = first + index * span
            target[:, home : home + size] = cols[member, :, first : first + size]
    from_seq.sent()
    for item in results:
        item.wait()
    for batch in range(batches):
        reduces[batch].sent()

        @pl.when(has_left)
        def _(batch=batch):
            pl.loop(0, need)(lambda step: halo(batch, step, seq).wait_send())

    heads_near.sent()
    others(group, own, lambda peer: gain_group(peer, own).wait_send())
    others(group, own, lambda peer: block_swap(peer, own).wait_send())
    others(seqs, seq, lambda peer: gain_seq(peer, seq).wait_send())


def attention_back(
    seqs, chips, block, query, kv_pad, low, lse, d_att, part_own, parts_one, parts_two, w, group_a, x,
    d_middle, gain, mlp_gain, out_part, collective,
):
    batches, length, span = query.shape
    padded = kv_pad.shape[1]
    rows, width = x.shape
    piece = rows // batches
    group = 2 * chips
    depth = w.shape[1]
    run = width // seqs
    share = run // group
    near = group // (128 // share)
    cells = part_own.shape[1]
    out_rows = out_part.shape[0] // seqs
    half, wide = jnp.bfloat16, jnp.float32
    part = 256 if batches * length <= 2048 else 128
    return pl.pallas_call(
        functools.partial(attention_back_kernel, seqs, chips, block),
        out_shape=[
            jax.ShapeDtypeStruct((rows, width), wide),
            jax.ShapeDtypeStruct((share, width), half),
            jax.ShapeDtypeStruct((share, width), half),
            jax.ShapeDtypeStruct((share, width), half),
            jax.ShapeDtypeStruct((out_rows, width), wide),
            jax.ShapeDtypeStruct((8, 128), wide),
            jax.ShapeDtypeStruct((share, cells // 2 * group), half),
            jax.ShapeDtypeStruct((share, cells // 2 * group), half),
        ],
        in_specs=[VMEM_SPEC] * 5
        + [ANY_SPEC] * 3
        + [VMEM_SPEC, ANY_SPEC, VMEM_SPEC, ANY_SPEC]
        + [VMEM_SPEC] * 3,
        out_specs=[ANY_SPEC, VMEM_SPEC, VMEM_SPEC, VMEM_SPEC, ANY_SPEC, VMEM_SPEC]
        + [ANY_SPEC] * 2,
        scratch_shapes=[
            pltpu.VMEM((rows, width), wide),
            pltpu.VMEM((out_rows, width), wide),
            pltpu.VMEM((share, cells // 2 * group), half),
            pltpu.VMEM((share, cells // 2 * group), half),
            sems(4),
            pltpu.VMEM((padded, span), wide),
            pltpu.VMEM((padded, span), wide),
            pltpu.VMEM((span, padded), half),
            pltpu.VMEM((batches, length, depth), half),
            pltpu.VMEM((batches, WINDOW, 2 * span), half),
            pltpu.VMEM((batches, WINDOW, 2 * span), half),
            pltpu.VMEM((2, seqs, share, cells), half),
            pltpu.VMEM((group, share, cells), half),
            pltpu.VMEM((group, share, cells), half),
            pltpu.VMEM((2, batches, length, part), half),
            pltpu.VMEM((width, depth), half),
            pltpu.VMEM((seqs - 1, run, depth), half),
            pltpu.VMEM((group, share, depth), half),
            pltpu.VMEM((seqs - 1, out_rows, width), half),
            pltpu.VMEM((batches, piece, width), wide),
            pltpu.VMEM((8, width), wide),
            pltpu.VMEM((near, seqs, 8, 128), wide),
            pltpu.VMEM((group, seqs, 8, 128), wide),
            pltpu.VMEM((seqs, 8, 128), wide),
            pltpu.VMEM((seqs, 8, 128), wide),
            pltpu.VMEM((2 * piece, TILE), wide),
            pltpu.VMEM((piece, width), wide),
            sems(batches, WINDOW // block),
            sems(batches, WINDOW // block),
            sems(2, seqs),
            sems(group),
            sems(group),
            pltpu.SemaphoreType.DMA,
            pltpu.SemaphoreType.DMA,
            sems(2),
            sems(seqs),
            sems(seqs),
            sems(group),
            sems(group),
            sems(seqs),
            sems(seqs),
            sems(group),
            sems(group),
            sems(seqs),
            sems(seqs),
        ]
        + PairReduce.scratch(chips, piece, width) * batches,
        compiler_params=comm_params(collective, 63),
        cost_estimate=cost(
            20 * batches * length * span * (WINDOW + block) + 4 * group * rows * width * depth,
            400 * MIB,
            3 * group * rows * width * 2,
        ),
        name="attention_back",
    )(
        query, kv_pad, low, lse, d_att, part_own, parts_one, parts_two, w, group_a, x,
        d_middle, gain, mlp_gain, out_part,
    )


def finish_kernel(count, *refs):
    sources, targets = refs[:-count], refs[-count:]
    for source, target in zip(sources, targets[:-1]):
        target[...] = source[...].astype(target.dtype)
    added = 0.0
    for source in sources[count - 1 :]:
        added = added + jnp.sum(source[...].astype(jnp.float32), axis=0)
    targets[-1][...] = added


def finish(steps, arrays, parts, kinds):
    in_specs, out_specs, out_shape = [], [], []
    for item, kind in zip(arrays + parts[:1], kinds):
        rows, width = item.shape[-2:]
        block = (rows // steps, width)
        out_specs.append(pl.BlockSpec(block, lambda i: (i, 0)))
        out_shape.append(jax.ShapeDtypeStruct((rows, width), kind))
        if item.ndim == 2:
            in_specs.append(out_specs[-1])
    for item in parts:
        in_specs.append(pl.BlockSpec((item.shape[0],) + block, lambda i: (0, i, 0)))
    return pl.pallas_call(
        functools.partial(finish_kernel, len(kinds)),
        grid=(steps,),
        in_specs=in_specs,
        out_specs=out_specs,
        out_shape=out_shape,
        compiler_params=pltpu.CompilerParams(vmem_limit_bytes=63 * MIB),
        name="finish",
    )(*arrays, *parts)


def doc_starts(lengths, positions, batches, seq_len):
    table = lengths.reshape(batches, -1, lengths.shape[1])
    starts = jnp.cumsum(table, axis=2) - table
    per_batch = seq_len // table.shape[1]
    begins = (starts + (jnp.arange(table.shape[1], dtype=jnp.int32) * per_batch)[None, :, None]).reshape(
        batches, -1
    )
    before = begins[:, None, :] <= positions[None, :, None]
    return jnp.max(jnp.where(before, begins[:, None, :], 0), axis=2)


def body(
    tokens,
    cotangent,
    lengths,
    gain_attn,
    w_query,
    w_key,
    w_value,
    w_out,
    gain_mlp,
    w_gate,
    w_up,
    w_down,
):
    batches, piece, width = tokens.shape
    seqs = lax.axis_size("seq")
    group = lax.axis_size("fsdp")
    chips = group // 2
    devices = seqs * group
    seq_len = piece * devices
    rows = batches * piece
    share = w_query.shape[0]
    span = width // group
    length = group * piece
    aligned = share == HEAD
    member = lax.axis_index("fsdp")

    x_rows = tokens.reshape(rows, width)
    cot_rows = cotangent.reshape(rows, width)
    if aligned:
        wo_part = lax.all_gather(w_out, "seq", axis=0, tiled=True)
    else:
        wo_all = lax.all_gather(w_out, ("seq", "fsdp"), axis=0, tiled=True)
        wo_part = lax.dynamic_slice_in_dim(wo_all, member * span, span, 0)

    lane = jnp.arange(128, dtype=jnp.int32)
    device = lax.axis_index("seq") * group + member
    fold = 128 // share
    here = lane // share == lax.rem(device, fold)
    both = jnp.stack([gain_attn, gain_mlp]).astype(jnp.float32)
    tile = jnp.where(here[None], jnp.tile(both, (1, fold)), 0.0)
    tile = jnp.pad(tile, ((0, 6), (0, 0)))[None]
    group_start = lax.axis_index("seq") * length
    positions = group_start + jnp.arange(length, dtype=jnp.int32)
    begins = doc_starts(lengths, positions, batches, seq_len)
    at = jnp.arange(length, dtype=jnp.int32)
    block = min(256, length)
    low = jnp.maximum(begins - group_start + WINDOW, at[None, :] + 1) - (at // block * block)[None, :]
    low = low[:, None, :]
    group_a, query, attended, lse, kv_pad, gains, w_heads, unit_own, wd_one = start(
        seqs, chips, batches, block, tile, x_rows, (w_query, w_key, w_value), (w_gate, w_up), w_down,
        low, 1,
    )
    gains = gains.transpose(1, 0, 2, 3).reshape(devices // fold, fold, 8, 128).sum(axis=1)
    gain_one = gains[:, 0].reshape(width)
    gain_two = gains[:, 1].reshape(width)
    middle, normed_b, group_d, w_units, wd_two = branch_sum(
        seqs, chips, attended, wo_part, cot_rows, unit_own.reshape(group * share, -1), w_down,
        x_rows, gain_two[None], 3,
    )
    w_units = w_units.reshape(width, -1)
    d_middle, d_branch, mlp_gain_part, hidden, unit_part, unit_one = feed_forward(
        seqs, chips, batches, normed_b, w_units, (wd_one, wd_two), group_d, middle, cot_rows,
        gain_two[None], 4,
    )
    d_attended, layer_out, out_part, unit_two, _, down_in = branch_back(
        seqs, chips, batches, d_branch, wo_part, attended, middle, hidden, (wd_one, wd_two),
        unit_part, group_d, 5,
    )
    if not aligned:
        whole = lax.dynamic_update_slice_in_dim(
            jnp.zeros((width, width), jnp.bfloat16), out_part, member * span, 0
        )
        out_part = lax.psum(whole, "fsdp").reshape(seqs, group, share, width)
        out_part = lax.dynamic_slice_in_dim(out_part, member, 1, 1).reshape(seqs * share, width)
    input_grad, wq_grad, wk_grad, wv_grad, wo_grad, gain_tile, gate_grad, up_grad = attention_back(
        seqs, chips, block, query, kv_pad, low, lse, d_attended, unit_part, unit_one, unit_two,
        w_heads, group_a, x_rows, d_middle, gain_one[None], mlp_gain_part, out_part, 6,
    )
    gain_grads = lax.dynamic_slice_in_dim(gain_tile[:2], lax.rem(device, fold) * share, share, 1)
    wide = jnp.float32
    (layer_out, input_grad, wq_grad, wk_grad, wv_grad, wo_grad, gate_grad, up_grad, down_grad) = finish(
        share // 16,
        [layer_out, input_grad, wq_grad, wk_grad, wv_grad, wo_grad, gate_grad, up_grad],
        [down_in],
        [jnp.bfloat16] + [wide] * 8,
    )
    return (
        layer_out.reshape(batches, piece, width),
        input_grad.reshape(batches, piece, width),
        gain_grads[0],
        wq_grad,
        wk_grad,
        wv_grad,
        wo_grad,
        gain_grads[1],
        gate_grad,
        up_grad,
        down_grad,
    )


def solution(mesh):
    spread = ("seq", "fsdp")
    tokens, rows, gains = P(None, spread, None), P(spread, None), P(spread)
    in_specs = (tokens, tokens, P(), gains, rows, rows, rows, rows, gains, rows, rows, rows)
    out_specs = (tokens, tokens, gains, rows, rows, rows, rows, gains, rows, rows, rows)
    return jax.shard_map(body, mesh=mesh, in_specs=in_specs, out_specs=out_specs, check_vma=False)
```

```python
import functools

import jax
import jax.numpy as jnp
from jax import lax
from jax.experimental import pallas as pl
from jax.experimental.pallas import tpu as pltpu
from jax.sharding import PartitionSpec as P

HEAD = 64
FF = 8192
WINDOW = 1024
PAIR = 128
TILE = 512
PARTS = 4
LOW = -1e30
EPS = 1e-05
MESH = pl.DeviceIdType.MESH
MIB = 2**20


def to_half(values):
    return values.astype(jnp.bfloat16)


def normalize(values, gain):
    return values * lax.rsqrt(jnp.mean(values * values, axis=-1, keepdims=True) + EPS) * gain


def contract_rows(left, right):
    return lax.dot_general(
        left, right, (((0,), (0,)), ((), ())), preferred_element_type=jnp.float32
    )


def dot_nt(left, right):
    return lax.dot_general(
        left, right, (((1,), (1,)), ((), ())), preferred_element_type=jnp.float32
    )


def dot_nn(left, right):
    return jnp.dot(left, right, preferred_element_type=jnp.float32)


def head_lanes(values, half):
    lane = lax.broadcasted_iota(jnp.int32, values.shape, 1)
    return jnp.where((lane >= HEAD) == (half == 1), values, jnp.zeros_like(values))


def masked_scores(k_rows, q_head, low):
    keys, block = k_rows.shape[0], q_head.shape[0]
    scores = dot_nt(k_rows, q_head)
    at = lax.broadcasted_iota(jnp.int32, (keys, block), 0)
    query = lax.broadcasted_iota(jnp.int32, (keys, block), 1)
    seen = (at >= low) & (at <= query + WINDOW)
    return jnp.where(seen, scores, LOW)


class Line:
    def __init__(self, chips):
        self.chips = chips
        self.own = lax.axis_index("fsdp")
        self.chip = self.own // 2
        self.core = lax.rem(self.own, 2)
        self.other = self.own + 1 - 2 * self.core
        self.has_left = self.chip > 0
        self.has_right = self.chip < chips - 1

    def greet(self):
        signal_group(self.other)
        pl.when(self.has_left)(lambda: signal_group(self.own - 2))
        pl.when(self.has_right)(lambda: signal_group(self.own + 2))
        return 1 + self.has_left.astype(jnp.int32) + self.has_right.astype(jnp.int32)


def signal_group(peer):
    barrier = pltpu.get_barrier_semaphore()
    pl.semaphore_signal(barrier, inc=1, device_id={"fsdp": peer}, device_id_type=MESH)


def signal_seq(peer):
    barrier = pltpu.get_barrier_semaphore()
    pl.semaphore_signal(barrier, inc=1, device_id={"seq": peer}, device_id_type=MESH)


def greet_group(group):
    own = lax.axis_index("fsdp")
    pl.loop(1, group)(lambda ahead: signal_group(lax.rem(own + ahead, group)))
    return group - 1


def greet_seq(seqs):
    own = lax.axis_index("seq")
    pl.loop(1, seqs)(lambda ahead: signal_seq(lax.rem(own + ahead, seqs)))
    return seqs - 1


def meet(count):
    pl.semaphore_wait(pltpu.get_barrier_semaphore(), count)


def rows_at(index, size):
    return pl.ds(pl.multiple_of(index * size, size), size)


class Spread:
    def __init__(self, line, first, buf, send, recv):
        self.line, self.first, self.buf, self.send, self.recv = line, first, buf, send, recv
        self.parts = recv.shape[1]
        self.size = first.shape[0] // self.parts

    def move(self, slot, part, way, peer, source=None):
        here = rows_at(part, self.size)
        return pltpu.make_async_remote_copy(
            src_ref=self.buf.at[slot, here] if source is None else source.at[here],
            dst_ref=self.buf.at[slot, here],
            send_sem=self.send.at[way, slot, part],
            recv_sem=self.recv.at[slot, part],
            device_id={"fsdp": peer},
            device_id_type=MESH,
        )

    def begin(self):
        line = self.line

        @pl.loop(0, self.parts)
        def _(part):
            pl.when(line.has_right)(
                lambda: self.move(line.own, part, 1, line.own + 2, self.first).start()
            )
            pl.when(line.has_left)(
                lambda: self.move(line.own, part, 0, line.own - 2, self.first).start()
            )
            self.move(line.own, part, 2, line.other, self.first).start()

    def relay_part(self, far, part):
        line = self.line

        @pl.when(line.chip - far >= 0)
        def _():
            slot = (line.chip - far) * 2 + line.core
            self.move(slot, part, 1, line.own).wait_recv()
            pl.when(line.has_right)(lambda: self.move(slot, part, 1, line.own + 2).start())
            self.move(slot, part, 2, line.other).start()

        @pl.when(line.chip + far < line.chips)
        def _():
            slot = (line.chip + far) * 2 + line.core
            self.move(slot, part, 0, line.own).wait_recv()
            pl.when(line.has_left)(lambda: self.move(slot, part, 0, line.own - 2).start())
            self.move(slot, part, 2, line.other).start()

    def relay(self, far):
        pl.loop(0, self.parts)(lambda part: self.relay_part(far, part))

    def across(self, slot):
        pl.loop(0, self.parts)(lambda part: self.move(slot, part, 2, self.line.own).wait_recv())

    def each(self, far, use):
        line = self.line

        @pl.loop(0, 4)
        def _(turn):
            side = lax.rem(turn, 2)
            over = turn // 2
            away = far - over
            source = line.chip + away * (2 * side - 1)
            valid = (away >= 0) & (away < line.chips) & (source >= 0) & (source < line.chips)
            valid = valid & ((side == 0) | (away > 0))

            @pl.when(valid)
            def _():
                slot = source * 2 + line.core + over * (1 - 2 * line.core)
                pl.when(over == 1)(lambda: self.across(slot))
                use(slot)

    def rest(self):
        pl.loop(0, self.line.chips)(lambda place: self.across(place * 2 + 1 - self.line.core))

    def sent(self):
        line = self.line

        @pl.loop(0, line.chips)
        def _(place):
            slot = place * 2 + line.core

            @pl.loop(0, self.parts)
            def _(part):
                self.move(slot, part, 2, line.other).wait_send()
                pl.when(line.has_right & (place <= line.chip))(
                    lambda: self.move(slot, part, 1, line.own + 2).wait_send()
                )
                pl.when(line.has_left & (place >= line.chip))(
                    lambda: self.move(slot, part, 0, line.own - 2).wait_send()
                )


class Reduce:
    def __init__(self, line, product, out, acc, cross_out, line_out, cross_in, line_in, send, recv):
        self.line, self.product, self.out, self.acc = line, product, out, acc
        self.cross_out, self.line_out, self.cross_in, self.line_in = cross_out, line_out, cross_in, line_in
        self.send, self.recv = send, recv
        self.tiles = line_out.shape[2] // TILE

    @staticmethod
    def scratch(chips, rows, width):
        part = pltpu.VMEM((chips, rows, width), jnp.bfloat16)
        return [
            pltpu.VMEM((rows, TILE), jnp.float32),
            pltpu.VMEM((2, rows, width), jnp.bfloat16),
            part,
            part,
            pltpu.VMEM((chips + 1, rows, width), jnp.bfloat16),
            pltpu.SemaphoreType.DMA((2, chips, width // TILE)),
            pltpu.SemaphoreType.DMA((2, chips + 1, width // TILE)),
        ]

    def cross(self, side, place, tile):
        here = rows_at(tile, TILE)
        return pltpu.make_async_remote_copy(
            src_ref=self.cross_out.at[side, :, here],
            dst_ref=self.cross_in.at[place, :, here],
            send_sem=self.send.at[0, place, tile],
            recv_sem=self.recv.at[0, place, tile],
            device_id={"fsdp": self.line.other},
            device_id_type=MESH,
        )

    def along(self, place, landing, tile, peer):
        here = rows_at(tile, TILE)
        return pltpu.make_async_remote_copy(
            src_ref=self.line_out.at[place, :, here],
            dst_ref=self.line_in.at[landing, :, here],
            send_sem=self.send.at[1, place, tile],
            recv_sem=self.recv.at[1, landing, tile],
            device_id={"fsdp": peer},
            device_id_type=MESH,
        )

    def where(self, away, side):
        line = self.line
        rightward = (line.chips - 1 - line.chip >= line.chip) == (side == 0)
        place = line.chip + jnp.where(rightward, away, -away)
        valid = (place >= 0) & (place < line.chips) & ((away > 0) | (side == 0))
        return valid, place, rightward

    def level(self, away, also):
        @pl.loop(0, 2)
        def _(side):
            valid, place, _ = self.where(away, side)

            @pl.when(valid)
            def _():
                @pl.loop(0, self.tiles)
                def _(tile):
                    got = self.product(place * 2 + 1 - self.line.core, tile)
                    self.cross_out[side, :, rows_at(tile, TILE)] = to_half(got)
                    self.cross(side, place, tile).start()

        @pl.loop(0, self.tiles)
        def _(tile):
            @pl.loop(0, 2)
            def _(side):
                valid, place, rightward = self.where(away, side)
                pl.when(valid)(lambda: self.close(away, side, place, rightward, tile))

            also(tile)

    def close(self, away, side, place, rightward, tile):
        line, acc = self.line, self.acc
        here = rows_at(tile, TILE)
        upstream = (rightward & line.has_left) | (jnp.logical_not(rightward) & line.has_right)
        acc[...] = self.product(place * 2 + line.core, tile)
        self.cross(side, place, tile).wait()
        acc[...] += self.cross_in[place, :, here].astype(jnp.float32)

        @pl.when(away > 0)
        def _():
            @pl.when(upstream)
            def _():
                self.along(place, place, tile, line.own).wait_recv()
                self.line_out[place, :, here] = to_half(
                    acc[...] + self.line_in[place, :, here].astype(jnp.float32)
                )

            @pl.when(jnp.logical_not(upstream))
            def _():
                self.line_out[place, :, here] = to_half(acc[...])

            @pl.when(rightward)
            def _():
                self.along(place, place, tile, line.own + 2).start()

            @pl.when(jnp.logical_not(rightward))
            def _():
                landing = jnp.where(away == 1, line.chips, place)
                self.along(place, landing, tile, line.own - 2).start()

        @pl.when(away == 0)
        def _():
            self.out[:, here] = acc[...]

            @pl.when(line.has_left)
            def _():
                self.along(place, place, tile, line.own).wait_recv()
                self.out[:, here] += self.line_in[place, :, here].astype(jnp.float32)

            @pl.when(line.has_right)
            def _():
                self.along(place, line.chips, tile, line.own).wait_recv()
                self.out[:, here] += self.line_in[line.chips, :, here].astype(jnp.float32)

    def sent(self):
        @pl.loop(0, self.line.chips)
        def _(place):
            @pl.when(place != self.line.chip)
            def _():
                pl.loop(0, self.tiles)(
                    lambda tile: self.along(place, place, tile, self.line.own).wait_send()
                )


class Swap:
    def __init__(self, group, source, target, send, recv, keep):
        self.group, self.source, self.target = group, source, target
        self.send, self.recv, self.keep = send, recv, keep
        self.own = lax.axis_index("fsdp")

    def move(self, peer, source):
        return pltpu.make_async_remote_copy(
            src_ref=self.source.at[peer],
            dst_ref=self.target.at[source],
            send_sem=self.send.at[peer],
            recv_sem=self.recv.at[source],
            device_id={"fsdp": peer},
            device_id_type=MESH,
        )

    def kept(self):
        return pltpu.make_async_copy(self.source.at[self.own], self.target.at[self.own], self.keep)

    def begin(self):
        self.kept().start()
        pl.loop(1, self.group)(
            lambda ahead: self.move(lax.rem(self.own + ahead, self.group), self.own).start()
        )

    def end(self):
        self.kept().wait()

        @pl.loop(1, self.group)
        def _(ahead):
            peer = lax.rem(self.own + ahead, self.group)
            self.move(peer, peer).wait_recv()
            self.move(peer, self.own).wait_send()


class Share:
    def __init__(self, seqs, source, target, send, recv, keep):
        self.seqs, self.source, self.target = seqs, source, target
        self.send, self.recv, self.keep = send, recv, keep
        self.own = lax.axis_index("seq")
        self.parts = send.shape[2]
        self.size = source.shape[0] // self.parts

    def move(self, peer, place, part):
        here = pl.ds(part * self.size, self.size)
        return pltpu.make_async_remote_copy(
            src_ref=self.source.at[here],
            dst_ref=self.target.at[place, here],
            send_sem=self.send.at[peer, 0, part],
            recv_sem=self.recv.at[place, 0, part],
            device_id={"seq": peer},
            device_id_type=MESH,
        )

    def relay(self, peer, place, part, side):
        here = pl.ds(part * self.size + side * (self.size // 2), self.size // 2)
        return pltpu.make_async_remote_copy(
            src_ref=self.target.at[place, here],
            dst_ref=self.target.at[place, here],
            send_sem=self.send.at[peer, 1, part],
            recv_sem=self.recv.at[place, side, part],
            device_id={"seq": peer},
            device_id_type=MESH,
        )

    def near(self):
        one = self.own + 1 - 2 * lax.rem(self.own, 2)
        two = lax.rem(self.own + 2, 4)
        return one, two, lax.rem(one + 2, 4)

    def kept(self):
        return pltpu.make_async_copy(self.source, self.target.at[self.own], self.keep)

    def begin(self):
        self.kept().start()
        for part in range(self.parts):
            if self.seqs == 4:
                one, two, _ = self.near()
                self.move(one, self.own, part).start()
                self.move(two, self.own, part).start()
            else:
                pl.loop(1, self.seqs)(
                    lambda ahead, part=part: self.move(
                        lax.rem(self.own + ahead, self.seqs), self.own, part
                    ).start()
                )

    def pass_on(self, parts):
        if self.seqs == 4:
            one, two, _ = self.near()
            for part in parts:
                self.move(one, one, part).wait_recv()
                self.relay(two, one, part, 0).start()
                self.move(two, two, part).wait_recv()
                self.relay(one, two, part, 1).start()

    def end(self):
        self.kept().wait()
        for part in range(self.parts):
            if self.seqs == 4:
                one, two, far = self.near()
                self.relay(two, far, part, 0).wait_recv()
                self.relay(one, far, part, 1).wait_recv()
                self.move(one, self.own, part).wait_send()
                self.move(two, self.own, part).wait_send()
                self.relay(two, one, part, 0).wait_send()
                self.relay(one, two, part, 1).wait_send()
            else:

                @pl.loop(1, self.seqs)
                def _(ahead, part=part):
                    peer = lax.rem(self.own + ahead, self.seqs)
                    self.move(peer, peer, part).wait_recv()
                    self.move(peer, self.own, part).wait_send()


def seq_peers(seqs):
    own = lax.axis_index("seq")
    if seqs == 4:
        one = own + 1 - 2 * lax.rem(own, 2)
        return [one, lax.rem(own + 2, 4)], [lax.rem(one + 2, 4)]
    ahead = [lax.rem(own + step, seqs) for step in range(1, seqs)]
    return ahead[:1], ahead[1:]


def near_count(seqs):
    return 2 if seqs == 4 else 1


class ToPeers:
    def __init__(self, seqs, peers, source, target, send, recv, first=0):
        self.peers, self.source, self.target, self.send, self.recv = peers, source, target, send, recv
        self.run, self.first = source.shape[0] // seqs, first

    def move(self, index):
        begin = pl.multiple_of(self.peers[index] * self.run + self.first, 16)
        return pltpu.make_async_remote_copy(
            src_ref=self.source.at[pl.ds(begin, self.target.shape[1])],
            dst_ref=self.target.at[index],
            send_sem=self.send.at[index],
            recv_sem=self.recv.at[index],
            device_id={"seq": self.peers[index]},
            device_id_type=MESH,
        )

    def begin(self):
        for index in range(len(self.peers)):
            self.move(index).start()

    def arrived(self):
        for index in range(len(self.peers)):
            self.move(index).wait_recv()

    def sent(self):
        for index in range(len(self.peers)):
            self.move(index).wait_send()

    def end(self):
        self.arrived()
        self.sent()


def load_halves(halves, target, load):
    copies = []
    rows = halves[0].shape[1]
    for index, half in enumerate(halves):
        for place in range(half.shape[0]):
            there = pl.ds((2 * place + index) * rows, rows)
            copies.append(pltpu.make_async_copy(half.at[place], target.at[there], load.at[index, place]))
    return copies


VMEM_SPEC = pl.BlockSpec(memory_space=pltpu.VMEM)
ANY_SPEC = pl.BlockSpec(memory_space=pl.ANY)


def comm_params(collective, mib=58):
    return pltpu.CompilerParams(
        collective_id=collective, has_side_effects=True, vmem_limit_bytes=mib * MIB
    )


def cost(flops, local, remote):
    return pl.CostEstimate(
        flops=flops, bytes_accessed=local, transcendentals=0, remote_bytes_transferred=remote
    )


def sems(*shape):
    return pltpu.SemaphoreType.DMA(shape)


def left_rows(a_ref, slot, rows):
    if len(a_ref.shape) == 2:
        return a_ref[rows_at(slot, rows), :]
    piece = rows // a_ref.shape[0]
    return jnp.concatenate(
        [a_ref[batch, rows_at(slot, piece), :] for batch in range(a_ref.shape[0])], axis=0
    )


def norm_back(rows, v_ref, e_ref, gain_ref, gain_acc, put):
    @pl.loop(0, rows // 32)
    def _(chunk):
        here = rows_at(chunk, 32)
        values = v_ref[here, :].astype(jnp.float32)
        error = e_ref[here, :]
        rate = lax.rsqrt(jnp.mean(values * values, axis=-1, keepdims=True) + EPS)
        unit = values * rate
        product = error * unit
        gain = gain_ref[0:1, :]
        mean = jnp.mean(product * gain, axis=-1, keepdims=True)
        gain_acc[...] += (product[0:8] + product[8:16]) + (product[16:24] + product[24:32])
        put(here, rate * (gain * error - unit * mean))


def add_from_seq(own_rows, got, here):
    added = own_rows.astype(jnp.float32)
    for index in range(got.shape[0]):
        added = added + got[index, here, :].astype(jnp.float32)
    return added


def column_parts(seqs, group, share, span):
    size = HEAD if share == HEAD else span
    parts = []
    for member in range(group):
        for run in range(span // size):
            home = (run * group + member) * size
            parts.append((member, run * size, home, size))
    return parts


def start_kernel(
    seqs, chips, batches, block, tile_ref, x_ref, wq_ref, wk_ref, wv_ref, gate_hbm, up_hbm, down_hbm, low_ref,
    g_ref, q_ref, out_ref, lse_ref, pad_ref, gains_ref, w_out_ref, own_units_ref, wd_ref,
    gate, up, units, blocks_ref, buf, normed, pad, vt, gain, gains, w,
    unit_sem, send, recv, keep, swap_send, share_send, w_recv,
    tile_send, tile_across, tile_recv, tile_back, w_keep, gain_keep,
    halo_send, halo_recv, pad_keep, unit_send, unit_recv, unit_keep,
    down_send, down_recv, down_keep,
):
    line = Line(chips)
    group = 2 * chips
    seq = lax.axis_index("seq")
    own = line.own
    share = blocks_ref.shape[1]
    rows, width = x_ref.shape
    piece = rows // batches
    length, span = q_ref.shape[1:]
    per = 128 * seqs * group // width
    steps, need = length // block, WINDOW // block
    has_left, has_right = seq > 0, seq < seqs - 1
    unit_loads = [
        pltpu.make_async_copy(gate_hbm, gate, unit_sem.at[0]),
        pltpu.make_async_copy(up_hbm, up, unit_sem.at[1]),
    ]
    for item in unit_loads:
        item.start()
    for index, source in enumerate((wq_ref, wk_ref, wv_ref)):
        for member, first, home, size in column_parts(seqs, group, share, span):
            first = first + index * span
            blocks_ref[member, :, first : first + size] = source[:, home : home + size]
    meet(greet_group(group) + greet_seq(seqs))

    def block_at(run, member):
        return w.at[rows_at(run * group + member, share)]

    def block_swap(peer, member):
        return pltpu.make_async_remote_copy(
            src_ref=blocks_ref.at[peer],
            dst_ref=block_at(seq, member),
            send_sem=swap_send.at[peer],
            recv_sem=w_recv.at[seq, member],
            device_id={"fsdp": peer},
            device_id_type=MESH,
        )

    def block_share(run, member, peer):
        return pltpu.make_async_remote_copy(
            src_ref=block_at(run, member),
            dst_ref=block_at(run, member),
            send_sem=share_send.at[peer, member],
            recv_sem=w_recv.at[run, member],
            device_id={"seq": peer},
            device_id_type=MESH,
        )

    def tile_to_seq(peer, place):
        return pltpu.make_async_remote_copy(
            src_ref=tile_ref.at[0],
            dst_ref=gains.at[own, place],
            send_sem=tile_send.at[peer],
            recv_sem=tile_recv.at[place],
            device_id={"seq": peer},
            device_id_type=MESH,
        )

    def tiles_to_group(peer, member):
        return pltpu.make_async_remote_copy(
            src_ref=gains.at[member],
            dst_ref=gains.at[member],
            send_sem=tile_across.at[peer],
            recv_sem=tile_back.at[member],
            device_id={"fsdp": peer},
            device_id_type=MESH,
        )

    def others(count, me, act):
        pl.loop(1, count)(lambda ahead: act(lax.rem(me + ahead, count)))

    others(seqs, seq, lambda peer: tile_to_seq(peer, seq).start())
    down = Share(
        seqs, down_hbm.at[pl.ds(0, wd_ref.shape[1])], wd_ref, down_send, down_recv, down_keep
    )
    down.begin()
    others(group, own, lambda peer: block_swap(peer, own).start())
    spreads = [
        Spread(line, x_ref.at[pl.ds(batch * piece, piece)], buf.at[batch], send.at[batch], recv.at[batch])
        for batch in range(batches)
    ]
    spreads[0].begin()
    gains[own, seq] = tile_ref[0]
    w[rows_at(seq * group + own, share), :] = blocks_ref[own]
    others(seqs, seq, lambda peer: block_share(seq, own, peer).start())
    for batch in range(batches):
        buf[batch, own] = x_ref[batch * piece : (batch + 1) * piece, :]
    others(seqs, seq, lambda peer: tile_to_seq(peer, peer).wait_recv())
    others(group, own, lambda peer: tiles_to_group(peer, own).start())
    for item in unit_loads:
        item.wait()
    cell = units.shape[2] // 2 // seqs
    for member in range(group):
        for run in range(seqs):
            home = (run * group + member) * cell
            for index, source in enumerate((gate, up)):
                first = (index * seqs + run) * cell
                units[member, :, first : first + cell] = source[:, home : home + cell]
    unit_swap = Swap(group, units, own_units_ref, unit_send, unit_recv, unit_keep)

    @pl.when(jnp.logical_not(has_left))
    def _():
        pad[:, :WINDOW, :] = jnp.zeros((batches, WINDOW, 2 * span), jnp.bfloat16)

    def pass_block(member):
        block_swap(member, member).wait_recv()
        others(seqs, seq, lambda peer: block_share(seq, member, peer).start())

    others(group, own, pass_block)
    down.pass_on([0])
    others(group, own, lambda peer: tiles_to_group(peer, peer).wait_recv())
    for column in range(width // 128):
        total = 0.0
        for place in range(column * per, (column + 1) * per):
            total = total + gains[place % group, place // group, 0:1, :]
        gain[0:1, column * 128 : (column + 1) * 128] = total

    def sides(far, act):
        @pl.loop(0, 2)
        def _(side):
            place = line.chip + far * (2 * side - 1)
            valid = (place >= 0) & (place < chips) & ((side == 0) | (far > 0))
            pl.when(valid)(lambda: act(place))

    def kept(batch, place):
        here = rows_at(place, block)
        return pltpu.make_async_copy(
            normed.at[batch, here], g_ref.at[batch, here], keep.at[batch, place]
        )

    def norm_pair(batch, place):
        spreads[batch].across(place * 2 + 1 - line.core)

        @pl.loop(0, 2)
        def _(member):
            @pl.loop(0, piece // 64)
            def _(chunk):
                values = buf[batch, place * 2 + member, rows_at(chunk, 64), :].astype(jnp.float32)
                there = pl.multiple_of(place * block + member * piece + chunk * 64, 64)
                normed[batch, pl.ds(there, 64), :] = to_half(normalize(values, gain[0:1, :]))

        kept(batch, place).start()

    def halo(batch, step, peer):
        there = pl.multiple_of(WINDOW + (step + steps - need) * block, block)
        return pltpu.make_async_remote_copy(
            src_ref=pad.at[batch, pl.ds(there, block)],
            dst_ref=pad.at[batch, rows_at(step, block)],
            send_sem=halo_send.at[batch, step],
            recv_sem=halo_recv.at[batch, step],
            device_id={"seq": peer},
            device_id_type=MESH,
        )

    def project(batch, place):
        here = rows_at(place, block)
        got = to_half(dot_nn(normed[batch, here, :], w[...]))
        q_ref[batch, here, :] = got[:, :span]
        pad[batch, pl.ds(pl.multiple_of(WINDOW + place * block, block), block), :] = got[:, span:]

        @pl.when(has_right & (place >= steps - need))
        def _():
            halo(batch, place - (steps - need), seq + 1).start()

    @pl.loop(0, chips)
    def _(far):
        pl.when(far > 0)(lambda: spreads[0].relay(far))
        pl.when(far == chips - 2)(spreads[1].begin)
        sides(far, lambda place: norm_pair(0, place))

    spreads[1].relay(1)

    def have_block(run, member):
        block_share(run, member, seq).wait_recv()

    others(seqs, seq, lambda run: pl.loop(0, group)(lambda member: have_block(run, member)))
    w_kept = pltpu.make_async_copy(w, w_out_ref, w_keep)
    w_kept.start()
    gains_kept = pltpu.make_async_copy(gains, gains_ref, gain_keep)
    gains_kept.start()
    pl.loop(0, steps)(lambda place: project(0, place))

    @pl.loop(2, chips)
    def _(far):
        spreads[1].relay(far)

    unit_swap.begin()

    @pl.loop(0, chips)
    def _(far):
        sides(far, lambda place: norm_pair(1, place))
        sides(far, lambda place: project(1, place))

    def pad_kept(batch):
        return pltpu.make_async_copy(pad.at[batch], pad_ref.at[batch], pad_keep.at[batch])

    for batch in range(batches):
        vt[:, WINDOW:] = pad[batch, WINDOW:, span:].T

        @pl.loop(0, steps)
        def _(turn, batch=batch):
            step = steps - 1 - turn

            @pl.when(step < need)
            def _():
                arrived = rows_at(step, block)
                pl.when(has_left)(lambda: halo(batch, step, seq).wait_recv())
                vt[:, arrived] = pad[batch, arrived, span:].T

            begin = pl.multiple_of(step * block, block)
            keys = pl.ds(begin, block + WINDOW)
            rows = pl.ds(begin, block)
            low = low_ref[batch, :, rows]
            for pair in range(span // PAIR):
                lanes = slice(pair * PAIR, (pair + 1) * PAIR)
                q_pair = q_ref[batch, rows, lanes] * jnp.asarray(HEAD**-0.5, jnp.bfloat16)
                k_rows = pad[batch, keys, lanes]
                values = vt[lanes, keys]
                mixed = []
                for half in range(2):
                    scores = masked_scores(k_rows, head_lanes(q_pair, half), low)
                    top = jnp.max(scores, axis=0, keepdims=True)
                    expo = jnp.exp(scores - top)
                    total = jnp.sum(expo, axis=0, keepdims=True)
                    mixed.append(dot_nn(values, to_half(expo)) / total)
                    row = pair * 2 + half
                    lse_ref[batch, row : row + 1, rows] = top + jnp.log(total)
                lane = lax.broadcasted_iota(jnp.int32, mixed[0].shape, 0)
                out_ref[batch, rows, lanes] = to_half(jnp.where(lane < HEAD, mixed[0], mixed[1]).T)

        pad_kept(batch).start()

    for batch in range(batches):
        spreads[batch].sent()
    others(seqs, seq, lambda peer: tile_to_seq(peer, seq).wait_send())
    others(group, own, lambda peer: block_swap(peer, own).wait_send())
    others(group, own, lambda peer: tiles_to_group(peer, own).wait_send())
    others(
        seqs,
        seq,
        lambda peer: pl.loop(0, group)(lambda member: block_share(seq, member, peer).wait_send()),
    )

    @pl.loop(0, need)
    def _(step):
        for batch in range(batches):
            pl.when(has_right)(lambda batch=batch: halo(batch, step, seq).wait_send())

    w_kept.wait()
    gains_kept.wait()
    unit_swap.end()
    down.end()
    for batch in range(batches):
        pad_kept(batch).wait()

        @pl.loop(0, steps)
        def _(place, batch=batch):
            kept(batch, place).wait()


def start(seqs, chips, batches, block, tile, x, weights, unit_weights, down, low, collective):
    rows, width = x.shape
    group = 2 * chips
    length = group * rows // batches
    share = weights[0].shape[0]
    span = width // group
    cols = 3 * span
    wide = unit_weights[0].shape[1]
    cells = 2 * wide // group
    piece = rows // batches
    padded = length + WINDOW
    half = jnp.bfloat16
    need = WINDOW // block
    return pl.pallas_call(
        functools.partial(start_kernel, seqs, chips, batches, block),
        out_shape=[
            jax.ShapeDtypeStruct((batches, length, width), half),
            jax.ShapeDtypeStruct((batches, length, span), half),
            jax.ShapeDtypeStruct((batches, length, span), half),
            jax.ShapeDtypeStruct((batches, span // HEAD, length), jnp.float32),
            jax.ShapeDtypeStruct((batches, padded, 2 * span), half),
            jax.ShapeDtypeStruct((group, seqs, 8, 128), jnp.float32),
            jax.ShapeDtypeStruct((width, cols), half),
            jax.ShapeDtypeStruct((group, share, cells), half),
            jax.ShapeDtypeStruct((seqs, down.shape[0] // 2, width), half),
        ],
        in_specs=[VMEM_SPEC] * 5 + [ANY_SPEC] * 3 + [VMEM_SPEC],
        out_specs=[ANY_SPEC] + [VMEM_SPEC] * 3 + [ANY_SPEC] * 5,
        scratch_shapes=[
            pltpu.VMEM((share, wide), half),
            pltpu.VMEM((share, wide), half),
            pltpu.VMEM((group, share, cells), half),
            pltpu.VMEM((group, share, cols), half),
            pltpu.VMEM((batches, group, piece, width), half),
            pltpu.VMEM((batches, length, width), half),
            pltpu.VMEM((batches, padded, 2 * span), half),
            pltpu.VMEM((span, padded), half),
            pltpu.VMEM((8, width), jnp.float32),
            pltpu.VMEM((group, seqs, 8, 128), jnp.float32),
            pltpu.VMEM((width, cols), half),
            sems(2),
            sems(batches, 3, group, PARTS // 2),
            sems(batches, group, PARTS // 2),
            sems(batches, chips),
            sems(group),
            sems(seqs, group),
            sems(seqs, group),
            sems(seqs),
            sems(group),
            sems(seqs),
            sems(group),
            pltpu.SemaphoreType.DMA,
            pltpu.SemaphoreType.DMA,
            sems(batches, need),
            sems(batches, need),
            sems(batches),
            sems(group),
            sems(group),
            pltpu.SemaphoreType.DMA,
            sems(seqs, 2, 1),
            sems(seqs, 2, 1),
            pltpu.SemaphoreType.DMA,
        ],
        compiler_params=comm_params(collective, 62),
        cost_estimate=cost(
            2 * group * rows * width * cols + 8 * batches * length * span * (WINDOW + block),
            300 * MIB,
            2 * group * rows * width * 2,
        ),
        name="start",
    )(tile, x, *weights, *unit_weights, down, low)


def branch_kernel(
    seqs, chips, a_ref, w_ref, d_ref, units_ref, down_hbm, x_ref, gain_ref,
    middle_ref, normed_ref, gd_ref, w_units_ref, wd_ref,
    out_ref, acc, cross_out, line_out, cross_in, line_in, sum_send, sum_recv,
    send, recv, d_keep, share_send, share_recv, share_keep,
    down_send, down_recv, down_keep,
):
    line = Line(chips)
    rows = out_ref.shape[0]

    def product(slot, tile):
        return dot_nn(left_rows(a_ref, slot, rows), w_ref[:, rows_at(tile, TILE)])

    meet(line.greet() + greet_seq(seqs))
    reduce = Reduce(
        line, product, out_ref, acc, cross_out, line_out, cross_in, line_in, sum_send, sum_recv
    )
    spread = Spread(line, d_ref, gd_ref, send, recv)
    units = Share(seqs, units_ref, w_units_ref, share_send, share_recv, share_keep)
    d_kept = pltpu.make_async_copy(d_ref, gd_ref.at[line.own], d_keep)
    half = wd_ref.shape[1]
    down = Share(seqs, down_hbm.at[pl.ds(half, half)], wd_ref, down_send, down_recv, down_keep)
    units.begin()
    down.begin()
    spread.begin()
    d_kept.start()

    @pl.loop(0, chips)
    def _(step):
        def also(tile):
            pl.when(step < chips - 1)(lambda: spread.relay_part(step + 1, tile))

        reduce.level(chips - 1 - step, also)

        pl.when(step == chips // 2 - 1)(lambda: units.pass_on([0, 1]))

        @pl.when(step == chips // 2)
        def _():
            units.pass_on([2, 3])
            down.pass_on([0])

    @pl.loop(0, rows // 32)
    def _(chunk):
        here = rows_at(chunk, 32)
        middle = x_ref[here, :].astype(jnp.float32) + out_ref[here, :]
        middle_ref[here, :] = middle
        normed_ref[here, :] = to_half(normalize(middle, gain_ref[0:1, :]))

    spread.rest()
    spread.sent()
    reduce.sent()
    d_kept.wait()
    units.end()
    down.end()


def branch_sum(seqs, chips, a, w, d_rows, units, down, x, gain, collective):
    rows, width = d_rows.shape
    group = 2 * chips
    half = jnp.bfloat16
    return pl.pallas_call(
        functools.partial(branch_kernel, seqs, chips),
        out_shape=[
            jax.ShapeDtypeStruct((rows, width), jnp.float32),
            jax.ShapeDtypeStruct((rows, width), half),
            jax.ShapeDtypeStruct((group, rows, width), half),
            jax.ShapeDtypeStruct((seqs,) + units.shape, half),
            jax.ShapeDtypeStruct((seqs, down.shape[0] // 2, width), half),
        ],
        in_specs=[VMEM_SPEC, VMEM_SPEC] + [ANY_SPEC] * 3 + [VMEM_SPEC, VMEM_SPEC],
        out_specs=[VMEM_SPEC, VMEM_SPEC] + [ANY_SPEC] * 3,
        scratch_shapes=[pltpu.VMEM((rows, width), jnp.float32)]
        + Reduce.scratch(chips, rows, width)
        + [sems(3, group, PARTS), sems(group, PARTS), pltpu.SemaphoreType.DMA]
        + [sems(seqs, 2, PARTS), sems(seqs, 2, PARTS), pltpu.SemaphoreType.DMA]
        + [sems(seqs, 2, 1), sems(seqs, 2, 1), pltpu.SemaphoreType.DMA],
        compiler_params=comm_params(collective),
        cost_estimate=cost(
            2 * group * rows * width * w.shape[0], 250 * MIB, 3 * group * rows * width * 2
        ),
        name="branch_sum",
    )(a, w, d_rows, units, down, x, gain)


class PairReduce:
    def __init__(self, line, product, out, acc, keep, cross_out, cross_in, line_out, line_in, send, recv):
        self.line, self.product, self.out, self.acc, self.keep = line, product, out, acc, keep
        self.cross_out, self.cross_in, self.line_out, self.line_in = cross_out, cross_in, line_out, line_in
        self.send, self.recv = send, recv
        self.tiles = keep.shape[1] // TILE

    @staticmethod
    def scratch(chips, piece, width):
        half = jnp.bfloat16
        return [
            pltpu.VMEM((piece, width), half),
            pltpu.VMEM((2, piece, width), half),
            pltpu.VMEM((2, piece, width), half),
            pltpu.VMEM((chips + 1, piece, width), half),
            pltpu.SemaphoreType.DMA((3, width // TILE)),
            pltpu.SemaphoreType.DMA((chips + 3, width // TILE)),
        ]

    def cross(self, parity, tile):
        here = rows_at(tile, TILE)
        return pltpu.make_async_remote_copy(
            src_ref=self.cross_out.at[:, here],
            dst_ref=self.cross_in.at[parity, :, here],
            send_sem=self.send.at[0, tile],
            recv_sem=self.recv.at[self.line.chips + 1 + parity, tile],
            device_id={"fsdp": self.line.other},
            device_id_type=MESH,
        )

    def along(self, parity, landing, tile, peer):
        here = rows_at(tile, TILE)
        return pltpu.make_async_remote_copy(
            src_ref=self.line_out.at[parity, :, here],
            dst_ref=self.line_in.at[landing, :, here],
            send_sem=self.send.at[1 + parity, tile],
            recv_sem=self.recv.at[landing, tile],
            device_id={"fsdp": peer},
            device_id_type=MESH,
        )

    def steps(self):
        return 2 * self.line.chips - 1

    def step(self, step):
        line, keep = self.line, self.keep
        piece = keep.shape[0]
        right_side = line.chips - 1 - line.chip
        away = line.chips - 1 - step // 2
        second = lax.rem(step, 2)
        rightward = (right_side >= line.chip) == (second == 0)
        place = line.chip + jnp.where(rightward, away, -away)
        longer = jnp.maximum(right_side, line.chip)
        shorter = jnp.minimum(right_side, line.chip)
        count = longer - away + jnp.maximum(shorter - away, 0) + second
        parity = lax.rem(count + 2 * line.chips, 2)
        upstream = (rightward & line.has_left) | (jnp.logical_not(rightward) & line.has_right)

        @pl.when((place >= 0) & (place < line.chips))
        def _():
            wide = self.acc.shape[1]

            @pl.loop(0, keep.shape[1] // wide)
            def _(tile):
                here = rows_at(tile, wide)
                self.acc[...] = self.product(place, here)
                self.cross_out[:, here] = to_half(self.acc[rows_at(1 - line.core, piece), :])
                keep[:, here] = self.acc[rows_at(line.core, piece), :]
                for piece_of in range(wide // TILE):
                    self.cross(parity, tile * (wide // TILE) + piece_of).start()

            @pl.loop(0, self.tiles)
            def _(tile):
                here = rows_at(tile, TILE)
                self.cross(parity, tile).wait()
                keep[:, here] += self.cross_in[parity, :, here].astype(jnp.float32)

                @pl.when(away > 0)
                def _():
                    pl.when(count >= 2)(
                        lambda: self.along(parity, place, tile, line.own).wait_send()
                    )

                    @pl.when(upstream)
                    def _():
                        self.along(parity, place, tile, line.own).wait_recv()
                        self.line_out[parity, :, here] = to_half(
                            keep[:, here] + self.line_in[place, :, here].astype(jnp.float32)
                        )

                    @pl.when(jnp.logical_not(upstream))
                    def _():
                        self.line_out[parity, :, here] = to_half(keep[:, here])

                    @pl.when(rightward)
                    def _():
                        self.along(parity, place, tile, line.own + 2).start()

                    @pl.when(jnp.logical_not(rightward))
                    def _():
                        landing = jnp.where(away == 1, line.chips, place)
                        self.along(parity, landing, tile, line.own - 2).start()

                @pl.when(away == 0)
                def _():
                    self.out[:, here] = keep[:, here]

                    @pl.when(line.has_left)
                    def _():
                        self.along(parity, place, tile, line.own).wait_recv()
                        self.out[:, here] += self.line_in[place, :, here].astype(jnp.float32)

                    @pl.when(line.has_right)
                    def _():
                        self.along(parity, line.chips, tile, line.own).wait_recv()
                        self.out[:, here] += self.line_in[line.chips, :, here].astype(jnp.float32)

    def sent(self):
        for count in range(max(self.line.chips - 3, 0), self.line.chips - 1):
            pl.loop(0, self.tiles)(
                lambda tile, parity=count % 2: self.along(parity, 0, tile, self.line.own).wait_send()
            )


def feed_kernel(
    seqs, chips, batches, x_ref, w_hbm, wd_one, wd_two, gd_hbm, v_ref, cot_ref, gain_ref,
    dm_ref, db_ref, gain_grad_ref, hidden_hbm, grad_hbm, grad_in,
    buf, d_buf, h_buf, w_ref, wd_ref, d_ref, tiles, totals, acc, keep,
    load, d_sem, h_sem, tile_sem, send, recv, part_send, part_recv, wd_load, *sums,
):
    line = Line(chips)
    rows, width = x_ref.shape
    piece = rows // batches
    pair = 2 * piece
    units = wd_ref.shape[0]
    part = min(units, 2 * TILE)
    block = tiles.shape[1]
    loads = [
        pltpu.make_async_copy(w_hbm, w_ref, load.at[0]),
    ] + load_halves([wd_one, wd_two], wd_ref, wd_load)
    for item in loads:
        item.start()
    meet(line.greet() + greet_seq(seqs))
    spreads = [
        Spread(
            line,
            x_ref.at[pl.ds(batch * piece, piece)],
            buf.at[batch],
            send.at[batch],
            recv.at[batch],
        )
        for batch in range(batches)
    ]
    spreads[0].begin()
    for batch in range(batches):
        buf[batch, line.own] = x_ref[batch * piece : (batch + 1) * piece, :]

    def fetch(batch, place, side):
        return [
            pltpu.make_async_copy(
                gd_hbm.at[place * 2 + core, pl.ds(batch * piece, piece)],
                d_buf.at[side, pl.ds(core * piece, piece)],
                d_sem.at[side, core],
            )
            for core in range(2)
        ]

    def stored(batch, place):
        return [
            pltpu.make_async_copy(
                h_buf.at[pl.ds(core * piece, piece)],
                hidden_hbm.at[
                    pl.ds(pl.multiple_of((place * 2 + core) * rows + batch * piece, piece), piece)
                ],
                h_sem.at[core],
            )
            for core in range(2)
        ]

    def sides(far, act):
        @pl.loop(0, 2)
        def _(side):
            place = line.chip + far * (2 * side - 1)
            valid = (place >= 0) & (place < chips) & ((side == 0) | (far > 0))
            pl.when(valid)(lambda: act(place, side))

    def take(batch, far):
        def begin(place, side):
            for item in fetch(batch, place, side):
                item.start()

        sides(far, begin)
        pl.when(far > 0)(lambda: spreads[batch].relay(far))

    def compute(batch, far):
        def act(place, side):
            spreads[batch].across(place * 2 + 1 - line.core)
            for item in fetch(batch, place, side):
                item.wait()

            def free():
                for item in stored(batch, place):
                    item.wait()

            if batch:
                free()
            else:
                pl.when((far > 0) | (side > 0))(free)
            there = rows_at(place, pair)

            @pl.loop(0, units // part)
            def _(tile):
                first = rows_at(tile, part)
                second = rows_at(units // part + tile, part)
                values = buf[batch, pl.ds(place * 2, 2), :, :].reshape(pair, width)
                gate = dot_nn(values, w_ref[:, first])
                up = dot_nn(values, w_ref[:, second])
                d_hidden = dot_nt(d_buf[side], wd_ref[first, :])
                sigma = jax.nn.sigmoid(gate)
                swish = gate * sigma
                h_buf[:, first] = to_half(swish * up)
                slope = sigma * (1.0 + gate * (1.0 - sigma))
                d_ref[batch, there, first] = to_half(d_hidden * up * slope)
                d_ref[batch, there, second] = to_half(d_hidden * swish)

            for item in stored(batch, place):
                item.start()

        sides(far, act)

    def product(batch):
        def get(place, here):
            return dot_nt(d_ref[batch, rows_at(place, pair), :], w_ref[here, :])

        return get

    reduces = [
        PairReduce(line, product(batch), totals.at[batch], acc, keep, *sums[6 * batch : 6 * batch + 6])
        for batch in range(batches)
    ]

    count = width // block
    seq = lax.axis_index("seq")

    near, far_off = seq_peers(seqs)
    soon = len(near)
    order = [peer * 2 for peer in near] + [peer * 2 for peer in far_off] + [seq * 2]
    order = order + [peer * 2 + 1 for peer in near] + [peer * 2 + 1 for peer in far_off] + [seq * 2 + 1]

    def tile_at(turn):
        tile = order[-1]
        for index in range(len(order) - 1):
            tile = jnp.where(turn == index, order[index], tile)
        return tile

    def grad_stored(turn):
        slot = lax.rem(turn, 2)
        return pltpu.make_async_copy(
            tiles.at[slot], grad_hbm.at[rows_at(tile_at(turn), block)], tile_sem.at[slot]
        )

    parts = ToPeers(seqs, near, grad_hbm, grad_in, part_send, part_recv)

    def leave(turn):
        grad_stored(turn).wait()
        for index in range(soon):
            pl.when(turn == index)(lambda index=index: parts.move(index).start())

    def weight_grad(turn):
        slot = lax.rem(turn, 2)
        size = min(4 * TILE, 2 * units)
        tile = tile_at(turn)

        @pl.loop(0, 2 * units // size)
        def _(column):
            here = rows_at(column, size)
            got = 0.0
            for batch in range(batches):
                left = buf[batch, :, :, rows_at(tile, block)].reshape(2 * chips * piece, block)
                got = got + contract_rows(left, d_ref[batch, :, here])
            tiles[slot, :, here] = to_half(got)

        pl.when(turn > 0)(lambda: leave(turn - 1))
        grad_stored(turn).start()

    def norm_batch(batch):
        own = pl.ds(batch * piece, piece)

        def put(here, d_values):
            there = pl.ds(pl.multiple_of(here.start + batch * piece, here.size), here.size)
            d_middle = cot_ref[there, :].astype(jnp.float32) + d_values
            dm_ref[there, :] = d_middle
            db_ref[there, :] = to_half(d_middle)

        norm_back(piece, v_ref.at[own], totals.at[batch], gain_ref, gain_grad_ref, put)

    gain_grad_ref[...] = jnp.zeros_like(gain_grad_ref)
    for item in loads:
        item.wait()
    last = 2 * chips - 2

    @pl.loop(0, chips)
    def _(far):
        take(0, far)
        pl.when(far == chips - 2)(spreads[1].begin)
        compute(0, far)

    @pl.loop(0, chips - 1)
    def _(far):
        take(1, far)
        reduces[0].step(2 * far)
        reduces[0].step(2 * far + 1)
        compute(1, far)

    take(1, chips - 1)
    compute(1, chips - 1)

    @pl.loop(0, 2)
    def _(step):
        reduces[1].step(step)
        weight_grad(step)

    reduces[0].step(last)
    norm_batch(0)

    @pl.loop(2, last)
    def _(step):
        reduces[1].step(step)
        pl.when(step < count)(lambda: weight_grad(step))

    @pl.loop(last, max(count, last))
    def _(tile):
        weight_grad(tile)

    reduces[1].step(last)
    norm_batch(1)
    for batch in range(batches):
        spreads[batch].sent()
        reduces[batch].sent()
    for item in stored(1, 0):
        item.wait()
    leave(count - 1)
    parts.end()


def feed_forward(seqs, chips, batches, x, w, wd_halves, group_d, middle, cot, gain, collective):
    rows, width = x.shape
    group = 2 * chips
    units = w.shape[1] // 2
    piece = rows // batches
    block = width // seqs // 2
    half = jnp.bfloat16
    return pl.pallas_call(
        functools.partial(feed_kernel, seqs, chips, batches),
        out_shape=[
            jax.ShapeDtypeStruct((rows, width), jnp.float32),
            jax.ShapeDtypeStruct((rows, width), half),
            jax.ShapeDtypeStruct((8, width), jnp.float32),
            jax.ShapeDtypeStruct((group * rows, units), half),
            jax.ShapeDtypeStruct((width, 2 * units), half),
            jax.ShapeDtypeStruct((near_count(seqs), block, 2 * units), half),
        ],
        in_specs=[VMEM_SPEC] + [ANY_SPEC] * 4 + [VMEM_SPEC] * 3,
        out_specs=[VMEM_SPEC] * 3 + [ANY_SPEC] * 3,
        scratch_shapes=[
            pltpu.VMEM((batches, group, piece, width), half),
            pltpu.VMEM((2, 2 * piece, width), half),
            pltpu.VMEM((2 * piece, units), half),
            pltpu.VMEM(w.shape, half),
            pltpu.VMEM((units, width), half),
            pltpu.VMEM((batches, group * piece, 2 * units), half),
            pltpu.VMEM((2, block, 2 * units), half),
            pltpu.VMEM((batches, piece, width), jnp.float32),
            pltpu.VMEM((2 * piece, 2 * TILE), jnp.float32),
            pltpu.VMEM((piece, width), jnp.float32),
            sems(2),
            sems(2, 2),
            sems(2),
            sems(2),
            sems(batches, 3, group, PARTS // 2),
            sems(batches, group, PARTS // 2),
            sems(seqs),
            sems(seqs),
            sems(2, seqs),
        ]
        + PairReduce.scratch(chips, piece, width) * batches,
        compiler_params=comm_params(collective, 63),
        cost_estimate=cost(
            14 * group * rows * width * units, 400 * MIB, 2 * group * rows * width * 2
        ),
        name="feed_forward",
    )(x, w, *wd_halves, group_d, middle, cot, gain)


def branch_back_kernel(
    seqs, chips, batches, x_ref, w_ref, att_ref, middle_ref, hidden_hbm, wd_one, wd_two, units_hbm, gd_hbm,
    d_ref, layer_ref, out_grad_ref, half_in, whole_in, down_hbm, down_in,
    out_ref, buf, hidden_ref, wd_ref, grad_acc, rights, tiles, send, recv, load, right_sem, tile_sem,
    part_send, part_recv, wd_load, down_send, down_recv, down_keep, acc, cross_out, line_out, cross_in, line_in, sum_send, sum_recv,
):
    line = Line(chips)
    rows = x_ref.shape[0]
    piece = rows // batches
    width = x_ref.shape[1]
    loads = [
        pltpu.make_async_copy(hidden_hbm, hidden_ref, load.at[0]),
    ] + load_halves([wd_one, wd_two], wd_ref, wd_load)
    for item in loads:
        item.start()

    def product(slot, tile):
        return dot_nn(left_rows(hidden_ref, slot, rows), wd_ref[:, rows_at(tile, TILE)])

    part = rights.shape[2]
    count = width // part

    def right(tile):
        slot = lax.rem(tile, 2)
        return pltpu.make_async_copy(
            gd_hbm.at[:, rows_at(tile, part)], rights.at[slot], right_sem.at[slot]
        )

    def stored(tile):
        slot = lax.rem(tile, 2)
        return pltpu.make_async_copy(
            tiles.at[slot], down_hbm.at[:, rows_at(tile, part)], tile_sem.at[slot]
        )

    def weight_grad(tile):
        right(tile).wait()
        pl.when(tile + 1 < count)(lambda: right(tile + 1).start())
        pl.when(tile >= 2)(lambda: stored(tile - 2).wait())
        slot = lax.rem(tile, 2)
        size = min(TILE, hidden_ref.shape[1])

        @pl.loop(0, hidden_ref.shape[1] // size)
        def _(row):
            here = rows_at(row, size)
            tiles[slot, here, :] = to_half(contract_rows(hidden_ref[:, here], rights[slot]))

        stored(tile).start()

    right(0).start()
    meet(line.greet() + greet_seq(seqs))
    near, far_off = seq_peers(seqs)
    soon = len(near)
    halves = ToPeers(
        seqs, near, units_hbm, half_in, part_send.at[0], part_recv.at[0], half_in.shape[1]
    )
    wholes = ToPeers(seqs, far_off, units_hbm, whole_in, part_send.at[1], part_recv.at[1])
    down = ToPeers(
        seqs, near, down_hbm, down_in.at[pl.ds(0, soon)], down_send, down_recv
    )
    down_kept = pltpu.make_async_copy(
        down_hbm.at[rows_at(lax.axis_index("seq"), down_in.shape[1])], down_in.at[soon], down_keep
    )
    spread = Spread(line, x_ref, buf, send, recv)
    reduce = Reduce(
        line, product, out_ref, acc, cross_out, line_out, cross_in, line_in, sum_send, sum_recv
    )
    spread.begin()
    halves.begin()
    wholes.begin()
    buf[line.own] = x_ref[...]
    grad_acc[...] = jnp.zeros_like(grad_acc)

    def use(slot):
        got = to_half(dot_nt(buf[slot], w_ref[...]))
        for batch in range(batches):
            d_ref[batch, rows_at(slot, piece), :] = got[batch * piece : (batch + 1) * piece]
        mixed = left_rows(att_ref, slot, rows)

        @pl.loop(0, width // TILE)
        def _(tile):
            here = rows_at(tile, TILE)
            grad_acc[:, here] += contract_rows(mixed, buf[slot, :, here])

    for item in loads:
        item.wait()

    reduce.level(chips - 1, lambda tile: None)
    pl.loop(0, count)(weight_grad)
    stored(count - 2).wait()
    stored(count - 1).wait()
    down.begin()
    down_kept.start()
    spread.relay(1)
    spread.each(0, use)

    @pl.loop(1, chips)
    def _(step):
        def also(tile):
            pl.when(step < chips - 1)(lambda: spread.relay_part(step + 1, tile))

        reduce.level(chips - 1 - step, also)
        spread.each(step, use)

    spread.each(chips, use)

    @pl.loop(0, rows // 32)
    def _(chunk):
        here = rows_at(chunk, 32)
        layer_ref[here, :] = to_half(middle_ref[here, :] + out_ref[here, :])

    out_grad_ref[...] = to_half(grad_acc[...])
    spread.sent()
    reduce.sent()
    halves.end()
    wholes.end()
    down.end()
    down_kept.wait()


def branch_back(seqs, chips, batches, x, w, attended, middle, hidden, wd_halves, unit_part, group_d, collective):
    rows, width = x.shape
    group = 2 * chips
    length = group * rows // batches
    span = w.shape[0]
    half = jnp.bfloat16
    part = 256 if group * rows <= 2048 else 128
    near, run = near_count(seqs), width // seqs
    units = hidden.shape[1]
    return pl.pallas_call(
        functools.partial(branch_back_kernel, seqs, chips, batches),
        out_shape=[
            jax.ShapeDtypeStruct((batches, length, span), half),
            jax.ShapeDtypeStruct((rows, width), half),
            jax.ShapeDtypeStruct((span, width), half),
            jax.ShapeDtypeStruct((near, run // 2, unit_part.shape[1]), half),
            jax.ShapeDtypeStruct((seqs - 1 - near, run, unit_part.shape[1]), half),
            jax.ShapeDtypeStruct((units, width), half),
            jax.ShapeDtypeStruct((near + 1, units // seqs, width), half),
        ],
        in_specs=[VMEM_SPEC] * 4 + [ANY_SPEC] * 5,
        out_specs=[VMEM_SPEC, VMEM_SPEC, VMEM_SPEC, ANY_SPEC, ANY_SPEC, ANY_SPEC, ANY_SPEC],
        scratch_shapes=[
            pltpu.VMEM((rows, width), jnp.float32),
            pltpu.VMEM((group, rows, width), half),
            pltpu.VMEM(hidden.shape, half),
            pltpu.VMEM((units, width), half),
            pltpu.VMEM((span, width), jnp.float32),
            pltpu.VMEM((2, group * rows, part), half),
            pltpu.VMEM((2, units, part), half),
            sems(3, group, PARTS),
            sems(group, PARTS),
            sems(2),
            sems(2),
            sems(2),
            sems(2, seqs),
            sems(2, seqs),
            sems(2, seqs),
            sems(seqs),
            sems(seqs),
            pltpu.SemaphoreType.DMA,
        ]
        + Reduce.scratch(chips, rows, width),
        compiler_params=comm_params(collective, 62),
        cost_estimate=cost(
            2 * group * rows * width * (2 * span + 2 * units),
            250 * MIB,
            2 * group * rows * width * 2,
        ),
        name="branch_back",
    )(x, w, attended, middle, hidden, *wd_halves, unit_part, group_d.reshape(group * rows, width))


def attention_back_kernel(
    seqs, chips, block, q_ref, pad_ref, low_ref, lse_ref, d_ref, part_hbm, in_one, in_two, in_far,
    w_ref, g_hbm, v_ref, dm_hbm, gain_ref, mlp_gain_ref, out_ref, down_hbm,
    grad_hbm, wq_ref, wk_ref, wv_ref, wo_hbm, tile_ref, gate_hbm, up_hbm, down_in,
    grad_ref, wo_ref, gate_ref, up_ref, result_sem, down_send, down_recv,
    dk, dv, kt, heads, back_out, back_in, unit_parts, unit_sums, units, lefts, parts, sums, cols, out_in,
    totals, gain_acc, gain_out, gain_in, gain_sum, gain_back, acc, keep,
    halo_send, halo_recv, unit_load, unit_send, unit_recv, unit_keep, dm_load, left_sem,
    part_send, part_recv, cols_send, cols_recv, out_send, out_recv,
    gain_send, gain_recv, back_send, back_recv, *line_sums,
):
    line = Line(chips)
    group = 2 * chips
    seq = lax.axis_index("seq")
    own = line.own
    batches, length, span = q_ref.shape
    rows, width = v_ref.shape
    piece = rows // batches
    pair_rows = 2 * piece
    depth = 3 * span
    run = width // seqs
    share = run // group
    part = lefts.shape[3]
    steps, need = length // block, WINDOW // block
    first = length - WINDOW
    has_left, has_right = seq > 0, seq < seqs - 1
    scale = jnp.asarray(HEAD**-0.5, jnp.bfloat16)

    def others(count, me, act):
        pl.loop(1, count)(lambda ahead: act(lax.rem(me + ahead, count)))

    def unit_loaded(turn, place, source):
        slot = lax.rem(turn, 2)
        return pltpu.make_async_copy(source, unit_parts.at[slot, place], unit_load.at[slot, place])

    def load_units(turn):
        member = lax.rem(own + turn, group)
        unit_loaded(turn, 0, part_hbm.at[rows_at(seq * group + member, share)]).start()
        soon = in_one.shape[0]
        for index in range(seqs - 1):

            def fetch(source, index=index):
                unit_loaded(turn, index + 1, source).start()

            if index < soon:

                @pl.when(member < chips)
                def _(index=index, fetch=fetch):
                    fetch(in_one.at[index, rows_at(member, share)])

                @pl.when(member >= chips)
                def _(index=index, fetch=fetch):
                    fetch(in_two.at[index, rows_at(member - chips, share)])

            else:
                fetch(in_far.at[index - soon, rows_at(member, share)])

    load_units(1)
    dm_loaded = pltpu.make_async_copy(dm_hbm, grad_ref, dm_load)
    dm_loaded.start()
    meet(greet_group(group) + greet_seq(seqs))
    near, far_off = seq_peers(seqs)
    down = ToPeers(seqs, far_off, down_hbm, down_in, down_send, down_recv)
    down.begin()
    swap = Swap(group, unit_sums, units, unit_send, unit_recv, unit_keep)

    @pl.loop(1, group + 1)
    def _(turn):
        member = lax.rem(own + turn, group)
        slot = lax.rem(turn, 2)
        pl.when(turn < group)(lambda: load_units(turn + 1))
        for place in range(seqs):
            unit_loaded(turn, place, part_hbm.at[rows_at(0, share)]).wait()

        @pl.loop(0, share // 16)
        def _(chunk):
            here = rows_at(chunk, 16)
            added = unit_parts[slot, 0, here, :].astype(jnp.float32)
            for place in range(1, seqs):
                added = added + unit_parts[slot, place, here, :].astype(jnp.float32)
            unit_sums[member, here, :] = to_half(added)

        pl.when(turn < group)(lambda: swap.move(member, own).start())
        pl.when(turn == group)(lambda: swap.kept().start())

    def halo(batch, step, peer):
        here = rows_at(step, block)
        return pltpu.make_async_remote_copy(
            src_ref=back_out.at[batch, here],
            dst_ref=back_in.at[batch, here],
            send_sem=halo_send.at[batch, step],
            recv_sem=halo_recv.at[batch, step],
            device_id={"seq": peer},
            device_id_type=MESH,
        )

    def attend_block(batch, step):
        begin = pl.multiple_of(step * block, block)
        keys = pl.ds(begin, block + WINDOW)
        rows = pl.ds(begin, block)
        low = low_ref[batch, :, rows]
        for pair in range(span // PAIR):
            lanes = slice(pair * PAIR, (pair + 1) * PAIR)
            q_pair = q_ref[batch, rows, lanes] * scale
            d_pair = d_ref[batch, rows, lanes]
            k_rows = pad_ref[batch, keys, lanes]
            v_rows = pad_ref[batch, keys, span + pair * PAIR : span + (pair + 1) * PAIR]
            k_cols = kt[lanes, keys]
            back = []
            for half in range(2):
                row = pair * 2 + half
                q_head = head_lanes(q_pair, half)
                d_head = head_lanes(d_pair, half)
                scores = masked_scores(k_rows, q_head, low)
                probs = jnp.exp(scores - lse_ref[batch, row : row + 1, rows])
                d_probs = dot_nt(v_rows, d_head)
                along = jnp.sum(probs * d_probs, axis=0, keepdims=True)
                d_scores = to_half(probs * (d_probs - along))
                dv[keys, lanes] += dot_nn(to_half(probs), d_head)
                dk[keys, lanes] += dot_nn(d_scores, q_head)
                back.append(dot_nn(k_cols, d_scores))
            at = lax.broadcasted_iota(jnp.int32, back[0].shape, 0)
            heads[batch, rows, lanes] = to_half(
                jnp.where(at < HEAD, back[0], back[1]).T
            )


        @pl.when(has_left & (step < need))
        def _():
            back_out[batch, rows, :span] = to_half(dk[rows, :])
            back_out[batch, rows, span:] = to_half(dv[rows, :])
            halo(batch, step, seq - 1).start()

        @pl.when(step == steps - 1)
        def _():
            heads[batch, :, span : 2 * span] = to_half(dk[WINDOW:, :])
            heads[batch, :, 2 * span :] = to_half(dv[WINDOW:, :])

    def add_halo(batch):
        @pl.when(has_right)
        def _():
            @pl.loop(0, need)
            def _(step):
                there = pl.ds(pl.multiple_of(step * block + first, block), block)
                halo(batch, step, seq).wait_recv()
                got = back_in[batch, rows_at(step, block), :].astype(jnp.float32)
                mine = heads[batch, there, span:].astype(jnp.float32)
                heads[batch, there, span:] = to_half(mine + got)

    def product(batch):
        def get(place, here):
            return dot_nt(heads[batch, rows_at(place, pair_rows), :], w_ref[here, :])

        return get

    reduces = [
        PairReduce(
            line, product(batch), totals.at[batch], acc, keep, *line_sums[6 * batch : 6 * batch + 6]
        )
        for batch in range(batches)
    ]
    last = 2 * chips - 2

    @pl.loop(0, 2 * steps)
    def _(turn):
        batch, step = turn // steps, lax.rem(turn, steps)

        @pl.when(step == 0)
        def _():
            kt[...] = pad_ref[batch, :, :span].T * scale
            dk[...] = jnp.zeros_like(dk)
            dv[...] = jnp.zeros_like(dv)

        attend_block(batch, step)
        after = turn - steps - 1
        pl.when(after == 0)(lambda: add_halo(0))

        @pl.when((after >= 0) & (2 * after < last))
        def _():
            reduces[0].step(2 * after)
            reduces[0].step(2 * after + 1)

    for after in range(steps - 1, chips - 1):
        reduces[0].step(2 * after)
        reduces[0].step(2 * after + 1)

    def left(tile):
        slot = lax.rem(tile, 2)
        return pltpu.make_async_copy(
            g_hbm.at[:, :, rows_at(tile, part)], lefts.at[slot], left_sem.at[slot]
        )

    heads_near = ToPeers(seqs, near + far_off, parts, sums, part_send, part_recv)
    left(0).start()
    add_halo(1)

    @pl.loop(0, width // part)
    def _(tile):
        left(tile).wait()
        pl.when(tile + 1 < width // part)(lambda: left(tile + 1).start())
        slot = lax.rem(tile, 2)
        got = contract_rows(lefts[slot, 0], heads[0])
        for batch in range(1, batches):
            got = got + contract_rows(lefts[slot, batch], heads[batch])
        parts[rows_at(tile, part), :] = to_half(got)

    heads_near.begin()
    from_seq = ToPeers(seqs, near + far_off, out_ref, out_in, out_send, out_recv)
    from_seq.begin()
    gain_acc[...] = jnp.zeros_like(gain_acc)
    dm_loaded.wait()

    def norm_batch(batch):
        mine = pl.ds(batch * piece, piece)

        def put(here, d_values):
            there = pl.ds(pl.multiple_of(here.start + batch * piece, here.size), here.size)
            grad_ref[there, :] += d_values

        norm_back(piece, v_ref.at[mine], totals.at[batch], gain_ref, gain_acc, put)

    pl.loop(0, 2)(reduces[1].step)
    reduces[0].step(last)
    norm_batch(0)
    pl.loop(2, last)(reduces[1].step)
    swap.end()
    cell = units.shape[2] // 2 // seqs
    for member in range(group):
        for place in range(seqs):
            column = (place * group + member) * cell
            for target, begin in ((gate_ref, 0), (up_ref, seqs * cell)):
                here = slice(begin + place * cell, begin + (place + 1) * cell)
                target[:, column : column + cell] = units[member, :, here]

    results = [
        pltpu.make_async_copy(source, target, result_sem.at[index])
        for index, (source, target) in enumerate(
            ((gate_ref, gate_hbm), (up_ref, up_hbm), (wo_ref, wo_hbm), (grad_ref, grad_hbm))
        )
    ]
    results[0].start()
    results[1].start()

    def block_swap(peer, member):
        return pltpu.make_async_remote_copy(
            src_ref=parts.at[rows_at(seq * group + peer, share)],
            dst_ref=cols.at[member],
            send_sem=cols_send.at[peer],
            recv_sem=cols_recv.at[member],
            device_id={"fsdp": peer},
            device_id_type=MESH,
        )

    heads_near.arrived()

    @pl.loop(0, run // 64)
    def _(chunk):
        here = rows_at(chunk, 64)
        there = pl.ds(pl.multiple_of(seq * run + chunk * 64, 64), 64)
        parts[there, :] = to_half(add_from_seq(parts[there, :], sums, here))

    others(group, own, lambda peer: block_swap(peer, own).start())
    cols[own] = parts[rows_at(seq * group + own, share), :]
    from_seq.arrived()
    out_rows = out_in.shape[1]
    wo_ref[...] = add_from_seq(out_ref[rows_at(seq, out_rows), :], out_in, slice(None))
    results[2].start()
    reduces[1].step(last)
    norm_batch(1)
    results[3].start()
    fold = 128 // share
    near = group // fold
    attn_row = jnp.sum(gain_acc[...], axis=0, keepdims=True)
    mlp_row = jnp.sum(mlp_gain_ref[...], axis=0, keepdims=True)
    gain_out[...] = jnp.zeros_like(gain_out)
    for place in range(width // 128):
        lanes = slice(place * 128, (place + 1) * 128)
        gain_out[place % near, place // near, 0:1, :] = attn_row[:, lanes]
        gain_out[place % near, place // near, 1:2, :] = mlp_row[:, lanes]

    def gain_group(peer, member):
        return pltpu.make_async_remote_copy(
            src_ref=gain_out.at[peer // fold],
            dst_ref=gain_in.at[member],
            send_sem=gain_send.at[peer],
            recv_sem=gain_recv.at[member],
            device_id={"fsdp": peer},
            device_id_type=MESH,
        )

    def gain_seq(peer, place):
        return pltpu.make_async_remote_copy(
            src_ref=gain_sum.at[peer],
            dst_ref=gain_back.at[place],
            send_sem=back_send.at[peer],
            recv_sem=back_recv.at[place],
            device_id={"seq": peer},
            device_id_type=MESH,
        )

    others(group, own, lambda peer: gain_group(peer, own).start())
    gain_in[own] = gain_out[own // fold]
    others(group, own, lambda peer: gain_group(peer, peer).wait_recv())
    gain_sum[...] = jnp.sum(gain_in[...], axis=0)
    others(seqs, seq, lambda peer: gain_seq(peer, seq).start())
    gain_back[seq] = gain_sum[seq]
    others(seqs, seq, lambda peer: gain_seq(peer, peer).wait_recv())
    tile_ref[...] = jnp.sum(gain_back[...], axis=0)
    others(group, own, lambda peer: block_swap(peer, peer).wait_recv())
    for index, target in enumerate((wq_ref, wk_ref, wv_ref)):
        for member, first, home, size in column_parts(seqs, group, share, span):
            first = first + index * span
            target[:, home : home + size] = cols[member, :, first : first + size]
    from_seq.sent()
    for item in results:
        item.wait()
    for batch in range(batches):
        reduces[batch].sent()

        @pl.when(has_left)
        def _(batch=batch):
            pl.loop(0, need)(lambda step: halo(batch, step, seq).wait_send())

    heads_near.sent()
    down.end()
    others(group, own, lambda peer: gain_group(peer, own).wait_send())
    others(group, own, lambda peer: block_swap(peer, own).wait_send())
    others(seqs, seq, lambda peer: gain_seq(peer, seq).wait_send())


def attention_back(
    seqs, chips, block, query, kv_pad, low, lse, d_att, part_own, parts_one, parts_two, parts_far, w, group_a,
    x, d_middle, gain, mlp_gain, out_part, down, collective,
):
    batches, length, span = query.shape
    padded = kv_pad.shape[1]
    rows, width = x.shape
    piece = rows // batches
    group = 2 * chips
    depth = w.shape[1]
    run = width // seqs
    share = run // group
    near = group // (128 // share)
    cells = part_own.shape[1]
    out_rows = out_part.shape[0] // seqs
    half, wide = jnp.bfloat16, jnp.float32
    part = 256 if batches * length <= 2048 else 128
    return pl.pallas_call(
        functools.partial(attention_back_kernel, seqs, chips, block),
        out_shape=[
            jax.ShapeDtypeStruct((rows, width), wide),
            jax.ShapeDtypeStruct((share, width), half),
            jax.ShapeDtypeStruct((share, width), half),
            jax.ShapeDtypeStruct((share, width), half),
            jax.ShapeDtypeStruct((out_rows, width), wide),
            jax.ShapeDtypeStruct((8, 128), wide),
            jax.ShapeDtypeStruct((share, cells // 2 * group), half),
            jax.ShapeDtypeStruct((share, cells // 2 * group), half),
            jax.ShapeDtypeStruct((seqs - 1 - near_count(seqs), down.shape[0] // seqs, width), half),
        ],
        in_specs=[VMEM_SPEC] * 5
        + [ANY_SPEC] * 4
        + [VMEM_SPEC, ANY_SPEC, VMEM_SPEC, ANY_SPEC]
        + [VMEM_SPEC] * 3
        + [ANY_SPEC],
        out_specs=[ANY_SPEC, VMEM_SPEC, VMEM_SPEC, VMEM_SPEC, ANY_SPEC, VMEM_SPEC]
        + [ANY_SPEC] * 3,
        scratch_shapes=[
            pltpu.VMEM((rows, width), wide),
            pltpu.VMEM((out_rows, width), wide),
            pltpu.VMEM((share, cells // 2 * group), half),
            pltpu.VMEM((share, cells // 2 * group), half),
            sems(4),
            sems(seqs),
            sems(seqs),
            pltpu.VMEM((padded, span), wide),
            pltpu.VMEM((padded, span), wide),
            pltpu.VMEM((span, padded), half),
            pltpu.VMEM((batches, length, depth), half),
            pltpu.VMEM((batches, WINDOW, 2 * span), half),
            pltpu.VMEM((batches, WINDOW, 2 * span), half),
            pltpu.VMEM((2, seqs, share, cells), half),
            pltpu.VMEM((group, share, cells), half),
            pltpu.VMEM((group, share, cells), half),
            pltpu.VMEM((2, batches, length, part), half),
            pltpu.VMEM((width, depth), half),
            pltpu.VMEM((seqs - 1, run, depth), half),
            pltpu.VMEM((group, share, depth), half),
            pltpu.VMEM((seqs - 1, out_rows, width), half),
            pltpu.VMEM((batches, piece, width), wide),
            pltpu.VMEM((8, width), wide),
            pltpu.VMEM((near, seqs, 8, 128), wide),
            pltpu.VMEM((group, seqs, 8, 128), wide),
            pltpu.VMEM((seqs, 8, 128), wide),
            pltpu.VMEM((seqs, 8, 128), wide),
            pltpu.VMEM((2 * piece, TILE), wide),
            pltpu.VMEM((piece, width), wide),
            sems(batches, WINDOW // block),
            sems(batches, WINDOW // block),
            sems(2, seqs),
            sems(group),
            sems(group),
            pltpu.SemaphoreType.DMA,
            pltpu.SemaphoreType.DMA,
            sems(2),
            sems(seqs),
            sems(seqs),
            sems(group),
            sems(group),
            sems(seqs),
            sems(seqs),
            sems(group),
            sems(group),
            sems(seqs),
            sems(seqs),
        ]
        + PairReduce.scratch(chips, piece, width) * batches,
        compiler_params=comm_params(collective, 63),
        cost_estimate=cost(
            20 * batches * length * span * (WINDOW + block) + 4 * group * rows * width * depth,
            400 * MIB,
            3 * group * rows * width * 2,
        ),
        name="attention_back",
    )(
        query, kv_pad, low, lse, d_att, part_own, parts_one, parts_two, parts_far, w, group_a, x,
        d_middle, gain, mlp_gain, out_part, down,
    )


def finish_kernel(count, *refs):
    sources, targets = refs[:-count], refs[-count:]
    for source, target in zip(sources, targets[:-1]):
        target[...] = source[...].astype(target.dtype)
    added = 0.0
    for source in sources[count - 1 :]:
        added = added + jnp.sum(source[...].astype(jnp.float32), axis=0)
    targets[-1][...] = added


def finish(steps, arrays, parts, kinds):
    in_specs, out_specs, out_shape = [], [], []
    for item, kind in zip(arrays + parts[:1], kinds):
        rows, width = item.shape[-2:]
        block = (rows // steps, width)
        out_specs.append(pl.BlockSpec(block, lambda i: (i, 0)))
        out_shape.append(jax.ShapeDtypeStruct((rows, width), kind))
        if item.ndim == 2:
            in_specs.append(out_specs[-1])
    for item in parts:
        in_specs.append(pl.BlockSpec((item.shape[0],) + block, lambda i: (0, i, 0)))
    return pl.pallas_call(
        functools.partial(finish_kernel, len(kinds)),
        grid=(steps,),
        in_specs=in_specs,
        out_specs=out_specs,
        out_shape=out_shape,
        compiler_params=pltpu.CompilerParams(vmem_limit_bytes=63 * MIB),
        name="finish",
    )(*arrays, *parts)


def doc_starts(lengths, positions, batches, seq_len):
    table = lengths.reshape(batches, -1, lengths.shape[1])
    starts = jnp.cumsum(table, axis=2) - table
    per_batch = seq_len // table.shape[1]
    begins = (starts + (jnp.arange(table.shape[1], dtype=jnp.int32) * per_batch)[None, :, None]).reshape(
        batches, -1
    )
    before = begins[:, None, :] <= positions[None, :, None]
    return jnp.max(jnp.where(before, begins[:, None, :], 0), axis=2)


def body(
    tokens,
    cotangent,
    lengths,
    gain_attn,
    w_query,
    w_key,
    w_value,
    w_out,
    gain_mlp,
    w_gate,
    w_up,
    w_down,
):
    batches, piece, width = tokens.shape
    seqs = lax.axis_size("seq")
    group = lax.axis_size("fsdp")
    chips = group // 2
    devices = seqs * group
    seq_len = piece * devices
    rows = batches * piece
    share = w_query.shape[0]
    span = width // group
    length = group * piece
    aligned = share == HEAD
    member = lax.axis_index("fsdp")

    x_rows = tokens.reshape(rows, width)
    cot_rows = cotangent.reshape(rows, width)
    if aligned:
        wo_part = lax.all_gather(w_out, "seq", axis=0, tiled=True)
    else:
        wo_all = lax.all_gather(w_out, ("seq", "fsdp"), axis=0, tiled=True)
        wo_part = lax.dynamic_slice_in_dim(wo_all, member * span, span, 0)

    lane = jnp.arange(128, dtype=jnp.int32)
    device = lax.axis_index("seq") * group + member
    fold = 128 // share
    here = lane // share == lax.rem(device, fold)
    both = jnp.stack([gain_attn, gain_mlp]).astype(jnp.float32)
    tile = jnp.where(here[None], jnp.tile(both, (1, fold)), 0.0)
    tile = jnp.pad(tile, ((0, 6), (0, 0)))[None]
    group_start = lax.axis_index("seq") * length
    positions = group_start + jnp.arange(length, dtype=jnp.int32)
    begins = doc_starts(lengths, positions, batches, seq_len)
    at = jnp.arange(length, dtype=jnp.int32)
    block = min(256, length)
    low = jnp.maximum(begins - group_start + WINDOW, at[None, :] + 1) - (at // block * block)[None, :]
    low = low[:, None, :]
    group_a, query, attended, lse, kv_pad, gains, w_heads, unit_own, wd_one = start(
        seqs, chips, batches, block, tile, x_rows, (w_query, w_key, w_value), (w_gate, w_up), w_down,
        low, 1,
    )
    gains = gains.transpose(1, 0, 2, 3).reshape(devices // fold, fold, 8, 128).sum(axis=1)
    gain_one = gains[:, 0].reshape(width)
    gain_two = gains[:, 1].reshape(width)
    middle, normed_b, group_d, w_units, wd_two = branch_sum(
        seqs, chips, attended, wo_part, cot_rows, unit_own.reshape(group * share, -1), w_down,
        x_rows, gain_two[None], 3,
    )
    w_units = w_units.reshape(width, -1)
    d_middle, d_branch, mlp_gain_part, hidden, unit_part, unit_one = feed_forward(
        seqs, chips, batches, normed_b, w_units, (wd_one, wd_two), group_d, middle, cot_rows,
        gain_two[None], 4,
    )
    d_attended, layer_out, out_part, unit_two, unit_far, down_part, down_near = branch_back(
        seqs, chips, batches, d_branch, wo_part, attended, middle, hidden, (wd_one, wd_two),
        unit_part, group_d, 5,
    )
    if not aligned:
        whole = lax.dynamic_update_slice_in_dim(
            jnp.zeros((width, width), jnp.bfloat16), out_part, member * span, 0
        )
        out_part = lax.psum(whole, "fsdp").reshape(seqs, group, share, width)
        out_part = lax.dynamic_slice_in_dim(out_part, member, 1, 1).reshape(seqs * share, width)
    (
        input_grad, wq_grad, wk_grad, wv_grad, wo_grad, gain_tile, gate_grad, up_grad, down_far,
    ) = attention_back(
        seqs, chips, block, query, kv_pad, low, lse, d_attended, unit_part, unit_one, unit_two,
        unit_far, w_heads, group_a, x_rows, d_middle, gain_one[None], mlp_gain_part, out_part,
        down_part, 6,
    )
    gain_grads = lax.dynamic_slice_in_dim(gain_tile[:2], lax.rem(device, fold) * share, share, 1)
    wide = jnp.float32
    (layer_out, input_grad, wq_grad, wk_grad, wv_grad, wo_grad, gate_grad, up_grad, down_grad) = finish(
        share // 16,
        [layer_out, input_grad, wq_grad, wk_grad, wv_grad, wo_grad, gate_grad, up_grad],
        [down_near, down_far],
        [jnp.bfloat16] + [wide] * 8,
    )
    return (
        layer_out.reshape(batches, piece, width),
        input_grad.reshape(batches, piece, width),
        gain_grads[0],
        wq_grad,
        wk_grad,
        wv_grad,
        wo_grad,
        gain_grads[1],
        gate_grad,
        up_grad,
        down_grad,
    )


def solution(mesh):
    spread = ("seq", "fsdp")
    tokens, rows, gains = P(None, spread, None), P(spread, None), P(spread)
    in_specs = (tokens, tokens, P(), gains, rows, rows, rows, rows, gains, rows, rows, rows)
    out_specs = (tokens, tokens, gains, rows, rows, rows, rows, gains, rows, rows, rows)
    return jax.shard_map(body, mesh=mesh, in_specs=in_specs, out_specs=out_specs, check_vma=False)
```

```python
import functools

import jax
import jax.numpy as jnp
from jax import lax
from jax.experimental import pallas as pl
from jax.experimental.pallas import tpu as pltpu
from jax.sharding import PartitionSpec as P

HEAD = 64
FF = 8192
WINDOW = 1024
PAIR = 128
TILE = 512
PARTS = 4
LOW = -1e30
EPS = 1e-05
MESH = pl.DeviceIdType.MESH
MIB = 2**20


def to_half(values):
    return values.astype(jnp.bfloat16)


def normalize(values, gain):
    return values * lax.rsqrt(jnp.mean(values * values, axis=-1, keepdims=True) + EPS) * gain


def contract_rows(left, right):
    return lax.dot_general(
        left, right, (((0,), (0,)), ((), ())), preferred_element_type=jnp.float32
    )


def dot_nt(left, right):
    return lax.dot_general(
        left, right, (((1,), (1,)), ((), ())), preferred_element_type=jnp.float32
    )


def dot_nn(left, right):
    return jnp.dot(left, right, preferred_element_type=jnp.float32)


def head_lanes(values, half):
    lane = lax.broadcasted_iota(jnp.int32, values.shape, 1)
    return jnp.where((lane >= HEAD) == (half == 1), values, jnp.zeros_like(values))


def masked_scores(k_rows, q_head, low):
    keys, block = k_rows.shape[0], q_head.shape[0]
    scores = dot_nt(k_rows, q_head)
    at = lax.broadcasted_iota(jnp.int32, (keys, block), 0)
    query = lax.broadcasted_iota(jnp.int32, (keys, block), 1)
    seen = (at >= low) & (at <= query + WINDOW)
    return jnp.where(seen, scores, LOW)


class Line:
    def __init__(self, chips):
        self.chips = chips
        self.own = lax.axis_index("fsdp")
        self.chip = self.own // 2
        self.core = lax.rem(self.own, 2)
        self.other = self.own + 1 - 2 * self.core
        self.has_left = self.chip > 0
        self.has_right = self.chip < chips - 1

    def greet(self):
        signal_group(self.other)
        pl.when(self.has_left)(lambda: signal_group(self.own - 2))
        pl.when(self.has_right)(lambda: signal_group(self.own + 2))
        return 1 + self.has_left.astype(jnp.int32) + self.has_right.astype(jnp.int32)


def signal_group(peer):
    barrier = pltpu.get_barrier_semaphore()
    pl.semaphore_signal(barrier, inc=1, device_id={"fsdp": peer}, device_id_type=MESH)


def signal_seq(peer):
    barrier = pltpu.get_barrier_semaphore()
    pl.semaphore_signal(barrier, inc=1, device_id={"seq": peer}, device_id_type=MESH)


def greet_group(group):
    own = lax.axis_index("fsdp")
    pl.loop(1, group)(lambda ahead: signal_group(lax.rem(own + ahead, group)))
    return group - 1


def greet_seq(seqs):
    own = lax.axis_index("seq")
    pl.loop(1, seqs)(lambda ahead: signal_seq(lax.rem(own + ahead, seqs)))
    return seqs - 1


def meet(count):
    pl.semaphore_wait(pltpu.get_barrier_semaphore(), count)


def rows_at(index, size):
    return pl.ds(pl.multiple_of(index * size, size), size)


class Spread:
    def __init__(self, line, first, buf, send, recv):
        self.line, self.first, self.buf, self.send, self.recv = line, first, buf, send, recv
        self.parts = recv.shape[1]
        self.size = first.shape[0] // self.parts

    def move(self, slot, part, way, peer, source=None):
        here = rows_at(part, self.size)
        return pltpu.make_async_remote_copy(
            src_ref=self.buf.at[slot, here] if source is None else source.at[here],
            dst_ref=self.buf.at[slot, here],
            send_sem=self.send.at[way, slot, part],
            recv_sem=self.recv.at[slot, part],
            device_id={"fsdp": peer},
            device_id_type=MESH,
        )

    def begin(self):
        line = self.line

        @pl.loop(0, self.parts)
        def _(part):
            pl.when(line.has_right)(
                lambda: self.move(line.own, part, 1, line.own + 2, self.first).start()
            )
            pl.when(line.has_left)(
                lambda: self.move(line.own, part, 0, line.own - 2, self.first).start()
            )
            self.move(line.own, part, 2, line.other, self.first).start()

    def relay_part(self, far, part):
        line = self.line

        @pl.when(line.chip - far >= 0)
        def _():
            slot = (line.chip - far) * 2 + line.core
            self.move(slot, part, 1, line.own).wait_recv()
            pl.when(line.has_right)(lambda: self.move(slot, part, 1, line.own + 2).start())
            self.move(slot, part, 2, line.other).start()

        @pl.when(line.chip + far < line.chips)
        def _():
            slot = (line.chip + far) * 2 + line.core
            self.move(slot, part, 0, line.own).wait_recv()
            pl.when(line.has_left)(lambda: self.move(slot, part, 0, line.own - 2).start())
            self.move(slot, part, 2, line.other).start()

    def relay(self, far):
        pl.loop(0, self.parts)(lambda part: self.relay_part(far, part))

    def across(self, slot):
        pl.loop(0, self.parts)(lambda part: self.move(slot, part, 2, self.line.own).wait_recv())

    def each(self, far, use):
        line = self.line

        @pl.loop(0, 4)
        def _(turn):
            side = lax.rem(turn, 2)
            over = turn // 2
            away = far - over
            source = line.chip + away * (2 * side - 1)
            valid = (away >= 0) & (away < line.chips) & (source >= 0) & (source < line.chips)
            valid = valid & ((side == 0) | (away > 0))

            @pl.when(valid)
            def _():
                slot = source * 2 + line.core + over * (1 - 2 * line.core)
                pl.when(over == 1)(lambda: self.across(slot))
                use(slot)

    def rest(self):
        pl.loop(0, self.line.chips)(lambda place: self.across(place * 2 + 1 - self.line.core))

    def sent(self):
        line = self.line

        @pl.loop(0, line.chips)
        def _(place):
            slot = place * 2 + line.core

            @pl.loop(0, self.parts)
            def _(part):
                self.move(slot, part, 2, line.other).wait_send()
                pl.when(line.has_right & (place <= line.chip))(
                    lambda: self.move(slot, part, 1, line.own + 2).wait_send()
                )
                pl.when(line.has_left & (place >= line.chip))(
                    lambda: self.move(slot, part, 0, line.own - 2).wait_send()
                )


class Reduce:
    def __init__(self, line, product, out, acc, cross_out, line_out, cross_in, line_in, send, recv):
        self.line, self.product, self.out, self.acc = line, product, out, acc
        self.cross_out, self.line_out, self.cross_in, self.line_in = cross_out, line_out, cross_in, line_in
        self.send, self.recv = send, recv
        self.tiles = line_out.shape[2] // TILE

    @staticmethod
    def scratch(chips, rows, width):
        part = pltpu.VMEM((chips, rows, width), jnp.bfloat16)
        return [
            pltpu.VMEM((rows, TILE), jnp.float32),
            pltpu.VMEM((2, rows, width), jnp.bfloat16),
            part,
            part,
            pltpu.VMEM((chips + 1, rows, width), jnp.bfloat16),
            pltpu.SemaphoreType.DMA((2, chips, width // TILE)),
            pltpu.SemaphoreType.DMA((2, chips + 1, width // TILE)),
        ]

    def cross(self, side, place, tile):
        here = rows_at(tile, TILE)
        return pltpu.make_async_remote_copy(
            src_ref=self.cross_out.at[side, :, here],
            dst_ref=self.cross_in.at[place, :, here],
            send_sem=self.send.at[0, place, tile],
            recv_sem=self.recv.at[0, place, tile],
            device_id={"fsdp": self.line.other},
            device_id_type=MESH,
        )

    def along(self, place, landing, tile, peer):
        here = rows_at(tile, TILE)
        return pltpu.make_async_remote_copy(
            src_ref=self.line_out.at[place, :, here],
            dst_ref=self.line_in.at[landing, :, here],
            send_sem=self.send.at[1, place, tile],
            recv_sem=self.recv.at[1, landing, tile],
            device_id={"fsdp": peer},
            device_id_type=MESH,
        )

    def where(self, away, side):
        line = self.line
        rightward = (line.chips - 1 - line.chip >= line.chip) == (side == 0)
        place = line.chip + jnp.where(rightward, away, -away)
        valid = (place >= 0) & (place < line.chips) & ((away > 0) | (side == 0))
        return valid, place, rightward

    def level(self, away, also):
        @pl.loop(0, 2)
        def _(side):
            valid, place, _ = self.where(away, side)

            @pl.when(valid)
            def _():
                @pl.loop(0, self.tiles)
                def _(tile):
                    got = self.product(place * 2 + 1 - self.line.core, tile)
                    self.cross_out[side, :, rows_at(tile, TILE)] = to_half(got)
                    self.cross(side, place, tile).start()

        @pl.loop(0, self.tiles)
        def _(tile):
            @pl.loop(0, 2)
            def _(side):
                valid, place, rightward = self.where(away, side)
                pl.when(valid)(lambda: self.close(away, side, place, rightward, tile))

            also(tile)

    def close(self, away, side, place, rightward, tile):
        line, acc = self.line, self.acc
        here = rows_at(tile, TILE)
        upstream = (rightward & line.has_left) | (jnp.logical_not(rightward) & line.has_right)
        acc[...] = self.product(place * 2 + line.core, tile)
        self.cross(side, place, tile).wait()
        acc[...] += self.cross_in[place, :, here].astype(jnp.float32)

        @pl.when(away > 0)
        def _():
            @pl.when(upstream)
            def _():
                self.along(place, place, tile, line.own).wait_recv()
                self.line_out[place, :, here] = to_half(
                    acc[...] + self.line_in[place, :, here].astype(jnp.float32)
                )

            @pl.when(jnp.logical_not(upstream))
            def _():
                self.line_out[place, :, here] = to_half(acc[...])

            @pl.when(rightward)
            def _():
                self.along(place, place, tile, line.own + 2).start()

            @pl.when(jnp.logical_not(rightward))
            def _():
                landing = jnp.where(away == 1, line.chips, place)
                self.along(place, landing, tile, line.own - 2).start()

        @pl.when(away == 0)
        def _():
            self.out[:, here] = acc[...]

            @pl.when(line.has_left)
            def _():
                self.along(place, place, tile, line.own).wait_recv()
                self.out[:, here] += self.line_in[place, :, here].astype(jnp.float32)

            @pl.when(line.has_right)
            def _():
                self.along(place, line.chips, tile, line.own).wait_recv()
                self.out[:, here] += self.line_in[line.chips, :, here].astype(jnp.float32)

    def sent(self):
        @pl.loop(0, self.line.chips)
        def _(place):
            @pl.when(place != self.line.chip)
            def _():
                pl.loop(0, self.tiles)(
                    lambda tile: self.along(place, place, tile, self.line.own).wait_send()
                )


class Swap:
    def __init__(self, group, source, target, send, recv, keep):
        self.group, self.source, self.target = group, source, target
        self.send, self.recv, self.keep = send, recv, keep
        self.own = lax.axis_index("fsdp")

    def move(self, peer, source):
        return pltpu.make_async_remote_copy(
            src_ref=self.source.at[peer],
            dst_ref=self.target.at[source],
            send_sem=self.send.at[peer],
            recv_sem=self.recv.at[source],
            device_id={"fsdp": peer},
            device_id_type=MESH,
        )

    def kept(self):
        return pltpu.make_async_copy(self.source.at[self.own], self.target.at[self.own], self.keep)

    def begin(self):
        self.kept().start()
        pl.loop(1, self.group)(
            lambda ahead: self.move(lax.rem(self.own + ahead, self.group), self.own).start()
        )

    def end(self):
        self.kept().wait()

        @pl.loop(1, self.group)
        def _(ahead):
            peer = lax.rem(self.own + ahead, self.group)
            self.move(peer, peer).wait_recv()
            self.move(peer, self.own).wait_send()


class Share:
    def __init__(self, seqs, source, target, send, recv, keep):
        self.seqs, self.source, self.target = seqs, source, target
        self.send, self.recv, self.keep = send, recv, keep
        self.own = lax.axis_index("seq")
        self.parts = send.shape[2]
        self.size = source.shape[0] // self.parts

    def move(self, peer, place, part):
        here = pl.ds(part * self.size, self.size)
        return pltpu.make_async_remote_copy(
            src_ref=self.source.at[here],
            dst_ref=self.target.at[place, here],
            send_sem=self.send.at[peer, 0, part],
            recv_sem=self.recv.at[place, 0, part],
            device_id={"seq": peer},
            device_id_type=MESH,
        )

    def relay(self, peer, place, part, side):
        here = pl.ds(part * self.size + side * (self.size // 2), self.size // 2)
        return pltpu.make_async_remote_copy(
            src_ref=self.target.at[place, here],
            dst_ref=self.target.at[place, here],
            send_sem=self.send.at[peer, 1, part],
            recv_sem=self.recv.at[place, side, part],
            device_id={"seq": peer},
            device_id_type=MESH,
        )

    def near(self):
        one = self.own + 1 - 2 * lax.rem(self.own, 2)
        two = lax.rem(self.own + 2, 4)
        return one, two, lax.rem(one + 2, 4)

    def kept(self):
        return pltpu.make_async_copy(self.source, self.target.at[self.own], self.keep)

    def begin(self):
        self.kept().start()
        for part in range(self.parts):
            if self.seqs == 4:
                one, two, _ = self.near()
                self.move(one, self.own, part).start()
                self.move(two, self.own, part).start()
            else:
                pl.loop(1, self.seqs)(
                    lambda ahead, part=part: self.move(
                        lax.rem(self.own + ahead, self.seqs), self.own, part
                    ).start()
                )

    def pass_on(self, parts):
        if self.seqs == 4:
            one, two, _ = self.near()
            for part in parts:
                self.move(one, one, part).wait_recv()
                self.relay(two, one, part, 0).start()
                self.move(two, two, part).wait_recv()
                self.relay(one, two, part, 1).start()

    def end(self):
        self.kept().wait()
        for part in range(self.parts):
            if self.seqs == 4:
                one, two, far = self.near()
                self.relay(two, far, part, 0).wait_recv()
                self.relay(one, far, part, 1).wait_recv()
                self.move(one, self.own, part).wait_send()
                self.move(two, self.own, part).wait_send()
                self.relay(two, one, part, 0).wait_send()
                self.relay(one, two, part, 1).wait_send()
            else:

                @pl.loop(1, self.seqs)
                def _(ahead, part=part):
                    peer = lax.rem(self.own + ahead, self.seqs)
                    self.move(peer, peer, part).wait_recv()
                    self.move(peer, self.own, part).wait_send()


def seq_peers(seqs):
    own = lax.axis_index("seq")
    if seqs == 4:
        one = own + 1 - 2 * lax.rem(own, 2)
        return [one, lax.rem(own + 2, 4)], [lax.rem(one + 2, 4)]
    ahead = [lax.rem(own + step, seqs) for step in range(1, seqs)]
    return ahead[:1], ahead[1:]


def near_count(seqs):
    return 2 if seqs == 4 else 1


class ToPeers:
    def __init__(self, seqs, peers, source, target, send, recv, first=0):
        self.peers, self.source, self.target, self.send, self.recv = peers, source, target, send, recv
        self.run, self.first = source.shape[0] // seqs, first

    def move(self, index):
        begin = pl.multiple_of(self.peers[index] * self.run + self.first, 16)
        return pltpu.make_async_remote_copy(
            src_ref=self.source.at[pl.ds(begin, self.target.shape[1])],
            dst_ref=self.target.at[index],
            send_sem=self.send.at[index],
            recv_sem=self.recv.at[index],
            device_id={"seq": self.peers[index]},
            device_id_type=MESH,
        )

    def begin(self):
        for index in range(len(self.peers)):
            self.move(index).start()

    def arrived(self):
        for index in range(len(self.peers)):
            self.move(index).wait_recv()

    def sent(self):
        for index in range(len(self.peers)):
            self.move(index).wait_send()

    def end(self):
        self.arrived()
        self.sent()


VMEM_SPEC = pl.BlockSpec(memory_space=pltpu.VMEM)
ANY_SPEC = pl.BlockSpec(memory_space=pl.ANY)


def comm_params(collective, mib=58):
    return pltpu.CompilerParams(
        collective_id=collective, has_side_effects=True, vmem_limit_bytes=mib * MIB
    )


def cost(flops, local, remote):
    return pl.CostEstimate(
        flops=flops, bytes_accessed=local, transcendentals=0, remote_bytes_transferred=remote
    )


def sems(*shape):
    return pltpu.SemaphoreType.DMA(shape)


def left_rows(a_ref, slot, rows):
    if len(a_ref.shape) == 2:
        return a_ref[rows_at(slot, rows), :]
    piece = rows // a_ref.shape[0]
    return jnp.concatenate(
        [a_ref[batch, rows_at(slot, piece), :] for batch in range(a_ref.shape[0])], axis=0
    )


def norm_back(rows, v_ref, e_ref, gain_ref, gain_acc, put):
    @pl.loop(0, rows // 32)
    def _(chunk):
        here = rows_at(chunk, 32)
        values = v_ref[here, :].astype(jnp.float32)
        error = e_ref[here, :]
        rate = lax.rsqrt(jnp.mean(values * values, axis=-1, keepdims=True) + EPS)
        unit = values * rate
        product = error * unit
        gain = gain_ref[0:1, :]
        mean = jnp.mean(product * gain, axis=-1, keepdims=True)
        gain_acc[...] += (product[0:8] + product[8:16]) + (product[16:24] + product[24:32])
        put(here, rate * (gain * error - unit * mean))


def add_from_seq(own_rows, got, here):
    added = own_rows.astype(jnp.float32)
    for index in range(got.shape[0]):
        added = added + got[index, here, :].astype(jnp.float32)
    return added


def column_parts(seqs, group, share, span):
    size = HEAD if share == HEAD else span
    parts = []
    for member in range(group):
        for run in range(span // size):
            home = (run * group + member) * size
            parts.append((member, run * size, home, size))
    return parts


def start_kernel(
    seqs, chips, batches, block, tile_ref, x_ref, wq_ref, wk_ref, wv_ref, gate_hbm, up_hbm, down_hbm, low_ref,
    g_ref, q_ref, out_ref, lse_ref, pad_ref, gains_ref, w_out_ref, own_units_ref, wd_ref,
    gate, up, units, blocks_ref, buf, normed, pad, vt, gain, gains, w,
    unit_sem, send, recv, keep, swap_send, share_send, w_recv,
    tile_send, tile_across, tile_recv, tile_back, w_keep, gain_keep,
    halo_send, halo_recv, pad_keep, unit_send, unit_recv, unit_keep,
    down_send, down_recv, down_keep,
):
    line = Line(chips)
    group = 2 * chips
    seq = lax.axis_index("seq")
    own = line.own
    share = blocks_ref.shape[1]
    rows, width = x_ref.shape
    piece = rows // batches
    length, span = q_ref.shape[1:]
    per = 128 * seqs * group // width
    steps, need = length // block, WINDOW // block
    has_left, has_right = seq > 0, seq < seqs - 1
    unit_loads = [
        pltpu.make_async_copy(gate_hbm, gate, unit_sem.at[0]),
        pltpu.make_async_copy(up_hbm, up, unit_sem.at[1]),
    ]
    for item in unit_loads:
        item.start()
    for index, source in enumerate((wq_ref, wk_ref, wv_ref)):
        for member, first, home, size in column_parts(seqs, group, share, span):
            first = first + index * span
            blocks_ref[member, :, first : first + size] = source[:, home : home + size]
    meet(greet_group(group) + greet_seq(seqs))

    def block_at(run, member):
        return w.at[rows_at(run * group + member, share)]

    def block_swap(peer, member):
        return pltpu.make_async_remote_copy(
            src_ref=blocks_ref.at[peer],
            dst_ref=block_at(seq, member),
            send_sem=swap_send.at[peer],
            recv_sem=w_recv.at[seq, member],
            device_id={"fsdp": peer},
            device_id_type=MESH,
        )

    def block_share(run, member, peer):
        return pltpu.make_async_remote_copy(
            src_ref=block_at(run, member),
            dst_ref=block_at(run, member),
            send_sem=share_send.at[peer, member],
            recv_sem=w_recv.at[run, member],
            device_id={"seq": peer},
            device_id_type=MESH,
        )

    def tile_to_seq(peer, place):
        return pltpu.make_async_remote_copy(
            src_ref=tile_ref.at[0],
            dst_ref=gains.at[own, place],
            send_sem=tile_send.at[peer],
            recv_sem=tile_recv.at[place],
            device_id={"seq": peer},
            device_id_type=MESH,
        )

    def tiles_to_group(peer, member):
        return pltpu.make_async_remote_copy(
            src_ref=gains.at[member],
            dst_ref=gains.at[member],
            send_sem=tile_across.at[peer],
            recv_sem=tile_back.at[member],
            device_id={"fsdp": peer},
            device_id_type=MESH,
        )

    def others(count, me, act):
        pl.loop(1, count)(lambda ahead: act(lax.rem(me + ahead, count)))

    others(seqs, seq, lambda peer: tile_to_seq(peer, seq).start())
    down = Share(seqs, down_hbm, wd_ref, down_send, down_recv, down_keep)
    down.begin()
    others(group, own, lambda peer: block_swap(peer, own).start())
    spreads = [
        Spread(line, x_ref.at[pl.ds(batch * piece, piece)], buf.at[batch], send.at[batch], recv.at[batch])
        for batch in range(batches)
    ]
    spreads[0].begin()
    gains[own, seq] = tile_ref[0]
    w[rows_at(seq * group + own, share), :] = blocks_ref[own]
    others(seqs, seq, lambda peer: block_share(seq, own, peer).start())
    for batch in range(batches):
        buf[batch, own] = x_ref[batch * piece : (batch + 1) * piece, :]
    others(seqs, seq, lambda peer: tile_to_seq(peer, peer).wait_recv())
    others(group, own, lambda peer: tiles_to_group(peer, own).start())
    for item in unit_loads:
        item.wait()
    cell = units.shape[2] // 2 // seqs
    for member in range(group):
        for run in range(seqs):
            home = (run * group + member) * cell
            for index, source in enumerate((gate, up)):
                first = (index * seqs + run) * cell
                units[member, :, first : first + cell] = source[:, home : home + cell]
    unit_swap = Swap(group, units, own_units_ref, unit_send, unit_recv, unit_keep)

    @pl.when(jnp.logical_not(has_left))
    def _():
        pad[:, :WINDOW, :] = jnp.zeros((batches, WINDOW, 2 * span), jnp.bfloat16)

    def pass_block(member):
        block_swap(member, member).wait_recv()
        others(seqs, seq, lambda peer: block_share(seq, member, peer).start())

    others(group, own, pass_block)
    down.pass_on([0])
    others(group, own, lambda peer: tiles_to_group(peer, peer).wait_recv())
    for column in range(width // 128):
        total = 0.0
        for place in range(column * per, (column + 1) * per):
            total = total + gains[place % group, place // group, 0:1, :]
        gain[0:1, column * 128 : (column + 1) * 128] = total

    def sides(far, act):
        @pl.loop(0, 2)
        def _(side):
            place = line.chip + far * (2 * side - 1)
            valid = (place >= 0) & (place < chips) & ((side == 0) | (far > 0))
            pl.when(valid)(lambda: act(place))

    def kept(batch, place):
        here = rows_at(place, block)
        return pltpu.make_async_copy(
            normed.at[batch, here], g_ref.at[batch, here], keep.at[batch, place]
        )

    def norm_pair(batch, place):
        spreads[batch].across(place * 2 + 1 - line.core)

        @pl.loop(0, 2)
        def _(member):
            @pl.loop(0, piece // 64)
            def _(chunk):
                values = buf[batch, place * 2 + member, rows_at(chunk, 64), :].astype(jnp.float32)
                there = pl.multiple_of(place * block + member * piece + chunk * 64, 64)
                normed[batch, pl.ds(there, 64), :] = to_half(normalize(values, gain[0:1, :]))

        kept(batch, place).start()

    def halo(batch, step, peer):
        there = pl.multiple_of(WINDOW + (step + steps - need) * block, block)
        return pltpu.make_async_remote_copy(
            src_ref=pad.at[batch, pl.ds(there, block)],
            dst_ref=pad.at[batch, rows_at(step, block)],
            send_sem=halo_send.at[batch, step],
            recv_sem=halo_recv.at[batch, step],
            device_id={"seq": peer},
            device_id_type=MESH,
        )

    def project(batch, place):
        here = rows_at(place, block)
        got = to_half(dot_nn(normed[batch, here, :], w[...]))
        q_ref[batch, here, :] = got[:, :span]
        pad[batch, pl.ds(pl.multiple_of(WINDOW + place * block, block), block), :] = got[:, span:]

        @pl.when(has_right & (place >= steps - need))
        def _():
            halo(batch, place - (steps - need), seq + 1).start()

    @pl.loop(0, chips)
    def _(far):
        pl.when(far > 0)(lambda: spreads[0].relay(far))
        pl.when(far == chips - 2)(spreads[1].begin)
        sides(far, lambda place: norm_pair(0, place))

    spreads[1].relay(1)

    def have_block(run, member):
        block_share(run, member, seq).wait_recv()

    others(seqs, seq, lambda run: pl.loop(0, group)(lambda member: have_block(run, member)))
    w_kept = pltpu.make_async_copy(w, w_out_ref, w_keep)
    w_kept.start()
    gains_kept = pltpu.make_async_copy(gains, gains_ref, gain_keep)
    gains_kept.start()
    pl.loop(0, steps)(lambda place: project(0, place))

    @pl.loop(2, chips)
    def _(far):
        spreads[1].relay(far)

    unit_swap.begin()

    @pl.loop(0, chips)
    def _(far):
        sides(far, lambda place: norm_pair(1, place))
        sides(far, lambda place: project(1, place))

    def pad_kept(batch):
        return pltpu.make_async_copy(pad.at[batch], pad_ref.at[batch], pad_keep.at[batch])

    for batch in range(batches):
        vt[:, WINDOW:] = pad[batch, WINDOW:, span:].T

        @pl.loop(0, steps)
        def _(turn, batch=batch):
            step = steps - 1 - turn

            @pl.when(step < need)
            def _():
                arrived = rows_at(step, block)
                pl.when(has_left)(lambda: halo(batch, step, seq).wait_recv())
                vt[:, arrived] = pad[batch, arrived, span:].T

            begin = pl.multiple_of(step * block, block)
            keys = pl.ds(begin, block + WINDOW)
            rows = pl.ds(begin, block)
            low = low_ref[batch, :, rows]
            for pair in range(span // PAIR):
                lanes = slice(pair * PAIR, (pair + 1) * PAIR)
                q_pair = q_ref[batch, rows, lanes] * jnp.asarray(HEAD**-0.5, jnp.bfloat16)
                k_rows = pad[batch, keys, lanes]
                values = vt[lanes, keys]
                mixed = []
                for half in range(2):
                    scores = masked_scores(k_rows, head_lanes(q_pair, half), low)
                    top = jnp.max(scores, axis=0, keepdims=True)
                    expo = jnp.exp(scores - top)
                    total = jnp.sum(expo, axis=0, keepdims=True)
                    mixed.append(dot_nn(values, to_half(expo)) / total)
                    row = pair * 2 + half
                    lse_ref[batch, row : row + 1, rows] = top + jnp.log(total)
                lane = lax.broadcasted_iota(jnp.int32, mixed[0].shape, 0)
                out_ref[batch, rows, lanes] = to_half(jnp.where(lane < HEAD, mixed[0], mixed[1]).T)

        pad_kept(batch).start()

    for batch in range(batches):
        spreads[batch].sent()
    others(seqs, seq, lambda peer: tile_to_seq(peer, seq).wait_send())
    others(group, own, lambda peer: block_swap(peer, own).wait_send())
    others(group, own, lambda peer: tiles_to_group(peer, own).wait_send())
    others(
        seqs,
        seq,
        lambda peer: pl.loop(0, group)(lambda member: block_share(seq, member, peer).wait_send()),
    )

    @pl.loop(0, need)
    def _(step):
        for batch in range(batches):
            pl.when(has_right)(lambda batch=batch: halo(batch, step, seq).wait_send())

    w_kept.wait()
    gains_kept.wait()
    unit_swap.end()
    down.end()
    for batch in range(batches):
        pad_kept(batch).wait()

        @pl.loop(0, steps)
        def _(place, batch=batch):
            kept(batch, place).wait()


def start(seqs, chips, batches, block, tile, x, weights, unit_weights, down, low, collective):
    rows, width = x.shape
    group = 2 * chips
    length = group * rows // batches
    share = weights[0].shape[0]
    span = width // group
    cols = 3 * span
    wide = unit_weights[0].shape[1]
    cells = 2 * wide // group
    piece = rows // batches
    padded = length + WINDOW
    half = jnp.bfloat16
    need = WINDOW // block
    return pl.pallas_call(
        functools.partial(start_kernel, seqs, chips, batches, block),
        out_shape=[
            jax.ShapeDtypeStruct((batches, length, width), half),
            jax.ShapeDtypeStruct((batches, length, span), half),
            jax.ShapeDtypeStruct((batches, length, span), half),
            jax.ShapeDtypeStruct((batches, span // HEAD, length), jnp.float32),
            jax.ShapeDtypeStruct((batches, padded, 2 * span), half),
            jax.ShapeDtypeStruct((group, seqs, 8, 128), jnp.float32),
            jax.ShapeDtypeStruct((width, cols), half),
            jax.ShapeDtypeStruct((group, share, cells), half),
            jax.ShapeDtypeStruct((seqs,) + down.shape, half),
        ],
        in_specs=[VMEM_SPEC] * 5 + [ANY_SPEC] * 3 + [VMEM_SPEC],
        out_specs=[ANY_SPEC] + [VMEM_SPEC] * 3 + [ANY_SPEC] * 5,
        scratch_shapes=[
            pltpu.VMEM((share, wide), half),
            pltpu.VMEM((share, wide), half),
            pltpu.VMEM((group, share, cells), half),
            pltpu.VMEM((group, share, cols), half),
            pltpu.VMEM((batches, group, piece, width), half),
            pltpu.VMEM((batches, length, width), half),
            pltpu.VMEM((batches, padded, 2 * span), half),
            pltpu.VMEM((span, padded), half),
            pltpu.VMEM((8, width), jnp.float32),
            pltpu.VMEM((group, seqs, 8, 128), jnp.float32),
            pltpu.VMEM((width, cols), half),
            sems(2),
            sems(batches, 3, group, PARTS // 2),
            sems(batches, group, PARTS // 2),
            sems(batches, chips),
            sems(group),
            sems(seqs, group),
            sems(seqs, group),
            sems(seqs),
            sems(group),
            sems(seqs),
            sems(group),
            pltpu.SemaphoreType.DMA,
            pltpu.SemaphoreType.DMA,
            sems(batches, need),
            sems(batches, need),
            sems(batches),
            sems(group),
            sems(group),
            pltpu.SemaphoreType.DMA,
            sems(seqs, 2, 1),
            sems(seqs, 2, 1),
            pltpu.SemaphoreType.DMA,
        ],
        compiler_params=comm_params(collective, 62),
        cost_estimate=cost(
            2 * group * rows * width * cols + 8 * batches * length * span * (WINDOW + block),
            300 * MIB,
            2 * group * rows * width * 2,
        ),
        name="start",
    )(tile, x, *weights, *unit_weights, down, low)


def branch_kernel(
    seqs, chips, a_ref, w_ref, d_ref, units_ref, x_ref, gain_ref,
    middle_ref, normed_ref, gd_ref, w_units_ref,
    out_ref, acc, cross_out, line_out, cross_in, line_in, sum_send, sum_recv,
    send, recv, d_keep, share_send, share_recv, share_keep,
):
    line = Line(chips)
    rows = out_ref.shape[0]

    def product(slot, tile):
        return dot_nn(left_rows(a_ref, slot, rows), w_ref[:, rows_at(tile, TILE)])

    meet(line.greet() + greet_seq(seqs))
    reduce = Reduce(
        line, product, out_ref, acc, cross_out, line_out, cross_in, line_in, sum_send, sum_recv
    )
    spread = Spread(line, d_ref, gd_ref, send, recv)
    units = Share(seqs, units_ref, w_units_ref, share_send, share_recv, share_keep)
    d_kept = pltpu.make_async_copy(d_ref, gd_ref.at[line.own], d_keep)
    units.begin()
    spread.begin()
    d_kept.start()

    @pl.loop(0, chips)
    def _(step):
        def also(tile):
            pl.when(step < chips - 1)(lambda: spread.relay_part(step + 1, tile))

        reduce.level(chips - 1 - step, also)

        pl.when(step == chips // 2)(lambda: units.pass_on(range(units.parts)))

    @pl.loop(0, rows // 32)
    def _(chunk):
        here = rows_at(chunk, 32)
        middle = x_ref[here, :].astype(jnp.float32) + out_ref[here, :]
        middle_ref[here, :] = middle
        normed_ref[here, :] = to_half(normalize(middle, gain_ref[0:1, :]))

    spread.rest()
    spread.sent()
    reduce.sent()
    d_kept.wait()
    units.end()


def branch_sum(seqs, chips, a, w, d_rows, units, x, gain, collective):
    rows, width = d_rows.shape
    group = 2 * chips
    half = jnp.bfloat16
    return pl.pallas_call(
        functools.partial(branch_kernel, seqs, chips),
        out_shape=[
            jax.ShapeDtypeStruct((rows, width), jnp.float32),
            jax.ShapeDtypeStruct((rows, width), half),
            jax.ShapeDtypeStruct((group, rows, width), half),
            jax.ShapeDtypeStruct((seqs,) + units.shape, half),
        ],
        in_specs=[VMEM_SPEC, VMEM_SPEC] + [ANY_SPEC] * 2 + [VMEM_SPEC, VMEM_SPEC],
        out_specs=[VMEM_SPEC, VMEM_SPEC] + [ANY_SPEC] * 2,
        scratch_shapes=[pltpu.VMEM((rows, width), jnp.float32)]
        + Reduce.scratch(chips, rows, width)
        + [sems(3, group, PARTS), sems(group, PARTS), pltpu.SemaphoreType.DMA]
        + [sems(seqs, 2, 1), sems(seqs, 2, 1), pltpu.SemaphoreType.DMA],
        compiler_params=comm_params(collective),
        cost_estimate=cost(
            2 * group * rows * width * w.shape[0], 250 * MIB, 3 * group * rows * width * 2
        ),
        name="branch_sum",
    )(a, w, d_rows, units, x, gain)


class PairReduce:
    def __init__(self, line, product, out, acc, keep, cross_out, cross_in, line_out, line_in, send, recv):
        self.line, self.product, self.out, self.acc, self.keep = line, product, out, acc, keep
        self.cross_out, self.cross_in, self.line_out, self.line_in = cross_out, cross_in, line_out, line_in
        self.send, self.recv = send, recv
        self.tiles = keep.shape[1] // TILE

    @staticmethod
    def scratch(chips, piece, width):
        half = jnp.bfloat16
        return [
            pltpu.VMEM((piece, width), half),
            pltpu.VMEM((2, piece, width), half),
            pltpu.VMEM((2, piece, width), half),
            pltpu.VMEM((chips + 1, piece, width), half),
            pltpu.SemaphoreType.DMA((3, width // TILE)),
            pltpu.SemaphoreType.DMA((chips + 3, width // TILE)),
        ]

    def cross(self, parity, tile):
        here = rows_at(tile, TILE)
        return pltpu.make_async_remote_copy(
            src_ref=self.cross_out.at[:, here],
            dst_ref=self.cross_in.at[parity, :, here],
            send_sem=self.send.at[0, tile],
            recv_sem=self.recv.at[self.line.chips + 1 + parity, tile],
            device_id={"fsdp": self.line.other},
            device_id_type=MESH,
        )

    def along(self, parity, landing, tile, peer):
        here = rows_at(tile, TILE)
        return pltpu.make_async_remote_copy(
            src_ref=self.line_out.at[parity, :, here],
            dst_ref=self.line_in.at[landing, :, here],
            send_sem=self.send.at[1 + parity, tile],
            recv_sem=self.recv.at[landing, tile],
            device_id={"fsdp": peer},
            device_id_type=MESH,
        )

    def steps(self):
        return 2 * self.line.chips - 1

    def step(self, step):
        line, keep = self.line, self.keep
        piece = keep.shape[0]
        right_side = line.chips - 1 - line.chip
        away = line.chips - 1 - step // 2
        second = lax.rem(step, 2)
        rightward = (right_side >= line.chip) == (second == 0)
        place = line.chip + jnp.where(rightward, away, -away)
        longer = jnp.maximum(right_side, line.chip)
        shorter = jnp.minimum(right_side, line.chip)
        count = longer - away + jnp.maximum(shorter - away, 0) + second
        parity = lax.rem(count + 2 * line.chips, 2)
        upstream = (rightward & line.has_left) | (jnp.logical_not(rightward) & line.has_right)

        @pl.when((place >= 0) & (place < line.chips))
        def _():
            wide = self.acc.shape[1]

            @pl.loop(0, keep.shape[1] // wide)
            def _(tile):
                here = rows_at(tile, wide)
                self.acc[...] = self.product(place, here)
                self.cross_out[:, here] = to_half(self.acc[rows_at(1 - line.core, piece), :])
                keep[:, here] = self.acc[rows_at(line.core, piece), :]
                for piece_of in range(wide // TILE):
                    self.cross(parity, tile * (wide // TILE) + piece_of).start()

            @pl.loop(0, self.tiles)
            def _(tile):
                here = rows_at(tile, TILE)
                self.cross(parity, tile).wait()
                keep[:, here] += self.cross_in[parity, :, here].astype(jnp.float32)

                @pl.when(away > 0)
                def _():
                    pl.when(count >= 2)(
                        lambda: self.along(parity, place, tile, line.own).wait_send()
                    )

                    @pl.when(upstream)
                    def _():
                        self.along(parity, place, tile, line.own).wait_recv()
                        self.line_out[parity, :, here] = to_half(
                            keep[:, here] + self.line_in[place, :, here].astype(jnp.float32)
                        )

                    @pl.when(jnp.logical_not(upstream))
                    def _():
                        self.line_out[parity, :, here] = to_half(keep[:, here])

                    @pl.when(rightward)
                    def _():
                        self.along(parity, place, tile, line.own + 2).start()

                    @pl.when(jnp.logical_not(rightward))
                    def _():
                        landing = jnp.where(away == 1, line.chips, place)
                        self.along(parity, landing, tile, line.own - 2).start()

                @pl.when(away == 0)
                def _():
                    self.out[:, here] = keep[:, here]

                    @pl.when(line.has_left)
                    def _():
                        self.along(parity, place, tile, line.own).wait_recv()
                        self.out[:, here] += self.line_in[place, :, here].astype(jnp.float32)

                    @pl.when(line.has_right)
                    def _():
                        self.along(parity, line.chips, tile, line.own).wait_recv()
                        self.out[:, here] += self.line_in[line.chips, :, here].astype(jnp.float32)

    def sent(self):
        for count in range(max(self.line.chips - 3, 0), self.line.chips - 1):
            pl.loop(0, self.tiles)(
                lambda tile, parity=count % 2: self.along(parity, 0, tile, self.line.own).wait_send()
            )


def feed_kernel(
    seqs, chips, batches, x_ref, w_hbm, wd_hbm, gd_hbm, v_ref, cot_ref, gain_ref,
    dm_ref, db_ref, gain_grad_ref, hidden_hbm, grad_hbm, grad_in,
    buf, d_buf, h_buf, w_ref, wd_ref, d_ref, tiles, totals, acc, keep,
    load, d_sem, h_sem, tile_sem, send, recv, part_send, part_recv, wd_load, *sums,
):
    line = Line(chips)
    rows, width = x_ref.shape
    piece = rows // batches
    pair = 2 * piece
    units = wd_ref.shape[0]
    part = min(units, 2 * TILE)
    block = tiles.shape[1]
    loads = [
        pltpu.make_async_copy(w_hbm, w_ref, load.at[0]),
        pltpu.make_async_copy(wd_hbm, wd_ref, wd_load),
    ]
    for item in loads:
        item.start()
    meet(line.greet() + greet_seq(seqs))
    spreads = [
        Spread(
            line,
            x_ref.at[pl.ds(batch * piece, piece)],
            buf.at[batch],
            send.at[batch],
            recv.at[batch],
        )
        for batch in range(batches)
    ]
    spreads[0].begin()
    for batch in range(batches):
        buf[batch, line.own] = x_ref[batch * piece : (batch + 1) * piece, :]

    def fetch(batch, place, side):
        return [
            pltpu.make_async_copy(
                gd_hbm.at[place * 2 + core, pl.ds(batch * piece, piece)],
                d_buf.at[side, pl.ds(core * piece, piece)],
                d_sem.at[side, core],
            )
            for core in range(2)
        ]

    def stored(batch, place):
        return [
            pltpu.make_async_copy(
                h_buf.at[pl.ds(core * piece, piece)],
                hidden_hbm.at[
                    pl.ds(pl.multiple_of((place * 2 + core) * rows + batch * piece, piece), piece)
                ],
                h_sem.at[core],
            )
            for core in range(2)
        ]

    def sides(far, act):
        @pl.loop(0, 2)
        def _(side):
            place = line.chip + far * (2 * side - 1)
            valid = (place >= 0) & (place < chips) & ((side == 0) | (far > 0))
            pl.when(valid)(lambda: act(place, side))

    def take(batch, far):
        def begin(place, side):
            for item in fetch(batch, place, side):
                item.start()

        sides(far, begin)
        pl.when(far > 0)(lambda: spreads[batch].relay(far))

    def compute(batch, far):
        def act(place, side):
            spreads[batch].across(place * 2 + 1 - line.core)
            for item in fetch(batch, place, side):
                item.wait()

            def free():
                for item in stored(batch, place):
                    item.wait()

            if batch:
                free()
            else:
                pl.when((far > 0) | (side > 0))(free)
            there = rows_at(place, pair)

            @pl.loop(0, units // part)
            def _(tile):
                first = rows_at(tile, part)
                second = rows_at(units // part + tile, part)
                values = buf[batch, pl.ds(place * 2, 2), :, :].reshape(pair, width)
                gate = dot_nn(values, w_ref[:, first])
                up = dot_nn(values, w_ref[:, second])
                d_hidden = dot_nt(d_buf[side], wd_ref[first, :])
                sigma = jax.nn.sigmoid(gate)
                swish = gate * sigma
                h_buf[:, first] = to_half(swish * up)
                slope = sigma * (1.0 + gate * (1.0 - sigma))
                d_ref[batch, there, first] = to_half(d_hidden * up * slope)
                d_ref[batch, there, second] = to_half(d_hidden * swish)

            for item in stored(batch, place):
                item.start()

        sides(far, act)

    def product(batch):
        def get(place, here):
            return dot_nt(d_ref[batch, rows_at(place, pair), :], w_ref[here, :])

        return get

    reduces = [
        PairReduce(line, product(batch), totals.at[batch], acc, keep, *sums[6 * batch : 6 * batch + 6])
        for batch in range(batches)
    ]

    count = width // block
    seq = lax.axis_index("seq")

    near, far_off = seq_peers(seqs)
    soon = len(near)
    order = [peer * 2 for peer in near] + [peer * 2 for peer in far_off] + [seq * 2]
    order = order + [peer * 2 + 1 for peer in near] + [peer * 2 + 1 for peer in far_off] + [seq * 2 + 1]

    def tile_at(turn):
        tile = order[-1]
        for index in range(len(order) - 1):
            tile = jnp.where(turn == index, order[index], tile)
        return tile

    def grad_stored(turn):
        slot = lax.rem(turn, 2)
        return pltpu.make_async_copy(
            tiles.at[slot], grad_hbm.at[rows_at(tile_at(turn), block)], tile_sem.at[slot]
        )

    parts = ToPeers(seqs, near, grad_hbm, grad_in, part_send, part_recv)

    def leave(turn):
        grad_stored(turn).wait()
        for index in range(soon):
            pl.when(turn == index)(lambda index=index: parts.move(index).start())

    def weight_grad(turn):
        slot = lax.rem(turn, 2)
        size = min(4 * TILE, 2 * units)
        tile = tile_at(turn)

        @pl.loop(0, 2 * units // size)
        def _(column):
            here = rows_at(column, size)
            got = 0.0
            for batch in range(batches):
                left = buf[batch, :, :, rows_at(tile, block)].reshape(2 * chips * piece, block)
                got = got + contract_rows(left, d_ref[batch, :, here])
            tiles[slot, :, here] = to_half(got)

        pl.when(turn > 0)(lambda: leave(turn - 1))
        grad_stored(turn).start()

    def norm_batch(batch):
        own = pl.ds(batch * piece, piece)

        def put(here, d_values):
            there = pl.ds(pl.multiple_of(here.start + batch * piece, here.size), here.size)
            d_middle = cot_ref[there, :].astype(jnp.float32) + d_values
            dm_ref[there, :] = d_middle
            db_ref[there, :] = to_half(d_middle)

        norm_back(piece, v_ref.at[own], totals.at[batch], gain_ref, gain_grad_ref, put)

    gain_grad_ref[...] = jnp.zeros_like(gain_grad_ref)
    for item in loads:
        item.wait()
    last = 2 * chips - 2

    @pl.loop(0, chips)
    def _(far):
        take(0, far)
        pl.when(far == chips - 2)(spreads[1].begin)
        compute(0, far)

    @pl.loop(0, chips - 1)
    def _(far):
        take(1, far)
        reduces[0].step(2 * far)
        reduces[0].step(2 * far + 1)
        compute(1, far)

    take(1, chips - 1)
    compute(1, chips - 1)

    @pl.loop(0, 2)
    def _(step):
        reduces[1].step(step)
        weight_grad(step)

    reduces[0].step(last)
    norm_batch(0)

    @pl.loop(2, last)
    def _(step):
        reduces[1].step(step)
        pl.when(step < count)(lambda: weight_grad(step))

    @pl.loop(last, max(count, last))
    def _(tile):
        weight_grad(tile)

    reduces[1].step(last)
    norm_batch(1)
    for batch in range(batches):
        spreads[batch].sent()
        reduces[batch].sent()
    for item in stored(1, 0):
        item.wait()
    leave(count - 1)
    parts.end()


def feed_forward(seqs, chips, batches, x, w, wd, group_d, middle, cot, gain, collective):
    rows, width = x.shape
    group = 2 * chips
    units = w.shape[1] // 2
    piece = rows // batches
    block = width // seqs // 2
    half = jnp.bfloat16
    return pl.pallas_call(
        functools.partial(feed_kernel, seqs, chips, batches),
        out_shape=[
            jax.ShapeDtypeStruct((rows, width), jnp.float32),
            jax.ShapeDtypeStruct((rows, width), half),
            jax.ShapeDtypeStruct((8, width), jnp.float32),
            jax.ShapeDtypeStruct((group * rows, units), half),
            jax.ShapeDtypeStruct((width, 2 * units), half),
            jax.ShapeDtypeStruct((near_count(seqs), block, 2 * units), half),
        ],
        in_specs=[VMEM_SPEC] + [ANY_SPEC] * 3 + [VMEM_SPEC] * 3,
        out_specs=[VMEM_SPEC] * 3 + [ANY_SPEC] * 3,
        scratch_shapes=[
            pltpu.VMEM((batches, group, piece, width), half),
            pltpu.VMEM((2, 2 * piece, width), half),
            pltpu.VMEM((2 * piece, units), half),
            pltpu.VMEM(w.shape, half),
            pltpu.VMEM((units, width), half),
            pltpu.VMEM((batches, group * piece, 2 * units), half),
            pltpu.VMEM((2, block, 2 * units), half),
            pltpu.VMEM((batches, piece, width), jnp.float32),
            pltpu.VMEM((2 * piece, 2 * TILE), jnp.float32),
            pltpu.VMEM((piece, width), jnp.float32),
            sems(2),
            sems(2, 2),
            sems(2),
            sems(2),
            sems(batches, 3, group, PARTS // 2),
            sems(batches, group, PARTS // 2),
            sems(seqs),
            sems(seqs),
            pltpu.SemaphoreType.DMA,
        ]
        + PairReduce.scratch(chips, piece, width) * batches,
        compiler_params=comm_params(collective, 63),
        cost_estimate=cost(
            14 * group * rows * width * units, 400 * MIB, 2 * group * rows * width * 2
        ),
        name="feed_forward",
    )(x, w, wd, group_d, middle, cot, gain)


def branch_back_kernel(
    seqs, chips, batches, x_ref, w_ref, att_ref, middle_ref, hidden_hbm, wd_hbm, units_hbm, gd_hbm,
    d_ref, layer_ref, out_grad_ref, half_in, whole_in, down_hbm, down_in,
    out_ref, buf, hidden_ref, wd_ref, grad_acc, rights, tiles, send, recv, load, right_sem, tile_sem,
    part_send, part_recv, wd_load, down_send, down_recv, down_keep, acc, cross_out, line_out, cross_in, line_in, sum_send, sum_recv,
):
    line = Line(chips)
    rows = x_ref.shape[0]
    piece = rows // batches
    width = x_ref.shape[1]
    loads = [
        pltpu.make_async_copy(hidden_hbm, hidden_ref, load.at[0]),
        pltpu.make_async_copy(wd_hbm, wd_ref, wd_load),
    ]
    for item in loads:
        item.start()

    def product(slot, tile):
        return dot_nn(left_rows(hidden_ref, slot, rows), wd_ref[:, rows_at(tile, TILE)])

    part = rights.shape[2]
    count = width // part

    def right(tile):
        slot = lax.rem(tile, 2)
        return pltpu.make_async_copy(
            gd_hbm.at[:, rows_at(tile, part)], rights.at[slot], right_sem.at[slot]
        )

    def stored(tile):
        slot = lax.rem(tile, 2)
        return pltpu.make_async_copy(
            tiles.at[slot], down_hbm.at[:, rows_at(tile, part)], tile_sem.at[slot]
        )

    def weight_grad(tile):
        right(tile).wait()
        pl.when(tile + 1 < count)(lambda: right(tile + 1).start())
        pl.when(tile >= 2)(lambda: stored(tile - 2).wait())
        slot = lax.rem(tile, 2)
        size = min(TILE, hidden_ref.shape[1])

        @pl.loop(0, hidden_ref.shape[1] // size)
        def _(row):
            here = rows_at(row, size)
            tiles[slot, here, :] = to_half(contract_rows(hidden_ref[:, here], rights[slot]))

        stored(tile).start()

    right(0).start()
    meet(line.greet() + greet_seq(seqs))
    near, far_off = seq_peers(seqs)
    soon = len(near)
    halves = ToPeers(
        seqs, near, units_hbm, half_in, part_send.at[0], part_recv.at[0], half_in.shape[1]
    )
    wholes = ToPeers(seqs, far_off, units_hbm, whole_in, part_send.at[1], part_recv.at[1])
    down = ToPeers(
        seqs, near, down_hbm, down_in.at[pl.ds(0, soon)], down_send, down_recv
    )
    down_kept = pltpu.make_async_copy(
        down_hbm.at[rows_at(lax.axis_index("seq"), down_in.shape[1])], down_in.at[soon], down_keep
    )
    spread = Spread(line, x_ref, buf, send, recv)
    reduce = Reduce(
        line, product, out_ref, acc, cross_out, line_out, cross_in, line_in, sum_send, sum_recv
    )
    spread.begin()
    halves.begin()
    wholes.begin()
    buf[line.own] = x_ref[...]
    grad_acc[...] = jnp.zeros_like(grad_acc)

    def use(slot):
        got = to_half(dot_nt(buf[slot], w_ref[...]))
        for batch in range(batches):
            d_ref[batch, rows_at(slot, piece), :] = got[batch * piece : (batch + 1) * piece]
        mixed = left_rows(att_ref, slot, rows)

        @pl.loop(0, width // TILE)
        def _(tile):
            here = rows_at(tile, TILE)
            grad_acc[:, here] += contract_rows(mixed, buf[slot, :, here])

    for item in loads:
        item.wait()

    reduce.level(chips - 1, lambda tile: None)
    pl.loop(0, count)(weight_grad)
    stored(count - 2).wait()
    stored(count - 1).wait()
    down.begin()
    down_kept.start()
    spread.relay(1)
    spread.each(0, use)

    @pl.loop(1, chips)
    def _(step):
        def also(tile):
            pl.when(step < chips - 1)(lambda: spread.relay_part(step + 1, tile))

        reduce.level(chips - 1 - step, also)
        spread.each(step, use)

    spread.each(chips, use)

    @pl.loop(0, rows // 32)
    def _(chunk):
        here = rows_at(chunk, 32)
        layer_ref[here, :] = to_half(middle_ref[here, :] + out_ref[here, :])

    out_grad_ref[...] = to_half(grad_acc[...])
    spread.sent()
    reduce.sent()
    halves.end()
    wholes.end()
    down.end()
    down_kept.wait()


def branch_back(seqs, chips, batches, x, w, attended, middle, hidden, wd, unit_part, group_d, collective):
    rows, width = x.shape
    group = 2 * chips
    length = group * rows // batches
    span = w.shape[0]
    half = jnp.bfloat16
    part = 256 if group * rows <= 2048 else 128
    near, run = near_count(seqs), width // seqs
    units = hidden.shape[1]
    return pl.pallas_call(
        functools.partial(branch_back_kernel, seqs, chips, batches),
        out_shape=[
            jax.ShapeDtypeStruct((batches, length, span), half),
            jax.ShapeDtypeStruct((rows, width), half),
            jax.ShapeDtypeStruct((span, width), half),
            jax.ShapeDtypeStruct((near, run // 2, unit_part.shape[1]), half),
            jax.ShapeDtypeStruct((seqs - 1 - near, run, unit_part.shape[1]), half),
            jax.ShapeDtypeStruct((units, width), half),
            jax.ShapeDtypeStruct((near + 1, units // seqs, width), half),
        ],
        in_specs=[VMEM_SPEC] * 4 + [ANY_SPEC] * 4,
        out_specs=[VMEM_SPEC, VMEM_SPEC, VMEM_SPEC, ANY_SPEC, ANY_SPEC, ANY_SPEC, ANY_SPEC],
        scratch_shapes=[
            pltpu.VMEM((rows, width), jnp.float32),
            pltpu.VMEM((group, rows, width), half),
            pltpu.VMEM(hidden.shape, half),
            pltpu.VMEM((units, width), half),
            pltpu.VMEM((span, width), jnp.float32),
            pltpu.VMEM((2, group * rows, part), half),
            pltpu.VMEM((2, units, part), half),
            sems(3, group, PARTS),
            sems(group, PARTS),
            sems(2),
            sems(2),
            sems(2),
            sems(2, seqs),
            sems(2, seqs),
            pltpu.SemaphoreType.DMA,
            sems(seqs),
            sems(seqs),
            pltpu.SemaphoreType.DMA,
        ]
        + Reduce.scratch(chips, rows, width),
        compiler_params=comm_params(collective, 62),
        cost_estimate=cost(
            2 * group * rows * width * (2 * span + 2 * units),
            250 * MIB,
            2 * group * rows * width * 2,
        ),
        name="branch_back",
    )(x, w, attended, middle, hidden, wd, unit_part, group_d.reshape(group * rows, width))


def attention_back_kernel(
    seqs, chips, block, q_ref, pad_ref, low_ref, lse_ref, d_ref, part_hbm, in_one, in_two, in_far,
    w_ref, g_hbm, v_ref, dm_hbm, gain_ref, mlp_gain_ref, out_ref, down_hbm,
    grad_hbm, wq_ref, wk_ref, wv_ref, wo_hbm, tile_ref, gate_hbm, up_hbm, down_in,
    grad_ref, wo_ref, gate_ref, up_ref, result_sem, down_send, down_recv,
    dk, dv, kt, heads, back_out, back_in, unit_parts, unit_sums, units, lefts, parts, sums, cols, out_in,
    totals, gain_acc, gain_out, gain_in, gain_sum, gain_back, acc, keep,
    halo_send, halo_recv, unit_load, unit_send, unit_recv, unit_keep, dm_load, left_sem,
    part_send, part_recv, cols_send, cols_recv, out_send, out_recv,
    gain_send, gain_recv, back_send, back_recv, *line_sums,
):
    line = Line(chips)
    group = 2 * chips
    seq = lax.axis_index("seq")
    own = line.own
    batches, length, span = q_ref.shape
    rows, width = v_ref.shape
    piece = rows // batches
    pair_rows = 2 * piece
    depth = 3 * span
    run = width // seqs
    share = run // group
    part = lefts.shape[3]
    steps, need = length // block, WINDOW // block
    first = length - WINDOW
    has_left, has_right = seq > 0, seq < seqs - 1
    scale = jnp.asarray(HEAD**-0.5, jnp.bfloat16)

    def others(count, me, act):
        pl.loop(1, count)(lambda ahead: act(lax.rem(me + ahead, count)))

    def unit_loaded(turn, place, source):
        slot = lax.rem(turn, 2)
        return pltpu.make_async_copy(source, unit_parts.at[slot, place], unit_load.at[slot, place])

    def load_units(turn):
        member = lax.rem(own + turn, group)
        unit_loaded(turn, 0, part_hbm.at[rows_at(seq * group + member, share)]).start()
        soon = in_one.shape[0]
        for index in range(seqs - 1):

            def fetch(source, index=index):
                unit_loaded(turn, index + 1, source).start()

            if index < soon:

                @pl.when(member < chips)
                def _(index=index, fetch=fetch):
                    fetch(in_one.at[index, rows_at(member, share)])

                @pl.when(member >= chips)
                def _(index=index, fetch=fetch):
                    fetch(in_two.at[index, rows_at(member - chips, share)])

            else:
                fetch(in_far.at[index - soon, rows_at(member, share)])

    load_units(1)
    dm_loaded = pltpu.make_async_copy(dm_hbm, grad_ref, dm_load)
    dm_loaded.start()
    meet(greet_group(group) + greet_seq(seqs))
    near, far_off = seq_peers(seqs)
    down = ToPeers(seqs, far_off, down_hbm, down_in, down_send, down_recv)
    down.begin()
    swap = Swap(group, unit_sums, units, unit_send, unit_recv, unit_keep)

    @pl.loop(1, group + 1)
    def _(turn):
        member = lax.rem(own + turn, group)
        slot = lax.rem(turn, 2)
        pl.when(turn < group)(lambda: load_units(turn + 1))
        for place in range(seqs):
            unit_loaded(turn, place, part_hbm.at[rows_at(0, share)]).wait()

        @pl.loop(0, share // 16)
        def _(chunk):
            here = rows_at(chunk, 16)
            added = unit_parts[slot, 0, here, :].astype(jnp.float32)
            for place in range(1, seqs):
                added = added + unit_parts[slot, place, here, :].astype(jnp.float32)
            unit_sums[member, here, :] = to_half(added)

        pl.when(turn < group)(lambda: swap.move(member, own).start())
        pl.when(turn == group)(lambda: swap.kept().start())

    def halo(batch, step, peer):
        here = rows_at(step, block)
        return pltpu.make_async_remote_copy(
            src_ref=back_out.at[batch, here],
            dst_ref=back_in.at[batch, here],
            send_sem=halo_send.at[batch, step],
            recv_sem=halo_recv.at[batch, step],
            device_id={"seq": peer},
            device_id_type=MESH,
        )

    def attend_block(batch, step):
        begin = pl.multiple_of(step * block, block)
        keys = pl.ds(begin, block + WINDOW)
        rows = pl.ds(begin, block)
        low = low_ref[batch, :, rows]
        for pair in range(span // PAIR):
            lanes = slice(pair * PAIR, (pair + 1) * PAIR)
            q_pair = q_ref[batch, rows, lanes] * scale
            d_pair = d_ref[batch, rows, lanes]
            k_rows = pad_ref[batch, keys, lanes]
            v_rows = pad_ref[batch, keys, span + pair * PAIR : span + (pair + 1) * PAIR]
            k_cols = kt[lanes, keys]
            back = []
            for half in range(2):
                row = pair * 2 + half
                q_head = head_lanes(q_pair, half)
                d_head = head_lanes(d_pair, half)
                scores = masked_scores(k_rows, q_head, low)
                probs = jnp.exp(scores - lse_ref[batch, row : row + 1, rows])
                d_probs = dot_nt(v_rows, d_head)
                along = jnp.sum(probs * d_probs, axis=0, keepdims=True)
                d_scores = to_half(probs * (d_probs - along))
                dv[keys, lanes] += dot_nn(to_half(probs), d_head)
                dk[keys, lanes] += dot_nn(d_scores, q_head)
                back.append(dot_nn(k_cols, d_scores))
            at = lax.broadcasted_iota(jnp.int32, back[0].shape, 0)
            heads[batch, rows, lanes] = to_half(
                jnp.where(at < HEAD, back[0], back[1]).T
            )


        @pl.when(has_left & (step < need))
        def _():
            back_out[batch, rows, :span] = to_half(dk[rows, :])
            back_out[batch, rows, span:] = to_half(dv[rows, :])
            halo(batch, step, seq - 1).start()

        @pl.when(step == steps - 1)
        def _():
            heads[batch, :, span : 2 * span] = to_half(dk[WINDOW:, :])
            heads[batch, :, 2 * span :] = to_half(dv[WINDOW:, :])

    def add_halo(batch):
        @pl.when(has_right)
        def _():
            @pl.loop(0, need)
            def _(step):
                there = pl.ds(pl.multiple_of(step * block + first, block), block)
                halo(batch, step, seq).wait_recv()
                got = back_in[batch, rows_at(step, block), :].astype(jnp.float32)
                mine = heads[batch, there, span:].astype(jnp.float32)
                heads[batch, there, span:] = to_half(mine + got)

    def product(batch):
        def get(place, here):
            return dot_nt(heads[batch, rows_at(place, pair_rows), :], w_ref[here, :])

        return get

    reduces = [
        PairReduce(
            line, product(batch), totals.at[batch], acc, keep, *line_sums[6 * batch : 6 * batch + 6]
        )
        for batch in range(batches)
    ]
    last = 2 * chips - 2

    @pl.loop(0, 2 * steps)
    def _(turn):
        batch, step = turn // steps, lax.rem(turn, steps)

        @pl.when(step == 0)
        def _():
            kt[...] = pad_ref[batch, :, :span].T * scale
            dk[...] = jnp.zeros_like(dk)
            dv[...] = jnp.zeros_like(dv)

        attend_block(batch, step)
        after = turn - steps - 1
        pl.when(after == 0)(lambda: add_halo(0))

        @pl.when((after >= 0) & (2 * after < last))
        def _():
            reduces[0].step(2 * after)
            reduces[0].step(2 * after + 1)

    for after in range(steps - 1, chips - 1):
        reduces[0].step(2 * after)
        reduces[0].step(2 * after + 1)

    def left(tile):
        slot = lax.rem(tile, 2)
        return pltpu.make_async_copy(
            g_hbm.at[:, :, rows_at(tile, part)], lefts.at[slot], left_sem.at[slot]
        )

    heads_near = ToPeers(seqs, near + far_off, parts, sums, part_send, part_recv)
    left(0).start()
    add_halo(1)

    @pl.loop(0, width // part)
    def _(tile):
        left(tile).wait()
        pl.when(tile + 1 < width // part)(lambda: left(tile + 1).start())
        slot = lax.rem(tile, 2)
        got = contract_rows(lefts[slot, 0], heads[0])
        for batch in range(1, batches):
            got = got + contract_rows(lefts[slot, batch], heads[batch])
        parts[rows_at(tile, part), :] = to_half(got)

    heads_near.begin()
    from_seq = ToPeers(seqs, near + far_off, out_ref, out_in, out_send, out_recv)
    from_seq.begin()
    gain_acc[...] = jnp.zeros_like(gain_acc)
    dm_loaded.wait()

    def norm_batch(batch):
        mine = pl.ds(batch * piece, piece)

        def put(here, d_values):
            there = pl.ds(pl.multiple_of(here.start + batch * piece, here.size), here.size)
            grad_ref[there, :] += d_values

        norm_back(piece, v_ref.at[mine], totals.at[batch], gain_ref, gain_acc, put)

    pl.loop(0, 2)(reduces[1].step)
    reduces[0].step(last)
    norm_batch(0)
    pl.loop(2, last)(reduces[1].step)
    swap.end()
    cell = units.shape[2] // 2 // seqs
    for member in range(group):
        for place in range(seqs):
            column = (place * group + member) * cell
            for target, begin in ((gate_ref, 0), (up_ref, seqs * cell)):
                here = slice(begin + place * cell, begin + (place + 1) * cell)
                target[:, column : column + cell] = units[member, :, here]

    results = [
        pltpu.make_async_copy(source, target, result_sem.at[index])
        for index, (source, target) in enumerate(
            ((gate_ref, gate_hbm), (up_ref, up_hbm), (wo_ref, wo_hbm), (grad_ref, grad_hbm))
        )
    ]
    results[0].start()
    results[1].start()

    def block_swap(peer, member):
        return pltpu.make_async_remote_copy(
            src_ref=parts.at[rows_at(seq * group + peer, share)],
            dst_ref=cols.at[member],
            send_sem=cols_send.at[peer],
            recv_sem=cols_recv.at[member],
            device_id={"fsdp": peer},
            device_id_type=MESH,
        )

    heads_near.arrived()

    @pl.loop(0, run // 64)
    def _(chunk):
        here = rows_at(chunk, 64)
        there = pl.ds(pl.multiple_of(seq * run + chunk * 64, 64), 64)
        parts[there, :] = to_half(add_from_seq(parts[there, :], sums, here))

    others(group, own, lambda peer: block_swap(peer, own).start())
    cols[own] = parts[rows_at(seq * group + own, share), :]
    from_seq.arrived()
    out_rows = out_in.shape[1]
    wo_ref[...] = add_from_seq(out_ref[rows_at(seq, out_rows), :], out_in, slice(None))
    results[2].start()
    reduces[1].step(last)
    norm_batch(1)
    results[3].start()
    fold = 128 // share
    near = group // fold
    attn_row = jnp.sum(gain_acc[...], axis=0, keepdims=True)
    mlp_row = jnp.sum(mlp_gain_ref[...], axis=0, keepdims=True)
    gain_out[...] = jnp.zeros_like(gain_out)
    for place in range(width // 128):
        lanes = slice(place * 128, (place + 1) * 128)
        gain_out[place % near, place // near, 0:1, :] = attn_row[:, lanes]
        gain_out[place % near, place // near, 1:2, :] = mlp_row[:, lanes]

    def gain_group(peer, member):
        return pltpu.make_async_remote_copy(
            src_ref=gain_out.at[peer // fold],
            dst_ref=gain_in.at[member],
            send_sem=gain_send.at[peer],
            recv_sem=gain_recv.at[member],
            device_id={"fsdp": peer},
            device_id_type=MESH,
        )

    def gain_seq(peer, place):
        return pltpu.make_async_remote_copy(
            src_ref=gain_sum.at[peer],
            dst_ref=gain_back.at[place],
            send_sem=back_send.at[peer],
            recv_sem=back_recv.at[place],
            device_id={"seq": peer},
            device_id_type=MESH,
        )

    others(group, own, lambda peer: gain_group(peer, own).start())
    gain_in[own] = gain_out[own // fold]
    others(group, own, lambda peer: gain_group(peer, peer).wait_recv())
    gain_sum[...] = jnp.sum(gain_in[...], axis=0)
    others(seqs, seq, lambda peer: gain_seq(peer, seq).start())
    gain_back[seq] = gain_sum[seq]
    others(seqs, seq, lambda peer: gain_seq(peer, peer).wait_recv())
    tile_ref[...] = jnp.sum(gain_back[...], axis=0)
    others(group, own, lambda peer: block_swap(peer, peer).wait_recv())
    for index, target in enumerate((wq_ref, wk_ref, wv_ref)):
        for member, first, home, size in column_parts(seqs, group, share, span):
            first = first + index * span
            target[:, home : home + size] = cols[member, :, first : first + size]
    from_seq.sent()
    for item in results:
        item.wait()
    for batch in range(batches):
        reduces[batch].sent()

        @pl.when(has_left)
        def _(batch=batch):
            pl.loop(0, need)(lambda step: halo(batch, step, seq).wait_send())

    heads_near.sent()
    down.end()
    others(group, own, lambda peer: gain_group(peer, own).wait_send())
    others(group, own, lambda peer: block_swap(peer, own).wait_send())
    others(seqs, seq, lambda peer: gain_seq(peer, seq).wait_send())


def attention_back(
    seqs, chips, block, query, kv_pad, low, lse, d_att, part_own, parts_one, parts_two, parts_far, w, group_a,
    x, d_middle, gain, mlp_gain, out_part, down, collective,
):
    batches, length, span = query.shape
    padded = kv_pad.shape[1]
    rows, width = x.shape
    piece = rows // batches
    group = 2 * chips
    depth = w.shape[1]
    run = width // seqs
    share = run // group
    near = group // (128 // share)
    cells = part_own.shape[1]
    out_rows = out_part.shape[0] // seqs
    half, wide = jnp.bfloat16, jnp.float32
    part = 256 if batches * length <= 2048 else 128
    return pl.pallas_call(
        functools.partial(attention_back_kernel, seqs, chips, block),
        out_shape=[
            jax.ShapeDtypeStruct((rows, width), wide),
            jax.ShapeDtypeStruct((share, width), half),
            jax.ShapeDtypeStruct((share, width), half),
            jax.ShapeDtypeStruct((share, width), half),
            jax.ShapeDtypeStruct((out_rows, width), wide),
            jax.ShapeDtypeStruct((8, 128), wide),
            jax.ShapeDtypeStruct((share, cells // 2 * group), half),
            jax.ShapeDtypeStruct((share, cells // 2 * group), half),
            jax.ShapeDtypeStruct((seqs - 1 - near_count(seqs), down.shape[0] // seqs, width), half),
        ],
        in_specs=[VMEM_SPEC] * 5
        + [ANY_SPEC] * 4
        + [VMEM_SPEC, ANY_SPEC, VMEM_SPEC, ANY_SPEC]
        + [VMEM_SPEC] * 3
        + [ANY_SPEC],
        out_specs=[ANY_SPEC, VMEM_SPEC, VMEM_SPEC, VMEM_SPEC, ANY_SPEC, VMEM_SPEC]
        + [ANY_SPEC] * 3,
        scratch_shapes=[
            pltpu.VMEM((rows, width), wide),
            pltpu.VMEM((out_rows, width), wide),
            pltpu.VMEM((share, cells // 2 * group), half),
            pltpu.VMEM((share, cells // 2 * group), half),
            sems(4),
            sems(seqs),
            sems(seqs),
            pltpu.VMEM((padded, span), wide),
            pltpu.VMEM((padded, span), wide),
            pltpu.VMEM((span, padded), half),
            pltpu.VMEM((batches, length, depth), half),
            pltpu.VMEM((batches, WINDOW, 2 * span), half),
            pltpu.VMEM((batches, WINDOW, 2 * span), half),
            pltpu.VMEM((2, seqs, share, cells), half),
            pltpu.VMEM((group, share, cells), half),
            pltpu.VMEM((group, share, cells), half),
            pltpu.VMEM((2, batches, length, part), half),
            pltpu.VMEM((width, depth), half),
            pltpu.VMEM((seqs - 1, run, depth), half),
            pltpu.VMEM((group, share, depth), half),
            pltpu.VMEM((seqs - 1, out_rows, width), half),
            pltpu.VMEM((batches, piece, width), wide),
            pltpu.VMEM((8, width), wide),
            pltpu.VMEM((near, seqs, 8, 128), wide),
            pltpu.VMEM((group, seqs, 8, 128), wide),
            pltpu.VMEM((seqs, 8, 128), wide),
            pltpu.VMEM((seqs, 8, 128), wide),
            pltpu.VMEM((2 * piece, TILE), wide),
            pltpu.VMEM((piece, width), wide),
            sems(batches, WINDOW // block),
            sems(batches, WINDOW // block),
            sems(2, seqs),
            sems(group),
            sems(group),
            pltpu.SemaphoreType.DMA,
            pltpu.SemaphoreType.DMA,
            sems(2),
            sems(seqs),
            sems(seqs),
            sems(group),
            sems(group),
            sems(seqs),
            sems(seqs),
            sems(group),
            sems(group),
            sems(seqs),
            sems(seqs),
        ]
        + PairReduce.scratch(chips, piece, width) * batches,
        compiler_params=comm_params(collective, 63),
        cost_estimate=cost(
            20 * batches * length * span * (WINDOW + block) + 4 * group * rows * width * depth,
            400 * MIB,
            3 * group * rows * width * 2,
        ),
        name="attention_back",
    )(
        query, kv_pad, low, lse, d_att, part_own, parts_one, parts_two, parts_far, w, group_a, x,
        d_middle, gain, mlp_gain, out_part, down,
    )


def finish_kernel(count, *refs):
    sources, targets = refs[:-count], refs[-count:]
    for source, target in zip(sources, targets[:-1]):
        target[...] = source[...].astype(target.dtype)
    added = 0.0
    for source in sources[count - 1 :]:
        added = added + jnp.sum(source[...].astype(jnp.float32), axis=0)
    targets[-1][...] = added


def finish(steps, arrays, parts, kinds):
    in_specs, out_specs, out_shape = [], [], []
    for item, kind in zip(arrays + parts[:1], kinds):
        rows, width = item.shape[-2:]
        block = (rows // steps, width)
        out_specs.append(pl.BlockSpec(block, lambda i: (i, 0)))
        out_shape.append(jax.ShapeDtypeStruct((rows, width), kind))
        if item.ndim == 2:
            in_specs.append(out_specs[-1])
    for item in parts:
        in_specs.append(pl.BlockSpec((item.shape[0],) + block, lambda i: (0, i, 0)))
    return pl.pallas_call(
        functools.partial(finish_kernel, len(kinds)),
        grid=(steps,),
        in_specs=in_specs,
        out_specs=out_specs,
        out_shape=out_shape,
        compiler_params=pltpu.CompilerParams(vmem_limit_bytes=63 * MIB),
        name="finish",
    )(*arrays, *parts)


def doc_starts(lengths, positions, batches, seq_len):
    table = lengths.reshape(batches, -1, lengths.shape[1])
    starts = jnp.cumsum(table, axis=2) - table
    per_batch = seq_len // table.shape[1]
    begins = (starts + (jnp.arange(table.shape[1], dtype=jnp.int32) * per_batch)[None, :, None]).reshape(
        batches, -1
    )
    before = begins[:, None, :] <= positions[None, :, None]
    return jnp.max(jnp.where(before, begins[:, None, :], 0), axis=2)


def body(
    tokens,
    cotangent,
    lengths,
    gain_attn,
    w_query,
    w_key,
    w_value,
    w_out,
    gain_mlp,
    w_gate,
    w_up,
    w_down,
):
    batches, piece, width = tokens.shape
    seqs = lax.axis_size("seq")
    group = lax.axis_size("fsdp")
    chips = group // 2
    devices = seqs * group
    seq_len = piece * devices
    rows = batches * piece
    share = w_query.shape[0]
    span = width // group
    length = group * piece
    aligned = share == HEAD
    member = lax.axis_index("fsdp")

    x_rows = tokens.reshape(rows, width)
    cot_rows = cotangent.reshape(rows, width)
    if aligned:
        wo_part = lax.all_gather(w_out, "seq", axis=0, tiled=True)
    else:
        wo_all = lax.all_gather(w_out, ("seq", "fsdp"), axis=0, tiled=True)
        wo_part = lax.dynamic_slice_in_dim(wo_all, member * span, span, 0)

    lane = jnp.arange(128, dtype=jnp.int32)
    device = lax.axis_index("seq") * group + member
    fold = 128 // share
    here = lane // share == lax.rem(device, fold)
    both = jnp.stack([gain_attn, gain_mlp]).astype(jnp.float32)
    tile = jnp.where(here[None], jnp.tile(both, (1, fold)), 0.0)
    tile = jnp.pad(tile, ((0, 6), (0, 0)))[None]
    group_start = lax.axis_index("seq") * length
    positions = group_start + jnp.arange(length, dtype=jnp.int32)
    begins = doc_starts(lengths, positions, batches, seq_len)
    at = jnp.arange(length, dtype=jnp.int32)
    block = min(256, length)
    low = jnp.maximum(begins - group_start + WINDOW, at[None, :] + 1) - (at // block * block)[None, :]
    low = low[:, None, :]
    group_a, query, attended, lse, kv_pad, gains, w_heads, unit_own, wd_part = start(
        seqs, chips, batches, block, tile, x_rows, (w_query, w_key, w_value), (w_gate, w_up), w_down,
        low, 1,
    )
    gains = gains.transpose(1, 0, 2, 3).reshape(devices // fold, fold, 8, 128).sum(axis=1)
    gain_one = gains[:, 0].reshape(width)
    gain_two = gains[:, 1].reshape(width)
    wd_part = wd_part.reshape(-1, width)
    middle, normed_b, group_d, w_units = branch_sum(
        seqs, chips, attended, wo_part, cot_rows, unit_own.reshape(group * share, -1),
        x_rows, gain_two[None], 3,
    )
    w_units = w_units.reshape(width, -1)
    d_middle, d_branch, mlp_gain_part, hidden, unit_part, unit_one = feed_forward(
        seqs, chips, batches, normed_b, w_units, wd_part, group_d, middle, cot_rows,
        gain_two[None], 4,
    )
    d_attended, layer_out, out_part, unit_two, unit_far, down_part, down_near = branch_back(
        seqs, chips, batches, d_branch, wo_part, attended, middle, hidden, wd_part,
        unit_part, group_d, 5,
    )
    if not aligned:
        whole = lax.dynamic_update_slice_in_dim(
            jnp.zeros((width, width), jnp.bfloat16), out_part, member * span, 0
        )
        out_part = lax.psum(whole, "fsdp").reshape(seqs, group, share, width)
        out_part = lax.dynamic_slice_in_dim(out_part, member, 1, 1).reshape(seqs * share, width)
    (
        input_grad, wq_grad, wk_grad, wv_grad, wo_grad, gain_tile, gate_grad, up_grad, down_far,
    ) = attention_back(
        seqs, chips, block, query, kv_pad, low, lse, d_attended, unit_part, unit_one, unit_two,
        unit_far, w_heads, group_a, x_rows, d_middle, gain_one[None], mlp_gain_part, out_part,
        down_part, 6,
    )
    gain_grads = lax.dynamic_slice_in_dim(gain_tile[:2], lax.rem(device, fold) * share, share, 1)
    wide = jnp.float32
    (layer_out, input_grad, wq_grad, wk_grad, wv_grad, wo_grad, gate_grad, up_grad, down_grad) = finish(
        share // 16,
        [layer_out, input_grad, wq_grad, wk_grad, wv_grad, wo_grad, gate_grad, up_grad],
        [down_near, down_far],
        [jnp.bfloat16] + [wide] * 8,
    )
    return (
        layer_out.reshape(batches, piece, width),
        input_grad.reshape(batches, piece, width),
        gain_grads[0],
        wq_grad,
        wk_grad,
        wv_grad,
        wo_grad,
        gain_grads[1],
        gate_grad,
        up_grad,
        down_grad,
    )


def solution(mesh):
    spread = ("seq", "fsdp")
    tokens, rows, gains = P(None, spread, None), P(spread, None), P(spread)
    in_specs = (tokens, tokens, P(), gains, rows, rows, rows, rows, gains, rows, rows, rows)
    out_specs = (tokens, tokens, gains, rows, rows, rows, rows, gains, rows, rows, rows)
    return jax.shard_map(body, mesh=mesh, in_specs=in_specs, out_specs=out_specs, check_vma=False)
```

```python
import functools

import jax
import jax.numpy as jnp
from jax import lax
from jax.experimental import pallas as pl
from jax.experimental.pallas import tpu as pltpu
from jax.sharding import PartitionSpec as P

HEAD = 64
FF = 8192
WINDOW = 1024
PAIR = 128
TILE = 512
PARTS = 4
LOW = -1e30
EPS = 1e-05
MESH = pl.DeviceIdType.MESH
MIB = 2**20


def to_half(values):
    return values.astype(jnp.bfloat16)


def normalize(values, gain):
    return values * lax.rsqrt(jnp.mean(values * values, axis=-1, keepdims=True) + EPS) * gain


def contract_rows(left, right):
    return lax.dot_general(
        left, right, (((0,), (0,)), ((), ())), preferred_element_type=jnp.float32
    )


def dot_nt(left, right):
    return lax.dot_general(
        left, right, (((1,), (1,)), ((), ())), preferred_element_type=jnp.float32
    )


def dot_nn(left, right):
    return jnp.dot(left, right, preferred_element_type=jnp.float32)


def head_lanes(values, half):
    lane = lax.broadcasted_iota(jnp.int32, values.shape, 1)
    return jnp.where((lane >= HEAD) == (half == 1), values, jnp.zeros_like(values))


def masked_scores(k_rows, q_head, low):
    keys, block = k_rows.shape[0], q_head.shape[0]
    scores = dot_nt(k_rows, q_head)
    at = lax.broadcasted_iota(jnp.int32, (keys, block), 0)
    query = lax.broadcasted_iota(jnp.int32, (keys, block), 1)
    seen = (at >= low) & (at <= query + WINDOW)
    return jnp.where(seen, scores, LOW)


class Line:
    def __init__(self, chips):
        self.chips = chips
        self.own = lax.axis_index("fsdp")
        self.chip = self.own // 2
        self.core = lax.rem(self.own, 2)
        self.other = self.own + 1 - 2 * self.core
        self.has_left = self.chip > 0
        self.has_right = self.chip < chips - 1

    def greet(self):
        signal_group(self.other)
        pl.when(self.has_left)(lambda: signal_group(self.own - 2))
        pl.when(self.has_right)(lambda: signal_group(self.own + 2))
        return 1 + self.has_left.astype(jnp.int32) + self.has_right.astype(jnp.int32)


def signal_group(peer):
    barrier = pltpu.get_barrier_semaphore()
    pl.semaphore_signal(barrier, inc=1, device_id={"fsdp": peer}, device_id_type=MESH)


def signal_seq(peer):
    barrier = pltpu.get_barrier_semaphore()
    pl.semaphore_signal(barrier, inc=1, device_id={"seq": peer}, device_id_type=MESH)


def greet_group(group):
    own = lax.axis_index("fsdp")
    pl.loop(1, group)(lambda ahead: signal_group(lax.rem(own + ahead, group)))
    return group - 1


def greet_seq(seqs):
    own = lax.axis_index("seq")
    pl.loop(1, seqs)(lambda ahead: signal_seq(lax.rem(own + ahead, seqs)))
    return seqs - 1


def meet(count):
    pl.semaphore_wait(pltpu.get_barrier_semaphore(), count)


def rows_at(index, size):
    return pl.ds(pl.multiple_of(index * size, size), size)


class Spread:
    def __init__(self, line, first, buf, send, recv):
        self.line, self.first, self.buf, self.send, self.recv = line, first, buf, send, recv
        self.parts = recv.shape[1]
        self.size = first.shape[0] // self.parts

    def move(self, slot, part, way, peer, source=None):
        here = rows_at(part, self.size)
        return pltpu.make_async_remote_copy(
            src_ref=self.buf.at[slot, here] if source is None else source.at[here],
            dst_ref=self.buf.at[slot, here],
            send_sem=self.send.at[way, slot, part],
            recv_sem=self.recv.at[slot, part],
            device_id={"fsdp": peer},
            device_id_type=MESH,
        )

    def begin(self):
        line = self.line

        @pl.loop(0, self.parts)
        def _(part):
            pl.when(line.has_right)(
                lambda: self.move(line.own, part, 1, line.own + 2, self.first).start()
            )
            pl.when(line.has_left)(
                lambda: self.move(line.own, part, 0, line.own - 2, self.first).start()
            )
            self.move(line.own, part, 2, line.other, self.first).start()

    def relay_part(self, far, part):
        line = self.line

        @pl.when(line.chip - far >= 0)
        def _():
            slot = (line.chip - far) * 2 + line.core
            self.move(slot, part, 1, line.own).wait_recv()
            pl.when(line.has_right)(lambda: self.move(slot, part, 1, line.own + 2).start())
            self.move(slot, part, 2, line.other).start()

        @pl.when(line.chip + far < line.chips)
        def _():
            slot = (line.chip + far) * 2 + line.core
            self.move(slot, part, 0, line.own).wait_recv()
            pl.when(line.has_left)(lambda: self.move(slot, part, 0, line.own - 2).start())
            self.move(slot, part, 2, line.other).start()

    def relay(self, far):
        pl.loop(0, self.parts)(lambda part: self.relay_part(far, part))

    def across(self, slot):
        pl.loop(0, self.parts)(lambda part: self.move(slot, part, 2, self.line.own).wait_recv())

    def each(self, far, use):
        line = self.line

        @pl.loop(0, 4)
        def _(turn):
            side = lax.rem(turn, 2)
            over = turn // 2
            away = far - over
            source = line.chip + away * (2 * side - 1)
            valid = (away >= 0) & (away < line.chips) & (source >= 0) & (source < line.chips)
            valid = valid & ((side == 0) | (away > 0))

            @pl.when(valid)
            def _():
                slot = source * 2 + line.core + over * (1 - 2 * line.core)
                pl.when(over == 1)(lambda: self.across(slot))
                use(slot)

    def rest(self):
        pl.loop(0, self.line.chips)(lambda place: self.across(place * 2 + 1 - self.line.core))

    def sent(self):
        line = self.line

        @pl.loop(0, line.chips)
        def _(place):
            slot = place * 2 + line.core

            @pl.loop(0, self.parts)
            def _(part):
                self.move(slot, part, 2, line.other).wait_send()
                pl.when(line.has_right & (place <= line.chip))(
                    lambda: self.move(slot, part, 1, line.own + 2).wait_send()
                )
                pl.when(line.has_left & (place >= line.chip))(
                    lambda: self.move(slot, part, 0, line.own - 2).wait_send()
                )


class Reduce:
    def __init__(self, line, product, out, acc, cross_out, line_out, cross_in, line_in, send, recv):
        self.line, self.product, self.out, self.acc = line, product, out, acc
        self.cross_out, self.line_out, self.cross_in, self.line_in = cross_out, line_out, cross_in, line_in
        self.send, self.recv = send, recv
        self.tiles = line_out.shape[2] // TILE

    @staticmethod
    def scratch(chips, rows, width):
        part = pltpu.VMEM((chips, rows, width), jnp.bfloat16)
        return [
            pltpu.VMEM((rows, TILE), jnp.float32),
            pltpu.VMEM((2, rows, width), jnp.bfloat16),
            part,
            part,
            pltpu.VMEM((chips + 1, rows, width), jnp.bfloat16),
            pltpu.SemaphoreType.DMA((2, chips, width // TILE)),
            pltpu.SemaphoreType.DMA((2, chips + 1, width // TILE)),
        ]

    def cross(self, side, place, tile):
        here = rows_at(tile, TILE)
        return pltpu.make_async_remote_copy(
            src_ref=self.cross_out.at[side, :, here],
            dst_ref=self.cross_in.at[place, :, here],
            send_sem=self.send.at[0, place, tile],
            recv_sem=self.recv.at[0, place, tile],
            device_id={"fsdp": self.line.other},
            device_id_type=MESH,
        )

    def along(self, place, landing, tile, peer):
        here = rows_at(tile, TILE)
        return pltpu.make_async_remote_copy(
            src_ref=self.line_out.at[place, :, here],
            dst_ref=self.line_in.at[landing, :, here],
            send_sem=self.send.at[1, place, tile],
            recv_sem=self.recv.at[1, landing, tile],
            device_id={"fsdp": peer},
            device_id_type=MESH,
        )

    def where(self, away, side):
        line = self.line
        rightward = (line.chips - 1 - line.chip >= line.chip) == (side == 0)
        place = line.chip + jnp.where(rightward, away, -away)
        valid = (place >= 0) & (place < line.chips) & ((away > 0) | (side == 0))
        return valid, place, rightward

    def level(self, away, also):
        @pl.loop(0, 2)
        def _(side):
            valid, place, _ = self.where(away, side)

            @pl.when(valid)
            def _():
                @pl.loop(0, self.tiles)
                def _(tile):
                    got = self.product(place * 2 + 1 - self.line.core, tile)
                    self.cross_out[side, :, rows_at(tile, TILE)] = to_half(got)
                    self.cross(side, place, tile).start()

        @pl.loop(0, self.tiles)
        def _(tile):
            @pl.loop(0, 2)
            def _(side):
                valid, place, rightward = self.where(away, side)
                pl.when(valid)(lambda: self.close(away, side, place, rightward, tile))

            also(tile)

    def close(self, away, side, place, rightward, tile):
        line, acc = self.line, self.acc
        here = rows_at(tile, TILE)
        upstream = (rightward & line.has_left) | (jnp.logical_not(rightward) & line.has_right)
        acc[...] = self.product(place * 2 + line.core, tile)
        self.cross(side, place, tile).wait()
        acc[...] += self.cross_in[place, :, here].astype(jnp.float32)

        @pl.when(away > 0)
        def _():
            @pl.when(upstream)
            def _():
                self.along(place, place, tile, line.own).wait_recv()
                self.line_out[place, :, here] = to_half(
                    acc[...] + self.line_in[place, :, here].astype(jnp.float32)
                )

            @pl.when(jnp.logical_not(upstream))
            def _():
                self.line_out[place, :, here] = to_half(acc[...])

            @pl.when(rightward)
            def _():
                self.along(place, place, tile, line.own + 2).start()

            @pl.when(jnp.logical_not(rightward))
            def _():
                landing = jnp.where(away == 1, line.chips, place)
                self.along(place, landing, tile, line.own - 2).start()

        @pl.when(away == 0)
        def _():
            self.out[:, here] = acc[...]

            @pl.when(line.has_left)
            def _():
                self.along(place, place, tile, line.own).wait_recv()
                self.out[:, here] += self.line_in[place, :, here].astype(jnp.float32)

            @pl.when(line.has_right)
            def _():
                self.along(place, line.chips, tile, line.own).wait_recv()
                self.out[:, here] += self.line_in[line.chips, :, here].astype(jnp.float32)

    def sent(self):
        @pl.loop(0, self.line.chips)
        def _(place):
            @pl.when(place != self.line.chip)
            def _():
                pl.loop(0, self.tiles)(
                    lambda tile: self.along(place, place, tile, self.line.own).wait_send()
                )


class Swap:
    def __init__(self, group, source, target, send, recv, keep):
        self.group, self.source, self.target = group, source, target
        self.send, self.recv, self.keep = send, recv, keep
        self.own = lax.axis_index("fsdp")

    def move(self, peer, source):
        return pltpu.make_async_remote_copy(
            src_ref=self.source.at[peer],
            dst_ref=self.target.at[source],
            send_sem=self.send.at[peer],
            recv_sem=self.recv.at[source],
            device_id={"fsdp": peer},
            device_id_type=MESH,
        )

    def kept(self):
        return pltpu.make_async_copy(self.source.at[self.own], self.target.at[self.own], self.keep)

    def begin(self):
        self.kept().start()
        pl.loop(1, self.group)(
            lambda ahead: self.move(lax.rem(self.own + ahead, self.group), self.own).start()
        )

    def end(self):
        self.kept().wait()

        @pl.loop(1, self.group)
        def _(ahead):
            peer = lax.rem(self.own + ahead, self.group)
            self.move(peer, peer).wait_recv()
            self.move(peer, self.own).wait_send()


class Share:
    def __init__(self, seqs, source, target, send, recv, keep):
        self.seqs, self.source, self.target = seqs, source, target
        self.send, self.recv, self.keep = send, recv, keep
        self.own = lax.axis_index("seq")
        self.parts = send.shape[2]
        self.size = source.shape[0] // self.parts

    def move(self, peer, place, part):
        here = pl.ds(part * self.size, self.size)
        return pltpu.make_async_remote_copy(
            src_ref=self.source.at[here],
            dst_ref=self.target.at[place, here],
            send_sem=self.send.at[peer, 0, part],
            recv_sem=self.recv.at[place, 0, part],
            device_id={"seq": peer},
            device_id_type=MESH,
        )

    def relay(self, peer, place, part, side):
        here = pl.ds(part * self.size + side * (self.size // 2), self.size // 2)
        return pltpu.make_async_remote_copy(
            src_ref=self.target.at[place, here],
            dst_ref=self.target.at[place, here],
            send_sem=self.send.at[peer, 1, part],
            recv_sem=self.recv.at[place, side, part],
            device_id={"seq": peer},
            device_id_type=MESH,
        )

    def near(self):
        one = self.own + 1 - 2 * lax.rem(self.own, 2)
        two = lax.rem(self.own + 2, 4)
        return one, two, lax.rem(one + 2, 4)

    def kept(self):
        return pltpu.make_async_copy(self.source, self.target.at[self.own], self.keep)

    def begin(self):
        self.kept().start()
        for part in range(self.parts):
            if self.seqs == 4:
                one, two, _ = self.near()
                self.move(one, self.own, part).start()
                self.move(two, self.own, part).start()
            else:
                pl.loop(1, self.seqs)(
                    lambda ahead, part=part: self.move(
                        lax.rem(self.own + ahead, self.seqs), self.own, part
                    ).start()
                )

    def pass_on(self, parts):
        if self.seqs == 4:
            one, two, _ = self.near()
            for part in parts:
                self.move(one, one, part).wait_recv()
                self.relay(two, one, part, 0).start()
                self.move(two, two, part).wait_recv()
                self.relay(one, two, part, 1).start()

    def end(self):
        self.kept().wait()
        for part in range(self.parts):
            if self.seqs == 4:
                one, two, far = self.near()
                self.relay(two, far, part, 0).wait_recv()
                self.relay(one, far, part, 1).wait_recv()
                self.move(one, self.own, part).wait_send()
                self.move(two, self.own, part).wait_send()
                self.relay(two, one, part, 0).wait_send()
                self.relay(one, two, part, 1).wait_send()
            else:

                @pl.loop(1, self.seqs)
                def _(ahead, part=part):
                    peer = lax.rem(self.own + ahead, self.seqs)
                    self.move(peer, peer, part).wait_recv()
                    self.move(peer, self.own, part).wait_send()


def seq_peers(seqs):
    own = lax.axis_index("seq")
    if seqs == 4:
        one = own + 1 - 2 * lax.rem(own, 2)
        return [one, lax.rem(own + 2, 4)], [lax.rem(one + 2, 4)]
    ahead = [lax.rem(own + step, seqs) for step in range(1, seqs)]
    return ahead[:1], ahead[1:]


def near_count(seqs):
    return 2 if seqs == 4 else 1


class ToPeers:
    def __init__(self, seqs, peers, source, target, send, recv, first=0):
        self.peers, self.source, self.target, self.send, self.recv = peers, source, target, send, recv
        self.run, self.first = source.shape[0] // seqs, first

    def move(self, index):
        begin = pl.multiple_of(self.peers[index] * self.run + self.first, 16)
        return pltpu.make_async_remote_copy(
            src_ref=self.source.at[pl.ds(begin, self.target.shape[1])],
            dst_ref=self.target.at[index],
            send_sem=self.send.at[index],
            recv_sem=self.recv.at[index],
            device_id={"seq": self.peers[index]},
            device_id_type=MESH,
        )

    def begin(self):
        for index in range(len(self.peers)):
            self.move(index).start()

    def arrived(self):
        for index in range(len(self.peers)):
            self.move(index).wait_recv()

    def sent(self):
        for index in range(len(self.peers)):
            self.move(index).wait_send()

    def end(self):
        self.arrived()
        self.sent()


def load_halves(halves, target, load):
    copies = []
    rows = halves[0].shape[1]
    for index, half in enumerate(halves):
        for place in range(half.shape[0]):
            there = pl.ds((2 * place + index) * rows, rows)
            copies.append(pltpu.make_async_copy(half.at[place], target.at[there], load.at[index, place]))
    return copies


VMEM_SPEC = pl.BlockSpec(memory_space=pltpu.VMEM)
ANY_SPEC = pl.BlockSpec(memory_space=pl.ANY)


def comm_params(collective, mib=58):
    return pltpu.CompilerParams(
        collective_id=collective, has_side_effects=True, vmem_limit_bytes=mib * MIB
    )


def cost(flops, local, remote):
    return pl.CostEstimate(
        flops=flops, bytes_accessed=local, transcendentals=0, remote_bytes_transferred=remote
    )


def sems(*shape):
    return pltpu.SemaphoreType.DMA(shape)


def left_rows(a_ref, slot, rows):
    if len(a_ref.shape) == 2:
        return a_ref[rows_at(slot, rows), :]
    piece = rows // a_ref.shape[0]
    return jnp.concatenate(
        [a_ref[batch, rows_at(slot, piece), :] for batch in range(a_ref.shape[0])], axis=0
    )


def norm_back(rows, v_ref, e_ref, gain_ref, gain_acc, put):
    @pl.loop(0, rows // 32)
    def _(chunk):
        here = rows_at(chunk, 32)
        values = v_ref[here, :].astype(jnp.float32)
        error = e_ref[here, :]
        rate = lax.rsqrt(jnp.mean(values * values, axis=-1, keepdims=True) + EPS)
        unit = values * rate
        product = error * unit
        gain = gain_ref[0:1, :]
        mean = jnp.mean(product * gain, axis=-1, keepdims=True)
        gain_acc[...] += (product[0:8] + product[8:16]) + (product[16:24] + product[24:32])
        put(here, rate * (gain * error - unit * mean))


def add_from_seq(own_rows, got, here):
    added = own_rows.astype(jnp.float32)
    for index in range(got.shape[0]):
        added = added + got[index, here, :].astype(jnp.float32)
    return added


def column_parts(seqs, group, share, span):
    size = HEAD if share == HEAD else span
    parts = []
    for member in range(group):
        for run in range(span // size):
            home = (run * group + member) * size
            parts.append((member, run * size, home, size))
    return parts


def start_kernel(
    seqs, chips, batches, block, tile_ref, x_ref, wq_ref, wk_ref, wv_ref, gate_hbm, up_hbm, down_hbm, low_ref,
    g_ref, q_ref, out_ref, lse_ref, pad_ref, gains_ref, w_out_ref, own_units_ref, wd_ref,
    gate, up, units, blocks_ref, buf, normed, pad, vt, gain, gains, w,
    unit_sem, send, recv, keep, swap_send, share_send, w_recv,
    tile_send, tile_across, tile_recv, tile_back, w_keep, gain_keep,
    halo_send, halo_recv, pad_keep, unit_send, unit_recv, unit_keep,
    down_send, down_recv, down_keep,
):
    line = Line(chips)
    group = 2 * chips
    seq = lax.axis_index("seq")
    own = line.own
    share = blocks_ref.shape[1]
    rows, width = x_ref.shape
    piece = rows // batches
    length, span = q_ref.shape[1:]
    per = 128 * seqs * group // width
    steps, need = length // block, WINDOW // block
    has_left, has_right = seq > 0, seq < seqs - 1
    unit_loads = [
        pltpu.make_async_copy(gate_hbm, gate, unit_sem.at[0]),
        pltpu.make_async_copy(up_hbm, up, unit_sem.at[1]),
    ]
    for item in unit_loads:
        item.start()
    for index, source in enumerate((wq_ref, wk_ref, wv_ref)):
        for member, first, home, size in column_parts(seqs, group, share, span):
            first = first + index * span
            blocks_ref[member, :, first : first + size] = source[:, home : home + size]
    meet(greet_group(group) + greet_seq(seqs))

    def block_at(run, member):
        return w.at[rows_at(run * group + member, share)]

    def block_swap(peer, member):
        return pltpu.make_async_remote_copy(
            src_ref=blocks_ref.at[peer],
            dst_ref=block_at(seq, member),
            send_sem=swap_send.at[peer],
            recv_sem=w_recv.at[seq, member],
            device_id={"fsdp": peer},
            device_id_type=MESH,
        )

    def block_share(run, member, peer):
        return pltpu.make_async_remote_copy(
            src_ref=block_at(run, member),
            dst_ref=block_at(run, member),
            send_sem=share_send.at[peer, member],
            recv_sem=w_recv.at[run, member],
            device_id={"seq": peer},
            device_id_type=MESH,
        )

    def tile_to_seq(peer, place):
        return pltpu.make_async_remote_copy(
            src_ref=tile_ref.at[0],
            dst_ref=gains.at[own, place],
            send_sem=tile_send.at[peer],
            recv_sem=tile_recv.at[place],
            device_id={"seq": peer},
            device_id_type=MESH,
        )

    def tiles_to_group(peer, member):
        return pltpu.make_async_remote_copy(
            src_ref=gains.at[member],
            dst_ref=gains.at[member],
            send_sem=tile_across.at[peer],
            recv_sem=tile_back.at[member],
            device_id={"fsdp": peer},
            device_id_type=MESH,
        )

    def others(count, me, act):
        pl.loop(1, count)(lambda ahead: act(lax.rem(me + ahead, count)))

    others(seqs, seq, lambda peer: tile_to_seq(peer, seq).start())
    down = Share(
        seqs, down_hbm.at[pl.ds(0, wd_ref.shape[1])], wd_ref, down_send, down_recv, down_keep
    )
    down.begin()
    others(group, own, lambda peer: block_swap(peer, own).start())
    spreads = [
        Spread(line, x_ref.at[pl.ds(batch * piece, piece)], buf.at[batch], send.at[batch], recv.at[batch])
        for batch in range(batches)
    ]
    spreads[0].begin()
    gains[own, seq] = tile_ref[0]
    w[rows_at(seq * group + own, share), :] = blocks_ref[own]
    others(seqs, seq, lambda peer: block_share(seq, own, peer).start())
    for batch in range(batches):
        buf[batch, own] = x_ref[batch * piece : (batch + 1) * piece, :]
    others(seqs, seq, lambda peer: tile_to_seq(peer, peer).wait_recv())
    others(group, own, lambda peer: tiles_to_group(peer, own).start())
    for item in unit_loads:
        item.wait()
    cell = units.shape[2] // 2 // seqs
    for member in range(group):
        for run in range(seqs):
            home = (run * group + member) * cell
            for index, source in enumerate((gate, up)):
                first = (index * seqs + run) * cell
                units[member, :, first : first + cell] = source[:, home : home + cell]
    unit_swap = Swap(group, units, own_units_ref, unit_send, unit_recv, unit_keep)

    @pl.when(jnp.logical_not(has_left))
    def _():
        pad[:, :WINDOW, :] = jnp.zeros((batches, WINDOW, 2 * span), jnp.bfloat16)

    def pass_block(member):
        block_swap(member, member).wait_recv()
        others(seqs, seq, lambda peer: block_share(seq, member, peer).start())

    others(group, own, pass_block)
    down.pass_on([0])
    others(group, own, lambda peer: tiles_to_group(peer, peer).wait_recv())
    for column in range(width // 128):
        total = 0.0
        for place in range(column * per, (column + 1) * per):
            total = total + gains[place % group, place // group, 0:1, :]
        gain[0:1, column * 128 : (column + 1) * 128] = total

    def sides(far, act):
        @pl.loop(0, 2)
        def _(side):
            place = line.chip + far * (2 * side - 1)
            valid = (place >= 0) & (place < chips) & ((side == 0) | (far > 0))
            pl.when(valid)(lambda: act(place))

    def kept(batch, place):
        here = rows_at(place, block)
        return pltpu.make_async_copy(
            normed.at[batch, here], g_ref.at[batch, here], keep.at[batch, place]
        )

    def norm_pair(batch, place):
        spreads[batch].across(place * 2 + 1 - line.core)

        @pl.loop(0, 2)
        def _(member):
            @pl.loop(0, piece // 64)
            def _(chunk):
                values = buf[batch, place * 2 + member, rows_at(chunk, 64), :].astype(jnp.float32)
                there = pl.multiple_of(place * block + member * piece + chunk * 64, 64)
                normed[batch, pl.ds(there, 64), :] = to_half(normalize(values, gain[0:1, :]))

        kept(batch, place).start()

    def halo(batch, step, peer):
        there = pl.multiple_of(WINDOW + (step + steps - need) * block, block)
        return pltpu.make_async_remote_copy(
            src_ref=pad.at[batch, pl.ds(there, block)],
            dst_ref=pad.at[batch, rows_at(step, block)],
            send_sem=halo_send.at[batch, step],
            recv_sem=halo_recv.at[batch, step],
            device_id={"seq": peer},
            device_id_type=MESH,
        )

    def project(batch, place):
        here = rows_at(place, block)
        got = to_half(dot_nn(normed[batch, here, :], w[...]))
        q_ref[batch, here, :] = got[:, :span]
        pad[batch, pl.ds(pl.multiple_of(WINDOW + place * block, block), block), :] = got[:, span:]

        @pl.when(has_right & (place >= steps - need))
        def _():
            halo(batch, place - (steps - need), seq + 1).start()

    @pl.loop(0, chips)
    def _(far):
        pl.when(far > 0)(lambda: spreads[0].relay(far))
        pl.when(far == chips - 2)(spreads[1].begin)
        sides(far, lambda place: norm_pair(0, place))

    spreads[1].relay(1)

    def have_block(run, member):
        block_share(run, member, seq).wait_recv()

    others(seqs, seq, lambda run: pl.loop(0, group)(lambda member: have_block(run, member)))
    w_kept = pltpu.make_async_copy(w, w_out_ref, w_keep)
    w_kept.start()
    gains_kept = pltpu.make_async_copy(gains, gains_ref, gain_keep)
    gains_kept.start()
    pl.loop(0, steps)(lambda place: project(0, place))

    @pl.loop(2, chips)
    def _(far):
        spreads[1].relay(far)

    unit_swap.begin()

    @pl.loop(0, chips)
    def _(far):
        sides(far, lambda place: norm_pair(1, place))
        sides(far, lambda place: project(1, place))

    def pad_kept(batch):
        return pltpu.make_async_copy(pad.at[batch], pad_ref.at[batch], pad_keep.at[batch])

    for batch in range(batches):
        vt[:, WINDOW:] = pad[batch, WINDOW:, span:].T

        @pl.loop(0, steps)
        def _(turn, batch=batch):
            step = steps - 1 - turn

            @pl.when(step < need)
            def _():
                arrived = rows_at(step, block)
                pl.when(has_left)(lambda: halo(batch, step, seq).wait_recv())
                vt[:, arrived] = pad[batch, arrived, span:].T

            begin = pl.multiple_of(step * block, block)
            keys = pl.ds(begin, block + WINDOW)
            rows = pl.ds(begin, block)
            low = low_ref[batch, :, rows]
            for pair in range(span // PAIR):
                lanes = slice(pair * PAIR, (pair + 1) * PAIR)
                q_pair = q_ref[batch, rows, lanes] * jnp.asarray(HEAD**-0.5, jnp.bfloat16)
                k_rows = pad[batch, keys, lanes]
                values = vt[lanes, keys]
                mixed = []
                for half in range(2):
                    scores = masked_scores(k_rows, head_lanes(q_pair, half), low)
                    top = jnp.max(scores, axis=0, keepdims=True)
                    expo = jnp.exp(scores - top)
                    total = jnp.sum(expo, axis=0, keepdims=True)
                    mixed.append(dot_nn(values, to_half(expo)) / total)
                    row = pair * 2 + half
                    lse_ref[batch, row : row + 1, rows] = top + jnp.log(total)
                lane = lax.broadcasted_iota(jnp.int32, mixed[0].shape, 0)
                out_ref[batch, rows, lanes] = to_half(jnp.where(lane < HEAD, mixed[0], mixed[1]).T)

        pad_kept(batch).start()

    for batch in range(batches):
        spreads[batch].sent()
    others(seqs, seq, lambda peer: tile_to_seq(peer, seq).wait_send())
    others(group, own, lambda peer: block_swap(peer, own).wait_send())
    others(group, own, lambda peer: tiles_to_group(peer, own).wait_send())
    others(
        seqs,
        seq,
        lambda peer: pl.loop(0, group)(lambda member: block_share(seq, member, peer).wait_send()),
    )

    @pl.loop(0, need)
    def _(step):
        for batch in range(batches):
            pl.when(has_right)(lambda batch=batch: halo(batch, step, seq).wait_send())

    w_kept.wait()
    gains_kept.wait()
    unit_swap.end()
    down.end()
    for batch in range(batches):
        pad_kept(batch).wait()

        @pl.loop(0, steps)
        def _(place, batch=batch):
            kept(batch, place).wait()


def start(seqs, chips, batches, block, tile, x, weights, unit_weights, down, low, collective):
    rows, width = x.shape
    group = 2 * chips
    length = group * rows // batches
    share = weights[0].shape[0]
    span = width // group
    cols = 3 * span
    wide = unit_weights[0].shape[1]
    cells = 2 * wide // group
    piece = rows // batches
    padded = length + WINDOW
    half = jnp.bfloat16
    need = WINDOW // block
    return pl.pallas_call(
        functools.partial(start_kernel, seqs, chips, batches, block),
        out_shape=[
            jax.ShapeDtypeStruct((batches, length, width), half),
            jax.ShapeDtypeStruct((batches, length, span), half),
            jax.ShapeDtypeStruct((batches, length, span), half),
            jax.ShapeDtypeStruct((batches, span // HEAD, length), jnp.float32),
            jax.ShapeDtypeStruct((batches, padded, 2 * span), half),
            jax.ShapeDtypeStruct((group, seqs, 8, 128), jnp.float32),
            jax.ShapeDtypeStruct((width, cols), half),
            jax.ShapeDtypeStruct((group, share, cells), half),
            jax.ShapeDtypeStruct((seqs, down.shape[0] // 2, width), half),
        ],
        in_specs=[VMEM_SPEC] * 5 + [ANY_SPEC] * 2 + [VMEM_SPEC] * 2,
        out_specs=[ANY_SPEC] + [VMEM_SPEC] * 3 + [ANY_SPEC] * 5,
        scratch_shapes=[
            pltpu.VMEM((share, wide), half),
            pltpu.VMEM((share, wide), half),
            pltpu.VMEM((group, share, cells), half),
            pltpu.VMEM((group, share, cols), half),
            pltpu.VMEM((batches, group, piece, width), half),
            pltpu.VMEM((batches, length, width), half),
            pltpu.VMEM((batches, padded, 2 * span), half),
            pltpu.VMEM((span, padded), half),
            pltpu.VMEM((8, width), jnp.float32),
            pltpu.VMEM((group, seqs, 8, 128), jnp.float32),
            pltpu.VMEM((width, cols), half),
            sems(2),
            sems(batches, 3, group, PARTS // 2),
            sems(batches, group, PARTS // 2),
            sems(batches, chips),
            sems(group),
            sems(seqs, group),
            sems(seqs, group),
            sems(seqs),
            sems(group),
            sems(seqs),
            sems(group),
            pltpu.SemaphoreType.DMA,
            pltpu.SemaphoreType.DMA,
            sems(batches, need),
            sems(batches, need),
            sems(batches),
            sems(group),
            sems(group),
            pltpu.SemaphoreType.DMA,
            sems(seqs, 2, 1),
            sems(seqs, 2, 1),
            pltpu.SemaphoreType.DMA,
        ],
        compiler_params=comm_params(collective, 62),
        cost_estimate=cost(
            2 * group * rows * width * cols + 8 * batches * length * span * (WINDOW + block),
            300 * MIB,
            2 * group * rows * width * 2,
        ),
        name="start",
    )(tile, x, *weights, *unit_weights, down, low)


def branch_kernel(
    seqs, chips, a_ref, w_ref, d_ref, units_ref, down_hbm, x_ref, gain_ref,
    middle_ref, normed_ref, gd_ref, w_units_ref, wd_ref,
    out_ref, acc, cross_out, line_out, cross_in, line_in, sum_send, sum_recv,
    send, recv, d_keep, share_send, share_recv, share_keep,
    down_send, down_recv, down_keep,
):
    line = Line(chips)
    rows = out_ref.shape[0]

    def product(slot, tile):
        return dot_nn(left_rows(a_ref, slot, rows), w_ref[:, rows_at(tile, TILE)])

    meet(line.greet() + greet_seq(seqs))
    reduce = Reduce(
        line, product, out_ref, acc, cross_out, line_out, cross_in, line_in, sum_send, sum_recv
    )
    spread = Spread(line, d_ref, gd_ref, send, recv)
    units = Share(seqs, units_ref, w_units_ref, share_send, share_recv, share_keep)
    d_kept = pltpu.make_async_copy(d_ref, gd_ref.at[line.own], d_keep)
    half = wd_ref.shape[1]
    down = Share(seqs, down_hbm.at[pl.ds(half, half)], wd_ref, down_send, down_recv, down_keep)
    down.begin()
    units.begin()
    spread.begin()
    d_kept.start()

    @pl.loop(0, chips)
    def _(step):
        def also(tile):
            @pl.when((step == chips // 2) & (tile == 0))
            def _():
                down.pass_on([0])
                units.pass_on([0])

            pl.when(step < chips - 1)(lambda: spread.relay_part(step + 1, tile))

        reduce.level(chips - 1 - step, also)


    @pl.loop(0, rows // 32)
    def _(chunk):
        here = rows_at(chunk, 32)
        middle = x_ref[here, :].astype(jnp.float32) + out_ref[here, :]
        middle_ref[here, :] = middle
        normed_ref[here, :] = to_half(normalize(middle, gain_ref[0:1, :]))

    spread.rest()
    spread.sent()
    reduce.sent()
    d_kept.wait()
    units.end()
    down.end()


def branch_sum(seqs, chips, a, w, d_rows, units, down, x, gain, collective):
    rows, width = d_rows.shape
    group = 2 * chips
    half = jnp.bfloat16
    return pl.pallas_call(
        functools.partial(branch_kernel, seqs, chips),
        out_shape=[
            jax.ShapeDtypeStruct((rows, width), jnp.float32),
            jax.ShapeDtypeStruct((rows, width), half),
            jax.ShapeDtypeStruct((group, rows, width), half),
            jax.ShapeDtypeStruct((seqs,) + units.shape, half),
            jax.ShapeDtypeStruct((seqs, down.shape[0] // 2, width), half),
        ],
        in_specs=[VMEM_SPEC] * 7,
        out_specs=[VMEM_SPEC, VMEM_SPEC] + [ANY_SPEC] * 3,
        scratch_shapes=[pltpu.VMEM((rows, width), jnp.float32)]
        + Reduce.scratch(chips, rows, width)
        + [sems(3, group, PARTS), sems(group, PARTS), pltpu.SemaphoreType.DMA]
        + [sems(seqs, 2, 1), sems(seqs, 2, 1), pltpu.SemaphoreType.DMA] * 2,
        compiler_params=comm_params(collective),
        cost_estimate=cost(
            2 * group * rows * width * w.shape[0], 250 * MIB, 3 * group * rows * width * 2
        ),
        name="branch_sum",
    )(a, w, d_rows, units, down, x, gain)


class PairReduce:
    def __init__(self, line, product, out, acc, keep, cross_out, cross_in, line_out, line_in, send, recv):
        self.line, self.product, self.out, self.acc, self.keep = line, product, out, acc, keep
        self.cross_out, self.cross_in, self.line_out, self.line_in = cross_out, cross_in, line_out, line_in
        self.send, self.recv = send, recv
        self.tiles = keep.shape[1] // TILE

    @staticmethod
    def scratch(chips, piece, width):
        half = jnp.bfloat16
        return [
            pltpu.VMEM((piece, width), half),
            pltpu.VMEM((2, piece, width), half),
            pltpu.VMEM((2, piece, width), half),
            pltpu.VMEM((chips + 1, piece, width), half),
            pltpu.SemaphoreType.DMA((3, width // TILE)),
            pltpu.SemaphoreType.DMA((chips + 3, width // TILE)),
        ]

    def cross(self, parity, tile):
        here = rows_at(tile, TILE)
        return pltpu.make_async_remote_copy(
            src_ref=self.cross_out.at[:, here],
            dst_ref=self.cross_in.at[parity, :, here],
            send_sem=self.send.at[0, tile],
            recv_sem=self.recv.at[self.line.chips + 1 + parity, tile],
            device_id={"fsdp": self.line.other},
            device_id_type=MESH,
        )

    def along(self, parity, landing, tile, peer):
        here = rows_at(tile, TILE)
        return pltpu.make_async_remote_copy(
            src_ref=self.line_out.at[parity, :, here],
            dst_ref=self.line_in.at[landing, :, here],
            send_sem=self.send.at[1 + parity, tile],
            recv_sem=self.recv.at[landing, tile],
            device_id={"fsdp": peer},
            device_id_type=MESH,
        )

    def steps(self):
        return 2 * self.line.chips - 1

    def step(self, step):
        line, keep = self.line, self.keep
        piece = keep.shape[0]
        right_side = line.chips - 1 - line.chip
        away = line.chips - 1 - step // 2
        second = lax.rem(step, 2)
        rightward = (right_side >= line.chip) == (second == 0)
        place = line.chip + jnp.where(rightward, away, -away)
        longer = jnp.maximum(right_side, line.chip)
        shorter = jnp.minimum(right_side, line.chip)
        count = longer - away + jnp.maximum(shorter - away, 0) + second
        parity = lax.rem(count + 2 * line.chips, 2)
        upstream = (rightward & line.has_left) | (jnp.logical_not(rightward) & line.has_right)

        @pl.when((place >= 0) & (place < line.chips))
        def _():
            wide = self.acc.shape[1]

            @pl.loop(0, keep.shape[1] // wide)
            def _(tile):
                here = rows_at(tile, wide)
                self.acc[...] = self.product(place, here)
                self.cross_out[:, here] = to_half(self.acc[rows_at(1 - line.core, piece), :])
                keep[:, here] = self.acc[rows_at(line.core, piece), :]
                for piece_of in range(wide // TILE):
                    self.cross(parity, tile * (wide // TILE) + piece_of).start()

            @pl.loop(0, self.tiles)
            def _(tile):
                here = rows_at(tile, TILE)
                self.cross(parity, tile).wait()
                keep[:, here] += self.cross_in[parity, :, here].astype(jnp.float32)

                @pl.when(away > 0)
                def _():
                    pl.when(count >= 2)(
                        lambda: self.along(parity, place, tile, line.own).wait_send()
                    )

                    @pl.when(upstream)
                    def _():
                        self.along(parity, place, tile, line.own).wait_recv()
                        self.line_out[parity, :, here] = to_half(
                            keep[:, here] + self.line_in[place, :, here].astype(jnp.float32)
                        )

                    @pl.when(jnp.logical_not(upstream))
                    def _():
                        self.line_out[parity, :, here] = to_half(keep[:, here])

                    @pl.when(rightward)
                    def _():
                        self.along(parity, place, tile, line.own + 2).start()

                    @pl.when(jnp.logical_not(rightward))
                    def _():
                        landing = jnp.where(away == 1, line.chips, place)
                        self.along(parity, landing, tile, line.own - 2).start()

                @pl.when(away == 0)
                def _():
                    self.out[:, here] = keep[:, here]

                    @pl.when(line.has_left)
                    def _():
                        self.along(parity, place, tile, line.own).wait_recv()
                        self.out[:, here] += self.line_in[place, :, here].astype(jnp.float32)

                    @pl.when(line.has_right)
                    def _():
                        self.along(parity, line.chips, tile, line.own).wait_recv()
                        self.out[:, here] += self.line_in[line.chips, :, here].astype(jnp.float32)

    def sent(self):
        for count in range(max(self.line.chips - 3, 0), self.line.chips - 1):
            pl.loop(0, self.tiles)(
                lambda tile, parity=count % 2: self.along(parity, 0, tile, self.line.own).wait_send()
            )


def feed_kernel(
    seqs, chips, batches, x_ref, w_hbm, wd_one, wd_two, gd_hbm, v_ref, cot_ref, gain_ref,
    dm_ref, db_ref, gain_grad_ref, hidden_hbm, grad_hbm, grad_in,
    buf, d_buf, h_buf, w_ref, wd_ref, d_ref, tiles, totals, acc, keep,
    load, d_sem, h_sem, tile_sem, send, recv, part_send, part_recv, wd_load, *sums,
):
    line = Line(chips)
    rows, width = x_ref.shape
    piece = rows // batches
    pair = 2 * piece
    units = wd_ref.shape[0]
    part = min(units, 2 * TILE)
    block = tiles.shape[1]
    loads = [
        pltpu.make_async_copy(w_hbm, w_ref, load.at[0]),
    ] + load_halves([wd_one, wd_two], wd_ref, wd_load)
    for item in loads:
        item.start()
    meet(line.greet() + greet_seq(seqs))
    spreads = [
        Spread(
            line,
            x_ref.at[pl.ds(batch * piece, piece)],
            buf.at[batch],
            send.at[batch],
            recv.at[batch],
        )
        for batch in range(batches)
    ]
    spreads[0].begin()
    for batch in range(batches):
        buf[batch, line.own] = x_ref[batch * piece : (batch + 1) * piece, :]

    def fetch(batch, place, side):
        return [
            pltpu.make_async_copy(
                gd_hbm.at[place * 2 + core, pl.ds(batch * piece, piece)],
                d_buf.at[side, pl.ds(core * piece, piece)],
                d_sem.at[side, core],
            )
            for core in range(2)
        ]

    def stored(batch, place):
        return [
            pltpu.make_async_copy(
                h_buf.at[pl.ds(core * piece, piece)],
                hidden_hbm.at[
                    pl.ds(pl.multiple_of((place * 2 + core) * rows + batch * piece, piece), piece)
                ],
                h_sem.at[core],
            )
            for core in range(2)
        ]

    def sides(far, act):
        @pl.loop(0, 2)
        def _(side):
            place = line.chip + far * (2 * side - 1)
            valid = (place >= 0) & (place < chips) & ((side == 0) | (far > 0))
            pl.when(valid)(lambda: act(place, side))

    def take(batch, far):
        def begin(place, side):
            for item in fetch(batch, place, side):
                item.start()

        sides(far, begin)
        pl.when(far > 0)(lambda: spreads[batch].relay(far))

    def compute(batch, far):
        def act(place, side):
            spreads[batch].across(place * 2 + 1 - line.core)
            for item in fetch(batch, place, side):
                item.wait()

            def free():
                for item in stored(batch, place):
                    item.wait()

            if batch:
                free()
            else:
                pl.when((far > 0) | (side > 0))(free)
            there = rows_at(place, pair)

            @pl.loop(0, units // part)
            def _(tile):
                first = rows_at(tile, part)
                second = rows_at(units // part + tile, part)
                values = buf[batch, pl.ds(place * 2, 2), :, :].reshape(pair, width)
                gate = dot_nn(values, w_ref[:, first])
                up = dot_nn(values, w_ref[:, second])
                d_hidden = dot_nt(d_buf[side], wd_ref[first, :])
                sigma = jax.nn.sigmoid(gate)
                swish = gate * sigma
                h_buf[:, first] = to_half(swish * up)
                slope = sigma * (1.0 + gate * (1.0 - sigma))
                d_ref[batch, there, first] = to_half(d_hidden * up * slope)
                d_ref[batch, there, second] = to_half(d_hidden * swish)

            for item in stored(batch, place):
                item.start()

        sides(far, act)

    def product(batch):
        def get(place, here):
            return dot_nt(d_ref[batch, rows_at(place, pair), :], w_ref[here, :])

        return get

    reduces = [
        PairReduce(line, product(batch), totals.at[batch], acc, keep, *sums[6 * batch : 6 * batch + 6])
        for batch in range(batches)
    ]

    count = width // block
    seq = lax.axis_index("seq")

    near, far_off = seq_peers(seqs)
    soon = len(near)
    order = [peer * 2 for peer in near] + [peer * 2 for peer in far_off] + [seq * 2]
    order = order + [peer * 2 + 1 for peer in near] + [peer * 2 + 1 for peer in far_off] + [seq * 2 + 1]

    def tile_at(turn):
        tile = order[-1]
        for index in range(len(order) - 1):
            tile = jnp.where(turn == index, order[index], tile)
        return tile

    def grad_stored(turn):
        slot = lax.rem(turn, 2)
        return pltpu.make_async_copy(
            tiles.at[slot], grad_hbm.at[rows_at(tile_at(turn), block)], tile_sem.at[slot]
        )

    parts = ToPeers(seqs, near, grad_hbm, grad_in, part_send, part_recv)

    def leave(turn):
        grad_stored(turn).wait()
        for index in range(soon):
            pl.when(turn == index)(lambda index=index: parts.move(index).start())

    def weight_grad(turn):
        slot = lax.rem(turn, 2)
        size = min(4 * TILE, 2 * units)
        tile = tile_at(turn)

        @pl.loop(0, 2 * units // size)
        def _(column):
            here = rows_at(column, size)
            got = 0.0
            for batch in range(batches):
                left = buf[batch, :, :, rows_at(tile, block)].reshape(2 * chips * piece, block)
                got = got + contract_rows(left, d_ref[batch, :, here])
            tiles[slot, :, here] = to_half(got)

        pl.when(turn > 0)(lambda: leave(turn - 1))
        grad_stored(turn).start()

    def norm_batch(batch):
        own = pl.ds(batch * piece, piece)

        def put(here, d_values):
            there = pl.ds(pl.multiple_of(here.start + batch * piece, here.size), here.size)
            d_middle = cot_ref[there, :].astype(jnp.float32) + d_values
            dm_ref[there, :] = d_middle
            db_ref[there, :] = to_half(d_middle)

        norm_back(piece, v_ref.at[own], totals.at[batch], gain_ref, gain_grad_ref, put)

    gain_grad_ref[...] = jnp.zeros_like(gain_grad_ref)
    for item in loads:
        item.wait()
    last = 2 * chips - 2

    @pl.loop(0, chips)
    def _(far):
        take(0, far)
        pl.when(far == chips - 2)(spreads[1].begin)
        compute(0, far)

    @pl.loop(0, chips - 1)
    def _(far):
        take(1, far)
        reduces[0].step(2 * far)
        reduces[0].step(2 * far + 1)
        compute(1, far)

    take(1, chips - 1)
    compute(1, chips - 1)

    @pl.loop(0, 2)
    def _(step):
        reduces[1].step(step)
        weight_grad(step)

    reduces[0].step(last)
    norm_batch(0)

    @pl.loop(2, last)
    def _(step):
        reduces[1].step(step)
        pl.when(step < count)(lambda: weight_grad(step))

    @pl.loop(last, max(count, last))
    def _(tile):
        weight_grad(tile)

    reduces[1].step(last)
    norm_batch(1)
    for batch in range(batches):
        spreads[batch].sent()
        reduces[batch].sent()
    for item in stored(1, 0):
        item.wait()
    leave(count - 1)
    parts.end()


def feed_forward(seqs, chips, batches, x, w, wd_halves, group_d, middle, cot, gain, collective):
    rows, width = x.shape
    group = 2 * chips
    units = w.shape[1] // 2
    piece = rows // batches
    block = width // seqs // 2
    half = jnp.bfloat16
    return pl.pallas_call(
        functools.partial(feed_kernel, seqs, chips, batches),
        out_shape=[
            jax.ShapeDtypeStruct((rows, width), jnp.float32),
            jax.ShapeDtypeStruct((rows, width), half),
            jax.ShapeDtypeStruct((8, width), jnp.float32),
            jax.ShapeDtypeStruct((group * rows, units), half),
            jax.ShapeDtypeStruct((width, 2 * units), half),
            jax.ShapeDtypeStruct((near_count(seqs), block, 2 * units), half),
        ],
        in_specs=[VMEM_SPEC] + [ANY_SPEC] * 4 + [VMEM_SPEC] * 3,
        out_specs=[VMEM_SPEC] * 3 + [ANY_SPEC] * 3,
        scratch_shapes=[
            pltpu.VMEM((batches, group, piece, width), half),
            pltpu.VMEM((2, 2 * piece, width), half),
            pltpu.VMEM((2 * piece, units), half),
            pltpu.VMEM(w.shape, half),
            pltpu.VMEM((units, width), half),
            pltpu.VMEM((batches, group * piece, 2 * units), half),
            pltpu.VMEM((2, block, 2 * units), half),
            pltpu.VMEM((batches, piece, width), jnp.float32),
            pltpu.VMEM((2 * piece, 2 * TILE), jnp.float32),
            pltpu.VMEM((piece, width), jnp.float32),
            sems(2),
            sems(2, 2),
            sems(2),
            sems(2),
            sems(batches, 3, group, PARTS // 2),
            sems(batches, group, PARTS // 2),
            sems(seqs),
            sems(seqs),
            sems(2, seqs),
        ]
        + PairReduce.scratch(chips, piece, width) * batches,
        compiler_params=comm_params(collective, 63),
        cost_estimate=cost(
            14 * group * rows * width * units, 400 * MIB, 2 * group * rows * width * 2
        ),
        name="feed_forward",
    )(x, w, *wd_halves, group_d, middle, cot, gain)


def branch_back_kernel(
    seqs, chips, batches, x_ref, w_ref, att_ref, middle_ref, hidden_hbm, wd_one, wd_two, units_hbm, gd_hbm,
    d_ref, layer_ref, out_grad_ref, half_in, whole_in, down_hbm, down_in,
    out_ref, buf, hidden_ref, wd_ref, grad_acc, rights, tiles, send, recv, load, right_sem, tile_sem,
    part_send, part_recv, wd_load, down_send, down_recv, down_keep, acc, cross_out, line_out, cross_in, line_in, sum_send, sum_recv,
):
    line = Line(chips)
    rows = x_ref.shape[0]
    piece = rows // batches
    width = x_ref.shape[1]
    loads = [
        pltpu.make_async_copy(hidden_hbm, hidden_ref, load.at[0]),
    ] + load_halves([wd_one, wd_two], wd_ref, wd_load)
    for item in loads:
        item.start()

    def product(slot, tile):
        return dot_nn(left_rows(hidden_ref, slot, rows), wd_ref[:, rows_at(tile, TILE)])

    part = rights.shape[2]
    count = width // part

    def right(tile):
        slot = lax.rem(tile, 2)
        return pltpu.make_async_copy(
            gd_hbm.at[:, rows_at(tile, part)], rights.at[slot], right_sem.at[slot]
        )

    def stored(tile):
        slot = lax.rem(tile, 2)
        return pltpu.make_async_copy(
            tiles.at[slot], down_hbm.at[:, rows_at(tile, part)], tile_sem.at[slot]
        )

    def weight_grad(tile):
        right(tile).wait()
        pl.when(tile + 1 < count)(lambda: right(tile + 1).start())
        pl.when(tile >= 2)(lambda: stored(tile - 2).wait())
        slot = lax.rem(tile, 2)
        size = min(TILE, hidden_ref.shape[1])

        @pl.loop(0, hidden_ref.shape[1] // size)
        def _(row):
            here = rows_at(row, size)
            tiles[slot, here, :] = to_half(contract_rows(hidden_ref[:, here], rights[slot]))

        stored(tile).start()

    right(0).start()
    meet(line.greet() + greet_seq(seqs))
    near, far_off = seq_peers(seqs)
    soon = len(near)
    halves = ToPeers(
        seqs, near, units_hbm, half_in, part_send.at[0], part_recv.at[0], half_in.shape[1]
    )
    wholes = ToPeers(seqs, far_off, units_hbm, whole_in, part_send.at[1], part_recv.at[1])
    down = ToPeers(
        seqs, near, down_hbm, down_in.at[pl.ds(0, soon)], down_send, down_recv
    )
    down_kept = pltpu.make_async_copy(
        down_hbm.at[rows_at(lax.axis_index("seq"), down_in.shape[1])], down_in.at[soon], down_keep
    )
    spread = Spread(line, x_ref, buf, send, recv)
    reduce = Reduce(
        line, product, out_ref, acc, cross_out, line_out, cross_in, line_in, sum_send, sum_recv
    )
    spread.begin()
    halves.begin()
    wholes.begin()
    buf[line.own] = x_ref[...]
    grad_acc[...] = jnp.zeros_like(grad_acc)

    def use(slot):
        got = to_half(dot_nt(buf[slot], w_ref[...]))
        for batch in range(batches):
            d_ref[batch, rows_at(slot, piece), :] = got[batch * piece : (batch + 1) * piece]
        mixed = left_rows(att_ref, slot, rows)

        @pl.loop(0, width // TILE)
        def _(tile):
            here = rows_at(tile, TILE)
            grad_acc[:, here] += contract_rows(mixed, buf[slot, :, here])

    for item in loads:
        item.wait()

    reduce.level(chips - 1, lambda tile: None)
    pl.loop(0, count)(weight_grad)
    stored(count - 2).wait()
    stored(count - 1).wait()
    down.begin()
    down_kept.start()
    spread.relay(1)
    spread.each(0, use)

    @pl.loop(1, chips)
    def _(step):
        def also(tile):
            pl.when(step < chips - 1)(lambda: spread.relay_part(step + 1, tile))

        reduce.level(chips - 1 - step, also)
        spread.each(step, use)

    spread.each(chips, use)

    @pl.loop(0, rows // 32)
    def _(chunk):
        here = rows_at(chunk, 32)
        layer_ref[here, :] = to_half(middle_ref[here, :] + out_ref[here, :])

    out_grad_ref[...] = to_half(grad_acc[...])
    spread.sent()
    reduce.sent()
    halves.end()
    wholes.end()
    down.end()
    down_kept.wait()


def branch_back(seqs, chips, batches, x, w, attended, middle, hidden, wd_halves, unit_part, group_d, collective):
    rows, width = x.shape
    group = 2 * chips
    length = group * rows // batches
    span = w.shape[0]
    half = jnp.bfloat16
    part = 256 if group * rows <= 2048 else 128
    near, run = near_count(seqs), width // seqs
    units = hidden.shape[1]
    return pl.pallas_call(
        functools.partial(branch_back_kernel, seqs, chips, batches),
        out_shape=[
            jax.ShapeDtypeStruct((batches, length, span), half),
            jax.ShapeDtypeStruct((rows, width), half),
            jax.ShapeDtypeStruct((span, width), half),
            jax.ShapeDtypeStruct((near, run // 2, unit_part.shape[1]), half),
            jax.ShapeDtypeStruct((seqs - 1 - near, run, unit_part.shape[1]), half),
            jax.ShapeDtypeStruct((units, width), half),
            jax.ShapeDtypeStruct((near + 1, units // seqs, width), half),
        ],
        in_specs=[VMEM_SPEC] * 4 + [ANY_SPEC] * 5,
        out_specs=[VMEM_SPEC, VMEM_SPEC, VMEM_SPEC, ANY_SPEC, ANY_SPEC, ANY_SPEC, ANY_SPEC],
        scratch_shapes=[
            pltpu.VMEM((rows, width), jnp.float32),
            pltpu.VMEM((group, rows, width), half),
            pltpu.VMEM(hidden.shape, half),
            pltpu.VMEM((units, width), half),
            pltpu.VMEM((span, width), jnp.float32),
            pltpu.VMEM((2, group * rows, part), half),
            pltpu.VMEM((2, units, part), half),
            sems(3, group, PARTS),
            sems(group, PARTS),
            sems(2),
            sems(2),
            sems(2),
            sems(2, seqs),
            sems(2, seqs),
            sems(2, seqs),
            sems(seqs),
            sems(seqs),
            pltpu.SemaphoreType.DMA,
        ]
        + Reduce.scratch(chips, rows, width),
        compiler_params=comm_params(collective, 62),
        cost_estimate=cost(
            2 * group * rows * width * (2 * span + 2 * units),
            250 * MIB,
            2 * group * rows * width * 2,
        ),
        name="branch_back",
    )(x, w, attended, middle, hidden, *wd_halves, unit_part, group_d.reshape(group * rows, width))


def attention_back_kernel(
    seqs, chips, block, q_ref, pad_ref, low_ref, lse_ref, d_ref, part_hbm, in_one, in_two, in_far,
    w_ref, g_hbm, v_ref, dm_hbm, gain_ref, mlp_gain_ref, out_ref, down_hbm,
    grad_hbm, wq_ref, wk_ref, wv_ref, wo_hbm, tile_ref, gate_hbm, up_hbm, down_in,
    grad_ref, wo_ref, gate_ref, up_ref, result_sem, down_send, down_recv,
    dk, dv, kt, heads, back_out, back_in, unit_parts, unit_sums, units, lefts, parts, sums, cols, out_in,
    totals, gain_acc, gain_out, gain_in, gain_sum, gain_back, acc, keep,
    halo_send, halo_recv, unit_load, unit_send, unit_recv, unit_keep, dm_load, left_sem,
    part_send, part_recv, cols_send, cols_recv, out_send, out_recv,
    gain_send, gain_recv, back_send, back_recv, *line_sums,
):
    line = Line(chips)
    group = 2 * chips
    seq = lax.axis_index("seq")
    own = line.own
    batches, length, span = q_ref.shape
    rows, width = v_ref.shape
    piece = rows // batches
    pair_rows = 2 * piece
    depth = 3 * span
    run = width // seqs
    share = run // group
    part = lefts.shape[3]
    steps, need = length // block, WINDOW // block
    first = length - WINDOW
    has_left, has_right = seq > 0, seq < seqs - 1
    scale = jnp.asarray(HEAD**-0.5, jnp.bfloat16)

    def others(count, me, act):
        pl.loop(1, count)(lambda ahead: act(lax.rem(me + ahead, count)))

    def unit_loaded(turn, place, source):
        slot = lax.rem(turn, 2)
        return pltpu.make_async_copy(source, unit_parts.at[slot, place], unit_load.at[slot, place])

    def load_units(turn):
        member = lax.rem(own + turn, group)
        unit_loaded(turn, 0, part_hbm.at[rows_at(seq * group + member, share)]).start()
        soon = in_one.shape[0]
        for index in range(seqs - 1):

            def fetch(source, index=index):
                unit_loaded(turn, index + 1, source).start()

            if index < soon:

                @pl.when(member < chips)
                def _(index=index, fetch=fetch):
                    fetch(in_one.at[index, rows_at(member, share)])

                @pl.when(member >= chips)
                def _(index=index, fetch=fetch):
                    fetch(in_two.at[index, rows_at(member - chips, share)])

            else:
                fetch(in_far.at[index - soon, rows_at(member, share)])

    load_units(1)
    dm_loaded = pltpu.make_async_copy(dm_hbm, grad_ref, dm_load)
    dm_loaded.start()
    meet(greet_group(group) + greet_seq(seqs))
    near, far_off = seq_peers(seqs)
    down = ToPeers(seqs, far_off, down_hbm, down_in, down_send, down_recv)
    down.begin()
    swap = Swap(group, unit_sums, units, unit_send, unit_recv, unit_keep)

    @pl.loop(1, group + 1)
    def _(turn):
        member = lax.rem(own + turn, group)
        slot = lax.rem(turn, 2)
        pl.when(turn < group)(lambda: load_units(turn + 1))
        for place in range(seqs):
            unit_loaded(turn, place, part_hbm.at[rows_at(0, share)]).wait()

        @pl.loop(0, share // 16)
        def _(chunk):
            here = rows_at(chunk, 16)
            added = unit_parts[slot, 0, here, :].astype(jnp.float32)
            for place in range(1, seqs):
                added = added + unit_parts[slot, place, here, :].astype(jnp.float32)
            unit_sums[member, here, :] = to_half(added)

        pl.when(turn < group)(lambda: swap.move(member, own).start())
        pl.when(turn == group)(lambda: swap.kept().start())

    def halo(batch, step, peer):
        here = rows_at(step, block)
        return pltpu.make_async_remote_copy(
            src_ref=back_out.at[batch, here],
            dst_ref=back_in.at[batch, here],
            send_sem=halo_send.at[batch, step],
            recv_sem=halo_recv.at[batch, step],
            device_id={"seq": peer},
            device_id_type=MESH,
        )

    def attend_block(batch, step):
        begin = pl.multiple_of(step * block, block)
        keys = pl.ds(begin, block + WINDOW)
        rows = pl.ds(begin, block)
        low = low_ref[batch, :, rows]
        for pair in range(span // PAIR):
            lanes = slice(pair * PAIR, (pair + 1) * PAIR)
            q_pair = q_ref[batch, rows, lanes] * scale
            d_pair = d_ref[batch, rows, lanes]
            k_rows = pad_ref[batch, keys, lanes]
            v_rows = pad_ref[batch, keys, span + pair * PAIR : span + (pair + 1) * PAIR]
            k_cols = kt[lanes, keys]
            back = []
            for half in range(2):
                row = pair * 2 + half
                q_head = head_lanes(q_pair, half)
                d_head = head_lanes(d_pair, half)
                scores = masked_scores(k_rows, q_head, low)
                probs = jnp.exp(scores - lse_ref[batch, row : row + 1, rows])
                d_probs = dot_nt(v_rows, d_head)
                along = jnp.sum(probs * d_probs, axis=0, keepdims=True)
                d_scores = to_half(probs * (d_probs - along))
                dv[keys, lanes] += dot_nn(to_half(probs), d_head)
                dk[keys, lanes] += dot_nn(d_scores, q_head)
                back.append(dot_nn(k_cols, d_scores))
            at = lax.broadcasted_iota(jnp.int32, back[0].shape, 0)
            heads[batch, rows, lanes] = to_half(
                jnp.where(at < HEAD, back[0], back[1]).T
            )


        @pl.when(has_left & (step < need))
        def _():
            back_out[batch, rows, :span] = to_half(dk[rows, :])
            back_out[batch, rows, span:] = to_half(dv[rows, :])
            halo(batch, step, seq - 1).start()

        @pl.when(step == steps - 1)
        def _():
            heads[batch, :, span : 2 * span] = to_half(dk[WINDOW:, :])
            heads[batch, :, 2 * span :] = to_half(dv[WINDOW:, :])

    def add_halo(batch):
        @pl.when(has_right)
        def _():
            @pl.loop(0, need)
            def _(step):
                there = pl.ds(pl.multiple_of(step * block + first, block), block)
                halo(batch, step, seq).wait_recv()
                got = back_in[batch, rows_at(step, block), :].astype(jnp.float32)
                mine = heads[batch, there, span:].astype(jnp.float32)
                heads[batch, there, span:] = to_half(mine + got)

    def product(batch):
        def get(place, here):
            return dot_nt(heads[batch, rows_at(place, pair_rows), :], w_ref[here, :])

        return get

    reduces = [
        PairReduce(
            line, product(batch), totals.at[batch], acc, keep, *line_sums[6 * batch : 6 * batch + 6]
        )
        for batch in range(batches)
    ]
    last = 2 * chips - 2

    @pl.loop(0, 2 * steps)
    def _(turn):
        batch, step = turn // steps, lax.rem(turn, steps)

        @pl.when(step == 0)
        def _():
            kt[...] = pad_ref[batch, :, :span].T * scale
            dk[...] = jnp.zeros_like(dk)
            dv[...] = jnp.zeros_like(dv)

        attend_block(batch, step)
        after = turn - steps - 1
        pl.when(after == 0)(lambda: add_halo(0))

        @pl.when((after >= 0) & (2 * after < last))
        def _():
            reduces[0].step(2 * after)
            reduces[0].step(2 * after + 1)

    for after in range(steps - 1, chips - 1):
        reduces[0].step(2 * after)
        reduces[0].step(2 * after + 1)

    def left(tile):
        slot = lax.rem(tile, 2)
        return pltpu.make_async_copy(
            g_hbm.at[:, :, rows_at(tile, part)], lefts.at[slot], left_sem.at[slot]
        )

    heads_near = ToPeers(seqs, near + far_off, parts, sums, part_send, part_recv)
    left(0).start()
    add_halo(1)

    @pl.loop(0, width // part)
    def _(tile):
        left(tile).wait()
        pl.when(tile + 1 < width // part)(lambda: left(tile + 1).start())
        slot = lax.rem(tile, 2)
        got = contract_rows(lefts[slot, 0], heads[0])
        for batch in range(1, batches):
            got = got + contract_rows(lefts[slot, batch], heads[batch])
        parts[rows_at(tile, part), :] = to_half(got)

    heads_near.begin()
    from_seq = ToPeers(seqs, near + far_off, out_ref, out_in, out_send, out_recv)
    from_seq.begin()
    gain_acc[...] = jnp.zeros_like(gain_acc)
    dm_loaded.wait()

    def norm_batch(batch):
        mine = pl.ds(batch * piece, piece)

        def put(here, d_values):
            there = pl.ds(pl.multiple_of(here.start + batch * piece, here.size), here.size)
            grad_ref[there, :] += d_values

        norm_back(piece, v_ref.at[mine], totals.at[batch], gain_ref, gain_acc, put)

    pl.loop(0, 2)(reduces[1].step)
    reduces[0].step(last)
    norm_batch(0)
    pl.loop(2, last)(reduces[1].step)
    swap.end()
    cell = units.shape[2] // 2 // seqs
    for member in range(group):
        for place in range(seqs):
            column = (place * group + member) * cell
            for target, begin in ((gate_ref, 0), (up_ref, seqs * cell)):
                here = slice(begin + place * cell, begin + (place + 1) * cell)
                target[:, column : column + cell] = units[member, :, here]

    results = [
        pltpu.make_async_copy(source, target, result_sem.at[index])
        for index, (source, target) in enumerate(
            ((gate_ref, gate_hbm), (up_ref, up_hbm), (wo_ref, wo_hbm), (grad_ref, grad_hbm))
        )
    ]
    results[0].start()
    results[1].start()

    def block_swap(peer, member):
        return pltpu.make_async_remote_copy(
            src_ref=parts.at[rows_at(seq * group + peer, share)],
            dst_ref=cols.at[member],
            send_sem=cols_send.at[peer],
            recv_sem=cols_recv.at[member],
            device_id={"fsdp": peer},
            device_id_type=MESH,
        )

    heads_near.arrived()

    @pl.loop(0, run // 64)
    def _(chunk):
        here = rows_at(chunk, 64)
        there = pl.ds(pl.multiple_of(seq * run + chunk * 64, 64), 64)
        parts[there, :] = to_half(add_from_seq(parts[there, :], sums, here))

    others(group, own, lambda peer: block_swap(peer, own).start())
    cols[own] = parts[rows_at(seq * group + own, share), :]
    from_seq.arrived()
    out_rows = out_in.shape[1]
    wo_ref[...] = add_from_seq(out_ref[rows_at(seq, out_rows), :], out_in, slice(None))
    results[2].start()
    reduces[1].step(last)
    norm_batch(1)
    results[3].start()
    fold = 128 // share
    near = group // fold
    attn_row = jnp.sum(gain_acc[...], axis=0, keepdims=True)
    mlp_row = jnp.sum(mlp_gain_ref[...], axis=0, keepdims=True)
    gain_out[...] = jnp.zeros_like(gain_out)
    for place in range(width // 128):
        lanes = slice(place * 128, (place + 1) * 128)
        gain_out[place % near, place // near, 0:1, :] = attn_row[:, lanes]
        gain_out[place % near, place // near, 1:2, :] = mlp_row[:, lanes]

    def gain_group(peer, member):
        return pltpu.make_async_remote_copy(
            src_ref=gain_out.at[peer // fold],
            dst_ref=gain_in.at[member],
            send_sem=gain_send.at[peer],
            recv_sem=gain_recv.at[member],
            device_id={"fsdp": peer},
            device_id_type=MESH,
        )

    def gain_seq(peer, place):
        return pltpu.make_async_remote_copy(
            src_ref=gain_sum.at[peer],
            dst_ref=gain_back.at[place],
            send_sem=back_send.at[peer],
            recv_sem=back_recv.at[place],
            device_id={"seq": peer},
            device_id_type=MESH,
        )

    others(group, own, lambda peer: gain_group(peer, own).start())
    gain_in[own] = gain_out[own // fold]
    others(group, own, lambda peer: gain_group(peer, peer).wait_recv())
    gain_sum[...] = jnp.sum(gain_in[...], axis=0)
    others(seqs, seq, lambda peer: gain_seq(peer, seq).start())
    gain_back[seq] = gain_sum[seq]
    others(seqs, seq, lambda peer: gain_seq(peer, peer).wait_recv())
    tile_ref[...] = jnp.sum(gain_back[...], axis=0)
    others(group, own, lambda peer: block_swap(peer, peer).wait_recv())
    for index, target in enumerate((wq_ref, wk_ref, wv_ref)):
        for member, first, home, size in column_parts(seqs, group, share, span):
            first = first + index * span
            target[:, home : home + size] = cols[member, :, first : first + size]
    from_seq.sent()
    for item in results:
        item.wait()
    for batch in range(batches):
        reduces[batch].sent()

        @pl.when(has_left)
        def _(batch=batch):
            pl.loop(0, need)(lambda step: halo(batch, step, seq).wait_send())

    heads_near.sent()
    down.end()
    others(group, own, lambda peer: gain_group(peer, own).wait_send())
    others(group, own, lambda peer: block_swap(peer, own).wait_send())
    others(seqs, seq, lambda peer: gain_seq(peer, seq).wait_send())


def attention_back(
    seqs, chips, block, query, kv_pad, low, lse, d_att, part_own, parts_one, parts_two, parts_far, w, group_a,
    x, d_middle, gain, mlp_gain, out_part, down, collective,
):
    batches, length, span = query.shape
    padded = kv_pad.shape[1]
    rows, width = x.shape
    piece = rows // batches
    group = 2 * chips
    depth = w.shape[1]
    run = width // seqs
    share = run // group
    near = group // (128 // share)
    cells = part_own.shape[1]
    out_rows = out_part.shape[0] // seqs
    half, wide = jnp.bfloat16, jnp.float32
    part = 256 if batches * length <= 2048 else 128
    return pl.pallas_call(
        functools.partial(attention_back_kernel, seqs, chips, block),
        out_shape=[
            jax.ShapeDtypeStruct((rows, width), wide),
            jax.ShapeDtypeStruct((share, width), half),
            jax.ShapeDtypeStruct((share, width), half),
            jax.ShapeDtypeStruct((share, width), half),
            jax.ShapeDtypeStruct((out_rows, width), wide),
            jax.ShapeDtypeStruct((8, 128), wide),
            jax.ShapeDtypeStruct((share, cells // 2 * group), half),
            jax.ShapeDtypeStruct((share, cells // 2 * group), half),
            jax.ShapeDtypeStruct((seqs - 1 - near_count(seqs), down.shape[0] // seqs, width), half),
        ],
        in_specs=[VMEM_SPEC] * 5
        + [ANY_SPEC] * 4
        + [VMEM_SPEC, ANY_SPEC, VMEM_SPEC, ANY_SPEC]
        + [VMEM_SPEC] * 3
        + [ANY_SPEC],
        out_specs=[ANY_SPEC, VMEM_SPEC, VMEM_SPEC, VMEM_SPEC, ANY_SPEC, VMEM_SPEC]
        + [ANY_SPEC] * 3,
        scratch_shapes=[
            pltpu.VMEM((rows, width), wide),
            pltpu.VMEM((out_rows, width), wide),
            pltpu.VMEM((share, cells // 2 * group), half),
            pltpu.VMEM((share, cells // 2 * group), half),
            sems(4),
            sems(seqs),
            sems(seqs),
            pltpu.VMEM((padded, span), wide),
            pltpu.VMEM((padded, span), wide),
            pltpu.VMEM((span, padded), half),
            pltpu.VMEM((batches, length, depth), half),
            pltpu.VMEM((batches, WINDOW, 2 * span), half),
            pltpu.VMEM((batches, WINDOW, 2 * span), half),
            pltpu.VMEM((2, seqs, share, cells), half),
            pltpu.VMEM((group, share, cells), half),
            pltpu.VMEM((group, share, cells), half),
            pltpu.VMEM((2, batches, length, part), half),
            pltpu.VMEM((width, depth), half),
            pltpu.VMEM((seqs - 1, run, depth), half),
            pltpu.VMEM((group, share, depth), half),
            pltpu.VMEM((seqs - 1, out_rows, width), half),
            pltpu.VMEM((batches, piece, width), wide),
            pltpu.VMEM((8, width), wide),
            pltpu.VMEM((near, seqs, 8, 128), wide),
            pltpu.VMEM((group, seqs, 8, 128), wide),
            pltpu.VMEM((seqs, 8, 128), wide),
            pltpu.VMEM((seqs, 8, 128), wide),
            pltpu.VMEM((2 * piece, TILE), wide),
            pltpu.VMEM((piece, width), wide),
            sems(batches, WINDOW // block),
            sems(batches, WINDOW // block),
            sems(2, seqs),
            sems(group),
            sems(group),
            pltpu.SemaphoreType.DMA,
            pltpu.SemaphoreType.DMA,
            sems(2),
            sems(seqs),
            sems(seqs),
            sems(group),
            sems(group),
            sems(seqs),
            sems(seqs),
            sems(group),
            sems(group),
            sems(seqs),
            sems(seqs),
        ]
        + PairReduce.scratch(chips, piece, width) * batches,
        compiler_params=comm_params(collective, 63),
        cost_estimate=cost(
            20 * batches * length * span * (WINDOW + block) + 4 * group * rows * width * depth,
            400 * MIB,
            3 * group * rows * width * 2,
        ),
        name="attention_back",
    )(
        query, kv_pad, low, lse, d_att, part_own, parts_one, parts_two, parts_far, w, group_a, x,
        d_middle, gain, mlp_gain, out_part, down,
    )


def finish_kernel(count, *refs):
    sources, targets = refs[:-count], refs[-count:]
    for source, target in zip(sources, targets[:-1]):
        target[...] = source[...].astype(target.dtype)
    added = 0.0
    for source in sources[count - 1 :]:
        added = added + jnp.sum(source[...].astype(jnp.float32), axis=0)
    targets[-1][...] = added


def finish(steps, arrays, parts, kinds):
    in_specs, out_specs, out_shape = [], [], []
    for item, kind in zip(arrays + parts[:1], kinds):
        rows, width = item.shape[-2:]
        block = (rows // steps, width)
        out_specs.append(pl.BlockSpec(block, lambda i: (i, 0)))
        out_shape.append(jax.ShapeDtypeStruct((rows, width), kind))
        if item.ndim == 2:
            in_specs.append(out_specs[-1])
    for item in parts:
        in_specs.append(pl.BlockSpec((item.shape[0],) + block, lambda i: (0, i, 0)))
    return pl.pallas_call(
        functools.partial(finish_kernel, len(kinds)),
        grid=(steps,),
        in_specs=in_specs,
        out_specs=out_specs,
        out_shape=out_shape,
        compiler_params=pltpu.CompilerParams(vmem_limit_bytes=63 * MIB),
        name="finish",
    )(*arrays, *parts)


def doc_starts(lengths, positions, batches, seq_len):
    table = lengths.reshape(batches, -1, lengths.shape[1])
    starts = jnp.cumsum(table, axis=2) - table
    per_batch = seq_len // table.shape[1]
    begins = (starts + (jnp.arange(table.shape[1], dtype=jnp.int32) * per_batch)[None, :, None]).reshape(
        batches, -1
    )
    before = begins[:, None, :] <= positions[None, :, None]
    return jnp.max(jnp.where(before, begins[:, None, :], 0), axis=2)


def body(
    tokens,
    cotangent,
    lengths,
    gain_attn,
    w_query,
    w_key,
    w_value,
    w_out,
    gain_mlp,
    w_gate,
    w_up,
    w_down,
):
    batches, piece, width = tokens.shape
    seqs = lax.axis_size("seq")
    group = lax.axis_size("fsdp")
    chips = group // 2
    devices = seqs * group
    seq_len = piece * devices
    rows = batches * piece
    share = w_query.shape[0]
    span = width // group
    length = group * piece
    aligned = share == HEAD
    member = lax.axis_index("fsdp")

    x_rows = tokens.reshape(rows, width)
    cot_rows = cotangent.reshape(rows, width)
    if aligned:
        wo_part = lax.all_gather(w_out, "seq", axis=0, tiled=True)
    else:
        wo_all = lax.all_gather(w_out, ("seq", "fsdp"), axis=0, tiled=True)
        wo_part = lax.dynamic_slice_in_dim(wo_all, member * span, span, 0)

    lane = jnp.arange(128, dtype=jnp.int32)
    device = lax.axis_index("seq") * group + member
    fold = 128 // share
    here = lane // share == lax.rem(device, fold)
    both = jnp.stack([gain_attn, gain_mlp]).astype(jnp.float32)
    tile = jnp.where(here[None], jnp.tile(both, (1, fold)), 0.0)
    tile = jnp.pad(tile, ((0, 6), (0, 0)))[None]
    group_start = lax.axis_index("seq") * length
    positions = group_start + jnp.arange(length, dtype=jnp.int32)
    begins = doc_starts(lengths, positions, batches, seq_len)
    at = jnp.arange(length, dtype=jnp.int32)
    block = min(256, length)
    low = jnp.maximum(begins - group_start + WINDOW, at[None, :] + 1) - (at // block * block)[None, :]
    low = low[:, None, :]
    group_a, query, attended, lse, kv_pad, gains, w_heads, unit_own, wd_one = start(
        seqs, chips, batches, block, tile, x_rows, (w_query, w_key, w_value), (w_gate, w_up), w_down,
        low, 1,
    )
    gains = gains.transpose(1, 0, 2, 3).reshape(devices // fold, fold, 8, 128).sum(axis=1)
    gain_one = gains[:, 0].reshape(width)
    gain_two = gains[:, 1].reshape(width)
    middle, normed_b, group_d, w_units, wd_two = branch_sum(
        seqs, chips, attended, wo_part, cot_rows, unit_own.reshape(group * share, -1), w_down,
        x_rows, gain_two[None], 3,
    )
    w_units = w_units.reshape(width, -1)
    d_middle, d_branch, mlp_gain_part, hidden, unit_part, unit_one = feed_forward(
        seqs, chips, batches, normed_b, w_units, (wd_one, wd_two), group_d, middle, cot_rows,
        gain_two[None], 4,
    )
    d_attended, layer_out, out_part, unit_two, unit_far, down_part, down_near = branch_back(
        seqs, chips, batches, d_branch, wo_part, attended, middle, hidden, (wd_one, wd_two),
        unit_part, group_d, 5,
    )
    if not aligned:
        whole = lax.dynamic_update_slice_in_dim(
            jnp.zeros((width, width), jnp.bfloat16), out_part, member * span, 0
        )
        out_part = lax.psum(whole, "fsdp").reshape(seqs, group, share, width)
        out_part = lax.dynamic_slice_in_dim(out_part, member, 1, 1).reshape(seqs * share, width)
    (
        input_grad, wq_grad, wk_grad, wv_grad, wo_grad, gain_tile, gate_grad, up_grad, down_far,
    ) = attention_back(
        seqs, chips, block, query, kv_pad, low, lse, d_attended, unit_part, unit_one, unit_two,
        unit_far, w_heads, group_a, x_rows, d_middle, gain_one[None], mlp_gain_part, out_part,
        down_part, 6,
    )
    gain_grads = lax.dynamic_slice_in_dim(gain_tile[:2], lax.rem(device, fold) * share, share, 1)
    wide = jnp.float32
    (layer_out, input_grad, wq_grad, wk_grad, wv_grad, wo_grad, gate_grad, up_grad, down_grad) = finish(
        share // 16,
        [layer_out, input_grad, wq_grad, wk_grad, wv_grad, wo_grad, gate_grad, up_grad],
        [down_near, down_far],
        [jnp.bfloat16] + [wide] * 8,
    )
    return (
        layer_out.reshape(batches, piece, width),
        input_grad.reshape(batches, piece, width),
        gain_grads[0],
        wq_grad,
        wk_grad,
        wv_grad,
        wo_grad,
        gain_grads[1],
        gate_grad,
        up_grad,
        down_grad,
    )


def solution(mesh):
    spread = ("seq", "fsdp")
    tokens, rows, gains = P(None, spread, None), P(spread, None), P(spread)
    in_specs = (tokens, tokens, P(), gains, rows, rows, rows, rows, gains, rows, rows, rows)
    out_specs = (tokens, tokens, gains, rows, rows, rows, rows, gains, rows, rows, rows)
    return jax.shard_map(body, mesh=mesh, in_specs=in_specs, out_specs=out_specs, check_vma=False)
```

```python
import functools

import jax
import jax.numpy as jnp
from jax import lax
from jax.experimental import pallas as pl
from jax.experimental.pallas import tpu as pltpu
from jax.sharding import PartitionSpec as P

HEAD = 64
FF = 8192
WINDOW = 1024
PAIR = 128
TILE = 512
PARTS = 4
LOW = -1e30
EPS = 1e-05
MESH = pl.DeviceIdType.MESH
MIB = 2**20


def to_half(values):
    return values.astype(jnp.bfloat16)


def normalize(values, gain):
    return values * lax.rsqrt(jnp.mean(values * values, axis=-1, keepdims=True) + EPS) * gain


def contract_rows(left, right):
    return lax.dot_general(
        left, right, (((0,), (0,)), ((), ())), preferred_element_type=jnp.float32
    )


def dot_nt(left, right):
    return lax.dot_general(
        left, right, (((1,), (1,)), ((), ())), preferred_element_type=jnp.float32
    )


def dot_nn(left, right):
    return jnp.dot(left, right, preferred_element_type=jnp.float32)


def head_lanes(values, half):
    lane = lax.broadcasted_iota(jnp.int32, values.shape, 1)
    return jnp.where((lane >= HEAD) == (half == 1), values, jnp.zeros_like(values))


def masked_scores(k_rows, q_head, low):
    keys, block = k_rows.shape[0], q_head.shape[0]
    scores = dot_nt(k_rows, q_head)
    at = lax.broadcasted_iota(jnp.int32, (keys, block), 0)
    query = lax.broadcasted_iota(jnp.int32, (keys, block), 1)
    seen = (at >= low) & (at <= query + WINDOW)
    return jnp.where(seen, scores, LOW)


class Line:
    def __init__(self, chips):
        self.chips = chips
        self.own = lax.axis_index("fsdp")
        self.chip = self.own // 2
        self.core = lax.rem(self.own, 2)
        self.other = self.own + 1 - 2 * self.core
        self.has_left = self.chip > 0
        self.has_right = self.chip < chips - 1

    def greet(self):
        signal_group(self.other)
        pl.when(self.has_left)(lambda: signal_group(self.own - 2))
        pl.when(self.has_right)(lambda: signal_group(self.own + 2))
        return 1 + self.has_left.astype(jnp.int32) + self.has_right.astype(jnp.int32)


def signal_group(peer):
    barrier = pltpu.get_barrier_semaphore()
    pl.semaphore_signal(barrier, inc=1, device_id={"fsdp": peer}, device_id_type=MESH)


def signal_seq(peer):
    barrier = pltpu.get_barrier_semaphore()
    pl.semaphore_signal(barrier, inc=1, device_id={"seq": peer}, device_id_type=MESH)


def greet_group(group):
    own = lax.axis_index("fsdp")
    pl.loop(1, group)(lambda ahead: signal_group(lax.rem(own + ahead, group)))
    return group - 1


def greet_seq(seqs):
    own = lax.axis_index("seq")
    pl.loop(1, seqs)(lambda ahead: signal_seq(lax.rem(own + ahead, seqs)))
    return seqs - 1


def meet(count):
    pl.semaphore_wait(pltpu.get_barrier_semaphore(), count)


def rows_at(index, size):
    return pl.ds(pl.multiple_of(index * size, size), size)


class Spread:
    def __init__(self, line, first, buf, send, recv):
        self.line, self.first, self.buf, self.send, self.recv = line, first, buf, send, recv
        self.parts = recv.shape[1]
        self.size = first.shape[0] // self.parts

    def move(self, slot, part, way, peer, source=None):
        here = rows_at(part, self.size)
        return pltpu.make_async_remote_copy(
            src_ref=self.buf.at[slot, here] if source is None else source.at[here],
            dst_ref=self.buf.at[slot, here],
            send_sem=self.send.at[way, slot, part],
            recv_sem=self.recv.at[slot, part],
            device_id={"fsdp": peer},
            device_id_type=MESH,
        )

    def begin(self):
        line = self.line

        @pl.loop(0, self.parts)
        def _(part):
            pl.when(line.has_right)(
                lambda: self.move(line.own, part, 1, line.own + 2, self.first).start()
            )
            pl.when(line.has_left)(
                lambda: self.move(line.own, part, 0, line.own - 2, self.first).start()
            )
            self.move(line.own, part, 2, line.other, self.first).start()

    def relay_part(self, far, part):
        line = self.line

        @pl.when(line.chip - far >= 0)
        def _():
            slot = (line.chip - far) * 2 + line.core
            self.move(slot, part, 1, line.own).wait_recv()
            pl.when(line.has_right)(lambda: self.move(slot, part, 1, line.own + 2).start())
            self.move(slot, part, 2, line.other).start()

        @pl.when(line.chip + far < line.chips)
        def _():
            slot = (line.chip + far) * 2 + line.core
            self.move(slot, part, 0, line.own).wait_recv()
            pl.when(line.has_left)(lambda: self.move(slot, part, 0, line.own - 2).start())
            self.move(slot, part, 2, line.other).start()

    def relay(self, far):
        pl.loop(0, self.parts)(lambda part: self.relay_part(far, part))

    def across(self, slot):
        pl.loop(0, self.parts)(lambda part: self.move(slot, part, 2, self.line.own).wait_recv())

    def each(self, far, use):
        line = self.line

        @pl.loop(0, 4)
        def _(turn):
            side = lax.rem(turn, 2)
            over = turn // 2
            away = far - over
            source = line.chip + away * (2 * side - 1)
            valid = (away >= 0) & (away < line.chips) & (source >= 0) & (source < line.chips)
            valid = valid & ((side == 0) | (away > 0))

            @pl.when(valid)
            def _():
                slot = source * 2 + line.core + over * (1 - 2 * line.core)
                pl.when(over == 1)(lambda: self.across(slot))
                use(slot)

    def rest(self):
        pl.loop(0, self.line.chips)(lambda place: self.across(place * 2 + 1 - self.line.core))

    def sent(self):
        line = self.line

        @pl.loop(0, line.chips)
        def _(place):
            slot = place * 2 + line.core

            @pl.loop(0, self.parts)
            def _(part):
                self.move(slot, part, 2, line.other).wait_send()
                pl.when(line.has_right & (place <= line.chip))(
                    lambda: self.move(slot, part, 1, line.own + 2).wait_send()
                )
                pl.when(line.has_left & (place >= line.chip))(
                    lambda: self.move(slot, part, 0, line.own - 2).wait_send()
                )


class Reduce:
    def __init__(self, line, product, out, acc, cross_out, line_out, cross_in, line_in, send, recv):
        self.line, self.product, self.out, self.acc = line, product, out, acc
        self.cross_out, self.line_out, self.cross_in, self.line_in = cross_out, line_out, cross_in, line_in
        self.send, self.recv = send, recv
        self.tiles = line_out.shape[2] // TILE

    @staticmethod
    def scratch(chips, rows, width):
        part = pltpu.VMEM((chips, rows, width), jnp.bfloat16)
        return [
            pltpu.VMEM((rows, TILE), jnp.float32),
            pltpu.VMEM((2, rows, width), jnp.bfloat16),
            part,
            part,
            pltpu.VMEM((chips + 1, rows, width), jnp.bfloat16),
            pltpu.SemaphoreType.DMA((2, chips, width // TILE)),
            pltpu.SemaphoreType.DMA((2, chips + 1, width // TILE)),
        ]

    def cross(self, side, place, tile):
        here = rows_at(tile, TILE)
        return pltpu.make_async_remote_copy(
            src_ref=self.cross_out.at[side, :, here],
            dst_ref=self.cross_in.at[place, :, here],
            send_sem=self.send.at[0, place, tile],
            recv_sem=self.recv.at[0, place, tile],
            device_id={"fsdp": self.line.other},
            device_id_type=MESH,
        )

    def along(self, place, landing, tile, peer):
        here = rows_at(tile, TILE)
        return pltpu.make_async_remote_copy(
            src_ref=self.line_out.at[place, :, here],
            dst_ref=self.line_in.at[landing, :, here],
            send_sem=self.send.at[1, place, tile],
            recv_sem=self.recv.at[1, landing, tile],
            device_id={"fsdp": peer},
            device_id_type=MESH,
        )

    def where(self, away, side):
        line = self.line
        rightward = (line.chips - 1 - line.chip >= line.chip) == (side == 0)
        place = line.chip + jnp.where(rightward, away, -away)
        valid = (place >= 0) & (place < line.chips) & ((away > 0) | (side == 0))
        return valid, place, rightward

    def level(self, away, also):
        @pl.loop(0, 2)
        def _(side):
            valid, place, _ = self.where(away, side)

            @pl.when(valid)
            def _():
                @pl.loop(0, self.tiles)
                def _(tile):
                    got = self.product(place * 2 + 1 - self.line.core, tile)
                    self.cross_out[side, :, rows_at(tile, TILE)] = to_half(got)
                    self.cross(side, place, tile).start()

        @pl.loop(0, self.tiles)
        def _(tile):
            @pl.loop(0, 2)
            def _(side):
                valid, place, rightward = self.where(away, side)
                pl.when(valid)(lambda: self.close(away, side, place, rightward, tile))

            also(tile)

    def close(self, away, side, place, rightward, tile):
        line, acc = self.line, self.acc
        here = rows_at(tile, TILE)
        upstream = (rightward & line.has_left) | (jnp.logical_not(rightward) & line.has_right)
        acc[...] = self.product(place * 2 + line.core, tile)
        self.cross(side, place, tile).wait()
        acc[...] += self.cross_in[place, :, here].astype(jnp.float32)

        @pl.when(away > 0)
        def _():
            @pl.when(upstream)
            def _():
                self.along(place, place, tile, line.own).wait_recv()
                self.line_out[place, :, here] = to_half(
                    acc[...] + self.line_in[place, :, here].astype(jnp.float32)
                )

            @pl.when(jnp.logical_not(upstream))
            def _():
                self.line_out[place, :, here] = to_half(acc[...])

            @pl.when(rightward)
            def _():
                self.along(place, place, tile, line.own + 2).start()

            @pl.when(jnp.logical_not(rightward))
            def _():
                landing = jnp.where(away == 1, line.chips, place)
                self.along(place, landing, tile, line.own - 2).start()

        @pl.when(away == 0)
        def _():
            self.out[:, here] = acc[...]

            @pl.when(line.has_left)
            def _():
                self.along(place, place, tile, line.own).wait_recv()
                self.out[:, here] += self.line_in[place, :, here].astype(jnp.float32)

            @pl.when(line.has_right)
            def _():
                self.along(place, line.chips, tile, line.own).wait_recv()
                self.out[:, here] += self.line_in[line.chips, :, here].astype(jnp.float32)

    def sent(self):
        @pl.loop(0, self.line.chips)
        def _(place):
            @pl.when(place != self.line.chip)
            def _():
                pl.loop(0, self.tiles)(
                    lambda tile: self.along(place, place, tile, self.line.own).wait_send()
                )


class Swap:
    def __init__(self, group, source, target, send, recv, keep):
        self.group, self.source, self.target = group, source, target
        self.send, self.recv, self.keep = send, recv, keep
        self.own = lax.axis_index("fsdp")

    def move(self, peer, source):
        return pltpu.make_async_remote_copy(
            src_ref=self.source.at[peer],
            dst_ref=self.target.at[source],
            send_sem=self.send.at[peer],
            recv_sem=self.recv.at[source],
            device_id={"fsdp": peer},
            device_id_type=MESH,
        )

    def kept(self):
        return pltpu.make_async_copy(self.source.at[self.own], self.target.at[self.own], self.keep)

    def begin(self):
        self.kept().start()
        pl.loop(1, self.group)(
            lambda ahead: self.move(lax.rem(self.own + ahead, self.group), self.own).start()
        )

    def end(self):
        self.kept().wait()

        @pl.loop(1, self.group)
        def _(ahead):
            peer = lax.rem(self.own + ahead, self.group)
            self.move(peer, peer).wait_recv()
            self.move(peer, self.own).wait_send()


class Share:
    def __init__(self, seqs, source, target, send, recv, keep):
        self.seqs, self.source, self.target = seqs, source, target
        self.send, self.recv, self.keep = send, recv, keep
        self.own = lax.axis_index("seq")
        self.parts = send.shape[2]
        self.size = source.shape[0] // self.parts

    def move(self, peer, place, part):
        here = pl.ds(part * self.size, self.size)
        return pltpu.make_async_remote_copy(
            src_ref=self.source.at[here],
            dst_ref=self.target.at[place, here],
            send_sem=self.send.at[peer, 0, part],
            recv_sem=self.recv.at[place, 0, part],
            device_id={"seq": peer},
            device_id_type=MESH,
        )

    def relay(self, peer, place, part, side):
        here = pl.ds(part * self.size + side * (self.size // 2), self.size // 2)
        return pltpu.make_async_remote_copy(
            src_ref=self.target.at[place, here],
            dst_ref=self.target.at[place, here],
            send_sem=self.send.at[peer, 1, part],
            recv_sem=self.recv.at[place, side, part],
            device_id={"seq": peer},
            device_id_type=MESH,
        )

    def near(self):
        one = self.own + 1 - 2 * lax.rem(self.own, 2)
        two = lax.rem(self.own + 2, 4)
        return one, two, lax.rem(one + 2, 4)

    def kept(self):
        return pltpu.make_async_copy(self.source, self.target.at[self.own], self.keep)

    def begin(self):
        self.kept().start()
        for part in range(self.parts):
            if self.seqs == 4:
                one, two, _ = self.near()
                self.move(one, self.own, part).start()
                self.move(two, self.own, part).start()
            else:
                pl.loop(1, self.seqs)(
                    lambda ahead, part=part: self.move(
                        lax.rem(self.own + ahead, self.seqs), self.own, part
                    ).start()
                )

    def pass_on(self, parts):
        if self.seqs == 4:
            one, two, _ = self.near()
            for part in parts:
                self.move(one, one, part).wait_recv()
                self.relay(two, one, part, 0).start()
                self.move(two, two, part).wait_recv()
                self.relay(one, two, part, 1).start()

    def end(self):
        self.kept().wait()
        for part in range(self.parts):
            if self.seqs == 4:
                one, two, far = self.near()
                self.relay(two, far, part, 0).wait_recv()
                self.relay(one, far, part, 1).wait_recv()
                self.move(one, self.own, part).wait_send()
                self.move(two, self.own, part).wait_send()
                self.relay(two, one, part, 0).wait_send()
                self.relay(one, two, part, 1).wait_send()
            else:

                @pl.loop(1, self.seqs)
                def _(ahead, part=part):
                    peer = lax.rem(self.own + ahead, self.seqs)
                    self.move(peer, peer, part).wait_recv()
                    self.move(peer, self.own, part).wait_send()


def seq_peers(seqs):
    own = lax.axis_index("seq")
    if seqs == 4:
        one = own + 1 - 2 * lax.rem(own, 2)
        return [one, lax.rem(own + 2, 4)], [lax.rem(one + 2, 4)]
    ahead = [lax.rem(own + step, seqs) for step in range(1, seqs)]
    return ahead[:1], ahead[1:]


def near_count(seqs):
    return 2 if seqs == 4 else 1


class ToPeers:
    def __init__(self, seqs, peers, source, target, send, recv, first=0):
        self.peers, self.source, self.target, self.send, self.recv = peers, source, target, send, recv
        self.run, self.first = source.shape[0] // seqs, first

    def move(self, index):
        begin = pl.multiple_of(self.peers[index] * self.run + self.first, 16)
        return pltpu.make_async_remote_copy(
            src_ref=self.source.at[pl.ds(begin, self.target.shape[1])],
            dst_ref=self.target.at[index],
            send_sem=self.send.at[index],
            recv_sem=self.recv.at[index],
            device_id={"seq": self.peers[index]},
            device_id_type=MESH,
        )

    def begin(self):
        for index in range(len(self.peers)):
            self.move(index).start()

    def arrived(self):
        for index in range(len(self.peers)):
            self.move(index).wait_recv()

    def sent(self):
        for index in range(len(self.peers)):
            self.move(index).wait_send()

    def end(self):
        self.arrived()
        self.sent()


def load_halves(halves, target, load):
    copies = []
    rows = halves[0].shape[1]
    for index, half in enumerate(halves):
        for place in range(half.shape[0]):
            there = pl.ds((2 * place + index) * rows, rows)
            copies.append(pltpu.make_async_copy(half.at[place], target.at[there], load.at[index, place]))
    return copies


VMEM_SPEC = pl.BlockSpec(memory_space=pltpu.VMEM)
ANY_SPEC = pl.BlockSpec(memory_space=pl.ANY)


def comm_params(collective, mib=58):
    return pltpu.CompilerParams(
        collective_id=collective, has_side_effects=True, vmem_limit_bytes=mib * MIB
    )


def cost(flops, local, remote):
    return pl.CostEstimate(
        flops=flops, bytes_accessed=local, transcendentals=0, remote_bytes_transferred=remote
    )


def sems(*shape):
    return pltpu.SemaphoreType.DMA(shape)


def left_rows(a_ref, slot, rows):
    if len(a_ref.shape) == 2:
        return a_ref[rows_at(slot, rows), :]
    piece = rows // a_ref.shape[0]
    return jnp.concatenate(
        [a_ref[batch, rows_at(slot, piece), :] for batch in range(a_ref.shape[0])], axis=0
    )


def norm_back(rows, v_ref, e_ref, gain_ref, gain_acc, put):
    @pl.loop(0, rows // 32)
    def _(chunk):
        here = rows_at(chunk, 32)
        values = v_ref[here, :].astype(jnp.float32)
        error = e_ref[here, :]
        rate = lax.rsqrt(jnp.mean(values * values, axis=-1, keepdims=True) + EPS)
        unit = values * rate
        product = error * unit
        gain = gain_ref[0:1, :]
        mean = jnp.mean(product * gain, axis=-1, keepdims=True)
        gain_acc[...] += (product[0:8] + product[8:16]) + (product[16:24] + product[24:32])
        put(here, rate * (gain * error - unit * mean))


def add_from_seq(own_rows, got, here):
    added = own_rows.astype(jnp.float32)
    for index in range(got.shape[0]):
        added = added + got[index, here, :].astype(jnp.float32)
    return added


def column_parts(seqs, group, share, span):
    size = HEAD if share == HEAD else span
    parts = []
    for member in range(group):
        for run in range(span // size):
            home = (run * group + member) * size
            parts.append((member, run * size, home, size))
    return parts


def start_kernel(
    seqs, chips, batches, block, tile_ref, x_ref, wq_ref, wk_ref, wv_ref, gate_hbm, up_hbm, down_hbm, low_ref,
    g_ref, q_ref, out_ref, lse_ref, pad_ref, gains_ref, w_out_ref, own_units_ref, wd_ref,
    gate, up, units, blocks_ref, buf, normed, pad, vt, gain, gains, w,
    unit_sem, send, recv, keep, swap_send, share_send, w_recv,
    tile_send, tile_across, tile_recv, tile_back, w_keep, gain_keep,
    halo_send, halo_recv, pad_keep, unit_send, unit_recv, unit_keep,
    down_send, down_recv, down_keep,
):
    line = Line(chips)
    group = 2 * chips
    seq = lax.axis_index("seq")
    own = line.own
    share = blocks_ref.shape[1]
    rows, width = x_ref.shape
    piece = rows // batches
    length, span = q_ref.shape[1:]
    per = 128 * seqs * group // width
    steps, need = length // block, WINDOW // block
    has_left, has_right = seq > 0, seq < seqs - 1
    unit_loads = [
        pltpu.make_async_copy(gate_hbm, gate, unit_sem.at[0]),
        pltpu.make_async_copy(up_hbm, up, unit_sem.at[1]),
    ]
    for item in unit_loads:
        item.start()
    for index, source in enumerate((wq_ref, wk_ref, wv_ref)):
        for member, first, home, size in column_parts(seqs, group, share, span):
            first = first + index * span
            blocks_ref[member, :, first : first + size] = source[:, home : home + size]
    meet(greet_group(group) + greet_seq(seqs))

    def block_at(run, member):
        return w.at[rows_at(run * group + member, share)]

    def block_swap(peer, member):
        return pltpu.make_async_remote_copy(
            src_ref=blocks_ref.at[peer],
            dst_ref=block_at(seq, member),
            send_sem=swap_send.at[peer],
            recv_sem=w_recv.at[seq, member],
            device_id={"fsdp": peer},
            device_id_type=MESH,
        )

    def block_share(run, member, peer):
        return pltpu.make_async_remote_copy(
            src_ref=block_at(run, member),
            dst_ref=block_at(run, member),
            send_sem=share_send.at[peer, member],
            recv_sem=w_recv.at[run, member],
            device_id={"seq": peer},
            device_id_type=MESH,
        )

    def tile_to_seq(peer, place):
        return pltpu.make_async_remote_copy(
            src_ref=tile_ref.at[0],
            dst_ref=gains.at[own, place],
            send_sem=tile_send.at[peer],
            recv_sem=tile_recv.at[place],
            device_id={"seq": peer},
            device_id_type=MESH,
        )

    def tiles_to_group(peer, member):
        return pltpu.make_async_remote_copy(
            src_ref=gains.at[member],
            dst_ref=gains.at[member],
            send_sem=tile_across.at[peer],
            recv_sem=tile_back.at[member],
            device_id={"fsdp": peer},
            device_id_type=MESH,
        )

    def others(count, me, act):
        pl.loop(1, count)(lambda ahead: act(lax.rem(me + ahead, count)))

    others(seqs, seq, lambda peer: tile_to_seq(peer, seq).start())
    down = Share(
        seqs, down_hbm.at[pl.ds(0, wd_ref.shape[1])], wd_ref, down_send, down_recv, down_keep
    )
    down.begin()
    others(group, own, lambda peer: block_swap(peer, own).start())
    spreads = [
        Spread(line, x_ref.at[pl.ds(batch * piece, piece)], buf.at[batch], send.at[batch], recv.at[batch])
        for batch in range(batches)
    ]
    spreads[0].begin()
    gains[own, seq] = tile_ref[0]
    w[rows_at(seq * group + own, share), :] = blocks_ref[own]
    others(seqs, seq, lambda peer: block_share(seq, own, peer).start())
    for batch in range(batches):
        buf[batch, own] = x_ref[batch * piece : (batch + 1) * piece, :]
    others(seqs, seq, lambda peer: tile_to_seq(peer, peer).wait_recv())
    others(group, own, lambda peer: tiles_to_group(peer, own).start())
    for item in unit_loads:
        item.wait()
    cell = units.shape[2] // 2 // seqs
    for member in range(group):
        for run in range(seqs):
            home = (run * group + member) * cell
            for index, source in enumerate((gate, up)):
                first = (index * seqs + run) * cell
                units[member, :, first : first + cell] = source[:, home : home + cell]
    unit_swap = Swap(group, units, own_units_ref, unit_send, unit_recv, unit_keep)

    @pl.when(jnp.logical_not(has_left))
    def _():
        pad[:, :WINDOW, :] = jnp.zeros((batches, WINDOW, 2 * span), jnp.bfloat16)

    def pass_block(member):
        block_swap(member, member).wait_recv()
        others(seqs, seq, lambda peer: block_share(seq, member, peer).start())

    others(group, own, pass_block)
    down.pass_on([0])
    others(group, own, lambda peer: tiles_to_group(peer, peer).wait_recv())
    for column in range(width // 128):
        total = 0.0
        for place in range(column * per, (column + 1) * per):
            total = total + gains[place % group, place // group, 0:1, :]
        gain[0:1, column * 128 : (column + 1) * 128] = total

    def sides(far, act):
        @pl.loop(0, 2)
        def _(side):
            place = line.chip + far * (2 * side - 1)
            valid = (place >= 0) & (place < chips) & ((side == 0) | (far > 0))
            pl.when(valid)(lambda: act(place))

    def kept(batch, place):
        here = rows_at(place, block)
        return pltpu.make_async_copy(
            normed.at[batch, here], g_ref.at[batch, here], keep.at[batch, place]
        )

    def norm_pair(batch, place):
        spreads[batch].across(place * 2 + 1 - line.core)

        @pl.loop(0, 2)
        def _(member):
            @pl.loop(0, piece // 64)
            def _(chunk):
                values = buf[batch, place * 2 + member, rows_at(chunk, 64), :].astype(jnp.float32)
                there = pl.multiple_of(place * block + member * piece + chunk * 64, 64)
                normed[batch, pl.ds(there, 64), :] = to_half(normalize(values, gain[0:1, :]))

        kept(batch, place).start()

    def halo(batch, step, peer):
        there = pl.multiple_of(WINDOW + (step + steps - need) * block, block)
        return pltpu.make_async_remote_copy(
            src_ref=pad.at[batch, pl.ds(there, block)],
            dst_ref=pad.at[batch, rows_at(step, block)],
            send_sem=halo_send.at[batch, step],
            recv_sem=halo_recv.at[batch, step],
            device_id={"seq": peer},
            device_id_type=MESH,
        )

    def project(batch, place):
        here = rows_at(place, block)
        got = to_half(dot_nn(normed[batch, here, :], w[...]))
        q_ref[batch, here, :] = got[:, :span]
        pad[batch, pl.ds(pl.multiple_of(WINDOW + place * block, block), block), :] = got[:, span:]

        @pl.when(has_right & (place >= steps - need))
        def _():
            halo(batch, place - (steps - need), seq + 1).start()

    @pl.loop(0, chips)
    def _(far):
        pl.when(far > 0)(lambda: spreads[0].relay(far))
        pl.when(far == chips - 2)(spreads[1].begin)
        sides(far, lambda place: norm_pair(0, place))

    spreads[1].relay(1)

    def have_block(run, member):
        block_share(run, member, seq).wait_recv()

    others(seqs, seq, lambda run: pl.loop(0, group)(lambda member: have_block(run, member)))
    w_kept = pltpu.make_async_copy(w, w_out_ref, w_keep)
    w_kept.start()
    gains_kept = pltpu.make_async_copy(gains, gains_ref, gain_keep)
    gains_kept.start()
    pl.loop(0, steps)(lambda place: project(0, place))

    @pl.loop(2, chips)
    def _(far):
        spreads[1].relay(far)

    unit_swap.begin()

    @pl.loop(0, chips)
    def _(far):
        sides(far, lambda place: norm_pair(1, place))
        sides(far, lambda place: project(1, place))

    def pad_kept(batch):
        return pltpu.make_async_copy(pad.at[batch], pad_ref.at[batch], pad_keep.at[batch])

    for batch in range(batches):
        vt[:, WINDOW:] = pad[batch, WINDOW:, span:].T

        @pl.loop(0, steps)
        def _(turn, batch=batch):
            step = steps - 1 - turn

            @pl.when(step < need)
            def _():
                arrived = rows_at(step, block)
                pl.when(has_left)(lambda: halo(batch, step, seq).wait_recv())
                vt[:, arrived] = pad[batch, arrived, span:].T

            begin = pl.multiple_of(step * block, block)
            keys = pl.ds(begin, block + WINDOW)
            rows = pl.ds(begin, block)
            low = low_ref[batch, :, rows]
            for pair in range(span // PAIR):
                lanes = slice(pair * PAIR, (pair + 1) * PAIR)
                q_pair = q_ref[batch, rows, lanes] * jnp.asarray(HEAD**-0.5, jnp.bfloat16)
                k_rows = pad[batch, keys, lanes]
                values = vt[lanes, keys]
                mixed = []
                for half in range(2):
                    scores = masked_scores(k_rows, head_lanes(q_pair, half), low)
                    top = jnp.max(scores, axis=0, keepdims=True)
                    expo = jnp.exp(scores - top)
                    total = jnp.sum(expo, axis=0, keepdims=True)
                    mixed.append(dot_nn(values, to_half(expo)) / total)
                    row = pair * 2 + half
                    lse_ref[batch, row : row + 1, rows] = top + jnp.log(total)
                lane = lax.broadcasted_iota(jnp.int32, mixed[0].shape, 0)
                out_ref[batch, rows, lanes] = to_half(jnp.where(lane < HEAD, mixed[0], mixed[1]).T)

        pad_kept(batch).start()

    for batch in range(batches):
        spreads[batch].sent()
    others(seqs, seq, lambda peer: tile_to_seq(peer, seq).wait_send())
    others(group, own, lambda peer: block_swap(peer, own).wait_send())
    others(group, own, lambda peer: tiles_to_group(peer, own).wait_send())
    others(
        seqs,
        seq,
        lambda peer: pl.loop(0, group)(lambda member: block_share(seq, member, peer).wait_send()),
    )

    @pl.loop(0, need)
    def _(step):
        for batch in range(batches):
            pl.when(has_right)(lambda batch=batch: halo(batch, step, seq).wait_send())

    w_kept.wait()
    gains_kept.wait()
    unit_swap.end()
    down.end()
    for batch in range(batches):
        pad_kept(batch).wait()

        @pl.loop(0, steps)
        def _(place, batch=batch):
            kept(batch, place).wait()


def start(seqs, chips, batches, block, tile, x, weights, unit_weights, down, low, collective):
    rows, width = x.shape
    group = 2 * chips
    length = group * rows // batches
    share = weights[0].shape[0]
    span = width // group
    cols = 3 * span
    wide = unit_weights[0].shape[1]
    cells = 2 * wide // group
    piece = rows // batches
    padded = length + WINDOW
    half = jnp.bfloat16
    need = WINDOW // block
    return pl.pallas_call(
        functools.partial(start_kernel, seqs, chips, batches, block),
        out_shape=[
            jax.ShapeDtypeStruct((batches, length, width), half),
            jax.ShapeDtypeStruct((batches, length, span), half),
            jax.ShapeDtypeStruct((batches, length, span), half),
            jax.ShapeDtypeStruct((batches, span // HEAD, length), jnp.float32),
            jax.ShapeDtypeStruct((batches, padded, 2 * span), half),
            jax.ShapeDtypeStruct((group, seqs, 8, 128), jnp.float32),
            jax.ShapeDtypeStruct((width, cols), half),
            jax.ShapeDtypeStruct((group, share, cells), half),
            jax.ShapeDtypeStruct((seqs, down.shape[0] // 2, width), half),
        ],
        in_specs=[VMEM_SPEC] * 5 + [ANY_SPEC] * 2 + [VMEM_SPEC] * 2,
        out_specs=[ANY_SPEC] + [VMEM_SPEC] * 3 + [ANY_SPEC] * 5,
        scratch_shapes=[
            pltpu.VMEM((share, wide), half),
            pltpu.VMEM((share, wide), half),
            pltpu.VMEM((group, share, cells), half),
            pltpu.VMEM((group, share, cols), half),
            pltpu.VMEM((batches, group, piece, width), half),
            pltpu.VMEM((batches, length, width), half),
            pltpu.VMEM((batches, padded, 2 * span), half),
            pltpu.VMEM((span, padded), half),
            pltpu.VMEM((8, width), jnp.float32),
            pltpu.VMEM((group, seqs, 8, 128), jnp.float32),
            pltpu.VMEM((width, cols), half),
            sems(2),
            sems(batches, 3, group, PARTS // 2),
            sems(batches, group, PARTS // 2),
            sems(batches, chips),
            sems(group),
            sems(seqs, group),
            sems(seqs, group),
            sems(seqs),
            sems(group),
            sems(seqs),
            sems(group),
            pltpu.SemaphoreType.DMA,
            pltpu.SemaphoreType.DMA,
            sems(batches, need),
            sems(batches, need),
            sems(batches),
            sems(group),
            sems(group),
            pltpu.SemaphoreType.DMA,
            sems(seqs, 2, 1),
            sems(seqs, 2, 1),
            pltpu.SemaphoreType.DMA,
        ],
        compiler_params=comm_params(collective, 62),
        cost_estimate=cost(
            2 * group * rows * width * cols + 8 * batches * length * span * (WINDOW + block),
            300 * MIB,
            2 * group * rows * width * 2,
        ),
        name="start",
    )(tile, x, *weights, *unit_weights, down, low)


def branch_kernel(
    seqs, chips, a_ref, w_ref, d_ref, units_ref, down_hbm, x_ref, gain_ref,
    middle_ref, normed_ref, gd_ref, w_units_ref, wd_ref,
    out_ref, acc, cross_out, line_out, cross_in, line_in, sum_send, sum_recv,
    send, recv, d_keep, share_send, share_recv, share_keep,
    down_send, down_recv, down_keep,
):
    line = Line(chips)
    rows = out_ref.shape[0]

    def product(slot, tile):
        return dot_nn(left_rows(a_ref, slot, rows), w_ref[:, rows_at(tile, TILE)])

    meet(line.greet() + greet_seq(seqs))
    reduce = Reduce(
        line, product, out_ref, acc, cross_out, line_out, cross_in, line_in, sum_send, sum_recv
    )
    spread = Spread(line, d_ref, gd_ref, send, recv)
    units = Share(seqs, units_ref, w_units_ref, share_send, share_recv, share_keep)
    d_kept = pltpu.make_async_copy(d_ref, gd_ref.at[line.own], d_keep)
    half = wd_ref.shape[1]
    down = Share(seqs, down_hbm.at[pl.ds(half, half)], wd_ref, down_send, down_recv, down_keep)
    down.begin()
    units.begin()
    spread.begin()
    d_kept.start()

    @pl.loop(0, chips)
    def _(step):
        def also(tile):
            @pl.when((step == chips // 2) & (tile == 0))
            def _():
                down.pass_on([0])
                units.pass_on([0])

            pl.when(step < chips - 1)(lambda: spread.relay_part(step + 1, tile))

        reduce.level(chips - 1 - step, also)


    @pl.loop(0, rows // 32)
    def _(chunk):
        here = rows_at(chunk, 32)
        middle = x_ref[here, :].astype(jnp.float32) + out_ref[here, :]
        middle_ref[here, :] = middle
        normed_ref[here, :] = to_half(normalize(middle, gain_ref[0:1, :]))

    spread.rest()
    spread.sent()
    reduce.sent()
    d_kept.wait()
    units.end()
    down.end()


def branch_sum(seqs, chips, a, w, d_rows, units, down, x, gain, collective):
    rows, width = d_rows.shape
    group = 2 * chips
    half = jnp.bfloat16
    return pl.pallas_call(
        functools.partial(branch_kernel, seqs, chips),
        out_shape=[
            jax.ShapeDtypeStruct((rows, width), jnp.float32),
            jax.ShapeDtypeStruct((rows, width), half),
            jax.ShapeDtypeStruct((group, rows, width), half),
            jax.ShapeDtypeStruct((seqs,) + units.shape, half),
            jax.ShapeDtypeStruct((seqs, down.shape[0] // 2, width), half),
        ],
        in_specs=[VMEM_SPEC] * 7,
        out_specs=[VMEM_SPEC, VMEM_SPEC] + [ANY_SPEC] * 3,
        scratch_shapes=[pltpu.VMEM((rows, width), jnp.float32)]
        + Reduce.scratch(chips, rows, width)
        + [sems(3, group, PARTS), sems(group, PARTS), pltpu.SemaphoreType.DMA]
        + [sems(seqs, 2, 1), sems(seqs, 2, 1), pltpu.SemaphoreType.DMA] * 2,
        compiler_params=comm_params(collective),
        cost_estimate=cost(
            2 * group * rows * width * w.shape[0], 250 * MIB, 3 * group * rows * width * 2
        ),
        name="branch_sum",
    )(a, w, d_rows, units, down, x, gain)


class PairReduce:
    def __init__(self, line, product, out, acc, keep, cross_out, cross_in, line_out, line_in, send, recv):
        self.line, self.product, self.out, self.acc, self.keep = line, product, out, acc, keep
        self.cross_out, self.cross_in, self.line_out, self.line_in = cross_out, cross_in, line_out, line_in
        self.send, self.recv = send, recv
        self.tiles = keep.shape[1] // TILE

    @staticmethod
    def scratch(chips, piece, width):
        half = jnp.bfloat16
        return [
            pltpu.VMEM((piece, width), half),
            pltpu.VMEM((2, piece, width), half),
            pltpu.VMEM((2, piece, width), half),
            pltpu.VMEM((chips + 1, piece, width), half),
            pltpu.SemaphoreType.DMA((3, width // TILE)),
            pltpu.SemaphoreType.DMA((chips + 3, width // TILE)),
        ]

    def cross(self, parity, tile):
        here = rows_at(tile, TILE)
        return pltpu.make_async_remote_copy(
            src_ref=self.cross_out.at[:, here],
            dst_ref=self.cross_in.at[parity, :, here],
            send_sem=self.send.at[0, tile],
            recv_sem=self.recv.at[self.line.chips + 1 + parity, tile],
            device_id={"fsdp": self.line.other},
            device_id_type=MESH,
        )

    def along(self, parity, landing, tile, peer):
        here = rows_at(tile, TILE)
        return pltpu.make_async_remote_copy(
            src_ref=self.line_out.at[parity, :, here],
            dst_ref=self.line_in.at[landing, :, here],
            send_sem=self.send.at[1 + parity, tile],
            recv_sem=self.recv.at[landing, tile],
            device_id={"fsdp": peer},
            device_id_type=MESH,
        )

    def steps(self):
        return 2 * self.line.chips - 1

    def step(self, step):
        line, keep = self.line, self.keep
        piece = keep.shape[0]
        right_side = line.chips - 1 - line.chip
        away = line.chips - 1 - step // 2
        second = lax.rem(step, 2)
        rightward = (right_side >= line.chip) == (second == 0)
        place = line.chip + jnp.where(rightward, away, -away)
        longer = jnp.maximum(right_side, line.chip)
        shorter = jnp.minimum(right_side, line.chip)
        count = longer - away + jnp.maximum(shorter - away, 0) + second
        parity = lax.rem(count + 2 * line.chips, 2)
        upstream = (rightward & line.has_left) | (jnp.logical_not(rightward) & line.has_right)

        @pl.when((place >= 0) & (place < line.chips))
        def _():
            wide = self.acc.shape[1]

            @pl.loop(0, keep.shape[1] // wide)
            def _(tile):
                here = rows_at(tile, wide)
                self.acc[...] = self.product(place, here)
                self.cross_out[:, here] = to_half(self.acc[rows_at(1 - line.core, piece), :])
                keep[:, here] = self.acc[rows_at(line.core, piece), :]
                for piece_of in range(wide // TILE):
                    self.cross(parity, tile * (wide // TILE) + piece_of).start()

            @pl.loop(0, self.tiles)
            def _(tile):
                here = rows_at(tile, TILE)
                self.cross(parity, tile).wait()
                keep[:, here] += self.cross_in[parity, :, here].astype(jnp.float32)

                @pl.when(away > 0)
                def _():
                    pl.when(count >= 2)(
                        lambda: self.along(parity, place, tile, line.own).wait_send()
                    )

                    @pl.when(upstream)
                    def _():
                        self.along(parity, place, tile, line.own).wait_recv()
                        self.line_out[parity, :, here] = to_half(
                            keep[:, here] + self.line_in[place, :, here].astype(jnp.float32)
                        )

                    @pl.when(jnp.logical_not(upstream))
                    def _():
                        self.line_out[parity, :, here] = to_half(keep[:, here])

                    @pl.when(rightward)
                    def _():
                        self.along(parity, place, tile, line.own + 2).start()

                    @pl.when(jnp.logical_not(rightward))
                    def _():
                        landing = jnp.where(away == 1, line.chips, place)
                        self.along(parity, landing, tile, line.own - 2).start()

                @pl.when(away == 0)
                def _():
                    self.out[:, here] = keep[:, here]

                    @pl.when(line.has_left)
                    def _():
                        self.along(parity, place, tile, line.own).wait_recv()
                        self.out[:, here] += self.line_in[place, :, here].astype(jnp.float32)

                    @pl.when(line.has_right)
                    def _():
                        self.along(parity, line.chips, tile, line.own).wait_recv()
                        self.out[:, here] += self.line_in[line.chips, :, here].astype(jnp.float32)

    def sent(self):
        for count in range(max(self.line.chips - 3, 0), self.line.chips - 1):
            pl.loop(0, self.tiles)(
                lambda tile, parity=count % 2: self.along(parity, 0, tile, self.line.own).wait_send()
            )


def feed_kernel(
    seqs, chips, batches, x_ref, w_hbm, wd_one, wd_two, gd_hbm, v_ref, cot_ref, gain_ref,
    dm_ref, db_ref, gain_grad_ref, hidden_hbm, grad_hbm, grad_in,
    buf, d_buf, h_buf, w_ref, wd_ref, d_ref, tiles, totals, acc, keep,
    load, d_sem, h_sem, tile_sem, send, recv, part_send, part_recv, wd_load, *sums,
):
    line = Line(chips)
    rows, width = x_ref.shape
    piece = rows // batches
    pair = 2 * piece
    units = wd_ref.shape[0]
    part = min(units, 2 * TILE)
    block = tiles.shape[1]
    loads = [
        pltpu.make_async_copy(w_hbm, w_ref, load.at[0]),
    ] + load_halves([wd_one, wd_two], wd_ref, wd_load)
    for item in loads:
        item.start()
    meet(line.greet() + greet_seq(seqs))
    spreads = [
        Spread(
            line,
            x_ref.at[pl.ds(batch * piece, piece)],
            buf.at[batch],
            send.at[batch],
            recv.at[batch],
        )
        for batch in range(batches)
    ]
    spreads[0].begin()
    for batch in range(batches):
        buf[batch, line.own] = x_ref[batch * piece : (batch + 1) * piece, :]

    def fetch(batch, place, side):
        return [
            pltpu.make_async_copy(
                gd_hbm.at[place * 2 + core, pl.ds(batch * piece, piece)],
                d_buf.at[side, pl.ds(core * piece, piece)],
                d_sem.at[side, core],
            )
            for core in range(2)
        ]

    def stored(batch, place):
        return [
            pltpu.make_async_copy(
                h_buf.at[pl.ds(core * piece, piece)],
                hidden_hbm.at[
                    pl.ds(pl.multiple_of((place * 2 + core) * rows + batch * piece, piece), piece)
                ],
                h_sem.at[core],
            )
            for core in range(2)
        ]

    def sides(far, act):
        @pl.loop(0, 2)
        def _(side):
            place = line.chip + far * (2 * side - 1)
            valid = (place >= 0) & (place < chips) & ((side == 0) | (far > 0))
            pl.when(valid)(lambda: act(place, side))

    def take(batch, far):
        def begin(place, side):
            for item in fetch(batch, place, side):
                item.start()

        sides(far, begin)
        pl.when(far > 0)(lambda: spreads[batch].relay(far))

    def compute(batch, far):
        def act(place, side):
            spreads[batch].across(place * 2 + 1 - line.core)
            for item in fetch(batch, place, side):
                item.wait()

            def free():
                for item in stored(batch, place):
                    item.wait()

            if batch:
                free()
            else:
                pl.when((far > 0) | (side > 0))(free)
            there = rows_at(place, pair)

            @pl.loop(0, units // part)
            def _(tile):
                first = rows_at(tile, part)
                second = rows_at(units // part + tile, part)
                values = buf[batch, pl.ds(place * 2, 2), :, :].reshape(pair, width)
                gate = dot_nn(values, w_ref[:, first])
                up = dot_nn(values, w_ref[:, second])
                d_hidden = dot_nt(d_buf[side], wd_ref[first, :])
                sigma = jax.nn.sigmoid(gate)
                swish = gate * sigma
                h_buf[:, first] = to_half(swish * up)
                slope = sigma * (1.0 + gate * (1.0 - sigma))
                d_ref[batch, there, first] = to_half(d_hidden * up * slope)
                d_ref[batch, there, second] = to_half(d_hidden * swish)

            for item in stored(batch, place):
                item.start()

        sides(far, act)

    def product(batch):
        def get(place, here):
            return dot_nt(d_ref[batch, rows_at(place, pair), :], w_ref[here, :])

        return get

    reduces = [
        PairReduce(line, product(batch), totals.at[batch], acc, keep, *sums[6 * batch : 6 * batch + 6])
        for batch in range(batches)
    ]

    count = width // block
    seq = lax.axis_index("seq")

    near, far_off = seq_peers(seqs)
    soon = len(near)
    order = [peer * 2 for peer in near] + [peer * 2 for peer in far_off] + [seq * 2]
    order = order + [peer * 2 + 1 for peer in near] + [peer * 2 + 1 for peer in far_off] + [seq * 2 + 1]

    def tile_at(turn):
        tile = order[-1]
        for index in range(len(order) - 1):
            tile = jnp.where(turn == index, order[index], tile)
        return tile

    def grad_stored(turn):
        slot = lax.rem(turn, 2)
        return pltpu.make_async_copy(
            tiles.at[slot], grad_hbm.at[rows_at(tile_at(turn), block)], tile_sem.at[slot]
        )

    parts = ToPeers(seqs, near, grad_hbm, grad_in, part_send, part_recv)

    def leave(turn):
        grad_stored(turn).wait()
        for index in range(soon):
            pl.when(turn == index)(lambda index=index: parts.move(index).start())

    def weight_grad(turn):
        slot = lax.rem(turn, 2)
        size = min(4 * TILE, 2 * units)
        tile = tile_at(turn)

        @pl.loop(0, 2 * units // size)
        def _(column):
            here = rows_at(column, size)
            got = 0.0
            for batch in range(batches):
                left = buf[batch, :, :, rows_at(tile, block)].reshape(2 * chips * piece, block)
                got = got + contract_rows(left, d_ref[batch, :, here])
            tiles[slot, :, here] = to_half(got)

        pl.when(turn > 0)(lambda: leave(turn - 1))
        grad_stored(turn).start()

    def norm_batch(batch):
        own = pl.ds(batch * piece, piece)

        def put(here, d_values):
            there = pl.ds(pl.multiple_of(here.start + batch * piece, here.size), here.size)
            d_middle = cot_ref[there, :].astype(jnp.float32) + d_values
            dm_ref[there, :] = d_middle
            db_ref[there, :] = to_half(d_middle)

        norm_back(piece, v_ref.at[own], totals.at[batch], gain_ref, gain_grad_ref, put)

    gain_grad_ref[...] = jnp.zeros_like(gain_grad_ref)
    for item in loads:
        item.wait()
    last = 2 * chips - 2

    @pl.loop(0, chips)
    def _(far):
        take(0, far)
        pl.when(far == chips - 2)(spreads[1].begin)
        compute(0, far)

    @pl.loop(0, chips - 1)
    def _(far):
        take(1, far)
        reduces[0].step(2 * far)
        reduces[0].step(2 * far + 1)
        compute(1, far)

    take(1, chips - 1)
    compute(1, chips - 1)

    @pl.loop(0, 2)
    def _(step):
        reduces[1].step(step)
        weight_grad(step)

    reduces[0].step(last)
    norm_batch(0)

    @pl.loop(2, last)
    def _(step):
        reduces[1].step(step)
        pl.when(step < count)(lambda: weight_grad(step))

    @pl.loop(last, max(count, last))
    def _(tile):
        weight_grad(tile)

    reduces[1].step(last)
    norm_batch(1)
    for batch in range(batches):
        spreads[batch].sent()
        reduces[batch].sent()
    for item in stored(1, 0):
        item.wait()
    leave(count - 1)
    parts.end()


def feed_forward(seqs, chips, batches, x, w, wd_halves, group_d, middle, cot, gain, collective):
    rows, width = x.shape
    group = 2 * chips
    units = w.shape[1] // 2
    piece = rows // batches
    block = width // seqs // 2
    half = jnp.bfloat16
    return pl.pallas_call(
        functools.partial(feed_kernel, seqs, chips, batches),
        out_shape=[
            jax.ShapeDtypeStruct((rows, width), jnp.float32),
            jax.ShapeDtypeStruct((rows, width), half),
            jax.ShapeDtypeStruct((8, width), jnp.float32),
            jax.ShapeDtypeStruct((group * rows, units), half),
            jax.ShapeDtypeStruct((width, 2 * units), half),
            jax.ShapeDtypeStruct((near_count(seqs), block, 2 * units), half),
        ],
        in_specs=[VMEM_SPEC] + [ANY_SPEC] * 4 + [VMEM_SPEC] * 3,
        out_specs=[VMEM_SPEC] * 3 + [ANY_SPEC] * 3,
        scratch_shapes=[
            pltpu.VMEM((batches, group, piece, width), half),
            pltpu.VMEM((2, 2 * piece, width), half),
            pltpu.VMEM((2 * piece, units), half),
            pltpu.VMEM(w.shape, half),
            pltpu.VMEM((units, width), half),
            pltpu.VMEM((batches, group * piece, 2 * units), half),
            pltpu.VMEM((2, block, 2 * units), half),
            pltpu.VMEM((batches, piece, width), jnp.float32),
            pltpu.VMEM((2 * piece, 2 * TILE), jnp.float32),
            pltpu.VMEM((piece, width), jnp.float32),
            sems(2),
            sems(2, 2),
            sems(2),
            sems(2),
            sems(batches, 3, group, PARTS // 2),
            sems(batches, group, PARTS // 2),
            sems(seqs),
            sems(seqs),
            sems(2, seqs),
        ]
        + PairReduce.scratch(chips, piece, width) * batches,
        compiler_params=comm_params(collective, 63),
        cost_estimate=cost(
            14 * group * rows * width * units, 400 * MIB, 2 * group * rows * width * 2
        ),
        name="feed_forward",
    )(x, w, *wd_halves, group_d, middle, cot, gain)


def branch_back_kernel(
    seqs, chips, batches, x_ref, w_ref, att_ref, middle_ref, hidden_hbm, wd_one, wd_two, units_hbm, gd_hbm,
    d_ref, layer_ref, out_grad_ref, half_in, whole_in, down_hbm, down_in, far_in,
    out_ref, buf, hidden_ref, wd_ref, grad_acc, rights, tiles, send, recv, load, right_sem, tile_sem,
    part_send, part_recv, wd_load, down_send, down_recv, far_send, far_recv, down_keep, acc, cross_out, line_out, cross_in, line_in, sum_send, sum_recv,
):
    line = Line(chips)
    rows = x_ref.shape[0]
    piece = rows // batches
    width = x_ref.shape[1]
    loads = [
        pltpu.make_async_copy(hidden_hbm, hidden_ref, load.at[0]),
    ] + load_halves([wd_one, wd_two], wd_ref, wd_load)
    for item in loads:
        item.start()

    def product(slot, tile):
        return dot_nn(left_rows(hidden_ref, slot, rows), wd_ref[:, rows_at(tile, TILE)])

    part = rights.shape[2]
    count = width // part

    def right(tile):
        slot = lax.rem(tile, 2)
        return pltpu.make_async_copy(
            gd_hbm.at[:, rows_at(tile, part)], rights.at[slot], right_sem.at[slot]
        )

    def stored(tile):
        slot = lax.rem(tile, 2)
        return pltpu.make_async_copy(
            tiles.at[slot], down_hbm.at[:, rows_at(tile, part)], tile_sem.at[slot]
        )

    def weight_grad(tile):
        right(tile).wait()
        pl.when(tile + 1 < count)(lambda: right(tile + 1).start())
        pl.when(tile >= 2)(lambda: stored(tile - 2).wait())
        slot = lax.rem(tile, 2)
        size = min(TILE, hidden_ref.shape[1])

        @pl.loop(0, hidden_ref.shape[1] // size)
        def _(row):
            here = rows_at(row, size)
            tiles[slot, here, :] = to_half(contract_rows(hidden_ref[:, here], rights[slot]))

        stored(tile).start()

    right(0).start()
    meet(line.greet() + greet_seq(seqs))
    near, far_off = seq_peers(seqs)
    soon = len(near)
    halves = ToPeers(
        seqs, near, units_hbm, half_in, part_send.at[0], part_recv.at[0], half_in.shape[1]
    )
    wholes = ToPeers(seqs, far_off, units_hbm, whole_in, part_send.at[1], part_recv.at[1])
    down = ToPeers(
        seqs, near, down_hbm, down_in.at[pl.ds(0, soon)], down_send, down_recv
    )
    down_far = ToPeers(seqs, far_off, down_hbm, far_in, far_send, far_recv)
    down_kept = pltpu.make_async_copy(
        down_hbm.at[rows_at(lax.axis_index("seq"), down_in.shape[1])], down_in.at[soon], down_keep
    )
    spread = Spread(line, x_ref, buf, send, recv)
    reduce = Reduce(
        line, product, out_ref, acc, cross_out, line_out, cross_in, line_in, sum_send, sum_recv
    )
    spread.begin()
    halves.begin()
    wholes.begin()
    buf[line.own] = x_ref[...]
    grad_acc[...] = jnp.zeros_like(grad_acc)

    def use(slot):
        got = to_half(dot_nt(buf[slot], w_ref[...]))
        for batch in range(batches):
            d_ref[batch, rows_at(slot, piece), :] = got[batch * piece : (batch + 1) * piece]
        mixed = left_rows(att_ref, slot, rows)

        @pl.loop(0, width // TILE)
        def _(tile):
            here = rows_at(tile, TILE)
            grad_acc[:, here] += contract_rows(mixed, buf[slot, :, here])

    for item in loads:
        item.wait()

    reduce.level(chips - 1, lambda tile: None)
    pl.loop(0, count)(weight_grad)
    stored(count - 2).wait()
    stored(count - 1).wait()
    down.begin()
    down_far.begin()
    down_kept.start()
    spread.relay(1)
    spread.each(0, use)

    @pl.loop(1, chips)
    def _(step):
        def also(tile):
            pl.when(step < chips - 1)(lambda: spread.relay_part(step + 1, tile))

        reduce.level(chips - 1 - step, also)
        spread.each(step, use)

    spread.each(chips, use)

    @pl.loop(0, rows // 32)
    def _(chunk):
        here = rows_at(chunk, 32)
        layer_ref[here, :] = to_half(middle_ref[here, :] + out_ref[here, :])

    out_grad_ref[...] = to_half(grad_acc[...])
    spread.sent()
    reduce.sent()
    halves.end()
    wholes.end()
    down.end()
    down_far.end()
    down_kept.wait()


def branch_back(seqs, chips, batches, x, w, attended, middle, hidden, wd_halves, unit_part, group_d, collective):
    rows, width = x.shape
    group = 2 * chips
    length = group * rows // batches
    span = w.shape[0]
    half = jnp.bfloat16
    part = 256 if group * rows <= 2048 else 128
    near, run = near_count(seqs), width // seqs
    units = hidden.shape[1]
    return pl.pallas_call(
        functools.partial(branch_back_kernel, seqs, chips, batches),
        out_shape=[
            jax.ShapeDtypeStruct((batches, length, span), half),
            jax.ShapeDtypeStruct((rows, width), half),
            jax.ShapeDtypeStruct((span, width), half),
            jax.ShapeDtypeStruct((near, run // 2, unit_part.shape[1]), half),
            jax.ShapeDtypeStruct((seqs - 1 - near, run, unit_part.shape[1]), half),
            jax.ShapeDtypeStruct((units, width), half),
            jax.ShapeDtypeStruct((near + 1, units // seqs, width), half),
            jax.ShapeDtypeStruct((seqs - 1 - near, units // seqs // 2, width), half),
        ],
        in_specs=[VMEM_SPEC] * 4 + [ANY_SPEC] * 5,
        out_specs=[VMEM_SPEC] * 3 + [ANY_SPEC] * 5,
        scratch_shapes=[
            pltpu.VMEM((rows, width), jnp.float32),
            pltpu.VMEM((group, rows, width), half),
            pltpu.VMEM(hidden.shape, half),
            pltpu.VMEM((units, width), half),
            pltpu.VMEM((span, width), jnp.float32),
            pltpu.VMEM((2, group * rows, part), half),
            pltpu.VMEM((2, units, part), half),
            sems(3, group, PARTS),
            sems(group, PARTS),
            sems(2),
            sems(2),
            sems(2),
            sems(2, seqs),
            sems(2, seqs),
            sems(2, seqs),
            sems(seqs),
            sems(seqs),
            sems(seqs),
            sems(seqs),
            pltpu.SemaphoreType.DMA,
        ]
        + Reduce.scratch(chips, rows, width),
        compiler_params=comm_params(collective, 62),
        cost_estimate=cost(
            2 * group * rows * width * (2 * span + 2 * units),
            250 * MIB,
            2 * group * rows * width * 2,
        ),
        name="branch_back",
    )(x, w, attended, middle, hidden, *wd_halves, unit_part, group_d.reshape(group * rows, width))


def attention_back_kernel(
    seqs, chips, block, q_ref, pad_ref, low_ref, lse_ref, d_ref, part_hbm, in_one, in_two, in_far,
    w_ref, g_hbm, v_ref, dm_hbm, gain_ref, mlp_gain_ref, out_ref, down_hbm,
    grad_hbm, wq_ref, wk_ref, wv_ref, wo_hbm, tile_ref, gate_hbm, up_hbm, down_in,
    grad_ref, wo_ref, gate_ref, up_ref, result_sem, down_send, down_recv,
    dk, dv, kt, heads, back_out, back_in, unit_parts, unit_sums, units, lefts, parts, sums, cols, out_in,
    totals, gain_acc, gain_out, gain_in, gain_sum, gain_back, acc, keep,
    halo_send, halo_recv, unit_load, unit_send, unit_recv, unit_keep, dm_load, left_sem,
    part_send, part_recv, cols_send, cols_recv, out_send, out_recv,
    gain_send, gain_recv, back_send, back_recv, *line_sums,
):
    line = Line(chips)
    group = 2 * chips
    seq = lax.axis_index("seq")
    own = line.own
    batches, length, span = q_ref.shape
    rows, width = v_ref.shape
    piece = rows // batches
    pair_rows = 2 * piece
    depth = 3 * span
    run = width // seqs
    share = run // group
    part = lefts.shape[3]
    steps, need = length // block, WINDOW // block
    first = length - WINDOW
    has_left, has_right = seq > 0, seq < seqs - 1
    scale = jnp.asarray(HEAD**-0.5, jnp.bfloat16)

    def others(count, me, act):
        pl.loop(1, count)(lambda ahead: act(lax.rem(me + ahead, count)))

    def unit_loaded(turn, place, source):
        slot = lax.rem(turn, 2)
        return pltpu.make_async_copy(source, unit_parts.at[slot, place], unit_load.at[slot, place])

    def load_units(turn):
        member = lax.rem(own + turn, group)
        unit_loaded(turn, 0, part_hbm.at[rows_at(seq * group + member, share)]).start()
        soon = in_one.shape[0]
        for index in range(seqs - 1):

            def fetch(source, index=index):
                unit_loaded(turn, index + 1, source).start()

            if index < soon:

                @pl.when(member < chips)
                def _(index=index, fetch=fetch):
                    fetch(in_one.at[index, rows_at(member, share)])

                @pl.when(member >= chips)
                def _(index=index, fetch=fetch):
                    fetch(in_two.at[index, rows_at(member - chips, share)])

            else:
                fetch(in_far.at[index - soon, rows_at(member, share)])

    load_units(1)
    dm_loaded = pltpu.make_async_copy(dm_hbm, grad_ref, dm_load)
    dm_loaded.start()
    meet(greet_group(group) + greet_seq(seqs))
    near, far_off = seq_peers(seqs)
    down = ToPeers(
        seqs, far_off, down_hbm, down_in, down_send, down_recv, down_in.shape[1]
    )
    down.begin()
    swap = Swap(group, unit_sums, units, unit_send, unit_recv, unit_keep)

    @pl.loop(1, group + 1)
    def _(turn):
        member = lax.rem(own + turn, group)
        slot = lax.rem(turn, 2)
        pl.when(turn < group)(lambda: load_units(turn + 1))
        for place in range(seqs):
            unit_loaded(turn, place, part_hbm.at[rows_at(0, share)]).wait()

        @pl.loop(0, share // 16)
        def _(chunk):
            here = rows_at(chunk, 16)
            added = unit_parts[slot, 0, here, :].astype(jnp.float32)
            for place in range(1, seqs):
                added = added + unit_parts[slot, place, here, :].astype(jnp.float32)
            unit_sums[member, here, :] = to_half(added)

        pl.when(turn < group)(lambda: swap.move(member, own).start())
        pl.when(turn == group)(lambda: swap.kept().start())

    def halo(batch, step, peer):
        here = rows_at(step, block)
        return pltpu.make_async_remote_copy(
            src_ref=back_out.at[batch, here],
            dst_ref=back_in.at[batch, here],
            send_sem=halo_send.at[batch, step],
            recv_sem=halo_recv.at[batch, step],
            device_id={"seq": peer},
            device_id_type=MESH,
        )

    def attend_block(batch, step):
        begin = pl.multiple_of(step * block, block)
        keys = pl.ds(begin, block + WINDOW)
        rows = pl.ds(begin, block)
        low = low_ref[batch, :, rows]
        for pair in range(span // PAIR):
            lanes = slice(pair * PAIR, (pair + 1) * PAIR)
            q_pair = q_ref[batch, rows, lanes] * scale
            d_pair = d_ref[batch, rows, lanes]
            k_rows = pad_ref[batch, keys, lanes]
            v_rows = pad_ref[batch, keys, span + pair * PAIR : span + (pair + 1) * PAIR]
            k_cols = kt[lanes, keys]
            back = []
            for half in range(2):
                row = pair * 2 + half
                q_head = head_lanes(q_pair, half)
                d_head = head_lanes(d_pair, half)
                scores = masked_scores(k_rows, q_head, low)
                probs = jnp.exp(scores - lse_ref[batch, row : row + 1, rows])
                d_probs = dot_nt(v_rows, d_head)
                along = jnp.sum(probs * d_probs, axis=0, keepdims=True)
                d_scores = to_half(probs * (d_probs - along))
                dv[keys, lanes] += dot_nn(to_half(probs), d_head)
                dk[keys, lanes] += dot_nn(d_scores, q_head)
                back.append(dot_nn(k_cols, d_scores))
            at = lax.broadcasted_iota(jnp.int32, back[0].shape, 0)
            heads[batch, rows, lanes] = to_half(
                jnp.where(at < HEAD, back[0], back[1]).T
            )


        @pl.when(has_left & (step < need))
        def _():
            back_out[batch, rows, :span] = to_half(dk[rows, :])
            back_out[batch, rows, span:] = to_half(dv[rows, :])
            halo(batch, step, seq - 1).start()

        @pl.when(step == steps - 1)
        def _():
            heads[batch, :, span : 2 * span] = to_half(dk[WINDOW:, :])
            heads[batch, :, 2 * span :] = to_half(dv[WINDOW:, :])

    def add_halo(batch):
        @pl.when(has_right)
        def _():
            @pl.loop(0, need)
            def _(step):
                there = pl.ds(pl.multiple_of(step * block + first, block), block)
                halo(batch, step, seq).wait_recv()
                got = back_in[batch, rows_at(step, block), :].astype(jnp.float32)
                mine = heads[batch, there, span:].astype(jnp.float32)
                heads[batch, there, span:] = to_half(mine + got)

    def product(batch):
        def get(place, here):
            return dot_nt(heads[batch, rows_at(place, pair_rows), :], w_ref[here, :])

        return get

    reduces = [
        PairReduce(
            line, product(batch), totals.at[batch], acc, keep, *line_sums[6 * batch : 6 * batch + 6]
        )
        for batch in range(batches)
    ]
    last = 2 * chips - 2

    @pl.loop(0, 2 * steps)
    def _(turn):
        batch, step = turn // steps, lax.rem(turn, steps)

        @pl.when(step == 0)
        def _():
            kt[...] = pad_ref[batch, :, :span].T * scale
            dk[...] = jnp.zeros_like(dk)
            dv[...] = jnp.zeros_like(dv)

        attend_block(batch, step)
        after = turn - steps - 1
        pl.when(after == 0)(lambda: add_halo(0))

        @pl.when((after >= 0) & (2 * after < last))
        def _():
            reduces[0].step(2 * after)
            reduces[0].step(2 * after + 1)

    for after in range(steps - 1, chips - 1):
        reduces[0].step(2 * after)
        reduces[0].step(2 * after + 1)

    def left(tile):
        slot = lax.rem(tile, 2)
        return pltpu.make_async_copy(
            g_hbm.at[:, :, rows_at(tile, part)], lefts.at[slot], left_sem.at[slot]
        )

    heads_near = ToPeers(seqs, near + far_off, parts, sums, part_send, part_recv)
    left(0).start()
    add_halo(1)

    @pl.loop(0, width // part)
    def _(tile):
        left(tile).wait()
        pl.when(tile + 1 < width // part)(lambda: left(tile + 1).start())
        slot = lax.rem(tile, 2)
        got = contract_rows(lefts[slot, 0], heads[0])
        for batch in range(1, batches):
            got = got + contract_rows(lefts[slot, batch], heads[batch])
        parts[rows_at(tile, part), :] = to_half(got)

    heads_near.begin()
    from_seq = ToPeers(seqs, near + far_off, out_ref, out_in, out_send, out_recv)
    from_seq.begin()
    gain_acc[...] = jnp.zeros_like(gain_acc)
    dm_loaded.wait()

    def norm_batch(batch):
        mine = pl.ds(batch * piece, piece)

        def put(here, d_values):
            there = pl.ds(pl.multiple_of(here.start + batch * piece, here.size), here.size)
            grad_ref[there, :] += d_values

        norm_back(piece, v_ref.at[mine], totals.at[batch], gain_ref, gain_acc, put)

    pl.loop(0, 2)(reduces[1].step)
    reduces[0].step(last)
    norm_batch(0)
    pl.loop(2, last)(reduces[1].step)
    swap.end()
    cell = units.shape[2] // 2 // seqs
    for member in range(group):
        for place in range(seqs):
            column = (place * group + member) * cell
            for target, begin in ((gate_ref, 0), (up_ref, seqs * cell)):
                here = slice(begin + place * cell, begin + (place + 1) * cell)
                target[:, column : column + cell] = units[member, :, here]

    results = [
        pltpu.make_async_copy(source, target, result_sem.at[index])
        for index, (source, target) in enumerate(
            ((gate_ref, gate_hbm), (up_ref, up_hbm), (wo_ref, wo_hbm), (grad_ref, grad_hbm))
        )
    ]
    results[0].start()
    results[1].start()

    def block_swap(peer, member):
        return pltpu.make_async_remote_copy(
            src_ref=parts.at[rows_at(seq * group + peer, share)],
            dst_ref=cols.at[member],
            send_sem=cols_send.at[peer],
            recv_sem=cols_recv.at[member],
            device_id={"fsdp": peer},
            device_id_type=MESH,
        )

    heads_near.arrived()

    @pl.loop(0, run // 64)
    def _(chunk):
        here = rows_at(chunk, 64)
        there = pl.ds(pl.multiple_of(seq * run + chunk * 64, 64), 64)
        parts[there, :] = to_half(add_from_seq(parts[there, :], sums, here))

    others(group, own, lambda peer: block_swap(peer, own).start())
    cols[own] = parts[rows_at(seq * group + own, share), :]
    from_seq.arrived()
    out_rows = out_in.shape[1]
    wo_ref[...] = add_from_seq(out_ref[rows_at(seq, out_rows), :], out_in, slice(None))
    results[2].start()
    reduces[1].step(last)
    norm_batch(1)
    results[3].start()
    fold = 128 // share
    near = group // fold
    attn_row = jnp.sum(gain_acc[...], axis=0, keepdims=True)
    mlp_row = jnp.sum(mlp_gain_ref[...], axis=0, keepdims=True)
    gain_out[...] = jnp.zeros_like(gain_out)
    for place in range(width // 128):
        lanes = slice(place * 128, (place + 1) * 128)
        gain_out[place % near, place // near, 0:1, :] = attn_row[:, lanes]
        gain_out[place % near, place // near, 1:2, :] = mlp_row[:, lanes]

    def gain_group(peer, member):
        return pltpu.make_async_remote_copy(
            src_ref=gain_out.at[peer // fold],
            dst_ref=gain_in.at[member],
            send_sem=gain_send.at[peer],
            recv_sem=gain_recv.at[member],
            device_id={"fsdp": peer},
            device_id_type=MESH,
        )

    def gain_seq(peer, place):
        return pltpu.make_async_remote_copy(
            src_ref=gain_sum.at[peer],
            dst_ref=gain_back.at[place],
            send_sem=back_send.at[peer],
            recv_sem=back_recv.at[place],
            device_id={"seq": peer},
            device_id_type=MESH,
        )

    others(group, own, lambda peer: gain_group(peer, own).start())
    gain_in[own] = gain_out[own // fold]
    others(group, own, lambda peer: gain_group(peer, peer).wait_recv())
    gain_sum[...] = jnp.sum(gain_in[...], axis=0)
    others(seqs, seq, lambda peer: gain_seq(peer, seq).start())
    gain_back[seq] = gain_sum[seq]
    others(seqs, seq, lambda peer: gain_seq(peer, peer).wait_recv())
    tile_ref[...] = jnp.sum(gain_back[...], axis=0)
    others(group, own, lambda peer: block_swap(peer, peer).wait_recv())
    for index, target in enumerate((wq_ref, wk_ref, wv_ref)):
        for member, first, home, size in column_parts(seqs, group, share, span):
            first = first + index * span
            target[:, home : home + size] = cols[member, :, first : first + size]
    from_seq.sent()
    for item in results:
        item.wait()
    for batch in range(batches):
        reduces[batch].sent()

        @pl.when(has_left)
        def _(batch=batch):
            pl.loop(0, need)(lambda step: halo(batch, step, seq).wait_send())

    heads_near.sent()
    down.end()
    others(group, own, lambda peer: gain_group(peer, own).wait_send())
    others(group, own, lambda peer: block_swap(peer, own).wait_send())
    others(seqs, seq, lambda peer: gain_seq(peer, seq).wait_send())


def attention_back(
    seqs, chips, block, query, kv_pad, low, lse, d_att, part_own, parts_one, parts_two, parts_far, w, group_a,
    x, d_middle, gain, mlp_gain, out_part, down, collective,
):
    batches, length, span = query.shape
    padded = kv_pad.shape[1]
    rows, width = x.shape
    piece = rows // batches
    group = 2 * chips
    depth = w.shape[1]
    run = width // seqs
    share = run // group
    near = group // (128 // share)
    cells = part_own.shape[1]
    out_rows = out_part.shape[0] // seqs
    half, wide = jnp.bfloat16, jnp.float32
    part = 256 if batches * length <= 2048 else 128
    return pl.pallas_call(
        functools.partial(attention_back_kernel, seqs, chips, block),
        out_shape=[
            jax.ShapeDtypeStruct((rows, width), wide),
            jax.ShapeDtypeStruct((share, width), half),
            jax.ShapeDtypeStruct((share, width), half),
            jax.ShapeDtypeStruct((share, width), half),
            jax.ShapeDtypeStruct((out_rows, width), wide),
            jax.ShapeDtypeStruct((8, 128), wide),
            jax.ShapeDtypeStruct((share, cells // 2 * group), half),
            jax.ShapeDtypeStruct((share, cells // 2 * group), half),
            jax.ShapeDtypeStruct(
                (seqs - 1 - near_count(seqs), down.shape[0] // seqs // 2, width), half
            ),
        ],
        in_specs=[VMEM_SPEC] * 5
        + [ANY_SPEC] * 4
        + [VMEM_SPEC, ANY_SPEC, VMEM_SPEC, ANY_SPEC]
        + [VMEM_SPEC] * 3
        + [ANY_SPEC],
        out_specs=[ANY_SPEC, VMEM_SPEC, VMEM_SPEC, VMEM_SPEC, ANY_SPEC, VMEM_SPEC]
        + [ANY_SPEC] * 3,
        scratch_shapes=[
            pltpu.VMEM((rows, width), wide),
            pltpu.VMEM((out_rows, width), wide),
            pltpu.VMEM((share, cells // 2 * group), half),
            pltpu.VMEM((share, cells // 2 * group), half),
            sems(4),
            sems(seqs),
            sems(seqs),
            pltpu.VMEM((padded, span), wide),
            pltpu.VMEM((padded, span), wide),
            pltpu.VMEM((span, padded), half),
            pltpu.VMEM((batches, length, depth), half),
            pltpu.VMEM((batches, WINDOW, 2 * span), half),
            pltpu.VMEM((batches, WINDOW, 2 * span), half),
            pltpu.VMEM((2, seqs, share, cells), half),
            pltpu.VMEM((group, share, cells), half),
            pltpu.VMEM((group, share, cells), half),
            pltpu.VMEM((2, batches, length, part), half),
            pltpu.VMEM((width, depth), half),
            pltpu.VMEM((seqs - 1, run, depth), half),
            pltpu.VMEM((group, share, depth), half),
            pltpu.VMEM((seqs - 1, out_rows, width), half),
            pltpu.VMEM((batches, piece, width), wide),
            pltpu.VMEM((8, width), wide),
            pltpu.VMEM((near, seqs, 8, 128), wide),
            pltpu.VMEM((group, seqs, 8, 128), wide),
            pltpu.VMEM((seqs, 8, 128), wide),
            pltpu.VMEM((seqs, 8, 128), wide),
            pltpu.VMEM((2 * piece, TILE), wide),
            pltpu.VMEM((piece, width), wide),
            sems(batches, WINDOW // block),
            sems(batches, WINDOW // block),
            sems(2, seqs),
            sems(group),
            sems(group),
            pltpu.SemaphoreType.DMA,
            pltpu.SemaphoreType.DMA,
            sems(2),
            sems(seqs),
            sems(seqs),
            sems(group),
            sems(group),
            sems(seqs),
            sems(seqs),
            sems(group),
            sems(group),
            sems(seqs),
            sems(seqs),
        ]
        + PairReduce.scratch(chips, piece, width) * batches,
        compiler_params=comm_params(collective, 63),
        cost_estimate=cost(
            20 * batches * length * span * (WINDOW + block) + 4 * group * rows * width * depth,
            400 * MIB,
            3 * group * rows * width * 2,
        ),
        name="attention_back",
    )(
        query, kv_pad, low, lse, d_att, part_own, parts_one, parts_two, parts_far, w, group_a, x,
        d_middle, gain, mlp_gain, out_part, down,
    )


def finish_kernel(count, *refs):
    sources, targets = refs[:-count], refs[-count:]
    for source, target in zip(sources, targets[:-1]):
        target[...] = source[...].astype(target.dtype)
    added = 0.0
    for source in sources[count - 1 :]:
        added = added + jnp.sum(source[...].astype(jnp.float32), axis=0)
    targets[-1][...] = added


def finish(steps, arrays, parts, kinds):
    in_specs, out_specs, out_shape = [], [], []
    for item, kind in zip(arrays + parts[:1], kinds):
        rows, width = item.shape[-2:]
        block = (rows // steps, width)
        out_specs.append(pl.BlockSpec(block, lambda i: (i, 0)))
        out_shape.append(jax.ShapeDtypeStruct((rows, width), kind))
        if item.ndim == 2:
            in_specs.append(out_specs[-1])
    for item in parts:
        in_specs.append(pl.BlockSpec((item.shape[0],) + block, lambda i: (0, i, 0)))
    return pl.pallas_call(
        functools.partial(finish_kernel, len(kinds)),
        grid=(steps,),
        in_specs=in_specs,
        out_specs=out_specs,
        out_shape=out_shape,
        compiler_params=pltpu.CompilerParams(vmem_limit_bytes=63 * MIB),
        name="finish",
    )(*arrays, *parts)


def doc_starts(lengths, positions, batches, seq_len):
    table = lengths.reshape(batches, -1, lengths.shape[1])
    starts = jnp.cumsum(table, axis=2) - table
    per_batch = seq_len // table.shape[1]
    begins = (starts + (jnp.arange(table.shape[1], dtype=jnp.int32) * per_batch)[None, :, None]).reshape(
        batches, -1
    )
    before = begins[:, None, :] <= positions[None, :, None]
    return jnp.max(jnp.where(before, begins[:, None, :], 0), axis=2)


def body(
    tokens,
    cotangent,
    lengths,
    gain_attn,
    w_query,
    w_key,
    w_value,
    w_out,
    gain_mlp,
    w_gate,
    w_up,
    w_down,
):
    batches, piece, width = tokens.shape
    seqs = lax.axis_size("seq")
    group = lax.axis_size("fsdp")
    chips = group // 2
    devices = seqs * group
    seq_len = piece * devices
    rows = batches * piece
    share = w_query.shape[0]
    span = width // group
    length = group * piece
    aligned = share == HEAD
    member = lax.axis_index("fsdp")

    x_rows = tokens.reshape(rows, width)
    cot_rows = cotangent.reshape(rows, width)
    if aligned:
        wo_part = lax.all_gather(w_out, "seq", axis=0, tiled=True)
    else:
        wo_all = lax.all_gather(w_out, ("seq", "fsdp"), axis=0, tiled=True)
        wo_part = lax.dynamic_slice_in_dim(wo_all, member * span, span, 0)

    lane = jnp.arange(128, dtype=jnp.int32)
    device = lax.axis_index("seq") * group + member
    fold = 128 // share
    here = lane // share == lax.rem(device, fold)
    both = jnp.stack([gain_attn, gain_mlp]).astype(jnp.float32)
    tile = jnp.where(here[None], jnp.tile(both, (1, fold)), 0.0)
    tile = jnp.pad(tile, ((0, 6), (0, 0)))[None]
    group_start = lax.axis_index("seq") * length
    positions = group_start + jnp.arange(length, dtype=jnp.int32)
    begins = doc_starts(lengths, positions, batches, seq_len)
    at = jnp.arange(length, dtype=jnp.int32)
    block = min(256, length)
    low = jnp.maximum(begins - group_start + WINDOW, at[None, :] + 1) - (at // block * block)[None, :]
    low = low[:, None, :]
    group_a, query, attended, lse, kv_pad, gains, w_heads, unit_own, wd_one = start(
        seqs, chips, batches, block, tile, x_rows, (w_query, w_key, w_value), (w_gate, w_up), w_down,
        low, 1,
    )
    gains = gains.transpose(1, 0, 2, 3).reshape(devices // fold, fold, 8, 128).sum(axis=1)
    gain_one = gains[:, 0].reshape(width)
    gain_two = gains[:, 1].reshape(width)
    middle, normed_b, group_d, w_units, wd_two = branch_sum(
        seqs, chips, attended, wo_part, cot_rows, unit_own.reshape(group * share, -1), w_down,
        x_rows, gain_two[None], 3,
    )
    w_units = w_units.reshape(width, -1)
    d_middle, d_branch, mlp_gain_part, hidden, unit_part, unit_one = feed_forward(
        seqs, chips, batches, normed_b, w_units, (wd_one, wd_two), group_d, middle, cot_rows,
        gain_two[None], 4,
    )
    d_attended, layer_out, out_part, unit_two, unit_far, down_part, down_near, far_one = branch_back(
        seqs, chips, batches, d_branch, wo_part, attended, middle, hidden, (wd_one, wd_two),
        unit_part, group_d, 5,
    )
    if not aligned:
        whole = lax.dynamic_update_slice_in_dim(
            jnp.zeros((width, width), jnp.bfloat16), out_part, member * span, 0
        )
        out_part = lax.psum(whole, "fsdp").reshape(seqs, group, share, width)
        out_part = lax.dynamic_slice_in_dim(out_part, member, 1, 1).reshape(seqs * share, width)
    (
        input_grad, wq_grad, wk_grad, wv_grad, wo_grad, gain_tile, gate_grad, up_grad, far_two,
    ) = attention_back(
        seqs, chips, block, query, kv_pad, low, lse, d_attended, unit_part, unit_one, unit_two,
        unit_far, w_heads, group_a, x_rows, d_middle, gain_one[None], mlp_gain_part, out_part,
        down_part, 6,
    )
    gain_grads = lax.dynamic_slice_in_dim(gain_tile[:2], lax.rem(device, fold) * share, share, 1)
    wide = jnp.float32
    (layer_out, input_grad, wq_grad, wk_grad, wv_grad, wo_grad, gate_grad, up_grad, down_grad) = finish(
        share // 16,
        [layer_out, input_grad, wq_grad, wk_grad, wv_grad, wo_grad, gate_grad, up_grad],
        [down_near, jnp.concatenate([far_one, far_two], axis=1)],
        [jnp.bfloat16] + [wide] * 8,
    )
    return (
        layer_out.reshape(batches, piece, width),
        input_grad.reshape(batches, piece, width),
        gain_grads[0],
        wq_grad,
        wk_grad,
        wv_grad,
        wo_grad,
        gain_grads[1],
        gate_grad,
        up_grad,
        down_grad,
    )


def solution(mesh):
    spread = ("seq", "fsdp")
    tokens, rows, gains = P(None, spread, None), P(spread, None), P(spread)
    in_specs = (tokens, tokens, P(), gains, rows, rows, rows, rows, gains, rows, rows, rows)
    out_specs = (tokens, tokens, gains, rows, rows, rows, rows, gains, rows, rows, rows)
    return jax.shard_map(body, mesh=mesh, in_specs=in_specs, out_specs=out_specs, check_vma=False)
```

```python
import functools

import jax
import jax.numpy as jnp
from jax import lax
from jax.experimental import pallas as pl
from jax.experimental.pallas import tpu as pltpu
from jax.sharding import PartitionSpec as P

HEAD = 64
FF = 8192
WINDOW = 1024
PAIR = 128
TILE = 512
PARTS = 4
LOW = -1e30
EPS = 1e-05
MESH = pl.DeviceIdType.MESH
MIB = 2**20


def to_half(values):
    return values.astype(jnp.bfloat16)


def normalize(values, gain):
    return values * lax.rsqrt(jnp.mean(values * values, axis=-1, keepdims=True) + EPS) * gain


def contract_rows(left, right):
    return lax.dot_general(
        left, right, (((0,), (0,)), ((), ())), preferred_element_type=jnp.float32
    )


def dot_nt(left, right):
    return lax.dot_general(
        left, right, (((1,), (1,)), ((), ())), preferred_element_type=jnp.float32
    )


def dot_nn(left, right):
    return jnp.dot(left, right, preferred_element_type=jnp.float32)


def head_lanes(values, half):
    lane = lax.broadcasted_iota(jnp.int32, values.shape, 1)
    return jnp.where((lane >= HEAD) == (half == 1), values, jnp.zeros_like(values))


def masked_scores(k_rows, q_head, low):
    keys, block = k_rows.shape[0], q_head.shape[0]
    scores = dot_nt(k_rows, q_head)
    at = lax.broadcasted_iota(jnp.int32, (keys, block), 0)
    query = lax.broadcasted_iota(jnp.int32, (keys, block), 1)
    seen = (at >= low) & (at <= query + WINDOW)
    return jnp.where(seen, scores, LOW)


class Line:
    def __init__(self, chips):
        self.chips = chips
        self.own = lax.axis_index("fsdp")
        self.chip = self.own // 2
        self.core = lax.rem(self.own, 2)
        self.other = self.own + 1 - 2 * self.core
        self.has_left = self.chip > 0
        self.has_right = self.chip < chips - 1

    def greet(self):
        signal_group(self.other)
        pl.when(self.has_left)(lambda: signal_group(self.own - 2))
        pl.when(self.has_right)(lambda: signal_group(self.own + 2))
        return 1 + self.has_left.astype(jnp.int32) + self.has_right.astype(jnp.int32)


def signal_group(peer):
    barrier = pltpu.get_barrier_semaphore()
    pl.semaphore_signal(barrier, inc=1, device_id={"fsdp": peer}, device_id_type=MESH)


def signal_seq(peer):
    barrier = pltpu.get_barrier_semaphore()
    pl.semaphore_signal(barrier, inc=1, device_id={"seq": peer}, device_id_type=MESH)


def greet_group(group):
    own = lax.axis_index("fsdp")
    pl.loop(1, group)(lambda ahead: signal_group(lax.rem(own + ahead, group)))
    return group - 1


def greet_seq(seqs):
    own = lax.axis_index("seq")
    pl.loop(1, seqs)(lambda ahead: signal_seq(lax.rem(own + ahead, seqs)))
    return seqs - 1


def meet(count):
    pl.semaphore_wait(pltpu.get_barrier_semaphore(), count)


def rows_at(index, size):
    return pl.ds(pl.multiple_of(index * size, size), size)


class Spread:
    def __init__(self, line, first, buf, send, recv):
        self.line, self.first, self.buf, self.send, self.recv = line, first, buf, send, recv
        self.parts = recv.shape[1]
        self.size = first.shape[0] // self.parts

    def move(self, slot, part, way, peer, source=None):
        here = rows_at(part, self.size)
        return pltpu.make_async_remote_copy(
            src_ref=self.buf.at[slot, here] if source is None else source.at[here],
            dst_ref=self.buf.at[slot, here],
            send_sem=self.send.at[way, slot, part],
            recv_sem=self.recv.at[slot, part],
            device_id={"fsdp": peer},
            device_id_type=MESH,
        )

    def begin(self):
        line = self.line

        @pl.loop(0, self.parts)
        def _(part):
            pl.when(line.has_right)(
                lambda: self.move(line.own, part, 1, line.own + 2, self.first).start()
            )
            pl.when(line.has_left)(
                lambda: self.move(line.own, part, 0, line.own - 2, self.first).start()
            )
            self.move(line.own, part, 2, line.other, self.first).start()

    def relay_part(self, far, part):
        line = self.line

        @pl.when(line.chip - far >= 0)
        def _():
            slot = (line.chip - far) * 2 + line.core
            self.move(slot, part, 1, line.own).wait_recv()
            pl.when(line.has_right)(lambda: self.move(slot, part, 1, line.own + 2).start())
            self.move(slot, part, 2, line.other).start()

        @pl.when(line.chip + far < line.chips)
        def _():
            slot = (line.chip + far) * 2 + line.core
            self.move(slot, part, 0, line.own).wait_recv()
            pl.when(line.has_left)(lambda: self.move(slot, part, 0, line.own - 2).start())
            self.move(slot, part, 2, line.other).start()

    def relay(self, far):
        pl.loop(0, self.parts)(lambda part: self.relay_part(far, part))

    def across(self, slot):
        pl.loop(0, self.parts)(lambda part: self.move(slot, part, 2, self.line.own).wait_recv())

    def each(self, far, use):
        line = self.line

        @pl.loop(0, 4)
        def _(turn):
            side = lax.rem(turn, 2)
            over = turn // 2
            away = far - over
            source = line.chip + away * (2 * side - 1)
            valid = (away >= 0) & (away < line.chips) & (source >= 0) & (source < line.chips)
            valid = valid & ((side == 0) | (away > 0))

            @pl.when(valid)
            def _():
                slot = source * 2 + line.core + over * (1 - 2 * line.core)
                pl.when(over == 1)(lambda: self.across(slot))
                use(slot)

    def rest(self):
        pl.loop(0, self.line.chips)(lambda place: self.across(place * 2 + 1 - self.line.core))

    def sent(self):
        line = self.line

        @pl.loop(0, line.chips)
        def _(place):
            slot = place * 2 + line.core

            @pl.loop(0, self.parts)
            def _(part):
                self.move(slot, part, 2, line.other).wait_send()
                pl.when(line.has_right & (place <= line.chip))(
                    lambda: self.move(slot, part, 1, line.own + 2).wait_send()
                )
                pl.when(line.has_left & (place >= line.chip))(
                    lambda: self.move(slot, part, 0, line.own - 2).wait_send()
                )


class Reduce:
    def __init__(self, line, product, out, acc, cross_out, line_out, cross_in, line_in, send, recv):
        self.line, self.product, self.out, self.acc = line, product, out, acc
        self.cross_out, self.line_out, self.cross_in, self.line_in = cross_out, line_out, cross_in, line_in
        self.send, self.recv = send, recv
        self.tiles = line_out.shape[2] // TILE

    @staticmethod
    def scratch(chips, rows, width):
        part = pltpu.VMEM((chips, rows, width), jnp.bfloat16)
        return [
            pltpu.VMEM((rows, TILE), jnp.float32),
            pltpu.VMEM((2, rows, width), jnp.bfloat16),
            part,
            part,
            pltpu.VMEM((chips + 1, rows, width), jnp.bfloat16),
            pltpu.SemaphoreType.DMA((2, chips, width // TILE)),
            pltpu.SemaphoreType.DMA((2, chips + 1, width // TILE)),
        ]

    def cross(self, side, place, tile):
        here = rows_at(tile, TILE)
        return pltpu.make_async_remote_copy(
            src_ref=self.cross_out.at[side, :, here],
            dst_ref=self.cross_in.at[place, :, here],
            send_sem=self.send.at[0, place, tile],
            recv_sem=self.recv.at[0, place, tile],
            device_id={"fsdp": self.line.other},
            device_id_type=MESH,
        )

    def along(self, place, landing, tile, peer):
        here = rows_at(tile, TILE)
        return pltpu.make_async_remote_copy(
            src_ref=self.line_out.at[place, :, here],
            dst_ref=self.line_in.at[landing, :, here],
            send_sem=self.send.at[1, place, tile],
            recv_sem=self.recv.at[1, landing, tile],
            device_id={"fsdp": peer},
            device_id_type=MESH,
        )

    def where(self, away, side):
        line = self.line
        rightward = (line.chips - 1 - line.chip >= line.chip) == (side == 0)
        place = line.chip + jnp.where(rightward, away, -away)
        valid = (place >= 0) & (place < line.chips) & ((away > 0) | (side == 0))
        return valid, place, rightward

    def level(self, away, also):
        @pl.loop(0, 2)
        def _(side):
            valid, place, _ = self.where(away, side)

            @pl.when(valid)
            def _():
                @pl.loop(0, self.tiles)
                def _(tile):
                    got = self.product(place * 2 + 1 - self.line.core, tile)
                    self.cross_out[side, :, rows_at(tile, TILE)] = to_half(got)
                    self.cross(side, place, tile).start()

        @pl.loop(0, self.tiles)
        def _(tile):
            @pl.loop(0, 2)
            def _(side):
                valid, place, rightward = self.where(away, side)
                pl.when(valid)(lambda: self.close(away, side, place, rightward, tile))

            also(tile)

    def close(self, away, side, place, rightward, tile):
        line, acc = self.line, self.acc
        here = rows_at(tile, TILE)
        upstream = (rightward & line.has_left) | (jnp.logical_not(rightward) & line.has_right)
        acc[...] = self.product(place * 2 + line.core, tile)
        self.cross(side, place, tile).wait()
        acc[...] += self.cross_in[place, :, here].astype(jnp.float32)

        @pl.when(away > 0)
        def _():
            @pl.when(upstream)
            def _():
                self.along(place, place, tile, line.own).wait_recv()
                self.line_out[place, :, here] = to_half(
                    acc[...] + self.line_in[place, :, here].astype(jnp.float32)
                )

            @pl.when(jnp.logical_not(upstream))
            def _():
                self.line_out[place, :, here] = to_half(acc[...])

            @pl.when(rightward)
            def _():
                self.along(place, place, tile, line.own + 2).start()

            @pl.when(jnp.logical_not(rightward))
            def _():
                landing = jnp.where(away == 1, line.chips, place)
                self.along(place, landing, tile, line.own - 2).start()

        @pl.when(away == 0)
        def _():
            self.out[:, here] = acc[...]

            @pl.when(line.has_left)
            def _():
                self.along(place, place, tile, line.own).wait_recv()
                self.out[:, here] += self.line_in[place, :, here].astype(jnp.float32)

            @pl.when(line.has_right)
            def _():
                self.along(place, line.chips, tile, line.own).wait_recv()
                self.out[:, here] += self.line_in[line.chips, :, here].astype(jnp.float32)

    def sent(self):
        @pl.loop(0, self.line.chips)
        def _(place):
            @pl.when(place != self.line.chip)
            def _():
                pl.loop(0, self.tiles)(
                    lambda tile: self.along(place, place, tile, self.line.own).wait_send()
                )


class Swap:
    def __init__(self, group, source, target, send, recv, keep):
        self.group, self.source, self.target = group, source, target
        self.send, self.recv, self.keep = send, recv, keep
        self.own = lax.axis_index("fsdp")

    def move(self, peer, source):
        return pltpu.make_async_remote_copy(
            src_ref=self.source.at[peer],
            dst_ref=self.target.at[source],
            send_sem=self.send.at[peer],
            recv_sem=self.recv.at[source],
            device_id={"fsdp": peer},
            device_id_type=MESH,
        )

    def kept(self):
        return pltpu.make_async_copy(self.source.at[self.own], self.target.at[self.own], self.keep)

    def begin(self):
        self.kept().start()
        pl.loop(1, self.group)(
            lambda ahead: self.move(lax.rem(self.own + ahead, self.group), self.own).start()
        )

    def end(self):
        self.kept().wait()

        @pl.loop(1, self.group)
        def _(ahead):
            peer = lax.rem(self.own + ahead, self.group)
            self.move(peer, peer).wait_recv()
            self.move(peer, self.own).wait_send()


class Share:
    def __init__(self, seqs, source, target, send, recv, keep):
        self.seqs, self.source, self.target = seqs, source, target
        self.send, self.recv, self.keep = send, recv, keep
        self.own = lax.axis_index("seq")
        self.parts = send.shape[2]
        self.size = source.shape[0] // self.parts

    def move(self, peer, place, part):
        here = pl.ds(part * self.size, self.size)
        return pltpu.make_async_remote_copy(
            src_ref=self.source.at[here],
            dst_ref=self.target.at[place, here],
            send_sem=self.send.at[peer, 0, part],
            recv_sem=self.recv.at[place, 0, part],
            device_id={"seq": peer},
            device_id_type=MESH,
        )

    def relay(self, peer, place, part, side):
        here = pl.ds(part * self.size + side * (self.size // 2), self.size // 2)
        return pltpu.make_async_remote_copy(
            src_ref=self.target.at[place, here],
            dst_ref=self.target.at[place, here],
            send_sem=self.send.at[peer, 1, part],
            recv_sem=self.recv.at[place, side, part],
            device_id={"seq": peer},
            device_id_type=MESH,
        )

    def near(self):
        one = self.own + 1 - 2 * lax.rem(self.own, 2)
        two = lax.rem(self.own + 2, 4)
        return one, two, lax.rem(one + 2, 4)

    def kept(self):
        return pltpu.make_async_copy(self.source, self.target.at[self.own], self.keep)

    def begin(self):
        self.kept().start()
        for part in range(self.parts):
            if self.seqs == 4:
                one, two, _ = self.near()
                self.move(one, self.own, part).start()
                self.move(two, self.own, part).start()
            else:
                pl.loop(1, self.seqs)(
                    lambda ahead, part=part: self.move(
                        lax.rem(self.own + ahead, self.seqs), self.own, part
                    ).start()
                )

    def pass_on(self, parts):
        if self.seqs == 4:
            one, two, _ = self.near()
            for part in parts:
                self.move(one, one, part).wait_recv()
                self.relay(two, one, part, 0).start()
                self.move(two, two, part).wait_recv()
                self.relay(one, two, part, 1).start()

    def end(self):
        self.kept().wait()
        for part in range(self.parts):
            if self.seqs == 4:
                one, two, far = self.near()
                self.relay(two, far, part, 0).wait_recv()
                self.relay(one, far, part, 1).wait_recv()
                self.move(one, self.own, part).wait_send()
                self.move(two, self.own, part).wait_send()
                self.relay(two, one, part, 0).wait_send()
                self.relay(one, two, part, 1).wait_send()
            else:

                @pl.loop(1, self.seqs)
                def _(ahead, part=part):
                    peer = lax.rem(self.own + ahead, self.seqs)
                    self.move(peer, peer, part).wait_recv()
                    self.move(peer, self.own, part).wait_send()


def seq_peers(seqs):
    own = lax.axis_index("seq")
    if seqs == 4:
        one = own + 1 - 2 * lax.rem(own, 2)
        return [one, lax.rem(own + 2, 4)], [lax.rem(one + 2, 4)]
    ahead = [lax.rem(own + step, seqs) for step in range(1, seqs)]
    return ahead[:1], ahead[1:]


def near_count(seqs):
    return 2 if seqs == 4 else 1


class ToPeers:
    def __init__(self, seqs, peers, source, target, send, recv, first=0):
        self.peers, self.source, self.target, self.send, self.recv = peers, source, target, send, recv
        self.run, self.first = source.shape[0] // seqs, first

    def move(self, index):
        begin = pl.multiple_of(self.peers[index] * self.run + self.first, 16)
        return pltpu.make_async_remote_copy(
            src_ref=self.source.at[pl.ds(begin, self.target.shape[1])],
            dst_ref=self.target.at[index],
            send_sem=self.send.at[index],
            recv_sem=self.recv.at[index],
            device_id={"seq": self.peers[index]},
            device_id_type=MESH,
        )

    def begin(self):
        for index in range(len(self.peers)):
            self.move(index).start()

    def arrived(self):
        for index in range(len(self.peers)):
            self.move(index).wait_recv()

    def sent(self):
        for index in range(len(self.peers)):
            self.move(index).wait_send()

    def end(self):
        self.arrived()
        self.sent()


def load_halves(halves, target, load):
    copies = []
    rows = halves[0].shape[1]
    for index, half in enumerate(halves):
        for place in range(half.shape[0]):
            there = pl.ds((2 * place + index) * rows, rows)
            copies.append(pltpu.make_async_copy(half.at[place], target.at[there], load.at[index, place]))
    return copies


VMEM_SPEC = pl.BlockSpec(memory_space=pltpu.VMEM)
ANY_SPEC = pl.BlockSpec(memory_space=pl.ANY)


def comm_params(collective, mib=58):
    return pltpu.CompilerParams(
        collective_id=collective, has_side_effects=True, vmem_limit_bytes=mib * MIB
    )


def cost(flops, local, remote):
    return pl.CostEstimate(
        flops=flops, bytes_accessed=local, transcendentals=0, remote_bytes_transferred=remote
    )


def sems(*shape):
    return pltpu.SemaphoreType.DMA(shape)


def left_rows(a_ref, slot, rows):
    if len(a_ref.shape) == 2:
        return a_ref[rows_at(slot, rows), :]
    piece = rows // a_ref.shape[0]
    return jnp.concatenate(
        [a_ref[batch, rows_at(slot, piece), :] for batch in range(a_ref.shape[0])], axis=0
    )


def norm_back(rows, v_ref, e_ref, gain_ref, gain_acc, put):
    @pl.loop(0, rows // 32)
    def _(chunk):
        here = rows_at(chunk, 32)
        values = v_ref[here, :].astype(jnp.float32)
        error = e_ref[here, :]
        rate = lax.rsqrt(jnp.mean(values * values, axis=-1, keepdims=True) + EPS)
        unit = values * rate
        product = error * unit
        gain = gain_ref[0:1, :]
        mean = jnp.mean(product * gain, axis=-1, keepdims=True)
        gain_acc[...] += (product[0:8] + product[8:16]) + (product[16:24] + product[24:32])
        put(here, rate * (gain * error - unit * mean))


def add_from_seq(own_rows, got, here):
    added = own_rows.astype(jnp.float32)
    for index in range(got.shape[0]):
        added = added + got[index, here, :].astype(jnp.float32)
    return added


def column_parts(seqs, group, share, span):
    size = HEAD if share == HEAD else span
    parts = []
    for member in range(group):
        for run in range(span // size):
            home = (run * group + member) * size
            parts.append((member, run * size, home, size))
    return parts


def start_kernel(
    seqs, chips, batches, block, tile_ref, x_ref, wq_ref, wk_ref, wv_ref, gate_hbm, up_hbm, down_hbm, low_ref,
    g_ref, q_ref, out_ref, lse_ref, pad_ref, gains_ref, w_out_ref, own_units_ref, wd_ref,
    gate, up, units, blocks_ref, buf, normed, pad, vt, gain, gains, w,
    unit_sem, send, recv, keep, swap_send, share_send, w_recv,
    tile_send, tile_across, tile_recv, tile_back, w_keep, gain_keep,
    halo_send, halo_recv, pad_keep, unit_send, unit_recv, unit_keep,
    down_send, down_recv, down_keep,
):
    line = Line(chips)
    group = 2 * chips
    seq = lax.axis_index("seq")
    own = line.own
    share = blocks_ref.shape[1]
    rows, width = x_ref.shape
    piece = rows // batches
    length, span = q_ref.shape[1:]
    per = 128 * seqs * group // width
    steps, need = length // block, WINDOW // block
    has_left, has_right = seq > 0, seq < seqs - 1
    unit_loads = [
        pltpu.make_async_copy(gate_hbm, gate, unit_sem.at[0]),
        pltpu.make_async_copy(up_hbm, up, unit_sem.at[1]),
    ]
    for item in unit_loads:
        item.start()
    for index, source in enumerate((wq_ref, wk_ref, wv_ref)):
        for member, first, home, size in column_parts(seqs, group, share, span):
            first = first + index * span
            blocks_ref[member, :, first : first + size] = source[:, home : home + size]
    meet(greet_group(group) + greet_seq(seqs))

    def block_at(run, member):
        return w.at[rows_at(run * group + member, share)]

    def block_swap(peer, member):
        return pltpu.make_async_remote_copy(
            src_ref=blocks_ref.at[peer],
            dst_ref=block_at(seq, member),
            send_sem=swap_send.at[peer],
            recv_sem=w_recv.at[seq, member],
            device_id={"fsdp": peer},
            device_id_type=MESH,
        )

    def block_share(run, member, peer):
        return pltpu.make_async_remote_copy(
            src_ref=block_at(run, member),
            dst_ref=block_at(run, member),
            send_sem=share_send.at[peer, member],
            recv_sem=w_recv.at[run, member],
            device_id={"seq": peer},
            device_id_type=MESH,
        )

    def tile_to_seq(peer, place):
        return pltpu.make_async_remote_copy(
            src_ref=tile_ref.at[0],
            dst_ref=gains.at[own, place],
            send_sem=tile_send.at[peer],
            recv_sem=tile_recv.at[place],
            device_id={"seq": peer},
            device_id_type=MESH,
        )

    def tiles_to_group(peer, member):
        return pltpu.make_async_remote_copy(
            src_ref=gains.at[member],
            dst_ref=gains.at[member],
            send_sem=tile_across.at[peer],
            recv_sem=tile_back.at[member],
            device_id={"fsdp": peer},
            device_id_type=MESH,
        )

    def others(count, me, act):
        pl.loop(1, count)(lambda ahead: act(lax.rem(me + ahead, count)))

    others(seqs, seq, lambda peer: tile_to_seq(peer, seq).start())
    down = Share(
        seqs, down_hbm.at[pl.ds(0, wd_ref.shape[1])], wd_ref, down_send, down_recv, down_keep
    )
    down.begin()
    others(group, own, lambda peer: block_swap(peer, own).start())
    spreads = [
        Spread(line, x_ref.at[pl.ds(batch * piece, piece)], buf.at[batch], send.at[batch], recv.at[batch])
        for batch in range(batches)
    ]
    spreads[0].begin()
    gains[own, seq] = tile_ref[0]
    w[rows_at(seq * group + own, share), :] = blocks_ref[own]
    others(seqs, seq, lambda peer: block_share(seq, own, peer).start())
    for batch in range(batches):
        buf[batch, own] = x_ref[batch * piece : (batch + 1) * piece, :]
    others(seqs, seq, lambda peer: tile_to_seq(peer, peer).wait_recv())
    others(group, own, lambda peer: tiles_to_group(peer, own).start())
    for item in unit_loads:
        item.wait()
    cell = units.shape[2] // 2 // seqs
    for member in range(group):
        for run in range(seqs):
            home = (run * group + member) * cell
            for index, source in enumerate((gate, up)):
                first = (index * seqs + run) * cell
                units[member, :, first : first + cell] = source[:, home : home + cell]
    unit_swap = Swap(group, units, own_units_ref, unit_send, unit_recv, unit_keep)

    @pl.when(jnp.logical_not(has_left))
    def _():
        pad[:, :WINDOW, :] = jnp.zeros((batches, WINDOW, 2 * span), jnp.bfloat16)

    def pass_block(member):
        block_swap(member, member).wait_recv()
        others(seqs, seq, lambda peer: block_share(seq, member, peer).start())

    others(group, own, pass_block)
    down.pass_on([0])
    others(group, own, lambda peer: tiles_to_group(peer, peer).wait_recv())
    for column in range(width // 128):
        total = 0.0
        for place in range(column * per, (column + 1) * per):
            total = total + gains[place % group, place // group, 0:1, :]
        gain[0:1, column * 128 : (column + 1) * 128] = total

    def sides(far, act):
        @pl.loop(0, 2)
        def _(side):
            place = line.chip + far * (2 * side - 1)
            valid = (place >= 0) & (place < chips) & ((side == 0) | (far > 0))
            pl.when(valid)(lambda: act(place))

    def kept(batch, place):
        here = rows_at(place, block)
        return pltpu.make_async_copy(
            normed.at[batch, here], g_ref.at[batch, here], keep.at[batch, place]
        )

    def norm_pair(batch, place):
        spreads[batch].across(place * 2 + 1 - line.core)

        @pl.loop(0, 2)
        def _(member):
            @pl.loop(0, piece // 64)
            def _(chunk):
                values = buf[batch, place * 2 + member, rows_at(chunk, 64), :].astype(jnp.float32)
                there = pl.multiple_of(place * block + member * piece + chunk * 64, 64)
                normed[batch, pl.ds(there, 64), :] = to_half(normalize(values, gain[0:1, :]))

        kept(batch, place).start()

    def halo(batch, step, peer):
        there = pl.multiple_of(WINDOW + (step + steps - need) * block, block)
        return pltpu.make_async_remote_copy(
            src_ref=pad.at[batch, pl.ds(there, block)],
            dst_ref=pad.at[batch, rows_at(step, block)],
            send_sem=halo_send.at[batch, step],
            recv_sem=halo_recv.at[batch, step],
            device_id={"seq": peer},
            device_id_type=MESH,
        )

    def project(batch, place):
        here = rows_at(place, block)
        got = to_half(dot_nn(normed[batch, here, :], w[...]))
        q_ref[batch, here, :] = got[:, :span]
        pad[batch, pl.ds(pl.multiple_of(WINDOW + place * block, block), block), :] = got[:, span:]

        @pl.when(has_right & (place >= steps - need))
        def _():
            halo(batch, place - (steps - need), seq + 1).start()

    @pl.loop(0, chips)
    def _(far):
        pl.when(far > 0)(lambda: spreads[0].relay(far))
        pl.when(far == chips - 2)(spreads[1].begin)
        sides(far, lambda place: norm_pair(0, place))

    spreads[1].relay(1)

    def have_block(run, member):
        block_share(run, member, seq).wait_recv()

    others(seqs, seq, lambda run: pl.loop(0, group)(lambda member: have_block(run, member)))
    w_kept = pltpu.make_async_copy(w, w_out_ref, w_keep)
    w_kept.start()
    gains_kept = pltpu.make_async_copy(gains, gains_ref, gain_keep)
    gains_kept.start()
    pl.loop(0, steps)(lambda place: project(0, place))

    @pl.loop(2, chips)
    def _(far):
        spreads[1].relay(far)

    unit_swap.begin()

    @pl.loop(0, chips)
    def _(far):
        sides(far, lambda place: norm_pair(1, place))
        sides(far, lambda place: project(1, place))

    def pad_kept(batch):
        return pltpu.make_async_copy(pad.at[batch], pad_ref.at[batch], pad_keep.at[batch])

    for batch in range(batches):
        vt[:, WINDOW:] = pad[batch, WINDOW:, span:].T

        @pl.loop(0, steps)
        def _(turn, batch=batch):
            step = steps - 1 - turn

            @pl.when(step < need)
            def _():
                arrived = rows_at(step, block)
                pl.when(has_left)(lambda: halo(batch, step, seq).wait_recv())
                vt[:, arrived] = pad[batch, arrived, span:].T

            begin = pl.multiple_of(step * block, block)
            keys = pl.ds(begin, block + WINDOW)
            rows = pl.ds(begin, block)
            low = low_ref[batch, :, rows]
            for pair in range(span // PAIR):
                lanes = slice(pair * PAIR, (pair + 1) * PAIR)
                q_pair = q_ref[batch, rows, lanes] * jnp.asarray(HEAD**-0.5, jnp.bfloat16)
                k_rows = pad[batch, keys, lanes]
                values = vt[lanes, keys]
                mixed = []
                for half in range(2):
                    scores = masked_scores(k_rows, head_lanes(q_pair, half), low)
                    top = jnp.max(scores, axis=0, keepdims=True)
                    expo = jnp.exp(scores - top)
                    total = jnp.sum(expo, axis=0, keepdims=True)
                    mixed.append(dot_nn(values, to_half(expo)) / total)
                    row = pair * 2 + half
                    lse_ref[batch, row : row + 1, rows] = top + jnp.log(total)
                lane = lax.broadcasted_iota(jnp.int32, mixed[0].shape, 0)
                out_ref[batch, rows, lanes] = to_half(jnp.where(lane < HEAD, mixed[0], mixed[1]).T)

        pad_kept(batch).start()

    for batch in range(batches):
        spreads[batch].sent()
    others(seqs, seq, lambda peer: tile_to_seq(peer, seq).wait_send())
    others(group, own, lambda peer: block_swap(peer, own).wait_send())
    others(group, own, lambda peer: tiles_to_group(peer, own).wait_send())
    others(
        seqs,
        seq,
        lambda peer: pl.loop(0, group)(lambda member: block_share(seq, member, peer).wait_send()),
    )

    @pl.loop(0, need)
    def _(step):
        for batch in range(batches):
            pl.when(has_right)(lambda batch=batch: halo(batch, step, seq).wait_send())

    w_kept.wait()
    gains_kept.wait()
    unit_swap.end()
    down.end()
    for batch in range(batches):
        pad_kept(batch).wait()

        @pl.loop(0, steps)
        def _(place, batch=batch):
            kept(batch, place).wait()


def start(seqs, chips, batches, block, tile, x, weights, unit_weights, down, low, collective):
    rows, width = x.shape
    group = 2 * chips
    length = group * rows // batches
    share = weights[0].shape[0]
    span = width // group
    cols = 3 * span
    wide = unit_weights[0].shape[1]
    cells = 2 * wide // group
    piece = rows // batches
    padded = length + WINDOW
    half = jnp.bfloat16
    need = WINDOW // block
    return pl.pallas_call(
        functools.partial(start_kernel, seqs, chips, batches, block),
        out_shape=[
            jax.ShapeDtypeStruct((batches, length, width), half),
            jax.ShapeDtypeStruct((batches, length, span), half),
            jax.ShapeDtypeStruct((batches, length, span), half),
            jax.ShapeDtypeStruct((batches, span // HEAD, length), jnp.float32),
            jax.ShapeDtypeStruct((batches, padded, 2 * span), half),
            jax.ShapeDtypeStruct((group, seqs, 8, 128), jnp.float32),
            jax.ShapeDtypeStruct((width, cols), half),
            jax.ShapeDtypeStruct((group, share, cells), half),
            jax.ShapeDtypeStruct((seqs, down.shape[0] // 2, width), half),
        ],
        in_specs=[VMEM_SPEC] * 5 + [ANY_SPEC] * 2 + [VMEM_SPEC] * 2,
        out_specs=[ANY_SPEC] + [VMEM_SPEC] * 3 + [ANY_SPEC] * 5,
        scratch_shapes=[
            pltpu.VMEM((share, wide), half),
            pltpu.VMEM((share, wide), half),
            pltpu.VMEM((group, share, cells), half),
            pltpu.VMEM((group, share, cols), half),
            pltpu.VMEM((batches, group, piece, width), half),
            pltpu.VMEM((batches, length, width), half),
            pltpu.VMEM((batches, padded, 2 * span), half),
            pltpu.VMEM((span, padded), half),
            pltpu.VMEM((8, width), jnp.float32),
            pltpu.VMEM((group, seqs, 8, 128), jnp.float32),
            pltpu.VMEM((width, cols), half),
            sems(2),
            sems(batches, 3, group, PARTS // 2),
            sems(batches, group, PARTS // 2),
            sems(batches, chips),
            sems(group),
            sems(seqs, group),
            sems(seqs, group),
            sems(seqs),
            sems(group),
            sems(seqs),
            sems(group),
            pltpu.SemaphoreType.DMA,
            pltpu.SemaphoreType.DMA,
            sems(batches, need),
            sems(batches, need),
            sems(batches),
            sems(group),
            sems(group),
            pltpu.SemaphoreType.DMA,
            sems(seqs, 2, 1),
            sems(seqs, 2, 1),
            pltpu.SemaphoreType.DMA,
        ],
        compiler_params=comm_params(collective, 62),
        cost_estimate=cost(
            2 * group * rows * width * cols + 8 * batches * length * span * (WINDOW + block),
            300 * MIB,
            2 * group * rows * width * 2,
        ),
        name="start",
    )(tile, x, *weights, *unit_weights, down, low)


def branch_kernel(
    seqs, chips, a_ref, w_ref, d_ref, units_ref, down_hbm, x_ref, gain_ref,
    middle_ref, normed_ref, gd_ref, w_units_ref, wd_ref,
    out_ref, acc, cross_out, line_out, cross_in, line_in, sum_send, sum_recv,
    send, recv, d_keep, share_send, share_recv, share_keep,
    down_send, down_recv, down_keep,
):
    line = Line(chips)
    rows = out_ref.shape[0]

    def product(slot, tile):
        return dot_nn(left_rows(a_ref, slot, rows), w_ref[:, rows_at(tile, TILE)])

    meet(line.greet() + greet_seq(seqs))
    reduce = Reduce(
        line, product, out_ref, acc, cross_out, line_out, cross_in, line_in, sum_send, sum_recv
    )
    spread = Spread(line, d_ref, gd_ref, send, recv)
    units = Share(seqs, units_ref, w_units_ref, share_send, share_recv, share_keep)
    d_kept = pltpu.make_async_copy(d_ref, gd_ref.at[line.own], d_keep)
    half = wd_ref.shape[1]
    down = Share(seqs, down_hbm.at[pl.ds(half, half)], wd_ref, down_send, down_recv, down_keep)
    down.begin()
    units.begin()
    spread.begin()
    d_kept.start()

    @pl.loop(0, chips)
    def _(step):
        def also(tile):
            @pl.when((step == chips // 2) & (tile == 0))
            def _():
                down.pass_on([0])
                units.pass_on([0])

            pl.when(step < chips - 1)(lambda: spread.relay_part(step + 1, tile))

        reduce.level(chips - 1 - step, also)


    @pl.loop(0, rows // 32)
    def _(chunk):
        here = rows_at(chunk, 32)
        middle = x_ref[here, :].astype(jnp.float32) + out_ref[here, :]
        middle_ref[here, :] = middle
        normed_ref[here, :] = to_half(normalize(middle, gain_ref[0:1, :]))

    spread.rest()
    spread.sent()
    reduce.sent()
    d_kept.wait()
    units.end()
    down.end()


def branch_sum(seqs, chips, a, w, d_rows, units, down, x, gain, collective):
    rows, width = d_rows.shape
    group = 2 * chips
    half = jnp.bfloat16
    return pl.pallas_call(
        functools.partial(branch_kernel, seqs, chips),
        out_shape=[
            jax.ShapeDtypeStruct((rows, width), jnp.float32),
            jax.ShapeDtypeStruct((rows, width), half),
            jax.ShapeDtypeStruct((group, rows, width), half),
            jax.ShapeDtypeStruct((seqs,) + units.shape, half),
            jax.ShapeDtypeStruct((seqs, down.shape[0] // 2, width), half),
        ],
        in_specs=[VMEM_SPEC] * 7,
        out_specs=[VMEM_SPEC, VMEM_SPEC] + [ANY_SPEC] * 3,
        scratch_shapes=[pltpu.VMEM((rows, width), jnp.float32)]
        + Reduce.scratch(chips, rows, width)
        + [sems(3, group, PARTS), sems(group, PARTS), pltpu.SemaphoreType.DMA]
        + [sems(seqs, 2, 1), sems(seqs, 2, 1), pltpu.SemaphoreType.DMA] * 2,
        compiler_params=comm_params(collective),
        cost_estimate=cost(
            2 * group * rows * width * w.shape[0], 250 * MIB, 3 * group * rows * width * 2
        ),
        name="branch_sum",
    )(a, w, d_rows, units, down, x, gain)


class PairReduce:
    def __init__(self, line, product, out, acc, keep, cross_out, cross_in, line_out, line_in, send, recv):
        self.line, self.product, self.out, self.acc, self.keep = line, product, out, acc, keep
        self.cross_out, self.cross_in, self.line_out, self.line_in = cross_out, cross_in, line_out, line_in
        self.send, self.recv = send, recv
        self.tiles = keep.shape[1] // TILE

    @staticmethod
    def scratch(chips, piece, width):
        half = jnp.bfloat16
        return [
            pltpu.VMEM((piece, width), half),
            pltpu.VMEM((2, piece, width), half),
            pltpu.VMEM((2, piece, width), half),
            pltpu.VMEM((chips + 1, piece, width), half),
            pltpu.SemaphoreType.DMA((3, width // TILE)),
            pltpu.SemaphoreType.DMA((chips + 3, width // TILE)),
        ]

    def cross(self, parity, tile):
        here = rows_at(tile, TILE)
        return pltpu.make_async_remote_copy(
            src_ref=self.cross_out.at[:, here],
            dst_ref=self.cross_in.at[parity, :, here],
            send_sem=self.send.at[0, tile],
            recv_sem=self.recv.at[self.line.chips + 1 + parity, tile],
            device_id={"fsdp": self.line.other},
            device_id_type=MESH,
        )

    def along(self, parity, landing, tile, peer):
        here = rows_at(tile, TILE)
        return pltpu.make_async_remote_copy(
            src_ref=self.line_out.at[parity, :, here],
            dst_ref=self.line_in.at[landing, :, here],
            send_sem=self.send.at[1 + parity, tile],
            recv_sem=self.recv.at[landing, tile],
            device_id={"fsdp": peer},
            device_id_type=MESH,
        )

    def steps(self):
        return 2 * self.line.chips - 1

    def step(self, step):
        line, keep = self.line, self.keep
        piece = keep.shape[0]
        right_side = line.chips - 1 - line.chip
        away = line.chips - 1 - step // 2
        second = lax.rem(step, 2)
        rightward = (right_side >= line.chip) == (second == 0)
        place = line.chip + jnp.where(rightward, away, -away)
        longer = jnp.maximum(right_side, line.chip)
        shorter = jnp.minimum(right_side, line.chip)
        count = longer - away + jnp.maximum(shorter - away, 0) + second
        parity = lax.rem(count + 2 * line.chips, 2)
        upstream = (rightward & line.has_left) | (jnp.logical_not(rightward) & line.has_right)

        @pl.when((place >= 0) & (place < line.chips))
        def _():
            wide = self.acc.shape[1]

            @pl.loop(0, keep.shape[1] // wide)
            def _(tile):
                here = rows_at(tile, wide)
                self.acc[...] = self.product(place, here)
                self.cross_out[:, here] = to_half(self.acc[rows_at(1 - line.core, piece), :])
                keep[:, here] = self.acc[rows_at(line.core, piece), :]
                for piece_of in range(wide // TILE):
                    self.cross(parity, tile * (wide // TILE) + piece_of).start()

            @pl.loop(0, self.tiles)
            def _(tile):
                here = rows_at(tile, TILE)
                self.cross(parity, tile).wait()
                keep[:, here] += self.cross_in[parity, :, here].astype(jnp.float32)

                @pl.when(away > 0)
                def _():
                    pl.when(count >= 2)(
                        lambda: self.along(parity, place, tile, line.own).wait_send()
                    )

                    @pl.when(upstream)
                    def _():
                        self.along(parity, place, tile, line.own).wait_recv()
                        self.line_out[parity, :, here] = to_half(
                            keep[:, here] + self.line_in[place, :, here].astype(jnp.float32)
                        )

                    @pl.when(jnp.logical_not(upstream))
                    def _():
                        self.line_out[parity, :, here] = to_half(keep[:, here])

                    @pl.when(rightward)
                    def _():
                        self.along(parity, place, tile, line.own + 2).start()

                    @pl.when(jnp.logical_not(rightward))
                    def _():
                        landing = jnp.where(away == 1, line.chips, place)
                        self.along(parity, landing, tile, line.own - 2).start()

                @pl.when(away == 0)
                def _():
                    self.out[:, here] = keep[:, here]

                    @pl.when(line.has_left)
                    def _():
                        self.along(parity, place, tile, line.own).wait_recv()
                        self.out[:, here] += self.line_in[place, :, here].astype(jnp.float32)

                    @pl.when(line.has_right)
                    def _():
                        self.along(parity, line.chips, tile, line.own).wait_recv()
                        self.out[:, here] += self.line_in[line.chips, :, here].astype(jnp.float32)

    def sent(self):
        for count in range(max(self.line.chips - 3, 0), self.line.chips - 1):
            pl.loop(0, self.tiles)(
                lambda tile, parity=count % 2: self.along(parity, 0, tile, self.line.own).wait_send()
            )


def feed_kernel(
    seqs, chips, batches, x_ref, w_hbm, wd_one, wd_two, gd_hbm, v_ref, cot_ref, gain_ref,
    dm_ref, db_ref, gain_grad_ref, hidden_hbm, grad_hbm, grad_in,
    buf, d_buf, h_buf, w_ref, wd_ref, d_ref, tiles, totals, acc, keep,
    load, d_sem, h_sem, tile_sem, send, recv, part_send, part_recv, wd_load, *sums,
):
    line = Line(chips)
    rows, width = x_ref.shape
    piece = rows // batches
    pair = 2 * piece
    units = wd_ref.shape[0]
    part = min(units, 2 * TILE)
    block = tiles.shape[1]
    loads = [
        pltpu.make_async_copy(w_hbm, w_ref, load.at[0]),
    ] + load_halves([wd_one, wd_two], wd_ref, wd_load)
    for item in loads:
        item.start()
    meet(line.greet() + greet_seq(seqs))
    spreads = [
        Spread(
            line,
            x_ref.at[pl.ds(batch * piece, piece)],
            buf.at[batch],
            send.at[batch],
            recv.at[batch],
        )
        for batch in range(batches)
    ]
    spreads[0].begin()
    for batch in range(batches):
        buf[batch, line.own] = x_ref[batch * piece : (batch + 1) * piece, :]

    def fetch(batch, place, side):
        return [
            pltpu.make_async_copy(
                gd_hbm.at[place * 2 + core, pl.ds(batch * piece, piece)],
                d_buf.at[side, pl.ds(core * piece, piece)],
                d_sem.at[side, core],
            )
            for core in range(2)
        ]

    def stored(batch, place):
        return [
            pltpu.make_async_copy(
                h_buf.at[pl.ds(core * piece, piece)],
                hidden_hbm.at[
                    pl.ds(pl.multiple_of((place * 2 + core) * rows + batch * piece, piece), piece)
                ],
                h_sem.at[core],
            )
            for core in range(2)
        ]

    def sides(far, act):
        @pl.loop(0, 2)
        def _(side):
            place = line.chip + far * (2 * side - 1)
            valid = (place >= 0) & (place < chips) & ((side == 0) | (far > 0))
            pl.when(valid)(lambda: act(place, side))

    def take(batch, far):
        def begin(place, side):
            for item in fetch(batch, place, side):
                item.start()

        sides(far, begin)
        pl.when(far > 0)(lambda: spreads[batch].relay(far))

    def compute(batch, far):
        def act(place, side):
            spreads[batch].across(place * 2 + 1 - line.core)
            for item in fetch(batch, place, side):
                item.wait()

            def free():
                for item in stored(batch, place):
                    item.wait()

            if batch:
                free()
            else:
                pl.when((far > 0) | (side > 0))(free)
            there = rows_at(place, pair)

            @pl.loop(0, units // part)
            def _(tile):
                first = rows_at(tile, part)
                second = rows_at(units // part + tile, part)
                values = buf[batch, pl.ds(place * 2, 2), :, :].reshape(pair, width)
                gate = dot_nn(values, w_ref[:, first])
                up = dot_nn(values, w_ref[:, second])
                d_hidden = dot_nt(d_buf[side], wd_ref[first, :])
                sigma = jax.nn.sigmoid(gate)
                swish = gate * sigma
                h_buf[:, first] = to_half(swish * up)
                slope = sigma * (1.0 + gate * (1.0 - sigma))
                d_ref[batch, there, first] = to_half(d_hidden * up * slope)
                d_ref[batch, there, second] = to_half(d_hidden * swish)

            for item in stored(batch, place):
                item.start()

        sides(far, act)

    def product(batch):
        def get(place, here):
            return dot_nt(d_ref[batch, rows_at(place, pair), :], w_ref[here, :])

        return get

    reduces = [
        PairReduce(line, product(batch), totals.at[batch], acc, keep, *sums[6 * batch : 6 * batch + 6])
        for batch in range(batches)
    ]

    count = width // block
    seq = lax.axis_index("seq")

    near, far_off = seq_peers(seqs)
    soon = len(near)
    order = [peer * 2 for peer in near] + [peer * 2 for peer in far_off] + [seq * 2]
    order = order + [peer * 2 + 1 for peer in near] + [peer * 2 + 1 for peer in far_off] + [seq * 2 + 1]

    def tile_at(turn):
        tile = order[-1]
        for index in range(len(order) - 1):
            tile = jnp.where(turn == index, order[index], tile)
        return tile

    def grad_stored(turn):
        slot = lax.rem(turn, 2)
        return pltpu.make_async_copy(
            tiles.at[slot], grad_hbm.at[rows_at(tile_at(turn), block)], tile_sem.at[slot]
        )

    parts = ToPeers(seqs, near, grad_hbm, grad_in, part_send, part_recv)

    def leave(turn):
        grad_stored(turn).wait()
        for index in range(soon):
            pl.when(turn == index)(lambda index=index: parts.move(index).start())

    def weight_grad(turn):
        slot = lax.rem(turn, 2)
        size = min(4 * TILE, 2 * units)
        tile = tile_at(turn)

        @pl.loop(0, 2 * units // size)
        def _(column):
            here = rows_at(column, size)
            got = 0.0
            for batch in range(batches):
                left = buf[batch, :, :, rows_at(tile, block)].reshape(2 * chips * piece, block)
                got = got + contract_rows(left, d_ref[batch, :, here])
            tiles[slot, :, here] = to_half(got)

        pl.when(turn > 0)(lambda: leave(turn - 1))
        grad_stored(turn).start()

    def norm_batch(batch):
        own = pl.ds(batch * piece, piece)

        def put(here, d_values):
            there = pl.ds(pl.multiple_of(here.start + batch * piece, here.size), here.size)
            d_middle = cot_ref[there, :].astype(jnp.float32) + d_values
            dm_ref[there, :] = d_middle
            db_ref[there, :] = to_half(d_middle)

        norm_back(piece, v_ref.at[own], totals.at[batch], gain_ref, gain_grad_ref, put)

    gain_grad_ref[...] = jnp.zeros_like(gain_grad_ref)
    for item in loads:
        item.wait()
    last = 2 * chips - 2

    @pl.loop(0, chips)
    def _(far):
        take(0, far)
        pl.when(far == chips - 2)(spreads[1].begin)
        compute(0, far)

    @pl.loop(0, chips - 1)
    def _(far):
        take(1, far)
        reduces[0].step(2 * far)
        reduces[0].step(2 * far + 1)
        compute(1, far)

    take(1, chips - 1)
    compute(1, chips - 1)

    @pl.loop(0, 2)
    def _(step):
        reduces[1].step(step)
        weight_grad(step)

    reduces[0].step(last)
    norm_batch(0)

    @pl.loop(2, last)
    def _(step):
        reduces[1].step(step)
        pl.when(step < count)(lambda: weight_grad(step))

    @pl.loop(last, max(count, last))
    def _(tile):
        weight_grad(tile)

    reduces[1].step(last)
    norm_batch(1)
    for batch in range(batches):
        spreads[batch].sent()
        reduces[batch].sent()
    for item in stored(1, 0):
        item.wait()
    leave(count - 1)
    parts.end()


def feed_forward(seqs, chips, batches, x, w, wd_halves, group_d, middle, cot, gain, collective):
    rows, width = x.shape
    group = 2 * chips
    units = w.shape[1] // 2
    piece = rows // batches
    block = width // seqs // 2
    half = jnp.bfloat16
    return pl.pallas_call(
        functools.partial(feed_kernel, seqs, chips, batches),
        out_shape=[
            jax.ShapeDtypeStruct((rows, width), jnp.float32),
            jax.ShapeDtypeStruct((rows, width), half),
            jax.ShapeDtypeStruct((8, width), jnp.float32),
            jax.ShapeDtypeStruct((group * rows, units), half),
            jax.ShapeDtypeStruct((width, 2 * units), half),
            jax.ShapeDtypeStruct((near_count(seqs), block, 2 * units), half),
        ],
        in_specs=[VMEM_SPEC] + [ANY_SPEC] * 4 + [VMEM_SPEC] * 3,
        out_specs=[VMEM_SPEC] * 3 + [ANY_SPEC] * 3,
        scratch_shapes=[
            pltpu.VMEM((batches, group, piece, width), half),
            pltpu.VMEM((2, 2 * piece, width), half),
            pltpu.VMEM((2 * piece, units), half),
            pltpu.VMEM(w.shape, half),
            pltpu.VMEM((units, width), half),
            pltpu.VMEM((batches, group * piece, 2 * units), half),
            pltpu.VMEM((2, block, 2 * units), half),
            pltpu.VMEM((batches, piece, width), jnp.float32),
            pltpu.VMEM((2 * piece, 2 * TILE), jnp.float32),
            pltpu.VMEM((piece, width), jnp.float32),
            sems(2),
            sems(2, 2),
            sems(2),
            sems(2),
            sems(batches, 3, group, PARTS // 2),
            sems(batches, group, PARTS // 2),
            sems(seqs),
            sems(seqs),
            sems(2, seqs),
        ]
        + PairReduce.scratch(chips, piece, width) * batches,
        compiler_params=comm_params(collective, 63),
        cost_estimate=cost(
            14 * group * rows * width * units, 400 * MIB, 2 * group * rows * width * 2
        ),
        name="feed_forward",
    )(x, w, *wd_halves, group_d, middle, cot, gain)


def branch_back_kernel(
    seqs, chips, batches, x_ref, w_ref, att_ref, middle_ref, hidden_hbm, wd_one, wd_two, units_hbm, gd_hbm,
    d_ref, layer_ref, out_grad_ref, half_in, whole_in, down_hbm, down_in, far_in,
    out_ref, buf, hidden_ref, wd_ref, grad_acc, rights, tiles, send, recv, load, right_sem, tile_sem,
    part_send, part_recv, wd_load, down_send, down_recv, far_send, far_recv, down_keep, acc, cross_out, line_out, cross_in, line_in, sum_send, sum_recv,
):
    line = Line(chips)
    rows = x_ref.shape[0]
    piece = rows // batches
    width = x_ref.shape[1]
    loads = [
        pltpu.make_async_copy(hidden_hbm, hidden_ref, load.at[0]),
    ] + load_halves([wd_one, wd_two], wd_ref, wd_load)
    for item in loads:
        item.start()

    def product(slot, tile):
        return dot_nn(left_rows(hidden_ref, slot, rows), wd_ref[:, rows_at(tile, TILE)])

    part = rights.shape[2]
    count = width // part

    def right(tile):
        slot = lax.rem(tile, 2)
        return pltpu.make_async_copy(
            gd_hbm.at[:, rows_at(tile, part)], rights.at[slot], right_sem.at[slot]
        )

    def stored(tile):
        slot = lax.rem(tile, 2)
        return pltpu.make_async_copy(
            tiles.at[slot], down_hbm.at[:, rows_at(tile, part)], tile_sem.at[slot]
        )

    def weight_grad(tile):
        right(tile).wait()
        pl.when(tile + 1 < count)(lambda: right(tile + 1).start())
        pl.when(tile >= 2)(lambda: stored(tile - 2).wait())
        slot = lax.rem(tile, 2)
        size = min(TILE, hidden_ref.shape[1])

        @pl.loop(0, hidden_ref.shape[1] // size)
        def _(row):
            here = rows_at(row, size)
            tiles[slot, here, :] = to_half(contract_rows(hidden_ref[:, here], rights[slot]))

        stored(tile).start()

    right(0).start()
    meet(line.greet() + greet_seq(seqs))
    near, far_off = seq_peers(seqs)
    soon = len(near)
    halves = ToPeers(
        seqs, near, units_hbm, half_in, part_send.at[0], part_recv.at[0], half_in.shape[1]
    )
    wholes = ToPeers(seqs, far_off, units_hbm, whole_in, part_send.at[1], part_recv.at[1])
    down = ToPeers(
        seqs, near, down_hbm, down_in.at[pl.ds(0, soon)], down_send, down_recv
    )
    down_far = ToPeers(seqs, far_off, down_hbm, far_in, far_send, far_recv)
    down_kept = pltpu.make_async_copy(
        down_hbm.at[rows_at(lax.axis_index("seq"), down_in.shape[1])], down_in.at[soon], down_keep
    )
    spread = Spread(line, x_ref, buf, send, recv)
    reduce = Reduce(
        line, product, out_ref, acc, cross_out, line_out, cross_in, line_in, sum_send, sum_recv
    )
    spread.begin()
    halves.begin()
    wholes.begin()
    buf[line.own] = x_ref[...]
    grad_acc[...] = jnp.zeros_like(grad_acc)

    def use(slot):
        got = to_half(dot_nt(buf[slot], w_ref[...]))
        for batch in range(batches):
            d_ref[batch, rows_at(slot, piece), :] = got[batch * piece : (batch + 1) * piece]
        mixed = left_rows(att_ref, slot, rows)

        @pl.loop(0, width // TILE)
        def _(tile):
            here = rows_at(tile, TILE)
            grad_acc[:, here] += contract_rows(mixed, buf[slot, :, here])

    for item in loads:
        item.wait()

    reduce.level(chips - 1, lambda tile: None)
    pl.loop(0, count)(weight_grad)
    stored(count - 2).wait()
    stored(count - 1).wait()
    down.begin()
    down_far.begin()
    down_kept.start()
    spread.relay(1)
    spread.each(0, use)

    @pl.loop(1, chips)
    def _(step):
        def also(tile):
            pl.when(step < chips - 1)(lambda: spread.relay_part(step + 1, tile))

        reduce.level(chips - 1 - step, also)
        spread.each(step, use)

    spread.each(chips, use)

    @pl.loop(0, rows // 32)
    def _(chunk):
        here = rows_at(chunk, 32)
        layer_ref[here, :] = to_half(middle_ref[here, :] + out_ref[here, :])

    out_grad_ref[...] = to_half(grad_acc[...])
    spread.sent()
    reduce.sent()
    halves.end()
    wholes.end()
    down.end()
    down_far.end()
    down_kept.wait()


def branch_back(seqs, chips, batches, x, w, attended, middle, hidden, wd_halves, unit_part, group_d, collective):
    rows, width = x.shape
    group = 2 * chips
    length = group * rows // batches
    span = w.shape[0]
    half = jnp.bfloat16
    part = 256 if group * rows <= 2048 else 128
    near, run = near_count(seqs), width // seqs
    units = hidden.shape[1]
    return pl.pallas_call(
        functools.partial(branch_back_kernel, seqs, chips, batches),
        out_shape=[
            jax.ShapeDtypeStruct((batches, length, span), half),
            jax.ShapeDtypeStruct((rows, width), half),
            jax.ShapeDtypeStruct((span, width), half),
            jax.ShapeDtypeStruct((near, run // 2, unit_part.shape[1]), half),
            jax.ShapeDtypeStruct((seqs - 1 - near, run, unit_part.shape[1]), half),
            jax.ShapeDtypeStruct((units, width), half),
            jax.ShapeDtypeStruct((near + 1, units // seqs, width), half),
            jax.ShapeDtypeStruct((seqs - 1 - near, units // seqs // 4, width), half),
        ],
        in_specs=[VMEM_SPEC] * 4 + [ANY_SPEC] * 5,
        out_specs=[VMEM_SPEC] * 3 + [ANY_SPEC] * 5,
        scratch_shapes=[
            pltpu.VMEM((rows, width), jnp.float32),
            pltpu.VMEM((group, rows, width), half),
            pltpu.VMEM(hidden.shape, half),
            pltpu.VMEM((units, width), half),
            pltpu.VMEM((span, width), jnp.float32),
            pltpu.VMEM((2, group * rows, part), half),
            pltpu.VMEM((2, units, part), half),
            sems(3, group, PARTS),
            sems(group, PARTS),
            sems(2),
            sems(2),
            sems(2),
            sems(2, seqs),
            sems(2, seqs),
            sems(2, seqs),
            sems(seqs),
            sems(seqs),
            sems(seqs),
            sems(seqs),
            pltpu.SemaphoreType.DMA,
        ]
        + Reduce.scratch(chips, rows, width),
        compiler_params=comm_params(collective, 62),
        cost_estimate=cost(
            2 * group * rows * width * (2 * span + 2 * units),
            250 * MIB,
            2 * group * rows * width * 2,
        ),
        name="branch_back",
    )(x, w, attended, middle, hidden, *wd_halves, unit_part, group_d.reshape(group * rows, width))


def attention_back_kernel(
    seqs, chips, block, q_ref, pad_ref, low_ref, lse_ref, d_ref, part_hbm, in_one, in_two, in_far,
    w_ref, g_hbm, v_ref, dm_hbm, gain_ref, mlp_gain_ref, out_ref, down_hbm,
    grad_hbm, wq_ref, wk_ref, wv_ref, wo_hbm, tile_ref, gate_hbm, up_hbm, down_in,
    grad_ref, wo_ref, gate_ref, up_ref, result_sem, down_send, down_recv,
    dk, dv, kt, heads, back_out, back_in, unit_parts, unit_sums, units, lefts, parts, sums, cols, out_in,
    totals, gain_acc, gain_out, gain_in, gain_sum, gain_back, acc, keep,
    halo_send, halo_recv, unit_load, unit_send, unit_recv, unit_keep, dm_load, left_sem,
    part_send, part_recv, cols_send, cols_recv, out_send, out_recv,
    gain_send, gain_recv, back_send, back_recv, *line_sums,
):
    line = Line(chips)
    group = 2 * chips
    seq = lax.axis_index("seq")
    own = line.own
    batches, length, span = q_ref.shape
    rows, width = v_ref.shape
    piece = rows // batches
    pair_rows = 2 * piece
    depth = 3 * span
    run = width // seqs
    share = run // group
    part = lefts.shape[3]
    steps, need = length // block, WINDOW // block
    first = length - WINDOW
    has_left, has_right = seq > 0, seq < seqs - 1
    scale = jnp.asarray(HEAD**-0.5, jnp.bfloat16)

    def others(count, me, act):
        pl.loop(1, count)(lambda ahead: act(lax.rem(me + ahead, count)))

    def unit_loaded(turn, place, source):
        slot = lax.rem(turn, 2)
        return pltpu.make_async_copy(source, unit_parts.at[slot, place], unit_load.at[slot, place])

    def load_units(turn):
        member = lax.rem(own + turn, group)
        unit_loaded(turn, 0, part_hbm.at[rows_at(seq * group + member, share)]).start()
        soon = in_one.shape[0]
        for index in range(seqs - 1):

            def fetch(source, index=index):
                unit_loaded(turn, index + 1, source).start()

            if index < soon:

                @pl.when(member < chips)
                def _(index=index, fetch=fetch):
                    fetch(in_one.at[index, rows_at(member, share)])

                @pl.when(member >= chips)
                def _(index=index, fetch=fetch):
                    fetch(in_two.at[index, rows_at(member - chips, share)])

            else:
                fetch(in_far.at[index - soon, rows_at(member, share)])

    load_units(1)
    dm_loaded = pltpu.make_async_copy(dm_hbm, grad_ref, dm_load)
    dm_loaded.start()
    meet(greet_group(group) + greet_seq(seqs))
    near, far_off = seq_peers(seqs)
    down = ToPeers(
        seqs, far_off, down_hbm, down_in, down_send, down_recv, down_in.shape[1] // 3
    )
    down.begin()
    swap = Swap(group, unit_sums, units, unit_send, unit_recv, unit_keep)

    @pl.loop(1, group + 1)
    def _(turn):
        member = lax.rem(own + turn, group)
        slot = lax.rem(turn, 2)
        pl.when(turn < group)(lambda: load_units(turn + 1))
        for place in range(seqs):
            unit_loaded(turn, place, part_hbm.at[rows_at(0, share)]).wait()

        @pl.loop(0, share // 16)
        def _(chunk):
            here = rows_at(chunk, 16)
            added = unit_parts[slot, 0, here, :].astype(jnp.float32)
            for place in range(1, seqs):
                added = added + unit_parts[slot, place, here, :].astype(jnp.float32)
            unit_sums[member, here, :] = to_half(added)

        pl.when(turn < group)(lambda: swap.move(member, own).start())
        pl.when(turn == group)(lambda: swap.kept().start())

    def halo(batch, step, peer):
        here = rows_at(step, block)
        return pltpu.make_async_remote_copy(
            src_ref=back_out.at[batch, here],
            dst_ref=back_in.at[batch, here],
            send_sem=halo_send.at[batch, step],
            recv_sem=halo_recv.at[batch, step],
            device_id={"seq": peer},
            device_id_type=MESH,
        )

    def attend_block(batch, step):
        begin = pl.multiple_of(step * block, block)
        keys = pl.ds(begin, block + WINDOW)
        rows = pl.ds(begin, block)
        low = low_ref[batch, :, rows]
        for pair in range(span // PAIR):
            lanes = slice(pair * PAIR, (pair + 1) * PAIR)
            q_pair = q_ref[batch, rows, lanes] * scale
            d_pair = d_ref[batch, rows, lanes]
            k_rows = pad_ref[batch, keys, lanes]
            v_rows = pad_ref[batch, keys, span + pair * PAIR : span + (pair + 1) * PAIR]
            k_cols = kt[lanes, keys]
            back = []
            for half in range(2):
                row = pair * 2 + half
                q_head = head_lanes(q_pair, half)
                d_head = head_lanes(d_pair, half)
                scores = masked_scores(k_rows, q_head, low)
                probs = jnp.exp(scores - lse_ref[batch, row : row + 1, rows])
                d_probs = dot_nt(v_rows, d_head)
                along = jnp.sum(probs * d_probs, axis=0, keepdims=True)
                d_scores = to_half(probs * (d_probs - along))
                dv[keys, lanes] += dot_nn(to_half(probs), d_head)
                dk[keys, lanes] += dot_nn(d_scores, q_head)
                back.append(dot_nn(k_cols, d_scores))
            at = lax.broadcasted_iota(jnp.int32, back[0].shape, 0)
            heads[batch, rows, lanes] = to_half(
                jnp.where(at < HEAD, back[0], back[1]).T
            )


        @pl.when(has_left & (step < need))
        def _():
            back_out[batch, rows, :span] = to_half(dk[rows, :])
            back_out[batch, rows, span:] = to_half(dv[rows, :])
            halo(batch, step, seq - 1).start()

        @pl.when(step == steps - 1)
        def _():
            heads[batch, :, span : 2 * span] = to_half(dk[WINDOW:, :])
            heads[batch, :, 2 * span :] = to_half(dv[WINDOW:, :])

    def add_halo(batch):
        @pl.when(has_right)
        def _():
            @pl.loop(0, need)
            def _(step):
                there = pl.ds(pl.multiple_of(step * block + first, block), block)
                halo(batch, step, seq).wait_recv()
                got = back_in[batch, rows_at(step, block), :].astype(jnp.float32)
                mine = heads[batch, there, span:].astype(jnp.float32)
                heads[batch, there, span:] = to_half(mine + got)

    def product(batch):
        def get(place, here):
            return dot_nt(heads[batch, rows_at(place, pair_rows), :], w_ref[here, :])

        return get

    reduces = [
        PairReduce(
            line, product(batch), totals.at[batch], acc, keep, *line_sums[6 * batch : 6 * batch + 6]
        )
        for batch in range(batches)
    ]
    last = 2 * chips - 2

    @pl.loop(0, 2 * steps)
    def _(turn):
        batch, step = turn // steps, lax.rem(turn, steps)

        @pl.when(step == 0)
        def _():
            kt[...] = pad_ref[batch, :, :span].T * scale
            dk[...] = jnp.zeros_like(dk)
            dv[...] = jnp.zeros_like(dv)

        attend_block(batch, step)
        after = turn - steps - 1
        pl.when(after == 0)(lambda: add_halo(0))

        @pl.when((after >= 0) & (2 * after < last))
        def _():
            reduces[0].step(2 * after)
            reduces[0].step(2 * after + 1)

    for after in range(steps - 1, chips - 1):
        reduces[0].step(2 * after)
        reduces[0].step(2 * after + 1)

    def left(tile):
        slot = lax.rem(tile, 2)
        return pltpu.make_async_copy(
            g_hbm.at[:, :, rows_at(tile, part)], lefts.at[slot], left_sem.at[slot]
        )

    heads_near = ToPeers(seqs, near + far_off, parts, sums, part_send, part_recv)
    left(0).start()
    add_halo(1)

    @pl.loop(0, width // part)
    def _(tile):
        left(tile).wait()
        pl.when(tile + 1 < width // part)(lambda: left(tile + 1).start())
        slot = lax.rem(tile, 2)
        got = contract_rows(lefts[slot, 0], heads[0])
        for batch in range(1, batches):
            got = got + contract_rows(lefts[slot, batch], heads[batch])
        parts[rows_at(tile, part), :] = to_half(got)

    heads_near.begin()
    from_seq = ToPeers(seqs, near + far_off, out_ref, out_in, out_send, out_recv)
    from_seq.begin()
    gain_acc[...] = jnp.zeros_like(gain_acc)
    dm_loaded.wait()

    def norm_batch(batch):
        mine = pl.ds(batch * piece, piece)

        def put(here, d_values):
            there = pl.ds(pl.multiple_of(here.start + batch * piece, here.size), here.size)
            grad_ref[there, :] += d_values

        norm_back(piece, v_ref.at[mine], totals.at[batch], gain_ref, gain_acc, put)

    pl.loop(0, 2)(reduces[1].step)
    reduces[0].step(last)
    norm_batch(0)
    pl.loop(2, last)(reduces[1].step)
    swap.end()
    cell = units.shape[2] // 2 // seqs
    for member in range(group):
        for place in range(seqs):
            column = (place * group + member) * cell
            for target, begin in ((gate_ref, 0), (up_ref, seqs * cell)):
                here = slice(begin + place * cell, begin + (place + 1) * cell)
                target[:, column : column + cell] = units[member, :, here]

    results = [
        pltpu.make_async_copy(source, target, result_sem.at[index])
        for index, (source, target) in enumerate(
            ((gate_ref, gate_hbm), (up_ref, up_hbm), (wo_ref, wo_hbm), (grad_ref, grad_hbm))
        )
    ]
    results[0].start()
    results[1].start()

    def block_swap(peer, member):
        return pltpu.make_async_remote_copy(
            src_ref=parts.at[rows_at(seq * group + peer, share)],
            dst_ref=cols.at[member],
            send_sem=cols_send.at[peer],
            recv_sem=cols_recv.at[member],
            device_id={"fsdp": peer},
            device_id_type=MESH,
        )

    heads_near.arrived()

    @pl.loop(0, run // 64)
    def _(chunk):
        here = rows_at(chunk, 64)
        there = pl.ds(pl.multiple_of(seq * run + chunk * 64, 64), 64)
        parts[there, :] = to_half(add_from_seq(parts[there, :], sums, here))

    others(group, own, lambda peer: block_swap(peer, own).start())
    cols[own] = parts[rows_at(seq * group + own, share), :]
    from_seq.arrived()
    out_rows = out_in.shape[1]
    wo_ref[...] = add_from_seq(out_ref[rows_at(seq, out_rows), :], out_in, slice(None))
    results[2].start()
    reduces[1].step(last)
    norm_batch(1)
    results[3].start()
    fold = 128 // share
    near = group // fold
    attn_row = jnp.sum(gain_acc[...], axis=0, keepdims=True)
    mlp_row = jnp.sum(mlp_gain_ref[...], axis=0, keepdims=True)
    gain_out[...] = jnp.zeros_like(gain_out)
    for place in range(width // 128):
        lanes = slice(place * 128, (place + 1) * 128)
        gain_out[place % near, place // near, 0:1, :] = attn_row[:, lanes]
        gain_out[place % near, place // near, 1:2, :] = mlp_row[:, lanes]

    def gain_group(peer, member):
        return pltpu.make_async_remote_copy(
            src_ref=gain_out.at[peer // fold],
            dst_ref=gain_in.at[member],
            send_sem=gain_send.at[peer],
            recv_sem=gain_recv.at[member],
            device_id={"fsdp": peer},
            device_id_type=MESH,
        )

    def gain_seq(peer, place):
        return pltpu.make_async_remote_copy(
            src_ref=gain_sum.at[peer],
            dst_ref=gain_back.at[place],
            send_sem=back_send.at[peer],
            recv_sem=back_recv.at[place],
            device_id={"seq": peer},
            device_id_type=MESH,
        )

    others(group, own, lambda peer: gain_group(peer, own).start())
    gain_in[own] = gain_out[own // fold]
    others(group, own, lambda peer: gain_group(peer, peer).wait_recv())
    gain_sum[...] = jnp.sum(gain_in[...], axis=0)
    others(seqs, seq, lambda peer: gain_seq(peer, seq).start())
    gain_back[seq] = gain_sum[seq]
    others(seqs, seq, lambda peer: gain_seq(peer, peer).wait_recv())
    tile_ref[...] = jnp.sum(gain_back[...], axis=0)
    others(group, own, lambda peer: block_swap(peer, peer).wait_recv())
    for index, target in enumerate((wq_ref, wk_ref, wv_ref)):
        for member, first, home, size in column_parts(seqs, group, share, span):
            first = first + index * span
            target[:, home : home + size] = cols[member, :, first : first + size]
    from_seq.sent()
    for item in results:
        item.wait()
    for batch in range(batches):
        reduces[batch].sent()

        @pl.when(has_left)
        def _(batch=batch):
            pl.loop(0, need)(lambda step: halo(batch, step, seq).wait_send())

    heads_near.sent()
    down.end()
    others(group, own, lambda peer: gain_group(peer, own).wait_send())
    others(group, own, lambda peer: block_swap(peer, own).wait_send())
    others(seqs, seq, lambda peer: gain_seq(peer, seq).wait_send())


def attention_back(
    seqs, chips, block, query, kv_pad, low, lse, d_att, part_own, parts_one, parts_two, parts_far, w, group_a,
    x, d_middle, gain, mlp_gain, out_part, down, collective,
):
    batches, length, span = query.shape
    padded = kv_pad.shape[1]
    rows, width = x.shape
    piece = rows // batches
    group = 2 * chips
    depth = w.shape[1]
    run = width // seqs
    share = run // group
    near = group // (128 // share)
    cells = part_own.shape[1]
    out_rows = out_part.shape[0] // seqs
    half, wide = jnp.bfloat16, jnp.float32
    part = 256 if batches * length <= 2048 else 128
    return pl.pallas_call(
        functools.partial(attention_back_kernel, seqs, chips, block),
        out_shape=[
            jax.ShapeDtypeStruct((rows, width), wide),
            jax.ShapeDtypeStruct((share, width), half),
            jax.ShapeDtypeStruct((share, width), half),
            jax.ShapeDtypeStruct((share, width), half),
            jax.ShapeDtypeStruct((out_rows, width), wide),
            jax.ShapeDtypeStruct((8, 128), wide),
            jax.ShapeDtypeStruct((share, cells // 2 * group), half),
            jax.ShapeDtypeStruct((share, cells // 2 * group), half),
            jax.ShapeDtypeStruct(
                (seqs - 1 - near_count(seqs), down.shape[0] // seqs // 4 * 3, width), half
            ),
        ],
        in_specs=[VMEM_SPEC] * 5
        + [ANY_SPEC] * 4
        + [VMEM_SPEC, ANY_SPEC, VMEM_SPEC, ANY_SPEC]
        + [VMEM_SPEC] * 3
        + [ANY_SPEC],
        out_specs=[ANY_SPEC, VMEM_SPEC, VMEM_SPEC, VMEM_SPEC, ANY_SPEC, VMEM_SPEC]
        + [ANY_SPEC] * 3,
        scratch_shapes=[
            pltpu.VMEM((rows, width), wide),
            pltpu.VMEM((out_rows, width), wide),
            pltpu.VMEM((share, cells // 2 * group), half),
            pltpu.VMEM((share, cells // 2 * group), half),
            sems(4),
            sems(seqs),
            sems(seqs),
            pltpu.VMEM((padded, span), wide),
            pltpu.VMEM((padded, span), wide),
            pltpu.VMEM((span, padded), half),
            pltpu.VMEM((batches, length, depth), half),
            pltpu.VMEM((batches, WINDOW, 2 * span), half),
            pltpu.VMEM((batches, WINDOW, 2 * span), half),
            pltpu.VMEM((2, seqs, share, cells), half),
            pltpu.VMEM((group, share, cells), half),
            pltpu.VMEM((group, share, cells), half),
            pltpu.VMEM((2, batches, length, part), half),
            pltpu.VMEM((width, depth), half),
            pltpu.VMEM((seqs - 1, run, depth), half),
            pltpu.VMEM((group, share, depth), half),
            pltpu.VMEM((seqs - 1, out_rows, width), half),
            pltpu.VMEM((batches, piece, width), wide),
            pltpu.VMEM((8, width), wide),
            pltpu.VMEM((near, seqs, 8, 128), wide),
            pltpu.VMEM((group, seqs, 8, 128), wide),
            pltpu.VMEM((seqs, 8, 128), wide),
            pltpu.VMEM((seqs, 8, 128), wide),
            pltpu.VMEM((2 * piece, TILE), wide),
            pltpu.VMEM((piece, width), wide),
            sems(batches, WINDOW // block),
            sems(batches, WINDOW // block),
            sems(2, seqs),
            sems(group),
            sems(group),
            pltpu.SemaphoreType.DMA,
            pltpu.SemaphoreType.DMA,
            sems(2),
            sems(seqs),
            sems(seqs),
            sems(group),
            sems(group),
            sems(seqs),
            sems(seqs),
            sems(group),
            sems(group),
            sems(seqs),
            sems(seqs),
        ]
        + PairReduce.scratch(chips, piece, width) * batches,
        compiler_params=comm_params(collective, 63),
        cost_estimate=cost(
            20 * batches * length * span * (WINDOW + block) + 4 * group * rows * width * depth,
            400 * MIB,
            3 * group * rows * width * 2,
        ),
        name="attention_back",
    )(
        query, kv_pad, low, lse, d_att, part_own, parts_one, parts_two, parts_far, w, group_a, x,
        d_middle, gain, mlp_gain, out_part, down,
    )


def finish_kernel(count, *refs):
    sources, targets = refs[:-count], refs[-count:]
    for source, target in zip(sources, targets[:-1]):
        target[...] = source[...].astype(target.dtype)
    added = 0.0
    for source in sources[count - 1 :]:
        added = added + jnp.sum(source[...].astype(jnp.float32), axis=0)
    targets[-1][...] = added


def finish(steps, arrays, parts, kinds):
    in_specs, out_specs, out_shape = [], [], []
    for item, kind in zip(arrays + parts[:1], kinds):
        rows, width = item.shape[-2:]
        block = (rows // steps, width)
        out_specs.append(pl.BlockSpec(block, lambda i: (i, 0)))
        out_shape.append(jax.ShapeDtypeStruct((rows, width), kind))
        if item.ndim == 2:
            in_specs.append(out_specs[-1])
    for item in parts:
        in_specs.append(pl.BlockSpec((item.shape[0],) + block, lambda i: (0, i, 0)))
    return pl.pallas_call(
        functools.partial(finish_kernel, len(kinds)),
        grid=(steps,),
        in_specs=in_specs,
        out_specs=out_specs,
        out_shape=out_shape,
        compiler_params=pltpu.CompilerParams(vmem_limit_bytes=63 * MIB),
        name="finish",
    )(*arrays, *parts)


def doc_starts(lengths, positions, batches, seq_len):
    table = lengths.reshape(batches, -1, lengths.shape[1])
    starts = jnp.cumsum(table, axis=2) - table
    per_batch = seq_len // table.shape[1]
    begins = (starts + (jnp.arange(table.shape[1], dtype=jnp.int32) * per_batch)[None, :, None]).reshape(
        batches, -1
    )
    before = begins[:, None, :] <= positions[None, :, None]
    return jnp.max(jnp.where(before, begins[:, None, :], 0), axis=2)


def body(
    tokens,
    cotangent,
    lengths,
    gain_attn,
    w_query,
    w_key,
    w_value,
    w_out,
    gain_mlp,
    w_gate,
    w_up,
    w_down,
):
    batches, piece, width = tokens.shape
    seqs = lax.axis_size("seq")
    group = lax.axis_size("fsdp")
    chips = group // 2
    devices = seqs * group
    seq_len = piece * devices
    rows = batches * piece
    share = w_query.shape[0]
    span = width // group
    length = group * piece
    aligned = share == HEAD
    member = lax.axis_index("fsdp")

    x_rows = tokens.reshape(rows, width)
    cot_rows = cotangent.reshape(rows, width)
    if aligned:
        wo_part = lax.all_gather(w_out, "seq", axis=0, tiled=True)
    else:
        wo_all = lax.all_gather(w_out, ("seq", "fsdp"), axis=0, tiled=True)
        wo_part = lax.dynamic_slice_in_dim(wo_all, member * span, span, 0)

    lane = jnp.arange(128, dtype=jnp.int32)
    device = lax.axis_index("seq") * group + member
    fold = 128 // share
    here = lane // share == lax.rem(device, fold)
    both = jnp.stack([gain_attn, gain_mlp]).astype(jnp.float32)
    tile = jnp.where(here[None], jnp.tile(both, (1, fold)), 0.0)
    tile = jnp.pad(tile, ((0, 6), (0, 0)))[None]
    group_start = lax.axis_index("seq") * length
    positions = group_start + jnp.arange(length, dtype=jnp.int32)
    begins = doc_starts(lengths, positions, batches, seq_len)
    at = jnp.arange(length, dtype=jnp.int32)
    block = min(256, length)
    low = jnp.maximum(begins - group_start + WINDOW, at[None, :] + 1) - (at // block * block)[None, :]
    low = low[:, None, :]
    group_a, query, attended, lse, kv_pad, gains, w_heads, unit_own, wd_one = start(
        seqs, chips, batches, block, tile, x_rows, (w_query, w_key, w_value), (w_gate, w_up), w_down,
        low, 1,
    )
    gains = gains.transpose(1, 0, 2, 3).reshape(devices // fold, fold, 8, 128).sum(axis=1)
    gain_one = gains[:, 0].reshape(width)
    gain_two = gains[:, 1].reshape(width)
    middle, normed_b, group_d, w_units, wd_two = branch_sum(
        seqs, chips, attended, wo_part, cot_rows, unit_own.reshape(group * share, -1), w_down,
        x_rows, gain_two[None], 3,
    )
    w_units = w_units.reshape(width, -1)
    d_middle, d_branch, mlp_gain_part, hidden, unit_part, unit_one = feed_forward(
        seqs, chips, batches, normed_b, w_units, (wd_one, wd_two), group_d, middle, cot_rows,
        gain_two[None], 4,
    )
    d_attended, layer_out, out_part, unit_two, unit_far, down_part, down_near, far_one = branch_back(
        seqs, chips, batches, d_branch, wo_part, attended, middle, hidden, (wd_one, wd_two),
        unit_part, group_d, 5,
    )
    if not aligned:
        whole = lax.dynamic_update_slice_in_dim(
            jnp.zeros((width, width), jnp.bfloat16), out_part, member * span, 0
        )
        out_part = lax.psum(whole, "fsdp").reshape(seqs, group, share, width)
        out_part = lax.dynamic_slice_in_dim(out_part, member, 1, 1).reshape(seqs * share, width)
    (
        input_grad, wq_grad, wk_grad, wv_grad, wo_grad, gain_tile, gate_grad, up_grad, far_two,
    ) = attention_back(
        seqs, chips, block, query, kv_pad, low, lse, d_attended, unit_part, unit_one, unit_two,
        unit_far, w_heads, group_a, x_rows, d_middle, gain_one[None], mlp_gain_part, out_part,
        down_part, 6,
    )
    gain_grads = lax.dynamic_slice_in_dim(gain_tile[:2], lax.rem(device, fold) * share, share, 1)
    wide = jnp.float32
    (layer_out, input_grad, wq_grad, wk_grad, wv_grad, wo_grad, gate_grad, up_grad, down_grad) = finish(
        share // 16,
        [layer_out, input_grad, wq_grad, wk_grad, wv_grad, wo_grad, gate_grad, up_grad],
        [down_near, jnp.concatenate([far_one, far_two], axis=1)],
        [jnp.bfloat16] + [wide] * 8,
    )
    return (
        layer_out.reshape(batches, piece, width),
        input_grad.reshape(batches, piece, width),
        gain_grads[0],
        wq_grad,
        wk_grad,
        wv_grad,
        wo_grad,
        gain_grads[1],
        gate_grad,
        up_grad,
        down_grad,
    )


def solution(mesh):
    spread = ("seq", "fsdp")
    tokens, rows, gains = P(None, spread, None), P(spread, None), P(spread)
    in_specs = (tokens, tokens, P(), gains, rows, rows, rows, rows, gains, rows, rows, rows)
    out_specs = (tokens, tokens, gains, rows, rows, rows, rows, gains, rows, rows, rows)
    return jax.shard_map(body, mesh=mesh, in_specs=in_specs, out_specs=out_specs, check_vma=False)
```
